32 devices in a mesh: lat: 8 (over y, x, core), lon: 4 (over z).
Axes of the slice: x: 2, y: 2, z: 4, core: 2. Of those that a mesh axis runs over, the one named last changes fastest.
Arguments:
- tokens: bfloat16 [2, 96, 96, 512], P(None, 'lat', 'lon'), may hold values from -48 to 48
- region_ids: int32 [2, 96, 96], replicated, may hold values from 0 to 3
- shifts: int32 [2], replicated, may hold values from 1 to 5, as said below
- fine_qkv: bfloat16 [512, 1536], replicated, may hold values from -2 to 2
- fine_proj: bfloat16 [512, 512], replicated, may hold values from -0.25 to 0.25
- merge_weight: bfloat16 [2048, 1024], replicated, may hold values from -0.125 to 0.125
- coarse_qkv: bfloat16 [1024, 1536], replicated, may hold values from -0.1875 to 0.1875
- coarse_proj: bfloat16 [512, 1024], replicated, may hold values from -0.25 to 0.25
Outputs:
- fine_out: bfloat16 [2, 96, 96, 512], P(None, 'lat', 'lon')
- coarse_out: bfloat16 [2, 48, 48, 1024], P(None, 'lat', 'lon')
The draws below stay inside these ranges and needn't reach their ends.
Inputs may be any that keep to these rules, and one draw needn't show every extreme that they name: `shifts`: entry 0 is the fine level's shift, entry 1 the coarse level's; one of them is 5.
All inputs are finite; a program needn't handle non-finite values.
Results may differ from the reference program's by a relative error of at most 0.012.
The reference program's roundings to bfloat16 on the way (of `normed`, `projected`, `probabilities`, `attended`, `output`, `stacked` and `merged`) count: a program that leaves them out, or rounds other values in their place, can miss the bound.
Values may be sent and summed in bfloat16 or wider, within the bound.
No kernel may reach another device: no remote copies, remote signals or barrier semaphores. Data moves between devices by JAX's collectives and lax.ppermute only.
A program may use at most 128 MiB of HBM per device.

```python
import jax
import jax.numpy as jnp
from jax import lax

D = 512
HEADS = 16
HD = 32
CD = 1024
CHEADS = 16
DEPTH = 2
WH = 6
WW = 12
REGIONS = 4
NLAT = 96
NLON = 96


def draw_tokens(key, part):
    key = jax.random.fold_in(key, 11)
    key_base = jax.random.fold_in(key, 0)
    shape = (DEPTH, NLAT, NLON, D)
    values = jax.random.normal(key_base, shape, jnp.float32)
    return jnp.clip(values, -48.0, 48.0).astype(jnp.bfloat16)


def draw_fine_qkv(key, part):
    key = jax.random.fold_in(key, 7)
    key_base = jax.random.fold_in(key, 0)
    inner_width = HEADS * HD
    values = jax.random.normal(key_base, (D, 3 * inner_width), jnp.float32) * D ** (-0.5)
    return jnp.clip(values, -2.0, 2.0).astype(jnp.bfloat16)


def draw_shifts(key, part):
    key = jax.random.fold_in(key, 5)
    key_other, key_first = jax.random.split(key, 2)
    other = jax.random.randint(key_other, (), 1, WH)
    which_first = jax.random.randint(key_first, (), 0, 2)
    return jnp.where(jnp.arange(2, dtype=jnp.int32) == which_first, WH - 1, other).astype(jnp.int32)


def touch_ends(values, own_key, smallest, high):
    index_at = [jax.random.randint(jax.random.fold_in(own_key, axis), (), 0, length) for axis, length in enumerate(values.shape)]
    widest = values.shape.index(max(values.shape))
    beside = index_at[:widest] + [(index_at[widest] + 1) % values.shape[widest]] + index_at[widest + 1:]
    return values.at[tuple(index_at)].set(smallest).at[tuple(beside)].set(high)


def scatter_about(rng, extent, deviation, bound, kind=jnp.bfloat16):
    array = jax.random.normal(rng, extent, jnp.float32) * deviation
    return jnp.minimum(jnp.maximum(array, -bound), bound).astype(kind)


def setup_inputs(seed: int = 0) -> dict:
    key_list = jax.random.split(jax.random.key(seed), 9)
    tokens = draw_tokens(jax.random.fold_in(key_list[8], 71), 0)
    region_ids = touch_ends(jax.random.randint(key_list[1], (DEPTH, NLAT, NLON), 0, REGIONS), jax.random.fold_in(key_list[1], 1), 0, REGIONS - 1).astype(jnp.int32)
    shifts = draw_shifts(jax.random.fold_in(key_list[8], 71), 0)
    fine_qkv = draw_fine_qkv(jax.random.fold_in(key_list[8], 71), 0)
    fine_proj = scatter_about(key_list[4], (HEADS * HD, D), (HEADS * HD) ** -0.5, 0.25)
    merge_weight = scatter_about(key_list[5], (4 * D, CD), (4 * D) ** -0.5, 0.125)
    coarse_qkv = scatter_about(key_list[6], (CD, 3 * CHEADS * HD), CD ** -0.5, 0.1875)
    coarse_proj = scatter_about(key_list[7], (CHEADS * HD, CD), (CHEADS * HD) ** -0.5, 0.25)
    return dict(tokens=tokens, region_ids=region_ids, shifts=shifts, fine_qkv=fine_qkv, fine_proj=fine_proj, merge_weight=merge_weight, coarse_qkv=coarse_qkv, coarse_proj=coarse_proj)


norm_eps = 1e-05

def layer_norm(activations):
    values = activations.astype(jnp.float32)
    center = lax.optimization_barrier(jnp.mean(values, axis=-1, keepdims=True))
    spread = lax.optimization_barrier(jnp.mean((values - center) ** 2, axis=-1, keepdims=True))
    return (values - center) * lax.rsqrt(spread + norm_eps)

def to_windows(tensor, row_windows, column_windows):
    layer_count = tensor.shape[0]
    tensor = tensor.reshape(layer_count, row_windows, WH, column_windows, WW, tensor.shape[-1])
    tensor = tensor.transpose(1, 3, 0, 2, 4, 5)
    return tensor.reshape(row_windows * column_windows, layer_count * WH * WW, tensor.shape[-1])

def window_attend(projected, lat_window, region, head_count):
    layer_count, row_count, column_count, triple = projected.shape
    inner_width = triple // 3
    row_windows = row_count // WH
    column_windows = column_count // WW
    windowed = to_windows(projected, row_windows, column_windows)
    lat_full = jnp.broadcast_to(lat_window[None, :, None, None], (layer_count, row_count, column_count, 1))
    lat_win = to_windows(lat_full, row_windows, column_windows)[..., 0]
    region_win = to_windows(region[..., None], row_windows, column_windows)[..., 0]
    window_total = windowed.shape[0]
    window_tokens = windowed.shape[1]
    queries = windowed[..., :inner_width].reshape(window_total, window_tokens, head_count, HD).astype(jnp.float32)
    key_block = windowed[..., inner_width:2 * inner_width].reshape(window_total, window_tokens, head_count, HD).astype(jnp.float32)
    value_block = windowed[..., 2 * inner_width:].reshape(window_total, window_tokens, head_count, HD).astype(jnp.float32)
    scores = jnp.einsum('wqhd,wkhd->whqk', queries, key_block) * (1.0 / HD ** 0.5)
    allowed = (lat_win[:, :, None] == lat_win[:, None, :]) & (region_win[:, :, None] == region_win[:, None, :])
    scores = jnp.where(allowed[:, None], scores, -1e+30)
    row_max = lax.optimization_barrier(jnp.max(scores, axis=-1, keepdims=True))
    weight_exp = jnp.exp(scores - row_max)
    probabilities = (weight_exp / lax.optimization_barrier(jnp.sum(weight_exp, axis=-1, keepdims=True))).astype(jnp.bfloat16)
    attended = jnp.einsum('whqk,wkhd->wqhd', probabilities.astype(jnp.float32), value_block).astype(jnp.bfloat16)
    attended = attended.reshape(row_windows, column_windows, layer_count, WH, WW, inner_width)
    attended = attended.transpose(2, 0, 3, 1, 4, 5)
    return attended.reshape(layer_count, row_count, column_count, inner_width)

def level(activations, region, shift_rows, weight_qkv, weight_proj, head_count):
    layer_count, lat_count, lon_count, feat_width = activations.shape
    normed = layer_norm(activations).astype(jnp.bfloat16)
    rolled = jnp.roll(normed, -shift_rows, axis=1)
    rolled = jnp.roll(rolled, -2 * shift_rows, axis=2)
    region_rolled = jnp.roll(region, -shift_rows, axis=1)
    region_rolled = jnp.roll(region_rolled, -2 * shift_rows, axis=2)
    global_rows = (jnp.arange(lat_count, dtype=jnp.int32) + shift_rows) % lat_count
    lat_window = jnp.floor_divide(global_rows - shift_rows, WH).astype(jnp.int32)

    def one_block(block_index):
        start = (block_index * WH).astype(jnp.int32)
        block_tokens = lax.dynamic_slice_in_dim(rolled, start, WH, 1)
        block_region = lax.dynamic_slice_in_dim(region_rolled, start, WH, 1)
        block_lat = lax.dynamic_slice_in_dim(lat_window, start, WH, 0)
        projected = jnp.dot(block_tokens, weight_qkv, preferred_element_type=jnp.float32).astype(jnp.bfloat16)
        return window_attend(projected, block_lat, block_region, head_count)
    blocks = lax.map(one_block, jnp.arange(lat_count // WH, dtype=jnp.int32))
    attended = blocks.transpose(1, 0, 2, 3, 4).reshape(layer_count, lat_count, lon_count, blocks.shape[-1])
    attended = jnp.roll(attended, shift_rows, axis=1)
    attended = jnp.roll(attended, 2 * shift_rows, axis=2)
    output = activations.astype(jnp.float32) + jnp.dot(attended, weight_proj, preferred_element_type=jnp.float32)
    return output.astype(jnp.bfloat16)

def merge_cells(activations, merge_weight):
    stacked = jnp.concatenate([activations[:, 0::2, 0::2], activations[:, 1::2, 0::2], activations[:, 0::2, 1::2], activations[:, 1::2, 1::2]], axis=-1)
    stacked = layer_norm(stacked).astype(jnp.bfloat16)
    return jnp.dot(stacked, merge_weight, preferred_element_type=jnp.float32).astype(jnp.bfloat16)

def reference(tokens, region_ids, shifts, fine_qkv, fine_proj, merge_weight, coarse_qkv, coarse_proj):
    fine_out = level(tokens, region_ids, shifts[0], fine_qkv, fine_proj, HEADS)
    merged = merge_cells(fine_out, merge_weight)
    coarse_out = level(merged, region_ids[:, 0::2, 0::2], shifts[1], coarse_qkv, coarse_proj, CHEADS)
    return (fine_out, coarse_out)
```

```python
import functools

import jax
import jax.numpy as jnp
import numpy as np
from jax import lax
from jax.experimental import pallas as pl
from jax.experimental.pallas import tpu as pltpu
from jax.sharding import PartitionSpec as P

HD = 32
WH = 6
WW = 12
TOK = 2 * WH * WW
EPS = 1e-05
BIG = 1e30
SCALE = float(np.log2(np.e) / np.sqrt(HD))

NT = (((1,), (1,)), ((), ()))
TN = (((0,), (0,)), ((), ()))
F32 = jnp.float32
BF16 = jnp.bfloat16


def up16(count):
    return -(-count // 16) * 16


def natural(rows, cols):
    return [(l, r, c) for l in range(2) for r in range(rows) for c in range(cols)]


def windowed(rows, cols):
    return [
        (l, wr * WH + r, wc * WW + c)
        for wr in range(rows // WH)
        for wc in range(cols // WW)
        for l in range(2)
        for r in range(WH)
        for c in range(WW)
    ]


class Shift:
    def __init__(self, rows, cols, d):
        self.rows, self.cols, self.d = rows, cols, d
        places = {"row": [], "col": [], "both": []}
        for l, r, c in natural(rows, cols):
            kind = self.kind(r, c)
            if kind != "own":
                places[kind].append((l, (r + d) % rows, (c + 2 * d) % cols))
        self.places = {k: v for k, v in places.items() if v}
        self.sizes = {k: up16(len(v)) for k, v in self.places.items()}

    def kind(self, r, c):
        row_in = 0 <= r + self.d < self.rows
        col_in = 0 <= c + 2 * self.d < self.cols
        return {(1, 1): "own", (0, 1): "row", (1, 0): "col", (0, 0): "both"}[row_in, col_in]

    def send_index(self, own_order):
        at = {place: n for n, place in enumerate(own_order)}
        index = []
        for k, v in self.places.items():
            index += [at[place] for place in v] + [-1] * (self.sizes[k] - len(v))
        return index

    def take_index(self, own_order, wanted):
        at = {("own",) + place: n for n, place in enumerate(own_order)}
        base = len(own_order)
        for k, v in self.places.items():
            for n, place in enumerate(v):
                at[(k,) + place] = base + n
            base += self.sizes[k]
        index = []
        for place in wanted:
            if place is None:
                index.append(-1)
                continue
            l, r, c = place
            index.append(at[self.kind(r, c), l, (r + self.d) % self.rows, (c + 2 * self.d) % self.cols])
        return index

    def exchange(self, pieces):
        if not pieces:
            return []
        step = -1 if self.d > 0 else 1
        lat, lon = lax.axis_size("lat"), lax.axis_size("lon")
        got = []
        for k, piece in zip(self.places, pieces):
            if k == "row":
                got.append(lax.ppermute(piece, "lat", [(i, (i + step) % lat) for i in range(lat)]))
            elif k == "col":
                got.append(lax.ppermute(piece, "lon", [(j, (j + step) % lon) for j in range(lon)]))
            else:
                pairs = [
                    (i * lon + j, (i + step) % lat * lon + (j + step) % lon)
                    for i in range(lat)
                    for j in range(lon)
                ]
                got.append(lax.ppermute(piece, ("lat", "lon"), pairs))
        return got


def column(index):
    return np.asarray(index, np.int32).reshape(-1, 1)


def select_rows(index, source):
    lane = lax.broadcasted_iota(jnp.int32, (index.shape[0], source.shape[0]), 1)
    pick = jnp.where(lane == index, 1.0, 0.0).astype(BF16)
    return jnp.dot(pick, source, preferred_element_type=F32)


def stack_rows(parts):
    return parts[0] if len(parts) == 1 else jnp.concatenate(parts, axis=0)


def layer_norm(values):
    center = jnp.mean(values, axis=-1, keepdims=True)
    values = values - center
    spread = jnp.mean(values * values, axis=-1, keepdims=True)
    return values * lax.rsqrt(spread + EPS)


def attend(q, k, v, key_id):
    lane = lax.broadcasted_iota(jnp.int32, (1, 128), 1)
    forbid = jnp.where(lane < 8, BIG, 0.0).astype(BF16)
    not_id = (key_id - 1).astype(BF16) * forbid
    parts = []
    for g in range(q.shape[1] // 128):
        at = slice(g * 128, g * 128 + 128)
        keys = jnp.concatenate([k[:, at], key_id], axis=1)
        queries = []
        for h in range(4):
            mine = jnp.where((lane >= h * HD) & (lane < (h + 1) * HD), 1.0, 0.0).astype(BF16)
            queries.append(jnp.concatenate([q[:, at] * mine, not_id], axis=1))
        scores = lax.dot_general(keys, stack_rows(queries), NT, preferred_element_type=F32)
        top = jnp.max(scores, axis=0, keepdims=True)
        weight = jnp.exp2((scores - top) * SCALE)
        total = jnp.sum(weight, axis=0, keepdims=True)
        out = lax.dot_general(v[:, at], weight.astype(BF16), TN, preferred_element_type=F32)
        out = out * (1.0 / total)
        for h in range(4):
            parts.append(out[h * HD : (h + 1) * HD, h * TOK : (h + 1) * TOK])
    return jnp.concatenate(parts, axis=0)


def call(body, outs, args, scratch=(), flops=0, moved=0, vmem=48):
    return pl.pallas_call(
        body,
        out_shape=outs,
        in_specs=[pl.BlockSpec(memory_space=pltpu.VMEM)] * len(args),
        out_specs=[pl.BlockSpec(memory_space=pltpu.VMEM)] * len(outs),
        scratch_shapes=list(scratch),
        compiler_params=pltpu.CompilerParams(vmem_limit_bytes=vmem << 20),
        cost_estimate=pl.CostEstimate(flops=flops, bytes_accessed=moved, transcendentals=0),
    )(*args)


def piece_shapes(shift, width):
    return [jax.ShapeDtypeStruct((n, width), BF16) for n in shift.sizes.values()]


def flat(ref):
    layers, rows, cols, width = ref.shape
    return ref[...].astype(F32).reshape(layers * rows * cols, width).astype(BF16)


def put_pieces(value, refs):
    at = 0
    for ref in refs:
        ref[...] = value[at : at + ref.shape[0]].astype(BF16)
        at += ref.shape[0]


def first_pieces(tokens, shift):
    _, rows, cols, width = tokens.shape
    index = column(shift.send_index(natural(rows, cols)))

    def body(tokens_ref, index_ref, *outs):
        put_pieces(select_rows(index_ref[...], flat(tokens_ref)), outs)

    return call(body, piece_shapes(shift, width), [tokens, index], flops=2 * index.size * 576 * 512, moved=1 << 20)


def id_kernel(regions, fine_places, coarse_places, rows, cols, a, big_a):
    _, lat, lon = regions.shape
    flat_regions = regions.reshape(2 * lat, lon)
    fine = np.asarray(fine_places, np.int32) + np.asarray([[0, a, 2 * a]], np.int32)
    coarse = np.asarray(coarse_places, np.int32) + np.asarray([[0, big_a, 2 * big_a]], np.int32)
    places = np.concatenate([fine, coarse * np.asarray([[1, 2, 2]], np.int32)], axis=0)
    count = places.shape[0]
    cuts = [column(places[:, n]) for n in range(3)]

    def body(regions_ref, layer_ref, row_ref, col_ref, fine_ref, coarse_ref):
        row = row_ref[...] + lax.axis_index("lat") * rows
        col = col_ref[...] + lax.axis_index("lon") * cols
        wrapped = (row < 0) | (row >= lat)
        row = jnp.where(row < 0, row + lat, row)
        row = jnp.where(row >= lat, row - lat, row)
        col = jnp.where(col < 0, col + lon, col)
        col = jnp.where(col >= lon, col - lon, col)
        picked = select_rows(row + layer_ref[...] * lat, regions_ref[...].astype(F32).astype(BF16))
        lane = lax.broadcasted_iota(jnp.int32, (count, lon), 1)
        ids = jnp.sum(jnp.where(lane == col, picked, 0.0), axis=1, keepdims=True)
        ids = ids + jnp.where(wrapped, 4.0, 0.0)
        lane = lax.broadcasted_iota(jnp.int32, (count, 128), 1).astype(F32)
        hot = jnp.where(lane == ids, 1.0, 0.0).astype(BF16)
        fine_ref[...] = hot[: len(fine_places)]
        coarse_ref[...] = hot[len(fine_places) :]

    outs = [
        jax.ShapeDtypeStruct((len(fine_places), 128), BF16),
        jax.ShapeDtypeStruct((len(coarse_places), 128), BF16),
    ]
    return call(body, outs, [flat_regions, *cuts], flops=1 << 28, moved=4 << 20)


def fine_level(tokens, pieces, key_id, w_qkv, w_proj, come, on, back):
    _, rows, cols, width = tokens.shape
    order = windowed(rows, cols)
    count = len(order)
    windows = count // TOK
    inner = w_proj.shape[0]
    take = column(come.take_index(natural(rows, cols), order))
    send = on.send_index(order) + back.send_index(order)
    extra = [column(send)] if send else []

    def body(*refs):
        tokens_ref, refs = refs[0], refs[1:]
        piece_refs, refs = refs[: len(pieces)], refs[len(pieces) :]
        id_ref, qkv_w_ref, proj_w_ref, take_ref, *refs = refs
        send_ref, refs = (refs[0], refs[1:]) if send else (None, refs)
        out_ref, *refs = refs
        piece_outs, (x_ref, qkv_ref) = refs[:-2], refs[-2:]
        source = stack_rows([flat(tokens_ref)] + [ref[...] for ref in piece_refs])
        x = select_rows(take_ref[...], source)
        x_ref[...] = x
        normed = layer_norm(x).astype(BF16)
        qkv_ref[...] = jnp.dot(normed, qkv_w_ref[...], preferred_element_type=F32).astype(BF16)

        def one(w, carry):
            at = pl.ds(pl.multiple_of(w * TOK, TOK), TOK)
            qkv = qkv_ref[at, :]
            out = attend(qkv[:, :inner], qkv[:, inner : 2 * inner], qkv[:, 2 * inner :], id_ref[at, :])
            out = lax.dot_general(out.astype(BF16), proj_w_ref[...], TN, preferred_element_type=F32)
            out_ref[at, :] = (x_ref[at, :] + out).astype(BF16)
            return carry

        lax.fori_loop(0, windows, one, 0)
        if send:
            put_pieces(select_rows(send_ref[...], out_ref[...]), piece_outs)

    outs = [jax.ShapeDtypeStruct((count, width), BF16)]
    outs += piece_shapes(on, width) + piece_shapes(back, width)
    scratch = [pltpu.VMEM((count, width), F32), pltpu.VMEM((count, 3 * inner), BF16)]
    args = [tokens, *pieces, key_id, w_qkv, w_proj, take, *extra]
    out, *sent = call(body, outs, args, scratch, flops=3 << 30, moved=6 << 20)
    cut = len(on.places)
    return out, sent[:cut], sent[cut:]


def coarse_level(fine, pieces, key_id, w_merge, w_qkv, w_proj, rows, cols, come, back):
    order = natural(rows // 2, cols // 2)
    count = len(order)
    quarter, width = w_merge.shape[0] // 4, w_merge.shape[1]
    inner = w_proj.shape[0]
    wanted = []
    for dr, dc in ((0, 0), (1, 0), (0, 1), (1, 1)):
        wanted += [(l, 2 * r + dr, 2 * c + dc) for l, r, c in order]
    take = column(come.take_index(windowed(rows, cols), wanted))
    send = back.send_index(order)

    def body(*refs):
        fine_ref, refs = refs[0], refs[1:]
        piece_refs, refs = refs[: len(pieces)], refs[len(pieces) :]
        id_ref, merge_ref, qkv_w_ref, proj_w_ref, take_ref, send_ref, out_ref, *piece_outs = refs
        source = stack_rows([fine_ref[...]] + [ref[...] for ref in piece_refs])
        x = select_rows(take_ref[...], source)
        x = jnp.concatenate([x[n * count : (n + 1) * count] for n in range(4)], axis=1)
        stacked = layer_norm(x).astype(BF16)
        merged = jnp.dot(stacked, merge_ref[...], preferred_element_type=F32).astype(BF16).astype(F32)
        normed = layer_norm(merged).astype(BF16)
        qkv = jnp.dot(normed, qkv_w_ref[...], preferred_element_type=F32).astype(BF16)
        out = attend(qkv[:, :inner], qkv[:, inner : 2 * inner], qkv[:, 2 * inner :], id_ref[...])
        out = lax.dot_general(out.astype(BF16), proj_w_ref[...], TN, preferred_element_type=F32)
        out = (merged + out).astype(BF16)
        out_ref[...] = out
        put_pieces(select_rows(send_ref[...], out), piece_outs)

    outs = [jax.ShapeDtypeStruct((count, width), BF16)] + piece_shapes(back, width)
    args = [fine, *pieces, key_id, w_merge, w_qkv, w_proj, take, column(send)]
    out, *sent = call(body, outs, args, flops=3 << 30, moved=12 << 20)
    return out, sent


def assemble(own, pieces, own_order, back, rows, cols):
    width = own.shape[1]
    padded = up16(cols) if cols % 8 else cols
    wanted = [
        (l, r, c) if c < cols else None for l in range(2) for r in range(rows) for c in range(padded)
    ]
    take = column(back.take_index(own_order, wanted))

    def body(own_ref, *refs):
        piece_refs, (take_ref, out_ref) = refs[:-2], refs[-2:]
        source = stack_rows([own_ref[...]] + [ref[...] for ref in piece_refs])
        out = select_rows(take_ref[...], source).reshape(2, rows, padded, width)
        out_ref[...] = out[:, :, :cols, :].astype(BF16)

    outs = [jax.ShapeDtypeStruct((2, rows, cols, width), BF16)]
    return call(body, outs, [own, *pieces, take], flops=1 << 30, moved=4 << 20)[0]


def frame(shift):
    return shift if shift <= WH // 2 else shift - WH


def plan(t0, t1):
    best = None
    for a in (t0, t0 - WH):
        for big_a in (t1, t1 - WH):
            if abs(2 * big_a - a) >= WH or 2 * abs(big_a) > WH:
                continue
            cost = (abs(a) + abs(2 * big_a - a) + abs(big_a), abs(a))
            if best is None or cost < best[0]:
                best = (cost, a, big_a)
    return best[1:]


def program(t0, t1, tokens, regions, fine_qkv, fine_proj, merge_weight, coarse_qkv, coarse_proj):
    _, rows, cols, _ = tokens.shape
    a, big_a = plan(t0, t1)
    fine_come = Shift(rows, cols, a)
    fine_back = Shift(rows, cols, -a)
    coarse_come = Shift(rows, cols, 2 * big_a - a)
    coarse_back = Shift(rows // 2, cols // 2, -big_a)

    pieces = fine_come.exchange(first_pieces(tokens, fine_come))
    fine_id, coarse_id = id_kernel(
        regions, windowed(rows, cols), natural(rows // 2, cols // 2), rows, cols, a, big_a
    )
    fine, on, back = fine_level(
        tokens, pieces, fine_id, fine_qkv, fine_proj, fine_come, coarse_come, fine_back
    )
    on = coarse_come.exchange(on)
    back = fine_back.exchange(back)
    coarse, coarse_sent = coarse_level(
        fine, on, coarse_id, merge_weight, coarse_qkv, coarse_proj, rows, cols, coarse_come, coarse_back
    )
    coarse_got = coarse_back.exchange(coarse_sent)
    fine_out = assemble(fine, back, windowed(rows, cols), fine_back, rows, cols)
    coarse_out = assemble(
        coarse, coarse_got, natural(rows // 2, cols // 2), coarse_back, rows // 2, cols // 2
    )
    return fine_out, coarse_out


def on_device(tokens, region_ids, shifts, *weights):
    pairs = [(WH - 1, t) for t in range(1, WH)] + [(t, WH - 1) for t in range(1, WH - 1)]
    which = jnp.where(shifts[0] == WH - 1, shifts[1] - 1, shifts[0] + WH - 2)
    branches = [functools.partial(program, t0, t1) for t0, t1 in pairs]
    return lax.switch(which, branches, tokens, region_ids, *weights)


def solution(mesh):
    return jax.shard_map(
        on_device,
        mesh=mesh,
        in_specs=(P(None, "lat", "lon", None), P(), P(), P(), P(), P(), P(), P()),
        out_specs=(P(None, "lat", "lon", None), P(None, "lat", "lon", None)),
        check_vma=False,
    )
```

```python
import functools

import jax
import jax.numpy as jnp
import numpy as np
from jax import lax
from jax.experimental import pallas as pl
from jax.experimental.pallas import tpu as pltpu
from jax.sharding import PartitionSpec as P

HD = 32
WH = 6
WW = 12
TOK = 2 * WH * WW
EPS = 1e-05
BIG = 1e30
SCALE = float(np.log2(np.e) / np.sqrt(HD))

NT = (((1,), (1,)), ((), ()))
TN = (((0,), (0,)), ((), ()))
F32 = jnp.float32
BF16 = jnp.bfloat16

PAIRS = [(WH - 1, t) for t in range(1, WH)] + [(t, WH - 1) for t in range(1, WH - 1)]


def up16(count):
    return -(-count // 16) * 16


def natural(rows, cols):
    return [(l, r, c) for l in range(2) for r in range(rows) for c in range(cols)]


def windowed(rows, cols):
    return [
        (l, wr * WH + r, wc * WW + c)
        for wr in range(rows // WH)
        for wc in range(cols // WW)
        for l in range(2)
        for r in range(WH)
        for c in range(WW)
    ]


def moved(order, d):
    return [(l, r + d, c + 2 * d) for l, r, c in order]


def exchange_places(held, wanted, rows, cols, sign):
    at = {place: n for n, place in enumerate(held)}
    found = []
    for dr, dc in ((sign, 0), (0, sign), (sign, sign)):
        numbers, places = [], []
        for l, r, c in sorted(set(wanted) - set(held)):
            n = at.get((l, r - dr * rows, c - dc * cols))
            if n is not None:
                numbers.append(n)
                places.append((l, r, c))
        found.append((numbers, places))
    return found


class Tables:
    def __init__(self, rows, cols):
        crows, ccols = rows // 2, cols // 2
        block, cblock = natural(rows, cols), natural(crows, ccols)
        cases = []
        for t0, t1 in PAIRS:
            a = t0 - WH
            big_a = t1 if t1 <= 2 else t1 - WH
            ahead = 1 if t0 < WH - 1 or t1 <= 2 else -1
            fine = moved(windowed(rows, cols), a)
            coarse = moved(cblock, big_a)
            quarters = [
                (l, 2 * r + dr, 2 * c + dc)
                for dr, dc in ((0, 0), (1, 0), (0, 1), (1, 1))
                for l, r, c in coarse
            ]
            one = exchange_places(block, fine, rows, cols, -1)
            wanted = quarters + (block if ahead > 0 else [])
            two = exchange_places(fine, wanted, rows, cols, ahead)
            back = 1 if big_a < 0 else -1
            three = exchange_places(coarse, cblock, crows, ccols, back)
            got = set(fine).union(*[places for _, places in two])
            four = exchange_places(fine, [p for p in block if p not in got], rows, cols, back)
            cases.append((a, big_a, ahead, back, fine, coarse, quarters, one, two, three, four))

        def sizes(which):
            return [up16(max(len(case[which][k][0]) for case in cases)) for k in range(3)]

        self.one, self.two, self.three, self.four = (sizes(n) for n in (7, 8, 9, 10))
        tables = {}
        for a, big_a, ahead, back, fine, coarse, quarters, one, two, three, four in cases:

            def send(found, room):
                return [n for (numbers, _), size in zip(found, room) for n in numbers + [-1] * (size - len(numbers))]

            def source(held, *exchanges):
                places = list(held)
                for found, room in exchanges:
                    for (_, got), size in zip(found, room):
                        places += got + [None] * (size - len(got))
                return {p: n for n, p in enumerate(places) if p is not None}

            first, second = source(block, (one, self.one)), source(fine, (two, self.two))
            third = source(coarse, (three, self.three))
            last = source(fine, (two, self.two), (four, self.four))
            out = [(l, r, c) for r in range(crows) for c in range(ccols) for l in range(2)]
            rows_of = dict(
                send_one=send(one, self.one),
                take_one=[first[p] for p in fine],
                send_two=send(two, self.two),
                take_two=[second[p] for p in quarters],
                send_three=send(three, self.three),
                send_four=send(four, self.four),
                fine_out=[last[p] for p in block],
                coarse_out=[third[p] for p in out],
            )
            for name, row in rows_of.items():
                row = np.asarray(row + [-1] * (-len(row) % 128), np.float32).reshape(-1, 128)
                tables.setdefault(name, []).append(row)
        self.tables = {name: np.stack(found) for name, found in tables.items()}


def case_of(shifts_ref):
    t0, t1 = shifts_ref[0], shifts_ref[1]
    return jnp.where(t0 == WH - 1, t1 - 1, t0 + WH - 2)


def columns_of(rows, count):
    parts = [jnp.broadcast_to(rows[j : j + 1], (128, 128)).T for j in range(rows.shape[0])]
    return stack_rows(parts)[:count]


def select_rows(index, source):
    lane = lax.broadcasted_iota(jnp.int32, (1, 128), 1).astype(F32)
    size = source.shape[0]
    pick = [jnp.where(index == lane + float(at), 1.0, 0.0).astype(BF16) for at in range(0, size, 128)]
    pick = jnp.concatenate(pick, axis=1)[:, :size]
    return jnp.dot(pick, source, preferred_element_type=F32)


def stack_rows(parts):
    return parts[0] if len(parts) == 1 else jnp.concatenate(parts, axis=0)


def layer_norm(values):
    center = jnp.mean(values, axis=-1, keepdims=True)
    values = values - center
    spread = jnp.mean(values * values, axis=-1, keepdims=True)
    return values * lax.rsqrt(spread + EPS)


def attend(q, k, v, key_id):
    lane = lax.broadcasted_iota(jnp.int32, (1, 128), 1)
    forbid = jnp.where(lane < 8, BIG, 0.0).astype(BF16)
    not_id = (key_id - 1).astype(BF16) * forbid
    parts = []
    for g in range(q.shape[1] // 128):
        at = slice(g * 128, g * 128 + 128)
        keys = jnp.concatenate([k[:, at], key_id], axis=1)
        queries = []
        for h in range(4):
            mine = jnp.where((lane >= h * HD) & (lane < (h + 1) * HD), 1.0, 0.0).astype(BF16)
            queries.append(jnp.concatenate([q[:, at] * mine, not_id], axis=1))
        scores = lax.dot_general(keys, stack_rows(queries), NT, preferred_element_type=F32)
        top = jnp.max(scores, axis=0, keepdims=True)
        weight = jnp.exp2((scores - top) * SCALE)
        total = jnp.sum(weight, axis=0, keepdims=True)
        out = lax.dot_general(v[:, at], weight.astype(BF16), TN, preferred_element_type=F32)
        out = out * (1.0 / total)
        for h in range(4):
            parts.append(out[h * HD : (h + 1) * HD, h * TOK : (h + 1) * TOK])
    return jnp.concatenate(parts, axis=0)


def call(body, outs, shifts, args, scratch=(), flops=0, moved_bytes=0, vmem=24):
    whole = pl.BlockSpec(memory_space=pltpu.VMEM)
    return pl.pallas_call(
        body,
        out_shape=outs,
        in_specs=[pl.BlockSpec(memory_space=pltpu.SMEM)] + [whole] * len(args),
        out_specs=[whole] * len(outs),
        scratch_shapes=list(scratch),
        compiler_params=pltpu.CompilerParams(vmem_limit_bytes=vmem << 20),
        cost_estimate=pl.CostEstimate(flops=flops, bytes_accessed=moved_bytes, transcendentals=0),
    )(shifts, *args)


def piece_shapes(sizes, width):
    return [jax.ShapeDtypeStruct((n, width), BF16) for n in sizes]


def flat(ref):
    layers, rows, cols, width = ref.shape
    return ref[...].astype(F32).reshape(layers * rows * cols, width).astype(BF16)


def put_pieces(value, refs):
    at = 0
    for ref in refs:
        ref[...] = value[at : at + ref.shape[0]].astype(BF16)
        at += ref.shape[0]


def exchange(pieces, sign):
    lat, lon = lax.axis_size("lat"), lax.axis_size("lon")
    row, col, both = pieces
    pairs = [((i + sign) % lat * lon + (j + sign) % lon, i * lon + j) for i in range(lat) for j in range(lon)]
    col = lax.ppermute(col, "lon", [((j + sign) % lon, j) for j in range(lon)])
    both = lax.ppermute(both, ("lat", "lon"), pairs)
    row = lax.ppermute(row, "lat", [((i + sign) % lat, i) for i in range(lat)])
    return [row, col, both]


def first_pieces(shifts, tokens, plan):
    def body(shifts_ref, tokens_ref, send_ref, *outs):
        index = columns_of(send_ref[case_of(shifts_ref)], sum(plan.one))
        put_pieces(select_rows(index, flat(tokens_ref)), outs)

    outs = piece_shapes(plan.one, tokens.shape[-1])
    return call(body, outs, shifts, [tokens, plan.tables["send_one"]], flops=1 << 28, moved_bytes=1 << 20)


def id_kernel(shifts, regions, rows, cols):
    _, lat, lon = regions.shape
    flat_regions = regions.reshape(2 * lat, lon)
    fine, coarse = windowed(rows, cols), natural(rows // 2, cols // 2)
    places = np.asarray(fine + coarse, np.float32)
    places[len(fine) :, 1:] *= 2
    pad = -len(places) % 128
    places = np.pad(places, ((0, pad), (0, 0))).T.reshape(3, -1, 128)
    is_fine = np.pad(np.ones(len(fine), np.float32), (0, len(coarse) + pad)).reshape(1, -1, 128)
    places = np.concatenate([places, is_fine])
    count = len(fine) + len(coarse)

    def body(shifts_ref, regions_ref, places_ref, fine_ref, coarse_ref):
        t0, t1 = shifts_ref[0], shifts_ref[1]
        a = (t0 - WH).astype(F32)
        big_a = (2 * jnp.where(case_of(shifts_ref) < 2, t1, t1 - WH)).astype(F32)
        is_fine = places_ref[3]
        d = is_fine * a + (1.0 - is_fine) * big_a
        row = places_ref[1] + d + (lax.axis_index("lat") * rows).astype(F32)
        col = places_ref[2] + 2.0 * d + (lax.axis_index("lon") * cols).astype(F32)
        wrapped = jnp.where((row < 0) | (row >= lat), 4.0, 0.0)
        row = jnp.where(row < 0, row + lat, jnp.where(row >= lat, row - lat, row))
        col = jnp.where(col < 0, col + lon, jnp.where(col >= lon, col - lon, col))
        row = columns_of(row + places_ref[0] * lat, count)
        col = columns_of(col, count)
        wrapped = columns_of(wrapped, count)
        picked = select_rows(row, regions_ref[...].astype(F32).astype(BF16))
        ids = jnp.zeros((count, 128), F32)
        for at in range(0, lon, 128):
            width = min(128, lon - at)
            lane = lax.broadcasted_iota(jnp.int32, (1, width), 1).astype(F32) + float(at)
            here = jnp.where(lane == col[:, :width], picked[:, at : at + width], 0.0)
            ids = ids + jnp.sum(here, axis=1, keepdims=True)
        lane = lax.broadcasted_iota(jnp.int32, (1, 128), 1).astype(F32)
        hot = jnp.where(lane == ids + wrapped, 1.0, 0.0).astype(BF16)
        fine_ref[...] = hot[: len(fine)]
        coarse_ref[...] = hot[len(fine) :]

    outs = [jax.ShapeDtypeStruct((len(fine), 128), BF16), jax.ShapeDtypeStruct((len(coarse), 128), BF16)]
    return call(body, outs, shifts, [flat_regions, places], flops=1 << 28, moved_bytes=4 << 20)


def fine_level(shifts, tokens, pieces, key_id, w_qkv, w_proj, plan):
    _, rows, cols, width = tokens.shape
    count = 2 * rows * cols
    inner = w_proj.shape[0]

    def body(shifts_ref, tokens_ref, row_ref, col_ref, both_ref, id_ref, qkv_w_ref, proj_w_ref, take_ref, send_ref, *refs):
        out_ref, *piece_outs, x_ref, qkv_ref = refs
        case = case_of(shifts_ref)
        source = stack_rows([flat(tokens_ref), row_ref[...], col_ref[...], both_ref[...]])
        x = select_rows(columns_of(take_ref[case], count), source)
        x_ref[...] = x
        normed = layer_norm(x).astype(BF16)
        qkv_ref[...] = jnp.dot(normed, qkv_w_ref[...], preferred_element_type=F32).astype(BF16)

        def one(w, carry):
            at = pl.ds(pl.multiple_of(w * TOK, TOK), TOK)
            qkv = qkv_ref[at, :]
            out = attend(qkv[:, :inner], qkv[:, inner : 2 * inner], qkv[:, 2 * inner :], id_ref[at, :])
            out = lax.dot_general(out.astype(BF16), proj_w_ref[...], TN, preferred_element_type=F32)
            out_ref[at, :] = (x_ref[at, :] + out).astype(BF16)
            return carry

        lax.fori_loop(0, count // TOK, one, 0)
        index = columns_of(send_ref[case], sum(plan.two))
        put_pieces(select_rows(index, out_ref[...]), piece_outs)

    outs = [jax.ShapeDtypeStruct((count, width), BF16)] + piece_shapes(plan.two, width)
    scratch = [pltpu.VMEM((count, width), F32), pltpu.VMEM((count, 3 * inner), BF16)]
    args = [tokens, *pieces, key_id, w_qkv, w_proj, plan.tables["take_one"], plan.tables["send_two"]]
    out, *sent = call(body, outs, shifts, args, scratch, flops=3 << 30, moved_bytes=6 << 20)
    return out, sent


def coarse_level(shifts, fine, pieces, key_id, w_merge, w_qkv, w_proj, plan):
    count = key_id.shape[0]
    width = w_merge.shape[1]
    half = fine.shape[1]
    inner = w_proj.shape[0]

    def body(shifts_ref, fine_ref, row_ref, col_ref, both_ref, id_ref, merge_ref, qkv_w_ref, proj_w_ref, *refs):
        take_ref, send_ref, fine_send_ref, out_ref, *piece_outs = refs
        case = case_of(shifts_ref)
        source = stack_rows([fine_ref[...], row_ref[...], col_ref[...], both_ref[...]])
        x = select_rows(columns_of(take_ref[case], 4 * count), source)
        x = jnp.concatenate([x[n * count : (n + 1) * count] for n in range(4)], axis=1)
        stacked = layer_norm(x).astype(BF16)
        merged = jnp.dot(stacked, merge_ref[...], preferred_element_type=F32).astype(BF16).astype(F32)
        normed = layer_norm(merged).astype(BF16)
        qkv = jnp.dot(normed, qkv_w_ref[...], preferred_element_type=F32).astype(BF16)
        out = attend(qkv[:, :inner], qkv[:, inner : 2 * inner], qkv[:, 2 * inner :], id_ref[...])
        out = lax.dot_general(out.astype(BF16), proj_w_ref[...], TN, preferred_element_type=F32)
        out = (merged + out).astype(BF16)
        out_ref[...] = out
        sent = select_rows(columns_of(send_ref[case], sum(plan.three)), out).astype(BF16)
        fine_sent = select_rows(columns_of(fine_send_ref[case], sum(plan.four)), fine_ref[...]).astype(BF16)
        at = fine_at = 0
        for ref, n, m in zip(piece_outs, plan.three, plan.four):
            ref[:n, :] = sent[at : at + n, :half]
            ref[n : 2 * n, :] = sent[at : at + n, half:]
            ref[2 * n :, :] = fine_sent[fine_at : fine_at + m]
            at += n
            fine_at += m

    sizes = [2 * n + m for n, m in zip(plan.three, plan.four)]
    outs = [jax.ShapeDtypeStruct((count, width), BF16)] + piece_shapes(sizes, half)
    args = [fine, *pieces, key_id, w_merge, w_qkv, w_proj]
    args += [plan.tables[name] for name in ("take_two", "send_three", "send_four")]
    out, *sent = call(body, outs, shifts, args, flops=3 << 30, moved_bytes=12 << 20)
    return out, sent


def outputs(shifts, fine, got_two, coarse, got_three, plan, rows, cols):
    half, width = fine.shape[1], coarse.shape[1]

    def body(shifts_ref, fine_ref, *refs):
        two, coarse_ref, three = refs[:3], refs[3], refs[4:7]
        fine_take_ref, coarse_take_ref, fine_out_ref, coarse_out_ref = refs[7:]
        case = case_of(shifts_ref)
        four = [ref[2 * n :, :] for ref, n in zip(three, plan.three)]
        source = stack_rows([fine_ref[...]] + [ref[...] for ref in two] + four)
        out = select_rows(columns_of(fine_take_ref[case], 2 * rows * cols), source)
        fine_out_ref[...] = out.reshape(2, rows, cols, half).astype(BF16)
        back = [
            jnp.concatenate([ref[:n, :], ref[n : 2 * n, :]], axis=1) for ref, n in zip(three, plan.three)
        ]
        source = stack_rows([coarse_ref[...]] + back)
        out = select_rows(columns_of(coarse_take_ref[case], coarse.shape[0]), source).astype(BF16)
        for n in range(coarse.shape[0] // 2):
            coarse_out_ref[n // (cols // 2), n % (cols // 2)] = out[2 * n : 2 * n + 2]

    outs = [
        jax.ShapeDtypeStruct((2, rows, cols, half), BF16),
        jax.ShapeDtypeStruct((rows // 2, cols // 2, 2, width), BF16),
    ]
    args = [fine, *got_two, coarse, *got_three, plan.tables["fine_out"], plan.tables["coarse_out"]]
    fine_out, coarse_out = call(body, outs, shifts, args, flops=1 << 30, moved_bytes=4 << 20)
    return fine_out, coarse_out.transpose(2, 0, 1, 3)


def on_device(tokens, regions, shifts, fine_qkv, fine_proj, merge_weight, coarse_qkv, coarse_proj):
    _, rows, cols, _ = tokens.shape
    plan = Tables(rows, cols)
    t0, t1 = shifts[0], shifts[1]
    both_ways = [functools.partial(exchange, sign=sign) for sign in (1, -1)]
    got_one = exchange(first_pieces(shifts, tokens, plan), -1)
    fine_id, coarse_id = id_kernel(shifts, regions, rows, cols)
    fine, sent = fine_level(shifts, tokens, got_one, fine_id, fine_qkv, fine_proj, plan)
    got_two = lax.cond((t0 < WH - 1) | (t1 <= 2), *both_ways, sent)
    coarse, sent = coarse_level(
        shifts, fine, got_two, coarse_id, merge_weight, coarse_qkv, coarse_proj, plan
    )
    got_three = lax.cond(t1 > 2, *both_ways, sent)
    return outputs(shifts, fine, got_two, coarse, got_three, plan, rows, cols)


def solution(mesh):
    return jax.shard_map(
        on_device,
        mesh=mesh,
        in_specs=(P(None, "lat", "lon", None), P(), P(), P(), P(), P(), P(), P()),
        out_specs=(P(None, "lat", "lon", None), P(None, "lat", "lon", None)),
        check_vma=False,
    )
```

```python
import functools

import jax
import jax.numpy as jnp
import numpy as np
from jax import lax
from jax.experimental import pallas as pl
from jax.experimental.pallas import tpu as pltpu
from jax.sharding import PartitionSpec as P

HD = 32
WH = 6
WW = 12
TOK = 2 * WH * WW
EPS = 1e-05
BIG = 1e30
SCALE = float(np.log2(np.e) / np.sqrt(HD))

NT = (((1,), (1,)), ((), ()))
TN = (((0,), (0,)), ((), ()))
F32 = jnp.float32
BF16 = jnp.bfloat16
I32 = jnp.int32

PAIRS = [(WH - 1, t) for t in range(1, WH)] + [(t, WH - 1) for t in range(1, WH - 1)]


def up16(count):
    return -(-count // 16) * 16


def natural(rows, cols):
    return [(l, r, c) for l in range(2) for r in range(rows) for c in range(cols)]


def windowed(rows, cols):
    return [
        (l, wr * WH + r, wc * WW + c)
        for wr in range(rows // WH)
        for wc in range(cols // WW)
        for l in range(2)
        for r in range(WH)
        for c in range(WW)
    ]


def moved(order, d):
    return [(l, r + d, c + 2 * d) for l, r, c in order]


def exchange_places(held, wanted, rows, cols, sign):
    at = {place: n for n, place in enumerate(held)}
    found = []
    for dr, dc in ((sign, 0), (0, sign), (sign, sign)):
        numbers, places = [], []
        for l, r, c in sorted(set(wanted) - set(held)):
            n = at.get((l, r - dr * rows, c - dc * cols))
            if n is not None:
                numbers.append(n)
                places.append((l, r, c))
        found.append((numbers, places))
    return found


def offsets(t0, t1):
    a = t0 if t0 <= 2 else t0 - WH
    big_a = t1 if t1 <= 2 else t1 - WH
    ahead = 1 if 2 * big_a > a or 2 * big_a - a == 0 and a < 0 else -1
    return a, big_a, ahead


def classes_of(needs, limits):
    which = [next(n for n, limit in enumerate(limits) if need[1] <= limit) for need in needs]
    sizes = [
        [up16(max(need[k] for need, w in zip(needs, which) if w == n)) for k in range(3)]
        for n in range(len(limits))
    ]
    return sizes, which


class Plan:
    def __init__(self, rows, cols):
        crows, ccols = rows // 2, cols // 2
        block, cblock = natural(rows, cols), natural(crows, ccols)
        cases = []
        for t0, t1 in PAIRS:
            a, big_a, ahead = offsets(t0, t1)
            fine = moved(windowed(rows, cols), a)
            coarse = moved(cblock, big_a)
            quarters = [
                (l, 2 * r + dr, 2 * c + dc)
                for dr, dc in ((0, 0), (1, 0), (0, 1), (1, 1))
                for l, r, c in coarse
            ]
            come = 1 if a > 0 else -1
            one = exchange_places(block, fine, rows, cols, come)
            home = [p for p in block if p not in set(fine)]
            wanted = quarters + (home if come == -ahead else [])
            two = exchange_places(fine, wanted, rows, cols, ahead)
            back = 1 if big_a < 0 else -1
            three = exchange_places(coarse, cblock, crows, ccols, back)
            got = set(fine).union(*[places for _, places in two])
            four = exchange_places(fine, [p for p in block if p not in got], rows, cols, back)
            cases.append((come, ahead, back, fine, coarse, quarters, one, two, three, four))

        def needs(which):
            return [[len(numbers) for numbers, _ in case[which]] for case in cases]

        self.one, one_class = classes_of(needs(6), [64, 512])
        self.two, two_class = classes_of(needs(7), [64, 128, 512])
        fine_back = [max(need) > 0 for need in needs(9)]
        self.three = []
        self.four = []
        for with_fine in (False, True):
            inside = [n for n, flag in enumerate(fine_back) if flag == with_fine]
            self.three.append([up16(max(needs(8)[n][k] for n in inside)) for k in range(3)])
            self.four.append([up16(max(needs(9)[n][k] for n in inside)) for k in range(3)])
        three_class = [int(flag) for flag in fine_back]

        def branches(which_class, direction):
            pairs = [(n, case[direction]) for n, case in zip(which_class, cases)]
            found = sorted(set(pairs))
            return found, [found.index(pair) for pair in pairs]

        self.one_branches, one_at = branches(one_class, 0)
        self.two_branches, two_at = branches(two_class, 1)
        self.three_branches, three_at = branches(three_class, 2)
        self.flags = dict(
            one_class=one_class, two_class=two_class, three_class=three_class,
            one_at=one_at, two_at=two_at, three_at=three_at,
            a=[offsets(*pair)[0] for pair in PAIRS], big_a=[offsets(*pair)[1] for pair in PAIRS],
        )

        found = {}
        for n, (come, ahead, back, fine, coarse, quarters, one, two, three, four) in enumerate(cases):

            def send(exchanged, room):
                return [n for (numbers, _), size in zip(exchanged, room) for n in numbers + [-1] * (size - len(numbers))]

            def source(held, *exchanges):
                places = list(held)
                for exchanged, room in exchanges:
                    for (_, got), size in zip(exchanged, room):
                        places += got + [None] * (size - len(got))
                return {p: n for n, p in enumerate(places) if p is not None}

            w = three_class[n]
            first, second = source(block, (one, self.one[-1])), source(fine, (two, self.two[-1]))
            third = source(coarse, (three, self.three[w]))
            last = source(fine, (two, self.two[-1]), (four, self.four[w]))
            out = [(l, r, c) for r in range(crows) for c in range(ccols) for l in range(2)]
            rows_of = dict(
                send_one=send(one, self.one[one_class[n]]),
                take_one=[first[p] for p in fine],
                send_two=send(two, self.two[two_class[n]]),
                take_two=[second[p] for p in quarters],
                send_three=send(three, self.three[w]),
                send_four=send(four, self.four[w]),
                fine_out=[last[p] for p in block],
                coarse_out=[third[p] for p in out],
            )
            for name, row in rows_of.items():
                found.setdefault(name, []).append(row)
        parts, self.at, top = [], {}, 0
        for name, lists in found.items():
            length = -(-max(len(row) for row in lists) // 128)
            part = np.full((len(PAIRS), length * 128), -1, np.float32)
            for n, row in enumerate(lists):
                part[n, : len(row)] = row
            parts.append(part.reshape(len(PAIRS), length, 128))
            self.at[name] = (top, length)
            top += length
        parts.append(np.zeros((len(PAIRS), -top % 8, 128), np.float32))
        self.table = np.concatenate(parts, axis=1)


def case_of(shifts_ref):
    t0, t1 = shifts_ref[0], shifts_ref[1]
    return jnp.where(t0 == WH - 1, t1 - 1, t0 + WH - 2)


def lookup(values, case):
    out = jnp.int32(values[0])
    for n, value in enumerate(values[1:], 1):
        out = jnp.where(case == n, value, out)
    return out


def columns_of(rows, count):
    parts = [jnp.broadcast_to(rows[j : j + 1], (128, 128)).T for j in range(-(-count // 128))]
    return stack_rows(parts)[:count]


def select_rows(index, source):
    lane = lax.broadcasted_iota(I32, (1, 128), 1).astype(F32)
    size = source.shape[0]
    pick = [jnp.where(index == lane + float(at), 1.0, 0.0).astype(BF16) for at in range(0, size, 128)]
    pick = jnp.concatenate(pick, axis=1)[:, :size]
    return jnp.dot(pick, source, preferred_element_type=F32)


def stack_rows(parts):
    return parts[0] if len(parts) == 1 else jnp.concatenate(parts, axis=0)


def layer_norm(values):
    center = jnp.mean(values, axis=-1, keepdims=True)
    values = values - center
    spread = jnp.mean(values * values, axis=-1, keepdims=True)
    return values * lax.rsqrt(spread + EPS)


def attend_windows(qkv_of, id_of, windows, inner, finish):
    lane = lax.broadcasted_iota(I32, (1, 128), 1)
    forbid = jnp.where(lane < 8, BIG, 0.0).astype(BF16)
    groups = inner // 128
    units = [(w, g) for w in range(windows) for g in range(groups)]
    scores, weights, outs = {}, {}, {}

    def score(w, g):
        key_id = id_of(w)
        not_id = (key_id - 1).astype(BF16) * forbid
        q = qkv_of(w, g * 128)
        keys = jnp.concatenate([qkv_of(w, inner + g * 128), key_id], axis=1)
        queries = []
        for h in range(4):
            mine = jnp.where((lane >= h * HD) & (lane < (h + 1) * HD), 1.0, 0.0).astype(BF16)
            queries.append(jnp.concatenate([q * mine, not_id], axis=1))
        scores[w, g] = lax.dot_general(keys, stack_rows(queries), NT, preferred_element_type=F32)

    def soften(w, g):
        s = scores.pop((w, g))
        weight = jnp.exp2((s - jnp.max(s, axis=0, keepdims=True)) * SCALE)
        weights[w, g] = weight.astype(BF16), 1.0 / jnp.sum(weight, axis=0, keepdims=True)

    def gather(w, g):
        weight, scale = weights.pop((w, g))
        out = lax.dot_general(qkv_of(w, 2 * inner + g * 128), weight, TN, preferred_element_type=F32) * scale
        outs[w, g] = [out[h * HD : (h + 1) * HD, h * TOK : (h + 1) * TOK] for h in range(4)]
        if g == groups - 1:
            finish(w, stack_rows([part for k in range(groups) for part in outs.pop((w, k))]).astype(BF16))

    for n in range(len(units) + 2):
        if n < len(units):
            score(*units[n])
        if 0 <= n - 1 < len(units):
            soften(*units[n - 1])
        if 0 <= n - 2 < len(units):
            gather(*units[n - 2])


ANY = pl.BlockSpec(memory_space=pl.ANY)
HBM = pl.BlockSpec(memory_space=pltpu.HBM)
VMEM = pl.BlockSpec(memory_space=pltpu.VMEM)
SMEM = pl.BlockSpec(memory_space=pltpu.SMEM)


def call(body, outs, out_specs, shifts, args, in_specs, scratch, copies, flops, moved_bytes, vmem=32):
    return pl.pallas_call(
        body,
        out_shape=outs,
        in_specs=[SMEM] + in_specs,
        out_specs=out_specs,
        scratch_shapes=list(scratch) + [pltpu.SemaphoreType.DMA((copies,))],
        compiler_params=pltpu.CompilerParams(vmem_limit_bytes=vmem << 20),
        cost_estimate=pl.CostEstimate(flops=flops, bytes_accessed=moved_bytes, transcendentals=0),
    )(shifts, *args)


def shapes(sizes, width):
    return [jax.ShapeDtypeStruct((n, width), BF16) for n in sizes]


class Copies:
    def __init__(self, sems):
        self.sems, self.used = sems, 0

    def __call__(self, src, dst):
        copy = pltpu.make_async_copy(src, dst, self.sems.at[self.used])
        self.used += 1
        copy.start()
        return copy


class Pieces:
    def __init__(self, refs, sizes, which, source, own, sems, sem_at):
        self.parts = []
        room = sizes[-1]
        for n, size in enumerate(sizes):
            at, copies, blank = own, [], []
            for k in range(3):
                copies.append((refs[3 * n + k], source.at[pl.ds(at, size[k])], sems.at[sem_at + k]))
                if size[k] < room[k]:
                    blank.append((at + size[k], room[k] - size[k]))
                at += room[k]
            self.parts.append((copies, blank))
        self.which, self.source = which, source
        for n, (copies, blank) in enumerate(self.parts):

            @pl.when(which == n)
            def _():
                for copy in copies:
                    pltpu.make_async_copy(*copy).start()
                for at, rows in blank:
                    source[at : at + rows, :] = jnp.zeros((rows, source.shape[1]), source.dtype)

    def wait(self):
        for n, (copies, _) in enumerate(self.parts):

            @pl.when(self.which == n)
            def _():
                for copy in copies:
                    pltpu.make_async_copy(*copy).wait()


def flat(ref):
    layers, rows, cols, width = ref.shape
    return ref[...].astype(F32).reshape(layers * rows * cols, width).astype(BF16)


def put_pieces(value, refs):
    at = 0
    for ref in refs:
        ref[...] = value[at : at + ref.shape[0]].astype(BF16)
        at += ref.shape[0]


def rows_of(plan, table_ref, name):
    top, length = plan.at[name]
    return table_ref[top : top + length, :]


def send_classes(plan, table_ref, name, source_ref, sizes, which, refs):
    for n, size in enumerate(sizes):

        @pl.when(which == n)
        def _():
            index = columns_of(rows_of(plan, table_ref, name), sum(size))
            put_pieces(select_rows(index, source_ref[...]), refs[3 * n : 3 * n + 3])


def exchange(pieces, sign):
    lat, lon = lax.axis_size("lat"), lax.axis_size("lon")
    row, col, both = pieces
    pairs = [((i + sign) % lat * lon + (j + sign) % lon, i * lon + j) for i in range(lat) for j in range(lon)]
    col = lax.ppermute(col, "lon", [((j + sign) % lon, j) for j in range(lon)])
    both = lax.ppermute(both, ("lat", "lon"), pairs)
    row = lax.ppermute(row, "lat", [((i + sign) % lat, i) for i in range(lat)])
    return [row, col, both]


def unused(like):
    return pl.pallas_call(
        lambda *refs: None,
        out_shape=[jax.ShapeDtypeStruct(x.shape, x.dtype) for x in like],
        out_specs=[ANY] * len(like),
    )()


def exchange_class(sent, which, sign):
    got = []
    for n in range(len(sent) // 3):
        mine = sent[3 * n : 3 * n + 3]
        got += exchange(mine, sign) if n == which else unused(mine)
    return got


def first_pieces(shifts, tokens, plan):
    width = tokens.shape[-1]
    sizes = plan.one

    def body(shifts_ref, tokens_ref, table_ref, *refs):
        outs, flags = refs[: 3 * len(sizes)], refs[3 * len(sizes) : 3 * len(sizes) + 3]
        held_ref, rows_ref, source_ref, sems = refs[3 * len(sizes) + 3 :]
        case = case_of(shifts_ref)
        start = Copies(sems)
        held = start(tokens_ref, held_ref)
        rows = start(table_ref.at[case], rows_ref)
        for ref, name in zip(flags, ("one_at", "two_at", "three_at")):
            ref[0] = lookup(plan.flags[name], case)
        rows.wait()
        held.wait()
        source_ref[...] = flat(held_ref)
        which = lookup(plan.flags["one_class"], case)
        send_classes(plan, rows_ref, "send_one", source_ref, sizes, which, outs)

    outs = [shape for size in sizes for shape in shapes(size, width)]
    specs = [VMEM] * len(outs) + [SMEM] * 3
    outs += [jax.ShapeDtypeStruct((1,), I32)] * 3
    scratch = [
        pltpu.VMEM(tokens.shape, BF16),
        pltpu.VMEM(plan.table.shape[1:], F32),
        pltpu.VMEM((tokens.size // width, width), BF16),
    ]
    *sent, one, two, three = call(
        body, outs, specs, shifts, [tokens, plan.table], [HBM, HBM], scratch, 2, 1 << 28, 1 << 20
    )
    return sent, one[0], two[0], three[0]


def id_kernel(shifts, regions, plan, rows, cols):
    _, lat, lon = regions.shape
    flat_regions = regions.reshape(2 * lat, lon)
    fine, coarse = windowed(rows, cols), natural(rows // 2, cols // 2)
    places = np.asarray(fine + coarse, np.float32)
    places[len(fine) :, 1:] *= 2
    pad = -len(places) % 128
    places = np.pad(places, ((0, pad), (0, 0))).T.reshape(3, -1, 128)
    is_fine = np.pad(np.ones(len(fine), np.float32), (0, len(coarse) + pad)).reshape(1, -1, 128)
    places = np.concatenate([places, is_fine])
    count = len(fine) + len(coarse)

    def body(shifts_ref, regions_hbm, places_hbm, fine_ref, coarse_ref, regions_ref, places_ref, sems):
        case = case_of(shifts_ref)
        start = Copies(sems)
        waits = [start(regions_hbm, regions_ref), start(places_hbm, places_ref)]
        for copy in waits:
            copy.wait()
        a = lookup(plan.flags["a"], case).astype(F32)
        big_a = 2.0 * lookup(plan.flags["big_a"], case).astype(F32)
        is_fine = places_ref[3]
        d = is_fine * a + (1.0 - is_fine) * big_a
        row = places_ref[1] + d + (lax.axis_index("lat") * rows).astype(F32)
        col = places_ref[2] + 2.0 * d + (lax.axis_index("lon") * cols).astype(F32)
        wrapped = jnp.where((row < 0) | (row >= lat), 4.0, 0.0)
        row = jnp.where(row < 0, row + lat, jnp.where(row >= lat, row - lat, row))
        col = jnp.where(col < 0, col + lon, jnp.where(col >= lon, col - lon, col))
        row = columns_of(row + places_ref[0] * lat, count)
        col = columns_of(col, count)
        wrapped = columns_of(wrapped, count)
        picked = select_rows(row, regions_ref[...].astype(F32).astype(BF16))
        ids = jnp.zeros((count, 128), F32)
        for at in range(0, lon, 128):
            width = min(128, lon - at)
            lane = lax.broadcasted_iota(I32, (1, width), 1).astype(F32) + float(at)
            here = jnp.where(lane == col[:, :width], picked[:, at : at + width], 0.0)
            ids = ids + jnp.sum(here, axis=1, keepdims=True)
        lane = lax.broadcasted_iota(I32, (1, 128), 1).astype(F32)
        hot = jnp.where(lane == ids + wrapped, 1.0, 0.0).astype(BF16)
        fine_ref[...] = hot[: len(fine)]
        coarse_ref[...] = hot[len(fine) :]

    outs = shapes([len(fine), len(coarse)], 128)
    scratch = [pltpu.VMEM(flat_regions.shape, I32), pltpu.VMEM(places.shape, F32)]
    return call(
        body, outs, [VMEM] * 2, shifts, [flat_regions, places], [HBM] * 2, scratch, 2, 1 << 28, 4 << 20
    )


def fine_level(shifts, tokens, pieces, key_id, w_qkv, w_proj, plan):
    _, rows, cols, width = tokens.shape
    count = 2 * rows * cols
    inner = w_proj.shape[0]
    kinds = 3 * len(plan.two)

    def body(shifts_ref, tokens_hbm, *refs):
        piece_refs, refs = refs[: len(pieces)], refs[len(pieces) :]
        id_hbm, qkv_w_hbm, proj_w_hbm, table_ref, out_hbm, *refs = refs
        piece_outs, refs = refs[:kinds], refs[kinds:]
        tokens_ref, source_ref, id_ref, qkv_w_ref, proj_w_ref, rows_ref, x_ref, qkv_ref, out_ref, sems = refs
        case = case_of(shifts_ref)
        start = Copies(sems)
        held = start(tokens_hbm, tokens_ref)
        index = start(table_ref.at[case], rows_ref)
        got = Pieces(piece_refs, plan.one, lookup(plan.flags["one_class"], case), source_ref, count, sems, 12)
        qkv_w, proj_w, ids = start(qkv_w_hbm, qkv_w_ref), start(proj_w_hbm, proj_w_ref), start(id_hbm, id_ref)
        index.wait()
        take = columns_of(rows_of(plan, rows_ref, "take_one"), count)
        held.wait()
        source_ref[:count, :] = flat(tokens_ref)
        got.wait()
        x = select_rows(take, source_ref[...])
        x_ref[...] = x
        normed = layer_norm(x).astype(BF16)
        qkv_w.wait()
        qkv_ref[...] = jnp.dot(normed, qkv_w_ref[...], preferred_element_type=F32).astype(BF16)
        proj_w.wait()
        ids.wait()
        leave = []

        def finish(w, out):
            at = slice(w * TOK, (w + 1) * TOK)
            out = lax.dot_general(out, proj_w_ref[...], TN, preferred_element_type=F32)
            out_ref[at, :] = (x_ref[at, :] + out).astype(BF16)
            leave.append(start(out_ref.at[pl.ds(w * TOK, TOK)], out_hbm.at[pl.ds(w * TOK, TOK)]))

        attend_windows(
            lambda w, at: qkv_ref[w * TOK : (w + 1) * TOK, at : at + 128],
            lambda w: id_ref[w * TOK : (w + 1) * TOK, :],
            count // TOK,
            inner,
            finish,
        )
        which = lookup(plan.flags["two_class"], case)
        send_classes(plan, rows_ref, "send_two", out_ref, plan.two, which, piece_outs)
        for copy in leave:
            copy.wait()

    outs = shapes([count], width) + [shape for size in plan.two for shape in shapes(size, width)]
    specs = [HBM] + [VMEM] * kinds
    scratch = [
        pltpu.VMEM(tokens.shape, BF16),
        pltpu.VMEM((count + sum(plan.one[-1]), width), BF16),
        pltpu.VMEM(key_id.shape, BF16),
        pltpu.VMEM(w_qkv.shape, BF16),
        pltpu.VMEM(w_proj.shape, BF16),
        pltpu.VMEM(plan.table.shape[1:], F32),
        pltpu.VMEM((count, width), F32),
        pltpu.VMEM((count, 3 * inner), BF16),
        pltpu.VMEM((count, width), BF16),
    ]
    args = [tokens, *pieces, key_id, w_qkv, w_proj, plan.table]
    in_specs = [HBM] + [ANY] * (len(pieces) + 1) + [HBM] * 3
    assert 5 + count // TOK <= 16
    out, *sent = call(body, outs, specs, shifts, args, in_specs, scratch, 16, 3 << 30, 6 << 20)
    return out, sent


def coarse_level(shifts, fine, pieces, key_id, w_merge, w_qkv, w_proj, plan):
    count = key_id.shape[0]
    width = w_merge.shape[1]
    own, half = fine.shape
    inner = w_proj.shape[0]
    kinds = 3 * len(plan.three)
    step = w_merge.shape[0] // 4

    def body(shifts_ref, fine_hbm, *refs):
        piece_refs, refs = refs[: len(pieces)], refs[len(pieces) :]
        id_hbm, merge_hbm, qkv_w_hbm, proj_w_hbm, table_ref, out_hbm, *refs = refs
        piece_outs, refs = refs[:kinds], refs[kinds:]
        source_ref, id_ref, merge_ref, qkv_w_ref, proj_w_ref, rows_ref, qkv_ref, out_ref, sems = refs
        case = case_of(shifts_ref)
        start = Copies(sems)
        index = start(table_ref.at[case], rows_ref)
        held = start(fine_hbm, source_ref.at[pl.ds(0, own)])
        got = Pieces(piece_refs, plan.two, lookup(plan.flags["two_class"], case), source_ref, own, sems, 12)
        merge_w = [
            start(merge_hbm.at[pl.ds(n * step, step)], merge_ref.at[pl.ds(n * step, step)]) for n in range(4)
        ]
        qkv_w, proj_w, ids = start(qkv_w_hbm, qkv_w_ref), start(proj_w_hbm, proj_w_ref), start(id_hbm, id_ref)
        index.wait()
        take = columns_of(rows_of(plan, rows_ref, "take_two"), 4 * count)
        held.wait()
        got.wait()
        x = select_rows(take, source_ref[...])
        x = jnp.concatenate([x[n * count : (n + 1) * count] for n in range(4)], axis=1)
        stacked = layer_norm(x).astype(BF16)
        for copy in merge_w:
            copy.wait()
        merged = jnp.dot(stacked, merge_ref[...], preferred_element_type=F32).astype(BF16).astype(F32)
        normed = layer_norm(merged).astype(BF16)
        qkv_w.wait()
        qkv_ref[...] = jnp.dot(normed, qkv_w_ref[...], preferred_element_type=F32).astype(BF16)
        ids.wait()
        proj_w.wait()

        def finish(w, out):
            out = lax.dot_general(out, proj_w_ref[...], TN, preferred_element_type=F32)
            out_ref[...] = (merged + out).astype(BF16)

        attend_windows(lambda w, at: qkv_ref[:, at : at + 128], lambda w: id_ref[...], 1, inner, finish)
        leave = start(out_ref, out_hbm)
        which = lookup(plan.flags["three_class"], case)
        for n, (sizes, fine_sizes) in enumerate(zip(plan.three, plan.four)):

            @pl.when(which == n)
            def _():
                sent = select_rows(columns_of(rows_of(plan, rows_ref, "send_three"), sum(sizes)), out_ref[...])
                sent = sent.astype(BF16)
                at = 0
                for ref, size in zip(piece_outs[3 * n :], sizes):
                    ref[:size, :] = sent[at : at + size, :half]
                    ref[size : 2 * size, :] = sent[at : at + size, half:]
                    at += size
                if sum(fine_sizes):
                    index = columns_of(rows_of(plan, rows_ref, "send_four"), sum(fine_sizes))
                    sent = select_rows(index, source_ref[:own, :]).astype(BF16)
                    at = 0
                    for ref, size, more in zip(piece_outs[3 * n :], sizes, fine_sizes):
                        ref[2 * size :, :] = sent[at : at + more]
                        at += more

        leave.wait()

    outs = shapes([count], width)
    for sizes, fine_sizes in zip(plan.three, plan.four):
        outs += shapes([2 * n + m for n, m in zip(sizes, fine_sizes)], half)
    specs = [HBM] + [VMEM] * kinds
    scratch = [
        pltpu.VMEM((own + sum(plan.two[-1]), half), BF16),
        pltpu.VMEM(key_id.shape, BF16),
        pltpu.VMEM(w_merge.shape, BF16),
        pltpu.VMEM(w_qkv.shape, BF16),
        pltpu.VMEM(w_proj.shape, BF16),
        pltpu.VMEM(plan.table.shape[1:], F32),
        pltpu.VMEM((count, 3 * inner), BF16),
        pltpu.VMEM((count, width), BF16),
    ]
    args = [fine, *pieces, key_id, w_merge, w_qkv, w_proj, plan.table]
    in_specs = [HBM] + [ANY] * (len(pieces) + 1) + [HBM] * 4
    out, *sent = call(body, outs, specs, shifts, args, in_specs, scratch, 16, 3 << 30, 12 << 20)
    return out, sent


def fine_output(shifts, fine, pieces, got, which, plan, rows, cols):
    own, width = fine.shape
    room = sum(plan.two[-1])
    extra = plan.four[which]

    def body(shifts_ref, fine_hbm, *refs):
        piece_refs, refs = refs[: len(pieces)], refs[len(pieces) :]
        got_refs, refs = refs[: len(got)], refs[len(got) :]
        table_ref, out_ref, source_ref, rows_ref, sems = refs
        case = case_of(shifts_ref)
        start = Copies(sems)
        waits = [start(table_ref.at[case], rows_ref), start(fine_hbm, source_ref.at[pl.ds(0, own)])]
        at = own + room
        for ref, size, more in zip(got_refs, plan.three[which], extra):
            waits.append(start(ref.at[pl.ds(2 * size, more)], source_ref.at[pl.ds(at, more)]))
            at += more
        pieces_in = Pieces(piece_refs, plan.two, lookup(plan.flags["two_class"], case), source_ref, own, sems, 8)
        for copy in waits:
            copy.wait()
        take = columns_of(rows_of(plan, rows_ref, "fine_out"), own)
        pieces_in.wait()
        out = select_rows(take, source_ref[...])
        out_ref[...] = out.reshape(2, rows, cols, width).astype(BF16)

    outs = [jax.ShapeDtypeStruct((2, rows, cols, width), BF16)]
    scratch = [
        pltpu.VMEM((own + room + (sum(extra) if got else 0), width), BF16),
        pltpu.VMEM(plan.table.shape[1:], F32),
    ]
    args = [fine, *pieces, *got, plan.table]
    in_specs = [HBM] + [ANY] * (len(pieces) + len(got)) + [HBM]
    return call(body, outs, [VMEM], shifts, args, in_specs, scratch, 16, 1 << 30, 4 << 20)[0]


def coarse_output(shifts, coarse, got, which, plan, rows, cols):
    own, width = coarse.shape
    half = width // 2
    sizes = plan.three[which]

    def body(shifts_ref, coarse_hbm, *refs):
        got_refs, (table_ref, out_ref, source_ref, rows_ref, sems) = refs[:3], refs[3:]
        start = Copies(sems)
        waits = [start(table_ref.at[case_of(shifts_ref)], rows_ref), start(coarse_hbm, source_ref.at[pl.ds(0, own)])]
        at = own
        for ref, size in zip(got_refs, sizes):
            for n in range(2):
                to = source_ref.at[pl.ds(at, size), pl.ds(n * half, half)]
                waits.append(start(ref.at[pl.ds(n * size, size)], to))
            at += size
        for copy in waits:
            copy.wait()
        take = columns_of(rows_of(plan, rows_ref, "coarse_out"), own)
        out = select_rows(take, source_ref[...]).astype(BF16)
        for n in range(own // 2):
            out_ref[n // cols, n % cols] = out[2 * n : 2 * n + 2]

    outs = [jax.ShapeDtypeStruct((rows, cols, 2, width), BF16)]
    scratch = [pltpu.VMEM((own + sum(sizes), width), BF16), pltpu.VMEM(plan.table.shape[1:], F32)]
    args = [coarse, *got, plan.table]
    out = call(body, outs, [VMEM], shifts, args, [HBM] + [ANY] * 3 + [HBM], scratch, 8, 1 << 28, 1 << 20)[0]
    return out.transpose(2, 0, 1, 3)


def on_device(tokens, regions, shifts, fine_qkv, fine_proj, merge_weight, coarse_qkv, coarse_proj):
    _, rows, cols, _ = tokens.shape
    plan = Plan(rows, cols)

    def first(which, sign, sent, shifts, regions):
        got = exchange_class(sent, which, sign)
        return got, id_kernel(shifts, regions, plan, rows, cols)

    def second(which, sign, sent):
        return exchange_class(sent, which, sign)

    def third(which, sign, sent, shifts, fine, pieces, coarse):
        got = exchange(sent[3 * which : 3 * which + 3], sign)
        fine_out = fine_output(shifts, fine, pieces, got if which else [], which, plan, rows, cols)
        return fine_out, coarse_output(shifts, coarse, got, which, plan, rows // 2, cols // 2)

    def branches(stage, pairs):
        return [functools.partial(stage, which, sign) for which, sign in pairs]

    sent, one, two, three = first_pieces(shifts, tokens, plan)
    got, (fine_id, coarse_id) = lax.switch(one, branches(first, plan.one_branches), sent, shifts, regions)
    fine, sent = fine_level(shifts, tokens, got, fine_id, fine_qkv, fine_proj, plan)
    got = lax.switch(two, branches(second, plan.two_branches), sent)
    coarse, sent = coarse_level(
        shifts, fine, got, coarse_id, merge_weight, coarse_qkv, coarse_proj, plan
    )
    return lax.switch(three, branches(third, plan.three_branches), sent, shifts, fine, got, coarse)


def solution(mesh):
    return jax.shard_map(
        on_device,
        mesh=mesh,
        in_specs=(P(None, "lat", "lon", None), P(), P(), P(), P(), P(), P(), P()),
        out_specs=(P(None, "lat", "lon", None), P(None, "lat", "lon", None)),
        check_vma=False,
    )
```

```python
import functools

import jax
import jax.numpy as jnp
import numpy as np
from jax import lax
from jax.experimental import pallas as pl
from jax.experimental.pallas import tpu as pltpu
from jax.sharding import PartitionSpec as P

HD = 32
WH = 6
WW = 12
TOK = 2 * WH * WW
EPS = 1e-05
BIG = 1e30
SCALE = float(np.log2(np.e) / np.sqrt(HD))

NT = (((1,), (1,)), ((), ()))
TN = (((0,), (0,)), ((), ()))
F32 = jnp.float32
BF16 = jnp.bfloat16
I32 = jnp.int32

PAIRS = [(WH - 1, t) for t in range(1, WH)] + [(t, WH - 1) for t in range(1, WH - 1)]


def up16(count):
    return -(-count // 16) * 16


def natural(rows, cols):
    return [(l, r, c) for l in range(2) for r in range(rows) for c in range(cols)]


def windowed(rows, cols):
    return [
        (l, wr * WH + r, wc * WW + c)
        for wr in range(rows // WH)
        for wc in range(cols // WW)
        for l in range(2)
        for r in range(WH)
        for c in range(WW)
    ]


def moved(order, d):
    return [(l, r + d, c + 2 * d) for l, r, c in order]


def exchange_places(held, wanted, rows, cols, sign):
    at = {place: n for n, place in enumerate(held)}
    found = []
    for dr, dc in ((sign, 0), (0, sign), (sign, sign)):
        numbers, places = [], []
        for l, r, c in sorted(set(wanted) - set(held)):
            n = at.get((l, r - dr * rows, c - dc * cols))
            if n is not None:
                numbers.append(n)
                places.append((l, r, c))
        found.append((numbers, places))
    return found


def offsets(t0, t1):
    a = t0 if t0 <= 2 else t0 - WH
    big_a = t1 if t1 <= 2 else t1 - WH
    ahead = 1 if 2 * big_a > a or 2 * big_a - a == 0 and a < 0 else -1
    return a, big_a, ahead


def classes_of(needs, limits):
    which = [next(n for n, limit in enumerate(limits) if need[1] <= limit) for need in needs]
    sizes = [
        [up16(max(need[k] for need, w in zip(needs, which) if w == n)) for k in range(3)]
        for n in range(len(limits))
    ]
    return sizes, which


class Plan:
    def __init__(self, rows, cols):
        crows, ccols = rows // 2, cols // 2
        block, cblock = natural(rows, cols), natural(crows, ccols)
        cases = []
        for t0, t1 in PAIRS:
            a, big_a, ahead = offsets(t0, t1)
            fine = moved(windowed(rows, cols), a)
            coarse = moved(cblock, big_a)
            quarters = [
                (l, 2 * r + dr, 2 * c + dc)
                for dr, dc in ((0, 0), (1, 0), (0, 1), (1, 1))
                for l, r, c in coarse
            ]
            come = 1 if a > 0 else -1
            one = exchange_places(block, fine, rows, cols, come)
            home = [p for p in block if p not in set(fine)]
            wanted = quarters + (home if come == -ahead else [])
            two = exchange_places(fine, wanted, rows, cols, ahead)
            back = 1 if big_a < 0 else -1
            three = exchange_places(coarse, cblock, crows, ccols, back)
            got = set(fine).union(*[places for _, places in two])
            four = exchange_places(fine, [p for p in block if p not in got], rows, cols, back)
            cases.append((come, ahead, back, fine, coarse, quarters, one, two, three, four))

        def needs(which):
            return [[len(numbers) for numbers, _ in case[which]] for case in cases]

        self.one, one_class = classes_of(needs(6), [64, 512])
        self.two, two_class = classes_of(needs(7), [64, 128, 512])
        fine_back = [max(need) > 0 for need in needs(9)]
        self.three = []
        self.four = []
        for with_fine in (False, True):
            inside = [n for n, flag in enumerate(fine_back) if flag == with_fine]
            self.three.append([up16(max(needs(8)[n][k] for n in inside)) for k in range(3)])
            self.four.append([up16(max(needs(9)[n][k] for n in inside)) for k in range(3)])
        three_class = [int(flag) for flag in fine_back]

        def branches(which_class, direction):
            pairs = [(n, case[direction]) for n, case in zip(which_class, cases)]
            found = sorted(set(pairs))
            return found, [found.index(pair) for pair in pairs]

        self.one_branches, one_at = branches(one_class, 0)
        self.two_branches, two_at = branches(two_class, 1)
        self.three_branches, three_at = branches(three_class, 2)
        self.flags = dict(
            one_class=one_class, two_class=two_class, three_class=three_class,
            one_at=one_at, two_at=two_at, three_at=three_at,
            a=[offsets(*pair)[0] for pair in PAIRS], big_a=[offsets(*pair)[1] for pair in PAIRS],
        )

        found = {}
        for n, (come, ahead, back, fine, coarse, quarters, one, two, three, four) in enumerate(cases):

            def send(exchanged, room):
                return [n for (numbers, _), size in zip(exchanged, room) for n in numbers + [-1] * (size - len(numbers))]

            def source(held, *exchanges):
                places = list(held)
                for exchanged, room in exchanges:
                    for (_, got), size in zip(exchanged, room):
                        places += got + [None] * (size - len(got))
                return {p: n for n, p in enumerate(places) if p is not None}

            w = three_class[n]
            first, second = source(block, (one, self.one[-1])), source(fine, (two, self.two[-1]))
            third = source(coarse, (three, self.three[w]))
            last = source(fine, (two, self.two[-1]), (four, self.four[w]))
            out = [(l, r, c) for r in range(crows) for c in range(ccols) for l in range(2)]
            rows_of = dict(
                send_one=send(one, self.one[one_class[n]]),
                take_one=[first[p] for p in fine],
                send_two=send(two, self.two[two_class[n]]),
                take_two=[second[p] for p in quarters],
                send_three=send(three, self.three[w]),
                send_four=send(four, self.four[w]),
                fine_out=[last[p] for p in block],
                coarse_out=[third[p] for p in out],
            )
            for name, row in rows_of.items():
                found.setdefault(name, []).append(row)
        parts, self.at, top = [], {}, 0
        for name, lists in found.items():
            length = -(-max(len(row) for row in lists) // 128)
            part = np.full((len(PAIRS), length * 128), -1, np.float32)
            for n, row in enumerate(lists):
                part[n, : len(row)] = row
            parts.append(part.reshape(len(PAIRS), length, 128))
            self.at[name] = (top, length)
            top += length
        parts.append(np.zeros((len(PAIRS), -top % 8, 128), np.float32))
        self.table = np.concatenate(parts, axis=1)


def case_of(shifts_ref):
    t0, t1 = shifts_ref[0], shifts_ref[1]
    return jnp.where(t0 == WH - 1, t1 - 1, t0 + WH - 2)


def lookup(values, case):
    out = jnp.int32(values[0])
    for n, value in enumerate(values[1:], 1):
        out = jnp.where(case == n, value, out)
    return out


def columns_of(rows, count):
    parts = [jnp.broadcast_to(rows[j : j + 1], (128, 128)).T for j in range(-(-count // 128))]
    return stack_rows(parts)[:count]


def select_rows(index, source):
    lane = lax.broadcasted_iota(I32, (1, 128), 1).astype(F32)
    size = source.shape[0]
    pick = [jnp.where(index == lane + float(at), 1.0, 0.0).astype(BF16) for at in range(0, size, 128)]
    pick = jnp.concatenate(pick, axis=1)[:, :size]
    return jnp.dot(pick, source, preferred_element_type=F32)


def stack_rows(parts):
    return parts[0] if len(parts) == 1 else jnp.concatenate(parts, axis=0)


def layer_norm(values):
    center = jnp.mean(values, axis=-1, keepdims=True)
    values = values - center
    spread = jnp.mean(values * values, axis=-1, keepdims=True)
    return values * lax.rsqrt(spread + EPS)


def attend_windows(qkv_of, id_of, windows, inner, finish):
    lane = lax.broadcasted_iota(I32, (1, 128), 1)
    forbid = jnp.where(lane < 8, BIG, 0.0).astype(BF16)
    groups = inner // 128
    units = [(w, g) for w in range(windows) for g in range(groups)]
    scores, weights, outs = {}, {}, {}

    def score(w, g):
        key_id = id_of(w)
        not_id = (key_id - 1).astype(BF16) * forbid
        q = qkv_of(w, g * 128)
        keys = jnp.concatenate([qkv_of(w, inner + g * 128), key_id], axis=1)
        queries = []
        for h in range(4):
            mine = jnp.where((lane >= h * HD) & (lane < (h + 1) * HD), 1.0, 0.0).astype(BF16)
            queries.append(jnp.concatenate([q * mine, not_id], axis=1))
        scores[w, g] = lax.dot_general(keys, stack_rows(queries), NT, preferred_element_type=F32)

    def soften(w, g):
        s = scores.pop((w, g))
        weight = jnp.exp2((s - jnp.max(s, axis=0, keepdims=True)) * SCALE)
        weights[w, g] = weight.astype(BF16), 1.0 / jnp.sum(weight, axis=0, keepdims=True)

    def gather(w, g):
        weight, scale = weights.pop((w, g))
        out = lax.dot_general(qkv_of(w, 2 * inner + g * 128), weight, TN, preferred_element_type=F32) * scale
        outs[w, g] = [out[h * HD : (h + 1) * HD, h * TOK : (h + 1) * TOK] for h in range(4)]
        if g == groups - 1:
            finish(w, stack_rows([part for k in range(groups) for part in outs.pop((w, k))]).astype(BF16))

    for n in range(len(units) + 2):
        if n < len(units):
            score(*units[n])
        if 0 <= n - 1 < len(units):
            soften(*units[n - 1])
        if 0 <= n - 2 < len(units):
            gather(*units[n - 2])


ANY = pl.BlockSpec(memory_space=pl.ANY)
HBM = pl.BlockSpec(memory_space=pltpu.HBM)
VMEM = pl.BlockSpec(memory_space=pltpu.VMEM)
SMEM = pl.BlockSpec(memory_space=pltpu.SMEM)


def call(body, outs, out_specs, shifts, args, in_specs, scratch, copies, flops, moved_bytes, vmem=32):
    args = [
        pltpu.with_memory_space_constraint(arg, pltpu.HBM) if spec is HBM else arg for arg, spec in zip(args, in_specs)
    ]
    return pl.pallas_call(
        body,
        out_shape=outs,
        in_specs=[SMEM] + in_specs,
        out_specs=out_specs,
        scratch_shapes=list(scratch) + [pltpu.SemaphoreType.DMA((copies,))],
        compiler_params=pltpu.CompilerParams(vmem_limit_bytes=vmem << 20),
        cost_estimate=pl.CostEstimate(flops=flops, bytes_accessed=moved_bytes, transcendentals=0),
    )(shifts, *args)


def shapes(sizes, width, space=pltpu.VMEM):
    return [space((n, width), BF16) for n in sizes]


class Copies:
    def __init__(self, sems):
        self.sems, self.used = sems, 0

    def __call__(self, src, dst):
        copy = pltpu.make_async_copy(src, dst, self.sems.at[self.used])
        self.used += 1
        copy.start()
        return copy


class Pieces:
    def __init__(self, refs, sizes, which, source, own, sems, sem_at):
        self.parts = []
        room = sizes[-1]
        for n, size in enumerate(sizes):
            at, copies, blank = own, [], []
            for k in range(3):
                copies.append((refs[3 * n + k], source.at[pl.ds(at, size[k])], sems.at[sem_at + k]))
                if size[k] < room[k]:
                    blank.append((at + size[k], room[k] - size[k]))
                at += room[k]
            self.parts.append((copies, blank))
        self.which, self.source = which, source
        for n, (copies, blank) in enumerate(self.parts):

            @pl.when(which == n)
            def _():
                for copy in copies:
                    pltpu.make_async_copy(*copy).start()
                for at, rows in blank:
                    source[at : at + rows, :] = jnp.zeros((rows, source.shape[1]), source.dtype)

    def wait(self):
        for n, (copies, _) in enumerate(self.parts):

            @pl.when(self.which == n)
            def _():
                for copy in copies:
                    pltpu.make_async_copy(*copy).wait()


def flat(ref):
    layers, rows, cols, width = ref.shape
    return ref[...].astype(F32).reshape(layers * rows * cols, width).astype(BF16)


def put_pieces(value, refs):
    at = 0
    for ref in refs:
        ref[...] = value[at : at + ref.shape[0]].astype(BF16)
        at += ref.shape[0]


def rows_of(plan, table_ref, name):
    top, length = plan.at[name]
    return table_ref[top : top + length, :]


def send_classes(plan, table_ref, name, source_ref, sizes, which, refs):
    for n, size in enumerate(sizes):

        @pl.when(which == n)
        def _():
            index = columns_of(rows_of(plan, table_ref, name), sum(size))
            put_pieces(select_rows(index, source_ref[...]), refs[3 * n : 3 * n + 3])


def exchange(pieces, sign):
    lat, lon = lax.axis_size("lat"), lax.axis_size("lon")
    row, col, both = pieces
    pairs = [((i + sign) % lat * lon + (j + sign) % lon, i * lon + j) for i in range(lat) for j in range(lon)]
    col = lax.ppermute(col, "lon", [((j + sign) % lon, j) for j in range(lon)])
    both = lax.ppermute(both, ("lat", "lon"), pairs)
    row = lax.ppermute(row, "lat", [((i + sign) % lat, i) for i in range(lat)])
    return [row, col, both]


def unused(like):
    return pl.pallas_call(
        lambda *refs: None,
        out_shape=[jax.ShapeDtypeStruct(x.shape, x.dtype) for x in like],
        out_specs=[ANY] * len(like),
    )()


def choose(index, branches, *args):
    flat_args, tree = jax.tree.flatten(args)
    out_trees = []

    def closed(branch):
        def run(*leaves):
            out, out_tree = jax.tree.flatten(branch(*jax.tree.unflatten(tree, leaves)))
            out_trees.append(out_tree)
            return out

        return jax.make_jaxpr(run)(*flat_args)

    out = lax.cond_p.bind(index, *flat_args, branches=tuple(closed(branch) for branch in branches))
    return jax.tree.unflatten(out_trees[0], out)


def exchange_class(sent, which, sign):
    got = []
    for n in range(len(sent) // 3):
        mine = sent[3 * n : 3 * n + 3]
        got += exchange(mine, sign) if n == which else unused(mine)
    return got


def first_pieces(shifts, tokens, plan):
    width = tokens.shape[-1]
    sizes = plan.one

    def body(shifts_ref, tokens_ref, table_ref, *refs):
        outs, flags = refs[: 3 * len(sizes)], refs[3 * len(sizes) : 3 * len(sizes) + 3]
        held_ref, rows_ref, source_ref, sems = refs[3 * len(sizes) + 3 :]
        case = case_of(shifts_ref)
        start = Copies(sems)
        held = start(tokens_ref, held_ref)
        rows = start(table_ref.at[case], rows_ref)
        for ref, name in zip(flags, ("one_at", "two_at", "three_at")):
            ref[0] = lookup(plan.flags[name], case)
        rows.wait()
        held.wait()
        source_ref[...] = flat(held_ref)
        which = lookup(plan.flags["one_class"], case)
        send_classes(plan, rows_ref, "send_one", source_ref, sizes, which, outs)

    outs = [shape for size in sizes for shape in shapes(size, width)]
    specs = [VMEM] * len(outs) + [SMEM] * 3
    outs += [jax.ShapeDtypeStruct((1,), I32)] * 3
    scratch = [
        pltpu.VMEM(tokens.shape, BF16),
        pltpu.VMEM(plan.table.shape[1:], F32),
        pltpu.VMEM((tokens.size // width, width), BF16),
    ]
    *sent, one, two, three = call(
        body, outs, specs, shifts, [tokens, plan.table], [HBM, HBM], scratch, 2, 1 << 28, 1 << 20
    )
    return sent, one[0], two[0], three[0]


def id_kernel(shifts, regions, plan, rows, cols):
    _, lat, lon = regions.shape
    flat_regions = regions.reshape(2 * lat, lon)
    fine, coarse = windowed(rows, cols), natural(rows // 2, cols // 2)
    places = np.asarray(fine + coarse, np.float32)
    places[len(fine) :, 1:] *= 2
    pad = -len(places) % 128
    places = np.pad(places, ((0, pad), (0, 0))).T.reshape(3, -1, 128)
    is_fine = np.pad(np.ones(len(fine), np.float32), (0, len(coarse) + pad)).reshape(1, -1, 128)
    places = np.concatenate([places, is_fine])
    count = len(fine) + len(coarse)

    def body(shifts_ref, regions_hbm, places_hbm, fine_ref, coarse_ref, regions_ref, places_ref, sems):
        case = case_of(shifts_ref)
        start = Copies(sems)
        waits = [start(regions_hbm, regions_ref), start(places_hbm, places_ref)]
        for copy in waits:
            copy.wait()
        a = lookup(plan.flags["a"], case).astype(F32)
        big_a = 2.0 * lookup(plan.flags["big_a"], case).astype(F32)
        is_fine = places_ref[3]
        d = is_fine * a + (1.0 - is_fine) * big_a
        row = places_ref[1] + d + (lax.axis_index("lat") * rows).astype(F32)
        col = places_ref[2] + 2.0 * d + (lax.axis_index("lon") * cols).astype(F32)
        wrapped = jnp.where((row < 0) | (row >= lat), 4.0, 0.0)
        row = jnp.where(row < 0, row + lat, jnp.where(row >= lat, row - lat, row))
        col = jnp.where(col < 0, col + lon, jnp.where(col >= lon, col - lon, col))
        row = columns_of(row + places_ref[0] * lat, count)
        col = columns_of(col, count)
        wrapped = columns_of(wrapped, count)
        picked = select_rows(row, regions_ref[...].astype(F32).astype(BF16))
        ids = jnp.zeros((count, 128), F32)
        for at in range(0, lon, 128):
            width = min(128, lon - at)
            lane = lax.broadcasted_iota(I32, (1, width), 1).astype(F32) + float(at)
            here = jnp.where(lane == col[:, :width], picked[:, at : at + width], 0.0)
            ids = ids + jnp.sum(here, axis=1, keepdims=True)
        lane = lax.broadcasted_iota(I32, (1, 128), 1).astype(F32)
        hot = jnp.where(lane == ids + wrapped, 1.0, 0.0).astype(BF16)
        fine_ref[...] = hot[: len(fine)]
        coarse_ref[...] = hot[len(fine) :]

    outs = shapes([len(fine), len(coarse)], 128)
    scratch = [pltpu.VMEM(flat_regions.shape, I32), pltpu.VMEM(places.shape, F32)]
    return call(
        body, outs, [VMEM] * 2, shifts, [flat_regions, places], [HBM] * 2, scratch, 2, 1 << 28, 4 << 20
    )


def fine_level(shifts, tokens, pieces, key_id, w_qkv, w_proj, plan):
    _, rows, cols, width = tokens.shape
    count = 2 * rows * cols
    inner = w_proj.shape[0]
    kinds = 3 * len(plan.two)

    def body(shifts_ref, tokens_hbm, *refs):
        piece_refs, refs = refs[: len(pieces)], refs[len(pieces) :]
        id_hbm, qkv_w_hbm, proj_w_hbm, table_ref, out_hbm, *refs = refs
        piece_outs, refs = refs[:kinds], refs[kinds:]
        tokens_ref, source_ref, id_ref, qkv_w_ref, proj_w_ref, rows_ref, x_ref, qkv_ref, out_ref, sems = refs
        case = case_of(shifts_ref)
        start = Copies(sems)
        held = start(tokens_hbm, tokens_ref)
        index = start(table_ref.at[case], rows_ref)
        got = Pieces(piece_refs, plan.one, lookup(plan.flags["one_class"], case), source_ref, count, sems, 12)
        qkv_w, proj_w, ids = start(qkv_w_hbm, qkv_w_ref), start(proj_w_hbm, proj_w_ref), start(id_hbm, id_ref)
        index.wait()
        take = columns_of(rows_of(plan, rows_ref, "take_one"), count)
        held.wait()
        source_ref[:count, :] = flat(tokens_ref)
        got.wait()
        x = select_rows(take, source_ref[...])
        x_ref[...] = x
        normed = layer_norm(x).astype(BF16)
        qkv_w.wait()
        qkv_ref[...] = jnp.dot(normed, qkv_w_ref[...], preferred_element_type=F32).astype(BF16)
        proj_w.wait()
        ids.wait()
        leave = []

        def finish(w, out):
            at = slice(w * TOK, (w + 1) * TOK)
            out = lax.dot_general(out, proj_w_ref[...], TN, preferred_element_type=F32)
            out_ref[at, :] = (x_ref[at, :] + out).astype(BF16)
            leave.append(start(out_ref.at[pl.ds(w * TOK, TOK)], out_hbm.at[pl.ds(w * TOK, TOK)]))

        attend_windows(
            lambda w, at: qkv_ref[w * TOK : (w + 1) * TOK, at : at + 128],
            lambda w: id_ref[w * TOK : (w + 1) * TOK, :],
            count // TOK,
            inner,
            finish,
        )
        which = lookup(plan.flags["two_class"], case)
        send_classes(plan, rows_ref, "send_two", out_ref, plan.two, which, piece_outs)
        for copy in leave:
            copy.wait()

    outs = shapes([count], width, pltpu.HBM) + [shape for size in plan.two for shape in shapes(size, width)]
    specs = [HBM] + [VMEM] * kinds
    scratch = [
        pltpu.VMEM(tokens.shape, BF16),
        pltpu.VMEM((count + sum(plan.one[-1]), width), BF16),
        pltpu.VMEM(key_id.shape, BF16),
        pltpu.VMEM(w_qkv.shape, BF16),
        pltpu.VMEM(w_proj.shape, BF16),
        pltpu.VMEM(plan.table.shape[1:], F32),
        pltpu.VMEM((count, width), F32),
        pltpu.VMEM((count, 3 * inner), BF16),
        pltpu.VMEM((count, width), BF16),
    ]
    args = [tokens, *pieces, key_id, w_qkv, w_proj, plan.table]
    in_specs = [HBM] + [ANY] * (len(pieces) + 1) + [HBM] * 3
    assert 5 + count // TOK <= 16
    out, *sent = call(body, outs, specs, shifts, args, in_specs, scratch, 16, 3 << 30, 6 << 20)
    return out, sent


def coarse_level(shifts, fine, pieces, key_id, w_merge, w_qkv, w_proj, plan):
    count = key_id.shape[0]
    width = w_merge.shape[1]
    own, half = fine.shape
    inner = w_proj.shape[0]
    kinds = 3 * len(plan.three)
    step = w_merge.shape[0] // 4

    def body(shifts_ref, fine_hbm, *refs):
        piece_refs, refs = refs[: len(pieces)], refs[len(pieces) :]
        id_hbm, merge_hbm, qkv_w_hbm, proj_w_hbm, table_ref, out_hbm, *refs = refs
        piece_outs, refs = refs[:kinds], refs[kinds:]
        source_ref, id_ref, merge_ref, qkv_w_ref, proj_w_ref, rows_ref, qkv_ref, out_ref, sems = refs
        case = case_of(shifts_ref)
        start = Copies(sems)
        index = start(table_ref.at[case], rows_ref)
        held = start(fine_hbm, source_ref.at[pl.ds(0, own)])
        got = Pieces(piece_refs, plan.two, lookup(plan.flags["two_class"], case), source_ref, own, sems, 12)
        merge_w = [
            start(merge_hbm.at[pl.ds(n * step, step)], merge_ref.at[pl.ds(n * step, step)]) for n in range(4)
        ]
        qkv_w, proj_w, ids = start(qkv_w_hbm, qkv_w_ref), start(proj_w_hbm, proj_w_ref), start(id_hbm, id_ref)
        index.wait()
        take = columns_of(rows_of(plan, rows_ref, "take_two"), 4 * count)
        held.wait()
        got.wait()
        x = select_rows(take, source_ref[...])
        x = jnp.concatenate([x[n * count : (n + 1) * count] for n in range(4)], axis=1)
        stacked = layer_norm(x).astype(BF16)
        for copy in merge_w:
            copy.wait()
        merged = jnp.dot(stacked, merge_ref[...], preferred_element_type=F32).astype(BF16).astype(F32)
        normed = layer_norm(merged).astype(BF16)
        qkv_w.wait()
        qkv_ref[...] = jnp.dot(normed, qkv_w_ref[...], preferred_element_type=F32).astype(BF16)
        ids.wait()
        proj_w.wait()

        def finish(w, out):
            out = lax.dot_general(out, proj_w_ref[...], TN, preferred_element_type=F32)
            out_ref[...] = (merged + out).astype(BF16)

        attend_windows(lambda w, at: qkv_ref[:, at : at + 128], lambda w: id_ref[...], 1, inner, finish)
        leave = start(out_ref, out_hbm)
        which = lookup(plan.flags["three_class"], case)
        for n, (sizes, fine_sizes) in enumerate(zip(plan.three, plan.four)):

            @pl.when(which == n)
            def _():
                sent = select_rows(columns_of(rows_of(plan, rows_ref, "send_three"), sum(sizes)), out_ref[...])
                sent = sent.astype(BF16)
                at = 0
                for ref, size in zip(piece_outs[3 * n :], sizes):
                    ref[:size, :] = sent[at : at + size, :half]
                    ref[size : 2 * size, :] = sent[at : at + size, half:]
                    at += size
                if sum(fine_sizes):
                    index = columns_of(rows_of(plan, rows_ref, "send_four"), sum(fine_sizes))
                    sent = select_rows(index, source_ref[:own, :]).astype(BF16)
                    at = 0
                    for ref, size, more in zip(piece_outs[3 * n :], sizes, fine_sizes):
                        ref[2 * size :, :] = sent[at : at + more]
                        at += more

        leave.wait()

    outs = shapes([count], width, pltpu.HBM)
    for sizes, fine_sizes in zip(plan.three, plan.four):
        outs += shapes([2 * n + m for n, m in zip(sizes, fine_sizes)], half)
    specs = [HBM] + [VMEM] * kinds
    scratch = [
        pltpu.VMEM((own + sum(plan.two[-1]), half), BF16),
        pltpu.VMEM(key_id.shape, BF16),
        pltpu.VMEM(w_merge.shape, BF16),
        pltpu.VMEM(w_qkv.shape, BF16),
        pltpu.VMEM(w_proj.shape, BF16),
        pltpu.VMEM(plan.table.shape[1:], F32),
        pltpu.VMEM((count, 3 * inner), BF16),
        pltpu.VMEM((count, width), BF16),
    ]
    args = [fine, *pieces, key_id, w_merge, w_qkv, w_proj, plan.table]
    in_specs = [HBM] + [ANY] * (len(pieces) + 1) + [HBM] * 4
    out, *sent = call(body, outs, specs, shifts, args, in_specs, scratch, 16, 3 << 30, 12 << 20)
    return out, sent


def fine_output(shifts, fine, pieces, got, which, plan, rows, cols):
    own, width = fine.shape
    room = sum(plan.two[-1])
    extra = plan.four[which]

    def body(shifts_ref, fine_hbm, *refs):
        piece_refs, refs = refs[: len(pieces)], refs[len(pieces) :]
        got_refs, refs = refs[: len(got)], refs[len(got) :]
        table_ref, out_ref, source_ref, rows_ref, sems = refs
        case = case_of(shifts_ref)
        start = Copies(sems)
        waits = [start(table_ref.at[case], rows_ref), start(fine_hbm, source_ref.at[pl.ds(0, own)])]
        at = own + room
        for ref, size, more in zip(got_refs, plan.three[which], extra):
            waits.append(start(ref.at[pl.ds(2 * size, more)], source_ref.at[pl.ds(at, more)]))
            at += more
        pieces_in = Pieces(piece_refs, plan.two, lookup(plan.flags["two_class"], case), source_ref, own, sems, 8)
        for copy in waits:
            copy.wait()
        take = columns_of(rows_of(plan, rows_ref, "fine_out"), own)
        pieces_in.wait()
        out = select_rows(take, source_ref[...])
        out_ref[...] = out.reshape(2, rows, cols, width).astype(BF16)

    outs = [jax.ShapeDtypeStruct((2, rows, cols, width), BF16)]
    scratch = [
        pltpu.VMEM((own + room + (sum(extra) if got else 0), width), BF16),
        pltpu.VMEM(plan.table.shape[1:], F32),
    ]
    args = [fine, *pieces, *got, plan.table]
    in_specs = [HBM] + [ANY] * (len(pieces) + len(got)) + [HBM]
    return call(body, outs, [VMEM], shifts, args, in_specs, scratch, 16, 1 << 30, 4 << 20)[0]


def coarse_output(shifts, coarse, got, which, plan, rows, cols):
    own, width = coarse.shape
    half = width // 2
    sizes = plan.three[which]

    def body(shifts_ref, coarse_hbm, *refs):
        got_refs, (table_ref, out_ref, source_ref, rows_ref, sems) = refs[:3], refs[3:]
        start = Copies(sems)
        waits = [start(table_ref.at[case_of(shifts_ref)], rows_ref), start(coarse_hbm, source_ref.at[pl.ds(0, own)])]
        at = own
        for ref, size in zip(got_refs, sizes):
            for n in range(2):
                to = source_ref.at[pl.ds(at, size), pl.ds(n * half, half)]
                waits.append(start(ref.at[pl.ds(n * size, size)], to))
            at += size
        for copy in waits:
            copy.wait()
        take = columns_of(rows_of(plan, rows_ref, "coarse_out"), own)
        out = select_rows(take, source_ref[...]).astype(BF16)
        for n in range(own // 2):
            out_ref[n // cols, n % cols] = out[2 * n : 2 * n + 2]

    outs = [jax.ShapeDtypeStruct((rows, cols, 2, width), BF16)]
    scratch = [pltpu.VMEM((own + sum(sizes), width), BF16), pltpu.VMEM(plan.table.shape[1:], F32)]
    args = [coarse, *got, plan.table]
    out = call(body, outs, [VMEM], shifts, args, [HBM] + [ANY] * 3 + [HBM], scratch, 8, 1 << 28, 1 << 20)[0]
    return out.transpose(2, 0, 1, 3)


def on_device(tokens, regions, shifts, fine_qkv, fine_proj, merge_weight, coarse_qkv, coarse_proj):
    _, rows, cols, _ = tokens.shape
    plan = Plan(rows, cols)

    def first(which, sign, sent, shifts, regions):
        got = exchange_class(sent, which, sign)
        return got, id_kernel(shifts, regions, plan, rows, cols)

    def second(which, sign, sent):
        return exchange_class(sent, which, sign)

    def third(which, sign, sent, shifts, fine, pieces, coarse):
        got = exchange(sent[3 * which : 3 * which + 3], sign)
        fine_out = fine_output(shifts, fine, pieces, got if which else [], which, plan, rows, cols)
        return fine_out, coarse_output(shifts, coarse, got, which, plan, rows // 2, cols // 2)

    def branches(stage, pairs):
        return [functools.partial(stage, which, sign) for which, sign in pairs]

    sent, one, two, three = first_pieces(shifts, tokens, plan)
    got, (fine_id, coarse_id) = choose(one, branches(first, plan.one_branches), sent, shifts, regions)
    fine, sent = fine_level(shifts, tokens, got, fine_id, fine_qkv, fine_proj, plan)
    got = choose(two, branches(second, plan.two_branches), sent)
    coarse, sent = coarse_level(
        shifts, fine, got, coarse_id, merge_weight, coarse_qkv, coarse_proj, plan
    )
    return choose(three, branches(third, plan.three_branches), sent, shifts, fine, got, coarse)


def solution(mesh):
    return jax.shard_map(
        on_device,
        mesh=mesh,
        in_specs=(P(None, "lat", "lon", None), P(), P(), P(), P(), P(), P(), P()),
        out_specs=(P(None, "lat", "lon", None), P(None, "lat", "lon", None)),
        check_vma=False,
    )
```

```python
import functools

import jax
import jax.numpy as jnp
import numpy as np
from jax import lax
from jax.experimental import pallas as pl
from jax.experimental.pallas import tpu as pltpu
from jax.sharding import PartitionSpec as P

HD = 32
WH = 6
WW = 12
TOK = 2 * WH * WW
EPS = 1e-05
BIG = 1e30
SCALE = float(np.log2(np.e) / np.sqrt(HD))

NT = (((1,), (1,)), ((), ()))
TN = (((0,), (0,)), ((), ()))
F32 = jnp.float32
BF16 = jnp.bfloat16
I32 = jnp.int32

PAIRS = [(WH - 1, t) for t in range(1, WH)] + [(t, WH - 1) for t in range(1, WH - 1)]


def up16(count):
    return -(-count // 16) * 16


def natural(rows, cols):
    return [(l, r, c) for l in range(2) for r in range(rows) for c in range(cols)]


def windowed(rows, cols):
    return [
        (l, wr * WH + r, wc * WW + c)
        for wr in range(rows // WH)
        for wc in range(cols // WW)
        for l in range(2)
        for r in range(WH)
        for c in range(WW)
    ]


def moved(order, d):
    return [(l, r + d, c + 2 * d) for l, r, c in order]


def exchange_places(held, wanted, rows, cols, sign):
    at = {place: n for n, place in enumerate(held)}
    found = []
    for dr, dc in ((sign, 0), (0, sign), (sign, sign)):
        numbers, places = [], []
        for l, r, c in sorted(set(wanted) - set(held)):
            n = at.get((l, r - dr * rows, c - dc * cols))
            if n is not None:
                numbers.append(n)
                places.append((l, r, c))
        found.append((numbers, places))
    return found


def offsets(t0, t1):
    a = t0 if t0 <= 2 else t0 - WH
    big_a = t1 if t1 <= 2 else t1 - WH
    ahead = 1 if 2 * big_a > a or 2 * big_a - a == 0 and a < 0 else -1
    return a, big_a, ahead


def classes_of(needs, limits):
    which = [next(n for n, limit in enumerate(limits) if need[1] <= limit) for need in needs]
    sizes = [
        [up16(max(need[k] for need, w in zip(needs, which) if w == n)) for k in range(3)]
        for n in range(len(limits))
    ]
    return sizes, which


class Plan:
    def __init__(self, rows, cols):
        crows, ccols = rows // 2, cols // 2
        block, cblock = natural(rows, cols), natural(crows, ccols)
        cases = []
        for t0, t1 in PAIRS:
            a, big_a, ahead = offsets(t0, t1)
            fine = moved(windowed(rows, cols), a)
            coarse = moved(cblock, big_a)
            quarters = [
                (l, 2 * r + dr, 2 * c + dc)
                for dr, dc in ((0, 0), (1, 0), (0, 1), (1, 1))
                for l, r, c in coarse
            ]
            come = 1 if a > 0 else -1
            one = exchange_places(block, fine, rows, cols, come)
            home = [p for p in block if p not in set(fine)]
            wanted = quarters + (home if come == -ahead else [])
            two = exchange_places(fine, wanted, rows, cols, ahead)
            back = 1 if big_a < 0 else -1
            three = exchange_places(coarse, cblock, crows, ccols, back)
            got = set(fine).union(*[places for _, places in two])
            four = exchange_places(fine, [p for p in block if p not in got], rows, cols, back)
            cases.append((come, ahead, back, fine, coarse, quarters, one, two, three, four))

        def needs(which):
            return [[len(numbers) for numbers, _ in case[which]] for case in cases]

        self.one, one_class = classes_of(needs(6), [64, 512])
        self.two, two_class = classes_of(needs(7), [64, 128, 512])
        fine_back = [max(need) > 0 for need in needs(9)]
        self.three = []
        self.four = []
        for with_fine in (False, True):
            inside = [n for n, flag in enumerate(fine_back) if flag == with_fine]
            self.three.append([up16(max(needs(8)[n][k] for n in inside)) for k in range(3)])
            self.four.append([up16(max(needs(9)[n][k] for n in inside)) for k in range(3)])
        three_class = [int(flag) for flag in fine_back]

        def branches(which_class, direction):
            pairs = [(n, case[direction]) for n, case in zip(which_class, cases)]
            found = sorted(set(pairs))
            return found, [found.index(pair) for pair in pairs]

        self.one_branches, one_at = branches(one_class, 0)
        self.two_branches, two_at = branches(two_class, 1)
        self.three_branches, three_at = branches(three_class, 2)
        self.flags = dict(
            one_class=one_class, two_class=two_class, three_class=three_class,
            one_at=one_at, two_at=two_at, three_at=three_at,
            a=[offsets(*pair)[0] for pair in PAIRS], big_a=[offsets(*pair)[1] for pair in PAIRS],
        )

        found = {}
        for n, (come, ahead, back, fine, coarse, quarters, one, two, three, four) in enumerate(cases):

            def send(exchanged, room):
                return [n for (numbers, _), size in zip(exchanged, room) for n in numbers + [-1] * (size - len(numbers))]

            def source(held, *exchanges):
                places = list(held)
                for exchanged, room in exchanges:
                    for (_, got), size in zip(exchanged, room):
                        places += got + [None] * (size - len(got))
                return {p: n for n, p in enumerate(places) if p is not None}

            w = three_class[n]
            first, second = source(block, (one, self.one[-1])), source(fine, (two, self.two[-1]))
            third = source(coarse, (three, self.three[w]))
            last = source(fine, (two, self.two[-1]), (four, self.four[w]))
            out = [(l, r, c) for r in range(crows) for c in range(ccols) for l in range(2)]
            rows_of = dict(
                send_one=send(one, self.one[one_class[n]]),
                take_one=[first[p] for p in fine],
                send_two=send(two, self.two[two_class[n]]),
                take_two=[second[p] for p in quarters],
                send_three=send(three, self.three[w]),
                send_four=send(four, self.four[w]),
                fine_out=[last[p] for p in block],
                coarse_out=[third[p] for p in out],
            )
            for name, row in rows_of.items():
                found.setdefault(name, []).append(row)
        parts, self.at, top = [], {}, 0
        for name, lists in found.items():
            length = -(-max(len(row) for row in lists) // 128)
            part = np.full((len(PAIRS), length * 128), -1, np.float32)
            for n, row in enumerate(lists):
                part[n, : len(row)] = row
            parts.append(part.reshape(len(PAIRS), length, 128))
            self.at[name] = (top, length)
            top += length
        parts.append(np.zeros((len(PAIRS), -top % 8, 128), np.float32))
        self.table = np.concatenate(parts, axis=1)


def case_of(shifts_ref):
    t0, t1 = shifts_ref[0], shifts_ref[1]
    return jnp.where(t0 == WH - 1, t1 - 1, t0 + WH - 2)


def lookup(values, case):
    out = jnp.int32(values[0])
    for n, value in enumerate(values[1:], 1):
        out = jnp.where(case == n, value, out)
    return out


def columns_of(rows, count):
    parts = [jnp.broadcast_to(rows[j : j + 1], (128, 128)).T for j in range(-(-count // 128))]
    return stack_rows(parts)[:count]


def select_rows(index, source):
    lane = lax.broadcasted_iota(I32, (1, 128), 1).astype(F32)
    size = source.shape[0]
    pick = [jnp.where(index == lane + float(at), 1.0, 0.0).astype(BF16) for at in range(0, size, 128)]
    pick = jnp.concatenate(pick, axis=1)[:, :size]
    return jnp.dot(pick, source, preferred_element_type=F32)


def stack_rows(parts):
    return parts[0] if len(parts) == 1 else jnp.concatenate(parts, axis=0)


def layer_norm(values):
    center = jnp.mean(values, axis=-1, keepdims=True)
    values = values - center
    spread = jnp.mean(values * values, axis=-1, keepdims=True)
    return values * lax.rsqrt(spread + EPS)


def attend_windows(qkv_of, id_of, windows, inner, finish):
    lane = lax.broadcasted_iota(I32, (1, 128), 1)
    forbid = jnp.where(lane < 8, BIG, 0.0).astype(BF16)
    groups = inner // 128
    units = [(w, g) for w in range(windows) for g in range(groups)]
    scores, weights, outs = {}, {}, {}

    def score(w, g):
        key_id = id_of(w)
        not_id = (key_id - 1).astype(BF16) * forbid
        q = qkv_of(w, g * 128)
        keys = jnp.concatenate([qkv_of(w, inner + g * 128), key_id], axis=1)
        queries = []
        for h in range(4):
            mine = jnp.where((lane >= h * HD) & (lane < (h + 1) * HD), 1.0, 0.0).astype(BF16)
            queries.append(jnp.concatenate([q * mine, not_id], axis=1))
        scores[w, g] = lax.dot_general(keys, stack_rows(queries), NT, preferred_element_type=F32)

    def soften(w, g):
        s = scores.pop((w, g))
        weight = jnp.exp2((s - jnp.max(s, axis=0, keepdims=True)) * SCALE)
        weights[w, g] = weight.astype(BF16), 1.0 / jnp.sum(weight, axis=0, keepdims=True)

    def gather(w, g):
        weight, scale = weights.pop((w, g))
        out = lax.dot_general(qkv_of(w, 2 * inner + g * 128), weight, TN, preferred_element_type=F32) * scale
        outs[w, g] = [out[h * HD : (h + 1) * HD, h * TOK : (h + 1) * TOK] for h in range(4)]
        if g == groups - 1:
            finish(w, stack_rows([part for k in range(groups) for part in outs.pop((w, k))]).astype(BF16))

    for n in range(len(units) + 2):
        if n < len(units):
            score(*units[n])
        if 0 <= n - 1 < len(units):
            soften(*units[n - 1])
        if 0 <= n - 2 < len(units):
            gather(*units[n - 2])


ANY = pl.BlockSpec(memory_space=pl.ANY)
HBM = pl.BlockSpec(memory_space=pltpu.HBM)
VMEM = pl.BlockSpec(memory_space=pltpu.VMEM)
SMEM = pl.BlockSpec(memory_space=pltpu.SMEM)


def call(body, outs, args, in_specs, scratch, copies, flops, moved_bytes, vmem=32):
    args = [
        pltpu.with_memory_space_constraint(arg, spec.memory_space) for arg, spec in zip(args, in_specs, strict=True)
    ]
    spaces = [getattr(out, "memory_space", pltpu.SMEM if out.dtype == I32 else pltpu.VMEM) for out in outs]
    out_specs = [pl.BlockSpec(memory_space=space) for space in spaces]
    return pl.pallas_call(
        body,
        out_shape=outs,
        in_specs=in_specs,
        out_specs=out_specs,
        scratch_shapes=list(scratch) + [pltpu.SemaphoreType.DMA((copies,))],
        compiler_params=pltpu.CompilerParams(vmem_limit_bytes=vmem << 20),
        cost_estimate=pl.CostEstimate(flops=flops, bytes_accessed=moved_bytes, transcendentals=0),
    )(*args)


def shapes(sizes, width, space=pltpu.VMEM):
    return [space((n, width), BF16) for n in sizes]


class Copies:
    def __init__(self, sems):
        self.sems, self.used = sems, 0

    def __call__(self, src, dst):
        copy = pltpu.make_async_copy(src, dst, self.sems.at[self.used])
        self.used += 1
        copy.start()
        return copy


def lay_pieces(refs, sizes, which, source):
    for n, size in enumerate(sizes):

        @pl.when(which == n)
        def _():
            at = 0
            for ref, rows, room in zip(refs[3 * n : 3 * n + 3], size, sizes[-1]):
                source[at : at + rows, :] = ref[...]
                if rows < room:
                    source[at + rows : at + room, :] = jnp.zeros((room - rows, source.shape[1]), source.dtype)
                at += room


def flat(ref):
    layers, rows, cols, width = ref.shape
    return ref[...].astype(F32).reshape(layers * rows * cols, width).astype(BF16)


def put_pieces(value, refs):
    at = 0
    for ref in refs:
        ref[...] = value[at : at + ref.shape[0]].astype(BF16)
        at += ref.shape[0]


def rows_of(plan, table_ref, name, *lead):
    top, length = plan.at[name]
    return table_ref[(*lead, slice(top, top + length), slice(None))]


def send_classes(plan, rows, source_ref, sizes, which, refs):
    for n, size in enumerate(sizes):

        @pl.when(which == n)
        def _():
            put_pieces(select_rows(columns_of(rows, sum(size)), source_ref[...]), refs[3 * n : 3 * n + 3])


def exchange(pieces, sign):
    lat, lon = lax.axis_size("lat"), lax.axis_size("lon")
    row, col, both = pieces
    pairs = [((i + sign) % lat * lon + (j + sign) % lon, i * lon + j) for i in range(lat) for j in range(lon)]
    col = lax.ppermute(col, "lon", [((j + sign) % lon, j) for j in range(lon)])
    both = lax.ppermute(both, ("lat", "lon"), pairs)
    row = lax.ppermute(row, "lat", [((i + sign) % lat, i) for i in range(lat)])
    return [row, col, both]


def unused(like):
    outs = [pltpu.VMEM(x.shape, x.dtype) for x in like]
    return pl.pallas_call(
        lambda *refs: None, out_shape=outs, out_specs=[pl.BlockSpec(memory_space=pltpu.VMEM)] * len(outs)
    )()


def choose(index, branches, *args):
    flat_args, tree = jax.tree.flatten(args)
    out_trees = []

    def closed(branch):
        def run(*leaves):
            out, out_tree = jax.tree.flatten(branch(*jax.tree.unflatten(tree, leaves)))
            out_trees.append(out_tree)
            return out

        return jax.make_jaxpr(run)(*flat_args)

    out = lax.cond_p.bind(index, *flat_args, branches=tuple(closed(branch) for branch in branches))
    return jax.tree.unflatten(out_trees[0], out)


def exchange_class(sent, which, sign):
    got = []
    for n in range(len(sent) // 3):
        mine = sent[3 * n : 3 * n + 3]
        got += exchange(mine, sign) if n == which else unused(mine)
    return got


FLAGS = ("one_class", "two_class", "three_class", "a", "big_a")


def first_pieces(shifts, tokens, plan):
    width = tokens.shape[-1]
    count = tokens.size // width
    sizes = plan.one
    kinds = 3 * len(sizes)

    def body(shifts_hbm, tokens_hbm, table_hbm, *refs):
        outs, refs = refs[:kinds], refs[kinds:]
        source_ref, rows_ref, flags_ref, *at_refs, shifts_ref, tokens_ref, table_ref, sems = refs
        start = Copies(sems)
        shift = start(shifts_hbm, shifts_ref)
        held = start(tokens_hbm, tokens_ref)
        table = start(table_hbm, table_ref)
        shift.wait()
        case = case_of(shifts_ref)
        for ref, name in zip(at_refs, ("one_at", "two_at", "three_at")):
            ref[0] = lookup(plan.flags[name], case)
        for n, name in enumerate(FLAGS):
            flags_ref[n] = lookup(plan.flags[name], case)
        which = lookup(plan.flags["one_class"], case)
        held.wait()
        source_ref[...] = flat(tokens_ref)
        table.wait()
        rows_ref[...] = table_ref[case]
        send_classes(plan, rows_of(plan, table_ref, "send_one", case), source_ref, sizes, which, outs)

    outs = [shape for size in sizes for shape in shapes(size, width)] + shapes([count], width)
    outs += [pltpu.VMEM(plan.table.shape[1:], F32), pltpu.SMEM((8,), I32)]
    outs += [jax.ShapeDtypeStruct((1,), I32)] * 3
    scratch = [pltpu.SMEM((2,), I32), pltpu.VMEM(tokens.shape, BF16), pltpu.VMEM(plan.table.shape, F32)]
    got = call(body, outs, [shifts, tokens, plan.table], [HBM] * 3, scratch, 3, 1 << 28, 1 << 20)
    sent, (source, rows, flags, one, two, three) = got[:kinds], got[kinds:]
    return sent, source, rows, flags, one[0], two[0], three[0]


def id_kernel(flags, regions, weights, plan, rows, cols):
    _, lat, lon = regions.shape
    flat_regions = regions.reshape(2 * lat, lon)
    fine, coarse = windowed(rows, cols), natural(rows // 2, cols // 2)
    places = np.asarray(fine + coarse, np.float32)
    places[len(fine) :, 1:] *= 2
    pad = -len(places) % 128
    places = np.pad(places, ((0, pad), (0, 0))).T.reshape(3, -1, 128)
    is_fine = np.pad(np.ones(len(fine), np.float32), (0, len(coarse) + pad)).reshape(1, -1, 128)
    places = np.concatenate([places, is_fine])
    count = len(fine) + len(coarse)

    def body(flags_ref, regions_hbm, places_hbm, *refs):
        weights_hbm, refs = refs[: len(weights)], refs[len(weights) :]
        fine_ref, coarse_ref, *refs = refs
        weight_refs, (regions_ref, places_ref, sems) = refs[: len(weights)], refs[len(weights) :]
        start = Copies(sems)
        waits = [start(regions_hbm, regions_ref), start(places_hbm, places_ref)]
        later = [start(src, dst) for src, dst in zip(weights_hbm, weight_refs)]
        for copy in waits:
            copy.wait()
        a = flags_ref[3].astype(F32)
        big_a = 2.0 * flags_ref[4].astype(F32)
        is_fine = places_ref[3]
        d = is_fine * a + (1.0 - is_fine) * big_a
        row = places_ref[1] + d + (lax.axis_index("lat") * rows).astype(F32)
        col = places_ref[2] + 2.0 * d + (lax.axis_index("lon") * cols).astype(F32)
        wrapped = jnp.where((row < 0) | (row >= lat), 4.0, 0.0)
        row = jnp.where(row < 0, row + lat, jnp.where(row >= lat, row - lat, row))
        col = jnp.where(col < 0, col + lon, jnp.where(col >= lon, col - lon, col))
        row = columns_of(row + places_ref[0] * lat, count)
        col = columns_of(col, count)
        wrapped = columns_of(wrapped, count)
        picked = select_rows(row, regions_ref[...].astype(F32).astype(BF16))
        ids = jnp.zeros((count, 128), F32)
        for at in range(0, lon, 128):
            width = min(128, lon - at)
            lane = lax.broadcasted_iota(I32, (1, width), 1).astype(F32) + float(at)
            here = jnp.where(lane == col[:, :width], picked[:, at : at + width], 0.0)
            ids = ids + jnp.sum(here, axis=1, keepdims=True)
        lane = lax.broadcasted_iota(I32, (1, 128), 1).astype(F32)
        hot = jnp.where(lane == ids + wrapped, 1.0, 0.0).astype(BF16)
        fine_ref[...] = hot[: len(fine)]
        coarse_ref[...] = hot[len(fine) :]
        for copy in later:
            copy.wait()

    outs = shapes([len(fine), len(coarse)], 128) + [pltpu.VMEM(w.shape, BF16) for w in weights]
    scratch = [pltpu.VMEM(flat_regions.shape, I32), pltpu.VMEM(places.shape, F32)]
    args = [flags, flat_regions, places, *weights]
    in_specs = [SMEM] + [HBM] * (2 + len(weights))
    fine_id, coarse_id, *weights = call(body, outs, args, in_specs, scratch, 2 + len(weights), 1 << 28, 4 << 20)
    return fine_id, coarse_id, weights


def fetch(weights):
    def body(*refs):
        sems = refs[-1]
        start = Copies(sems)
        for copy in [start(src, dst) for src, dst in zip(refs[: len(weights)], refs[len(weights) : -1])]:
            copy.wait()

    outs = [pltpu.VMEM(w.shape, BF16) for w in weights]
    size = sum(2 * w.size for w in weights)
    return call(body, outs, weights, [HBM] * len(weights), [], len(weights), 0, size)


def fine_level(flags, tokens, pieces, key_id, w_qkv, w_proj, rows, plan):
    count, width = tokens.shape
    inner = w_proj.shape[0]
    kinds = 3 * len(plan.two)

    def body(flags_ref, tokens_ref, *refs):
        piece_refs, refs = refs[: len(pieces)], refs[len(pieces) :]
        id_ref, qkv_w_ref, proj_w_ref, rows_ref, out_ref, *refs = refs
        piece_outs, (source_ref, x_ref, qkv_ref, _) = refs[:kinds], refs[kinds:]
        lay_pieces(piece_refs, plan.one, flags_ref[0], source_ref)
        take = columns_of(rows_of(plan, rows_ref, "take_one"), count)
        x = select_rows(take, tokens_ref[...]) + select_rows(take - float(count), source_ref[...])
        x_ref[...] = x
        normed = layer_norm(x).astype(BF16)
        qkv_ref[...] = jnp.dot(normed, qkv_w_ref[...], preferred_element_type=F32).astype(BF16)

        def finish(w, out):
            at = slice(w * TOK, (w + 1) * TOK)
            out = lax.dot_general(out, proj_w_ref[...], TN, preferred_element_type=F32)
            out_ref[at, :] = (x_ref[at, :] + out).astype(BF16)

        attend_windows(
            lambda w, at: qkv_ref[w * TOK : (w + 1) * TOK, at : at + 128],
            lambda w: id_ref[w * TOK : (w + 1) * TOK, :],
            count // TOK,
            inner,
            finish,
        )
        send_classes(plan, rows_of(plan, rows_ref, "send_two"), out_ref, plan.two, flags_ref[1], piece_outs)

    outs = shapes([count], width) + [shape for size in plan.two for shape in shapes(size, width)]
    scratch = [
        pltpu.VMEM((sum(plan.one[-1]), width), BF16),
        pltpu.VMEM((count, width), F32),
        pltpu.VMEM((count, 3 * inner), BF16),
    ]
    args = [flags, tokens, *pieces, key_id, w_qkv, w_proj, rows]
    out, *sent = call(body, outs, args, [SMEM] + [VMEM] * (len(args) - 1), scratch, 1, 3 << 30, 6 << 20)
    return out, sent


def coarse_level(flags, fine, pieces, key_id, w_merge, w_qkv, w_proj, rows, plan):
    count = key_id.shape[0]
    width = w_merge.shape[1]
    own, half = fine.shape
    inner = w_proj.shape[0]
    kinds = 3 * len(plan.three)

    def body(flags_ref, fine_ref, *refs):
        piece_refs, refs = refs[: len(pieces)], refs[len(pieces) :]
        id_ref, merge_ref, qkv_w_ref, proj_w_ref, rows_ref, out_ref, *refs = refs
        piece_outs, (source_ref, qkv_ref, _) = refs[:kinds], refs[kinds:]
        lay_pieces(piece_refs, plan.two, flags_ref[1], source_ref)
        take = columns_of(rows_of(plan, rows_ref, "take_two"), 4 * count)
        x = select_rows(take, fine_ref[...]) + select_rows(take - float(own), source_ref[...])
        x = jnp.concatenate([x[n * count : (n + 1) * count] for n in range(4)], axis=1)
        stacked = layer_norm(x).astype(BF16)
        merged = jnp.dot(stacked, merge_ref[...], preferred_element_type=F32).astype(BF16).astype(F32)
        normed = layer_norm(merged).astype(BF16)
        qkv_ref[...] = jnp.dot(normed, qkv_w_ref[...], preferred_element_type=F32).astype(BF16)

        def finish(w, out):
            out = lax.dot_general(out, proj_w_ref[...], TN, preferred_element_type=F32)
            out_ref[...] = (merged + out).astype(BF16)

        attend_windows(lambda w, at: qkv_ref[:, at : at + 128], lambda w: id_ref[...], 1, inner, finish)
        for n, (sizes, fine_sizes) in enumerate(zip(plan.three, plan.four)):

            @pl.when(flags_ref[2] == n)
            def _():
                sent = select_rows(columns_of(rows_of(plan, rows_ref, "send_three"), sum(sizes)), out_ref[...])
                sent = sent.astype(BF16)
                at = 0
                for ref, size in zip(piece_outs[3 * n :], sizes):
                    ref[:size, :] = sent[at : at + size, :half]
                    ref[size : 2 * size, :] = sent[at : at + size, half:]
                    at += size
                if sum(fine_sizes):
                    index = columns_of(rows_of(plan, rows_ref, "send_four"), sum(fine_sizes))
                    sent = select_rows(index, fine_ref[...]).astype(BF16)
                    at = 0
                    for ref, size, more in zip(piece_outs[3 * n :], sizes, fine_sizes):
                        ref[2 * size :, :] = sent[at : at + more]
                        at += more

    outs = shapes([count], width)
    for sizes, fine_sizes in zip(plan.three, plan.four):
        outs += shapes([2 * n + m for n, m in zip(sizes, fine_sizes)], half)
    scratch = [pltpu.VMEM((sum(plan.two[-1]), half), BF16), pltpu.VMEM((count, 3 * inner), BF16)]
    args = [flags, fine, *pieces, key_id, w_merge, w_qkv, w_proj, rows]
    out, *sent = call(body, outs, args, [SMEM] + [VMEM] * (len(args) - 1), scratch, 1, 3 << 30, 12 << 20)
    return out, sent


def fine_output(flags, fine, pieces, rows, plan, block_rows, block_cols, partial):
    own, width = fine.shape

    def body(flags_ref, fine_ref, *refs):
        piece_refs, (rows_ref, out_ref, source_ref, _) = refs[: len(pieces)], refs[len(pieces) :]
        lay_pieces(piece_refs, plan.two, flags_ref[1], source_ref)
        take = columns_of(rows_of(plan, rows_ref, "fine_out"), own)
        out = select_rows(take, fine_ref[...]) + select_rows(take - float(own), source_ref[...])
        out_ref[...] = (out if partial else out.reshape(out_ref.shape)).astype(BF16)

    outs = [jax.ShapeDtypeStruct((2, block_rows, block_cols, width), BF16)]
    if partial:
        outs = shapes([own], width)
    scratch = [pltpu.VMEM((sum(plan.two[-1]), width), BF16)]
    args = [flags, fine, *pieces, rows]
    return call(body, outs, args, [SMEM] + [VMEM] * (len(args) - 1), scratch, 1, 1 << 30, 4 << 20)[0]


def coarse_output(coarse, got, rows, which, plan, block_rows, block_cols, part=None):
    own, width = coarse.shape
    half = width // 2
    sizes, more = plan.three[which], plan.four[which]
    parts = [] if part is None else [part]

    def body(coarse_ref, *refs):
        got_refs, refs = refs[:3], refs[3:]
        part_refs, (rows_ref, out_ref, *fine_outs, _) = refs[: len(parts)], refs[len(parts) :]
        back = [
            jnp.concatenate([ref[:size, :], ref[size : 2 * size, :]], axis=1) for ref, size in zip(got_refs, sizes)
        ]
        take = columns_of(rows_of(plan, rows_ref, "coarse_out"), own)
        out = select_rows(take, stack_rows([coarse_ref[...]] + back)).astype(BF16)
        for n in range(own // 2):
            out_ref[n // block_cols, n % block_cols] = out[2 * n : 2 * n + 2]
        for part_ref, fine_ref in zip(part_refs, fine_outs):
            fine = stack_rows([ref[2 * size :, :] for ref, size in zip(got_refs, sizes)])
            base = part_ref.shape[0] + sum(plan.two[-1])
            take = columns_of(rows_of(plan, rows_ref, "fine_out"), part_ref.shape[0]) - float(base)
            out = part_ref[...].astype(F32) + select_rows(take, fine)
            fine_ref[...] = out.reshape(fine_ref.shape).astype(BF16)

    outs = [jax.ShapeDtypeStruct((block_rows, block_cols, 2, width), BF16)]
    outs += [jax.ShapeDtypeStruct((2, 2 * block_rows, 2 * block_cols, half), BF16) for _ in parts]
    args = [coarse, *got, *parts, rows]
    out, *fine = call(body, outs, args, [VMEM] * len(args), [], 1, 1 << 28, 1 << 20)
    return out.transpose(2, 0, 1, 3), *fine


def on_device(tokens, regions, shifts, fine_qkv, fine_proj, merge_weight, coarse_qkv, coarse_proj):
    _, rows, cols, _ = tokens.shape
    plan = Plan(rows, cols)

    def first(which, sign, sent, flags, regions, weights):
        got = exchange_class(sent, which, sign)
        return got, id_kernel(flags, regions, weights, plan, rows, cols)

    def second(which, sign, sent, weights):
        return exchange_class(sent, which, sign), fetch(weights)

    def third(which, sign, sent, flags, fine, pieces, coarse, table):
        got = exchange(sent[3 * which : 3 * which + 3], sign)
        fine_out = fine_output(flags, fine, pieces, table, plan, rows, cols, which == 1)
        place = (table, which, plan, rows // 2, cols // 2)
        if which == 1:
            coarse_out, fine_out = coarse_output(coarse, got, *place, part=fine_out)
        else:
            (coarse_out,) = coarse_output(coarse, got, *place)
        return fine_out, coarse_out

    def branches(stage, pairs):
        return [functools.partial(stage, which, sign) for which, sign in pairs]

    sent, source, table, flags, one, two, three = first_pieces(shifts, tokens, plan)
    got, (fine_id, coarse_id, weights) = choose(
        one, branches(first, plan.one_branches), sent, flags, regions, [fine_qkv, fine_proj]
    )
    fine, sent = fine_level(flags, source, got, fine_id, *weights, table, plan)
    weights = [merge_weight, coarse_qkv, coarse_proj]
    got, weights = choose(two, branches(second, plan.two_branches), sent, weights)
    coarse, sent = coarse_level(flags, fine, got, coarse_id, *weights, table, plan)
    return choose(three, branches(third, plan.three_branches), sent, flags, fine, got, coarse, table)


def solution(mesh):
    return jax.shard_map(
        on_device,
        mesh=mesh,
        in_specs=(P(None, "lat", "lon", None), P(), P(), P(), P(), P(), P(), P()),
        out_specs=(P(None, "lat", "lon", None), P(None, "lat", "lon", None)),
        check_vma=False,
    )
```

```python
import functools

import jax
import jax.numpy as jnp
import numpy as np
from jax import lax
from jax.experimental import pallas as pl
from jax.experimental.pallas import tpu as pltpu
from jax.sharding import PartitionSpec as P

HD = 32
WH = 6
WW = 12
TOK = 2 * WH * WW
EPS = 1e-05
BIG = 1e30
SCALE = float(np.log2(np.e) / np.sqrt(HD))

NT = (((1,), (1,)), ((), ()))
TN = (((0,), (0,)), ((), ()))
F32 = jnp.float32
BF16 = jnp.bfloat16
I32 = jnp.int32

PAIRS = [(WH - 1, t) for t in range(1, WH)] + [(t, WH - 1) for t in range(1, WH - 1)]


def up16(count):
    return -(-count // 16) * 16


def natural(rows, cols):
    return [(l, r, c) for l in range(2) for r in range(rows) for c in range(cols)]


def windowed(rows, cols):
    return [
        (l, wr * WH + r, wc * WW + c)
        for wr in range(rows // WH)
        for wc in range(cols // WW)
        for l in range(2)
        for r in range(WH)
        for c in range(WW)
    ]


def moved(order, d):
    return [(l, r + d, c + 2 * d) for l, r, c in order]


def exchange_places(held, wanted, rows, cols, sign):
    at = {place: n for n, place in enumerate(held)}
    found = []
    for dr, dc in ((sign, 0), (0, sign), (sign, sign)):
        numbers, places = [], []
        for l, r, c in sorted(set(wanted) - set(held)):
            n = at.get((l, r - dr * rows, c - dc * cols))
            if n is not None:
                numbers.append(n)
                places.append((l, r, c))
        found.append((numbers, places))
    return found


def offsets(t0, t1):
    a = t0 if t0 <= 2 else t0 - WH
    big_a = t1 if t1 <= 2 else t1 - WH
    ahead = 1 if 2 * big_a > a or 2 * big_a - a == 0 and a < 0 else -1
    return a, big_a, ahead


def classes_of(needs, limits):
    which = [next(n for n, limit in enumerate(limits) if need[1] <= limit) for need in needs]
    sizes = [
        [up16(max(need[k] for need, w in zip(needs, which) if w == n)) for k in range(3)]
        for n in range(len(limits))
    ]
    return sizes, which


class Plan:
    def __init__(self, rows, cols):
        crows, ccols = rows // 2, cols // 2
        block, cblock = natural(rows, cols), natural(crows, ccols)
        cases = []
        for t0, t1 in PAIRS:
            a, big_a, ahead = offsets(t0, t1)
            fine = moved(windowed(rows, cols), a)
            coarse = moved(cblock, big_a)
            quarters = [
                (l, 2 * r + dr, 2 * c + dc)
                for dr, dc in ((0, 0), (1, 0), (0, 1), (1, 1))
                for l, r, c in coarse
            ]
            come = 1 if a > 0 else -1
            one = exchange_places(block, fine, rows, cols, come)
            home = [p for p in block if p not in set(fine)]
            wanted = quarters + (home if come == -ahead else [])
            two = exchange_places(fine, wanted, rows, cols, ahead)
            back = 1 if big_a < 0 else -1
            three = exchange_places(coarse, cblock, crows, ccols, back)
            got = set(fine).union(*[places for _, places in two])
            four = exchange_places(fine, [p for p in block if p not in got], rows, cols, back)
            cases.append((come, ahead, back, fine, coarse, quarters, one, two, three, four))

        def needs(which):
            return [[len(numbers) for numbers, _ in case[which]] for case in cases]

        self.one, one_class = classes_of(needs(6), [64, 512])
        self.two, two_class = classes_of(needs(7), [64, 128, 512])
        fine_back = [max(need) > 0 for need in needs(9)]
        self.three = []
        self.four = []
        for with_fine in (False, True):
            inside = [n for n, flag in enumerate(fine_back) if flag == with_fine]
            self.three.append([up16(max(needs(8)[n][k] for n in inside)) for k in range(3)])
            self.four.append([up16(max(needs(9)[n][k] for n in inside)) for k in range(3)])
        three_class = [int(flag) for flag in fine_back]

        def branches(which_class, direction):
            pairs = [(n, case[direction]) for n, case in zip(which_class, cases)]
            found = sorted(set(pairs))
            return found, [found.index(pair) for pair in pairs]

        self.one_branches, one_at = branches(one_class, 0)
        self.two_branches, two_at = branches(two_class, 1)
        self.three_branches, three_at = branches(three_class, 2)
        self.flags = dict(
            one_class=one_class, two_class=two_class, three_class=three_class,
            one_at=one_at, two_at=two_at, three_at=three_at,
            a=[offsets(*pair)[0] for pair in PAIRS], big_a=[offsets(*pair)[1] for pair in PAIRS],
        )

        found = {}
        for n, (come, ahead, back, fine, coarse, quarters, one, two, three, four) in enumerate(cases):

            def send(exchanged, room):
                return [n for (numbers, _), size in zip(exchanged, room) for n in numbers + [-1] * (size - len(numbers))]

            def source(held, *exchanges):
                places = list(held)
                for exchanged, room in exchanges:
                    for (_, got), size in zip(exchanged, room):
                        places += got + [None] * (size - len(got))
                return {p: n for n, p in enumerate(places) if p is not None}

            w = three_class[n]
            first, second = source(block, (one, self.one[-1])), source(fine, (two, self.two[-1]))
            third = source(coarse, (three, self.three[w]))
            last = source(fine, (two, self.two[-1]), (four, self.four[w]))
            out = [(l, r, c) for r in range(crows) for c in range(ccols) for l in range(2)]
            rows_of = dict(
                send_one=send(one, self.one[one_class[n]]),
                take_one=[first[p] for p in fine],
                send_two=send(two, self.two[two_class[n]]),
                take_two=[second[p] for p in quarters],
                send_three=send(three, self.three[w]),
                send_four=send(four, self.four[w]),
                fine_out=[last[p] for p in block],
                coarse_out=[third[p] for p in out],
            )
            for name, row in rows_of.items():
                found.setdefault(name, []).append(row)
        parts, self.at, top = [], {}, 0
        for name, lists in found.items():
            length = -(-max(len(row) for row in lists) // 128)
            part = np.full((len(PAIRS), length * 128), -1, np.float32)
            for n, row in enumerate(lists):
                part[n, : len(row)] = row
            parts.append(part.reshape(len(PAIRS), length, 128))
            self.at[name] = (top, length)
            top += length
        parts.append(np.zeros((len(PAIRS), -top % 8, 128), np.float32))
        self.table = np.concatenate(parts, axis=1)


def case_of(shifts_ref):
    t0, t1 = shifts_ref[0], shifts_ref[1]
    return jnp.where(t0 == WH - 1, t1 - 1, t0 + WH - 2)


def lookup(values, case):
    out = jnp.int32(values[0])
    for n, value in enumerate(values[1:], 1):
        out = jnp.where(case == n, value, out)
    return out


def columns_of(rows, count):
    parts = [jnp.broadcast_to(rows[j : j + 1], (128, 128)).T for j in range(-(-count // 128))]
    return stack_rows(parts)[:count]


def select_rows(index, source):
    lane = lax.broadcasted_iota(I32, (1, 128), 1).astype(F32)
    size = source.shape[0]
    pick = [jnp.where(index == lane + float(at), 1.0, 0.0).astype(BF16) for at in range(0, size, 128)]
    pick = jnp.concatenate(pick, axis=1)[:, :size]
    return jnp.dot(pick, source, preferred_element_type=F32)


def stack_rows(parts):
    return parts[0] if len(parts) == 1 else jnp.concatenate(parts, axis=0)


def layer_norm(values):
    center = jnp.mean(values, axis=-1, keepdims=True)
    values = values - center
    spread = jnp.mean(values * values, axis=-1, keepdims=True)
    return values * lax.rsqrt(spread + EPS)


def attend_windows(qkv_of, id_of, windows, inner, finish):
    lane = lax.broadcasted_iota(I32, (1, 128), 1)
    forbid = jnp.where(lane < 8, BIG, 0.0).astype(BF16)
    groups = inner // 128
    units = [(w, g) for w in range(windows) for g in range(groups)]
    scores, weights, outs = {}, {}, {}

    def score(w, g):
        key_id = id_of(w)
        not_id = (key_id - 1).astype(BF16) * forbid
        q = qkv_of(w, g * 128)
        keys = jnp.concatenate([qkv_of(w, inner + g * 128), key_id], axis=1)
        queries = []
        for h in range(4):
            mine = jnp.where((lane >= h * HD) & (lane < (h + 1) * HD), 1.0, 0.0).astype(BF16)
            queries.append(jnp.concatenate([q * mine, not_id], axis=1))
        scores[w, g] = lax.dot_general(keys, stack_rows(queries), NT, preferred_element_type=F32)

    def soften(w, g):
        s = scores.pop((w, g))
        weight = jnp.exp2((s - jnp.max(s, axis=0, keepdims=True)) * SCALE)
        weights[w, g] = weight.astype(BF16), 1.0 / jnp.sum(weight, axis=0, keepdims=True)

    def gather(w, g):
        weight, scale = weights.pop((w, g))
        out = lax.dot_general(qkv_of(w, 2 * inner + g * 128), weight, TN, preferred_element_type=F32) * scale
        outs[w, g] = [out[h * HD : (h + 1) * HD, h * TOK : (h + 1) * TOK] for h in range(4)]
        if g == groups - 1:
            finish(w, stack_rows([part for k in range(groups) for part in outs.pop((w, k))]).astype(BF16))

    for n in range(len(units) + 2):
        if n < len(units):
            score(*units[n])
        if 0 <= n - 1 < len(units):
            soften(*units[n - 1])
        if 0 <= n - 2 < len(units):
            gather(*units[n - 2])


ANY = pl.BlockSpec(memory_space=pl.ANY)
HBM = pl.BlockSpec(memory_space=pltpu.HBM)
VMEM = pl.BlockSpec(memory_space=pltpu.VMEM)
SMEM = pl.BlockSpec(memory_space=pltpu.SMEM)


def call(body, outs, args, in_specs, scratch, copies, flops, moved_bytes, vmem=32):
    args = [
        pltpu.with_memory_space_constraint(arg, spec.memory_space) for arg, spec in zip(args, in_specs, strict=True)
    ]
    spaces = [getattr(out, "memory_space", pltpu.SMEM if out.dtype == I32 else pltpu.VMEM) for out in outs]
    out_specs = [pl.BlockSpec(memory_space=space) for space in spaces]
    return pl.pallas_call(
        body,
        out_shape=outs,
        in_specs=in_specs,
        out_specs=out_specs,
        scratch_shapes=list(scratch) + [pltpu.SemaphoreType.DMA((copies,))],
        compiler_params=pltpu.CompilerParams(vmem_limit_bytes=vmem << 20),
        cost_estimate=pl.CostEstimate(flops=flops, bytes_accessed=moved_bytes, transcendentals=0),
    )(*args)


def shapes(sizes, width, space=pltpu.VMEM):
    return [space((n, width), BF16) for n in sizes]


class Copies:
    def __init__(self, sems):
        self.sems, self.used = sems, 0

    def __call__(self, src, dst):
        copy = pltpu.make_async_copy(src, dst, self.sems.at[self.used])
        self.used += 1
        copy.start()
        return copy


def lay_pieces(refs, sizes, which, source):
    for n, size in enumerate(sizes):

        @pl.when(which == n)
        def _():
            at = 0
            for ref, rows, room in zip(refs[3 * n : 3 * n + 3], size, sizes[-1]):
                source[at : at + rows, :] = ref[...]
                if rows < room:
                    source[at + rows : at + room, :] = jnp.zeros((room - rows, source.shape[1]), source.dtype)
                at += room


def flat(ref):
    layers, rows, cols, width = ref.shape
    return ref[...].astype(F32).reshape(layers * rows * cols, width).astype(BF16)


def put_pieces(value, refs):
    at = 0
    for ref in refs:
        ref[...] = value[at : at + ref.shape[0]].astype(BF16)
        at += ref.shape[0]


def rows_of(plan, table_ref, name, *lead):
    top, length = plan.at[name]
    return table_ref[(*lead, slice(top, top + length), slice(None))]


def send_classes(plan, rows, source_ref, sizes, which, refs):
    for n, size in enumerate(sizes):

        @pl.when(which == n)
        def _():
            put_pieces(select_rows(columns_of(rows, sum(size)), source_ref[...]), refs[3 * n : 3 * n + 3])


def exchange(pieces, sign):
    lat, lon = lax.axis_size("lat"), lax.axis_size("lon")
    row, col, both = pieces
    pairs = [((i + sign) % lat * lon + (j + sign) % lon, i * lon + j) for i in range(lat) for j in range(lon)]
    col = lax.ppermute(col, "lon", [((j + sign) % lon, j) for j in range(lon)])
    both = lax.ppermute(both, ("lat", "lon"), pairs)
    row = lax.ppermute(row, "lat", [((i + sign) % lat, i) for i in range(lat)])
    return [row, col, both]


def unused(like):
    outs = [pltpu.VMEM(x.shape, x.dtype) for x in like]
    return pl.pallas_call(
        lambda *refs: None, out_shape=outs, out_specs=[pl.BlockSpec(memory_space=pltpu.VMEM)] * len(outs)
    )()


def choose(index, branches, *args):
    flat_args, tree = jax.tree.flatten(args)
    out_trees = []

    def closed(branch):
        def run(*leaves):
            out, out_tree = jax.tree.flatten(branch(*jax.tree.unflatten(tree, leaves)))
            out_trees.append(out_tree)
            return out

        return jax.make_jaxpr(run)(*flat_args)

    out = lax.cond_p.bind(index, *flat_args, branches=tuple(closed(branch) for branch in branches))
    return jax.tree.unflatten(out_trees[0], out)


def exchange_class(sent, which, sign):
    got = []
    for n in range(len(sent) // 3):
        mine = sent[3 * n : 3 * n + 3]
        got += exchange(mine, sign) if n == which else unused(mine)
    return got


FLAGS = ("one_class", "two_class", "three_class", "a", "big_a")


def first_pieces(shifts, tokens, plan):
    width = tokens.shape[-1]
    count = tokens.size // width
    sizes = plan.one
    kinds = 3 * len(sizes)

    def body(shifts_hbm, tokens_hbm, table_hbm, *refs):
        outs, refs = refs[:kinds], refs[kinds:]
        rows_ref, flags_ref, *at_refs, shifts_ref, tokens_ref, table_ref, source_ref, sems = refs
        start = Copies(sems)
        shift = start(shifts_hbm, shifts_ref)
        held = start(tokens_hbm, tokens_ref)
        table = start(table_hbm, table_ref)
        shift.wait()
        case = case_of(shifts_ref)
        for ref, name in zip(at_refs, ("one_at", "two_at", "three_at")):
            ref[0] = lookup(plan.flags[name], case)
        for n, name in enumerate(FLAGS):
            flags_ref[n] = lookup(plan.flags[name], case)
        which = lookup(plan.flags["one_class"], case)
        held.wait()
        source_ref[...] = flat(tokens_ref)
        table.wait()
        rows_ref[...] = table_ref[case]
        send_classes(plan, rows_of(plan, table_ref, "send_one", case), source_ref, sizes, which, outs)

    outs = [shape for size in sizes for shape in shapes(size, width)]
    outs += [pltpu.VMEM(plan.table.shape[1:], F32), pltpu.SMEM((8,), I32)]
    outs += [jax.ShapeDtypeStruct((1,), I32)] * 3
    scratch = [pltpu.SMEM((2,), I32), pltpu.VMEM(tokens.shape, BF16), pltpu.VMEM(plan.table.shape, F32)]
    scratch += [pltpu.VMEM((count, width), BF16)]
    got = call(body, outs, [shifts, tokens, plan.table], [HBM] * 3, scratch, 3, 1 << 28, 1 << 20)
    sent, (rows, flags, one, two, three) = got[:kinds], got[kinds:]
    return sent, rows, flags, one[0], two[0], three[0]


def before_fine(flags, regions, tokens, table, weights, plan):
    _, lat, lon = regions.shape
    _, rows, cols, width = tokens.shape
    flat_regions = regions.reshape(2 * lat, lon)
    fine, coarse = windowed(rows, cols), natural(rows // 2, cols // 2)
    places = np.asarray(fine + coarse, np.float32)
    places[len(fine) :, 1:] *= 2
    pad = -len(places) % 128
    places = np.pad(places, ((0, pad), (0, 0))).T.reshape(3, -1, 128)
    is_fine = np.pad(np.ones(len(fine), np.float32), (0, len(coarse) + pad)).reshape(1, -1, 128)
    places = np.concatenate([places, is_fine])
    count = len(fine) + len(coarse)

    def body(flags_ref, rows_ref, regions_hbm, places_hbm, tokens_hbm, *refs):
        weights_hbm, refs = refs[: len(weights)], refs[len(weights) :]
        fine_ref, coarse_ref, x_ref, *refs = refs
        weight_refs, (regions_ref, places_ref, tokens_ref, sems) = refs[: len(weights)], refs[len(weights) :]
        start = Copies(sems)
        waits = [start(regions_hbm, regions_ref), start(places_hbm, places_ref)]
        held = start(tokens_hbm, tokens_ref)
        later = [start(src, dst) for src, dst in zip(weights_hbm, weight_refs)]
        for copy in waits:
            copy.wait()
        a = flags_ref[3].astype(F32)
        big_a = 2.0 * flags_ref[4].astype(F32)
        is_fine = places_ref[3]
        d = is_fine * a + (1.0 - is_fine) * big_a
        row = places_ref[1] + d + (lax.axis_index("lat") * rows).astype(F32)
        col = places_ref[2] + 2.0 * d + (lax.axis_index("lon") * cols).astype(F32)
        wrapped = jnp.where((row < 0) | (row >= lat), 4.0, 0.0)
        row = jnp.where(row < 0, row + lat, jnp.where(row >= lat, row - lat, row))
        col = jnp.where(col < 0, col + lon, jnp.where(col >= lon, col - lon, col))
        row = columns_of(row + places_ref[0] * lat, count)
        col = columns_of(col, count)
        wrapped = columns_of(wrapped, count)
        picked = select_rows(row, regions_ref[...].astype(F32).astype(BF16))
        ids = jnp.zeros((count, 128), F32)
        for at in range(0, lon, 128):
            size = min(128, lon - at)
            lane = lax.broadcasted_iota(I32, (1, size), 1).astype(F32) + float(at)
            here = jnp.where(lane == col[:, :size], picked[:, at : at + size], 0.0)
            ids = ids + jnp.sum(here, axis=1, keepdims=True)
        lane = lax.broadcasted_iota(I32, (1, 128), 1).astype(F32)
        hot = jnp.where(lane == ids + wrapped, 1.0, 0.0).astype(BF16)
        fine_ref[...] = hot[: len(fine)]
        coarse_ref[...] = hot[len(fine) :]
        held.wait()
        take = columns_of(rows_of(plan, rows_ref, "take_one"), len(fine))
        x_ref[...] = select_rows(take, flat(tokens_ref)).astype(BF16)
        for copy in later:
            copy.wait()

    outs = shapes([len(fine), len(coarse)], 128) + shapes([len(fine)], width)
    outs += [pltpu.VMEM(w.shape, BF16) for w in weights]
    scratch = [pltpu.VMEM(flat_regions.shape, I32), pltpu.VMEM(places.shape, F32), pltpu.VMEM(tokens.shape, BF16)]
    args = [flags, table, flat_regions, places, tokens, *weights]
    in_specs = [SMEM, VMEM] + [HBM] * (3 + len(weights))
    fine_id, coarse_id, x, *weights = call(body, outs, args, in_specs, scratch, 3 + len(weights), 1 << 28, 4 << 20)
    return fine_id, coarse_id, x, weights


CHUNK = 512


def before_coarse(fine, table, weights, plan):
    own, width = fine.shape
    cuts = [(n, at) for n, w in enumerate(weights) for at in range(0, w.shape[0], CHUNK)]

    def body(rows_ref, fine_hbm, *refs):
        weights_hbm, refs = refs[: len(weights)], refs[len(weights) :]
        x_ref, *chunk_refs, fine_ref, sems = refs
        start = Copies(sems)
        held = start(fine_hbm, fine_ref)
        later = [start(weights_hbm[n].at[pl.ds(at, CHUNK)], ref) for (n, at), ref in zip(cuts, chunk_refs)]
        take = columns_of(rows_of(plan, rows_ref, "take_two"), x_ref.shape[0])
        held.wait()
        x_ref[...] = select_rows(take, fine_ref[...]).astype(BF16)
        for copy in later:
            copy.wait()

    outs = shapes([own], width) + [pltpu.VMEM((CHUNK, weights[n].shape[1]), BF16) for n, _ in cuts]
    size = sum(2 * w.size for w in weights)
    args = [table, fine, *weights]
    in_specs = [VMEM] + [HBM] * (1 + len(weights))
    scratch = [pltpu.VMEM(fine.shape, BF16)]
    x, *chunks = call(body, outs, args, in_specs, scratch, 1 + len(cuts), 1 << 28, size)
    return x, [[chunk for (m, _), chunk in zip(cuts, chunks) if m == n] for n in range(len(weights))]


def fine_level(flags, x_own, pieces, key_id, w_qkv, w_proj, rows, plan):
    count, width = x_own.shape
    inner = w_proj.shape[0]
    kinds = 3 * len(plan.two)

    def body(flags_ref, own_ref, *refs):
        piece_refs, refs = refs[: len(pieces)], refs[len(pieces) :]
        id_ref, qkv_w_ref, proj_w_ref, rows_ref, out_hbm, *refs = refs
        piece_outs, (source_ref, x_ref, qkv_ref, out_ref, sems) = refs[:kinds], refs[kinds:]
        start = Copies(sems)
        leave = []
        lay_pieces(piece_refs, plan.one, flags_ref[0], source_ref)
        take = columns_of(rows_of(plan, rows_ref, "take_one"), count) - float(count)
        x = own_ref[...].astype(F32) + select_rows(take, source_ref[...])
        x_ref[...] = x
        normed = layer_norm(x).astype(BF16)
        qkv_ref[...] = jnp.dot(normed, qkv_w_ref[...], preferred_element_type=F32).astype(BF16)

        def finish(w, out):
            at = slice(w * TOK, (w + 1) * TOK)
            out = lax.dot_general(out, proj_w_ref[...], TN, preferred_element_type=F32)
            out_ref[at, :] = (x_ref[at, :] + out).astype(BF16)
            leave.append(start(out_ref.at[pl.ds(w * TOK, TOK)], out_hbm.at[pl.ds(w * TOK, TOK)]))

        attend_windows(
            lambda w, at: qkv_ref[w * TOK : (w + 1) * TOK, at : at + 128],
            lambda w: id_ref[w * TOK : (w + 1) * TOK, :],
            count // TOK,
            inner,
            finish,
        )
        send_classes(plan, rows_of(plan, rows_ref, "send_two"), out_ref, plan.two, flags_ref[1], piece_outs)
        for copy in leave:
            copy.wait()

    outs = shapes([count], width, pltpu.HBM) + [shape for size in plan.two for shape in shapes(size, width)]
    scratch = [
        pltpu.VMEM((sum(plan.one[-1]), width), BF16),
        pltpu.VMEM((count, width), F32),
        pltpu.VMEM((count, 3 * inner), BF16),
        pltpu.VMEM((count, width), BF16),
    ]
    args = [flags, x_own, *pieces, key_id, w_qkv, w_proj, rows]
    in_specs = [SMEM] + [VMEM] * (len(args) - 1)
    out, *sent = call(body, outs, args, in_specs, scratch, count // TOK, 3 << 30, 6 << 20)
    return out, sent


def coarse_level(flags, fine, x_own, pieces, key_id, weights, rows, plan):
    count = key_id.shape[0]
    width = weights[0][0].shape[1]
    own, half = fine.shape
    inner = CHUNK * len(weights[2])
    kinds = 3 * len(plan.three)
    chunks = [chunk for w in weights for chunk in w]

    def product(x, refs):
        parts = [
            jnp.dot(x[:, n * CHUNK : (n + 1) * CHUNK], ref[...], preferred_element_type=F32)
            for n, ref in enumerate(refs)
        ]
        return functools.reduce(jnp.add, parts)

    def body(flags_ref, fine_hbm, own_ref, *refs):
        piece_refs, refs = refs[: len(pieces)], refs[len(pieces) :]
        chunk_refs, refs = refs[: len(chunks)], refs[len(chunks) :]
        merge_refs = chunk_refs[: len(weights[0])]
        qkv_refs = chunk_refs[len(weights[0]) : -len(weights[2])]
        (proj_w_ref,) = chunk_refs[-len(weights[2]) :]
        id_ref, rows_ref, out_ref, *refs = refs
        piece_outs, (source_ref, qkv_ref, fine_ref, sems) = refs[:kinds], refs[kinds:]
        needs_fine = flags_ref[2] == 1

        @pl.when(needs_fine)
        def _():
            pltpu.make_async_copy(fine_hbm, fine_ref, sems.at[0]).start()

        lay_pieces(piece_refs, plan.two, flags_ref[1], source_ref)
        take = columns_of(rows_of(plan, rows_ref, "take_two"), 4 * count) - float(own)
        x = own_ref[...].astype(F32) + select_rows(take, source_ref[...])
        x = jnp.concatenate([x[n * count : (n + 1) * count] for n in range(4)], axis=1)
        stacked = layer_norm(x).astype(BF16)
        merged = product(stacked, merge_refs).astype(BF16).astype(F32)
        normed = layer_norm(merged).astype(BF16)
        qkv_ref[...] = product(normed, qkv_refs).astype(BF16)

        def finish(w, out):
            out = lax.dot_general(out, proj_w_ref[...], TN, preferred_element_type=F32)
            out_ref[...] = (merged + out).astype(BF16)

        attend_windows(lambda w, at: qkv_ref[:, at : at + 128], lambda w: id_ref[...], 1, inner, finish)
        for n, (sizes, fine_sizes) in enumerate(zip(plan.three, plan.four)):

            @pl.when(flags_ref[2] == n)
            def _():
                sent = select_rows(columns_of(rows_of(plan, rows_ref, "send_three"), sum(sizes)), out_ref[...])
                sent = sent.astype(BF16)
                at = 0
                for ref, size in zip(piece_outs[3 * n :], sizes):
                    ref[:size, :] = sent[at : at + size, :half]
                    ref[size : 2 * size, :] = sent[at : at + size, half:]
                    at += size
                if sum(fine_sizes):
                    pltpu.make_async_copy(fine_hbm, fine_ref, sems.at[0]).wait()
                    index = columns_of(rows_of(plan, rows_ref, "send_four"), sum(fine_sizes))
                    sent = select_rows(index, fine_ref[...]).astype(BF16)
                    at = 0
                    for ref, size, more in zip(piece_outs[3 * n :], sizes, fine_sizes):
                        ref[2 * size :, :] = sent[at : at + more]
                        at += more

    outs = shapes([count], width)
    for sizes, fine_sizes in zip(plan.three, plan.four):
        outs += shapes([2 * n + m for n, m in zip(sizes, fine_sizes)], half)
    scratch = [pltpu.VMEM((sum(plan.two[-1]), half), BF16), pltpu.VMEM((count, 3 * inner), BF16)]
    scratch += [pltpu.VMEM(fine.shape, BF16)]
    args = [flags, fine, x_own, *pieces, *chunks, key_id, rows]
    in_specs = [SMEM, HBM] + [VMEM] * (len(args) - 2)
    out, *sent = call(body, outs, args, in_specs, scratch, 1, 3 << 30, 12 << 20)
    return out, sent


def fine_output(flags, fine, pieces, rows, plan, block_rows, block_cols, partial):
    own, width = fine.shape

    def body(flags_ref, fine_hbm, *refs):
        piece_refs, (rows_ref, out_ref, source_ref, fine_ref, sems) = refs[: len(pieces)], refs[len(pieces) :]
        held = Copies(sems)(fine_hbm, fine_ref)
        lay_pieces(piece_refs, plan.two, flags_ref[1], source_ref)
        take = columns_of(rows_of(plan, rows_ref, "fine_out"), own)
        held.wait()
        out = select_rows(take, fine_ref[...]) + select_rows(take - float(own), source_ref[...])
        out_ref[...] = (out if partial else out.reshape(out_ref.shape)).astype(BF16)

    outs = [jax.ShapeDtypeStruct((2, block_rows, block_cols, width), BF16)]
    if partial:
        outs = shapes([own], width)
    scratch = [pltpu.VMEM((sum(plan.two[-1]), width), BF16), pltpu.VMEM(fine.shape, BF16)]
    args = [flags, fine, *pieces, rows]
    return call(body, outs, args, [SMEM, HBM] + [VMEM] * (len(args) - 2), scratch, 1, 1 << 30, 4 << 20)[0]


def coarse_output(coarse, got, rows, which, plan, block_rows, block_cols, part=None):
    own, width = coarse.shape
    half = width // 2
    sizes, more = plan.three[which], plan.four[which]
    parts = [] if part is None else [part]

    def body(coarse_ref, *refs):
        got_refs, refs = refs[:3], refs[3:]
        part_refs, (rows_ref, out_ref, *fine_outs, _) = refs[: len(parts)], refs[len(parts) :]
        back = [
            jnp.concatenate([ref[:size, :], ref[size : 2 * size, :]], axis=1) for ref, size in zip(got_refs, sizes)
        ]
        take = columns_of(rows_of(plan, rows_ref, "coarse_out"), own)
        out = select_rows(take, stack_rows([coarse_ref[...]] + back)).astype(BF16)
        for n in range(own // 2):
            out_ref[n // block_cols, n % block_cols] = out[2 * n : 2 * n + 2]
        for part_ref, fine_ref in zip(part_refs, fine_outs):
            fine = stack_rows([ref[2 * size :, :] for ref, size in zip(got_refs, sizes)])
            base = part_ref.shape[0] + sum(plan.two[-1])
            take = columns_of(rows_of(plan, rows_ref, "fine_out"), part_ref.shape[0]) - float(base)
            out = part_ref[...].astype(F32) + select_rows(take, fine)
            fine_ref[...] = out.reshape(fine_ref.shape).astype(BF16)

    outs = [jax.ShapeDtypeStruct((block_rows, block_cols, 2, width), BF16)]
    outs += [jax.ShapeDtypeStruct((2, 2 * block_rows, 2 * block_cols, half), BF16) for _ in parts]
    args = [coarse, *got, *parts, rows]
    out, *fine = call(body, outs, args, [VMEM] * len(args), [], 1, 1 << 28, 1 << 20)
    return out.transpose(2, 0, 1, 3), *fine


def on_device(tokens, regions, shifts, fine_qkv, fine_proj, merge_weight, coarse_qkv, coarse_proj):
    _, rows, cols, _ = tokens.shape
    plan = Plan(rows, cols)

    def first(which, sign, sent, *args):
        return exchange_class(sent, which, sign), before_fine(*args, plan)

    def second(which, sign, sent, *args):
        return exchange_class(sent, which, sign), before_coarse(*args, plan)

    def third(which, sign, sent, flags, fine, pieces, coarse, table):
        got = exchange(sent[3 * which : 3 * which + 3], sign)
        fine_out = fine_output(flags, fine, pieces, table, plan, rows, cols, which == 1)
        place = (table, which, plan, rows // 2, cols // 2)
        if which == 1:
            coarse_out, fine_out = coarse_output(coarse, got, *place, part=fine_out)
        else:
            (coarse_out,) = coarse_output(coarse, got, *place)
        return fine_out, coarse_out

    def branches(stage, pairs):
        return [functools.partial(stage, which, sign) for which, sign in pairs]

    sent, table, flags, one, two, three = first_pieces(shifts, tokens, plan)
    got, (fine_id, coarse_id, x, weights) = choose(
        one, branches(first, plan.one_branches), sent, flags, regions, tokens, table, [fine_qkv, fine_proj]
    )
    fine, sent = fine_level(flags, x, got, fine_id, *weights, table, plan)
    weights = [merge_weight, coarse_qkv, coarse_proj]
    got, (x, weights) = choose(two, branches(second, plan.two_branches), sent, fine, table, weights)
    coarse, sent = coarse_level(flags, fine, x, got, coarse_id, weights, table, plan)
    return choose(three, branches(third, plan.three_branches), sent, flags, fine, got, coarse, table)


def solution(mesh):
    return jax.shard_map(
        on_device,
        mesh=mesh,
        in_specs=(P(None, "lat", "lon", None), P(), P(), P(), P(), P(), P(), P()),
        out_specs=(P(None, "lat", "lon", None), P(None, "lat", "lon", None)),
        check_vma=False,
    )
```

```python
import functools

import jax
import jax.numpy as jnp
import numpy as np
from jax import lax
from jax.experimental import pallas as pl
from jax.experimental.pallas import tpu as pltpu
from jax.sharding import PartitionSpec as P

HD = 32
WH = 6
WW = 12
TOK = 2 * WH * WW
EPS = 1e-05
BIG = 1e30
SCALE = float(np.log2(np.e) / np.sqrt(HD))

NT = (((1,), (1,)), ((), ()))
TN = (((0,), (0,)), ((), ()))
F32 = jnp.float32
BF16 = jnp.bfloat16
I32 = jnp.int32

PAIRS = [(WH - 1, t) for t in range(1, WH)] + [(t, WH - 1) for t in range(1, WH - 1)]


def up16(count):
    return -(-count // 16) * 16


def natural(rows, cols):
    return [(l, r, c) for l in range(2) for r in range(rows) for c in range(cols)]


def windowed(rows, cols):
    return [
        (l, wr * WH + r, wc * WW + c)
        for wr in range(rows // WH)
        for wc in range(cols // WW)
        for l in range(2)
        for r in range(WH)
        for c in range(WW)
    ]


def moved(order, d):
    return [(l, r + d, c + 2 * d) for l, r, c in order]


def exchange_places(held, wanted, rows, cols, sign):
    at = {place: n for n, place in enumerate(held)}
    found = []
    for dr, dc in ((sign, 0), (0, sign), (sign, sign)):
        numbers, places = [], []
        for l, r, c in sorted(set(wanted) - set(held)):
            n = at.get((l, r - dr * rows, c - dc * cols))
            if n is not None:
                numbers.append(n)
                places.append((l, r, c))
        found.append((numbers, places))
    return found


def offsets(t0, t1):
    a = t0 if t0 <= 2 else t0 - WH
    big_a = t1 if t1 <= 2 else t1 - WH
    ahead = 1 if 2 * big_a > a or 2 * big_a - a == 0 and a < 0 else -1
    return a, big_a, ahead


def classes_of(needs, limits):
    which = [next(n for n, limit in enumerate(limits) if need[1] <= limit) for need in needs]
    sizes = [
        [up16(max(need[k] for need, w in zip(needs, which) if w == n)) for k in range(3)]
        for n in range(len(limits))
    ]
    return sizes, which


class Plan:
    def __init__(self, rows, cols):
        crows, ccols = rows // 2, cols // 2
        block, cblock = natural(rows, cols), natural(crows, ccols)
        cases = []
        for t0, t1 in PAIRS:
            a, big_a, ahead = offsets(t0, t1)
            fine = moved(windowed(rows, cols), a)
            coarse = moved(cblock, big_a)
            quarters = [
                (l, 2 * r + dr, 2 * c + dc)
                for dr, dc in ((0, 0), (1, 0), (0, 1), (1, 1))
                for l, r, c in coarse
            ]
            come = 1 if a > 0 else -1
            one = exchange_places(block, fine, rows, cols, come)
            home = [p for p in block if p not in set(fine)]
            wanted = quarters + (home if come == -ahead else [])
            two = exchange_places(fine, wanted, rows, cols, ahead)
            back = 1 if big_a < 0 else -1
            three = exchange_places(coarse, cblock, crows, ccols, back)
            got = set(fine).union(*[places for _, places in two])
            four = exchange_places(fine, [p for p in block if p not in got], rows, cols, back)
            cases.append((come, ahead, back, fine, coarse, quarters, one, two, three, four))

        def needs(which):
            return [[len(numbers) for numbers, _ in case[which]] for case in cases]

        self.one, one_class = classes_of(needs(6), [64, 512])
        self.two, two_class = classes_of(needs(7), [64, 128, 512])
        fine_back = [max(need) > 0 for need in needs(9)]
        self.three = []
        self.four = []
        for with_fine in (False, True):
            inside = [n for n, flag in enumerate(fine_back) if flag == with_fine]
            self.three.append([up16(max(needs(8)[n][k] for n in inside)) for k in range(3)])
            self.four.append([up16(max(needs(9)[n][k] for n in inside)) for k in range(3)])
        three_class = [int(flag) for flag in fine_back]

        def branches(which_class, direction):
            pairs = [(n, case[direction]) for n, case in zip(which_class, cases)]
            found = sorted(set(pairs))
            return found, [found.index(pair) for pair in pairs]

        self.one_branches, one_at = branches(one_class, 0)
        self.two_branches, two_at = branches(two_class, 1)
        self.three_branches, three_at = branches(three_class, 2)
        self.flags = dict(
            one_class=one_class, two_class=two_class, three_class=three_class,
            one_at=one_at, two_at=two_at, three_at=three_at,
            a=[offsets(*pair)[0] for pair in PAIRS], big_a=[offsets(*pair)[1] for pair in PAIRS],
        )

        found = {}
        for n, (come, ahead, back, fine, coarse, quarters, one, two, three, four) in enumerate(cases):

            def send(exchanged, room):
                return [n for (numbers, _), size in zip(exchanged, room) for n in numbers + [-1] * (size - len(numbers))]

            def source(held, *exchanges):
                places = list(held)
                for exchanged, room in exchanges:
                    for (_, got), size in zip(exchanged, room):
                        places += got + [None] * (size - len(got))
                return {p: n for n, p in enumerate(places) if p is not None}

            w = three_class[n]
            first, second = source(block, (one, self.one[-1])), source(fine, (two, self.two[-1]))
            third = source(coarse, (three, self.three[w]))
            last = source(fine, (two, self.two[-1]), (four, self.four[w]))
            out = [(l, r, c) for r in range(crows) for c in range(ccols) for l in range(2)]
            rows_of = dict(
                send_one=send(one, self.one[one_class[n]]),
                take_one=[first[p] for p in fine],
                send_two=send(two, self.two[two_class[n]]),
                take_two=[second[p] for p in quarters],
                send_three=send(three, self.three[w]),
                send_four=send(four, self.four[w]),
                fine_out=[last[p] for p in block],
                coarse_out=[third[p] for p in out],
            )
            for name, row in rows_of.items():
                found.setdefault(name, []).append(row)
        parts, self.at, top = [], {}, 0
        for name, lists in found.items():
            length = -(-max(len(row) for row in lists) // 128)
            part = np.full((len(PAIRS), length * 128), -1, np.float32)
            for n, row in enumerate(lists):
                part[n, : len(row)] = row
            parts.append(part.reshape(len(PAIRS), length, 128))
            self.at[name] = (top, length)
            top += length
        parts.append(np.zeros((len(PAIRS), -top % 8, 128), np.float32))
        self.table = np.concatenate(parts, axis=1)


def case_of(shifts_ref):
    t0, t1 = shifts_ref[0], shifts_ref[1]
    return jnp.where(t0 == WH - 1, t1 - 1, t0 + WH - 2)


def lookup(values, case):
    out = jnp.int32(values[0])
    for n, value in enumerate(values[1:], 1):
        out = jnp.where(case == n, value, out)
    return out


def columns_of(rows, count):
    parts = [jnp.broadcast_to(rows[j : j + 1], (128, 128)).T for j in range(-(-count // 128))]
    return stack_rows(parts)[:count]


def select_rows(index, source):
    lane = lax.broadcasted_iota(I32, (1, 128), 1).astype(F32)
    size = source.shape[0]
    pick = [jnp.where(index == lane + float(at), 1.0, 0.0).astype(BF16) for at in range(0, size, 128)]
    pick = jnp.concatenate(pick, axis=1)[:, :size]
    return jnp.dot(pick, source, preferred_element_type=F32)


def stack_rows(parts):
    return parts[0] if len(parts) == 1 else jnp.concatenate(parts, axis=0)


def layer_norm(values):
    center = jnp.mean(values, axis=-1, keepdims=True)
    values = values - center
    spread = jnp.mean(values * values, axis=-1, keepdims=True)
    return values * lax.rsqrt(spread + EPS)


def attend_windows(qkv_of, id_of, windows, inner, finish):
    lane = lax.broadcasted_iota(I32, (1, 128), 1)
    forbid = jnp.where(lane < 8, BIG, 0.0).astype(BF16)
    groups = inner // 128
    units = [(w, g) for w in range(windows) for g in range(groups)]
    scores, weights, outs = {}, {}, {}

    def score(w, g):
        key_id = id_of(w)
        not_id = (key_id - 1).astype(BF16) * forbid
        q = qkv_of(w, g * 128)
        keys = jnp.concatenate([qkv_of(w, inner + g * 128), key_id], axis=1)
        queries = []
        for h in range(4):
            mine = jnp.where((lane >= h * HD) & (lane < (h + 1) * HD), 1.0, 0.0).astype(BF16)
            queries.append(jnp.concatenate([q * mine, not_id], axis=1))
        scores[w, g] = lax.dot_general(keys, stack_rows(queries), NT, preferred_element_type=F32)

    def soften(w, g):
        s = scores.pop((w, g))
        weight = jnp.exp2((s - jnp.max(s, axis=0, keepdims=True)) * SCALE)
        weights[w, g] = weight.astype(BF16), 1.0 / jnp.sum(weight, axis=0, keepdims=True)

    def gather(w, g):
        weight, scale = weights.pop((w, g))
        out = lax.dot_general(qkv_of(w, 2 * inner + g * 128), weight, TN, preferred_element_type=F32) * scale
        outs[w, g] = [out[h * HD : (h + 1) * HD, h * TOK : (h + 1) * TOK] for h in range(4)]
        if g == groups - 1:
            finish(w, stack_rows([part for k in range(groups) for part in outs.pop((w, k))]).astype(BF16))

    for n in range(len(units) + 2):
        if n < len(units):
            score(*units[n])
        if 0 <= n - 1 < len(units):
            soften(*units[n - 1])
        if 0 <= n - 2 < len(units):
            gather(*units[n - 2])


ANY = pl.BlockSpec(memory_space=pl.ANY)
HBM = pl.BlockSpec(memory_space=pltpu.HBM)
VMEM = pl.BlockSpec(memory_space=pltpu.VMEM)
SMEM = pl.BlockSpec(memory_space=pltpu.SMEM)


def call(body, outs, args, in_specs, scratch, copies, flops, moved_bytes, vmem=8):
    args = [
        pltpu.with_memory_space_constraint(arg, spec.memory_space) for arg, spec in zip(args, in_specs, strict=True)
    ]
    spaces = [getattr(out, "memory_space", pltpu.SMEM if out.dtype == I32 else pltpu.VMEM) for out in outs]
    out_specs = [pl.BlockSpec(memory_space=space) for space in spaces]
    return pl.pallas_call(
        body,
        out_shape=outs,
        in_specs=in_specs,
        out_specs=out_specs,
        scratch_shapes=list(scratch) + [pltpu.SemaphoreType.DMA((copies,))],
        compiler_params=pltpu.CompilerParams(vmem_limit_bytes=vmem << 20),
        cost_estimate=pl.CostEstimate(flops=flops, bytes_accessed=moved_bytes, transcendentals=0),
    )(*args)


def shapes(sizes, width, space=pltpu.VMEM):
    return [space((n, width), BF16) for n in sizes]


class Copies:
    def __init__(self, sems):
        self.sems, self.used = sems, 0

    def __call__(self, src, dst):
        copy = pltpu.make_async_copy(src, dst, self.sems.at[self.used])
        self.used += 1
        copy.start()
        return copy


def lay_pieces(refs, sizes, which, source):
    for n, size in enumerate(sizes):

        @pl.when(which == n)
        def _():
            at = 0
            for ref, rows, room in zip(refs[3 * n : 3 * n + 3], size, sizes[-1]):
                source[at : at + rows, :] = ref[...]
                if rows < room:
                    source[at + rows : at + room, :] = jnp.zeros((room - rows, source.shape[1]), source.dtype)
                at += room


def flat(ref):
    layers, rows, cols, width = ref.shape
    return ref[...].astype(F32).reshape(layers * rows * cols, width).astype(BF16)


def put_pieces(value, refs):
    at = 0
    for ref in refs:
        ref[...] = value[at : at + ref.shape[0]].astype(BF16)
        at += ref.shape[0]


def rows_of(plan, table_ref, name, *lead):
    top, length = plan.at[name]
    return table_ref[(*lead, slice(top, top + length), slice(None))]


def send_classes(plan, rows, source_ref, sizes, which, refs):
    for n, size in enumerate(sizes):

        @pl.when(which == n)
        def _():
            put_pieces(select_rows(columns_of(rows, sum(size)), source_ref[...]), refs[3 * n : 3 * n + 3])


def exchange(pieces, sign):
    lat, lon = lax.axis_size("lat"), lax.axis_size("lon")
    row, col, both = pieces
    pairs = [((i + sign) % lat * lon + (j + sign) % lon, i * lon + j) for i in range(lat) for j in range(lon)]
    col = lax.ppermute(col, "lon", [((j + sign) % lon, j) for j in range(lon)])
    both = lax.ppermute(both, ("lat", "lon"), pairs)
    row = lax.ppermute(row, "lat", [((i + sign) % lat, i) for i in range(lat)])
    return [row, col, both]


def unused(like):
    outs = [jax.ShapeDtypeStruct(x.shape, x.dtype) for x in like]
    return pl.pallas_call(lambda *refs: None, out_shape=outs, out_specs=[ANY] * len(outs))()


def choose(index, branches, *args):
    flat_args, tree = jax.tree.flatten(args)
    out_trees = []

    def closed(branch):
        def run(*leaves):
            out, out_tree = jax.tree.flatten(branch(*jax.tree.unflatten(tree, leaves)))
            out_trees.append(out_tree)
            return out

        return jax.make_jaxpr(run)(*flat_args)

    out = lax.cond_p.bind(index, *flat_args, branches=tuple(closed(branch) for branch in branches))
    return jax.tree.unflatten(out_trees[0], out)


def exchange_class(sent, which, sign):
    got = []
    for n in range(len(sent) // 3):
        mine = sent[3 * n : 3 * n + 3]
        got += exchange(mine, sign) if n == which else unused(mine)
    return got


FLAGS = ("one_class", "two_class", "three_class", "a", "big_a")


def first_pieces(shifts, tokens, plan):
    width = tokens.shape[-1]
    count = tokens.size // width
    sizes = plan.one
    kinds = 3 * len(sizes)

    def body(shifts_hbm, tokens_hbm, table_hbm, *refs):
        outs, refs = refs[:kinds], refs[kinds:]
        rows_ref, flags_ref, *at_refs, shifts_ref, tokens_ref, table_ref, source_ref, sems = refs
        start = Copies(sems)
        shift = start(shifts_hbm, shifts_ref)
        held = start(tokens_hbm, tokens_ref)
        table = start(table_hbm, table_ref)
        shift.wait()
        case = case_of(shifts_ref)
        for ref, name in zip(at_refs, ("one_at", "two_at", "three_at")):
            ref[0] = lookup(plan.flags[name], case)
        for n, name in enumerate(FLAGS):
            flags_ref[n] = lookup(plan.flags[name], case)
        which = lookup(plan.flags["one_class"], case)
        held.wait()
        source_ref[...] = flat(tokens_ref)
        table.wait()
        rows_ref[...] = table_ref[case]
        send_classes(plan, rows_of(plan, table_ref, "send_one", case), source_ref, sizes, which, outs)

    outs = [shape for size in sizes for shape in shapes(size, width)]
    outs += [pltpu.VMEM(plan.table.shape[1:], F32), pltpu.SMEM((8,), I32)]
    outs += [jax.ShapeDtypeStruct((1,), I32)] * 3
    scratch = [pltpu.SMEM((2,), I32), pltpu.VMEM(tokens.shape, BF16), pltpu.VMEM(plan.table.shape, F32)]
    scratch += [pltpu.VMEM((count, width), BF16)]
    got = call(body, outs, [shifts, tokens, plan.table], [HBM] * 3, scratch, 3, 1 << 28, 1 << 20)
    sent, (rows, flags, one, two, three) = got[:kinds], got[kinds:]
    return sent, rows, flags, one[0], two[0], three[0]


def before_fine(flags, regions, tokens, table, weights, plan):
    _, lat, lon = regions.shape
    _, rows, cols, width = tokens.shape
    flat_regions = regions.reshape(2 * lat, lon)
    fine, coarse = windowed(rows, cols), natural(rows // 2, cols // 2)
    places = np.asarray(fine + coarse, np.float32)
    places[len(fine) :, 1:] *= 2
    pad = -len(places) % 128
    places = np.pad(places, ((0, pad), (0, 0))).T.reshape(3, -1, 128)
    is_fine = np.pad(np.ones(len(fine), np.float32), (0, len(coarse) + pad)).reshape(1, -1, 128)
    places = np.concatenate([places, is_fine])
    count = len(fine) + len(coarse)

    def body(flags_ref, rows_ref, regions_hbm, places_hbm, tokens_hbm, *refs):
        weights_hbm, refs = refs[: len(weights)], refs[len(weights) :]
        fine_ref, coarse_ref, x_ref, *refs = refs
        weight_refs, (regions_ref, places_ref, tokens_ref, sems) = refs[: len(weights)], refs[len(weights) :]
        start = Copies(sems)
        waits = [start(regions_hbm, regions_ref), start(places_hbm, places_ref)]
        held = start(tokens_hbm, tokens_ref)
        later = [start(src, dst) for src, dst in zip(weights_hbm, weight_refs)]
        for copy in waits:
            copy.wait()
        a = flags_ref[3].astype(F32)
        big_a = 2.0 * flags_ref[4].astype(F32)
        is_fine = places_ref[3]
        d = is_fine * a + (1.0 - is_fine) * big_a
        row = places_ref[1] + d + (lax.axis_index("lat") * rows).astype(F32)
        col = places_ref[2] + 2.0 * d + (lax.axis_index("lon") * cols).astype(F32)
        wrapped = jnp.where((row < 0) | (row >= lat), 4.0, 0.0)
        row = jnp.where(row < 0, row + lat, jnp.where(row >= lat, row - lat, row))
        col = jnp.where(col < 0, col + lon, jnp.where(col >= lon, col - lon, col))
        row = columns_of(row + places_ref[0] * lat, count)
        col = columns_of(col, count)
        wrapped = columns_of(wrapped, count)
        picked = select_rows(row, regions_ref[...].astype(F32).astype(BF16))
        ids = jnp.zeros((count, 128), F32)
        for at in range(0, lon, 128):
            size = min(128, lon - at)
            lane = lax.broadcasted_iota(I32, (1, size), 1).astype(F32) + float(at)
            here = jnp.where(lane == col[:, :size], picked[:, at : at + size], 0.0)
            ids = ids + jnp.sum(here, axis=1, keepdims=True)
        lane = lax.broadcasted_iota(I32, (1, 128), 1).astype(F32)
        hot = jnp.where(lane == ids + wrapped, 1.0, 0.0).astype(BF16)
        fine_ref[...] = hot[: len(fine)]
        coarse_ref[...] = hot[len(fine) :]
        held.wait()
        take = columns_of(rows_of(plan, rows_ref, "take_one"), len(fine))
        x_ref[...] = select_rows(take, flat(tokens_ref)).astype(BF16)
        for copy in later:
            copy.wait()

    outs = shapes([len(fine), len(coarse)], 128) + shapes([len(fine)], width)
    outs += [pltpu.VMEM(w.shape, BF16) for w in weights]
    scratch = [pltpu.VMEM(flat_regions.shape, I32), pltpu.VMEM(places.shape, F32), pltpu.VMEM(tokens.shape, BF16)]
    args = [flags, table, flat_regions, places, tokens, *weights]
    in_specs = [SMEM, VMEM] + [HBM] * (3 + len(weights))
    fine_id, coarse_id, x, *weights = call(body, outs, args, in_specs, scratch, 3 + len(weights), 1 << 28, 4 << 20)
    return fine_id, coarse_id, x, weights


CHUNK = 512


def before_coarse(fine, table, weights, plan):
    own, width = fine.shape
    cuts = [(n, at) for n, w in enumerate(weights) for at in range(0, w.shape[0], CHUNK)]

    def body(rows_ref, fine_hbm, *refs):
        weights_hbm, refs = refs[: len(weights)], refs[len(weights) :]
        x_ref, *chunk_refs, fine_ref, sems = refs
        start = Copies(sems)
        held = start(fine_hbm, fine_ref)
        later = [start(weights_hbm[n].at[pl.ds(at, CHUNK)], ref) for (n, at), ref in zip(cuts, chunk_refs)]
        take = columns_of(rows_of(plan, rows_ref, "take_two"), x_ref.shape[0])
        held.wait()
        x_ref[...] = select_rows(take, fine_ref[...]).astype(BF16)
        for copy in later:
            copy.wait()

    outs = shapes([own], width) + [pltpu.VMEM((CHUNK, weights[n].shape[1]), BF16) for n, _ in cuts]
    size = sum(2 * w.size for w in weights)
    args = [table, fine, *weights]
    in_specs = [VMEM] + [HBM] * (1 + len(weights))
    scratch = [pltpu.VMEM(fine.shape, BF16)]
    x, *chunks = call(body, outs, args, in_specs, scratch, 1 + len(cuts), 1 << 28, size)
    return x, [[chunk for (m, _), chunk in zip(cuts, chunks) if m == n] for n in range(len(weights))]


def fine_level(flags, x_own, pieces, key_id, w_qkv, w_proj, rows, plan):
    count, width = x_own.shape
    inner = w_proj.shape[0]
    kinds = 3 * len(plan.two)

    def body(flags_ref, own_ref, *refs):
        piece_refs, refs = refs[: len(pieces)], refs[len(pieces) :]
        id_ref, qkv_w_ref, proj_w_ref, rows_ref, out_hbm, *refs = refs
        piece_outs, (source_ref, x_ref, qkv_ref, out_ref, sems) = refs[:kinds], refs[kinds:]
        start = Copies(sems)
        leave = []
        lay_pieces(piece_refs, plan.one, flags_ref[0], source_ref)
        take = columns_of(rows_of(plan, rows_ref, "take_one"), count) - float(count)
        x = own_ref[...].astype(F32) + select_rows(take, source_ref[...])
        x_ref[...] = x
        normed = layer_norm(x).astype(BF16)
        qkv_ref[...] = jnp.dot(normed, qkv_w_ref[...], preferred_element_type=F32).astype(BF16)

        def finish(w, out):
            at = slice(w * TOK, (w + 1) * TOK)
            out = lax.dot_general(out, proj_w_ref[...], TN, preferred_element_type=F32)
            out_ref[at, :] = (x_ref[at, :] + out).astype(BF16)
            leave.append(start(out_ref.at[pl.ds(w * TOK, TOK)], out_hbm.at[pl.ds(w * TOK, TOK)]))

        attend_windows(
            lambda w, at: qkv_ref[w * TOK : (w + 1) * TOK, at : at + 128],
            lambda w: id_ref[w * TOK : (w + 1) * TOK, :],
            count // TOK,
            inner,
            finish,
        )
        send_classes(plan, rows_of(plan, rows_ref, "send_two"), out_ref, plan.two, flags_ref[1], piece_outs)
        for copy in leave:
            copy.wait()

    outs = shapes([count], width, pltpu.HBM) + [shape for size in plan.two for shape in shapes(size, width)]
    scratch = [
        pltpu.VMEM((sum(plan.one[-1]), width), BF16),
        pltpu.VMEM((count, width), F32),
        pltpu.VMEM((count, 3 * inner), BF16),
        pltpu.VMEM((count, width), BF16),
    ]
    args = [flags, x_own, *pieces, key_id, w_qkv, w_proj, rows]
    in_specs = [SMEM] + [VMEM] * (len(args) - 1)
    out, *sent = call(body, outs, args, in_specs, scratch, count // TOK, 3 << 30, 6 << 20, 14)
    return out, sent


def coarse_level(flags, fine, x_own, pieces, key_id, weights, rows, plan):
    count = key_id.shape[0]
    width = weights[0][0].shape[1]
    own, half = fine.shape
    inner = CHUNK * len(weights[2])
    kinds = 3 * len(plan.three)
    chunks = [chunk for w in weights for chunk in w]

    def product(x, refs):
        parts = [
            jnp.dot(x[:, n * CHUNK : (n + 1) * CHUNK], ref[...], preferred_element_type=F32)
            for n, ref in enumerate(refs)
        ]
        return functools.reduce(jnp.add, parts)

    def body(flags_ref, fine_hbm, own_ref, *refs):
        piece_refs, refs = refs[: len(pieces)], refs[len(pieces) :]
        chunk_refs, refs = refs[: len(chunks)], refs[len(chunks) :]
        merge_refs = chunk_refs[: len(weights[0])]
        qkv_refs = chunk_refs[len(weights[0]) : -len(weights[2])]
        (proj_w_ref,) = chunk_refs[-len(weights[2]) :]
        id_ref, rows_ref, out_ref, *refs = refs
        piece_outs, (source_ref, qkv_ref, fine_ref, sems) = refs[:kinds], refs[kinds:]
        needs_fine = flags_ref[2] == 1

        @pl.when(needs_fine)
        def _():
            pltpu.make_async_copy(fine_hbm, fine_ref, sems.at[0]).start()

        lay_pieces(piece_refs, plan.two, flags_ref[1], source_ref)
        take = columns_of(rows_of(plan, rows_ref, "take_two"), 4 * count) - float(own)
        x = own_ref[...].astype(F32) + select_rows(take, source_ref[...])
        x = jnp.concatenate([x[n * count : (n + 1) * count] for n in range(4)], axis=1)
        stacked = layer_norm(x).astype(BF16)
        merged = product(stacked, merge_refs).astype(BF16).astype(F32)
        normed = layer_norm(merged).astype(BF16)
        qkv_ref[...] = product(normed, qkv_refs).astype(BF16)

        def finish(w, out):
            out = lax.dot_general(out, proj_w_ref[...], TN, preferred_element_type=F32)
            out_ref[...] = (merged + out).astype(BF16)

        attend_windows(lambda w, at: qkv_ref[:, at : at + 128], lambda w: id_ref[...], 1, inner, finish)
        for n, (sizes, fine_sizes) in enumerate(zip(plan.three, plan.four)):

            @pl.when(flags_ref[2] == n)
            def _():
                sent = select_rows(columns_of(rows_of(plan, rows_ref, "send_three"), sum(sizes)), out_ref[...])
                sent = sent.astype(BF16)
                at = 0
                for ref, size in zip(piece_outs[3 * n :], sizes):
                    ref[:size, :] = sent[at : at + size, :half]
                    ref[size : 2 * size, :] = sent[at : at + size, half:]
                    at += size
                if sum(fine_sizes):
                    pltpu.make_async_copy(fine_hbm, fine_ref, sems.at[0]).wait()
                    index = columns_of(rows_of(plan, rows_ref, "send_four"), sum(fine_sizes))
                    sent = select_rows(index, fine_ref[...]).astype(BF16)
                    at = 0
                    for ref, size, more in zip(piece_outs[3 * n :], sizes, fine_sizes):
                        ref[2 * size :, :] = sent[at : at + more]
                        at += more

    outs = shapes([count], width)
    for sizes, fine_sizes in zip(plan.three, plan.four):
        outs += shapes([2 * n + m for n, m in zip(sizes, fine_sizes)], half)
    scratch = [pltpu.VMEM((sum(plan.two[-1]), half), BF16), pltpu.VMEM((count, 3 * inner), BF16)]
    scratch += [pltpu.VMEM(fine.shape, BF16)]
    args = [flags, fine, x_own, *pieces, *chunks, key_id, rows]
    in_specs = [SMEM, HBM] + [VMEM] * (len(args) - 2)
    out, *sent = call(body, outs, args, in_specs, scratch, 1, 3 << 30, 12 << 20, 14)
    return out, sent


def fine_output(flags, fine, pieces, rows, plan, block_rows, block_cols, partial):
    own, width = fine.shape

    def body(flags_ref, fine_hbm, *refs):
        piece_refs, (rows_ref, out_ref, source_ref, fine_ref, sems) = refs[: len(pieces)], refs[len(pieces) :]
        held = Copies(sems)(fine_hbm, fine_ref)
        lay_pieces(piece_refs, plan.two, flags_ref[1], source_ref)
        take = columns_of(rows_of(plan, rows_ref, "fine_out"), own)
        held.wait()
        out = select_rows(take, fine_ref[...]) + select_rows(take - float(own), source_ref[...])
        out_ref[...] = (out if partial else out.reshape(out_ref.shape)).astype(BF16)

    outs = [jax.ShapeDtypeStruct((2, block_rows, block_cols, width), BF16)]
    if partial:
        outs = shapes([own], width)
    scratch = [pltpu.VMEM((sum(plan.two[-1]), width), BF16), pltpu.VMEM(fine.shape, BF16)]
    args = [flags, fine, *pieces, rows]
    return call(body, outs, args, [SMEM, HBM] + [VMEM] * (len(args) - 2), scratch, 1, 1 << 30, 4 << 20)[0]


def coarse_output(coarse, got, rows, which, plan, block_rows, block_cols, part=None):
    own, width = coarse.shape
    half = width // 2
    sizes, more = plan.three[which], plan.four[which]
    parts = [] if part is None else [part]

    def body(coarse_ref, *refs):
        got_refs, refs = refs[:3], refs[3:]
        part_refs, (rows_ref, out_ref, *fine_outs, _) = refs[: len(parts)], refs[len(parts) :]
        back = [
            jnp.concatenate([ref[:size, :], ref[size : 2 * size, :]], axis=1) for ref, size in zip(got_refs, sizes)
        ]
        take = columns_of(rows_of(plan, rows_ref, "coarse_out"), own)
        out = select_rows(take, stack_rows([coarse_ref[...]] + back)).astype(BF16)
        for n in range(own // 2):
            out_ref[n // block_cols, n % block_cols] = out[2 * n : 2 * n + 2]
        for part_ref, fine_ref in zip(part_refs, fine_outs):
            fine = stack_rows([ref[2 * size :, :] for ref, size in zip(got_refs, sizes)])
            base = part_ref.shape[0] + sum(plan.two[-1])
            take = columns_of(rows_of(plan, rows_ref, "fine_out"), part_ref.shape[0]) - float(base)
            out = part_ref[...].astype(F32) + select_rows(take, fine)
            fine_ref[...] = out.reshape(fine_ref.shape).astype(BF16)

    outs = [jax.ShapeDtypeStruct((block_rows, block_cols, 2, width), BF16)]
    outs += [jax.ShapeDtypeStruct((2, 2 * block_rows, 2 * block_cols, half), BF16) for _ in parts]
    args = [coarse, *got, *parts, rows]
    out, *fine = call(body, outs, args, [VMEM] * len(args), [], 1, 1 << 28, 1 << 20)
    return out.transpose(2, 0, 1, 3), *fine


def on_device(tokens, regions, shifts, fine_qkv, fine_proj, merge_weight, coarse_qkv, coarse_proj):
    _, rows, cols, _ = tokens.shape
    plan = Plan(rows, cols)

    def first(which, sign, sent, *args):
        return exchange_class(sent, which, sign), before_fine(*args, plan)

    def second(which, sign, sent, *args):
        return exchange_class(sent, which, sign), before_coarse(*args, plan)

    def third(which, sign, sent, flags, fine, pieces, coarse, table):
        got = exchange(sent[3 * which : 3 * which + 3], sign)
        fine_out = fine_output(flags, fine, pieces, table, plan, rows, cols, which == 1)
        place = (table, which, plan, rows // 2, cols // 2)
        if which == 1:
            coarse_out, fine_out = coarse_output(coarse, got, *place, part=fine_out)
        else:
            (coarse_out,) = coarse_output(coarse, got, *place)
        return fine_out, coarse_out

    def branches(stage, pairs):
        return [functools.partial(stage, which, sign) for which, sign in pairs]

    sent, table, flags, one, two, three = first_pieces(shifts, tokens, plan)
    got, (fine_id, coarse_id, x, weights) = choose(
        one, branches(first, plan.one_branches), sent, flags, regions, tokens, table, [fine_qkv, fine_proj]
    )
    fine, sent = fine_level(flags, x, got, fine_id, *weights, table, plan)
    weights = [merge_weight, coarse_qkv, coarse_proj]
    got, (x, weights) = choose(two, branches(second, plan.two_branches), sent, fine, table, weights)
    coarse, sent = coarse_level(flags, fine, x, got, coarse_id, weights, table, plan)
    return choose(three, branches(third, plan.three_branches), sent, flags, fine, got, coarse, table)


def solution(mesh):
    return jax.shard_map(
        on_device,
        mesh=mesh,
        in_specs=(P(None, "lat", "lon", None), P(), P(), P(), P(), P(), P(), P()),
        out_specs=(P(None, "lat", "lon", None), P(None, "lat", "lon", None)),
        check_vma=False,
    )
```

```python
import functools

import jax
import jax.numpy as jnp
import numpy as np
from jax import lax
from jax.experimental import pallas as pl
from jax.experimental.pallas import tpu as pltpu
from jax.sharding import PartitionSpec as P

HD = 32
WH = 6
WW = 12
TOK = 2 * WH * WW
EPS = 1e-05
BIG = 1e30
SCALE = float(np.log2(np.e) / np.sqrt(HD))

NT = (((1,), (1,)), ((), ()))
F32 = jnp.float32
BF16 = jnp.bfloat16
I32 = jnp.int32

PAIRS = [(WH - 1, t) for t in range(1, WH)] + [(t, WH - 1) for t in range(1, WH - 1)]


def up16(count):
    return -(-count // 16) * 16


def natural(rows, cols):
    return [(l, r, c) for l in range(2) for r in range(rows) for c in range(cols)]


def windowed(rows, cols):
    return [
        (l, wr * WH + r, wc * WW + c)
        for wr in range(rows // WH)
        for wc in range(cols // WW)
        for l in range(2)
        for r in range(WH)
        for c in range(WW)
    ]


def moved(order, d):
    return [(l, r + d, c + 2 * d) for l, r, c in order]


def exchange_places(held, wanted, rows, cols, sign):
    at = {place: n for n, place in enumerate(held)}
    found = []
    for dr, dc in ((sign, 0), (0, sign), (sign, sign)):
        numbers, places = [], []
        for l, r, c in sorted(set(wanted) - set(held)):
            n = at.get((l, r - dr * rows, c - dc * cols))
            if n is not None:
                numbers.append(n)
                places.append((l, r, c))
        found.append((numbers, places))
    return found


def offsets(t0, t1):
    a = t0 if t0 <= 2 else t0 - WH
    big_a = t1 if t1 <= 2 else t1 - WH
    ahead = 1 if 2 * big_a > a or 2 * big_a - a == 0 and a < 0 else -1
    return a, big_a, ahead


def classes_of(needs, limits):
    which = [next(n for n, limit in enumerate(limits) if need[1] <= limit) for need in needs]
    sizes = [
        [up16(max(need[k] for need, w in zip(needs, which) if w == n)) for k in range(3)]
        for n in range(len(limits))
    ]
    return sizes, which


class Plan:
    def __init__(self, rows, cols):
        crows, ccols = rows // 2, cols // 2
        block, cblock = natural(rows, cols), natural(crows, ccols)
        cases = []
        for t0, t1 in PAIRS:
            a, big_a, ahead = offsets(t0, t1)
            fine = moved(windowed(rows, cols), a)
            coarse = moved(cblock, big_a)
            quarters = [
                (l, 2 * r + dr, 2 * c + dc)
                for dr, dc in ((0, 0), (1, 0), (0, 1), (1, 1))
                for l, r, c in coarse
            ]
            come = 1 if a > 0 else -1
            one = exchange_places(block, fine, rows, cols, come)
            home = [p for p in block if p not in set(fine)]
            wanted = quarters + (home if come == -ahead else [])
            two = exchange_places(fine, wanted, rows, cols, ahead)
            back = 1 if big_a < 0 else -1
            three = exchange_places(coarse, cblock, crows, ccols, back)
            got = set(fine).union(*[places for _, places in two])
            four = exchange_places(fine, [p for p in block if p not in got], rows, cols, back)
            cases.append((come, ahead, back, fine, coarse, quarters, one, two, three, four))

        def needs(which):
            return [[len(numbers) for numbers, _ in case[which]] for case in cases]

        self.one, one_class = classes_of(needs(6), [64, 512])
        self.two, two_class = classes_of(needs(7), [64, 128, 512])
        fine_back = [max(need) > 0 for need in needs(9)]
        self.three = []
        self.four = []
        for with_fine in (False, True):
            inside = [n for n, flag in enumerate(fine_back) if flag == with_fine]
            self.three.append([up16(max(needs(8)[n][k] for n in inside)) for k in range(3)])
            self.four.append([up16(max(needs(9)[n][k] for n in inside)) for k in range(3)])
        three_class = [int(flag) for flag in fine_back]

        def branches(which_class, direction):
            pairs = [(n, case[direction]) for n, case in zip(which_class, cases)]
            found = sorted(set(pairs))
            return found, [found.index(pair) for pair in pairs]

        self.one_branches, one_at = branches(one_class, 0)
        self.two_branches, two_at = branches(two_class, 1)
        self.three_branches, three_at = branches(three_class, 2)
        self.flags = dict(
            one_class=one_class, two_class=two_class, three_class=three_class,
            one_at=one_at, two_at=two_at, three_at=three_at,
            a=[offsets(*pair)[0] for pair in PAIRS], big_a=[offsets(*pair)[1] for pair in PAIRS],
        )

        found = {}
        for n, (come, ahead, back, fine, coarse, quarters, one, two, three, four) in enumerate(cases):

            def send(exchanged, room):
                return [n for (numbers, _), size in zip(exchanged, room) for n in numbers + [-1] * (size - len(numbers))]

            def source(held, *exchanges):
                places = list(held)
                for exchanged, room in exchanges:
                    for (_, got), size in zip(exchanged, room):
                        places += got + [None] * (size - len(got))
                return {p: n for n, p in enumerate(places) if p is not None}

            w = three_class[n]
            first, second = source(block, (one, self.one[-1])), source(fine, (two, self.two[-1]))
            third = source(coarse, (three, self.three[w]))
            last = source(fine, (two, self.two[-1]), (four, self.four[w]))
            out = [(l, r, c) for r in range(crows) for c in range(ccols) for l in range(2)]
            rows_of = dict(
                send_one=send(one, self.one[one_class[n]]),
                take_one=[first[p] for p in fine],
                send_two=send(two, self.two[two_class[n]]),
                take_two=[second[p] for p in quarters],
                send_three=send(three, self.three[w]),
                send_four=send(four, self.four[w]),
                fine_out=[last[p] for p in block],
                coarse_out=[third[p] for p in out],
            )
            for name, row in rows_of.items():
                found.setdefault(name, []).append(row)
        parts, self.at, top = [], {}, 0
        for name, lists in found.items():
            length = -(-max(len(row) for row in lists) // 128)
            part = np.full((len(PAIRS), length * 128), -1, np.float32)
            for n, row in enumerate(lists):
                part[n, : len(row)] = row
            parts.append(part.reshape(len(PAIRS), length, 128))
            self.at[name] = (top, length)
            top += length
        parts.append(np.zeros((len(PAIRS), -top % 8, 128), np.float32))
        self.table = np.concatenate(parts, axis=1)


def case_of(shifts_ref):
    t0, t1 = shifts_ref[0], shifts_ref[1]
    return jnp.where(t0 == WH - 1, t1 - 1, t0 + WH - 2)


def lookup(values, case):
    out = jnp.int32(values[0])
    for n, value in enumerate(values[1:], 1):
        out = jnp.where(case == n, value, out)
    return out


def columns_of(rows, count):
    parts = [jnp.broadcast_to(rows[j : j + 1], (128, 128)).T for j in range(-(-count // 128))]
    return stack_rows(parts)[:count]


def select_rows(index, source):
    lane = lax.broadcasted_iota(I32, (1, 128), 1).astype(F32)
    size = source.shape[0]
    pick = [jnp.where(index == lane + float(at), 1.0, 0.0).astype(BF16) for at in range(0, size, 128)]
    pick = jnp.concatenate(pick, axis=1)[:, :size]
    return jnp.dot(pick, source, preferred_element_type=F32)


def stack_rows(parts):
    return parts[0] if len(parts) == 1 else jnp.concatenate(parts, axis=0)


def layer_norm(values):
    center = jnp.mean(values, axis=-1, keepdims=True)
    values = values - center
    spread = jnp.mean(values * values, axis=-1, keepdims=True)
    return values * lax.rsqrt(spread + EPS)


def attend_windows(qkv_of, id_of, windows, inner, finish):
    lane = lax.broadcasted_iota(I32, (1, 128), 1)
    forbid = jnp.where(lane < 8, BIG, 0.0).astype(BF16)
    groups = inner // 128
    units = [(w, g) for w in range(windows) for g in range(groups)]
    scores, weights, outs = {}, {}, {}

    def score(w, g):
        key_id = id_of(w)
        not_id = (key_id - 1).astype(BF16) * forbid
        q = qkv_of(w, g * 128)
        keys = jnp.concatenate([qkv_of(w, inner + g * 128), key_id], axis=1)
        queries = []
        for h in range(4):
            mine = jnp.where((lane >= h * HD) & (lane < (h + 1) * HD), 1.0, 0.0).astype(BF16)
            queries.append(jnp.concatenate([q * mine, not_id], axis=1))
        scores[w, g] = lax.dot_general(stack_rows(queries), keys, NT, preferred_element_type=F32)

    def soften(w, g):
        s = scores.pop((w, g))
        weights[w, g] = jnp.exp2((s - jnp.max(s, axis=1, keepdims=True)) * SCALE).astype(BF16)

    def gather(w, g):
        v = qkv_of(w, 2 * inner + g * 128)
        values = jnp.concatenate([v, jnp.ones_like(v)], axis=1)
        out = jnp.dot(weights.pop((w, g)), values, preferred_element_type=F32)
        out = out[:, :128] * (1.0 / out[:, 128:])
        picked = out[:TOK]
        for h in range(1, 4):
            picked = jnp.where(lane < h * HD, picked, out[h * TOK : (h + 1) * TOK])
        outs[w, g] = picked.astype(BF16)
        if g == groups - 1:
            finish(w, jnp.concatenate([outs.pop((w, k)) for k in range(groups)], axis=1))

    for n in range(len(units) + 2):
        if n < len(units):
            score(*units[n])
        if 0 <= n - 1 < len(units):
            soften(*units[n - 1])
        if 0 <= n - 2 < len(units):
            gather(*units[n - 2])


ANY = pl.BlockSpec(memory_space=pl.ANY)
HBM = pl.BlockSpec(memory_space=pltpu.HBM)
VMEM = pl.BlockSpec(memory_space=pltpu.VMEM)
SMEM = pl.BlockSpec(memory_space=pltpu.SMEM)


def call(body, outs, args, in_specs, scratch, copies, flops, moved_bytes, vmem=8):
    args = [
        pltpu.with_memory_space_constraint(arg, spec.memory_space) for arg, spec in zip(args, in_specs, strict=True)
    ]
    spaces = [getattr(out, "memory_space", pltpu.SMEM if out.dtype == I32 else pltpu.VMEM) for out in outs]
    out_specs = [pl.BlockSpec(memory_space=space) for space in spaces]
    return pl.pallas_call(
        body,
        out_shape=outs,
        in_specs=in_specs,
        out_specs=out_specs,
        scratch_shapes=list(scratch) + [pltpu.SemaphoreType.DMA((copies,))],
        compiler_params=pltpu.CompilerParams(vmem_limit_bytes=vmem << 20),
        cost_estimate=pl.CostEstimate(flops=flops, bytes_accessed=moved_bytes, transcendentals=0),
    )(*args)


def shapes(sizes, width, space=pltpu.VMEM):
    return [space((n, width), BF16) for n in sizes]


class Copies:
    def __init__(self, sems):
        self.sems, self.used = sems, 0

    def __call__(self, src, dst):
        copy = pltpu.make_async_copy(src, dst, self.sems.at[self.used])
        self.used += 1
        copy.start()
        return copy


def lay_pieces(refs, sizes, which, source):
    for n, size in enumerate(sizes):

        @pl.when(which == n)
        def _():
            at = 0
            for ref, rows, room in zip(refs[3 * n : 3 * n + 3], size, sizes[-1]):
                source[at : at + rows, :] = ref[...]
                if rows < room:
                    source[at + rows : at + room, :] = jnp.zeros((room - rows, source.shape[1]), source.dtype)
                at += room


def flat(ref):
    layers, rows, cols, width = ref.shape
    return ref[...].astype(F32).reshape(layers * rows * cols, width).astype(BF16)


def put_pieces(value, refs):
    at = 0
    for ref in refs:
        ref[...] = value[at : at + ref.shape[0]].astype(BF16)
        at += ref.shape[0]


def rows_of(plan, table_ref, name, *lead):
    top, length = plan.at[name]
    return table_ref[(*lead, slice(top, top + length), slice(None))]


def send_classes(plan, rows, source_ref, sizes, which, refs):
    for n, size in enumerate(sizes):

        @pl.when(which == n)
        def _():
            put_pieces(select_rows(columns_of(rows, sum(size)), source_ref[...]), refs[3 * n : 3 * n + 3])


def exchange(pieces, sign):
    lat, lon = lax.axis_size("lat"), lax.axis_size("lon")
    row, col, both = pieces
    pairs = [((i + sign) % lat * lon + (j + sign) % lon, i * lon + j) for i in range(lat) for j in range(lon)]
    col = lax.ppermute(col, "lon", [((j + sign) % lon, j) for j in range(lon)])
    both = lax.ppermute(both, ("lat", "lon"), pairs)
    row = lax.ppermute(row, "lat", [((i + sign) % lat, i) for i in range(lat)])
    return [row, col, both]


def unused(like):
    outs = [jax.ShapeDtypeStruct(x.shape, x.dtype) for x in like]
    return pl.pallas_call(lambda *refs: None, out_shape=outs, out_specs=[ANY] * len(outs))()


def choose(index, branches, *args):
    flat_args, tree = jax.tree.flatten(args)
    out_trees = []

    def closed(branch):
        def run(*leaves):
            out, out_tree = jax.tree.flatten(branch(*jax.tree.unflatten(tree, leaves)))
            out_trees.append(out_tree)
            return out

        return jax.make_jaxpr(run)(*flat_args)

    out = lax.cond_p.bind(index, *flat_args, branches=tuple(closed(branch) for branch in branches))
    return jax.tree.unflatten(out_trees[0], out)


def exchange_class(sent, which, sign):
    got = []
    for n in range(len(sent) // 3):
        mine = sent[3 * n : 3 * n + 3]
        got += exchange(mine, sign) if n == which else unused(mine)
    return got


FLAGS = ("one_class", "two_class", "three_class", "a", "big_a")


def first_pieces(shifts, tokens, plan):
    width = tokens.shape[-1]
    count = tokens.size // width
    sizes = plan.one
    kinds = 3 * len(sizes)

    def body(shifts_hbm, tokens_hbm, table_hbm, *refs):
        outs, refs = refs[:kinds], refs[kinds:]
        rows_ref, flags_ref, *at_refs, shifts_ref, tokens_ref, table_ref, source_ref, sems = refs
        start = Copies(sems)
        shift = start(shifts_hbm, shifts_ref)
        held = start(tokens_hbm, tokens_ref)
        table = start(table_hbm, table_ref)
        shift.wait()
        case = case_of(shifts_ref)
        for ref, name in zip(at_refs, ("one_at", "two_at", "three_at")):
            ref[0] = lookup(plan.flags[name], case)
        for n, name in enumerate(FLAGS):
            flags_ref[n] = lookup(plan.flags[name], case)
        which = lookup(plan.flags["one_class"], case)
        held.wait()
        source_ref[...] = flat(tokens_ref)
        table.wait()
        rows_ref[...] = table_ref[case]
        send_classes(plan, rows_of(plan, table_ref, "send_one", case), source_ref, sizes, which, outs)

    outs = [shape for size in sizes for shape in shapes(size, width)]
    outs += [pltpu.VMEM(plan.table.shape[1:], F32), pltpu.SMEM((8,), I32)]
    outs += [jax.ShapeDtypeStruct((1,), I32)] * 3
    scratch = [pltpu.SMEM((2,), I32), pltpu.VMEM(tokens.shape, BF16), pltpu.VMEM(plan.table.shape, F32)]
    scratch += [pltpu.VMEM((count, width), BF16)]
    got = call(body, outs, [shifts, tokens, plan.table], [HBM] * 3, scratch, 3, 1 << 28, 1 << 20)
    sent, (rows, flags, one, two, three) = got[:kinds], got[kinds:]
    return sent, rows, flags, one[0], two[0], three[0]


def before_fine(flags, regions, tokens, table, weights, plan):
    _, lat, lon = regions.shape
    _, rows, cols, width = tokens.shape
    flat_regions = regions.reshape(2 * lat, lon)
    fine, coarse = windowed(rows, cols), natural(rows // 2, cols // 2)
    places = np.asarray(fine + coarse, np.float32)
    places[len(fine) :, 1:] *= 2
    pad = -len(places) % 128
    places = np.pad(places, ((0, pad), (0, 0))).T.reshape(3, -1, 128)
    is_fine = np.pad(np.ones(len(fine), np.float32), (0, len(coarse) + pad)).reshape(1, -1, 128)
    places = np.concatenate([places, is_fine])
    count = len(fine) + len(coarse)

    def body(flags_ref, rows_ref, regions_hbm, places_hbm, tokens_hbm, *refs):
        weights_hbm, refs = refs[: len(weights)], refs[len(weights) :]
        fine_ref, coarse_hbm, x_ref, *refs = refs
        weight_refs, (regions_ref, places_ref, tokens_ref, coarse_ref, sems) = refs[: len(weights)], refs[len(weights) :]
        start = Copies(sems)
        waits = [start(regions_hbm, regions_ref), start(places_hbm, places_ref)]
        held = start(tokens_hbm, tokens_ref)
        later = [start(src, dst) for src, dst in zip(weights_hbm, weight_refs)]
        for copy in waits:
            copy.wait()
        a = flags_ref[3].astype(F32)
        big_a = 2.0 * flags_ref[4].astype(F32)
        is_fine = places_ref[3]
        d = is_fine * a + (1.0 - is_fine) * big_a
        row = places_ref[1] + d + (lax.axis_index("lat") * rows).astype(F32)
        col = places_ref[2] + 2.0 * d + (lax.axis_index("lon") * cols).astype(F32)
        wrapped = jnp.where((row < 0) | (row >= lat), 4.0, 0.0)
        row = jnp.where(row < 0, row + lat, jnp.where(row >= lat, row - lat, row))
        col = jnp.where(col < 0, col + lon, jnp.where(col >= lon, col - lon, col))
        row = columns_of(row + places_ref[0] * lat, count)
        col = columns_of(col, count)
        wrapped = columns_of(wrapped, count)
        picked = select_rows(row, regions_ref[...].astype(F32).astype(BF16))
        ids = jnp.zeros((count, 128), F32)
        for at in range(0, lon, 128):
            size = min(128, lon - at)
            lane = lax.broadcasted_iota(I32, (1, size), 1).astype(F32) + float(at)
            here = jnp.where(lane == col[:, :size], picked[:, at : at + size], 0.0)
            ids = ids + jnp.sum(here, axis=1, keepdims=True)
        lane = lax.broadcasted_iota(I32, (1, 128), 1).astype(F32)
        hot = jnp.where(lane == ids + wrapped, 1.0, 0.0).astype(BF16)
        fine_ref[...] = hot[: len(fine)]
        coarse_ref[...] = hot[len(fine) :]
        later.append(start(coarse_ref, coarse_hbm))
        held.wait()
        take = columns_of(rows_of(plan, rows_ref, "take_one"), len(fine))
        x_ref[...] = select_rows(take, flat(tokens_ref)).astype(BF16)
        for copy in later:
            copy.wait()

    outs = shapes([len(fine)], 128) + shapes([len(coarse)], 128, pltpu.HBM) + shapes([len(fine)], width)
    outs += [pltpu.VMEM(w.shape, BF16) for w in weights]
    scratch = [pltpu.VMEM(flat_regions.shape, I32), pltpu.VMEM(places.shape, F32), pltpu.VMEM(tokens.shape, BF16)]
    scratch += [pltpu.VMEM((len(coarse), 128), BF16)]
    args = [flags, table, flat_regions, places, tokens, *weights]
    in_specs = [SMEM, VMEM] + [HBM] * (3 + len(weights))
    fine_id, coarse_id, x, *weights = call(body, outs, args, in_specs, scratch, 4 + len(weights), 1 << 28, 4 << 20)
    return fine_id, coarse_id, x, weights


def before_coarse(fine, table, plan):
    own, width = fine.shape

    def body(rows_ref, fine_hbm, x_ref, fine_ref, sems):
        held = Copies(sems)(fine_hbm, fine_ref)
        take = columns_of(rows_of(plan, rows_ref, "take_two"), own)
        held.wait()
        x_ref[...] = select_rows(take, fine_ref[...]).astype(BF16)

    scratch = [pltpu.VMEM(fine.shape, BF16)]
    return call(body, shapes([own], width), [table, fine], [VMEM, HBM], scratch, 1, 1 << 28, 1 << 20)[0]


def fine_level(flags, x_own, pieces, key_id, w_qkv, w_proj, rows, plan):
    count, width = x_own.shape
    inner = w_proj.shape[0]
    kinds = 3 * len(plan.two)

    def body(flags_ref, own_ref, *refs):
        piece_refs, refs = refs[: len(pieces)], refs[len(pieces) :]
        id_ref, qkv_w_ref, proj_w_ref, rows_ref, out_hbm, *refs = refs
        piece_outs, (source_ref, x_ref, qkv_ref, out_ref, sems) = refs[:kinds], refs[kinds:]
        start = Copies(sems)
        leave = []
        lay_pieces(piece_refs, plan.one, flags_ref[0], source_ref)
        take = columns_of(rows_of(plan, rows_ref, "take_one"), count) - float(count)
        x = own_ref[...].astype(F32) + select_rows(take, source_ref[...])
        x_ref[...] = x
        normed = layer_norm(x).astype(BF16)
        qkv_ref[...] = jnp.dot(normed, qkv_w_ref[...], preferred_element_type=F32).astype(BF16)

        def finish(w, out):
            at = slice(w * TOK, (w + 1) * TOK)
            out = jnp.dot(out, proj_w_ref[...], preferred_element_type=F32)
            out_ref[at, :] = (x_ref[at, :] + out).astype(BF16)
            leave.append(start(out_ref.at[pl.ds(w * TOK, TOK)], out_hbm.at[pl.ds(w * TOK, TOK)]))

        attend_windows(
            lambda w, at: qkv_ref[w * TOK : (w + 1) * TOK, at : at + 128],
            lambda w: id_ref[w * TOK : (w + 1) * TOK, :],
            count // TOK,
            inner,
            finish,
        )
        send_classes(plan, rows_of(plan, rows_ref, "send_two"), out_ref, plan.two, flags_ref[1], piece_outs)
        for copy in leave:
            copy.wait()

    outs = shapes([count], width, pltpu.HBM) + [shape for size in plan.two for shape in shapes(size, width)]
    scratch = [
        pltpu.VMEM((sum(plan.one[-1]), width), BF16),
        pltpu.VMEM((count, width), F32),
        pltpu.VMEM((count, 3 * inner), BF16),
        pltpu.VMEM((count, width), BF16),
    ]
    args = [flags, x_own, *pieces, key_id, w_qkv, w_proj, rows]
    in_specs = [SMEM] + [VMEM] * (len(args) - 1)
    out, *sent = call(body, outs, args, in_specs, scratch, count // TOK, 3 << 30, 6 << 20, 14)
    return out, sent


def coarse_level(flags, fine, x_own, pieces, key_id, w_merge, w_qkv, w_proj, rows, plan):
    count = key_id.shape[0]
    depth, width = w_merge.shape
    own, half = fine.shape
    inner = w_proj.shape[0]
    kinds = 3 * len(plan.three)

    def body(flags_ref, fine_hbm, id_hbm, merge_hbm, qkv_w_hbm, proj_w_hbm, own_ref, *refs):
        piece_refs, refs = refs[: len(pieces)], refs[len(pieces) :]
        rows_ref, out_ref, *refs = refs
        piece_outs, refs = refs[:kinds], refs[kinds:]
        source_ref, qkv_ref, fine_ref, id_ref, merge_ref, qkv_w_ref, proj_w_ref, sems = refs
        start = Copies(sems)

        def bring(src, dst):
            return [
                (at, start(src.at[pl.ds(at, half)], dst.at[pl.ds(at, half)])) for at in range(0, src.shape[0], half)
            ]

        def product(x, ref, copies):
            parts = []
            for at, copy in copies:
                copy.wait()
                parts.append(jnp.dot(x[:, at : at + half], ref[at : at + half, :], preferred_element_type=F32))
            return functools.reduce(jnp.add, parts)

        merge_w, qkv_w = bring(merge_hbm, merge_ref), bring(qkv_w_hbm, qkv_w_ref)
        ids, proj_w = start(id_hbm, id_ref), start(proj_w_hbm, proj_w_ref)
        fine_copy = (fine_hbm, fine_ref, sems.at[start.used])

        @pl.when(flags_ref[2] == 1)
        def _():
            pltpu.make_async_copy(*fine_copy).start()

        lay_pieces(piece_refs, plan.two, flags_ref[1], source_ref)
        take = columns_of(rows_of(plan, rows_ref, "take_two"), 4 * count) - float(own)
        x = own_ref[...].astype(F32) + select_rows(take, source_ref[...])
        x = jnp.concatenate([x[n * count : (n + 1) * count] for n in range(4)], axis=1)
        stacked = layer_norm(x).astype(BF16)
        merged = product(stacked, merge_ref, merge_w).astype(BF16).astype(F32)
        normed = layer_norm(merged).astype(BF16)
        qkv_ref[...] = product(normed, qkv_w_ref, qkv_w).astype(BF16)
        ids.wait()
        proj_w.wait()

        def finish(w, out):
            out = jnp.dot(out, proj_w_ref[...], preferred_element_type=F32)
            out_ref[...] = (merged + out).astype(BF16)

        attend_windows(lambda w, at: qkv_ref[:, at : at + 128], lambda w: id_ref[...], 1, inner, finish)
        for n, (sizes, fine_sizes) in enumerate(zip(plan.three, plan.four)):

            @pl.when(flags_ref[2] == n)
            def _():
                sent = select_rows(columns_of(rows_of(plan, rows_ref, "send_three"), sum(sizes)), out_ref[...])
                sent = sent.astype(BF16)
                at = 0
                for ref, size in zip(piece_outs[3 * n :], sizes):
                    ref[:size, :] = sent[at : at + size, :half]
                    ref[size : 2 * size, :] = sent[at : at + size, half:]
                    at += size
                if sum(fine_sizes):
                    pltpu.make_async_copy(*fine_copy).wait()
                    index = columns_of(rows_of(plan, rows_ref, "send_four"), sum(fine_sizes))
                    sent = select_rows(index, fine_ref[...]).astype(BF16)
                    at = 0
                    for ref, size, more in zip(piece_outs[3 * n :], sizes, fine_sizes):
                        ref[2 * size :, :] = sent[at : at + more]
                        at += more

    outs = shapes([count], width)
    for sizes, fine_sizes in zip(plan.three, plan.four):
        outs += shapes([2 * n + m for n, m in zip(sizes, fine_sizes)], half)
    scratch = [pltpu.VMEM((sum(plan.two[-1]), half), BF16), pltpu.VMEM((count, 3 * inner), BF16)]
    scratch += [pltpu.VMEM(x.shape, BF16) for x in (fine, key_id, w_merge, w_qkv, w_proj)]
    args = [flags, fine, key_id, w_merge, w_qkv, w_proj, x_own, *pieces, rows]
    in_specs = [SMEM] + [HBM] * 5 + [VMEM] * (len(args) - 6)
    copies = depth // half + width // half + 3
    out, *sent = call(body, outs, args, in_specs, scratch, copies, 3 << 30, 12 << 20, 24)
    return out, sent


def fine_output(flags, fine, pieces, rows, plan, block_rows, block_cols, partial):
    own, width = fine.shape

    def body(flags_ref, fine_hbm, *refs):
        piece_refs, (rows_ref, out_ref, source_ref, fine_ref, sems) = refs[: len(pieces)], refs[len(pieces) :]
        held = Copies(sems)(fine_hbm, fine_ref)
        lay_pieces(piece_refs, plan.two, flags_ref[1], source_ref)
        take = columns_of(rows_of(plan, rows_ref, "fine_out"), own)
        held.wait()
        out = select_rows(take, fine_ref[...]) + select_rows(take - float(own), source_ref[...])
        out_ref[...] = (out if partial else out.reshape(out_ref.shape)).astype(BF16)

    outs = [jax.ShapeDtypeStruct((2, block_rows, block_cols, width), BF16)]
    if partial:
        outs = shapes([own], width)
    scratch = [pltpu.VMEM((sum(plan.two[-1]), width), BF16), pltpu.VMEM(fine.shape, BF16)]
    args = [flags, fine, *pieces, rows]
    return call(body, outs, args, [SMEM, HBM] + [VMEM] * (len(args) - 2), scratch, 1, 1 << 30, 4 << 20)[0]


def coarse_output(coarse, got, rows, which, plan, block_rows, block_cols, part=None):
    own, width = coarse.shape
    half = width // 2
    sizes, more = plan.three[which], plan.four[which]
    parts = [] if part is None else [part]

    def body(coarse_ref, *refs):
        got_refs, refs = refs[:3], refs[3:]
        part_refs, (rows_ref, out_ref, *fine_outs, _) = refs[: len(parts)], refs[len(parts) :]
        back = [
            jnp.concatenate([ref[:size, :], ref[size : 2 * size, :]], axis=1) for ref, size in zip(got_refs, sizes)
        ]
        take = columns_of(rows_of(plan, rows_ref, "coarse_out"), own)
        out = select_rows(take, stack_rows([coarse_ref[...]] + back)).astype(BF16)
        for n in range(own // 2):
            out_ref[n // block_cols, n % block_cols] = out[2 * n : 2 * n + 2]
        for part_ref, fine_ref in zip(part_refs, fine_outs):
            fine = stack_rows([ref[2 * size :, :] for ref, size in zip(got_refs, sizes)])
            base = part_ref.shape[0] + sum(plan.two[-1])
            take = columns_of(rows_of(plan, rows_ref, "fine_out"), part_ref.shape[0]) - float(base)
            out = part_ref[...].astype(F32) + select_rows(take, fine)
            fine_ref[...] = out.reshape(fine_ref.shape).astype(BF16)

    outs = [jax.ShapeDtypeStruct((block_rows, block_cols, 2, width), BF16)]
    outs += [jax.ShapeDtypeStruct((2, 2 * block_rows, 2 * block_cols, half), BF16) for _ in parts]
    args = [coarse, *got, *parts, rows]
    out, *fine = call(body, outs, args, [VMEM] * len(args), [], 1, 1 << 28, 1 << 20)
    return out.transpose(2, 0, 1, 3), *fine


def on_device(tokens, regions, shifts, fine_qkv, fine_proj, merge_weight, coarse_qkv, coarse_proj):
    _, rows, cols, _ = tokens.shape
    plan = Plan(rows, cols)

    def first(which, sign, sent, *args):
        return exchange_class(sent, which, sign), before_fine(*args, plan)

    def second(which, sign, sent, *args):
        return exchange_class(sent, which, sign), before_coarse(*args, plan)

    def third(which, sign, sent, flags, fine, pieces, coarse, table):
        got = exchange(sent[3 * which : 3 * which + 3], sign)
        fine_out = fine_output(flags, fine, pieces, table, plan, rows, cols, which == 1)
        place = (table, which, plan, rows // 2, cols // 2)
        if which == 1:
            coarse_out, fine_out = coarse_output(coarse, got, *place, part=fine_out)
        else:
            (coarse_out,) = coarse_output(coarse, got, *place)
        return fine_out, coarse_out

    def branches(stage, pairs):
        return [functools.partial(stage, which, sign) for which, sign in pairs]

    sent, table, flags, one, two, three = first_pieces(shifts, tokens, plan)
    got, (fine_id, coarse_id, x, weights) = choose(
        one, branches(first, plan.one_branches), sent, flags, regions, tokens, table, [fine_qkv, fine_proj]
    )
    fine, sent = fine_level(flags, x, got, fine_id, *weights, table, plan)
    got, x = choose(two, branches(second, plan.two_branches), sent, fine, table)
    coarse, sent = coarse_level(
        flags, fine, x, got, coarse_id, merge_weight, coarse_qkv, coarse_proj, table, plan
    )
    return choose(three, branches(third, plan.three_branches), sent, flags, fine, got, coarse, table)


def solution(mesh):
    return jax.shard_map(
        on_device,
        mesh=mesh,
        in_specs=(P(None, "lat", "lon", None), P(), P(), P(), P(), P(), P(), P()),
        out_specs=(P(None, "lat", "lon", None), P(None, "lat", "lon", None)),
        check_vma=False,
    )
```

```python
import functools

import jax
import jax.numpy as jnp
import numpy as np
from jax import lax
from jax.experimental import pallas as pl
from jax.experimental.pallas import tpu as pltpu
from jax.sharding import PartitionSpec as P

HD = 32
WH = 6
WW = 12
TOK = 2 * WH * WW
EPS = 1e-05
BIG = 1e30
SCALE = float(np.log2(np.e) / np.sqrt(HD))

NT = (((1,), (1,)), ((), ()))
F32 = jnp.float32
BF16 = jnp.bfloat16
I32 = jnp.int32

PAIRS = [(WH - 1, t) for t in range(1, WH)] + [(t, WH - 1) for t in range(1, WH - 1)]


def up16(count):
    return -(-count // 16) * 16


def natural(rows, cols):
    return [(l, r, c) for l in range(2) for r in range(rows) for c in range(cols)]


def windowed(rows, cols):
    return [
        (l, wr * WH + r, wc * WW + c)
        for wr in range(rows // WH)
        for wc in range(cols // WW)
        for l in range(2)
        for r in range(WH)
        for c in range(WW)
    ]


def moved(order, d):
    return [(l, r + d, c + 2 * d) for l, r, c in order]


def exchange_places(held, wanted, rows, cols, sign):
    at = {place: n for n, place in enumerate(held)}
    found = []
    for dr, dc in ((sign, 0), (0, sign), (sign, sign)):
        numbers, places = [], []
        for l, r, c in sorted(set(wanted) - set(held)):
            n = at.get((l, r - dr * rows, c - dc * cols))
            if n is not None:
                numbers.append(n)
                places.append((l, r, c))
        found.append((numbers, places))
    return found


def offsets(t0, t1):
    a = t0 if t0 <= 2 else t0 - WH
    big_a = t1 if t1 <= 2 else t1 - WH
    ahead = 1 if 2 * big_a > a or 2 * big_a - a == 0 and a < 0 else -1
    return a, big_a, ahead


def classes_of(needs, limits):
    which = [next(n for n, limit in enumerate(limits) if need[1] <= limit) for need in needs]
    sizes = [
        [up16(max(need[k] for need, w in zip(needs, which) if w == n)) for k in range(3)]
        for n in range(len(limits))
    ]
    return sizes, which


class Plan:
    def __init__(self, rows, cols):
        crows, ccols = rows // 2, cols // 2
        block, cblock = natural(rows, cols), natural(crows, ccols)
        cases = []
        for t0, t1 in PAIRS:
            a, big_a, ahead = offsets(t0, t1)
            fine = moved(windowed(rows, cols), a)
            coarse = moved(cblock, big_a)
            quarters = [
                (l, 2 * r + dr, 2 * c + dc)
                for dr, dc in ((0, 0), (1, 0), (0, 1), (1, 1))
                for l, r, c in coarse
            ]
            come = 1 if a > 0 else -1
            one = exchange_places(block, fine, rows, cols, come)
            home = [p for p in block if p not in set(fine)]
            wanted = quarters + (home if come == -ahead else [])
            two = exchange_places(fine, wanted, rows, cols, ahead)
            back = 1 if big_a < 0 else -1
            three = exchange_places(coarse, cblock, crows, ccols, back)
            got = set(fine).union(*[places for _, places in two])
            four = exchange_places(fine, [p for p in block if p not in got], rows, cols, back)
            cases.append((come, ahead, back, fine, coarse, quarters, one, two, three, four))

        def needs(which):
            return [[len(numbers) for numbers, _ in case[which]] for case in cases]

        self.one, one_class = classes_of(needs(6), [64, 512])
        self.two, two_class = classes_of(needs(7), [64, 128, 512])
        fine_back = [max(need) > 0 for need in needs(9)]
        self.three = []
        self.four = []
        for with_fine in (False, True):
            inside = [n for n, flag in enumerate(fine_back) if flag == with_fine]
            self.three.append([up16(max(needs(8)[n][k] for n in inside)) for k in range(3)])
            self.four.append([up16(max(needs(9)[n][k] for n in inside)) for k in range(3)])
        three_class = [int(flag) for flag in fine_back]

        def branches(which_class, direction):
            pairs = [(n, case[direction]) for n, case in zip(which_class, cases)]
            found = sorted(set(pairs))
            return found, [found.index(pair) for pair in pairs]

        self.one_branches, one_at = branches(one_class, 0)
        self.two_branches, two_at = branches(two_class, 1)
        self.three_branches, three_at = branches(three_class, 2)
        self.flags = dict(
            one_class=one_class, two_class=two_class, three_class=three_class,
            one_at=one_at, two_at=two_at, three_at=three_at,
            a=[offsets(*pair)[0] for pair in PAIRS], big_a=[offsets(*pair)[1] for pair in PAIRS],
        )

        found = {}
        for n, (come, ahead, back, fine, coarse, quarters, one, two, three, four) in enumerate(cases):

            def send(exchanged, room):
                return [n for (numbers, _), size in zip(exchanged, room) for n in numbers + [-1] * (size - len(numbers))]

            def source(held, *exchanges):
                places = list(held)
                for exchanged, room in exchanges:
                    for (_, got), size in zip(exchanged, room):
                        places += got + [None] * (size - len(got))
                return {p: n for n, p in enumerate(places) if p is not None}

            w = three_class[n]
            first, second = source(block, (one, self.one[-1])), source(fine, (two, self.two[-1]))
            third = source(coarse, (three, self.three[w]))
            last = source(fine, (two, self.two[-1]), (four, self.four[w]))
            out = [(l, r, c) for r in range(crows) for c in range(ccols) for l in range(2)]
            rows_of = dict(
                send_one=send(one, self.one[one_class[n]]),
                take_one=[first[p] for p in fine],
                send_two=send(two, self.two[two_class[n]]),
                take_two=[second[p] for p in quarters],
                send_three=send(three, self.three[w]),
                send_four=send(four, self.four[w]),
                fine_out=[last[p] for p in block],
                coarse_out=[third[p] for p in out],
            )
            for name, row in rows_of.items():
                found.setdefault(name, []).append(row)
        parts, self.at, top = [], {}, 0
        for name, lists in found.items():
            length = -(-max(len(row) for row in lists) // 128)
            part = np.full((len(PAIRS), length * 128), -1, np.float32)
            for n, row in enumerate(lists):
                part[n, : len(row)] = row
            parts.append(part.reshape(len(PAIRS), length, 128))
            self.at[name] = (top, length)
            top += length
        parts.append(np.zeros((len(PAIRS), -top % 8, 128), np.float32))
        self.table = np.concatenate(parts, axis=1)


def case_of(shifts_ref):
    t0, t1 = shifts_ref[0], shifts_ref[1]
    return jnp.where(t0 == WH - 1, t1 - 1, t0 + WH - 2)


def lookup(values, case):
    out = jnp.int32(values[0])
    for n, value in enumerate(values[1:], 1):
        out = jnp.where(case == n, value, out)
    return out


def columns_of(rows, count):
    parts = [jnp.broadcast_to(rows[j : j + 1], (128, 128)).T for j in range(-(-count // 128))]
    return stack_rows(parts)[:count]


def select_rows(index, source):
    lane = lax.broadcasted_iota(I32, (1, 128), 1).astype(F32)
    size = source.shape[0]
    pick = [jnp.where(index == lane + float(at), 1.0, 0.0).astype(BF16) for at in range(0, size, 128)]
    pick = jnp.concatenate(pick, axis=1)[:, :size]
    return jnp.dot(pick, source, preferred_element_type=F32)


def stack_rows(parts):
    return parts[0] if len(parts) == 1 else jnp.concatenate(parts, axis=0)


def layer_norm(values):
    center = jnp.mean(values, axis=-1, keepdims=True)
    values = values - center
    spread = jnp.mean(values * values, axis=-1, keepdims=True)
    return values * lax.rsqrt(spread + EPS)


def attend_windows(qkv_of, id_of, windows, inner, finish):
    lane = lax.broadcasted_iota(I32, (1, 128), 1)
    forbid = jnp.where(lane < 8, BIG, 0.0).astype(BF16)
    groups = inner // 128
    units = [(w, g) for w in range(windows) for g in range(groups)]
    scores, weights, outs = {}, {}, {}

    def score(w, g):
        key_id = id_of(w)
        not_id = (key_id - 1).astype(BF16) * forbid
        q = qkv_of(w, g * 128)
        keys = jnp.concatenate([qkv_of(w, inner + g * 128), key_id], axis=1)
        queries = []
        for h in range(4):
            mine = jnp.where((lane >= h * HD) & (lane < (h + 1) * HD), 1.0, 0.0).astype(BF16)
            queries.append(jnp.concatenate([q * mine, not_id], axis=1))
        scores[w, g] = lax.dot_general(stack_rows(queries), keys, NT, preferred_element_type=F32)

    def soften(w, g):
        s = scores.pop((w, g))
        weights[w, g] = jnp.exp2((s - jnp.max(s, axis=1, keepdims=True)) * SCALE).astype(BF16)

    def gather(w, g):
        v = qkv_of(w, 2 * inner + g * 128)
        values = jnp.concatenate([v, jnp.ones_like(v)], axis=1)
        out = jnp.dot(weights.pop((w, g)), values, preferred_element_type=F32)
        out = out[:, :128] * (1.0 / out[:, 128:])
        picked = out[:TOK]
        for h in range(1, 4):
            picked = jnp.where(lane < h * HD, picked, out[h * TOK : (h + 1) * TOK])
        outs[w, g] = picked.astype(BF16)
        if g == groups - 1:
            finish(w, jnp.concatenate([outs.pop((w, k)) for k in range(groups)], axis=1))

    for n in range(len(units) + 2):
        if n < len(units):
            score(*units[n])
        if 0 <= n - 1 < len(units):
            soften(*units[n - 1])
        if 0 <= n - 2 < len(units):
            gather(*units[n - 2])


ANY = pl.BlockSpec(memory_space=pl.ANY)
HBM = pl.BlockSpec(memory_space=pltpu.HBM)
VMEM = pl.BlockSpec(memory_space=pltpu.VMEM)
SMEM = pl.BlockSpec(memory_space=pltpu.SMEM)


def call(body, outs, args, in_specs, scratch, copies, flops, moved_bytes, vmem=8):
    args = [
        pltpu.with_memory_space_constraint(arg, spec.memory_space) for arg, spec in zip(args, in_specs, strict=True)
    ]
    spaces = [getattr(out, "memory_space", pltpu.SMEM if out.dtype == I32 else pltpu.VMEM) for out in outs]
    out_specs = [pl.BlockSpec(memory_space=space) for space in spaces]
    return pl.pallas_call(
        body,
        out_shape=outs,
        in_specs=in_specs,
        out_specs=out_specs,
        scratch_shapes=list(scratch) + [pltpu.SemaphoreType.DMA((copies,))],
        compiler_params=pltpu.CompilerParams(vmem_limit_bytes=vmem << 20),
        cost_estimate=pl.CostEstimate(flops=flops, bytes_accessed=moved_bytes, transcendentals=0),
    )(*args)


def shapes(sizes, width, space=pltpu.VMEM):
    return [space((n, width), BF16) for n in sizes]


class Copies:
    def __init__(self, sems):
        self.sems, self.used = sems, 0

    def __call__(self, src, dst):
        copy = pltpu.make_async_copy(src, dst, self.sems.at[self.used])
        self.used += 1
        copy.start()
        return copy


def lay_pieces(refs, sizes, which, source):
    for n, size in enumerate(sizes):

        @pl.when(which == n)
        def _():
            at = 0
            for ref, rows, room in zip(refs[3 * n : 3 * n + 3], size, sizes[-1]):
                source[at : at + rows, :] = ref[...]
                if rows < room:
                    source[at + rows : at + room, :] = jnp.zeros((room - rows, source.shape[1]), source.dtype)
                at += room


def flat(ref):
    layers, rows, cols, width = ref.shape
    return ref[...].astype(F32).reshape(layers * rows * cols, width).astype(BF16)


def put_pieces(value, refs):
    at = 0
    for ref in refs:
        ref[...] = value[at : at + ref.shape[0]].astype(BF16)
        at += ref.shape[0]


def rows_of(plan, table_ref, name, *lead):
    top, length = plan.at[name]
    return table_ref[(*lead, slice(top, top + length), slice(None))]


def send_classes(plan, rows, source_ref, sizes, which, refs):
    for n, size in enumerate(sizes):

        @pl.when(which == n)
        def _():
            put_pieces(select_rows(columns_of(rows, sum(size)), source_ref[...]), refs[3 * n : 3 * n + 3])


def exchange(pieces, sign):
    lat, lon = lax.axis_size("lat"), lax.axis_size("lon")
    row, col, both = pieces
    pairs = [((i + sign) % lat * lon + (j + sign) % lon, i * lon + j) for i in range(lat) for j in range(lon)]
    col = lax.ppermute(col, "lon", [((j + sign) % lon, j) for j in range(lon)])
    both = lax.ppermute(both, ("lat", "lon"), pairs)
    row = lax.ppermute(row, "lat", [((i + sign) % lat, i) for i in range(lat)])
    return [row, col, both]


def unused(like):
    outs = [jax.ShapeDtypeStruct(x.shape, x.dtype) for x in like]
    return pl.pallas_call(lambda *refs: None, out_shape=outs, out_specs=[ANY] * len(outs))()


def choose(index, branches, *args):
    flat_args, tree = jax.tree.flatten(args)
    out_trees = []

    def closed(branch):
        def run(*leaves):
            out, out_tree = jax.tree.flatten(branch(*jax.tree.unflatten(tree, leaves)))
            out_trees.append(out_tree)
            return out

        return jax.make_jaxpr(run)(*flat_args)

    out = lax.cond_p.bind(index, *flat_args, branches=tuple(closed(branch) for branch in branches))
    return jax.tree.unflatten(out_trees[0], out)


def exchange_class(sent, which, sign):
    got = []
    for n in range(len(sent) // 3):
        mine = sent[3 * n : 3 * n + 3]
        got += exchange(mine, sign) if n == which else unused(mine)
    return got


FLAGS = ("one_class", "two_class", "three_class", "a", "big_a")


def first_pieces(shifts, tokens, plan):
    width = tokens.shape[-1]
    count = tokens.size // width
    sizes = plan.one
    kinds = 3 * len(sizes)

    def body(shifts_hbm, tokens_hbm, table_hbm, *refs):
        outs, refs = refs[:kinds], refs[kinds:]
        rows_ref, flags_ref, *at_refs, shifts_ref, tokens_ref, table_ref, source_ref, sems = refs
        start = Copies(sems)
        shift = start(shifts_hbm, shifts_ref)
        held = start(tokens_hbm, tokens_ref)
        table = start(table_hbm, table_ref)
        shift.wait()
        case = case_of(shifts_ref)
        for ref, name in zip(at_refs, ("one_at", "two_at", "three_at")):
            ref[0] = lookup(plan.flags[name], case)
        for n, name in enumerate(FLAGS):
            flags_ref[n] = lookup(plan.flags[name], case)
        which = lookup(plan.flags["one_class"], case)
        held.wait()
        source_ref[...] = flat(tokens_ref)
        table.wait()
        rows_ref[...] = table_ref[case]
        send_classes(plan, rows_of(plan, table_ref, "send_one", case), source_ref, sizes, which, outs)

    outs = [shape for size in sizes for shape in shapes(size, width)]
    outs += [pltpu.VMEM(plan.table.shape[1:], F32), pltpu.SMEM((8,), I32)]
    outs += [pltpu.SMEM((1,), I32)] * 3
    scratch = [pltpu.SMEM((2,), I32), pltpu.VMEM(tokens.shape, BF16), pltpu.VMEM(plan.table.shape, F32)]
    scratch += [pltpu.VMEM((count, width), BF16)]
    got = call(body, outs, [shifts, tokens, plan.table], [HBM] * 3, scratch, 3, 1 << 28, 1 << 20)
    sent, (rows, flags, one, two, three) = got[:kinds], got[kinds:]
    return sent, rows, flags, one[0], two[0], three[0]


def before_fine(flags, regions, tokens, table, weights, plan):
    _, lat, lon = regions.shape
    _, rows, cols, width = tokens.shape
    flat_regions = regions.reshape(2 * lat, lon)
    fine, coarse = windowed(rows, cols), natural(rows // 2, cols // 2)
    places = np.asarray(fine + coarse, np.float32)
    places[len(fine) :, 1:] *= 2
    pad = -len(places) % 128
    places = np.pad(places, ((0, pad), (0, 0))).T.reshape(3, -1, 128)
    is_fine = np.pad(np.ones(len(fine), np.float32), (0, len(coarse) + pad)).reshape(1, -1, 128)
    places = np.concatenate([places, is_fine])
    count = len(fine) + len(coarse)

    def body(flags_ref, rows_ref, regions_hbm, places_hbm, tokens_hbm, *refs):
        weights_hbm, refs = refs[: len(weights)], refs[len(weights) :]
        fine_ref, coarse_hbm, x_ref, *refs = refs
        weight_refs, (regions_ref, places_ref, tokens_ref, coarse_ref, sems) = refs[: len(weights)], refs[len(weights) :]
        start = Copies(sems)
        waits = [start(regions_hbm, regions_ref), start(places_hbm, places_ref)]
        held = start(tokens_hbm, tokens_ref)
        later = [start(src, dst) for src, dst in zip(weights_hbm, weight_refs)]
        for copy in waits:
            copy.wait()
        a = flags_ref[3].astype(F32)
        big_a = 2.0 * flags_ref[4].astype(F32)
        is_fine = places_ref[3]
        d = is_fine * a + (1.0 - is_fine) * big_a
        row = places_ref[1] + d + (lax.axis_index("lat") * rows).astype(F32)
        col = places_ref[2] + 2.0 * d + (lax.axis_index("lon") * cols).astype(F32)
        wrapped = jnp.where((row < 0) | (row >= lat), 4.0, 0.0)
        row = jnp.where(row < 0, row + lat, jnp.where(row >= lat, row - lat, row))
        col = jnp.where(col < 0, col + lon, jnp.where(col >= lon, col - lon, col))
        row = columns_of(row + places_ref[0] * lat, count)
        col = columns_of(col, count)
        wrapped = columns_of(wrapped, count)
        picked = select_rows(row, regions_ref[...].astype(F32).astype(BF16))
        ids = jnp.zeros((count, 128), F32)
        for at in range(0, lon, 128):
            size = min(128, lon - at)
            lane = lax.broadcasted_iota(I32, (1, size), 1).astype(F32) + float(at)
            here = jnp.where(lane == col[:, :size], picked[:, at : at + size], 0.0)
            ids = ids + jnp.sum(here, axis=1, keepdims=True)
        lane = lax.broadcasted_iota(I32, (1, 128), 1).astype(F32)
        hot = jnp.where(lane == ids + wrapped, 1.0, 0.0).astype(BF16)
        fine_ref[...] = hot[: len(fine)]
        coarse_ref[...] = hot[len(fine) :]
        later.append(start(coarse_ref, coarse_hbm))
        held.wait()
        take = columns_of(rows_of(plan, rows_ref, "take_one"), len(fine))
        x_ref[...] = select_rows(take, flat(tokens_ref)).astype(BF16)
        for copy in later:
            copy.wait()

    outs = shapes([len(fine)], 128) + shapes([len(coarse)], 128, pltpu.HBM) + shapes([len(fine)], width)
    outs += [pltpu.VMEM(w.shape, BF16) for w in weights]
    scratch = [pltpu.VMEM(flat_regions.shape, I32), pltpu.VMEM(places.shape, F32), pltpu.VMEM(tokens.shape, BF16)]
    scratch += [pltpu.VMEM((len(coarse), 128), BF16)]
    args = [flags, table, flat_regions, places, tokens, *weights]
    in_specs = [SMEM, VMEM] + [HBM] * (3 + len(weights))
    fine_id, coarse_id, x, *weights = call(body, outs, args, in_specs, scratch, 4 + len(weights), 1 << 28, 4 << 20)
    return fine_id, coarse_id, x, weights


def before_coarse(fine, table, plan):
    own, width = fine.shape

    def body(rows_ref, fine_hbm, x_ref, part_hbm, fine_ref, part_ref, sems):
        start = Copies(sems)
        held = start(fine_hbm, fine_ref)
        take = columns_of(rows_of(plan, rows_ref, "fine_out"), own)
        held.wait()
        part_ref[...] = select_rows(take, fine_ref[...]).astype(BF16)
        leave = start(part_ref, part_hbm)
        take = columns_of(rows_of(plan, rows_ref, "take_two"), own)
        x_ref[...] = select_rows(take, fine_ref[...]).astype(BF16)
        leave.wait()

    outs = shapes([own], width) + shapes([own], width, pltpu.HBM)
    scratch = [pltpu.VMEM(fine.shape, BF16)] * 2
    return call(body, outs, [table, fine], [VMEM, HBM], scratch, 2, 1 << 28, 2 << 20)


def fine_level(flags, x_own, pieces, key_id, w_qkv, w_proj, rows, plan):
    count, width = x_own.shape
    inner = w_proj.shape[0]
    kinds = 3 * len(plan.two)

    def body(flags_ref, own_ref, *refs):
        piece_refs, refs = refs[: len(pieces)], refs[len(pieces) :]
        id_ref, qkv_w_ref, proj_w_ref, rows_ref, out_hbm, *refs = refs
        piece_outs, (source_ref, x_ref, qkv_ref, out_ref, sems) = refs[:kinds], refs[kinds:]
        start = Copies(sems)
        leave = []
        lay_pieces(piece_refs, plan.one, flags_ref[0], source_ref)
        take = columns_of(rows_of(plan, rows_ref, "take_one"), count) - float(count)
        x = own_ref[...].astype(F32) + select_rows(take, source_ref[...])
        x_ref[...] = x
        normed = layer_norm(x).astype(BF16)
        qkv_ref[...] = jnp.dot(normed, qkv_w_ref[...], preferred_element_type=F32).astype(BF16)

        def finish(w, out):
            at = slice(w * TOK, (w + 1) * TOK)
            out = jnp.dot(out, proj_w_ref[...], preferred_element_type=F32)
            out_ref[at, :] = (x_ref[at, :] + out).astype(BF16)
            leave.append(start(out_ref.at[pl.ds(w * TOK, TOK)], out_hbm.at[pl.ds(w * TOK, TOK)]))

        attend_windows(
            lambda w, at: qkv_ref[w * TOK : (w + 1) * TOK, at : at + 128],
            lambda w: id_ref[w * TOK : (w + 1) * TOK, :],
            count // TOK,
            inner,
            finish,
        )
        send_classes(plan, rows_of(plan, rows_ref, "send_two"), out_ref, plan.two, flags_ref[1], piece_outs)
        for copy in leave:
            copy.wait()

    outs = shapes([count], width, pltpu.HBM) + [shape for size in plan.two for shape in shapes(size, width)]
    scratch = [
        pltpu.VMEM((sum(plan.one[-1]), width), BF16),
        pltpu.VMEM((count, width), F32),
        pltpu.VMEM((count, 3 * inner), BF16),
        pltpu.VMEM((count, width), BF16),
    ]
    args = [flags, x_own, *pieces, key_id, w_qkv, w_proj, rows]
    in_specs = [SMEM] + [VMEM] * (len(args) - 1)
    out, *sent = call(body, outs, args, in_specs, scratch, count // TOK, 3 << 30, 6 << 20, 14)
    return out, sent


def coarse_level(flags, fine, x_own, pieces, key_id, w_merge, w_qkv, w_proj, rows, plan):
    count = key_id.shape[0]
    depth, width = w_merge.shape
    own, half = fine.shape
    inner = w_proj.shape[0]
    kinds = 3 * len(plan.three)

    def body(flags_ref, fine_hbm, id_hbm, merge_hbm, qkv_w_hbm, proj_w_hbm, own_ref, *refs):
        piece_refs, refs = refs[: len(pieces)], refs[len(pieces) :]
        rows_ref, out_ref, *refs = refs
        piece_outs, refs = refs[:kinds], refs[kinds:]
        source_ref, qkv_ref, fine_ref, id_ref, merge_ref, qkv_w_ref, proj_w_ref, sems = refs
        start = Copies(sems)

        def bring(src, dst):
            return [
                (at, start(src.at[pl.ds(at, half)], dst.at[pl.ds(at, half)])) for at in range(0, src.shape[0], half)
            ]

        def product(x, ref, copies):
            parts = []
            for at, copy in copies:
                copy.wait()
                parts.append(jnp.dot(x[:, at : at + half], ref[at : at + half, :], preferred_element_type=F32))
            return functools.reduce(jnp.add, parts)

        merge_w, qkv_w = bring(merge_hbm, merge_ref), bring(qkv_w_hbm, qkv_w_ref)
        ids, proj_w = start(id_hbm, id_ref), start(proj_w_hbm, proj_w_ref)
        fine_copy = (fine_hbm, fine_ref, sems.at[start.used])

        @pl.when(flags_ref[2] == 1)
        def _():
            pltpu.make_async_copy(*fine_copy).start()

        lay_pieces(piece_refs, plan.two, flags_ref[1], source_ref)
        take = columns_of(rows_of(plan, rows_ref, "take_two"), 4 * count) - float(own)
        x = own_ref[...].astype(F32) + select_rows(take, source_ref[...])
        x = jnp.concatenate([x[n * count : (n + 1) * count] for n in range(4)], axis=1)
        stacked = layer_norm(x).astype(BF16)
        merged = product(stacked, merge_ref, merge_w).astype(BF16).astype(F32)
        normed = layer_norm(merged).astype(BF16)
        qkv_ref[...] = product(normed, qkv_w_ref, qkv_w).astype(BF16)
        ids.wait()
        proj_w.wait()

        def finish(w, out):
            out = jnp.dot(out, proj_w_ref[...], preferred_element_type=F32)
            out_ref[...] = (merged + out).astype(BF16)

        attend_windows(lambda w, at: qkv_ref[:, at : at + 128], lambda w: id_ref[...], 1, inner, finish)
        for n, (sizes, fine_sizes) in enumerate(zip(plan.three, plan.four)):

            @pl.when(flags_ref[2] == n)
            def _():
                sent = select_rows(columns_of(rows_of(plan, rows_ref, "send_three"), sum(sizes)), out_ref[...])
                sent = sent.astype(BF16)
                at = 0
                for ref, size in zip(piece_outs[3 * n :], sizes):
                    ref[:size, :] = sent[at : at + size, :half]
                    ref[size : 2 * size, :] = sent[at : at + size, half:]
                    at += size
                if sum(fine_sizes):
                    pltpu.make_async_copy(*fine_copy).wait()
                    index = columns_of(rows_of(plan, rows_ref, "send_four"), sum(fine_sizes))
                    sent = select_rows(index, fine_ref[...]).astype(BF16)
                    at = 0
                    for ref, size, more in zip(piece_outs[3 * n :], sizes, fine_sizes):
                        ref[2 * size :, :] = sent[at : at + more]
                        at += more

    outs = shapes([count], width)
    for sizes, fine_sizes in zip(plan.three, plan.four):
        outs += shapes([2 * n + m for n, m in zip(sizes, fine_sizes)], half)
    scratch = [pltpu.VMEM((sum(plan.two[-1]), half), BF16), pltpu.VMEM((count, 3 * inner), BF16)]
    scratch += [pltpu.VMEM(x.shape, BF16) for x in (fine, key_id, w_merge, w_qkv, w_proj)]
    args = [flags, fine, key_id, w_merge, w_qkv, w_proj, x_own, *pieces, rows]
    in_specs = [SMEM] + [HBM] * 5 + [VMEM] * (len(args) - 6)
    copies = depth // half + width // half + 3
    out, *sent = call(body, outs, args, in_specs, scratch, copies, 3 << 30, 12 << 20, 24)
    return out, sent


def fine_output(flags, part, pieces, rows, plan, block_rows, block_cols, partial):
    own, width = part.shape

    def body(flags_ref, part_hbm, *refs):
        piece_refs, (rows_ref, out_ref, source_ref, part_ref, stage_ref, sems) = refs[: len(pieces)], refs[len(pieces) :]
        start = Copies(sems)
        cuts = [pl.ds(at, TOK) for at in range(0, own, TOK)]
        held = [start(part_hbm.at[cut], part_ref.at[cut]) for cut in cuts]
        lay_pieces(piece_refs, plan.two, flags_ref[1], source_ref)
        take = columns_of(rows_of(plan, rows_ref, "fine_out"), own) - float(own)
        leave = []
        for n, (cut, copy) in enumerate(zip(cuts, held)):
            got = select_rows(take[n * TOK : (n + 1) * TOK], source_ref[...])
            copy.wait()
            out = part_ref[cut, :].astype(F32) + got
            if partial:
                out_ref[cut, :] = out.astype(BF16)
            else:
                lines = TOK // block_cols
                layer, line = divmod(n * lines, block_rows)
                there = (layer, pl.ds(line, lines))
                stage_ref[there] = out.reshape(lines, block_cols, width).astype(BF16)
                leave.append(start(stage_ref.at[there], out_ref.at[there]))
        for copy in leave:
            copy.wait()

    shape = (2, block_rows, block_cols, width)
    outs = shapes([own], width) if partial else [pltpu.HBM(shape, BF16)]
    scratch = [pltpu.VMEM((sum(plan.two[-1]), width), BF16), pltpu.VMEM(part.shape, BF16), pltpu.VMEM(shape, BF16)]
    args = [flags, part, *pieces, rows]
    in_specs = [SMEM, HBM] + [VMEM] * (len(args) - 2)
    return call(body, outs, args, in_specs, scratch, 2 * own // TOK, 1 << 30, 4 << 20)[0]


def coarse_output(coarse, got, rows, which, plan, block_rows, block_cols, part=None):
    own, width = coarse.shape
    half = width // 2
    sizes, more = plan.three[which], plan.four[which]
    parts = [] if part is None else [part]

    def body(coarse_ref, *refs):
        got_refs, refs = refs[:3], refs[3:]
        part_refs, (rows_ref, out_ref, *fine_outs, _) = refs[: len(parts)], refs[len(parts) :]
        back = [
            jnp.concatenate([ref[:size, :], ref[size : 2 * size, :]], axis=1) for ref, size in zip(got_refs, sizes)
        ]
        take = columns_of(rows_of(plan, rows_ref, "coarse_out"), own)
        out = select_rows(take, stack_rows([coarse_ref[...]] + back)).astype(BF16)
        for n in range(own // 2):
            out_ref[n // block_cols, n % block_cols] = out[2 * n : 2 * n + 2]
        for part_ref, fine_ref in zip(part_refs, fine_outs):
            fine = stack_rows([ref[2 * size :, :] for ref, size in zip(got_refs, sizes)])
            base = part_ref.shape[0] + sum(plan.two[-1])
            take = columns_of(rows_of(plan, rows_ref, "fine_out"), part_ref.shape[0]) - float(base)
            out = part_ref[...].astype(F32) + select_rows(take, fine)
            fine_ref[...] = out.reshape(fine_ref.shape).astype(BF16)

    outs = [jax.ShapeDtypeStruct((block_rows, block_cols, 2, width), BF16)]
    outs += [jax.ShapeDtypeStruct((2, 2 * block_rows, 2 * block_cols, half), BF16) for _ in parts]
    args = [coarse, *got, *parts, rows]
    out, *fine = call(body, outs, args, [VMEM] * len(args), [], 1, 1 << 28, 1 << 20)
    return out.transpose(2, 0, 1, 3), *fine


def on_device(tokens, regions, shifts, fine_qkv, fine_proj, merge_weight, coarse_qkv, coarse_proj):
    _, rows, cols, _ = tokens.shape
    plan = Plan(rows, cols)

    def first(which, sign, sent, *args):
        return exchange_class(sent, which, sign), before_fine(*args, plan)

    def second(which, sign, sent, *args):
        return exchange_class(sent, which, sign), before_coarse(*args, plan)

    def third(which, sign, sent, flags, part, pieces, coarse, table):
        got = exchange(sent[3 * which : 3 * which + 3], sign)
        fine_out = fine_output(flags, part, pieces, table, plan, rows, cols, which == 1)
        place = (table, which, plan, rows // 2, cols // 2)
        if which == 1:
            coarse_out, fine_out = coarse_output(coarse, got, *place, part=fine_out)
        else:
            (coarse_out,) = coarse_output(coarse, got, *place)
        return fine_out, coarse_out

    def branches(stage, pairs):
        return [functools.partial(stage, which, sign) for which, sign in pairs]

    sent, table, flags, one, two, three = first_pieces(shifts, tokens, plan)
    got, (fine_id, coarse_id, x, weights) = choose(
        one, branches(first, plan.one_branches), sent, flags, regions, tokens, table, [fine_qkv, fine_proj]
    )
    fine, sent = fine_level(flags, x, got, fine_id, *weights, table, plan)
    got, (x, part) = choose(two, branches(second, plan.two_branches), sent, fine, table)
    coarse, sent = coarse_level(
        flags, fine, x, got, coarse_id, merge_weight, coarse_qkv, coarse_proj, table, plan
    )
    return choose(three, branches(third, plan.three_branches), sent, flags, part, got, coarse, table)


def solution(mesh):
    return jax.shard_map(
        on_device,
        mesh=mesh,
        in_specs=(P(None, "lat", "lon", None), P(), P(), P(), P(), P(), P(), P()),
        out_specs=(P(None, "lat", "lon", None), P(None, "lat", "lon", None)),
        check_vma=False,
    )
```

```python
import functools

import jax
import jax.numpy as jnp
import numpy as np
from jax import lax
from jax.experimental import pallas as pl
from jax.experimental.pallas import tpu as pltpu
from jax.sharding import PartitionSpec as P

HD = 32
WH = 6
WW = 12
TOK = 2 * WH * WW
EPS = 1e-05
BIG = 1e30
SCALE = float(np.log2(np.e) / np.sqrt(HD))

NT = (((1,), (1,)), ((), ()))
F32 = jnp.float32
BF16 = jnp.bfloat16
I32 = jnp.int32

PAIRS = [(WH - 1, t) for t in range(1, WH)] + [(t, WH - 1) for t in range(1, WH - 1)]


def up16(count):
    return -(-count // 16) * 16


def natural(rows, cols):
    return [(l, r, c) for l in range(2) for r in range(rows) for c in range(cols)]


def windowed(rows, cols):
    return [
        (l, wr * WH + r, wc * WW + c)
        for wr in range(rows // WH)
        for wc in range(cols // WW)
        for l in range(2)
        for r in range(WH)
        for c in range(WW)
    ]


def moved(order, d):
    return [(l, r + d, c + 2 * d) for l, r, c in order]


def exchange_places(held, wanted, rows, cols, sign):
    at = {place: n for n, place in enumerate(held)}
    found = []
    for dr, dc in ((sign, 0), (0, sign), (sign, sign)):
        numbers, places = [], []
        for l, r, c in sorted(set(wanted) - set(held)):
            n = at.get((l, r - dr * rows, c - dc * cols))
            if n is not None:
                numbers.append(n)
                places.append((l, r, c))
        found.append((numbers, places))
    return found


def offsets(t0, t1):
    a = t0 if t0 <= 2 else t0 - WH
    big_a = t1 if t1 <= 2 else t1 - WH
    ahead = 1 if 2 * big_a > a or 2 * big_a - a == 0 and a < 0 else -1
    return a, big_a, ahead


def classes_of(needs, slack):
    rounded = [tuple(-(-size // 8) * 8 for size in need) for need in needs]
    heavy = [sum(need[1:3]) * 2 + sum(need[4:]) for need in rounded]
    limits = []
    for size in sorted(set(heavy)):
        if not limits or size > limits[-1][0] * slack:
            limits.append([size, size])
        limits[-1][1] = size
    which = [next(n for n, limit in enumerate(limits) if size <= limit[1]) for size in heavy]
    sizes = [
        [max(need[k] for need, w in zip(rounded, which) if w == n) for k in range(len(needs[0]))]
        for n in range(len(limits))
    ]
    return sizes, which


def rooms(sizes):
    return [up16(max(size[k] for size in sizes)) for k in range(len(sizes[0]))]


class Plan:
    def __init__(self, rows, cols):
        crows, ccols = rows // 2, cols // 2
        block, cblock = natural(rows, cols), natural(crows, ccols)
        cases = []
        for t0, t1 in PAIRS:
            a, big_a, ahead = offsets(t0, t1)
            fine = moved(windowed(rows, cols), a)
            coarse = moved(cblock, big_a)
            quarters = [
                (l, 2 * r + dr, 2 * c + dc)
                for dr, dc in ((0, 0), (1, 0), (0, 1), (1, 1))
                for l, r, c in coarse
            ]
            come = 1 if a > 0 else -1
            one = exchange_places(block, fine, rows, cols, come)
            home = [p for p in block if p not in set(fine)]
            wanted = quarters + (home if come == -ahead else [])
            two = exchange_places(fine, wanted, rows, cols, ahead)
            back = 1 if big_a < 0 else -1
            three = exchange_places(coarse, cblock, crows, ccols, back)
            got = set(fine).union(*[places for _, places in two])
            four = exchange_places(fine, [p for p in block if p not in got], rows, cols, back)
            cases.append((come, ahead, back, fine, coarse, quarters, one, two, three, four))

        def needs(which):
            return [[len(numbers) for numbers, _ in case[which]] for case in cases]

        self.one, one_class = classes_of(needs(6), 1.15)
        self.two, two_class = classes_of(needs(7), 1.15)
        sizes, three_class = classes_of([three + four for three, four in zip(needs(8), needs(9))], 1.0)
        self.three, self.four = [size[:3] for size in sizes], [size[3:] for size in sizes]
        self.room_one, self.room_two = rooms(self.one), rooms(self.two)
        self.room_three, self.room_four = rooms(self.three), rooms(self.four)

        def branches(which_class, direction):
            pairs = [(n, case[direction]) for n, case in zip(which_class, cases)]
            found = sorted(set(pairs))
            return found, [found.index(pair) for pair in pairs]

        self.one_branches, one_at = branches(one_class, 0)
        self.two_branches, two_at = branches(two_class, 1)
        self.three_branches, three_at = branches(three_class, 2)
        self.flags = dict(
            three_class=three_class,
            one_at=one_at, two_at=two_at, three_at=three_at,
            a=[offsets(*pair)[0] for pair in PAIRS], big_a=[offsets(*pair)[1] for pair in PAIRS],
        )

        found = {}
        for n, (come, ahead, back, fine, coarse, quarters, one, two, three, four) in enumerate(cases):

            def send(exchanged, room):
                return [n for (numbers, _), size in zip(exchanged, room) for n in numbers + [-1] * (size - len(numbers))]

            def source(held, *exchanges):
                places = list(held)
                for exchanged, room in exchanges:
                    for (_, got), size in zip(exchanged, room):
                        places += got + [None] * (size - len(got))
                return {p: n for n, p in enumerate(places) if p is not None}

            first, second = source(block, (one, self.room_one)), source(fine, (two, self.room_two))
            third = source(coarse, (three, self.room_three))
            last = source(fine, (two, self.room_two), (four, self.room_four))
            out = [(l, r, c) for r in range(crows) for c in range(ccols) for l in range(2)]
            rows_of = dict(
                send_one=send(one, self.room_one),
                take_one=[first[p] for p in fine],
                send_two=send(two, self.room_two),
                take_two=[second[p] for p in quarters],
                send_three=send(three, self.room_three),
                send_four=send(four, self.room_four),
                fine_out=[last[p] for p in block],
                coarse_out=[third[p] for p in out],
            )
            for name, row in rows_of.items():
                found.setdefault(name, []).append(row)
        parts, self.at, top = [], {}, 0
        for name, lists in found.items():
            length = -(-max(len(row) for row in lists) // 128)
            part = np.full((len(PAIRS), length * 128), -1, np.float32)
            for n, row in enumerate(lists):
                part[n, : len(row)] = row
            parts.append(part.reshape(len(PAIRS), length, 128))
            self.at[name] = (top, length)
            top += length
        parts.append(np.zeros((len(PAIRS), -top % 8, 128), np.float32))
        self.table = np.concatenate(parts, axis=1)


def case_of(shifts_ref):
    t0, t1 = shifts_ref[0], shifts_ref[1]
    return jnp.where(t0 == WH - 1, t1 - 1, t0 + WH - 2)


def lookup(values, case):
    out = jnp.int32(values[0])
    for n, value in enumerate(values[1:], 1):
        out = jnp.where(case == n, value, out)
    return out


def columns_of(rows, count):
    parts = [jnp.broadcast_to(rows[j : j + 1], (128, 128)).T for j in range(-(-count // 128))]
    return stack_rows(parts)[:count]


def select_rows(index, source):
    lane = lax.broadcasted_iota(I32, (1, 128), 1).astype(F32)
    size = source.shape[0]
    pick = [jnp.where(index == lane + float(at), 1.0, 0.0).astype(BF16) for at in range(0, size, 128)]
    pick = jnp.concatenate(pick, axis=1)[:, :size]
    return jnp.dot(pick, source, preferred_element_type=F32)


def stack_rows(parts):
    return parts[0] if len(parts) == 1 else jnp.concatenate(parts, axis=0)


def layer_norm(values):
    center = jnp.mean(values, axis=-1, keepdims=True)
    values = values - center
    spread = jnp.mean(values * values, axis=-1, keepdims=True)
    return values * lax.rsqrt(spread + EPS)


def attend_windows(qkv_of, id_of, windows, inner, finish):
    lane = lax.broadcasted_iota(I32, (1, 128), 1)
    forbid = jnp.where(lane < 8, BIG, 0.0).astype(BF16)
    groups = inner // 128
    units = [(w, g) for w in range(windows) for g in range(groups)]
    scores, weights, outs = {}, {}, {}

    def score(w, g):
        key_id = id_of(w)
        not_id = (key_id - 1).astype(BF16) * forbid
        q = qkv_of(w, g * 128)
        keys = jnp.concatenate([qkv_of(w, inner + g * 128), key_id], axis=1)
        queries = []
        for h in range(4):
            mine = jnp.where((lane >= h * HD) & (lane < (h + 1) * HD), 1.0, 0.0).astype(BF16)
            queries.append(jnp.concatenate([q * mine, not_id], axis=1))
        scores[w, g] = lax.dot_general(stack_rows(queries), keys, NT, preferred_element_type=F32)

    def soften(w, g):
        s = scores.pop((w, g))
        weights[w, g] = jnp.exp2((s - jnp.max(s, axis=1, keepdims=True)) * SCALE).astype(BF16)

    def gather(w, g):
        v = qkv_of(w, 2 * inner + g * 128)
        values = jnp.concatenate([v, jnp.ones_like(v)], axis=1)
        out = jnp.dot(weights.pop((w, g)), values, preferred_element_type=F32)
        out = out[:, :128] * (1.0 / out[:, 128:])
        picked = out[:TOK]
        for h in range(1, 4):
            picked = jnp.where(lane < h * HD, picked, out[h * TOK : (h + 1) * TOK])
        outs[w, g] = picked.astype(BF16)
        if g == groups - 1:
            finish(w, jnp.concatenate([outs.pop((w, k)) for k in range(groups)], axis=1))

    for n in range(len(units) + 2):
        if n < len(units):
            score(*units[n])
        if 0 <= n - 1 < len(units):
            soften(*units[n - 1])
        if 0 <= n - 2 < len(units):
            gather(*units[n - 2])


ANY = pl.BlockSpec(memory_space=pl.ANY)
HBM = pl.BlockSpec(memory_space=pltpu.HBM)
VMEM = pl.BlockSpec(memory_space=pltpu.VMEM)
SMEM = pl.BlockSpec(memory_space=pltpu.SMEM)


def call(body, outs, args, in_specs, scratch, copies, flops, moved_bytes, vmem=8):
    args = [
        pltpu.with_memory_space_constraint(arg, spec.memory_space) for arg, spec in zip(args, in_specs, strict=True)
    ]
    spaces = [getattr(out, "memory_space", pltpu.SMEM if out.dtype == I32 else pltpu.VMEM) for out in outs]
    out_specs = [pl.BlockSpec(memory_space=space) for space in spaces]
    return pl.pallas_call(
        body,
        out_shape=outs,
        in_specs=in_specs,
        out_specs=out_specs,
        scratch_shapes=list(scratch) + [pltpu.SemaphoreType.DMA((copies,))],
        compiler_params=pltpu.CompilerParams(vmem_limit_bytes=vmem << 20),
        cost_estimate=pl.CostEstimate(flops=flops, bytes_accessed=moved_bytes, transcendentals=0),
    )(*args)


def shapes(sizes, width, space=pltpu.VMEM):
    return [space((n, width), BF16) for n in sizes]


class Copies:
    def __init__(self, sems):
        self.sems, self.used = sems, 0

    def __call__(self, src, dst):
        copy = pltpu.make_async_copy(src, dst, self.sems.at[self.used])
        self.used += 1
        copy.start()
        return copy


def lay(pieces, room):
    width = pieces[0].shape[1]

    def body(*refs):
        out_ref = refs[len(pieces)]
        at = 0
        for ref, space in zip(refs, room):
            rows = ref.shape[0]
            out_ref[at : at + rows, :] = ref[...]
            if rows < space:
                out_ref[at + rows : at + space, :] = jnp.zeros((space - rows, width), BF16)
            at += space

    return call(body, shapes([sum(room)], width), pieces, [VMEM] * 3, [], 1, 0, 1 << 18)[0]


def flat(ref):
    layers, rows, cols, width = ref.shape
    return ref[...].astype(F32).reshape(layers * rows * cols, width).astype(BF16)


def put_pieces(value, refs):
    at = 0
    for ref in refs:
        ref[...] = value[at : at + ref.shape[0]].astype(BF16)
        at += ref.shape[0]


def rows_of(plan, table_ref, name, *lead):
    top, length = plan.at[name]
    return table_ref[(*lead, slice(top, top + length), slice(None))]


def exchange(pieces, sizes, sign):
    lat, lon = lax.axis_size("lat"), lax.axis_size("lon")
    row, col, both = [piece[:size] for piece, size in zip(pieces, sizes)]
    pairs = [((i + sign) % lat * lon + (j + sign) % lon, i * lon + j) for i in range(lat) for j in range(lon)]
    col = lax.ppermute(col, "lon", [((j + sign) % lon, j) for j in range(lon)])
    both = lax.ppermute(both, ("lat", "lon"), pairs)
    row = lax.ppermute(row, "lat", [((i + sign) % lat, i) for i in range(lat)])
    return [row, col, both]


def choose(index, branches, *args):
    flat_args, tree = jax.tree.flatten(args)
    out_trees = []

    def closed(branch):
        def run(*leaves):
            out, out_tree = jax.tree.flatten(branch(*jax.tree.unflatten(tree, leaves)))
            out_trees.append(out_tree)
            return out

        return jax.make_jaxpr(run)(*flat_args)

    out = lax.cond_p.bind(index, *flat_args, branches=tuple(closed(branch) for branch in branches))
    return jax.tree.unflatten(out_trees[0], out)


FLAGS = ("three_class", "a", "big_a")


def first_pieces(shifts, tokens, plan):
    width = tokens.shape[-1]
    count = tokens.size // width
    kinds = 3

    def body(shifts_hbm, tokens_hbm, table_hbm, *refs):
        outs, refs = refs[:kinds], refs[kinds:]
        rows_ref, flags_ref, *at_refs, shifts_ref, tokens_ref, table_ref, source_ref, sems = refs
        start = Copies(sems)
        shift = start(shifts_hbm, shifts_ref)
        held = start(tokens_hbm, tokens_ref)
        table = start(table_hbm, table_ref)
        shift.wait()
        case = case_of(shifts_ref)
        for ref, name in zip(at_refs, ("one_at", "two_at", "three_at")):
            ref[0] = lookup(plan.flags[name], case)
        for n, name in enumerate(FLAGS):
            flags_ref[n] = lookup(plan.flags[name], case)
        held.wait()
        source_ref[...] = flat(tokens_ref)
        table.wait()
        rows_ref[...] = table_ref[case]
        index = columns_of(rows_of(plan, table_ref, "send_one", case), sum(plan.room_one))
        put_pieces(select_rows(index, source_ref[...]), outs)

    outs = shapes(plan.room_one, width)
    outs += [pltpu.VMEM(plan.table.shape[1:], F32), pltpu.SMEM((8,), I32)]
    outs += [pltpu.SMEM((1,), I32)] * 3
    scratch = [pltpu.SMEM((2,), I32), pltpu.VMEM(tokens.shape, BF16), pltpu.VMEM(plan.table.shape, F32)]
    scratch += [pltpu.VMEM((count, width), BF16)]
    got = call(body, outs, [shifts, tokens, plan.table], [HBM] * 3, scratch, 3, 1 << 28, 1 << 20)
    sent, (rows, flags, one, two, three) = got[:kinds], got[kinds:]
    return sent, rows, flags, one[0], two[0], three[0]


def before_fine(flags, regions, tokens, table, weights, plan):
    _, lat, lon = regions.shape
    _, rows, cols, width = tokens.shape
    flat_regions = regions.reshape(2 * lat, lon)
    fine, coarse = windowed(rows, cols), natural(rows // 2, cols // 2)
    places = np.asarray(fine + coarse, np.float32)
    places[len(fine) :, 1:] *= 2
    pad = -len(places) % 128
    places = np.pad(places, ((0, pad), (0, 0))).T.reshape(3, -1, 128)
    is_fine = np.pad(np.ones(len(fine), np.float32), (0, len(coarse) + pad)).reshape(1, -1, 128)
    places = np.concatenate([places, is_fine])
    count = len(fine) + len(coarse)

    def body(flags_ref, rows_ref, regions_hbm, places_hbm, tokens_hbm, *refs):
        weights_hbm, refs = refs[: len(weights)], refs[len(weights) :]
        fine_ref, coarse_hbm, x_ref, *refs = refs
        weight_refs, (regions_ref, places_ref, tokens_ref, coarse_ref, sems) = refs[: len(weights)], refs[len(weights) :]
        start = Copies(sems)
        waits = [start(regions_hbm, regions_ref), start(places_hbm, places_ref)]
        held = start(tokens_hbm, tokens_ref)
        later = [start(src, dst) for src, dst in zip(weights_hbm, weight_refs)]
        for copy in waits:
            copy.wait()
        a = flags_ref[1].astype(F32)
        big_a = 2.0 * flags_ref[2].astype(F32)
        is_fine = places_ref[3]
        d = is_fine * a + (1.0 - is_fine) * big_a
        row = places_ref[1] + d + (lax.axis_index("lat") * rows).astype(F32)
        col = places_ref[2] + 2.0 * d + (lax.axis_index("lon") * cols).astype(F32)
        wrapped = jnp.where((row < 0) | (row >= lat), 4.0, 0.0)
        row = jnp.where(row < 0, row + lat, jnp.where(row >= lat, row - lat, row))
        col = jnp.where(col < 0, col + lon, jnp.where(col >= lon, col - lon, col))
        row = columns_of(row + places_ref[0] * lat, count)
        col = columns_of(col, count)
        wrapped = columns_of(wrapped, count)
        picked = select_rows(row, regions_ref[...].astype(F32).astype(BF16))
        ids = jnp.zeros((count, 128), F32)
        for at in range(0, lon, 128):
            size = min(128, lon - at)
            lane = lax.broadcasted_iota(I32, (1, size), 1).astype(F32) + float(at)
            here = jnp.where(lane == col[:, :size], picked[:, at : at + size], 0.0)
            ids = ids + jnp.sum(here, axis=1, keepdims=True)
        lane = lax.broadcasted_iota(I32, (1, 128), 1).astype(F32)
        hot = jnp.where(lane == ids + wrapped, 1.0, 0.0).astype(BF16)
        fine_ref[...] = hot[: len(fine)]
        coarse_ref[...] = hot[len(fine) :]
        later.append(start(coarse_ref, coarse_hbm))
        held.wait()
        take = columns_of(rows_of(plan, rows_ref, "take_one"), len(fine))
        x_ref[...] = select_rows(take, flat(tokens_ref)).astype(BF16)
        for copy in later:
            copy.wait()

    outs = shapes([len(fine)], 128) + shapes([len(coarse)], 128, pltpu.HBM) + shapes([len(fine)], width)
    outs += [pltpu.VMEM(w.shape, BF16) for w in weights]
    scratch = [pltpu.VMEM(flat_regions.shape, I32), pltpu.VMEM(places.shape, F32), pltpu.VMEM(tokens.shape, BF16)]
    scratch += [pltpu.VMEM((len(coarse), 128), BF16)]
    args = [flags, table, flat_regions, places, tokens, *weights]
    in_specs = [SMEM, VMEM] + [HBM] * (3 + len(weights))
    fine_id, coarse_id, x, *weights = call(body, outs, args, in_specs, scratch, 4 + len(weights), 1 << 28, 4 << 20)
    return fine_id, coarse_id, x, weights


def before_coarse(fine, table, plan):
    own, width = fine.shape

    def body(rows_ref, fine_hbm, x_ref, part_hbm, fine_ref, part_ref, sems):
        start = Copies(sems)
        held = start(fine_hbm, fine_ref)
        take = columns_of(rows_of(plan, rows_ref, "fine_out"), own)
        held.wait()
        part_ref[...] = select_rows(take, fine_ref[...]).astype(BF16)
        leave = start(part_ref, part_hbm)
        take = columns_of(rows_of(plan, rows_ref, "take_two"), own)
        x_ref[...] = select_rows(take, fine_ref[...]).astype(BF16)
        leave.wait()

    outs = shapes([own], width) + shapes([own], width, pltpu.HBM)
    scratch = [pltpu.VMEM(fine.shape, BF16)] * 2
    return call(body, outs, [table, fine], [VMEM, HBM], scratch, 2, 1 << 28, 2 << 20)


def fine_level(x_own, source, key_id, w_qkv, w_proj, rows, plan):
    count, width = x_own.shape
    inner = w_proj.shape[0]

    def body(own_ref, source_ref, id_ref, qkv_w_ref, proj_w_ref, rows_ref, out_hbm, *refs):
        *piece_outs, x_ref, qkv_ref, out_ref, sems = refs
        start = Copies(sems)
        leave = []
        take = columns_of(rows_of(plan, rows_ref, "take_one"), count) - float(count)
        x = own_ref[...].astype(F32) + select_rows(take, source_ref[...])
        x_ref[...] = x
        normed = layer_norm(x).astype(BF16)
        qkv_ref[...] = jnp.dot(normed, qkv_w_ref[...], preferred_element_type=F32).astype(BF16)

        def finish(w, out):
            at = slice(w * TOK, (w + 1) * TOK)
            out = jnp.dot(out, proj_w_ref[...], preferred_element_type=F32)
            out_ref[at, :] = (x_ref[at, :] + out).astype(BF16)
            leave.append(start(out_ref.at[pl.ds(w * TOK, TOK)], out_hbm.at[pl.ds(w * TOK, TOK)]))

        attend_windows(
            lambda w, at: qkv_ref[w * TOK : (w + 1) * TOK, at : at + 128],
            lambda w: id_ref[w * TOK : (w + 1) * TOK, :],
            count // TOK,
            inner,
            finish,
        )
        index = columns_of(rows_of(plan, rows_ref, "send_two"), sum(plan.room_two))
        put_pieces(select_rows(index, out_ref[...]), piece_outs)
        for copy in leave:
            copy.wait()

    outs = shapes([count], width, pltpu.HBM) + shapes(plan.room_two, width)
    scratch = [
        pltpu.VMEM((count, width), F32),
        pltpu.VMEM((count, 3 * inner), BF16),
        pltpu.VMEM((count, width), BF16),
    ]
    args = [x_own, source, key_id, w_qkv, w_proj, rows]
    out, *sent = call(body, outs, args, [VMEM] * len(args), scratch, count // TOK, 3 << 30, 6 << 20, 14)
    return out, sent


def coarse_level(flags, fine, x_own, source, key_id, w_merge, w_qkv, w_proj, rows, plan):
    count = key_id.shape[0]
    depth, width = w_merge.shape
    own, half = fine.shape
    inner = w_proj.shape[0]

    def body(flags_ref, fine_hbm, id_hbm, merge_hbm, qkv_w_hbm, proj_w_hbm, own_ref, source_ref, rows_ref, *refs):
        out_ref, *piece_outs = refs[:4]
        qkv_ref, fine_ref, id_ref, merge_ref, qkv_w_ref, proj_w_ref, sems = refs[4:]
        start = Copies(sems)
        with_fine = [n for n, sizes in enumerate(plan.four) if sum(sizes)]
        needs_fine = functools.reduce(jnp.logical_or, [flags_ref[0] == n for n in with_fine])

        def bring(src, dst):
            return [
                (at, start(src.at[pl.ds(at, half)], dst.at[pl.ds(at, half)])) for at in range(0, src.shape[0], half)
            ]

        def product(x, ref, copies):
            parts = []
            for at, copy in copies:
                copy.wait()
                parts.append(jnp.dot(x[:, at : at + half], ref[at : at + half, :], preferred_element_type=F32))
            return functools.reduce(jnp.add, parts)

        merge_w, qkv_w = bring(merge_hbm, merge_ref), bring(qkv_w_hbm, qkv_w_ref)
        ids, proj_w = start(id_hbm, id_ref), start(proj_w_hbm, proj_w_ref)
        fine_copy = (fine_hbm, fine_ref, sems.at[start.used])

        @pl.when(needs_fine)
        def _():
            pltpu.make_async_copy(*fine_copy).start()

        take = columns_of(rows_of(plan, rows_ref, "take_two"), 4 * count) - float(own)
        x = own_ref[...].astype(F32) + select_rows(take, source_ref[...])
        x = jnp.concatenate([x[n * count : (n + 1) * count] for n in range(4)], axis=1)
        stacked = layer_norm(x).astype(BF16)
        merged = product(stacked, merge_ref, merge_w).astype(BF16).astype(F32)
        normed = layer_norm(merged).astype(BF16)
        qkv_ref[...] = product(normed, qkv_w_ref, qkv_w).astype(BF16)
        ids.wait()
        proj_w.wait()

        def finish(w, out):
            out = jnp.dot(out, proj_w_ref[...], preferred_element_type=F32)
            out_ref[...] = (merged + out).astype(BF16)

        attend_windows(lambda w, at: qkv_ref[:, at : at + 128], lambda w: id_ref[...], 1, inner, finish)
        sent = select_rows(columns_of(rows_of(plan, rows_ref, "send_three"), sum(plan.room_three)), out_ref[...])
        sent = sent.astype(BF16)
        for n, sizes in enumerate(plan.three):

            @pl.when(flags_ref[0] == n)
            def _():
                at = 0
                for ref, size, space in zip(piece_outs, sizes, plan.room_three):
                    ref[:size, :] = sent[at : at + size, :half]
                    ref[size : 2 * size, :] = sent[at : at + size, half:]
                    at += space

        @pl.when(needs_fine)
        def _():
            pltpu.make_async_copy(*fine_copy).wait()
            index = columns_of(rows_of(plan, rows_ref, "send_four"), sum(plan.room_four))
            sent = select_rows(index, fine_ref[...]).astype(BF16)
            for n in with_fine:

                @pl.when(flags_ref[0] == n)
                def _():
                    at = 0
                    for ref, size, more, space in zip(piece_outs, plan.three[n], plan.four[n], plan.room_four):
                        ref[2 * size : 2 * size + more, :] = sent[at : at + more]
                        at += space

    most = [max(2 * three[k] + four[k] for three, four in zip(plan.three, plan.four)) for k in range(3)]
    outs = shapes([count], width) + shapes(most, half)
    scratch = [pltpu.VMEM((count, 3 * inner), BF16)]
    scratch += [pltpu.VMEM(x.shape, BF16) for x in (fine, key_id, w_merge, w_qkv, w_proj)]
    args = [flags, fine, key_id, w_merge, w_qkv, w_proj, x_own, source, rows]
    in_specs = [SMEM] + [HBM] * 5 + [VMEM] * (len(args) - 6)
    copies = depth // half + width // half + 3
    out, *sent = call(body, outs, args, in_specs, scratch, copies, 3 << 30, 12 << 20, 24)
    return out, sent


def fine_output(part, source, rows, plan, block_rows, block_cols, partial):
    own, width = part.shape

    def body(part_hbm, source_ref, rows_ref, out_ref, part_ref, stage_ref, sems):
        start = Copies(sems)
        cuts = [pl.ds(at, TOK) for at in range(0, own, TOK)]
        held = [start(part_hbm.at[cut], part_ref.at[cut]) for cut in cuts]
        take = columns_of(rows_of(plan, rows_ref, "fine_out"), own) - float(own)
        leave = []
        for n, (cut, copy) in enumerate(zip(cuts, held)):
            got = select_rows(take[n * TOK : (n + 1) * TOK], source_ref[...])
            copy.wait()
            out = part_ref[cut, :].astype(F32) + got
            if partial:
                out_ref[cut, :] = out.astype(BF16)
            else:
                lines = TOK // block_cols
                layer, line = divmod(n * lines, block_rows)
                there = (layer, pl.ds(line, lines))
                stage_ref[there] = out.reshape(lines, block_cols, width).astype(BF16)
                leave.append(start(stage_ref.at[there], out_ref.at[there]))
        for copy in leave:
            copy.wait()

    shape = (2, block_rows, block_cols, width)
    outs = shapes([own], width) if partial else [pltpu.HBM(shape, BF16)]
    scratch = [pltpu.VMEM(part.shape, BF16), pltpu.VMEM(shape, BF16)]
    return call(body, outs, [part, source, rows], [HBM, VMEM, VMEM], scratch, 2 * own // TOK, 1 << 30, 4 << 20)[0]


def coarse_output(coarse, got, rows, which, plan, block_rows, block_cols, part=None):
    own, width = coarse.shape
    half = width // 2
    sizes, more = plan.three[which], plan.four[which]
    parts = [] if part is None else [part]

    def padded(parts, sizes, room):
        out = []
        for value, size, space in zip(parts, sizes, room):
            out.append(value)
            if size < space:
                out.append(jnp.zeros((space - size, value.shape[1]), F32))
        return out

    def body(coarse_ref, *refs):
        got_refs, refs = refs[:3], refs[3:]
        part_refs, (rows_ref, out_ref, *fine_outs, _) = refs[: len(parts)], refs[len(parts) :]
        got = [ref[...].astype(F32) for ref in got_refs]
        back = [jnp.concatenate([x[:size], x[size : 2 * size]], axis=1) for x, size in zip(got, sizes)]
        source = stack_rows([coarse_ref[...].astype(F32)] + padded(back, sizes, plan.room_three))
        out = select_rows(columns_of(rows_of(plan, rows_ref, "coarse_out"), own), source.astype(BF16)).astype(BF16)
        for n in range(own // 2):
            out_ref[n // block_cols, n % block_cols] = out[2 * n : 2 * n + 2]
        for part_ref, fine_ref in zip(part_refs, fine_outs):
            fine = stack_rows(padded([x[2 * size :] for x, size in zip(got, sizes)], more, plan.room_four))
            base = part_ref.shape[0] + sum(plan.room_two)
            take = columns_of(rows_of(plan, rows_ref, "fine_out"), part_ref.shape[0]) - float(base)
            out = part_ref[...].astype(F32) + select_rows(take, fine.astype(BF16))
            fine_ref[...] = out.reshape(fine_ref.shape).astype(BF16)

    outs = [jax.ShapeDtypeStruct((block_rows, block_cols, 2, width), BF16)]
    outs += [jax.ShapeDtypeStruct((2, 2 * block_rows, 2 * block_cols, half), BF16) for _ in parts]
    args = [coarse, *got, *parts, rows]
    out, *fine = call(body, outs, args, [VMEM] * len(args), [], 1, 1 << 28, 1 << 20)
    return out.transpose(2, 0, 1, 3), *fine


def on_device(tokens, regions, shifts, fine_qkv, fine_proj, merge_weight, coarse_qkv, coarse_proj):
    _, rows, cols, _ = tokens.shape
    plan = Plan(rows, cols)

    def first(which, sign, sent, *args):
        got = exchange(sent, plan.one[which], sign)
        return lay(got, plan.room_one), before_fine(*args, plan)

    def second(which, sign, sent, *args):
        got = exchange(sent, plan.two[which], sign)
        return lay(got, plan.room_two), before_coarse(*args, plan)

    def third(which, sign, sent, part, source, coarse, table):
        sizes = [2 * n + m for n, m in zip(plan.three[which], plan.four[which])]
        got = exchange(sent, sizes, sign)
        partial = sum(plan.four[which]) > 0
        fine_out = fine_output(part, source, table, plan, rows, cols, partial)
        place = (table, which, plan, rows // 2, cols // 2)
        if partial:
            coarse_out, fine_out = coarse_output(coarse, got, *place, part=fine_out)
        else:
            (coarse_out,) = coarse_output(coarse, got, *place)
        return fine_out, coarse_out

    def branches(stage, pairs):
        return [functools.partial(stage, which, sign) for which, sign in pairs]

    sent, table, flags, one, two, three = first_pieces(shifts, tokens, plan)
    got, (fine_id, coarse_id, x, weights) = choose(
        one, branches(first, plan.one_branches), sent, flags, regions, tokens, table, [fine_qkv, fine_proj]
    )
    fine, sent = fine_level(x, got, fine_id, *weights, table, plan)
    got, (x, part) = choose(two, branches(second, plan.two_branches), sent, fine, table)
    coarse, sent = coarse_level(
        flags, fine, x, got, coarse_id, merge_weight, coarse_qkv, coarse_proj, table, plan
    )
    return choose(three, branches(third, plan.three_branches), sent, part, got, coarse, table)


def solution(mesh):
    return jax.shard_map(
        on_device,
        mesh=mesh,
        in_specs=(P(None, "lat", "lon", None), P(), P(), P(), P(), P(), P(), P()),
        out_specs=(P(None, "lat", "lon", None), P(None, "lat", "lon", None)),
        check_vma=False,
    )
```

```python
import functools

import jax
import jax.numpy as jnp
import numpy as np
from jax import lax
from jax.experimental import pallas as pl
from jax.experimental.pallas import tpu as pltpu
from jax.sharding import PartitionSpec as P

HD = 32
WH = 6
WW = 12
TOK = 2 * WH * WW
EPS = 1e-05
BIG = 1e30
SCALE = float(np.log2(np.e) / np.sqrt(HD))

NT = (((1,), (1,)), ((), ()))
F32 = jnp.float32
BF16 = jnp.bfloat16
I32 = jnp.int32

PAIRS = [(WH - 1, t) for t in range(1, WH)] + [(t, WH - 1) for t in range(1, WH - 1)]


def up16(count):
    return -(-count // 16) * 16


def natural(rows, cols):
    return [(l, r, c) for l in range(2) for r in range(rows) for c in range(cols)]


def windowed(rows, cols):
    return [
        (l, wr * WH + r, wc * WW + c)
        for wr in range(rows // WH)
        for wc in range(cols // WW)
        for l in range(2)
        for r in range(WH)
        for c in range(WW)
    ]


def moved(order, d):
    return [(l, r + d, c + 2 * d) for l, r, c in order]


def exchange_places(held, wanted, rows, cols, sign):
    at = {place: n for n, place in enumerate(held)}
    found = []
    for dr, dc in ((sign, 0), (0, sign), (sign, sign)):
        numbers, places = [], []
        for l, r, c in sorted(set(wanted) - set(held)):
            n = at.get((l, r - dr * rows, c - dc * cols))
            if n is not None:
                numbers.append(n)
                places.append((l, r, c))
        found.append((numbers, places))
    return found


def offsets(t0, t1):
    a = t0 if t0 <= 2 else t0 - WH
    big_a = t1 if t1 <= 2 else t1 - WH
    ahead = 1 if 2 * big_a > a or 2 * big_a - a == 0 and a < 0 else -1
    return a, big_a, ahead


def classes_of(needs, slack):
    rounded = [tuple(-(-size // 8) * 8 for size in need) for need in needs]
    heavy = [sum(need[1:3]) * 2 + sum(need[4:]) for need in rounded]
    limits = []
    for size in sorted(set(heavy)):
        if not limits or size > limits[-1][0] * slack:
            limits.append([size, size])
        limits[-1][1] = size
    which = [next(n for n, limit in enumerate(limits) if size <= limit[1]) for size in heavy]
    sizes = [
        [max(need[k] for need, w in zip(rounded, which) if w == n) for k in range(len(needs[0]))]
        for n in range(len(limits))
    ]
    return sizes, which


def rooms(sizes):
    return [up16(max(size[k] for size in sizes)) for k in range(len(sizes[0]))]


class Plan:
    def __init__(self, rows, cols):
        crows, ccols = rows // 2, cols // 2
        block, cblock = natural(rows, cols), natural(crows, ccols)
        cases = []
        for t0, t1 in PAIRS:
            a, big_a, ahead = offsets(t0, t1)
            fine = moved(windowed(rows, cols), a)
            coarse = moved(cblock, big_a)
            quarters = [
                (l, 2 * r + dr, 2 * c + dc)
                for dr, dc in ((0, 0), (1, 0), (0, 1), (1, 1))
                for l, r, c in coarse
            ]
            come = 1 if a > 0 else -1
            one = exchange_places(block, fine, rows, cols, come)
            home = [p for p in block if p not in set(fine)]
            wanted = quarters + (home if come == -ahead else [])
            two = exchange_places(fine, wanted, rows, cols, ahead)
            back = 1 if big_a < 0 else -1
            three = exchange_places(coarse, cblock, crows, ccols, back)
            got = set(fine).union(*[places for _, places in two])
            four = exchange_places(fine, [p for p in block if p not in got], rows, cols, back)
            cases.append((come, ahead, back, fine, coarse, quarters, one, two, three, four))

        def needs(which):
            return [[len(numbers) for numbers, _ in case[which]] for case in cases]

        self.one, one_class = classes_of(needs(6), 1.15)
        self.two, two_class = classes_of(needs(7), 1.15)
        sizes, three_class = classes_of([three + four for three, four in zip(needs(8), needs(9))], 1.0)
        self.three, self.four = [size[:3] for size in sizes], [size[3:] for size in sizes]
        self.room_one, self.room_two = rooms(self.one), rooms(self.two)
        self.room_three, self.room_four = rooms(self.three), rooms(self.four)

        def branches(which_class, direction):
            pairs = [(n, case[direction]) for n, case in zip(which_class, cases)]
            found = sorted(set(pairs))
            return found, [found.index(pair) for pair in pairs]

        self.one_branches, one_at = branches(one_class, 0)
        self.two_branches, two_at = branches(two_class, 1)
        self.three_branches, three_at = branches(three_class, 2)
        self.flags = dict(
            three_class=three_class,
            one_at=one_at, two_at=two_at, three_at=three_at,
            a=[offsets(*pair)[0] for pair in PAIRS], big_a=[offsets(*pair)[1] for pair in PAIRS],
        )

        found = {}
        for n, (come, ahead, back, fine, coarse, quarters, one, two, three, four) in enumerate(cases):

            def send(exchanged, room):
                return [n for (numbers, _), size in zip(exchanged, room) for n in numbers + [-1] * (size - len(numbers))]

            def source(held, *exchanges):
                places = list(held)
                for exchanged, room in exchanges:
                    for (_, got), size in zip(exchanged, room):
                        places += got + [None] * (size - len(got))
                return {p: n for n, p in enumerate(places) if p is not None}

            first, second = source(block, (one, self.room_one)), source(fine, (two, self.room_two))
            third = source(coarse, (three, self.room_three))
            last = source(fine, (two, self.room_two), (four, self.room_four))
            out = [(l, r, c) for r in range(crows) for c in range(ccols) for l in range(2)]
            rows_of = dict(
                send_one=send(one, self.room_one),
                take_one=[first[p] for p in fine],
                send_two=send(two, self.room_two),
                take_two=[second[p] for p in quarters],
                send_three=send(three, self.room_three),
                send_four=send(four, self.room_four),
                fine_out=[last[p] for p in block],
                coarse_out=[third[p] for p in out],
            )
            for name, row in rows_of.items():
                found.setdefault(name, []).append(row)
        parts, self.at, top = [], {}, 0
        for name, lists in found.items():
            length = -(-max(len(row) for row in lists) // 128)
            part = np.full((len(PAIRS), length * 128), -1, np.float32)
            for n, row in enumerate(lists):
                part[n, : len(row)] = row
            parts.append(part.reshape(len(PAIRS), length, 128))
            self.at[name] = (top, length)
            top += length
        parts.append(np.zeros((len(PAIRS), -top % 8, 128), np.float32))
        self.table = np.concatenate(parts, axis=1)


def case_of(shifts_ref):
    t0, t1 = shifts_ref[0], shifts_ref[1]
    return jnp.where(t0 == WH - 1, t1 - 1, t0 + WH - 2)


def lookup(values, case):
    out = jnp.int32(values[0])
    for n, value in enumerate(values[1:], 1):
        out = jnp.where(case == n, value, out)
    return out


def columns_of(rows, count):
    parts = [jnp.broadcast_to(rows[j : j + 1], (128, 128)).T for j in range(-(-count // 128))]
    return stack_rows(parts)[:count]


def select_rows(index, source):
    lane = lax.broadcasted_iota(I32, (1, 128), 1).astype(F32)
    size = source.shape[0]
    pick = [jnp.where(index == lane + float(at), 1.0, 0.0).astype(BF16) for at in range(0, size, 128)]
    pick = jnp.concatenate(pick, axis=1)[:, :size]
    return jnp.dot(pick, source, preferred_element_type=F32)


def stack_rows(parts):
    return parts[0] if len(parts) == 1 else jnp.concatenate(parts, axis=0)


def layer_norm(values):
    center = jnp.mean(values, axis=-1, keepdims=True)
    values = values - center
    spread = jnp.mean(values * values, axis=-1, keepdims=True)
    return values * lax.rsqrt(spread + EPS)


def attend_windows(qkv_of, id_of, windows, inner, finish):
    lane = lax.broadcasted_iota(I32, (1, 128), 1)
    forbid = jnp.where(lane < 8, BIG, 0.0).astype(BF16)
    groups = inner // 128
    units = [(w, g) for w in range(windows) for g in range(groups)]
    scores, weights, outs = {}, {}, {}

    def score(w, g):
        key_id = id_of(w)
        not_id = (key_id - 1).astype(BF16) * forbid
        q = qkv_of(w, g * 128)
        keys = jnp.concatenate([qkv_of(w, inner + g * 128), key_id], axis=1)
        queries = []
        for h in range(4):
            mine = jnp.where((lane >= h * HD) & (lane < (h + 1) * HD), 1.0, 0.0).astype(BF16)
            queries.append(jnp.concatenate([q * mine, not_id], axis=1))
        scores[w, g] = lax.dot_general(stack_rows(queries), keys, NT, preferred_element_type=F32)

    def soften(w, g):
        s = scores.pop((w, g))
        weights[w, g] = jnp.exp2((s - jnp.max(s, axis=1, keepdims=True)) * SCALE).astype(BF16)

    def gather(w, g):
        v = qkv_of(w, 2 * inner + g * 128)
        values = jnp.concatenate([v, jnp.ones_like(v)], axis=1)
        out = jnp.dot(weights.pop((w, g)), values, preferred_element_type=F32)
        out = out[:, :128] * (1.0 / out[:, 128:])
        picked = out[:TOK]
        for h in range(1, 4):
            picked = jnp.where(lane < h * HD, picked, out[h * TOK : (h + 1) * TOK])
        outs[w, g] = picked.astype(BF16)
        if g == groups - 1:
            finish(w, jnp.concatenate([outs.pop((w, k)) for k in range(groups)], axis=1))

    for n in range(len(units) + 2):
        if n < len(units):
            score(*units[n])
        if 0 <= n - 1 < len(units):
            soften(*units[n - 1])
        if 0 <= n - 2 < len(units):
            gather(*units[n - 2])


ANY = pl.BlockSpec(memory_space=pl.ANY)
HBM = pl.BlockSpec(memory_space=pltpu.HBM)
VMEM = pl.BlockSpec(memory_space=pltpu.VMEM)
SMEM = pl.BlockSpec(memory_space=pltpu.SMEM)


def call(body, outs, args, in_specs, scratch, copies, flops, moved_bytes, vmem=8):
    args = [
        pltpu.with_memory_space_constraint(arg, spec.memory_space) for arg, spec in zip(args, in_specs, strict=True)
    ]
    spaces = [getattr(out, "memory_space", pltpu.SMEM if out.dtype == I32 else pltpu.VMEM) for out in outs]
    out_specs = [pl.BlockSpec(memory_space=space) for space in spaces]
    return pl.pallas_call(
        body,
        out_shape=outs,
        in_specs=in_specs,
        out_specs=out_specs,
        scratch_shapes=list(scratch) + [pltpu.SemaphoreType.DMA((copies,))],
        compiler_params=pltpu.CompilerParams(vmem_limit_bytes=vmem << 20),
        cost_estimate=pl.CostEstimate(flops=flops, bytes_accessed=moved_bytes, transcendentals=0),
    )(*args)


def shapes(sizes, width, space=pltpu.VMEM):
    return [space((n, width), BF16) for n in sizes]


class Copies:
    def __init__(self, sems):
        self.sems, self.used = sems, 0

    def __call__(self, src, dst):
        copy = pltpu.make_async_copy(src, dst, self.sems.at[self.used])
        self.used += 1
        copy.start()
        return copy


def lay(pieces, room):
    width = pieces[0].shape[1]

    def body(*refs):
        out_ref = refs[len(pieces)]
        at = 0
        for ref, space in zip(refs, room):
            rows = ref.shape[0]
            out_ref[at : at + rows, :] = ref[...]
            if rows < space:
                out_ref[at + rows : at + space, :] = jnp.zeros((space - rows, width), BF16)
            at += space

    return call(body, shapes([sum(room)], width), pieces, [VMEM] * 3, [], 1, 0, 1 << 18)[0]


def flat(ref):
    layers, rows, cols, width = ref.shape
    return ref[...].astype(F32).reshape(layers * rows * cols, width).astype(BF16)


def put_pieces(value, refs):
    at = 0
    for ref in refs:
        ref[...] = value[at : at + ref.shape[0]].astype(BF16)
        at += ref.shape[0]


def rows_of(plan, table_ref, name, *lead):
    top, length = plan.at[name]
    return table_ref[(*lead, slice(top, top + length), slice(None))]


def exchange(pieces, sizes, sign):
    lat, lon = lax.axis_size("lat"), lax.axis_size("lon")
    row, col, both = [piece[:size] for piece, size in zip(pieces, sizes)]
    pairs = [((i + sign) % lat * lon + (j + sign) % lon, i * lon + j) for i in range(lat) for j in range(lon)]
    col = lax.ppermute(col, "lon", [((j + sign) % lon, j) for j in range(lon)])
    both = lax.ppermute(both, ("lat", "lon"), pairs)
    row = lax.ppermute(row, "lat", [((i + sign) % lat, i) for i in range(lat)])
    return [row, col, both]


def choose(index, branches, *args):
    flat_args, tree = jax.tree.flatten(args)
    out_trees = []

    def closed(branch):
        def run(*leaves):
            out, out_tree = jax.tree.flatten(branch(*jax.tree.unflatten(tree, leaves)))
            out_trees.append(out_tree)
            return out

        return jax.make_jaxpr(run)(*flat_args)

    out = lax.cond_p.bind(index, *flat_args, branches=tuple(closed(branch) for branch in branches))
    return jax.tree.unflatten(out_trees[0], out)


FLAGS = ("three_class", "a", "big_a")


def first_pieces(shifts, tokens, plan):
    width = tokens.shape[-1]
    count = tokens.size // width
    kinds = 3

    def body(shifts_hbm, tokens_hbm, table_hbm, *refs):
        outs, refs = refs[:kinds], refs[kinds:]
        rows_ref, flags_ref, *at_refs, shifts_ref, tokens_ref, table_ref, source_ref, sems = refs
        start = Copies(sems)
        shift = start(shifts_hbm, shifts_ref)
        held = start(tokens_hbm, tokens_ref)
        table = start(table_hbm, table_ref)
        shift.wait()
        case = case_of(shifts_ref)
        for ref, name in zip(at_refs, ("one_at", "two_at", "three_at")):
            ref[0] = lookup(plan.flags[name], case)
        for n, name in enumerate(FLAGS):
            flags_ref[n] = lookup(plan.flags[name], case)
        held.wait()
        source_ref[...] = flat(tokens_ref)
        table.wait()
        rows_ref[...] = table_ref[case]
        index = columns_of(rows_of(plan, table_ref, "send_one", case), sum(plan.room_one))
        put_pieces(select_rows(index, source_ref[...]), outs)

    outs = shapes(plan.room_one, width)
    outs += [pltpu.VMEM(plan.table.shape[1:], F32), pltpu.SMEM((8,), I32)]
    outs += [pltpu.SMEM((1,), I32)] * 3
    scratch = [pltpu.SMEM((2,), I32), pltpu.VMEM(tokens.shape, BF16), pltpu.VMEM(plan.table.shape, F32)]
    scratch += [pltpu.VMEM((count, width), BF16)]
    got = call(body, outs, [shifts, tokens, plan.table], [HBM] * 3, scratch, 3, 1 << 28, 1 << 20)
    sent, (rows, flags, one, two, three) = got[:kinds], got[kinds:]
    return sent, rows, flags, one[0], two[0], three[0]


def before_fine(flags, regions, tokens, table, weights, plan):
    _, lat, lon = regions.shape
    _, rows, cols, width = tokens.shape
    flat_regions = regions.reshape(2 * lat, lon)
    fine, coarse = windowed(rows, cols), natural(rows // 2, cols // 2)
    places = np.asarray(fine + coarse, np.float32)
    places[len(fine) :, 1:] *= 2
    pad = -len(places) % 128
    places = np.pad(places, ((0, pad), (0, 0))).T.reshape(3, -1, 128)
    is_fine = np.pad(np.ones(len(fine), np.float32), (0, len(coarse) + pad)).reshape(1, -1, 128)
    places = np.concatenate([places, is_fine])
    count = len(fine) + len(coarse)

    def body(flags_ref, rows_ref, regions_hbm, places_hbm, tokens_hbm, *refs):
        weights_hbm, refs = refs[: len(weights)], refs[len(weights) :]
        fine_hbm, coarse_hbm, x_ref, *refs = refs
        weight_refs, (regions_ref, places_ref, tokens_ref, id_ref, sems) = refs[: len(weights)], refs[len(weights) :]
        start = Copies(sems)
        waits = [start(regions_hbm, regions_ref), start(places_hbm, places_ref)]
        held = start(tokens_hbm, tokens_ref)
        later = [start(src, dst) for src, dst in zip(weights_hbm, weight_refs)]
        for copy in waits:
            copy.wait()
        a = flags_ref[1].astype(F32)
        big_a = 2.0 * flags_ref[2].astype(F32)
        is_fine = places_ref[3]
        d = is_fine * a + (1.0 - is_fine) * big_a
        row = places_ref[1] + d + (lax.axis_index("lat") * rows).astype(F32)
        col = places_ref[2] + 2.0 * d + (lax.axis_index("lon") * cols).astype(F32)
        wrapped = jnp.where((row < 0) | (row >= lat), 4.0, 0.0)
        row = jnp.where(row < 0, row + lat, jnp.where(row >= lat, row - lat, row))
        col = jnp.where(col < 0, col + lon, jnp.where(col >= lon, col - lon, col))
        row = columns_of(row + places_ref[0] * lat, count)
        col = columns_of(col, count)
        wrapped = columns_of(wrapped, count)
        picked = select_rows(row, regions_ref[...].astype(F32).astype(BF16))
        ids = jnp.zeros((count, 128), F32)
        for at in range(0, lon, 128):
            size = min(128, lon - at)
            lane = lax.broadcasted_iota(I32, (1, size), 1).astype(F32) + float(at)
            here = jnp.where(lane == col[:, :size], picked[:, at : at + size], 0.0)
            ids = ids + jnp.sum(here, axis=1, keepdims=True)
        lane = lax.broadcasted_iota(I32, (1, 128), 1).astype(F32)
        hot = jnp.where(lane == ids + wrapped, 1.0, 0.0).astype(BF16)
        id_ref[...] = hot
        later.append(start(id_ref.at[pl.ds(0, len(fine))], fine_hbm))
        later.append(start(id_ref.at[pl.ds(len(fine), len(coarse))], coarse_hbm))
        held.wait()
        take = columns_of(rows_of(plan, rows_ref, "take_one"), len(fine))
        x_ref[...] = select_rows(take, flat(tokens_ref)).astype(BF16)
        for copy in later:
            copy.wait()

    outs = shapes([len(fine), len(coarse)], 128, pltpu.HBM) + shapes([len(fine)], width)
    outs += [pltpu.VMEM(w.shape, BF16) for w in weights]
    scratch = [pltpu.VMEM(flat_regions.shape, I32), pltpu.VMEM(places.shape, F32), pltpu.VMEM(tokens.shape, BF16)]
    scratch += [pltpu.VMEM((count, 128), BF16)]
    args = [flags, table, flat_regions, places, tokens, *weights]
    in_specs = [SMEM, VMEM] + [HBM] * (3 + len(weights))
    fine_id, coarse_id, x, *weights = call(body, outs, args, in_specs, scratch, 5 + len(weights), 1 << 28, 4 << 20)
    return fine_id, coarse_id, x, weights


def before_coarse(fine, table, weight, plan):
    own, width = fine.shape
    half = weight.shape[0] // 2

    def body(rows_ref, fine_hbm, weight_hbm, x_ref, part_hbm, weight_ref, fine_ref, part_ref, sems):
        start = Copies(sems)
        held = start(fine_hbm, fine_ref)
        later = start(weight_hbm.at[pl.ds(0, half)], weight_ref)
        take = columns_of(rows_of(plan, rows_ref, "fine_out"), own)
        held.wait()
        part_ref[...] = select_rows(take, fine_ref[...]).astype(BF16)
        leave = start(part_ref, part_hbm)
        take = columns_of(rows_of(plan, rows_ref, "take_two"), own)
        x_ref[...] = select_rows(take, fine_ref[...]).astype(BF16)
        leave.wait()
        later.wait()

    outs = shapes([own], width) + shapes([own], width, pltpu.HBM) + shapes([half], weight.shape[1])
    scratch = [pltpu.VMEM(fine.shape, BF16)] * 2
    return call(body, outs, [table, fine, weight], [VMEM, HBM, HBM], scratch, 3, 1 << 28, 4 << 20)


def fine_level(x_own, source, key_id, w_qkv, w_proj, rows, plan):
    count, width = x_own.shape
    inner = w_proj.shape[0]

    def body(own_ref, source_ref, id_hbm, qkv_w_ref, proj_w_ref, rows_ref, out_hbm, *refs):
        *piece_outs, x_ref, qkv_ref, out_ref, id_ref, sems = refs
        start = Copies(sems)
        ids = start(id_hbm, id_ref)
        leave = []
        take = columns_of(rows_of(plan, rows_ref, "take_one"), count) - float(count)
        x = own_ref[...].astype(F32) + select_rows(take, source_ref[...])
        x_ref[...] = x
        normed = layer_norm(x).astype(BF16)
        qkv_ref[...] = jnp.dot(normed, qkv_w_ref[...], preferred_element_type=F32).astype(BF16)

        def finish(w, out):
            at = slice(w * TOK, (w + 1) * TOK)
            out = jnp.dot(out, proj_w_ref[...], preferred_element_type=F32)
            out_ref[at, :] = (x_ref[at, :] + out).astype(BF16)
            leave.append(start(out_ref.at[pl.ds(w * TOK, TOK)], out_hbm.at[pl.ds(w * TOK, TOK)]))

        ids.wait()
        attend_windows(
            lambda w, at: qkv_ref[w * TOK : (w + 1) * TOK, at : at + 128],
            lambda w: id_ref[w * TOK : (w + 1) * TOK, :],
            count // TOK,
            inner,
            finish,
        )
        index = columns_of(rows_of(plan, rows_ref, "send_two"), sum(plan.room_two))
        put_pieces(select_rows(index, out_ref[...]), piece_outs)
        for copy in leave:
            copy.wait()

    outs = shapes([count], width, pltpu.HBM) + shapes(plan.room_two, width)
    scratch = [
        pltpu.VMEM((count, width), F32),
        pltpu.VMEM((count, 3 * inner), BF16),
        pltpu.VMEM((count, width), BF16),
        pltpu.VMEM(key_id.shape, BF16),
    ]
    args = [x_own, source, key_id, w_qkv, w_proj, rows]
    in_specs = [VMEM, VMEM, HBM, VMEM, VMEM, VMEM]
    out, *sent = call(body, outs, args, in_specs, scratch, 1 + count // TOK, 3 << 30, 6 << 20, 14)
    return out, sent


def coarse_level(flags, fine, x_own, source, key_id, merge_first, w_merge, w_qkv, w_proj, rows, plan):
    count = key_id.shape[0]
    depth, width = w_merge.shape
    own, half = fine.shape
    inner = w_proj.shape[0]

    def body(
        flags_ref, fine_hbm, id_hbm, merge_hbm, qkv_w_hbm, proj_w_hbm, own_ref, source_ref, first_ref, rows_ref, *refs
    ):
        out_ref, *piece_outs = refs[:4]
        qkv_ref, fine_ref, id_ref, merge_ref, qkv_w_ref, proj_w_ref, sems = refs[4:]
        start = Copies(sems)
        with_fine = [n for n, sizes in enumerate(plan.four) if sum(sizes)]
        needs_fine = functools.reduce(jnp.logical_or, [flags_ref[0] == n for n in with_fine])

        def bring(src, dst):
            return [
                (at, start(src.at[pl.ds(at, half)], dst.at[pl.ds(at, half)])) for at in range(0, src.shape[0], half)
            ]

        def product(x, ref, copies):
            parts = []
            for at, copy in copies:
                copy.wait()
                parts.append(jnp.dot(x[:, at : at + half], ref[at : at + half, :], preferred_element_type=F32))
            return functools.reduce(jnp.add, parts)

        here = first_ref.shape[0]
        merge_w = bring(merge_hbm.at[pl.ds(here, depth - here)], merge_ref)
        qkv_w = bring(qkv_w_hbm, qkv_w_ref)
        ids, proj_w = start(id_hbm, id_ref), start(proj_w_hbm, proj_w_ref)
        fine_copy = (fine_hbm, fine_ref, sems.at[start.used])

        @pl.when(needs_fine)
        def _():
            pltpu.make_async_copy(*fine_copy).start()

        take = columns_of(rows_of(plan, rows_ref, "take_two"), 4 * count) - float(own)
        x = own_ref[...].astype(F32) + select_rows(take, source_ref[...])
        x = jnp.concatenate([x[n * count : (n + 1) * count] for n in range(4)], axis=1)
        stacked = layer_norm(x).astype(BF16)
        merged = jnp.dot(stacked[:, :here], first_ref[...], preferred_element_type=F32)
        merged = (merged + product(stacked[:, here:], merge_ref, merge_w)).astype(BF16).astype(F32)
        normed = layer_norm(merged).astype(BF16)
        qkv_ref[...] = product(normed, qkv_w_ref, qkv_w).astype(BF16)
        ids.wait()
        proj_w.wait()

        def finish(w, out):
            out = jnp.dot(out, proj_w_ref[...], preferred_element_type=F32)
            out_ref[...] = (merged + out).astype(BF16)

        attend_windows(lambda w, at: qkv_ref[:, at : at + 128], lambda w: id_ref[...], 1, inner, finish)
        sent = select_rows(columns_of(rows_of(plan, rows_ref, "send_three"), sum(plan.room_three)), out_ref[...])
        sent = sent.astype(BF16)
        for n, sizes in enumerate(plan.three):

            @pl.when(flags_ref[0] == n)
            def _():
                at = 0
                for ref, size, space in zip(piece_outs, sizes, plan.room_three):
                    ref[:size, :] = sent[at : at + size, :half]
                    ref[size : 2 * size, :] = sent[at : at + size, half:]
                    at += space

        @pl.when(needs_fine)
        def _():
            pltpu.make_async_copy(*fine_copy).wait()
            index = columns_of(rows_of(plan, rows_ref, "send_four"), sum(plan.room_four))
            sent = select_rows(index, fine_ref[...]).astype(BF16)
            for n in with_fine:

                @pl.when(flags_ref[0] == n)
                def _():
                    at = 0
                    for ref, size, more, space in zip(piece_outs, plan.three[n], plan.four[n], plan.room_four):
                        ref[2 * size : 2 * size + more, :] = sent[at : at + more]
                        at += space

    most = [max(2 * three[k] + four[k] for three, four in zip(plan.three, plan.four)) for k in range(3)]
    outs = shapes([count], width) + shapes(most, half)
    scratch = [pltpu.VMEM((count, 3 * inner), BF16)]
    scratch += [pltpu.VMEM(x.shape, BF16) for x in (fine, key_id, merge_first, w_qkv, w_proj)]
    args = [flags, fine, key_id, w_merge, w_qkv, w_proj, x_own, source, merge_first, rows]
    in_specs = [SMEM] + [HBM] * 5 + [VMEM] * (len(args) - 6)
    copies = depth // half + width // half + 3
    out, *sent = call(body, outs, args, in_specs, scratch, copies, 3 << 30, 12 << 20, 24)
    return out, sent


def fine_output(part, source, rows, plan, block_rows, block_cols, partial):
    own, width = part.shape

    def body(part_hbm, source_ref, rows_ref, out_ref, part_ref, stage_ref, sems):
        start = Copies(sems)
        cuts = [pl.ds(at, TOK) for at in range(0, own, TOK)]
        held = [start(part_hbm.at[cut], part_ref.at[cut]) for cut in cuts]
        take = columns_of(rows_of(plan, rows_ref, "fine_out"), own) - float(own)
        leave = []
        for n, (cut, copy) in enumerate(zip(cuts, held)):
            got = select_rows(take[n * TOK : (n + 1) * TOK], source_ref[...])
            copy.wait()
            out = part_ref[cut, :].astype(F32) + got
            if partial:
                out_ref[cut, :] = out.astype(BF16)
            else:
                lines = TOK // block_cols
                layer, line = divmod(n * lines, block_rows)
                there = (layer, pl.ds(line, lines))
                stage_ref[there] = out.reshape(lines, block_cols, width).astype(BF16)
                leave.append(start(stage_ref.at[there], out_ref.at[there]))
        for copy in leave:
            copy.wait()

    shape = (2, block_rows, block_cols, width)
    outs = shapes([own], width) if partial else [pltpu.HBM(shape, BF16)]
    scratch = [pltpu.VMEM(part.shape, BF16), pltpu.VMEM(shape, BF16)]
    return call(body, outs, [part, source, rows], [HBM, VMEM, VMEM], scratch, 2 * own // TOK, 1 << 30, 4 << 20)[0]


def coarse_output(coarse, got, rows, which, plan, block_rows, block_cols, part=None):
    own, width = coarse.shape
    half = width // 2
    sizes, more = plan.three[which], plan.four[which]
    parts = [] if part is None else [part]

    def padded(parts, sizes, room):
        out = []
        for value, size, space in zip(parts, sizes, room):
            out.append(value)
            if size < space:
                out.append(jnp.zeros((space - size, value.shape[1]), F32))
        return out

    def body(coarse_ref, *refs):
        got_refs, refs = refs[:3], refs[3:]
        part_refs, (rows_ref, out_ref, *fine_outs, _) = refs[: len(parts)], refs[len(parts) :]
        got = [ref[...].astype(F32) for ref in got_refs]
        back = [jnp.concatenate([x[:size], x[size : 2 * size]], axis=1) for x, size in zip(got, sizes)]
        source = stack_rows([coarse_ref[...].astype(F32)] + padded(back, sizes, plan.room_three))
        out = select_rows(columns_of(rows_of(plan, rows_ref, "coarse_out"), own), source.astype(BF16)).astype(BF16)
        for n in range(own // 2):
            out_ref[n // block_cols, n % block_cols] = out[2 * n : 2 * n + 2]
        for part_ref, fine_ref in zip(part_refs, fine_outs):
            fine = stack_rows(padded([x[2 * size :] for x, size in zip(got, sizes)], more, plan.room_four))
            base = part_ref.shape[0] + sum(plan.room_two)
            take = columns_of(rows_of(plan, rows_ref, "fine_out"), part_ref.shape[0]) - float(base)
            out = part_ref[...].astype(F32) + select_rows(take, fine.astype(BF16))
            fine_ref[...] = out.reshape(fine_ref.shape).astype(BF16)

    outs = [jax.ShapeDtypeStruct((block_rows, block_cols, 2, width), BF16)]
    outs += [jax.ShapeDtypeStruct((2, 2 * block_rows, 2 * block_cols, half), BF16) for _ in parts]
    args = [coarse, *got, *parts, rows]
    out, *fine = call(body, outs, args, [VMEM] * len(args), [], 1, 1 << 28, 1 << 20)
    return out.transpose(2, 0, 1, 3), *fine


def on_device(tokens, regions, shifts, fine_qkv, fine_proj, merge_weight, coarse_qkv, coarse_proj):
    _, rows, cols, _ = tokens.shape
    plan = Plan(rows, cols)

    def first(which, sign, sent, *args):
        got = exchange(sent, plan.one[which], sign)
        return lay(got, plan.room_one), before_fine(*args, plan)

    def second(which, sign, sent, *args):
        got = exchange(sent, plan.two[which], sign)
        return lay(got, plan.room_two), before_coarse(*args, plan)

    def third(which, sign, sent, part, source, coarse, table):
        sizes = [2 * n + m for n, m in zip(plan.three[which], plan.four[which])]
        got = exchange(sent, sizes, sign)
        partial = sum(plan.four[which]) > 0
        fine_out = fine_output(part, source, table, plan, rows, cols, partial)
        place = (table, which, plan, rows // 2, cols // 2)
        if partial:
            coarse_out, fine_out = coarse_output(coarse, got, *place, part=fine_out)
        else:
            (coarse_out,) = coarse_output(coarse, got, *place)
        return fine_out, coarse_out

    def branches(stage, pairs):
        return [functools.partial(stage, which, sign) for which, sign in pairs]

    sent, table, flags, one, two, three = first_pieces(shifts, tokens, plan)
    got, (fine_id, coarse_id, x, weights) = choose(
        one, branches(first, plan.one_branches), sent, flags, regions, tokens, table, [fine_qkv, fine_proj]
    )
    fine, sent = fine_level(x, got, fine_id, *weights, table, plan)
    got, (x, part, merge_first) = choose(two, branches(second, plan.two_branches), sent, fine, table, merge_weight)
    coarse, sent = coarse_level(
        flags, fine, x, got, coarse_id, merge_first, merge_weight, coarse_qkv, coarse_proj, table, plan
    )
    return choose(three, branches(third, plan.three_branches), sent, part, got, coarse, table)


def solution(mesh):
    return jax.shard_map(
        on_device,
        mesh=mesh,
        in_specs=(P(None, "lat", "lon", None), P(), P(), P(), P(), P(), P(), P()),
        out_specs=(P(None, "lat", "lon", None), P(None, "lat", "lon", None)),
        check_vma=False,
    )
```

```python
import functools

import jax
import jax.numpy as jnp
import numpy as np
from jax import lax
from jax.experimental import pallas as pl
from jax.experimental.pallas import tpu as pltpu
from jax.sharding import PartitionSpec as P

HD = 32
WH = 6
WW = 12
TOK = 2 * WH * WW
EPS = 1e-05
BIG = 1e30
SCALE = float(np.log2(np.e) / np.sqrt(HD))

NT = (((1,), (1,)), ((), ()))
F32 = jnp.float32
BF16 = jnp.bfloat16
I32 = jnp.int32

PAIRS = [(WH - 1, t) for t in range(1, WH)] + [(t, WH - 1) for t in range(1, WH - 1)]


def up16(count):
    return -(-count // 16) * 16


def natural(rows, cols):
    return [(l, r, c) for l in range(2) for r in range(rows) for c in range(cols)]


def windowed(rows, cols):
    return [
        (l, wr * WH + r, wc * WW + c)
        for wr in range(rows // WH)
        for wc in range(cols // WW)
        for l in range(2)
        for r in range(WH)
        for c in range(WW)
    ]


def moved(order, d):
    return [(l, r + d, c + 2 * d) for l, r, c in order]


def exchange_places(held, wanted, rows, cols, sign):
    at = {place: n for n, place in enumerate(held)}
    found = []
    for dr, dc in ((sign, 0), (0, sign), (sign, sign)):
        numbers, places = [], []
        for l, r, c in sorted(set(wanted) - set(held)):
            n = at.get((l, r - dr * rows, c - dc * cols))
            if n is not None:
                numbers.append(n)
                places.append((l, r, c))
        found.append((numbers, places))
    return found


def offsets(t0, t1):
    a = t0 if t0 <= 2 else t0 - WH
    big_a = t1 if t1 <= 2 else t1 - WH
    ahead = 1 if 2 * big_a > a or 2 * big_a - a == 0 and a < 0 else -1
    return a, big_a, ahead


def classes_of(needs, slack):
    rounded = [tuple(-(-size // 8) * 8 for size in need) for need in needs]
    heavy = [sum(need[1:3]) * 2 + sum(need[4:]) for need in rounded]
    limits = []
    for size in sorted(set(heavy)):
        if not limits or size > limits[-1][0] * slack:
            limits.append([size, size])
        limits[-1][1] = size
    which = [next(n for n, limit in enumerate(limits) if size <= limit[1]) for size in heavy]
    sizes = [
        [max(need[k] for need, w in zip(rounded, which) if w == n) for k in range(len(needs[0]))]
        for n in range(len(limits))
    ]
    return sizes, which


def rooms(sizes):
    return [up16(max(size[k] for size in sizes)) for k in range(len(sizes[0]))]


class Plan:
    def __init__(self, rows, cols):
        crows, ccols = rows // 2, cols // 2
        block, cblock = natural(rows, cols), natural(crows, ccols)
        cases = []
        for t0, t1 in PAIRS:
            a, big_a, ahead = offsets(t0, t1)
            fine = moved(windowed(rows, cols), a)
            coarse = moved(cblock, big_a)
            quarters = [
                (l, 2 * r + dr, 2 * c + dc)
                for dr, dc in ((0, 0), (1, 0), (0, 1), (1, 1))
                for l, r, c in coarse
            ]
            come = 1 if a > 0 else -1
            one = exchange_places(block, fine, rows, cols, come)
            home = [p for p in block if p not in set(fine)]
            wanted = quarters + (home if come == -ahead else [])
            two = exchange_places(fine, wanted, rows, cols, ahead)
            back = 1 if big_a < 0 else -1
            three = exchange_places(coarse, cblock, crows, ccols, back)
            got = set(fine).union(*[places for _, places in two])
            four = exchange_places(fine, [p for p in block if p not in got], rows, cols, back)
            cases.append((come, ahead, back, fine, coarse, quarters, one, two, three, four))

        def needs(which):
            return [[len(numbers) for numbers, _ in case[which]] for case in cases]

        self.one, one_class = classes_of(needs(6), 1.15)
        self.two, two_class = classes_of(needs(7), 1.15)
        sizes, three_class = classes_of([three + four for three, four in zip(needs(8), needs(9))], 1.0)
        self.three, self.four = [size[:3] for size in sizes], [size[3:] for size in sizes]
        self.room_one, self.room_two = rooms(self.one), rooms(self.two)
        self.room_three, self.room_four = rooms(self.three), rooms(self.four)

        def branches(which_class, direction):
            pairs = [(n, case[direction]) for n, case in zip(which_class, cases)]
            found = sorted(set(pairs))
            return found, [found.index(pair) for pair in pairs]

        self.one_branches, one_at = branches(one_class, 0)
        self.two_branches, two_at = branches(two_class, 1)
        self.three_branches, three_at = branches(three_class, 2)
        self.flags = dict(
            three_class=three_class,
            one_at=one_at, two_at=two_at, three_at=three_at,
            a=[offsets(*pair)[0] for pair in PAIRS], big_a=[offsets(*pair)[1] for pair in PAIRS],
        )

        found = {}
        for n, (come, ahead, back, fine, coarse, quarters, one, two, three, four) in enumerate(cases):

            def send(exchanged, room):
                return [n for (numbers, _), size in zip(exchanged, room) for n in numbers + [-1] * (size - len(numbers))]

            def source(held, *exchanges):
                places = list(held)
                for exchanged, room in exchanges:
                    for (_, got), size in zip(exchanged, room):
                        places += got + [None] * (size - len(got))
                return {p: n for n, p in enumerate(places) if p is not None}

            first, second = source(block, (one, self.room_one)), source(fine, (two, self.room_two))
            third = source(coarse, (three, self.room_three))
            last = source(fine, (two, self.room_two), (four, self.room_four))
            out = [(l, r, c) for r in range(crows) for c in range(ccols) for l in range(2)]
            rows_of = dict(
                send_one=send(one, self.room_one),
                take_one=[first[p] for p in fine],
                send_two=send(two, self.room_two),
                take_two=[second[p] for p in quarters],
                send_three=send(three, self.room_three),
                send_four=send(four, self.room_four),
                fine_out=[last[p] for p in block],
                coarse_out=[third[p] for p in out],
            )
            for name, row in rows_of.items():
                found.setdefault(name, []).append(row)
        parts, self.at, top = [], {}, 0
        for name, lists in found.items():
            length = -(-max(len(row) for row in lists) // 128)
            part = np.full((len(PAIRS), length * 128), -1, np.float32)
            for n, row in enumerate(lists):
                part[n, : len(row)] = row
            parts.append(part.reshape(len(PAIRS), length, 128))
            self.at[name] = (top, length)
            top += length
        parts.append(np.zeros((len(PAIRS), -top % 8, 128), np.float32))
        self.table = np.concatenate(parts, axis=1)


def case_of(shifts_ref):
    t0, t1 = shifts_ref[0], shifts_ref[1]
    return jnp.where(t0 == WH - 1, t1 - 1, t0 + WH - 2)


def lookup(values, case):
    out = jnp.int32(values[0])
    for n, value in enumerate(values[1:], 1):
        out = jnp.where(case == n, value, out)
    return out


def columns_of(rows, count):
    parts = [jnp.broadcast_to(rows[j : j + 1], (128, 128)).T for j in range(-(-count // 128))]
    return stack_rows(parts)[:count]


def select_rows(index, source):
    lane = lax.broadcasted_iota(I32, (1, 128), 1).astype(F32)
    size = source.shape[0]
    pick = [jnp.where(index == lane + float(at), 1.0, 0.0).astype(BF16) for at in range(0, size, 128)]
    pick = jnp.concatenate(pick, axis=1)[:, :size]
    return jnp.dot(pick, source, preferred_element_type=F32)


def stack_rows(parts):
    return parts[0] if len(parts) == 1 else jnp.concatenate(parts, axis=0)


def layer_norm(values):
    center = jnp.mean(values, axis=-1, keepdims=True)
    values = values - center
    spread = jnp.mean(values * values, axis=-1, keepdims=True)
    return values * lax.rsqrt(spread + EPS)


def attend_windows(qkv_of, id_of, windows, inner, finish):
    lane = lax.broadcasted_iota(I32, (1, 128), 1)
    forbid = jnp.where(lane < 8, BIG, 0.0).astype(BF16)
    groups = inner // 128
    units = [(w, g) for w in range(windows) for g in range(groups)]
    scores, weights, outs = {}, {}, {}

    def score(w, g):
        key_id = id_of(w)
        not_id = (key_id - 1).astype(BF16) * forbid
        q = qkv_of(w, g * 128)
        keys = jnp.concatenate([qkv_of(w, inner + g * 128), key_id], axis=1)
        queries = []
        for h in range(4):
            mine = jnp.where((lane >= h * HD) & (lane < (h + 1) * HD), 1.0, 0.0).astype(BF16)
            queries.append(jnp.concatenate([q * mine, not_id], axis=1))
        scores[w, g] = lax.dot_general(stack_rows(queries), keys, NT, preferred_element_type=F32)

    def soften(w, g):
        s = scores.pop((w, g))
        weights[w, g] = jnp.exp2((s - jnp.max(s, axis=1, keepdims=True)) * SCALE).astype(BF16)

    def gather(w, g):
        v = qkv_of(w, 2 * inner + g * 128)
        values = jnp.concatenate([v, jnp.ones_like(v)], axis=1)
        out = jnp.dot(weights.pop((w, g)), values, preferred_element_type=F32)
        out = out[:, :128] * (1.0 / out[:, 128:])
        picked = out[:TOK]
        for h in range(1, 4):
            picked = jnp.where(lane < h * HD, picked, out[h * TOK : (h + 1) * TOK])
        outs[w, g] = picked.astype(BF16)
        if g == groups - 1:
            finish(w, jnp.concatenate([outs.pop((w, k)) for k in range(groups)], axis=1))

    for n in range(len(units) + 2):
        if n < len(units):
            score(*units[n])
        if 0 <= n - 1 < len(units):
            soften(*units[n - 1])
        if 0 <= n - 2 < len(units):
            gather(*units[n - 2])


ANY = pl.BlockSpec(memory_space=pl.ANY)
HBM = pl.BlockSpec(memory_space=pltpu.HBM)
VMEM = pl.BlockSpec(memory_space=pltpu.VMEM)
SMEM = pl.BlockSpec(memory_space=pltpu.SMEM)


def call(body, outs, args, in_specs, scratch, copies, flops, moved_bytes, vmem=8):
    args = [
        pltpu.with_memory_space_constraint(arg, spec.memory_space) for arg, spec in zip(args, in_specs, strict=True)
    ]
    spaces = [getattr(out, "memory_space", pltpu.SMEM if out.dtype == I32 else pltpu.VMEM) for out in outs]
    out_specs = [pl.BlockSpec(memory_space=space) for space in spaces]
    return pl.pallas_call(
        body,
        out_shape=outs,
        in_specs=in_specs,
        out_specs=out_specs,
        scratch_shapes=list(scratch) + [pltpu.SemaphoreType.DMA((copies,))],
        compiler_params=pltpu.CompilerParams(vmem_limit_bytes=vmem << 20),
        cost_estimate=pl.CostEstimate(flops=flops, bytes_accessed=moved_bytes, transcendentals=0),
    )(*args)


def shapes(sizes, width, space=pltpu.VMEM):
    return [space((n, width), BF16) for n in sizes]


class Copies:
    def __init__(self, sems):
        self.sems, self.used = sems, 0

    def __call__(self, src, dst):
        copy = pltpu.make_async_copy(src, dst, self.sems.at[self.used])
        self.used += 1
        copy.start()
        return copy


def lay(pieces, room):
    width = pieces[0].shape[1]

    def body(*refs):
        out_ref = refs[len(pieces)]
        at = 0
        for ref, space in zip(refs, room):
            rows = ref.shape[0]
            out_ref[at : at + rows, :] = ref[...]
            if rows < space:
                out_ref[at + rows : at + space, :] = jnp.zeros((space - rows, width), BF16)
            at += space

    return call(body, shapes([sum(room)], width), pieces, [VMEM] * 3, [], 1, 0, 1 << 18)[0]


def flat(ref):
    layers, rows, cols, width = ref.shape
    return ref[...].astype(F32).reshape(layers * rows * cols, width).astype(BF16)


def put_pieces(value, refs):
    at = 0
    for ref in refs:
        ref[...] = value[at : at + ref.shape[0]].astype(BF16)
        at += ref.shape[0]


def rows_of(plan, table_ref, name, *lead):
    top, length = plan.at[name]
    return table_ref[(*lead, slice(top, top + length), slice(None))]


def exchange(pieces, sizes, sign):
    lat, lon = lax.axis_size("lat"), lax.axis_size("lon")
    row, col, both = [piece[:size] for piece, size in zip(pieces, sizes)]
    pairs = [((i + sign) % lat * lon + (j + sign) % lon, i * lon + j) for i in range(lat) for j in range(lon)]
    col = lax.ppermute(col, "lon", [((j + sign) % lon, j) for j in range(lon)])
    both = lax.ppermute(both, ("lat", "lon"), pairs)
    row = lax.ppermute(row, "lat", [((i + sign) % lat, i) for i in range(lat)])
    return [row, col, both]


def choose(index, branches, *args):
    flat_args, tree = jax.tree.flatten(args)
    out_trees = []

    def closed(branch):
        def run(*leaves):
            out, out_tree = jax.tree.flatten(branch(*jax.tree.unflatten(tree, leaves)))
            out_trees.append(out_tree)
            return out

        return jax.make_jaxpr(run)(*flat_args)

    out = lax.cond_p.bind(index, *flat_args, branches=tuple(closed(branch) for branch in branches))
    return jax.tree.unflatten(out_trees[0], out)


FLAGS = ("three_class", "a", "big_a")


def first_pieces(shifts, tokens, plan):
    width = tokens.shape[-1]
    count = tokens.size // width
    kinds = 3

    def body(shifts_hbm, tokens_hbm, table_hbm, *refs):
        outs, refs = refs[:kinds], refs[kinds:]
        rows_ref, flags_ref, *at_refs, shifts_ref, tokens_ref, table_ref, source_ref, sems = refs
        start = Copies(sems)
        shift = start(shifts_hbm, shifts_ref)
        held = start(tokens_hbm, tokens_ref)
        table = start(table_hbm, table_ref)
        shift.wait()
        case = case_of(shifts_ref)
        for ref, name in zip(at_refs, ("one_at", "two_at", "three_at")):
            ref[0] = lookup(plan.flags[name], case)
        for n, name in enumerate(FLAGS):
            flags_ref[n] = lookup(plan.flags[name], case)
        held.wait()
        source_ref[...] = flat(tokens_ref)
        table.wait()
        rows_ref[...] = table_ref[case]
        index = columns_of(rows_of(plan, table_ref, "send_one", case), sum(plan.room_one))
        put_pieces(select_rows(index, source_ref[...]), outs)

    outs = shapes(plan.room_one, width)
    outs += [pltpu.VMEM(plan.table.shape[1:], F32), pltpu.SMEM((8,), I32)]
    outs += [pltpu.SMEM((1,), I32)] * 3
    scratch = [pltpu.SMEM((2,), I32), pltpu.VMEM(tokens.shape, BF16), pltpu.VMEM(plan.table.shape, F32)]
    scratch += [pltpu.VMEM((count, width), BF16)]
    got = call(body, outs, [shifts, tokens, plan.table], [HBM] * 3, scratch, 3, 1 << 28, 1 << 20)
    sent, (rows, flags, one, two, three) = got[:kinds], got[kinds:]
    return sent, rows, flags, one[0], two[0], three[0]


def before_fine(flags, regions, tokens, table, weights, plan):
    _, lat, lon = regions.shape
    _, rows, cols, width = tokens.shape
    flat_regions = regions.reshape(2 * lat, lon)
    fine, coarse = windowed(rows, cols), natural(rows // 2, cols // 2)

    def lanes(places, scale, is_fine):
        places = np.asarray([(l, scale * r, scale * c, is_fine) for l, r, c in places], np.float32)
        return np.pad(places, ((0, -len(places) % 128), (0, 0))).T.reshape(4, -1, 128)

    places = np.concatenate([lanes(fine, 1, 1), lanes(coarse, 2, 0)], axis=1)
    lines = places.shape[1]
    count = 128 * lines

    def body(flags_ref, rows_ref, regions_hbm, places_hbm, tokens_hbm, *refs):
        weights_hbm, refs = refs[: len(weights)], refs[len(weights) :]
        id_ref, x_ref, *refs = refs
        weight_refs, (regions_ref, places_ref, tokens_ref, sems) = refs[: len(weights)], refs[len(weights) :]
        start = Copies(sems)
        waits = [start(regions_hbm, regions_ref), start(places_hbm, places_ref)]
        held = start(tokens_hbm, tokens_ref)
        later = [start(src, dst) for src, dst in zip(weights_hbm, weight_refs)]
        for copy in waits:
            copy.wait()
        a = flags_ref[1].astype(F32)
        big_a = 2.0 * flags_ref[2].astype(F32)
        is_fine = places_ref[3]
        d = is_fine * a + (1.0 - is_fine) * big_a
        row = places_ref[1] + d + (lax.axis_index("lat") * rows).astype(F32)
        col = places_ref[2] + 2.0 * d + (lax.axis_index("lon") * cols).astype(F32)
        wrapped = jnp.where((row < 0) | (row >= lat), 4.0, 0.0)
        row = jnp.where(row < 0, row + lat, jnp.where(row >= lat, row - lat, row))
        col = jnp.where(col < 0, col + lon, jnp.where(col >= lon, col - lon, col))
        row = columns_of(row + places_ref[0] * lat, count)
        col = columns_of(col, count)
        wrapped = columns_of(wrapped, count)
        picked = select_rows(row, regions_ref[...].astype(F32).astype(BF16))
        ids = jnp.zeros((count, 128), F32)
        for at in range(0, lon, 128):
            size = min(128, lon - at)
            lane = lax.broadcasted_iota(I32, (1, size), 1).astype(F32) + float(at)
            here = jnp.where(lane == col[:, :size], picked[:, at : at + size], 0.0)
            ids = ids + jnp.sum(here, axis=1, keepdims=True)
        ids = ids + wrapped
        for n in range(lines):
            id_ref[n : n + 1, :] = ids[n * 128 : (n + 1) * 128].T[:1]
        held.wait()
        take = columns_of(rows_of(plan, rows_ref, "take_one"), len(fine))
        x_ref[...] = select_rows(take, flat(tokens_ref)).astype(BF16)
        for copy in later:
            copy.wait()

    outs = [pltpu.VMEM((lines, 128), F32)] + shapes([len(fine)], width)
    outs += [pltpu.VMEM(w.shape, BF16) for w in weights]
    scratch = [pltpu.VMEM(flat_regions.shape, I32), pltpu.VMEM(places.shape, F32), pltpu.VMEM(tokens.shape, BF16)]
    args = [flags, table, flat_regions, places, tokens, *weights]
    in_specs = [SMEM, VMEM] + [HBM] * (3 + len(weights))
    ids, x, *weights = call(body, outs, args, in_specs, scratch, 3 + len(weights), 1 << 28, 4 << 20)
    return ids, x, weights


def id_columns(lines, count):
    lane = lax.broadcasted_iota(I32, (1, 128), 1).astype(F32)
    return jnp.where(columns_of(lines, count) == lane, 1.0, 0.0).astype(BF16)


def before_coarse(fine, table, weight, plan):
    own, width = fine.shape
    half = 3 * weight.shape[0] // 8

    def body(rows_ref, fine_hbm, weight_hbm, x_ref, part_hbm, weight_ref, fine_ref, part_ref, sems):
        start = Copies(sems)
        held = start(fine_hbm, fine_ref)
        later = start(weight_hbm.at[pl.ds(0, half)], weight_ref)
        take = columns_of(rows_of(plan, rows_ref, "fine_out"), own)
        held.wait()
        part_ref[...] = select_rows(take, fine_ref[...]).astype(BF16)
        leave = start(part_ref, part_hbm)
        take = columns_of(rows_of(plan, rows_ref, "take_two"), own)
        x_ref[...] = select_rows(take, fine_ref[...]).astype(BF16)
        leave.wait()
        later.wait()

    outs = shapes([own], width) + shapes([own], width, pltpu.HBM) + shapes([half], weight.shape[1])
    scratch = [pltpu.VMEM(fine.shape, BF16)] * 2
    return call(body, outs, [table, fine, weight], [VMEM, HBM, HBM], scratch, 3, 1 << 28, 4 << 20)


def fine_level(x_own, source, ids, w_qkv, w_proj, rows, plan):
    count, width = x_own.shape
    inner = w_proj.shape[0]

    def body(own_ref, source_ref, ids_ref, qkv_w_ref, proj_w_ref, rows_ref, out_hbm, *refs):
        *piece_outs, x_ref, qkv_ref, out_ref, id_ref, sems = refs
        start = Copies(sems)
        id_ref[...] = id_columns(ids_ref[: -(-count // 128), :], count)
        leave = []
        take = columns_of(rows_of(plan, rows_ref, "take_one"), count) - float(count)
        x = own_ref[...].astype(F32) + select_rows(take, source_ref[...])
        x_ref[...] = x
        normed = layer_norm(x).astype(BF16)
        qkv_ref[...] = jnp.dot(normed, qkv_w_ref[...], preferred_element_type=F32).astype(BF16)

        def finish(w, out):
            at = slice(w * TOK, (w + 1) * TOK)
            out = jnp.dot(out, proj_w_ref[...], preferred_element_type=F32)
            out_ref[at, :] = (x_ref[at, :] + out).astype(BF16)
            leave.append(start(out_ref.at[pl.ds(w * TOK, TOK)], out_hbm.at[pl.ds(w * TOK, TOK)]))

        attend_windows(
            lambda w, at: qkv_ref[w * TOK : (w + 1) * TOK, at : at + 128],
            lambda w: id_ref[w * TOK : (w + 1) * TOK, :],
            count // TOK,
            inner,
            finish,
        )
        index = columns_of(rows_of(plan, rows_ref, "send_two"), sum(plan.room_two))
        put_pieces(select_rows(index, out_ref[...]), piece_outs)
        for copy in leave:
            copy.wait()

    outs = shapes([count], width, pltpu.HBM) + shapes(plan.room_two, width)
    scratch = [
        pltpu.VMEM((count, width), F32),
        pltpu.VMEM((count, 3 * inner), BF16),
        pltpu.VMEM((count, width), BF16),
        pltpu.VMEM((count, 128), BF16),
    ]
    args = [x_own, source, ids, w_qkv, w_proj, rows]
    out, *sent = call(body, outs, args, [VMEM] * len(args), scratch, count // TOK, 3 << 30, 6 << 20, 14)
    return out, sent


def coarse_level(flags, fine, x_own, source, ids, merge_first, w_merge, w_qkv, w_proj, rows, plan):
    depth, width = w_merge.shape
    own, half = fine.shape
    count = own // 4
    inner = w_proj.shape[0]

    def body(
        flags_ref, fine_hbm, merge_hbm, qkv_w_hbm, proj_w_hbm, own_ref, source_ref, ids_ref, first_ref, rows_ref, *refs
    ):
        out_ref, *piece_outs = refs[:4]
        qkv_ref, fine_ref, id_ref, merge_ref, qkv_w_ref, proj_w_ref, sems = refs[4:]
        start = Copies(sems)
        with_fine = [n for n, sizes in enumerate(plan.four) if sum(sizes)]
        needs_fine = functools.reduce(jnp.logical_or, [flags_ref[0] == n for n in with_fine])

        def bring(src, dst):
            cuts = [(at, min(half, src.shape[0] - at)) for at in range(0, src.shape[0], half)]
            return [(at, size, start(src.at[pl.ds(at, size)], dst.at[pl.ds(at, size)])) for at, size in cuts]

        def product(x, ref, copies):
            parts = []
            for at, size, copy in copies:
                copy.wait()
                parts.append(jnp.dot(x[:, at : at + size], ref[at : at + size, :], preferred_element_type=F32))
            return functools.reduce(jnp.add, parts)

        here = first_ref.shape[0]
        merge_w = bring(merge_hbm.at[pl.ds(here, depth - here)], merge_ref)
        qkv_w = bring(qkv_w_hbm, qkv_w_ref)
        proj_w = start(proj_w_hbm, proj_w_ref)
        fine_copy = (fine_hbm, fine_ref, sems.at[start.used])

        @pl.when(needs_fine)
        def _():
            pltpu.make_async_copy(*fine_copy).start()

        id_ref[...] = id_columns(ids_ref[-(-own // 128) :, :], count)
        take = columns_of(rows_of(plan, rows_ref, "take_two"), 4 * count) - float(own)
        x = own_ref[...].astype(F32) + select_rows(take, source_ref[...])
        x = jnp.concatenate([x[n * count : (n + 1) * count] for n in range(4)], axis=1)
        stacked = layer_norm(x).astype(BF16)
        merged = jnp.dot(stacked[:, :here], first_ref[...], preferred_element_type=F32)
        merged = (merged + product(stacked[:, here:], merge_ref, merge_w)).astype(BF16).astype(F32)
        normed = layer_norm(merged).astype(BF16)
        qkv_ref[...] = product(normed, qkv_w_ref, qkv_w).astype(BF16)
        proj_w.wait()

        def finish(w, out):
            out = jnp.dot(out, proj_w_ref[...], preferred_element_type=F32)
            out_ref[...] = (merged + out).astype(BF16)

        attend_windows(lambda w, at: qkv_ref[:, at : at + 128], lambda w: id_ref[...], 1, inner, finish)
        sent = select_rows(columns_of(rows_of(plan, rows_ref, "send_three"), sum(plan.room_three)), out_ref[...])
        sent = sent.astype(BF16)
        for n, sizes in enumerate(plan.three):

            @pl.when(flags_ref[0] == n)
            def _():
                at = 0
                for ref, size, space in zip(piece_outs, sizes, plan.room_three):
                    ref[:size, :] = sent[at : at + size, :half]
                    ref[size : 2 * size, :] = sent[at : at + size, half:]
                    at += space

        @pl.when(needs_fine)
        def _():
            pltpu.make_async_copy(*fine_copy).wait()
            index = columns_of(rows_of(plan, rows_ref, "send_four"), sum(plan.room_four))
            sent = select_rows(index, fine_ref[...]).astype(BF16)
            for n in with_fine:

                @pl.when(flags_ref[0] == n)
                def _():
                    at = 0
                    for ref, size, more, space in zip(piece_outs, plan.three[n], plan.four[n], plan.room_four):
                        ref[2 * size : 2 * size + more, :] = sent[at : at + more]
                        at += space

    most = [max(2 * three[k] + four[k] for three, four in zip(plan.three, plan.four)) for k in range(3)]
    outs = shapes([count], width) + shapes(most, half)
    scratch = [pltpu.VMEM((count, 3 * inner), BF16)]
    shapes_in = [fine.shape, (count, 128), (depth - merge_first.shape[0], width), w_qkv.shape, w_proj.shape]
    scratch += [pltpu.VMEM(shape, BF16) for shape in shapes_in]
    args = [flags, fine, w_merge, w_qkv, w_proj, x_own, source, ids, merge_first, rows]
    in_specs = [SMEM] + [HBM] * 4 + [VMEM] * (len(args) - 5)
    copies = depth // half + width // half + 3
    out, *sent = call(body, outs, args, in_specs, scratch, copies, 3 << 30, 12 << 20, 24)
    return out, sent


def fine_output(part, source, rows, plan, block_rows, block_cols, partial):
    own, width = part.shape

    def body(part_hbm, source_ref, rows_ref, out_ref, part_ref, stage_ref, sems):
        start = Copies(sems)
        cuts = [pl.ds(at, TOK) for at in range(0, own, TOK)]
        held = [start(part_hbm.at[cut], part_ref.at[cut]) for cut in cuts]
        take = columns_of(rows_of(plan, rows_ref, "fine_out"), own) - float(own)
        leave = []
        for n, (cut, copy) in enumerate(zip(cuts, held)):
            got = select_rows(take[n * TOK : (n + 1) * TOK], source_ref[...])
            copy.wait()
            out = part_ref[cut, :].astype(F32) + got
            if partial:
                out_ref[cut, :] = out.astype(BF16)
            else:
                lines = TOK // block_cols
                layer, line = divmod(n * lines, block_rows)
                there = (layer, pl.ds(line, lines))
                stage_ref[there] = out.reshape(lines, block_cols, width).astype(BF16)
                leave.append(start(stage_ref.at[there], out_ref.at[there]))
        for copy in leave:
            copy.wait()

    shape = (2, block_rows, block_cols, width)
    outs = shapes([own], width) if partial else [pltpu.HBM(shape, BF16)]
    scratch = [pltpu.VMEM(part.shape, BF16), pltpu.VMEM(shape, BF16)]
    return call(body, outs, [part, source, rows], [HBM, VMEM, VMEM], scratch, 2 * own // TOK, 1 << 30, 4 << 20)[0]


def coarse_output(coarse, got, rows, which, plan, block_rows, block_cols, part=None):
    own, width = coarse.shape
    half = width // 2
    sizes, more = plan.three[which], plan.four[which]
    parts = [] if part is None else [part]

    def padded(parts, sizes, room):
        out = []
        for value, size, space in zip(parts, sizes, room):
            out.append(value)
            if size < space:
                out.append(jnp.zeros((space - size, value.shape[1]), F32))
        return out

    def body(coarse_ref, *refs):
        got_refs, refs = refs[:3], refs[3:]
        part_refs, (rows_ref, out_ref, *fine_outs, _) = refs[: len(parts)], refs[len(parts) :]
        got = [ref[...].astype(F32) for ref in got_refs]
        back = [jnp.concatenate([x[:size], x[size : 2 * size]], axis=1) for x, size in zip(got, sizes)]
        source = stack_rows([coarse_ref[...].astype(F32)] + padded(back, sizes, plan.room_three))
        out = select_rows(columns_of(rows_of(plan, rows_ref, "coarse_out"), own), source.astype(BF16)).astype(BF16)
        for n in range(own // 2):
            out_ref[n // block_cols, n % block_cols] = out[2 * n : 2 * n + 2]
        for part_ref, fine_ref in zip(part_refs, fine_outs):
            fine = stack_rows(padded([x[2 * size :] for x, size in zip(got, sizes)], more, plan.room_four))
            base = part_ref.shape[0] + sum(plan.room_two)
            take = columns_of(rows_of(plan, rows_ref, "fine_out"), part_ref.shape[0]) - float(base)
            out = part_ref[...].astype(F32) + select_rows(take, fine.astype(BF16))
            fine_ref[...] = out.reshape(fine_ref.shape).astype(BF16)

    outs = [jax.ShapeDtypeStruct((block_rows, block_cols, 2, width), BF16)]
    outs += [jax.ShapeDtypeStruct((2, 2 * block_rows, 2 * block_cols, half), BF16) for _ in parts]
    args = [coarse, *got, *parts, rows]
    out, *fine = call(body, outs, args, [VMEM] * len(args), [], 1, 1 << 28, 1 << 20)
    return out.transpose(2, 0, 1, 3), *fine


def on_device(tokens, regions, shifts, fine_qkv, fine_proj, merge_weight, coarse_qkv, coarse_proj):
    _, rows, cols, _ = tokens.shape
    plan = Plan(rows, cols)

    def first(which, sign, sent, *args):
        got = exchange(sent, plan.one[which], sign)
        return lay(got, plan.room_one), before_fine(*args, plan)

    def second(which, sign, sent, *args):
        got = exchange(sent, plan.two[which], sign)
        return lay(got, plan.room_two), before_coarse(*args, plan)

    def third(which, sign, sent, part, source, coarse, table):
        sizes = [2 * n + m for n, m in zip(plan.three[which], plan.four[which])]
        got = exchange(sent, sizes, sign)
        partial = sum(plan.four[which]) > 0
        fine_out = fine_output(part, source, table, plan, rows, cols, partial)
        place = (table, which, plan, rows // 2, cols // 2)
        if partial:
            coarse_out, fine_out = coarse_output(coarse, got, *place, part=fine_out)
        else:
            (coarse_out,) = coarse_output(coarse, got, *place)
        return fine_out, coarse_out

    def branches(stage, pairs):
        return [functools.partial(stage, which, sign) for which, sign in pairs]

    sent, table, flags, one, two, three = first_pieces(shifts, tokens, plan)
    got, (ids, x, weights) = choose(
        one, branches(first, plan.one_branches), sent, flags, regions, tokens, table, [fine_qkv, fine_proj]
    )
    fine, sent = fine_level(x, got, ids, *weights, table, plan)
    got, (x, part, merge_first) = choose(two, branches(second, plan.two_branches), sent, fine, table, merge_weight)
    coarse, sent = coarse_level(
        flags, fine, x, got, ids, merge_first, merge_weight, coarse_qkv, coarse_proj, table, plan
    )
    return choose(three, branches(third, plan.three_branches), sent, part, got, coarse, table)


def solution(mesh):
    return jax.shard_map(
        on_device,
        mesh=mesh,
        in_specs=(P(None, "lat", "lon", None), P(), P(), P(), P(), P(), P(), P()),
        out_specs=(P(None, "lat", "lon", None), P(None, "lat", "lon", None)),
        check_vma=False,
    )
```

```python
import functools

import jax
import jax.numpy as jnp
import numpy as np
from jax import lax
from jax.experimental import pallas as pl
from jax.experimental.pallas import tpu as pltpu
from jax.sharding import PartitionSpec as P

HD = 32
WH = 6
WW = 12
TOK = 2 * WH * WW
EPS = 1e-05
BIG = 1e30
SCALE = float(np.log2(np.e) / np.sqrt(HD))

NT = (((1,), (1,)), ((), ()))
TN = (((0,), (0,)), ((), ()))
F32 = jnp.float32
BF16 = jnp.bfloat16
I32 = jnp.int32

PAIRS = [(WH - 1, t) for t in range(1, WH)] + [(t, WH - 1) for t in range(1, WH - 1)]


def up16(count):
    return -(-count // 16) * 16


def natural(rows, cols):
    return [(l, r, c) for l in range(2) for r in range(rows) for c in range(cols)]


def windowed(rows, cols):
    return [
        (l, wr * WH + r, wc * WW + c)
        for wr in range(rows // WH)
        for wc in range(cols // WW)
        for l in range(2)
        for r in range(WH)
        for c in range(WW)
    ]


def moved(order, d):
    return [(l, r + d, c + 2 * d) for l, r, c in order]


def exchange_places(held, wanted, rows, cols, sign):
    at = {place: n for n, place in enumerate(held)}
    found = []
    for dr, dc in ((sign, 0), (0, sign), (sign, sign)):
        numbers, places = [], []
        for l, r, c in sorted(set(wanted) - set(held)):
            n = at.get((l, r - dr * rows, c - dc * cols))
            if n is not None:
                numbers.append(n)
                places.append((l, r, c))
        found.append((numbers, places))
    return found


def offsets(t0, t1):
    a = t0 if t0 <= 2 else t0 - WH
    big_a = t1 if t1 <= 2 else t1 - WH
    ahead = 1 if 2 * big_a > a or 2 * big_a - a == 0 and a < 0 else -1
    return a, big_a, ahead


def classes_of(needs, slack):
    rounded = [tuple(-(-size // 8) * 8 for size in need) for need in needs]
    heavy = [sum(need[1:3]) * 2 + sum(need[4:]) for need in rounded]
    limits = []
    for size in sorted(set(heavy)):
        if not limits or size > limits[-1][0] * slack:
            limits.append([size, size])
        limits[-1][1] = size
    which = [next(n for n, limit in enumerate(limits) if size <= limit[1]) for size in heavy]
    sizes = [
        [max(need[k] for need, w in zip(rounded, which) if w == n) for k in range(len(needs[0]))]
        for n in range(len(limits))
    ]
    return sizes, which


def rooms(sizes):
    return [up16(max(size[k] for size in sizes)) for k in range(len(sizes[0]))]


class Plan:
    def __init__(self, rows, cols):
        crows, ccols = rows // 2, cols // 2
        block, cblock = natural(rows, cols), natural(crows, ccols)
        cases = []
        for t0, t1 in PAIRS:
            a, big_a, ahead = offsets(t0, t1)
            fine = moved(windowed(rows, cols), a)
            coarse = moved(cblock, big_a)
            quarters = [
                (l, 2 * r + dr, 2 * c + dc)
                for dr, dc in ((0, 0), (1, 0), (0, 1), (1, 1))
                for l, r, c in coarse
            ]
            come = 1 if a > 0 else -1
            one = exchange_places(block, fine, rows, cols, come)
            home = [p for p in block if p not in set(fine)]
            wanted = quarters + (home if come == -ahead else [])
            two = exchange_places(fine, wanted, rows, cols, ahead)
            back = 1 if big_a < 0 else -1
            three = exchange_places(coarse, cblock, crows, ccols, back)
            got = set(fine).union(*[places for _, places in two])
            four = exchange_places(fine, [p for p in block if p not in got], rows, cols, back)
            cases.append((come, ahead, back, fine, coarse, quarters, one, two, three, four))

        def needs(which):
            return [[len(numbers) for numbers, _ in case[which]] for case in cases]

        self.one, one_class = classes_of(needs(6), 1.15)
        self.two, two_class = classes_of(needs(7), 1.15)
        sizes, three_class = classes_of([three + four for three, four in zip(needs(8), needs(9))], 1.0)
        self.three, self.four = [size[:3] for size in sizes], [size[3:] for size in sizes]
        self.room_one, self.room_two = rooms(self.one), rooms(self.two)
        self.room_three, self.room_four = rooms(self.three), rooms(self.four)

        def branches(which_class, direction):
            pairs = [(n, case[direction]) for n, case in zip(which_class, cases)]
            found = sorted(set(pairs))
            return found, [found.index(pair) for pair in pairs]

        self.one_branches, one_at = branches(one_class, 0)
        self.two_branches, two_at = branches(two_class, 1)
        self.three_branches, three_at = branches(three_class, 2)
        self.flags = dict(
            three_class=three_class,
            one_at=one_at, two_at=two_at, three_at=three_at,
            a=[offsets(*pair)[0] for pair in PAIRS], big_a=[offsets(*pair)[1] for pair in PAIRS],
        )

        found = {}
        for n, (come, ahead, back, fine, coarse, quarters, one, two, three, four) in enumerate(cases):

            def send(exchanged, room):
                return [n for (numbers, _), size in zip(exchanged, room) for n in numbers + [-1] * (size - len(numbers))]

            def source(held, *exchanges):
                places = list(held)
                for exchanged, room in exchanges:
                    for (_, got), size in zip(exchanged, room):
                        places += got + [None] * (size - len(got))
                return {p: n for n, p in enumerate(places) if p is not None}

            first, second = source(block, (one, self.room_one)), source(fine, (two, self.room_two))
            third = source(coarse, (three, self.room_three))
            last = source(fine, (two, self.room_two), (four, self.room_four))
            out = [(l, r, c) for r in range(crows) for c in range(ccols) for l in range(2)]
            rows_of = dict(
                send_one=send(one, self.room_one),
                take_one=[first[p] for p in fine],
                send_two=send(two, self.room_two),
                take_two=[second[p] for p in quarters],
                send_three=send(three, self.room_three),
                send_four=send(four, self.room_four),
                fine_out=[last[p] for p in block],
                coarse_out=[third[p] for p in out],
            )
            for name, row in rows_of.items():
                found.setdefault(name, []).append(row)
        parts, self.at, top = [], {}, 0
        for name, lists in found.items():
            length = -(-max(len(row) for row in lists) // 128)
            part = np.full((len(PAIRS), length * 128), -1, np.float32)
            for n, row in enumerate(lists):
                part[n, : len(row)] = row
            parts.append(part.reshape(len(PAIRS), length, 128))
            self.at[name] = (top, length)
            top += length
        parts.append(np.zeros((len(PAIRS), -top % 8, 128), np.float32))
        self.table = np.concatenate(parts, axis=1)


def case_of(shifts_ref):
    t0, t1 = shifts_ref[0], shifts_ref[1]
    return jnp.where(t0 == WH - 1, t1 - 1, t0 + WH - 2)


def lookup(values, case):
    out = jnp.int32(values[0])
    for n, value in enumerate(values[1:], 1):
        out = jnp.where(case == n, value, out)
    return out


def columns_of(rows, count):
    parts = [jnp.broadcast_to(rows[j : j + 1], (128, 128)).T for j in range(-(-count // 128))]
    return stack_rows(parts)[:count]


def select_rows(index, source):
    lane = lax.broadcasted_iota(I32, (1, 128), 1).astype(F32)
    size = source.shape[0]
    pick = [jnp.where(index == lane + float(at), 1.0, 0.0).astype(BF16) for at in range(0, size, 128)]
    pick = jnp.concatenate(pick, axis=1)[:, :size]
    return jnp.dot(pick, source, preferred_element_type=F32)


def stack_rows(parts):
    return parts[0] if len(parts) == 1 else jnp.concatenate(parts, axis=0)


def layer_norm(values):
    center = jnp.mean(values, axis=-1, keepdims=True)
    values = values - center
    spread = jnp.mean(values * values, axis=-1, keepdims=True)
    return values * lax.rsqrt(spread + EPS)


def attend_windows(qkv_of, id_of, windows, inner, finish):
    lane = lax.broadcasted_iota(I32, (1, 128), 1)
    forbid = jnp.where(lane < 8, BIG, 0.0).astype(BF16)
    groups = inner // 128
    units = [(w, g) for w in range(windows) for g in range(groups)]
    scores, weights, outs = {}, {}, {}

    def score(w, g):
        key_id = id_of(w)
        not_id = (key_id - 1).astype(BF16) * forbid
        q = qkv_of(w, g * 128)
        keys = jnp.concatenate([qkv_of(w, inner + g * 128), key_id], axis=1)
        queries = []
        for h in range(4):
            mine = jnp.where((lane >= h * HD) & (lane < (h + 1) * HD), 1.0, 0.0).astype(BF16)
            queries.append(jnp.concatenate([q * mine, not_id], axis=1))
        scores[w, g] = lax.dot_general(stack_rows(queries), keys, NT, preferred_element_type=F32)

    def soften(w, g):
        s = scores.pop((w, g))
        weights[w, g] = jnp.exp2((s - jnp.max(s, axis=1, keepdims=True)) * SCALE).astype(BF16)

    def gather(w, g):
        v = qkv_of(w, 2 * inner + g * 128)
        values = jnp.concatenate([v, jnp.ones_like(v)], axis=1)
        out = jnp.dot(weights.pop((w, g)), values, preferred_element_type=F32)
        picked, total = out[:TOK, :128], out[:TOK, 128:]
        for h in range(1, 4):
            rows = slice(h * TOK, (h + 1) * TOK)
            picked = jnp.where(lane < h * HD, picked, out[rows, :128])
            total = jnp.where(lane < h * HD, total, out[rows, 128:])
        outs[w, g] = (picked / total).astype(BF16)
        if g == groups - 1:
            finish(w, jnp.concatenate([outs.pop((w, k)) for k in range(groups)], axis=1))

    for n in range(len(units) + 2):
        if n < len(units):
            score(*units[n])
        if 0 <= n - 1 < len(units):
            soften(*units[n - 1])
        if 0 <= n - 2 < len(units):
            gather(*units[n - 2])


ANY = pl.BlockSpec(memory_space=pl.ANY)
HBM = pl.BlockSpec(memory_space=pltpu.HBM)
VMEM = pl.BlockSpec(memory_space=pltpu.VMEM)
SMEM = pl.BlockSpec(memory_space=pltpu.SMEM)


def call(body, outs, args, in_specs, scratch, copies, flops, moved_bytes, vmem=8):
    args = [
        pltpu.with_memory_space_constraint(arg, spec.memory_space) for arg, spec in zip(args, in_specs, strict=True)
    ]
    spaces = [getattr(out, "memory_space", pltpu.SMEM if out.dtype == I32 else pltpu.VMEM) for out in outs]
    out_specs = [pl.BlockSpec(memory_space=space) for space in spaces]
    return pl.pallas_call(
        body,
        out_shape=outs,
        in_specs=in_specs,
        out_specs=out_specs,
        scratch_shapes=list(scratch) + [pltpu.SemaphoreType.DMA((copies,))],
        compiler_params=pltpu.CompilerParams(vmem_limit_bytes=vmem << 20),
        cost_estimate=pl.CostEstimate(flops=flops, bytes_accessed=moved_bytes, transcendentals=0),
    )(*args)


def shapes(sizes, width, space=pltpu.VMEM):
    return [space((n, width), BF16) for n in sizes]


class Copies:
    def __init__(self, sems):
        self.sems, self.used = sems, 0

    def __call__(self, src, dst):
        copy = pltpu.make_async_copy(src, dst, self.sems.at[self.used])
        self.used += 1
        copy.start()
        return copy


def lay(pieces, room):
    width = pieces[0].shape[1]

    def body(*refs):
        out_ref = refs[len(pieces)]
        at = 0
        for ref, space in zip(refs, room):
            rows = ref.shape[0]
            out_ref[at : at + rows, :] = ref[...]
            if rows < space:
                out_ref[at + rows : at + space, :] = jnp.zeros((space - rows, width), BF16)
            at += space

    return call(body, shapes([sum(room)], width), pieces, [VMEM] * 3, [], 1, 0, 1 << 18)[0]


def flat(ref):
    layers, rows, cols, width = ref.shape
    return ref[...].astype(F32).reshape(layers * rows * cols, width).astype(BF16)


def put_pieces(value, refs):
    at = 0
    for ref in refs:
        ref[...] = value[at : at + ref.shape[0]].astype(BF16)
        at += ref.shape[0]


def rows_of(plan, table_ref, name, *lead):
    top, length = plan.at[name]
    return table_ref[(*lead, slice(top, top + length), slice(None))]


def exchange(pieces, sizes, sign):
    lat, lon = lax.axis_size("lat"), lax.axis_size("lon")
    row, col, both = [piece[:size] for piece, size in zip(pieces, sizes)]
    pairs = [((i + sign) % lat * lon + (j + sign) % lon, i * lon + j) for i in range(lat) for j in range(lon)]
    col = lax.ppermute(col, "lon", [((j + sign) % lon, j) for j in range(lon)])
    both = lax.ppermute(both, ("lat", "lon"), pairs)
    row = lax.ppermute(row, "lat", [((i + sign) % lat, i) for i in range(lat)])
    return [row, col, both]


def choose(index, branches, *args):
    flat_args, tree = jax.tree.flatten(args)
    out_trees = []

    def closed(branch):
        def run(*leaves):
            out, out_tree = jax.tree.flatten(branch(*jax.tree.unflatten(tree, leaves)))
            out_trees.append(out_tree)
            return out

        return jax.make_jaxpr(run)(*flat_args)

    out = lax.cond_p.bind(index, *flat_args, branches=tuple(closed(branch) for branch in branches))
    return jax.tree.unflatten(out_trees[0], out)


FLAGS = ("three_class", "a", "big_a")


def first_pieces(shifts, tokens, plan):
    width = tokens.shape[-1]
    count = tokens.size // width
    kinds = 3

    def body(shifts_hbm, tokens_hbm, table_hbm, *refs):
        outs, refs = refs[:kinds], refs[kinds:]
        rows_ref, flags_ref, *at_refs, shifts_ref, tokens_ref, table_ref, source_ref, sems = refs
        start = Copies(sems)
        shift = start(shifts_hbm, shifts_ref)
        held = start(tokens_hbm, tokens_ref)
        table = start(table_hbm, table_ref)
        shift.wait()
        case = case_of(shifts_ref)
        for ref, name in zip(at_refs, ("one_at", "two_at", "three_at")):
            ref[0] = lookup(plan.flags[name], case)
        for n, name in enumerate(FLAGS):
            flags_ref[n] = lookup(plan.flags[name], case)
        held.wait()
        source_ref[...] = flat(tokens_ref)
        table.wait()
        rows_ref[...] = table_ref[case]
        index = columns_of(rows_of(plan, table_ref, "send_one", case), sum(plan.room_one))
        put_pieces(select_rows(index, source_ref[...]), outs)

    outs = shapes(plan.room_one, width)
    outs += [pltpu.VMEM(plan.table.shape[1:], F32), pltpu.SMEM((8,), I32)]
    outs += [pltpu.SMEM((1,), I32)] * 3
    scratch = [pltpu.SMEM((2,), I32), pltpu.VMEM(tokens.shape, BF16), pltpu.VMEM(plan.table.shape, F32)]
    scratch += [pltpu.VMEM((count, width), BF16)]
    got = call(body, outs, [shifts, tokens, plan.table], [HBM] * 3, scratch, 3, 1 << 28, 1 << 20)
    sent, (rows, flags, one, two, three) = got[:kinds], got[kinds:]
    return sent, rows, flags, one[0], two[0], three[0]


def before_fine(flags, regions, tokens, table, weights, plan):
    _, lat, lon = regions.shape
    _, rows, cols, width = tokens.shape
    flat_regions = regions.reshape(2 * lat, lon)
    fine, coarse = windowed(rows, cols), natural(rows // 2, cols // 2)

    def lanes(places, scale, is_fine):
        places = np.asarray([(l, scale * r, scale * c, is_fine) for l, r, c in places], np.float32)
        return np.pad(places, ((0, -len(places) % 128), (0, 0))).T.reshape(4, -1, 128)

    places = np.concatenate([lanes(fine, 1, 1), lanes(coarse, 2, 0)], axis=1)
    lines = places.shape[1]

    def body(flags_ref, rows_ref, regions_hbm, places_hbm, tokens_hbm, *refs):
        weights_hbm, refs = refs[: len(weights)], refs[len(weights) :]
        id_ref, x_ref, *refs = refs
        weight_refs, (regions_ref, places_ref, tokens_ref, sems) = refs[: len(weights)], refs[len(weights) :]
        start = Copies(sems)
        waits = [start(regions_hbm, regions_ref), start(places_hbm, places_ref)]
        held = start(tokens_hbm, tokens_ref)
        later = [start(src, dst) for src, dst in zip(weights_hbm, weight_refs)]
        for copy in waits:
            copy.wait()
        a = flags_ref[1].astype(F32)
        big_a = 2.0 * flags_ref[2].astype(F32)
        is_fine = places_ref[3]
        d = is_fine * a + (1.0 - is_fine) * big_a
        row = places_ref[1] + d + (lax.axis_index("lat") * rows).astype(F32)
        col = places_ref[2] + 2.0 * d + (lax.axis_index("lon") * cols).astype(F32)
        wrapped = jnp.where((row < 0) | (row >= lat), 4.0, 0.0)
        row = jnp.where(row < 0, row + lat, jnp.where(row >= lat, row - lat, row))
        col = jnp.where(col < 0, col + lon, jnp.where(col >= lon, col - lon, col))
        row = row + places_ref[0] * lat

        def along(values):
            return jnp.concatenate([values[n : n + 1] for n in range(lines)], axis=1)

        line = lax.broadcasted_iota(I32, (2 * lat, 1), 0).astype(F32)
        pick = jnp.where(line == along(row), 1.0, 0.0).astype(BF16)
        known = regions_ref[...].astype(F32).astype(BF16)
        picked = lax.dot_general(known, pick, TN, preferred_element_type=F32)
        line = lax.broadcasted_iota(I32, (lon, 1), 0).astype(F32)
        ids = jnp.sum(jnp.where(line == along(col), picked, 0.0), axis=0, keepdims=True) + along(wrapped)
        for n in range(lines):
            id_ref[n : n + 1, :] = ids[:, n * 128 : (n + 1) * 128]
        held.wait()
        take = columns_of(rows_of(plan, rows_ref, "take_one"), len(fine))
        x_ref[...] = select_rows(take, flat(tokens_ref)).astype(BF16)
        for copy in later:
            copy.wait()

    outs = [pltpu.VMEM((lines, 128), F32)] + shapes([len(fine)], width)
    outs += [pltpu.VMEM(w.shape, BF16) for w in weights]
    scratch = [pltpu.VMEM(flat_regions.shape, I32), pltpu.VMEM(places.shape, F32), pltpu.VMEM(tokens.shape, BF16)]
    args = [flags, table, flat_regions, places, tokens, *weights]
    in_specs = [SMEM, VMEM] + [HBM] * (3 + len(weights))
    ids, x, *weights = call(body, outs, args, in_specs, scratch, 3 + len(weights), 1 << 28, 4 << 20)
    return ids, x, weights


def id_columns(lines, count):
    lane = lax.broadcasted_iota(I32, (1, 128), 1).astype(F32)
    return jnp.where(columns_of(lines, count) == lane, 1.0, 0.0).astype(BF16)


def before_coarse(fine, table, weight, plan):
    own, width = fine.shape
    half = 3 * weight.shape[0] // 8

    def body(rows_ref, fine_hbm, weight_hbm, x_ref, part_hbm, weight_ref, fine_ref, part_ref, sems):
        start = Copies(sems)
        held = start(fine_hbm, fine_ref)
        later = start(weight_hbm.at[pl.ds(0, half)], weight_ref)
        take = columns_of(rows_of(plan, rows_ref, "fine_out"), own)
        held.wait()
        part_ref[...] = select_rows(take, fine_ref[...]).astype(BF16)
        leave = start(part_ref, part_hbm)
        take = columns_of(rows_of(plan, rows_ref, "take_two"), own)
        x_ref[...] = select_rows(take, fine_ref[...]).astype(BF16)
        leave.wait()
        later.wait()

    outs = shapes([own], width) + shapes([own], width, pltpu.HBM) + shapes([half], weight.shape[1])
    scratch = [pltpu.VMEM(fine.shape, BF16)] * 2
    return call(body, outs, [table, fine, weight], [VMEM, HBM, HBM], scratch, 3, 1 << 28, 4 << 20)


def fine_level(x_own, source, ids, w_qkv, w_proj, rows, plan):
    count, width = x_own.shape
    inner = w_proj.shape[0]

    def body(own_ref, source_ref, ids_ref, qkv_w_ref, proj_w_ref, rows_ref, out_hbm, *refs):
        *piece_outs, x_ref, qkv_ref, out_ref, id_ref, sems = refs
        start = Copies(sems)
        id_ref[...] = id_columns(ids_ref[: -(-count // 128), :], count)
        leave = []
        take = columns_of(rows_of(plan, rows_ref, "take_one"), count) - float(count)
        x = own_ref[...].astype(F32) + select_rows(take, source_ref[...])
        x_ref[...] = x
        normed = layer_norm(x).astype(BF16)
        qkv_ref[...] = jnp.dot(normed, qkv_w_ref[...], preferred_element_type=F32).astype(BF16)

        def finish(w, out):
            at = slice(w * TOK, (w + 1) * TOK)
            out = jnp.dot(out, proj_w_ref[...], preferred_element_type=F32)
            out_ref[at, :] = (x_ref[at, :] + out).astype(BF16)
            leave.append(start(out_ref.at[pl.ds(w * TOK, TOK)], out_hbm.at[pl.ds(w * TOK, TOK)]))

        attend_windows(
            lambda w, at: qkv_ref[w * TOK : (w + 1) * TOK, at : at + 128],
            lambda w: id_ref[w * TOK : (w + 1) * TOK, :],
            count // TOK,
            inner,
            finish,
        )
        index = columns_of(rows_of(plan, rows_ref, "send_two"), sum(plan.room_two))
        put_pieces(select_rows(index, out_ref[...]), piece_outs)
        for copy in leave:
            copy.wait()

    outs = shapes([count], width, pltpu.HBM) + shapes(plan.room_two, width)
    scratch = [
        pltpu.VMEM((count, width), F32),
        pltpu.VMEM((count, 3 * inner), BF16),
        pltpu.VMEM((count, width), BF16),
        pltpu.VMEM((count, 128), BF16),
    ]
    args = [x_own, source, ids, w_qkv, w_proj, rows]
    out, *sent = call(body, outs, args, [VMEM] * len(args), scratch, count // TOK, 3 << 30, 6 << 20, 14)
    return out, sent


def coarse_level(flags, fine, x_own, source, ids, merge_first, w_merge, w_qkv, w_proj, rows, plan):
    depth, width = w_merge.shape
    own, half = fine.shape
    count = own // 4
    inner = w_proj.shape[0]

    def body(
        flags_ref, fine_hbm, merge_hbm, qkv_w_hbm, proj_w_hbm, own_ref, source_ref, ids_ref, first_ref, rows_ref, *refs
    ):
        out_ref, *piece_outs = refs[:4]
        qkv_ref, fine_ref, id_ref, merge_ref, qkv_w_ref, proj_w_ref, sems = refs[4:]
        start = Copies(sems)
        with_fine = [n for n, sizes in enumerate(plan.four) if sum(sizes)]
        needs_fine = functools.reduce(jnp.logical_or, [flags_ref[0] == n for n in with_fine])

        def bring(src, dst):
            cuts = [(at, min(half, src.shape[0] - at)) for at in range(0, src.shape[0], half)]
            return [(at, size, start(src.at[pl.ds(at, size)], dst.at[pl.ds(at, size)])) for at, size in cuts]

        def product(x, ref, copies):
            parts = []
            for at, size, copy in copies:
                copy.wait()
                parts.append(jnp.dot(x[:, at : at + size], ref[at : at + size, :], preferred_element_type=F32))
            return functools.reduce(jnp.add, parts)

        here = first_ref.shape[0]
        merge_w = bring(merge_hbm.at[pl.ds(here, depth - here)], merge_ref)
        qkv_w = bring(qkv_w_hbm, qkv_w_ref)
        proj_w = start(proj_w_hbm, proj_w_ref)
        fine_copy = (fine_hbm, fine_ref, sems.at[start.used])

        @pl.when(needs_fine)
        def _():
            pltpu.make_async_copy(*fine_copy).start()

        id_ref[...] = id_columns(ids_ref[-(-own // 128) :, :], count)
        take = columns_of(rows_of(plan, rows_ref, "take_two"), 4 * count) - float(own)
        x = own_ref[...].astype(F32) + select_rows(take, source_ref[...])
        x = jnp.concatenate([x[n * count : (n + 1) * count] for n in range(4)], axis=1)
        stacked = layer_norm(x).astype(BF16)
        merged = jnp.dot(stacked[:, :here], first_ref[...], preferred_element_type=F32)
        merged = (merged + product(stacked[:, here:], merge_ref, merge_w)).astype(BF16).astype(F32)
        normed = layer_norm(merged).astype(BF16)
        qkv_ref[...] = product(normed, qkv_w_ref, qkv_w).astype(BF16)
        proj_w.wait()

        def finish(w, out):
            out = jnp.dot(out, proj_w_ref[...], preferred_element_type=F32)
            out_ref[...] = (merged + out).astype(BF16)

        attend_windows(lambda w, at: qkv_ref[:, at : at + 128], lambda w: id_ref[...], 1, inner, finish)
        sent = select_rows(columns_of(rows_of(plan, rows_ref, "send_three"), sum(plan.room_three)), out_ref[...])
        sent = sent.astype(BF16)
        for n, sizes in enumerate(plan.three):

            @pl.when(flags_ref[0] == n)
            def _():
                at = 0
                for ref, size, space in zip(piece_outs, sizes, plan.room_three):
                    ref[:size, :] = sent[at : at + size, :half]
                    ref[size : 2 * size, :] = sent[at : at + size, half:]
                    at += space

        @pl.when(needs_fine)
        def _():
            pltpu.make_async_copy(*fine_copy).wait()
            index = columns_of(rows_of(plan, rows_ref, "send_four"), sum(plan.room_four))
            sent = select_rows(index, fine_ref[...]).astype(BF16)
            for n in with_fine:

                @pl.when(flags_ref[0] == n)
                def _():
                    at = 0
                    for ref, size, more, space in zip(piece_outs, plan.three[n], plan.four[n], plan.room_four):
                        ref[2 * size : 2 * size + more, :] = sent[at : at + more]
                        at += space

    most = [max(2 * three[k] + four[k] for three, four in zip(plan.three, plan.four)) for k in range(3)]
    outs = shapes([count], width) + shapes(most, half)
    scratch = [pltpu.VMEM((count, 3 * inner), BF16)]
    shapes_in = [fine.shape, (count, 128), (depth - merge_first.shape[0], width), w_qkv.shape, w_proj.shape]
    scratch += [pltpu.VMEM(shape, BF16) for shape in shapes_in]
    args = [flags, fine, w_merge, w_qkv, w_proj, x_own, source, ids, merge_first, rows]
    in_specs = [SMEM] + [HBM] * 4 + [VMEM] * (len(args) - 5)
    copies = depth // half + width // half + 3
    out, *sent = call(body, outs, args, in_specs, scratch, copies, 3 << 30, 12 << 20, 24)
    return out, sent


def fine_output(part, source, rows, plan, block_rows, block_cols, partial):
    own, width = part.shape

    def body(part_hbm, source_ref, rows_ref, out_ref, part_ref, stage_ref, sems):
        start = Copies(sems)
        cuts = [pl.ds(at, TOK) for at in range(0, own, TOK)]
        held = [start(part_hbm.at[cut], part_ref.at[cut]) for cut in cuts]
        take = columns_of(rows_of(plan, rows_ref, "fine_out"), own) - float(own)
        leave = []
        for n, (cut, copy) in enumerate(zip(cuts, held)):
            got = select_rows(take[n * TOK : (n + 1) * TOK], source_ref[...])
            copy.wait()
            out = part_ref[cut, :].astype(F32) + got
            if partial:
                out_ref[cut, :] = out.astype(BF16)
            else:
                lines = TOK // block_cols
                layer, line = divmod(n * lines, block_rows)
                there = (layer, pl.ds(line, lines))
                stage_ref[there] = out.reshape(lines, block_cols, width).astype(BF16)
                leave.append(start(stage_ref.at[there], out_ref.at[there]))
        for copy in leave:
            copy.wait()

    shape = (2, block_rows, block_cols, width)
    outs = shapes([own], width) if partial else [pltpu.HBM(shape, BF16)]
    scratch = [pltpu.VMEM(part.shape, BF16), pltpu.VMEM(shape, BF16)]
    return call(body, outs, [part, source, rows], [HBM, VMEM, VMEM], scratch, 2 * own // TOK, 1 << 30, 4 << 20)[0]


def coarse_output(coarse, got, rows, which, plan, block_rows, block_cols, part=None):
    own, width = coarse.shape
    half = width // 2
    sizes, more = plan.three[which], plan.four[which]
    parts = [] if part is None else [part]

    def padded(parts, sizes, room):
        out = []
        for value, size, space in zip(parts, sizes, room):
            out.append(value)
            if size < space:
                out.append(jnp.zeros((space - size, value.shape[1]), F32))
        return out

    def body(coarse_ref, *refs):
        got_refs, refs = refs[:3], refs[3:]
        part_refs, (rows_ref, out_ref, *fine_outs, _) = refs[: len(parts)], refs[len(parts) :]
        got = [ref[...].astype(F32) for ref in got_refs]
        back = [jnp.concatenate([x[:size], x[size : 2 * size]], axis=1) for x, size in zip(got, sizes)]
        source = stack_rows([coarse_ref[...].astype(F32)] + padded(back, sizes, plan.room_three))
        out = select_rows(columns_of(rows_of(plan, rows_ref, "coarse_out"), own), source.astype(BF16)).astype(BF16)
        for n in range(own // 2):
            out_ref[n // block_cols, n % block_cols] = out[2 * n : 2 * n + 2]
        for part_ref, fine_ref in zip(part_refs, fine_outs):
            fine = stack_rows(padded([x[2 * size :] for x, size in zip(got, sizes)], more, plan.room_four))
            base = part_ref.shape[0] + sum(plan.room_two)
            take = columns_of(rows_of(plan, rows_ref, "fine_out"), part_ref.shape[0]) - float(base)
            out = part_ref[...].astype(F32) + select_rows(take, fine.astype(BF16))
            fine_ref[...] = out.reshape(fine_ref.shape).astype(BF16)

    outs = [jax.ShapeDtypeStruct((block_rows, block_cols, 2, width), BF16)]
    outs += [jax.ShapeDtypeStruct((2, 2 * block_rows, 2 * block_cols, half), BF16) for _ in parts]
    args = [coarse, *got, *parts, rows]
    out, *fine = call(body, outs, args, [VMEM] * len(args), [], 1, 1 << 28, 1 << 20)
    return out.transpose(2, 0, 1, 3), *fine


def on_device(tokens, regions, shifts, fine_qkv, fine_proj, merge_weight, coarse_qkv, coarse_proj):
    _, rows, cols, _ = tokens.shape
    plan = Plan(rows, cols)

    def first(which, sign, sent, *args):
        got = exchange(sent, plan.one[which], sign)
        return lay(got, plan.room_one), before_fine(*args, plan)

    def second(which, sign, sent, *args):
        got = exchange(sent, plan.two[which], sign)
        return lay(got, plan.room_two), before_coarse(*args, plan)

    def third(which, sign, sent, part, source, coarse, table):
        sizes = [2 * n + m for n, m in zip(plan.three[which], plan.four[which])]
        got = exchange(sent, sizes, sign)
        partial = sum(plan.four[which]) > 0
        fine_out = fine_output(part, source, table, plan, rows, cols, partial)
        place = (table, which, plan, rows // 2, cols // 2)
        if partial:
            coarse_out, fine_out = coarse_output(coarse, got, *place, part=fine_out)
        else:
            (coarse_out,) = coarse_output(coarse, got, *place)
        return fine_out, coarse_out

    def branches(stage, pairs):
        return [functools.partial(stage, which, sign) for which, sign in pairs]

    sent, table, flags, one, two, three = first_pieces(shifts, tokens, plan)
    got, (ids, x, weights) = choose(
        one, branches(first, plan.one_branches), sent, flags, regions, tokens, table, [fine_qkv, fine_proj]
    )
    fine, sent = fine_level(x, got, ids, *weights, table, plan)
    got, (x, part, merge_first) = choose(two, branches(second, plan.two_branches), sent, fine, table, merge_weight)
    coarse, sent = coarse_level(
        flags, fine, x, got, ids, merge_first, merge_weight, coarse_qkv, coarse_proj, table, plan
    )
    return choose(three, branches(third, plan.three_branches), sent, part, got, coarse, table)


def solution(mesh):
    return jax.shard_map(
        on_device,
        mesh=mesh,
        in_specs=(P(None, "lat", "lon", None), P(), P(), P(), P(), P(), P(), P()),
        out_specs=(P(None, "lat", "lon", None), P(None, "lat", "lon", None)),
        check_vma=False,
    )
```

```python
import functools

import jax
import jax.numpy as jnp
import numpy as np
from jax import lax
from jax.experimental import pallas as pl
from jax.experimental.pallas import tpu as pltpu
from jax.sharding import PartitionSpec as P

HD = 32
WH = 6
WW = 12
TOK = 2 * WH * WW
EPS = 1e-05
BIG = 1e30
SCALE = float(np.log2(np.e) / np.sqrt(HD))

NT = (((1,), (1,)), ((), ()))
TN = (((0,), (0,)), ((), ()))
F32 = jnp.float32
BF16 = jnp.bfloat16
I32 = jnp.int32

PAIRS = [(WH - 1, t) for t in range(1, WH)] + [(t, WH - 1) for t in range(1, WH - 1)]


def up16(count):
    return -(-count // 16) * 16


def natural(rows, cols):
    return [(l, r, c) for l in range(2) for r in range(rows) for c in range(cols)]


def windowed(rows, cols):
    return [
        (l, wr * WH + r, wc * WW + c)
        for wr in range(rows // WH)
        for wc in range(cols // WW)
        for l in range(2)
        for r in range(WH)
        for c in range(WW)
    ]


def moved(order, d):
    return [(l, r + d, c + 2 * d) for l, r, c in order]


def exchange_places(held, wanted, rows, cols, sign):
    at = {place: n for n, place in enumerate(held)}
    found = []
    for dr, dc in ((sign, 0), (0, sign), (sign, sign)):
        numbers, places = [], []
        for l, r, c in sorted(set(wanted) - set(held)):
            n = at.get((l, r - dr * rows, c - dc * cols))
            if n is not None:
                numbers.append(n)
                places.append((l, r, c))
        found.append((numbers, places))
    return found


def offsets(t0, t1):
    a = t0 if t0 <= 2 else t0 - WH
    big_a = t1 if t1 <= 2 else t1 - WH
    ahead = 1 if 2 * big_a > a or 2 * big_a - a == 0 and a < 0 else -1
    return a, big_a, ahead


def classes_of(needs, slack):
    rounded = [tuple(-(-size // 8) * 8 for size in need) for need in needs]
    heavy = [sum(need[1:3]) * 2 + sum(need[4:]) for need in rounded]
    limits = []
    for size in sorted(set(heavy)):
        if not limits or size > limits[-1][0] * slack:
            limits.append([size, size])
        limits[-1][1] = size
    which = [next(n for n, limit in enumerate(limits) if size <= limit[1]) for size in heavy]
    sizes = [
        [max(need[k] for need, w in zip(rounded, which) if w == n) for k in range(len(needs[0]))]
        for n in range(len(limits))
    ]
    return sizes, which


def rooms(sizes):
    return [up16(max(size[k] for size in sizes)) for k in range(len(sizes[0]))]


class Plan:
    def __init__(self, rows, cols):
        crows, ccols = rows // 2, cols // 2
        block, cblock = natural(rows, cols), natural(crows, ccols)
        cases = []
        for t0, t1 in PAIRS:
            a, big_a, ahead = offsets(t0, t1)
            fine = moved(windowed(rows, cols), a)
            coarse = moved(cblock, big_a)
            quarters = [
                (l, 2 * r + dr, 2 * c + dc)
                for dr, dc in ((0, 0), (1, 0), (0, 1), (1, 1))
                for l, r, c in coarse
            ]
            come = 1 if a > 0 else -1
            one = exchange_places(block, fine, rows, cols, come)
            home = [p for p in block if p not in set(fine)]
            wanted = quarters + (home if come == -ahead else [])
            two = exchange_places(fine, wanted, rows, cols, ahead)
            back = 1 if big_a < 0 else -1
            three = exchange_places(coarse, cblock, crows, ccols, back)
            got = set(fine).union(*[places for _, places in two])
            four = exchange_places(fine, [p for p in block if p not in got], rows, cols, back)
            cases.append((come, ahead, back, fine, coarse, quarters, one, two, three, four))

        def needs(which):
            return [[len(numbers) for numbers, _ in case[which]] for case in cases]

        self.one, one_class = classes_of(needs(6), 1.15)
        self.two, two_class = classes_of(needs(7), 1.15)
        sizes, three_class = classes_of([three + four for three, four in zip(needs(8), needs(9))], 1.0)
        self.three, self.four = [size[:3] for size in sizes], [size[3:] for size in sizes]
        self.room_one, self.room_two = rooms(self.one), rooms(self.two)
        self.room_three, self.room_four = rooms(self.three), rooms(self.four)

        def branches(which_class, direction):
            pairs = [(n, case[direction]) for n, case in zip(which_class, cases)]
            found = sorted(set(pairs))
            return found, [found.index(pair) for pair in pairs]

        self.one_branches, one_at = branches(one_class, 0)
        self.two_branches, two_at = branches(two_class, 1)
        self.three_branches, three_at = branches(three_class, 2)
        self.flags = dict(
            three_class=three_class,
            one_at=one_at, two_at=two_at, three_at=three_at,
            a=[offsets(*pair)[0] for pair in PAIRS], big_a=[offsets(*pair)[1] for pair in PAIRS],
        )

        found = {}
        for n, (come, ahead, back, fine, coarse, quarters, one, two, three, four) in enumerate(cases):

            def send(exchanged, room):
                return [n for (numbers, _), size in zip(exchanged, room) for n in numbers + [-1] * (size - len(numbers))]

            def source(held, *exchanges):
                places = list(held)
                for exchanged, room in exchanges:
                    for (_, got), size in zip(exchanged, room):
                        places += got + [None] * (size - len(got))
                return {p: n for n, p in enumerate(places) if p is not None}

            first, second = source(block, (one, self.room_one)), source(fine, (two, self.room_two))
            third = source(coarse, (three, self.room_three))
            last = source(fine, (two, self.room_two), (four, self.room_four))
            out = [(l, r, c) for r in range(crows) for c in range(ccols) for l in range(2)]
            rows_of = dict(
                send_one=send(one, self.room_one),
                take_one=[first[p] for p in fine],
                send_two=send(two, self.room_two),
                take_two=[second[p] for p in quarters],
                send_three=send(three, self.room_three),
                send_four=send(four, self.room_four),
                fine_out=[last[p] for p in block],
                coarse_out=[third[p] for p in out],
            )
            for name, row in rows_of.items():
                found.setdefault(name, []).append(row)
        parts, self.at, top = [], {}, 0
        for name, lists in found.items():
            length = -(-max(len(row) for row in lists) // 128)
            part = np.full((len(PAIRS), length * 128), -1, np.float32)
            for n, row in enumerate(lists):
                part[n, : len(row)] = row
            parts.append(part.reshape(len(PAIRS), length, 128))
            self.at[name] = (top, length)
            top += length
        parts.append(np.zeros((len(PAIRS), -top % 8, 128), np.float32))
        self.table = np.concatenate(parts, axis=1)


def case_of(shifts_ref):
    t0, t1 = shifts_ref[0], shifts_ref[1]
    return jnp.where(t0 == WH - 1, t1 - 1, t0 + WH - 2)


def lookup(values, case):
    out = jnp.int32(values[0])
    for n, value in enumerate(values[1:], 1):
        out = jnp.where(case == n, value, out)
    return out


def columns_of(rows, count):
    parts = [jnp.broadcast_to(rows[j : j + 1], (128, 128)).T for j in range(-(-count // 128))]
    return stack_rows(parts)[:count]


def select_rows(index, source):
    lane = lax.broadcasted_iota(I32, (1, 128), 1).astype(F32)
    size = source.shape[0]
    pick = [jnp.where(index == lane + float(at), 1.0, 0.0).astype(BF16) for at in range(0, size, 128)]
    pick = jnp.concatenate(pick, axis=1)[:, :size]
    return jnp.dot(pick, source, preferred_element_type=F32)


def stack_rows(parts):
    return parts[0] if len(parts) == 1 else jnp.concatenate(parts, axis=0)


def layer_norm(values):
    center = jnp.mean(values, axis=-1, keepdims=True)
    values = values - center
    spread = jnp.mean(values * values, axis=-1, keepdims=True)
    return values * lax.rsqrt(spread + EPS)


def attend_windows(qkv_of, key_ids, query_ids, windows, inner, finish):
    lane = lax.broadcasted_iota(I32, (1, 256), 1)
    units = [(w, g) for w in range(windows) for g in range(inner // 256)]
    scores, weights, outs = {}, {}, {}

    def score(w, g):
        q, k = qkv_of(w, g * 256), qkv_of(w, inner + g * 256)
        masks = [jnp.where((lane >= h * HD) & (lane < (h + 1) * HD), 1.0, 0.0).astype(BF16) for h in range(8)]
        queries = stack_rows([q * mine for mine in masks])
        scores[w, g] = lax.dot_general(k, queries, NT, preferred_element_type=F32)

    def soften(w, g):
        s = jnp.where(key_ids(w) == query_ids(w), scores.pop((w, g)), -BIG)
        weight = jnp.exp2((s - jnp.max(s, axis=0, keepdims=True)) * SCALE)
        weights[w, g] = weight.astype(BF16), 1.0 / jnp.sum(weight, axis=0, keepdims=True)

    def gather(w, g):
        weight, scale = weights.pop((w, g))
        values = qkv_of(w, 2 * inner + g * 256).T
        parts = []
        for at in range(0, 8 * TOK, 256):
            end = min(at + 256, 8 * TOK)
            first, last = at // TOK, (end - 1) // TOK
            out = jnp.dot(values[first * HD : (last + 1) * HD], weight[:, at:end], preferred_element_type=F32)
            picked = out[:HD]
            for h in range(first + 1, last + 1):
                mine = out[(h - first) * HD : (h - first + 1) * HD]
                picked = jnp.where(lane[:, : end - at] < h * TOK - at, picked, mine)
            parts.append(picked)
        out = (jnp.concatenate(parts, axis=1) * scale).astype(BF16)
        outs[w, g] = [out[:, h * TOK : (h + 1) * TOK] for h in range(8)]
        if g == inner // 256 - 1:
            finish(w, stack_rows([part for k in range(inner // 256) for part in outs.pop((w, k))]))

    for n in range(len(units) + 2):
        if n < len(units):
            score(*units[n])
        if 0 <= n - 1 < len(units):
            soften(*units[n - 1])
        if 0 <= n - 2 < len(units):
            gather(*units[n - 2])


ANY = pl.BlockSpec(memory_space=pl.ANY)
HBM = pl.BlockSpec(memory_space=pltpu.HBM)
VMEM = pl.BlockSpec(memory_space=pltpu.VMEM)
SMEM = pl.BlockSpec(memory_space=pltpu.SMEM)


def call(body, outs, args, in_specs, scratch, copies, flops, moved_bytes, vmem=8):
    args = [
        pltpu.with_memory_space_constraint(arg, spec.memory_space) for arg, spec in zip(args, in_specs, strict=True)
    ]
    spaces = [getattr(out, "memory_space", pltpu.SMEM if out.dtype == I32 else pltpu.VMEM) for out in outs]
    out_specs = [pl.BlockSpec(memory_space=space) for space in spaces]
    return pl.pallas_call(
        body,
        out_shape=outs,
        in_specs=in_specs,
        out_specs=out_specs,
        scratch_shapes=list(scratch) + [pltpu.SemaphoreType.DMA((copies,))],
        compiler_params=pltpu.CompilerParams(vmem_limit_bytes=vmem << 20),
        cost_estimate=pl.CostEstimate(flops=flops, bytes_accessed=moved_bytes, transcendentals=0),
    )(*args)


def shapes(sizes, width, space=pltpu.VMEM):
    return [space((n, width), BF16) for n in sizes]


class Copies:
    def __init__(self, sems):
        self.sems, self.used = sems, 0

    def __call__(self, src, dst):
        copy = pltpu.make_async_copy(src, dst, self.sems.at[self.used])
        self.used += 1
        copy.start()
        return copy


def lay(pieces, room):
    width = pieces[0].shape[1]

    def body(*refs):
        out_ref = refs[len(pieces)]
        at = 0
        for ref, space in zip(refs, room):
            rows = ref.shape[0]
            out_ref[at : at + rows, :] = ref[...]
            if rows < space:
                out_ref[at + rows : at + space, :] = jnp.zeros((space - rows, width), BF16)
            at += space

    return call(body, shapes([sum(room)], width), pieces, [VMEM] * 3, [], 1, 0, 1 << 18)[0]


def flat(ref):
    layers, rows, cols, width = ref.shape
    return ref[...].astype(F32).reshape(layers * rows * cols, width).astype(BF16)


def put_pieces(value, refs):
    at = 0
    for ref in refs:
        ref[...] = value[at : at + ref.shape[0]].astype(BF16)
        at += ref.shape[0]


def rows_of(plan, table_ref, name, *lead):
    top, length = plan.at[name]
    return table_ref[(*lead, slice(top, top + length), slice(None))]


def exchange(pieces, sizes, sign):
    lat, lon = lax.axis_size("lat"), lax.axis_size("lon")
    row, col, both = [piece[:size] for piece, size in zip(pieces, sizes)]
    pairs = [((i + sign) % lat * lon + (j + sign) % lon, i * lon + j) for i in range(lat) for j in range(lon)]
    col = lax.ppermute(col, "lon", [((j + sign) % lon, j) for j in range(lon)])
    both = lax.ppermute(both, ("lat", "lon"), pairs)
    row = lax.ppermute(row, "lat", [((i + sign) % lat, i) for i in range(lat)])
    return [row, col, both]


def choose(index, branches, *args):
    flat_args, tree = jax.tree.flatten(args)
    out_trees = []

    def closed(branch):
        def run(*leaves):
            out, out_tree = jax.tree.flatten(branch(*jax.tree.unflatten(tree, leaves)))
            out_trees.append(out_tree)
            return out

        return jax.make_jaxpr(run)(*flat_args)

    out = lax.cond_p.bind(index, *flat_args, branches=tuple(closed(branch) for branch in branches))
    return jax.tree.unflatten(out_trees[0], out)


FLAGS = ("three_class", "a", "big_a")


def first_pieces(shifts, tokens, plan):
    width = tokens.shape[-1]
    count = tokens.size // width
    kinds = 3

    def body(shifts_hbm, tokens_hbm, table_hbm, *refs):
        outs, refs = refs[:kinds], refs[kinds:]
        rows_ref, flags_ref, *at_refs, shifts_ref, tokens_ref, table_ref, source_ref, sems = refs
        start = Copies(sems)
        shift = start(shifts_hbm, shifts_ref)
        held = start(tokens_hbm, tokens_ref)
        table = start(table_hbm, table_ref)
        shift.wait()
        case = case_of(shifts_ref)
        for ref, name in zip(at_refs, ("one_at", "two_at", "three_at")):
            ref[0] = lookup(plan.flags[name], case)
        for n, name in enumerate(FLAGS):
            flags_ref[n] = lookup(plan.flags[name], case)
        held.wait()
        source_ref[...] = flat(tokens_ref)
        table.wait()
        rows_ref[...] = table_ref[case]
        index = columns_of(rows_of(plan, table_ref, "send_one", case), sum(plan.room_one))
        put_pieces(select_rows(index, source_ref[...]), outs)

    outs = shapes(plan.room_one, width)
    outs += [pltpu.VMEM(plan.table.shape[1:], F32), pltpu.SMEM((8,), I32)]
    outs += [pltpu.SMEM((1,), I32)] * 3
    scratch = [pltpu.SMEM((2,), I32), pltpu.VMEM(tokens.shape, BF16), pltpu.VMEM(plan.table.shape, F32)]
    scratch += [pltpu.VMEM((count, width), BF16)]
    got = call(body, outs, [shifts, tokens, plan.table], [HBM] * 3, scratch, 3, 1 << 28, 1 << 20)
    sent, (rows, flags, one, two, three) = got[:kinds], got[kinds:]
    return sent, rows, flags, one[0], two[0], three[0]


def before_fine(flags, regions, tokens, table, weights, plan):
    _, lat, lon = regions.shape
    _, rows, cols, width = tokens.shape
    flat_regions = regions.reshape(2 * lat, lon)
    fine, coarse = windowed(rows, cols), natural(rows // 2, cols // 2)

    def lanes(places, scale, is_fine):
        places = np.asarray([(l, scale * r, scale * c, is_fine) for l, r, c in places], np.float32)
        return np.pad(places, ((0, -len(places) % 128), (0, 0))).T.reshape(4, -1, 128)

    places = np.concatenate([lanes(fine, 1, 1), lanes(coarse, 2, 0)], axis=1)
    lines = places.shape[1]

    def body(flags_ref, rows_ref, regions_hbm, places_hbm, tokens_hbm, *refs):
        weights_hbm, refs = refs[: len(weights)], refs[len(weights) :]
        id_ref, x_ref, *refs = refs
        weight_refs, (regions_ref, places_ref, tokens_ref, sems) = refs[: len(weights)], refs[len(weights) :]
        start = Copies(sems)
        waits = [start(regions_hbm, regions_ref), start(places_hbm, places_ref)]
        held = start(tokens_hbm, tokens_ref)
        later = [start(src, dst) for src, dst in zip(weights_hbm, weight_refs)]
        for copy in waits:
            copy.wait()
        a = flags_ref[1].astype(F32)
        big_a = 2.0 * flags_ref[2].astype(F32)
        is_fine = places_ref[3]
        d = is_fine * a + (1.0 - is_fine) * big_a
        row = places_ref[1] + d + (lax.axis_index("lat") * rows).astype(F32)
        col = places_ref[2] + 2.0 * d + (lax.axis_index("lon") * cols).astype(F32)
        wrapped = jnp.where((row < 0) | (row >= lat), 4.0, 0.0)
        row = jnp.where(row < 0, row + lat, jnp.where(row >= lat, row - lat, row))
        col = jnp.where(col < 0, col + lon, jnp.where(col >= lon, col - lon, col))
        row = row + places_ref[0] * lat

        def along(values):
            return jnp.concatenate([values[n : n + 1] for n in range(lines)], axis=1)

        line = lax.broadcasted_iota(I32, (2 * lat, 1), 0).astype(F32)
        pick = jnp.where(line == along(row), 1.0, 0.0).astype(BF16)
        known = regions_ref[...].astype(F32).astype(BF16)
        picked = lax.dot_general(known, pick, TN, preferred_element_type=F32)
        line = lax.broadcasted_iota(I32, (lon, 1), 0).astype(F32)
        ids = jnp.sum(jnp.where(line == along(col), picked, 0.0), axis=0, keepdims=True) + along(wrapped)
        for n in range(lines):
            id_ref[n : n + 1, :] = ids[:, n * 128 : (n + 1) * 128]
        held.wait()
        take = columns_of(rows_of(plan, rows_ref, "take_one"), len(fine))
        x_ref[...] = select_rows(take, flat(tokens_ref)).astype(BF16)
        for copy in later:
            copy.wait()

    outs = [pltpu.VMEM((lines, 128), F32)] + shapes([len(fine)], width)
    outs += [pltpu.VMEM(w.shape, BF16) for w in weights]
    scratch = [pltpu.VMEM(flat_regions.shape, I32), pltpu.VMEM(places.shape, F32), pltpu.VMEM(tokens.shape, BF16)]
    args = [flags, table, flat_regions, places, tokens, *weights]
    in_specs = [SMEM, VMEM] + [HBM] * (3 + len(weights))
    ids, x, *weights = call(body, outs, args, in_specs, scratch, 3 + len(weights), 1 << 28, 4 << 20)
    return ids, x, weights


def along_lanes(lines, at):
    flat_lines = jnp.concatenate([lines[n : n + 1] for n in range(lines.shape[0])], axis=1)
    return jnp.concatenate([flat_lines[:, at : at + TOK]] * 8, axis=1)


def before_coarse(fine, table, weight, plan):
    own, width = fine.shape
    half = 3 * weight.shape[0] // 8

    def body(rows_ref, fine_hbm, weight_hbm, x_ref, part_hbm, weight_ref, fine_ref, part_ref, sems):
        start = Copies(sems)
        held = start(fine_hbm, fine_ref)
        later = start(weight_hbm.at[pl.ds(0, half)], weight_ref)
        take = columns_of(rows_of(plan, rows_ref, "fine_out"), own)
        held.wait()
        part_ref[...] = select_rows(take, fine_ref[...]).astype(BF16)
        leave = start(part_ref, part_hbm)
        take = columns_of(rows_of(plan, rows_ref, "take_two"), own)
        x_ref[...] = select_rows(take, fine_ref[...]).astype(BF16)
        leave.wait()
        later.wait()

    outs = shapes([own], width) + shapes([own], width, pltpu.HBM) + shapes([half], weight.shape[1])
    scratch = [pltpu.VMEM(fine.shape, BF16)] * 2
    return call(body, outs, [table, fine, weight], [VMEM, HBM, HBM], scratch, 3, 1 << 28, 4 << 20)


def fine_level(x_own, source, ids, w_qkv, w_proj, rows, plan):
    count, width = x_own.shape
    inner = w_proj.shape[0]

    def body(own_ref, source_ref, ids_ref, qkv_w_ref, proj_w_ref, rows_ref, out_hbm, *refs):
        *piece_outs, x_ref, qkv_ref, out_ref, id_ref, sems = refs
        start = Copies(sems)
        lines = ids_ref[: -(-count // 128), :]
        id_ref[...] = columns_of(lines, count)
        leave = []
        take = columns_of(rows_of(plan, rows_ref, "take_one"), count) - float(count)
        x = own_ref[...].astype(F32) + select_rows(take, source_ref[...])
        x_ref[...] = x
        normed = layer_norm(x).astype(BF16)
        qkv_ref[...] = jnp.dot(normed, qkv_w_ref[...], preferred_element_type=F32).astype(BF16)

        def finish(w, out):
            at = slice(w * TOK, (w + 1) * TOK)
            out = lax.dot_general(out, proj_w_ref[...], TN, preferred_element_type=F32)
            out_ref[at, :] = (x_ref[at, :] + out).astype(BF16)
            leave.append(start(out_ref.at[pl.ds(w * TOK, TOK)], out_hbm.at[pl.ds(w * TOK, TOK)]))

        attend_windows(
            lambda w, at: qkv_ref[w * TOK : (w + 1) * TOK, at : at + 256],
            lambda w: id_ref[w * TOK : (w + 1) * TOK, :1],
            lambda w: along_lanes(lines, w * TOK),
            count // TOK,
            inner,
            finish,
        )
        index = columns_of(rows_of(plan, rows_ref, "send_two"), sum(plan.room_two))
        put_pieces(select_rows(index, out_ref[...]), piece_outs)
        for copy in leave:
            copy.wait()

    outs = shapes([count], width, pltpu.HBM) + shapes(plan.room_two, width)
    scratch = [
        pltpu.VMEM((count, width), F32),
        pltpu.VMEM((count, 3 * inner), BF16),
        pltpu.VMEM((count, width), BF16),
        pltpu.VMEM((count, 128), F32),
    ]
    args = [x_own, source, ids, w_qkv, w_proj, rows]
    out, *sent = call(body, outs, args, [VMEM] * len(args), scratch, count // TOK, 3 << 30, 6 << 20, 14)
    return out, sent


def coarse_level(flags, fine, x_own, source, ids, merge_first, w_merge, w_qkv, w_proj, rows, plan):
    depth, width = w_merge.shape
    own, half = fine.shape
    count = own // 4
    inner = w_proj.shape[0]

    def body(
        flags_ref, fine_hbm, merge_hbm, qkv_w_hbm, proj_w_hbm, own_ref, source_ref, ids_ref, first_ref, rows_ref, *refs
    ):
        out_ref, *piece_outs = refs[:4]
        qkv_ref, id_ref, fine_ref, merge_ref, qkv_w_ref, proj_w_ref, sems = refs[4:]
        start = Copies(sems)
        with_fine = [n for n, sizes in enumerate(plan.four) if sum(sizes)]
        needs_fine = functools.reduce(jnp.logical_or, [flags_ref[0] == n for n in with_fine])

        def bring(src, dst):
            cuts = [(at, min(half, src.shape[0] - at)) for at in range(0, src.shape[0], half)]
            return [(at, size, start(src.at[pl.ds(at, size)], dst.at[pl.ds(at, size)])) for at, size in cuts]

        def product(x, ref, copies):
            parts = []
            for at, size, copy in copies:
                copy.wait()
                parts.append(jnp.dot(x[:, at : at + size], ref[at : at + size, :], preferred_element_type=F32))
            return functools.reduce(jnp.add, parts)

        here = first_ref.shape[0]
        merge_w = bring(merge_hbm.at[pl.ds(here, depth - here)], merge_ref)
        qkv_w = bring(qkv_w_hbm, qkv_w_ref)
        proj_w = start(proj_w_hbm, proj_w_ref)
        fine_copy = (fine_hbm, fine_ref, sems.at[start.used])

        @pl.when(needs_fine)
        def _():
            pltpu.make_async_copy(*fine_copy).start()

        lines = ids_ref[-(-own // 128) :, :]
        id_ref[...] = columns_of(lines, count)
        take = columns_of(rows_of(plan, rows_ref, "take_two"), 4 * count) - float(own)
        x = own_ref[...].astype(F32) + select_rows(take, source_ref[...])
        x = jnp.concatenate([x[n * count : (n + 1) * count] for n in range(4)], axis=1)
        stacked = layer_norm(x).astype(BF16)
        merged = jnp.dot(stacked[:, :here], first_ref[...], preferred_element_type=F32)
        merged = (merged + product(stacked[:, here:], merge_ref, merge_w)).astype(BF16).astype(F32)
        normed = layer_norm(merged).astype(BF16)
        qkv_ref[...] = product(normed, qkv_w_ref, qkv_w).astype(BF16)
        proj_w.wait()

        def finish(w, out):
            out = lax.dot_general(out, proj_w_ref[...], TN, preferred_element_type=F32)
            out_ref[...] = (merged + out).astype(BF16)

        attend_windows(
            lambda w, at: qkv_ref[:, at : at + 256],
            lambda w: id_ref[:, :1],
            lambda w: along_lanes(lines, 0),
            1,
            inner,
            finish,
        )
        sent = select_rows(columns_of(rows_of(plan, rows_ref, "send_three"), sum(plan.room_three)), out_ref[...])
        sent = sent.astype(BF16)
        for n, sizes in enumerate(plan.three):

            @pl.when(flags_ref[0] == n)
            def _():
                at = 0
                for ref, size, space in zip(piece_outs, sizes, plan.room_three):
                    ref[:size, :] = sent[at : at + size, :half]
                    ref[size : 2 * size, :] = sent[at : at + size, half:]
                    at += space

        @pl.when(needs_fine)
        def _():
            pltpu.make_async_copy(*fine_copy).wait()
            index = columns_of(rows_of(plan, rows_ref, "send_four"), sum(plan.room_four))
            sent = select_rows(index, fine_ref[...]).astype(BF16)
            for n in with_fine:

                @pl.when(flags_ref[0] == n)
                def _():
                    at = 0
                    for ref, size, more, space in zip(piece_outs, plan.three[n], plan.four[n], plan.room_four):
                        ref[2 * size : 2 * size + more, :] = sent[at : at + more]
                        at += space

    most = [max(2 * three[k] + four[k] for three, four in zip(plan.three, plan.four)) for k in range(3)]
    outs = shapes([count], width) + shapes(most, half)
    scratch = [pltpu.VMEM((count, 3 * inner), BF16), pltpu.VMEM((count, 128), F32)]
    shapes_in = [fine.shape, (depth - merge_first.shape[0], width), w_qkv.shape, w_proj.shape]
    scratch += [pltpu.VMEM(shape, BF16) for shape in shapes_in]
    args = [flags, fine, w_merge, w_qkv, w_proj, x_own, source, ids, merge_first, rows]
    in_specs = [SMEM] + [HBM] * 4 + [VMEM] * (len(args) - 5)
    copies = depth // half + width // half + 3
    out, *sent = call(body, outs, args, in_specs, scratch, copies, 3 << 30, 12 << 20, 24)
    return out, sent


def fine_output(part, source, rows, plan, block_rows, block_cols, partial):
    own, width = part.shape

    def body(part_hbm, source_ref, rows_ref, out_ref, part_ref, stage_ref, sems):
        start = Copies(sems)
        cuts = [pl.ds(at, TOK) for at in range(0, own, TOK)]
        held = [start(part_hbm.at[cut], part_ref.at[cut]) for cut in cuts]
        take = columns_of(rows_of(plan, rows_ref, "fine_out"), own) - float(own)
        leave = []
        for n, (cut, copy) in enumerate(zip(cuts, held)):
            got = select_rows(take[n * TOK : (n + 1) * TOK], source_ref[...])
            copy.wait()
            out = part_ref[cut, :].astype(F32) + got
            if partial:
                out_ref[cut, :] = out.astype(BF16)
            else:
                lines = TOK // block_cols
                layer, line = divmod(n * lines, block_rows)
                there = (layer, pl.ds(line, lines))
                stage_ref[there] = out.reshape(lines, block_cols, width).astype(BF16)
                leave.append(start(stage_ref.at[there], out_ref.at[there]))
        for copy in leave:
            copy.wait()

    shape = (2, block_rows, block_cols, width)
    outs = shapes([own], width) if partial else [pltpu.HBM(shape, BF16)]
    scratch = [pltpu.VMEM(part.shape, BF16), pltpu.VMEM(shape, BF16)]
    return call(body, outs, [part, source, rows], [HBM, VMEM, VMEM], scratch, 2 * own // TOK, 1 << 30, 4 << 20)[0]


def coarse_output(coarse, got, rows, which, plan, block_rows, block_cols, part=None):
    own, width = coarse.shape
    half = width // 2
    sizes, more = plan.three[which], plan.four[which]
    parts = [] if part is None else [part]

    def padded(parts, sizes, room):
        out = []
        for value, size, space in zip(parts, sizes, room):
            out.append(value)
            if size < space:
                out.append(jnp.zeros((space - size, value.shape[1]), F32))
        return out

    def body(coarse_ref, *refs):
        got_refs, refs = refs[:3], refs[3:]
        part_refs, (rows_ref, out_ref, *fine_outs, _) = refs[: len(parts)], refs[len(parts) :]
        got = [ref[...].astype(F32) for ref in got_refs]
        back = [jnp.concatenate([x[:size], x[size : 2 * size]], axis=1) for x, size in zip(got, sizes)]
        source = stack_rows([coarse_ref[...].astype(F32)] + padded(back, sizes, plan.room_three))
        out = select_rows(columns_of(rows_of(plan, rows_ref, "coarse_out"), own), source.astype(BF16)).astype(BF16)
        for n in range(own // 2):
            out_ref[n // block_cols, n % block_cols] = out[2 * n : 2 * n + 2]
        for part_ref, fine_ref in zip(part_refs, fine_outs):
            fine = stack_rows(padded([x[2 * size :] for x, size in zip(got, sizes)], more, plan.room_four))
            base = part_ref.shape[0] + sum(plan.room_two)
            take = columns_of(rows_of(plan, rows_ref, "fine_out"), part_ref.shape[0]) - float(base)
            out = part_ref[...].astype(F32) + select_rows(take, fine.astype(BF16))
            fine_ref[...] = out.reshape(fine_ref.shape).astype(BF16)

    outs = [jax.ShapeDtypeStruct((block_rows, block_cols, 2, width), BF16)]
    outs += [jax.ShapeDtypeStruct((2, 2 * block_rows, 2 * block_cols, half), BF16) for _ in parts]
    args = [coarse, *got, *parts, rows]
    out, *fine = call(body, outs, args, [VMEM] * len(args), [], 1, 1 << 28, 1 << 20)
    return out.transpose(2, 0, 1, 3), *fine


def on_device(tokens, regions, shifts, fine_qkv, fine_proj, merge_weight, coarse_qkv, coarse_proj):
    _, rows, cols, _ = tokens.shape
    plan = Plan(rows, cols)

    def first(which, sign, sent, *args):
        got = exchange(sent, plan.one[which], sign)
        return lay(got, plan.room_one), before_fine(*args, plan)

    def second(which, sign, sent, *args):
        got = exchange(sent, plan.two[which], sign)
        return lay(got, plan.room_two), before_coarse(*args, plan)

    def third(which, sign, sent, part, source, coarse, table):
        sizes = [2 * n + m for n, m in zip(plan.three[which], plan.four[which])]
        got = exchange(sent, sizes, sign)
        partial = sum(plan.four[which]) > 0
        fine_out = fine_output(part, source, table, plan, rows, cols, partial)
        place = (table, which, plan, rows // 2, cols // 2)
        if partial:
            coarse_out, fine_out = coarse_output(coarse, got, *place, part=fine_out)
        else:
            (coarse_out,) = coarse_output(coarse, got, *place)
        return fine_out, coarse_out

    def branches(stage, pairs):
        return [functools.partial(stage, which, sign) for which, sign in pairs]

    sent, table, flags, one, two, three = first_pieces(shifts, tokens, plan)
    got, (ids, x, weights) = choose(
        one, branches(first, plan.one_branches), sent, flags, regions, tokens, table, [fine_qkv, fine_proj]
    )
    fine, sent = fine_level(x, got, ids, *weights, table, plan)
    got, (x, part, merge_first) = choose(two, branches(second, plan.two_branches), sent, fine, table, merge_weight)
    coarse, sent = coarse_level(
        flags, fine, x, got, ids, merge_first, merge_weight, coarse_qkv, coarse_proj, table, plan
    )
    return choose(three, branches(third, plan.three_branches), sent, part, got, coarse, table)


def solution(mesh):
    return jax.shard_map(
        on_device,
        mesh=mesh,
        in_specs=(P(None, "lat", "lon", None), P(), P(), P(), P(), P(), P(), P()),
        out_specs=(P(None, "lat", "lon", None), P(None, "lat", "lon", None)),
        check_vma=False,
    )
```

```python
import functools

import jax
import jax.numpy as jnp
import numpy as np
from jax import lax
from jax.experimental import pallas as pl
from jax.experimental.pallas import tpu as pltpu
from jax.sharding import PartitionSpec as P

HD = 32
WH = 6
WW = 12
TOK = 2 * WH * WW
EPS = 1e-05
BIG = 1e30
SCALE = float(np.log2(np.e) / np.sqrt(HD))

NT = (((1,), (1,)), ((), ()))
TN = (((0,), (0,)), ((), ()))
F32 = jnp.float32
BF16 = jnp.bfloat16
I32 = jnp.int32

PAIRS = [(WH - 1, t) for t in range(1, WH)] + [(t, WH - 1) for t in range(1, WH - 1)]


def up16(count):
    return -(-count // 16) * 16


def natural(rows, cols):
    return [(l, r, c) for l in range(2) for r in range(rows) for c in range(cols)]


def windowed(rows, cols):
    return [
        (l, wr * WH + r, wc * WW + c)
        for wr in range(rows // WH)
        for wc in range(cols // WW)
        for l in range(2)
        for r in range(WH)
        for c in range(WW)
    ]


def moved(order, d):
    return [(l, r + d, c + 2 * d) for l, r, c in order]


def exchange_places(held, wanted, rows, cols, sign):
    at = {place: n for n, place in enumerate(held)}
    found = []
    for dr, dc in ((sign, 0), (0, sign), (sign, sign)):
        numbers, places = [], []
        for l, r, c in sorted(set(wanted) - set(held)):
            n = at.get((l, r - dr * rows, c - dc * cols))
            if n is not None:
                numbers.append(n)
                places.append((l, r, c))
        found.append((numbers, places))
    return found


def offsets(t0, t1):
    a = t0 if t0 <= 2 else t0 - WH
    big_a = t1 if t1 <= 2 else t1 - WH
    ahead = 1 if 2 * big_a > a or 2 * big_a - a == 0 and a < 0 else -1
    return a, big_a, ahead


def classes_of(needs, slack):
    rounded = [tuple(-(-size // 8) * 8 for size in need) for need in needs]
    heavy = [sum(need[1:3]) * 2 + sum(need[4:]) for need in rounded]
    limits = []
    for size in sorted(set(heavy)):
        if not limits or size > limits[-1][0] * slack:
            limits.append([size, size])
        limits[-1][1] = size
    which = [next(n for n, limit in enumerate(limits) if size <= limit[1]) for size in heavy]
    sizes = [
        [max(need[k] for need, w in zip(rounded, which) if w == n) for k in range(len(needs[0]))]
        for n in range(len(limits))
    ]
    return sizes, which


def rooms(sizes):
    return [up16(max(size[k] for size in sizes)) for k in range(len(sizes[0]))]


class Plan:
    def __init__(self, rows, cols):
        crows, ccols = rows // 2, cols // 2
        block, cblock = natural(rows, cols), natural(crows, ccols)
        cases = []
        for t0, t1 in PAIRS:
            a, big_a, ahead = offsets(t0, t1)
            fine = moved(windowed(rows, cols), a)
            coarse = moved(cblock, big_a)
            quarters = [
                (l, 2 * r + dr, 2 * c + dc)
                for dr, dc in ((0, 0), (1, 0), (0, 1), (1, 1))
                for l, r, c in coarse
            ]
            come = 1 if a > 0 else -1
            one = exchange_places(block, fine, rows, cols, come)
            home = [p for p in block if p not in set(fine)]
            wanted = quarters + (home if come == -ahead else [])
            two = exchange_places(fine, wanted, rows, cols, ahead)
            back = 1 if big_a < 0 else -1
            three = exchange_places(coarse, cblock, crows, ccols, back)
            got = set(fine).union(*[places for _, places in two])
            four = exchange_places(fine, [p for p in block if p not in got], rows, cols, back)
            cases.append((come, ahead, back, fine, coarse, quarters, one, two, three, four))

        def needs(which):
            return [[len(numbers) for numbers, _ in case[which]] for case in cases]

        self.one, one_class = classes_of(needs(6), 1.15)
        self.two, two_class = classes_of(needs(7), 1.15)
        sizes, three_class = classes_of([three + four for three, four in zip(needs(8), needs(9))], 1.0)
        self.three, self.four = [size[:3] for size in sizes], [size[3:] for size in sizes]
        self.room_one, self.room_two = rooms(self.one), rooms(self.two)
        self.room_three, self.room_four = rooms(self.three), rooms(self.four)

        def branches(which_class, direction):
            pairs = [(n, case[direction]) for n, case in zip(which_class, cases)]
            found = sorted(set(pairs))
            return found, [found.index(pair) for pair in pairs]

        self.one_branches, one_at = branches(one_class, 0)
        self.two_branches, two_at = branches(two_class, 1)
        self.three_branches, three_at = branches(three_class, 2)
        self.flags = dict(
            three_class=three_class,
            one_at=one_at, two_at=two_at, three_at=three_at,
            a=[offsets(*pair)[0] for pair in PAIRS], big_a=[offsets(*pair)[1] for pair in PAIRS],
        )

        found = {}
        for n, (come, ahead, back, fine, coarse, quarters, one, two, three, four) in enumerate(cases):

            def send(exchanged, room):
                return [n for (numbers, _), size in zip(exchanged, room) for n in numbers + [-1] * (size - len(numbers))]

            def source(held, *exchanges):
                places = list(held)
                for exchanged, room in exchanges:
                    for (_, got), size in zip(exchanged, room):
                        places += got + [None] * (size - len(got))
                return {p: n for n, p in enumerate(places) if p is not None}

            first, second = source(block, (one, self.room_one)), source(fine, (two, self.room_two))
            third = source(coarse, (three, self.room_three))
            last = source(fine, (two, self.room_two), (four, self.room_four))
            out = [(l, r, c) for r in range(crows) for c in range(ccols) for l in range(2)]
            rows_of = dict(
                send_one=send(one, self.room_one),
                take_one=[first[p] for p in fine],
                send_two=send(two, self.room_two),
                take_two=[second[p] for p in quarters],
                send_three=send(three, self.room_three),
                send_four=send(four, self.room_four),
                fine_out=[last[p] for p in block],
                coarse_out=[third[p] for p in out],
            )
            for name, row in rows_of.items():
                found.setdefault(name, []).append(row)
        parts, self.at, top = [], {}, 0
        for name, lists in found.items():
            length = -(-max(len(row) for row in lists) // 128)
            part = np.full((len(PAIRS), length * 128), -1, np.float32)
            for n, row in enumerate(lists):
                part[n, : len(row)] = row
            parts.append(part.reshape(len(PAIRS), length, 128))
            self.at[name] = (top, length)
            top += length
        parts.append(np.zeros((len(PAIRS), -top % 8, 128), np.float32))
        self.table = np.concatenate(parts, axis=1)


def case_of(shifts_ref):
    t0, t1 = shifts_ref[0], shifts_ref[1]
    return jnp.where(t0 == WH - 1, t1 - 1, t0 + WH - 2)


def lookup(values, case):
    out = jnp.int32(values[0])
    for n, value in enumerate(values[1:], 1):
        out = jnp.where(case == n, value, out)
    return out


def columns_of(rows, count):
    parts = [jnp.broadcast_to(rows[j : j + 1], (128, 128)).T for j in range(-(-count // 128))]
    return stack_rows(parts)[:count]


def select_rows(index, source):
    lane = lax.broadcasted_iota(I32, (1, 128), 1).astype(F32)
    size = source.shape[0]
    pick = [jnp.where(index == lane + float(at), 1.0, 0.0).astype(BF16) for at in range(0, size, 128)]
    pick = jnp.concatenate(pick, axis=1)[:, :size]
    return jnp.dot(pick, source, preferred_element_type=F32)


def stack_rows(parts):
    return parts[0] if len(parts) == 1 else jnp.concatenate(parts, axis=0)


def layer_norm(values):
    center = jnp.mean(values, axis=-1, keepdims=True)
    values = values - center
    spread = jnp.mean(values * values, axis=-1, keepdims=True)
    return values * lax.rsqrt(spread + EPS)


def attend_windows(qkv_of, id_of, windows, inner, finish):
    lane = lax.broadcasted_iota(I32, (1, 128), 1)
    forbid = jnp.where(lane < 8, BIG, 0.0).astype(BF16)
    groups = inner // 128
    units = [(w, g) for w in range(windows) for g in range(groups)]
    scores, weights, outs = {}, {}, {}

    def score(w, g):
        key_id = id_of(w)
        not_id = (key_id - 1).astype(BF16) * forbid
        q = qkv_of(w, g * 128)
        keys = jnp.concatenate([qkv_of(w, inner + g * 128), key_id], axis=1)
        queries = []
        for h in range(4):
            mine = jnp.where((lane >= h * HD) & (lane < (h + 1) * HD), 1.0, 0.0).astype(BF16)
            queries.append(jnp.concatenate([q * mine, not_id], axis=1))
        scores[w, g] = lax.dot_general(stack_rows(queries), keys, NT, preferred_element_type=F32)

    def soften(w, g):
        s = scores.pop((w, g))
        weights[w, g] = jnp.exp2((s - jnp.max(s, axis=1, keepdims=True)) * SCALE).astype(BF16)

    def gather(w, g):
        v = qkv_of(w, 2 * inner + g * 128)
        values = jnp.concatenate([v, jnp.ones_like(v)], axis=1)
        out = jnp.dot(weights.pop((w, g)), values, preferred_element_type=F32)
        picked, total = out[:TOK, :128], out[:TOK, 128:]
        for h in range(1, 4):
            rows = slice(h * TOK, (h + 1) * TOK)
            picked = jnp.where(lane < h * HD, picked, out[rows, :128])
            total = jnp.where(lane < h * HD, total, out[rows, 128:])
        outs[w, g] = (picked / total).astype(BF16)
        if g == groups - 1:
            finish(w, jnp.concatenate([outs.pop((w, k)) for k in range(groups)], axis=1))

    for n in range(len(units) + 2):
        if n < len(units):
            score(*units[n])
        if 0 <= n - 1 < len(units):
            soften(*units[n - 1])
        if 0 <= n - 2 < len(units):
            gather(*units[n - 2])


ANY = pl.BlockSpec(memory_space=pl.ANY)
HBM = pl.BlockSpec(memory_space=pltpu.HBM)
VMEM = pl.BlockSpec(memory_space=pltpu.VMEM)
SMEM = pl.BlockSpec(memory_space=pltpu.SMEM)


def call(body, outs, args, in_specs, scratch, copies, flops, moved_bytes, vmem=8):
    args = [
        pltpu.with_memory_space_constraint(arg, spec.memory_space) for arg, spec in zip(args, in_specs, strict=True)
    ]
    spaces = [getattr(out, "memory_space", pltpu.SMEM if out.dtype == I32 else pltpu.VMEM) for out in outs]
    out_specs = [pl.BlockSpec(memory_space=space) for space in spaces]
    return pl.pallas_call(
        body,
        out_shape=outs,
        in_specs=in_specs,
        out_specs=out_specs,
        scratch_shapes=list(scratch) + [pltpu.SemaphoreType.DMA((copies,))],
        compiler_params=pltpu.CompilerParams(vmem_limit_bytes=vmem << 20),
        cost_estimate=pl.CostEstimate(flops=flops, bytes_accessed=moved_bytes, transcendentals=0),
    )(*args)


def shapes(sizes, width, space=pltpu.VMEM):
    return [space((n, width), BF16) for n in sizes]


class Copies:
    def __init__(self, sems):
        self.sems, self.used = sems, 0

    def __call__(self, src, dst):
        copy = pltpu.make_async_copy(src, dst, self.sems.at[self.used])
        self.used += 1
        copy.start()
        return copy


def lay(pieces, room):
    width = pieces[0].shape[1]

    def body(*refs):
        out_ref = refs[len(pieces)]
        at = 0
        for ref, space in zip(refs, room):
            rows = ref.shape[0]
            out_ref[at : at + rows, :] = ref[...]
            if rows < space:
                out_ref[at + rows : at + space, :] = jnp.zeros((space - rows, width), BF16)
            at += space

    return call(body, shapes([sum(room)], width), pieces, [VMEM] * 3, [], 1, 0, 1 << 18)[0]


def flat(ref):
    layers, rows, cols, width = ref.shape
    return ref[...].astype(F32).reshape(layers * rows * cols, width).astype(BF16)


def put_pieces(value, refs):
    at = 0
    for ref in refs:
        ref[...] = value[at : at + ref.shape[0]].astype(BF16)
        at += ref.shape[0]


def rows_of(plan, table_ref, name, *lead):
    top, length = plan.at[name]
    return table_ref[(*lead, slice(top, top + length), slice(None))]


def exchange(pieces, sizes, sign):
    lat, lon = lax.axis_size("lat"), lax.axis_size("lon")
    row, col, both = [piece[:size] for piece, size in zip(pieces, sizes)]
    pairs = [((i + sign) % lat * lon + (j + sign) % lon, i * lon + j) for i in range(lat) for j in range(lon)]
    col = lax.ppermute(col, "lon", [((j + sign) % lon, j) for j in range(lon)])
    both = lax.ppermute(both, ("lat", "lon"), pairs)
    row = lax.ppermute(row, "lat", [((i + sign) % lat, i) for i in range(lat)])
    return [row, col, both]


def choose(index, branches, *args):
    flat_args, tree = jax.tree.flatten(args)
    out_trees = []

    def closed(branch):
        def run(*leaves):
            out, out_tree = jax.tree.flatten(branch(*jax.tree.unflatten(tree, leaves)))
            out_trees.append(out_tree)
            return out

        return jax.make_jaxpr(run)(*flat_args)

    out = lax.cond_p.bind(index, *flat_args, branches=tuple(closed(branch) for branch in branches))
    return jax.tree.unflatten(out_trees[0], out)


FLAGS = ("three_class", "a", "big_a")


def first_pieces(shifts, tokens, plan):
    width = tokens.shape[-1]
    count = tokens.size // width
    kinds = 3

    def body(shifts_hbm, tokens_hbm, table_hbm, *refs):
        outs, refs = refs[:kinds], refs[kinds:]
        source_ref, rows_ref, flags_ref, *at_refs, shifts_ref, tokens_ref, table_ref, sems = refs
        start = Copies(sems)
        shift = start(shifts_hbm, shifts_ref)
        held = start(tokens_hbm, tokens_ref)
        table = start(table_hbm, table_ref)
        shift.wait()
        case = case_of(shifts_ref)
        for ref, name in zip(at_refs, ("one_at", "two_at", "three_at")):
            ref[0] = lookup(plan.flags[name], case)
        for n, name in enumerate(FLAGS):
            flags_ref[n] = lookup(plan.flags[name], case)
        held.wait()
        source_ref[...] = flat(tokens_ref)
        table.wait()
        rows_ref[...] = table_ref[case]
        index = columns_of(rows_of(plan, table_ref, "send_one", case), sum(plan.room_one))
        put_pieces(select_rows(index, source_ref[...]), outs)

    outs = shapes([*plan.room_one, count], width)
    outs += [pltpu.VMEM(plan.table.shape[1:], F32), pltpu.SMEM((8,), I32)]
    outs += [pltpu.SMEM((1,), I32)] * 3
    scratch = [pltpu.SMEM((2,), I32), pltpu.VMEM(tokens.shape, BF16), pltpu.VMEM(plan.table.shape, F32)]
    got = call(body, outs, [shifts, tokens, plan.table], [HBM] * 3, scratch, 3, 1 << 28, 1 << 20)
    sent, (source, rows, flags, one, two, three) = got[:kinds], got[kinds:]
    return sent, source, rows, flags, one[0], two[0], three[0]


def before_fine(flags, regions, tokens, table, weights, plan, rows, cols):
    _, lat, lon = regions.shape
    width = tokens.shape[1]
    flat_regions = regions.reshape(2 * lat, lon)
    fine, coarse = windowed(rows, cols), natural(rows // 2, cols // 2)

    def lanes(places, scale, is_fine):
        places = np.asarray([(l, scale * r, scale * c, is_fine) for l, r, c in places], np.float32)
        return np.pad(places, ((0, -len(places) % 128), (0, 0))).T.reshape(4, -1, 128)

    places = np.concatenate([lanes(fine, 1, 1), lanes(coarse, 2, 0)], axis=1)
    lines = places.shape[1]

    def body(flags_ref, rows_ref, tokens_ref, regions_hbm, places_hbm, *refs):
        weights_hbm, refs = refs[: len(weights)], refs[len(weights) :]
        id_ref, x_ref, *refs = refs
        weight_refs, (regions_ref, places_ref, sems) = refs[: len(weights)], refs[len(weights) :]
        start = Copies(sems)
        waits = [start(regions_hbm, regions_ref), start(places_hbm, places_ref)]
        later = [start(src, dst) for src, dst in zip(weights_hbm, weight_refs)]
        for copy in waits:
            copy.wait()
        a = flags_ref[1].astype(F32)
        big_a = 2.0 * flags_ref[2].astype(F32)
        is_fine = places_ref[3]
        d = is_fine * a + (1.0 - is_fine) * big_a
        row = places_ref[1] + d + (lax.axis_index("lat") * rows).astype(F32)
        col = places_ref[2] + 2.0 * d + (lax.axis_index("lon") * cols).astype(F32)
        wrapped = jnp.where((row < 0) | (row >= lat), 4.0, 0.0)
        row = jnp.where(row < 0, row + lat, jnp.where(row >= lat, row - lat, row))
        col = jnp.where(col < 0, col + lon, jnp.where(col >= lon, col - lon, col))
        row = row + places_ref[0] * lat

        def along(values):
            return jnp.concatenate([values[n : n + 1] for n in range(lines)], axis=1)

        line = lax.broadcasted_iota(I32, (2 * lat, 1), 0).astype(F32)
        pick = jnp.where(line == along(row), 1.0, 0.0).astype(BF16)
        known = regions_ref[...].astype(F32).astype(BF16)
        picked = lax.dot_general(known, pick, TN, preferred_element_type=F32)
        line = lax.broadcasted_iota(I32, (lon, 1), 0).astype(F32)
        ids = jnp.sum(jnp.where(line == along(col), picked, 0.0), axis=0, keepdims=True) + along(wrapped)
        for n in range(lines):
            id_ref[n : n + 1, :] = ids[:, n * 128 : (n + 1) * 128]
        take = columns_of(rows_of(plan, rows_ref, "take_one"), len(fine))
        x_ref[...] = select_rows(take, tokens_ref[...]).astype(BF16)
        for copy in later:
            copy.wait()

    outs = [pltpu.VMEM((lines, 128), F32)] + shapes([len(fine)], width)
    outs += [pltpu.VMEM(w.shape, BF16) for w in weights]
    scratch = [pltpu.VMEM(flat_regions.shape, I32), pltpu.VMEM(places.shape, F32)]
    args = [flags, table, tokens, flat_regions, places, *weights]
    in_specs = [SMEM, VMEM, VMEM] + [HBM] * (2 + len(weights))
    ids, x, *weights = call(body, outs, args, in_specs, scratch, 2 + len(weights), 1 << 28, 4 << 20)
    return ids, x, weights


def id_columns(lines, count):
    lane = lax.broadcasted_iota(I32, (1, 128), 1).astype(F32)
    return jnp.where(columns_of(lines, count) == lane, 1.0, 0.0).astype(BF16)


def before_coarse(flags, fine, table, weight, plan):
    own, width = fine.shape
    half = 3 * weight.shape[0] // 8

    def body(flags_ref, rows_ref, fine_ref, weight_hbm, x_ref, part_hbm, home_ref, weight_ref, part_ref, sems):
        start = Copies(sems)
        later = start(weight_hbm.at[pl.ds(0, half)], weight_ref)
        take = columns_of(rows_of(plan, rows_ref, "fine_out"), own)
        part_ref[...] = select_rows(take, fine_ref[...]).astype(BF16)
        leave = start(part_ref, part_hbm)
        take = columns_of(rows_of(plan, rows_ref, "take_two"), own)
        x_ref[...] = select_rows(take, fine_ref[...]).astype(BF16)

        @pl.when(needs_fine(flags_ref, plan))
        def _():
            index = columns_of(rows_of(plan, rows_ref, "send_four"), sum(plan.room_four))
            home_ref[...] = select_rows(index, fine_ref[...]).astype(BF16)

        leave.wait()
        later.wait()

    outs = shapes([own], width) + shapes([own], width, pltpu.HBM)
    outs += shapes([sum(plan.room_four)], width) + shapes([half], weight.shape[1])
    scratch = [pltpu.VMEM(fine.shape, BF16)]
    args = [flags, table, fine, weight]
    return call(body, outs, args, [SMEM, VMEM, VMEM, HBM], scratch, 2, 1 << 28, 4 << 20)


def needs_fine(flags_ref, plan):
    with_fine = [n for n, sizes in enumerate(plan.four) if sum(sizes)]
    return functools.reduce(jnp.logical_or, [flags_ref[0] == n for n in with_fine])


def fine_level(x_own, source, ids, w_qkv, w_proj, rows, plan):
    count, width = x_own.shape
    inner = w_proj.shape[0]

    def body(own_ref, source_ref, ids_ref, qkv_w_ref, proj_w_ref, rows_ref, out_ref, *refs):
        *piece_outs, x_ref, qkv_ref, id_ref, _ = refs
        id_ref[...] = id_columns(ids_ref[: -(-count // 128), :], count)
        take = columns_of(rows_of(plan, rows_ref, "take_one"), count) - float(count)
        x = own_ref[...].astype(F32) + select_rows(take, source_ref[...])
        x_ref[...] = x
        normed = layer_norm(x).astype(BF16)
        qkv_ref[...] = jnp.dot(normed, qkv_w_ref[...], preferred_element_type=F32).astype(BF16)

        def finish(w, out):
            at = slice(w * TOK, (w + 1) * TOK)
            out = jnp.dot(out, proj_w_ref[...], preferred_element_type=F32)
            out_ref[at, :] = (x_ref[at, :] + out).astype(BF16)

        attend_windows(
            lambda w, at: qkv_ref[w * TOK : (w + 1) * TOK, at : at + 128],
            lambda w: id_ref[w * TOK : (w + 1) * TOK, :],
            count // TOK,
            inner,
            finish,
        )
        index = columns_of(rows_of(plan, rows_ref, "send_two"), sum(plan.room_two))
        put_pieces(select_rows(index, out_ref[...]), piece_outs)

    outs = shapes([count, *plan.room_two], width)
    scratch = [
        pltpu.VMEM((count, width), F32),
        pltpu.VMEM((count, 3 * inner), BF16),
        pltpu.VMEM((count, 128), BF16),
    ]
    args = [x_own, source, ids, w_qkv, w_proj, rows]
    out, *sent = call(body, outs, args, [VMEM] * len(args), scratch, 1, 3 << 30, 6 << 20, 14)
    return out, sent


def coarse_level(flags, home, x_own, source, ids, merge_first, w_merge, w_qkv, w_proj, rows, plan):
    depth, width = w_merge.shape
    own, half = x_own.shape
    count = own // 4
    inner = w_proj.shape[0]

    def body(
        flags_ref, merge_hbm, qkv_w_hbm, proj_w_hbm, home_ref, own_ref, source_ref, ids_ref, first_ref, rows_ref, *refs
    ):
        out_ref, *piece_outs = refs[:4]
        qkv_ref, id_ref, merge_ref, qkv_w_ref, proj_w_ref, sems = refs[4:]
        start = Copies(sems)
        def bring(src, dst):
            cuts = [(at, min(half, src.shape[0] - at)) for at in range(0, src.shape[0], half)]
            return [(at, size, start(src.at[pl.ds(at, size)], dst.at[pl.ds(at, size)])) for at, size in cuts]

        def product(x, ref, copies):
            parts = []
            for at, size, copy in copies:
                copy.wait()
                parts.append(jnp.dot(x[:, at : at + size], ref[at : at + size, :], preferred_element_type=F32))
            return functools.reduce(jnp.add, parts)

        here = first_ref.shape[0]
        merge_w = bring(merge_hbm.at[pl.ds(here, depth - here)], merge_ref)
        qkv_w = bring(qkv_w_hbm, qkv_w_ref)
        proj_w = start(proj_w_hbm, proj_w_ref)
        id_ref[...] = id_columns(ids_ref[-(-own // 128) :, :], count)
        take = columns_of(rows_of(plan, rows_ref, "take_two"), 4 * count) - float(own)
        x = own_ref[...].astype(F32) + select_rows(take, source_ref[...])
        x = jnp.concatenate([x[n * count : (n + 1) * count] for n in range(4)], axis=1)
        stacked = layer_norm(x).astype(BF16)
        merged = jnp.dot(stacked[:, :here], first_ref[...], preferred_element_type=F32)
        merged = (merged + product(stacked[:, here:], merge_ref, merge_w)).astype(BF16).astype(F32)
        normed = layer_norm(merged).astype(BF16)
        qkv_ref[...] = product(normed, qkv_w_ref, qkv_w).astype(BF16)
        proj_w.wait()

        def finish(w, out):
            out = jnp.dot(out, proj_w_ref[...], preferred_element_type=F32)
            out_ref[...] = (merged + out).astype(BF16)

        attend_windows(lambda w, at: qkv_ref[:, at : at + 128], lambda w: id_ref[...], 1, inner, finish)
        sent = select_rows(columns_of(rows_of(plan, rows_ref, "send_three"), sum(plan.room_three)), out_ref[...])
        sent = sent.astype(BF16)
        for n, sizes in enumerate(plan.three):

            @pl.when(flags_ref[0] == n)
            def _():
                at = 0
                for ref, size, space in zip(piece_outs, sizes, plan.room_three):
                    ref[:size, :] = sent[at : at + size, :half]
                    ref[size : 2 * size, :] = sent[at : at + size, half:]
                    at += space

        for n, fine_sizes in enumerate(plan.four):
            if sum(fine_sizes):

                @pl.when(flags_ref[0] == n)
                def _():
                    at = 0
                    for ref, size, more, space in zip(piece_outs, plan.three[n], fine_sizes, plan.room_four):
                        ref[2 * size : 2 * size + more, :] = home_ref[at : at + more, :]
                        at += space

    most = [max(2 * three[k] + four[k] for three, four in zip(plan.three, plan.four)) for k in range(3)]
    outs = shapes([count], width) + shapes(most, half)
    scratch = [pltpu.VMEM((count, 3 * inner), BF16)]
    shapes_in = [(count, 128), (depth - merge_first.shape[0], width), w_qkv.shape, w_proj.shape]
    scratch += [pltpu.VMEM(shape, BF16) for shape in shapes_in]
    args = [flags, w_merge, w_qkv, w_proj, home, x_own, source, ids, merge_first, rows]
    in_specs = [SMEM] + [HBM] * 3 + [VMEM] * (len(args) - 4)
    copies = depth // half + width // half + 3
    out, *sent = call(body, outs, args, in_specs, scratch, copies, 3 << 30, 12 << 20, 24)
    return out, sent


def fine_output(part, source, rows, plan, block_rows, block_cols, partial):
    own, width = part.shape

    def body(part_hbm, source_ref, rows_ref, out_ref, part_ref, stage_ref, sems):
        start = Copies(sems)
        cuts = [pl.ds(at, TOK) for at in range(0, own, TOK)]
        held = [start(part_hbm.at[cut], part_ref.at[cut]) for cut in cuts]
        take = columns_of(rows_of(plan, rows_ref, "fine_out"), own) - float(own)
        leave = []
        for n, (cut, copy) in enumerate(zip(cuts, held)):
            got = select_rows(take[n * TOK : (n + 1) * TOK], source_ref[...])
            copy.wait()
            out = part_ref[cut, :].astype(F32) + got
            if partial:
                out_ref[cut, :] = out.astype(BF16)
            else:
                lines = TOK // block_cols
                layer, line = divmod(n * lines, block_rows)
                there = (layer, pl.ds(line, lines))
                stage_ref[there] = out.reshape(lines, block_cols, width).astype(BF16)
                leave.append(start(stage_ref.at[there], out_ref.at[there]))
        for copy in leave:
            copy.wait()

    shape = (2, block_rows, block_cols, width)
    outs = shapes([own], width) if partial else [pltpu.HBM(shape, BF16)]
    scratch = [pltpu.VMEM(part.shape, BF16), pltpu.VMEM(shape, BF16)]
    return call(body, outs, [part, source, rows], [HBM, VMEM, VMEM], scratch, 2 * own // TOK, 1 << 30, 4 << 20)[0]


def coarse_output(coarse, got, rows, which, plan, block_rows, block_cols, part=None):
    own, width = coarse.shape
    half = width // 2
    sizes, more = plan.three[which], plan.four[which]
    parts = [] if part is None else [part]

    def padded(parts, sizes, room):
        out = []
        for value, size, space in zip(parts, sizes, room):
            out.append(value)
            if size < space:
                out.append(jnp.zeros((space - size, value.shape[1]), F32))
        return out

    def body(coarse_ref, *refs):
        got_refs, refs = refs[:3], refs[3:]
        part_refs, (rows_ref, out_ref, *fine_outs, _) = refs[: len(parts)], refs[len(parts) :]
        got = [ref[...].astype(F32) for ref in got_refs]
        back = [jnp.concatenate([x[:size], x[size : 2 * size]], axis=1) for x, size in zip(got, sizes)]
        source = stack_rows([coarse_ref[...].astype(F32)] + padded(back, sizes, plan.room_three))
        out = select_rows(columns_of(rows_of(plan, rows_ref, "coarse_out"), own), source.astype(BF16)).astype(BF16)
        for n in range(own // 2):
            out_ref[n // block_cols, n % block_cols] = out[2 * n : 2 * n + 2]
        for part_ref, fine_ref in zip(part_refs, fine_outs):
            fine = stack_rows(padded([x[2 * size :] for x, size in zip(got, sizes)], more, plan.room_four))
            base = part_ref.shape[0] + sum(plan.room_two)
            take = columns_of(rows_of(plan, rows_ref, "fine_out"), part_ref.shape[0]) - float(base)
            out = part_ref[...].astype(F32) + select_rows(take, fine.astype(BF16))
            fine_ref[...] = out.reshape(fine_ref.shape).astype(BF16)

    outs = [jax.ShapeDtypeStruct((block_rows, block_cols, 2, width), BF16)]
    outs += [jax.ShapeDtypeStruct((2, 2 * block_rows, 2 * block_cols, half), BF16) for _ in parts]
    args = [coarse, *got, *parts, rows]
    out, *fine = call(body, outs, args, [VMEM] * len(args), [], 1, 1 << 28, 1 << 20)
    return out.transpose(2, 0, 1, 3), *fine


def on_device(tokens, regions, shifts, fine_qkv, fine_proj, merge_weight, coarse_qkv, coarse_proj):
    _, rows, cols, _ = tokens.shape
    plan = Plan(rows, cols)

    def first(which, sign, sent, *args):
        got = exchange(sent, plan.one[which], sign)
        return lay(got, plan.room_one), before_fine(*args, plan, rows, cols)

    def second(which, sign, sent, *args):
        got = exchange(sent, plan.two[which], sign)
        return lay(got, plan.room_two), before_coarse(*args, plan)

    def third(which, sign, sent, part, source, coarse, table):
        sizes = [2 * n + m for n, m in zip(plan.three[which], plan.four[which])]
        got = exchange(sent, sizes, sign)
        partial = sum(plan.four[which]) > 0
        fine_out = fine_output(part, source, table, plan, rows, cols, partial)
        place = (table, which, plan, rows // 2, cols // 2)
        if partial:
            coarse_out, fine_out = coarse_output(coarse, got, *place, part=fine_out)
        else:
            (coarse_out,) = coarse_output(coarse, got, *place)
        return fine_out, coarse_out

    def branches(stage, pairs):
        return [functools.partial(stage, which, sign) for which, sign in pairs]

    sent, source, table, flags, one, two, three = first_pieces(shifts, tokens, plan)
    got, (ids, x, weights) = choose(
        one, branches(first, plan.one_branches), sent, flags, regions, source, table, [fine_qkv, fine_proj]
    )
    fine, sent = fine_level(x, got, ids, *weights, table, plan)
    got, (x, part, home, merge_first) = choose(
        two, branches(second, plan.two_branches), sent, flags, fine, table, merge_weight
    )
    coarse, sent = coarse_level(
        flags, home, x, got, ids, merge_first, merge_weight, coarse_qkv, coarse_proj, table, plan
    )
    return choose(three, branches(third, plan.three_branches), sent, part, got, coarse, table)


def solution(mesh):
    return jax.shard_map(
        on_device,
        mesh=mesh,
        in_specs=(P(None, "lat", "lon", None), P(), P(), P(), P(), P(), P(), P()),
        out_specs=(P(None, "lat", "lon", None), P(None, "lat", "lon", None)),
        check_vma=False,
    )
```

```python
import functools

import jax
import jax.numpy as jnp
import numpy as np
from jax import lax
from jax.experimental import pallas as pl
from jax.experimental.pallas import tpu as pltpu
from jax.sharding import PartitionSpec as P

HD = 32
WH = 6
WW = 12
TOK = 2 * WH * WW
EPS = 1e-05
BIG = 1e30
SCALE = float(np.log2(np.e) / np.sqrt(HD))

NT = (((1,), (1,)), ((), ()))
TN = (((0,), (0,)), ((), ()))
F32 = jnp.float32
BF16 = jnp.bfloat16
I32 = jnp.int32

PAIRS = [(WH - 1, t) for t in range(1, WH)] + [(t, WH - 1) for t in range(1, WH - 1)]


def up16(count):
    return -(-count // 16) * 16


def natural(rows, cols):
    return [(l, r, c) for l in range(2) for r in range(rows) for c in range(cols)]


def windowed(rows, cols):
    return [
        (l, wr * WH + r, wc * WW + c)
        for wr in range(rows // WH)
        for wc in range(cols // WW)
        for l in range(2)
        for r in range(WH)
        for c in range(WW)
    ]


def moved(order, d):
    return [(l, r + d, c + 2 * d) for l, r, c in order]


def exchange_places(held, wanted, rows, cols, sign):
    at = {place: n for n, place in enumerate(held)}
    found = []
    for dr, dc in ((sign, 0), (0, sign), (sign, sign)):
        numbers, places = [], []
        for l, r, c in sorted(set(wanted) - set(held)):
            n = at.get((l, r - dr * rows, c - dc * cols))
            if n is not None:
                numbers.append(n)
                places.append((l, r, c))
        found.append((numbers, places))
    return found


def offsets(t0, t1):
    a = t0 if t0 <= 2 else t0 - WH
    big_a = t1 if t1 <= 2 else t1 - WH
    ahead = 1 if 2 * big_a > a or 2 * big_a - a == 0 and a < 0 else -1
    return a, big_a, ahead


def classes_of(needs, slack):
    rounded = [tuple(-(-size // 8) * 8 for size in need) for need in needs]
    heavy = [sum(need[1:3]) * 2 + sum(need[4:]) for need in rounded]
    limits = []
    for size in sorted(set(heavy)):
        if not limits or size > limits[-1][0] * slack:
            limits.append([size, size])
        limits[-1][1] = size
    which = [next(n for n, limit in enumerate(limits) if size <= limit[1]) for size in heavy]
    sizes = [
        [max(need[k] for need, w in zip(rounded, which) if w == n) for k in range(len(needs[0]))]
        for n in range(len(limits))
    ]
    return sizes, which


def rooms(sizes):
    return [up16(max(size[k] for size in sizes)) for k in range(len(sizes[0]))]


class Plan:
    def __init__(self, rows, cols):
        crows, ccols = rows // 2, cols // 2
        block, cblock = natural(rows, cols), natural(crows, ccols)
        cases = []
        for t0, t1 in PAIRS:
            a, big_a, ahead = offsets(t0, t1)
            fine = moved(windowed(rows, cols), a)
            coarse = moved(cblock, big_a)
            quarters = [
                (l, 2 * r + dr, 2 * c + dc)
                for dr, dc in ((0, 0), (1, 0), (0, 1), (1, 1))
                for l, r, c in coarse
            ]
            come = 1 if a > 0 else -1
            one = exchange_places(block, fine, rows, cols, come)
            home = [p for p in block if p not in set(fine)]
            wanted = quarters + (home if come == -ahead else [])
            two = exchange_places(fine, wanted, rows, cols, ahead)
            back = 1 if big_a < 0 else -1
            three = exchange_places(coarse, cblock, crows, ccols, back)
            got = set(fine).union(*[places for _, places in two])
            four = exchange_places(fine, [p for p in block if p not in got], rows, cols, back)
            cases.append((come, ahead, back, fine, coarse, quarters, one, two, three, four))

        def needs(which):
            return [[len(numbers) for numbers, _ in case[which]] for case in cases]

        self.one, one_class = classes_of(needs(6), 1.15)
        self.two, two_class = classes_of(needs(7), 1.15)
        sizes, three_class = classes_of([three + four for three, four in zip(needs(8), needs(9))], 1.0)
        self.three, self.four = [size[:3] for size in sizes], [size[3:] for size in sizes]
        self.room_one, self.room_two = rooms(self.one), rooms(self.two)
        self.room_three, self.room_four = rooms(self.three), rooms(self.four)

        def branches(which_class, direction):
            pairs = [(n, case[direction]) for n, case in zip(which_class, cases)]
            found = sorted(set(pairs))
            return found, [found.index(pair) for pair in pairs]

        self.one_branches, one_at = branches(one_class, 0)
        self.two_branches, two_at = branches(two_class, 1)
        self.three_branches, three_at = branches(three_class, 2)
        self.flags = dict(
            three_class=three_class,
            one_at=one_at, two_at=two_at, three_at=three_at,
            a=[offsets(*pair)[0] for pair in PAIRS], big_a=[offsets(*pair)[1] for pair in PAIRS],
        )

        found = {}
        for n, (come, ahead, back, fine, coarse, quarters, one, two, three, four) in enumerate(cases):

            def send(exchanged, room):
                return [n for (numbers, _), size in zip(exchanged, room) for n in numbers + [-1] * (size - len(numbers))]

            def source(held, *exchanges):
                places = list(held)
                for exchanged, room in exchanges:
                    for (_, got), size in zip(exchanged, room):
                        places += got + [None] * (size - len(got))
                return {p: n for n, p in enumerate(places) if p is not None}

            first, second = source(block, (one, self.room_one)), source(fine, (two, self.room_two))
            third = source(coarse, (three, self.room_three))
            last = source(fine, (two, self.room_two), (four, self.room_four))
            out = [(l, r, c) for r in range(crows) for c in range(ccols) for l in range(2)]
            rows_of = dict(
                send_one=send(one, self.room_one),
                take_one=[first[p] for p in fine],
                send_two=send(two, self.room_two),
                take_two=[second[p] for p in quarters],
                send_three=send(three, self.room_three),
                send_four=send(four, self.room_four),
                fine_out=[last[p] for p in block],
                coarse_out=[third[p] for p in out],
            )
            for name, row in rows_of.items():
                found.setdefault(name, []).append(row)
        parts, self.at, top = [], {}, 0
        for name, lists in found.items():
            length = -(-max(len(row) for row in lists) // 128)
            part = np.full((len(PAIRS), length * 128), -1, np.float32)
            for n, row in enumerate(lists):
                part[n, : len(row)] = row
            parts.append(part.reshape(len(PAIRS), length, 128))
            self.at[name] = (top, length)
            top += length
        parts.append(np.zeros((len(PAIRS), -top % 8, 128), np.float32))
        self.table = np.concatenate(parts, axis=1)


def case_of(shifts_ref):
    t0, t1 = shifts_ref[0], shifts_ref[1]
    return jnp.where(t0 == WH - 1, t1 - 1, t0 + WH - 2)


def lookup(values, case):
    out = jnp.int32(values[0])
    for n, value in enumerate(values[1:], 1):
        out = jnp.where(case == n, value, out)
    return out


def columns_of(rows, count):
    parts = [jnp.broadcast_to(rows[j : j + 1], (128, 128)).T for j in range(-(-count // 128))]
    return stack_rows(parts)[:count]


def select_rows(index, source):
    lane = lax.broadcasted_iota(I32, (1, 128), 1).astype(F32)
    size = source.shape[0]
    pick = [jnp.where(index == lane + float(at), 1.0, 0.0).astype(BF16) for at in range(0, size, 128)]
    pick = jnp.concatenate(pick, axis=1)[:, :size]
    return jnp.dot(pick, source, preferred_element_type=F32)


def stack_rows(parts):
    return parts[0] if len(parts) == 1 else jnp.concatenate(parts, axis=0)


def layer_norm(values):
    center = jnp.mean(values, axis=-1, keepdims=True)
    values = values - center
    spread = jnp.mean(values * values, axis=-1, keepdims=True)
    return values * lax.rsqrt(spread + EPS)


def attend_windows(qkv_of, id_of, windows, inner, finish):
    lane = lax.broadcasted_iota(I32, (1, 128), 1)
    forbid = jnp.where(lane < 8, BIG, 0.0).astype(BF16)
    groups = inner // 128
    units = [(w, g) for w in range(windows) for g in range(groups)]
    scores, weights, outs = {}, {}, {}

    def score(w, g):
        key_id = id_of(w)
        not_id = (key_id - 1).astype(BF16) * forbid
        q = qkv_of(w, g * 128)
        keys = jnp.concatenate([qkv_of(w, inner + g * 128), key_id], axis=1)
        queries = []
        for h in range(4):
            mine = jnp.where((lane >= h * HD) & (lane < (h + 1) * HD), 1.0, 0.0).astype(BF16)
            queries.append(jnp.concatenate([q * mine, not_id], axis=1))
        scores[w, g] = lax.dot_general(stack_rows(queries), keys, NT, preferred_element_type=F32)

    def soften(w, g):
        s = scores.pop((w, g))
        weights[w, g] = jnp.exp2((s - jnp.max(s, axis=1, keepdims=True)) * SCALE).astype(BF16)

    def gather(w, g):
        v = qkv_of(w, 2 * inner + g * 128)
        values = jnp.concatenate([v, jnp.ones_like(v)], axis=1)
        out = jnp.dot(weights.pop((w, g)), values, preferred_element_type=F32)
        picked, total = out[:TOK, :128], out[:TOK, 128:]
        for h in range(1, 4):
            rows = slice(h * TOK, (h + 1) * TOK)
            picked = jnp.where(lane < h * HD, picked, out[rows, :128])
            total = jnp.where(lane < h * HD, total, out[rows, 128:])
        outs[w, g] = (picked / total).astype(BF16)
        if g == groups - 1:
            finish(w, jnp.concatenate([outs.pop((w, k)) for k in range(groups)], axis=1))

    for n in range(len(units) + 2):
        if n < len(units):
            score(*units[n])
        if 0 <= n - 1 < len(units):
            soften(*units[n - 1])
        if 0 <= n - 2 < len(units):
            gather(*units[n - 2])


ANY = pl.BlockSpec(memory_space=pl.ANY)
HBM = pl.BlockSpec(memory_space=pltpu.HBM)
VMEM = pl.BlockSpec(memory_space=pltpu.VMEM)
SMEM = pl.BlockSpec(memory_space=pltpu.SMEM)


def call(body, outs, args, in_specs, scratch, copies, flops, moved_bytes, vmem=8):
    args = [
        pltpu.with_memory_space_constraint(arg, spec.memory_space) for arg, spec in zip(args, in_specs, strict=True)
    ]
    spaces = [getattr(out, "memory_space", pltpu.SMEM if out.dtype == I32 else pltpu.VMEM) for out in outs]
    out_specs = [pl.BlockSpec(memory_space=space) for space in spaces]
    return pl.pallas_call(
        body,
        out_shape=outs,
        in_specs=in_specs,
        out_specs=out_specs,
        scratch_shapes=list(scratch) + [pltpu.SemaphoreType.DMA((copies,))],
        compiler_params=pltpu.CompilerParams(vmem_limit_bytes=vmem << 20),
        cost_estimate=pl.CostEstimate(flops=flops, bytes_accessed=moved_bytes, transcendentals=0),
    )(*args)


def shapes(sizes, width, space=pltpu.VMEM):
    return [space((n, width), BF16) for n in sizes]


class Copies:
    def __init__(self, sems):
        self.sems, self.used = sems, 0

    def __call__(self, src, dst):
        copy = pltpu.make_async_copy(src, dst, self.sems.at[self.used])
        self.used += 1
        copy.start()
        return copy


def lay(pieces, room):
    width = pieces[0].shape[1]

    def body(*refs):
        out_ref = refs[len(pieces)]
        at = 0
        for ref, space in zip(refs, room):
            rows = ref.shape[0]
            out_ref[at : at + rows, :] = ref[...]
            if rows < space:
                out_ref[at + rows : at + space, :] = jnp.zeros((space - rows, width), BF16)
            at += space

    return call(body, shapes([sum(room)], width), pieces, [VMEM] * 3, [], 1, 0, 1 << 18)[0]


def flat(ref):
    layers, rows, cols, width = ref.shape
    return ref[...].astype(F32).reshape(layers * rows * cols, width).astype(BF16)


def put_pieces(value, refs):
    at = 0
    for ref in refs:
        ref[...] = value[at : at + ref.shape[0]].astype(BF16)
        at += ref.shape[0]


def rows_of(plan, table_ref, name, *lead):
    top, length = plan.at[name]
    return table_ref[(*lead, slice(top, top + length), slice(None))]


def exchange(pieces, sizes, sign):
    lat, lon = lax.axis_size("lat"), lax.axis_size("lon")
    row, col, both = [piece[:size] for piece, size in zip(pieces, sizes)]
    pairs = [((i + sign) % lat * lon + (j + sign) % lon, i * lon + j) for i in range(lat) for j in range(lon)]
    col = lax.ppermute(col, "lon", [((j + sign) % lon, j) for j in range(lon)])
    both = lax.ppermute(both, ("lat", "lon"), pairs)
    row = lax.ppermute(row, "lat", [((i + sign) % lat, i) for i in range(lat)])
    return [row, col, both]


def choose(index, branches, *args):
    flat_args, tree = jax.tree.flatten(args)
    out_trees = []

    def closed(branch):
        def run(*leaves):
            out, out_tree = jax.tree.flatten(branch(*jax.tree.unflatten(tree, leaves)))
            out_trees.append(out_tree)
            return out

        return jax.make_jaxpr(run)(*flat_args)

    out = lax.cond_p.bind(index, *flat_args, branches=tuple(closed(branch) for branch in branches))
    return jax.tree.unflatten(out_trees[0], out)


FLAGS = ("three_class", "a", "big_a")


def first_pieces(shifts, tokens, plan):
    width = tokens.shape[-1]
    count = tokens.size // width
    kinds = 3

    def body(shifts_hbm, tokens_hbm, table_hbm, *refs):
        outs, refs = refs[:kinds], refs[kinds:]
        source_ref, rows_ref, flags_ref, *at_refs, shifts_ref, tokens_ref, table_ref, sems = refs
        start = Copies(sems)
        shift = start(shifts_hbm, shifts_ref)
        held = start(tokens_hbm, tokens_ref)
        table = start(table_hbm, table_ref)
        shift.wait()
        case = case_of(shifts_ref)
        for ref, name in zip(at_refs, ("one_at", "two_at", "three_at")):
            ref[0] = lookup(plan.flags[name], case)
        for n, name in enumerate(FLAGS):
            flags_ref[n] = lookup(plan.flags[name], case)
        held.wait()
        source_ref[...] = flat(tokens_ref)
        table.wait()
        rows_ref[...] = table_ref[case]
        index = columns_of(rows_of(plan, table_ref, "send_one", case), sum(plan.room_one))
        put_pieces(select_rows(index, source_ref[...]), outs)

    outs = shapes([*plan.room_one, count], width)
    outs += [pltpu.VMEM(plan.table.shape[1:], F32), pltpu.SMEM((8,), I32)]
    outs += [pltpu.SMEM((1,), I32)] * 3
    scratch = [pltpu.SMEM((2,), I32), pltpu.VMEM(tokens.shape, BF16), pltpu.VMEM(plan.table.shape, F32)]
    got = call(body, outs, [shifts, tokens, plan.table], [HBM] * 3, scratch, 3, 1 << 28, 1 << 20)
    sent, (source, rows, flags, one, two, three) = got[:kinds], got[kinds:]
    return sent, source, rows, flags, one[0], two[0], three[0]


def before_fine(flags, regions, tokens, table, weights, plan, rows, cols):
    _, lat, lon = regions.shape
    width = tokens.shape[1]
    flat_regions = regions.reshape(2 * lat, lon)
    fine, coarse = windowed(rows, cols), natural(rows // 2, cols // 2)

    def lanes(places, scale, is_fine):
        places = np.asarray([(l, scale * r, scale * c, is_fine) for l, r, c in places], np.float32)
        return np.pad(places, ((0, -len(places) % 128), (0, 0))).T.reshape(4, -1, 128)

    places = np.concatenate([lanes(fine, 1, 1), lanes(coarse, 2, 0)], axis=1)
    lines = places.shape[1]

    def body(flags_ref, rows_ref, tokens_ref, regions_hbm, places_hbm, *refs):
        weights_hbm, refs = refs[: len(weights)], refs[len(weights) :]
        id_ref, x_ref, *refs = refs
        weight_refs, (regions_ref, places_ref, sems) = refs[: len(weights)], refs[len(weights) :]
        start = Copies(sems)
        waits = [start(regions_hbm, regions_ref), start(places_hbm, places_ref)]
        later = [start(src, dst) for src, dst in zip(weights_hbm, weight_refs)]
        for copy in waits:
            copy.wait()
        a = flags_ref[1].astype(F32)
        big_a = 2.0 * flags_ref[2].astype(F32)
        is_fine = places_ref[3]
        d = is_fine * a + (1.0 - is_fine) * big_a
        row = places_ref[1] + d + (lax.axis_index("lat") * rows).astype(F32)
        col = places_ref[2] + 2.0 * d + (lax.axis_index("lon") * cols).astype(F32)
        wrapped = jnp.where((row < 0) | (row >= lat), 4.0, 0.0)
        row = jnp.where(row < 0, row + lat, jnp.where(row >= lat, row - lat, row))
        col = jnp.where(col < 0, col + lon, jnp.where(col >= lon, col - lon, col))
        row = row + places_ref[0] * lat

        def along(values):
            return jnp.concatenate([values[n : n + 1] for n in range(lines)], axis=1)

        line = lax.broadcasted_iota(I32, (2 * lat, 1), 0).astype(F32)
        pick = jnp.where(line == along(row), 1.0, 0.0).astype(BF16)
        known = regions_ref[...].astype(F32).astype(BF16)
        picked = lax.dot_general(known, pick, TN, preferred_element_type=F32)
        line = lax.broadcasted_iota(I32, (lon, 1), 0).astype(F32)
        ids = jnp.sum(jnp.where(line == along(col), picked, 0.0), axis=0, keepdims=True) + along(wrapped)
        for n in range(lines):
            id_ref[n : n + 1, :] = ids[:, n * 128 : (n + 1) * 128]
        take = columns_of(rows_of(plan, rows_ref, "take_one"), len(fine))
        x_ref[...] = select_rows(take, tokens_ref[...]).astype(BF16)
        for copy in later:
            copy.wait()

    outs = [pltpu.VMEM((lines, 128), F32)] + shapes([len(fine)], width)
    outs += [pltpu.VMEM(w.shape, BF16) for w in weights]
    scratch = [pltpu.VMEM(flat_regions.shape, I32), pltpu.VMEM(places.shape, F32)]
    args = [flags, table, tokens, flat_regions, places, *weights]
    in_specs = [SMEM, VMEM, VMEM] + [HBM] * (2 + len(weights))
    ids, x, *weights = call(body, outs, args, in_specs, scratch, 2 + len(weights), 1 << 28, 4 << 20)
    return ids, x, weights


def id_columns(lines, count):
    lane = lax.broadcasted_iota(I32, (1, 128), 1).astype(F32)
    return jnp.where(columns_of(lines, count) == lane, 1.0, 0.0).astype(BF16)


def before_coarse(flags, fine, table, weight, plan):
    own, width = fine.shape
    half = 5 * weight.shape[0] // 16

    def body(flags_ref, rows_ref, fine_ref, weight_hbm, x_ref, part_hbm, home_ref, weight_ref, part_ref, sems):
        start = Copies(sems)
        later = start(weight_hbm.at[pl.ds(0, half)], weight_ref)
        take = columns_of(rows_of(plan, rows_ref, "fine_out"), own)
        part_ref[...] = select_rows(take, fine_ref[...]).astype(BF16)
        leave = start(part_ref, part_hbm)
        take = columns_of(rows_of(plan, rows_ref, "take_two"), own)
        x_ref[...] = select_rows(take, fine_ref[...]).astype(BF16)

        @pl.when(needs_fine(flags_ref, plan))
        def _():
            index = columns_of(rows_of(plan, rows_ref, "send_four"), sum(plan.room_four))
            home_ref[...] = select_rows(index, fine_ref[...]).astype(BF16)

        leave.wait()
        later.wait()

    outs = shapes([own], width) + shapes([own], width, pltpu.HBM)
    outs += shapes([sum(plan.room_four)], width) + shapes([half], weight.shape[1])
    scratch = [pltpu.VMEM(fine.shape, BF16)]
    args = [flags, table, fine, weight]
    return call(body, outs, args, [SMEM, VMEM, VMEM, HBM], scratch, 2, 1 << 28, 4 << 20)


def needs_fine(flags_ref, plan):
    with_fine = [n for n, sizes in enumerate(plan.four) if sum(sizes)]
    return functools.reduce(jnp.logical_or, [flags_ref[0] == n for n in with_fine])


def fine_level(x_own, source, ids, w_qkv, w_proj, rows, plan):
    count, width = x_own.shape
    inner = w_proj.shape[0]

    def body(own_ref, source_ref, ids_ref, qkv_w_ref, proj_w_hbm, rows_ref, out_ref, *refs):
        *piece_outs, x_ref, qkv_ref, id_ref, proj_w_ref, sems = refs
        proj_w = Copies(sems)(proj_w_hbm, proj_w_ref)
        id_ref[...] = id_columns(ids_ref[: -(-count // 128), :], count)
        take = columns_of(rows_of(plan, rows_ref, "take_one"), count) - float(count)
        x = own_ref[...].astype(F32) + select_rows(take, source_ref[...])
        x_ref[...] = x
        normed = layer_norm(x).astype(BF16)
        qkv_ref[...] = jnp.dot(normed, qkv_w_ref[...], preferred_element_type=F32).astype(BF16)

        def finish(w, out):
            at = slice(w * TOK, (w + 1) * TOK)
            out = jnp.dot(out, proj_w_ref[...], preferred_element_type=F32)
            out_ref[at, :] = (x_ref[at, :] + out).astype(BF16)

        proj_w.wait()
        attend_windows(
            lambda w, at: qkv_ref[w * TOK : (w + 1) * TOK, at : at + 128],
            lambda w: id_ref[w * TOK : (w + 1) * TOK, :],
            count // TOK,
            inner,
            finish,
        )
        index = columns_of(rows_of(plan, rows_ref, "send_two"), sum(plan.room_two))
        put_pieces(select_rows(index, out_ref[...]), piece_outs)

    outs = shapes([count, *plan.room_two], width)
    scratch = [
        pltpu.VMEM((count, width), F32),
        pltpu.VMEM((count, 3 * inner), BF16),
        pltpu.VMEM((count, 128), BF16),
        pltpu.VMEM(w_proj.shape, BF16),
    ]
    args = [x_own, source, ids, w_qkv, w_proj, rows]
    out, *sent = call(body, outs, args, [VMEM] * 4 + [HBM, VMEM], scratch, 1, 3 << 30, 6 << 20, 14)
    return out, sent


def coarse_level(flags, home, x_own, source, ids, merge_first, w_merge, w_qkv, w_proj, rows, plan):
    depth, width = w_merge.shape
    own, half = x_own.shape
    count = own // 4
    inner = w_proj.shape[0]

    def body(
        flags_ref, merge_hbm, qkv_w_hbm, proj_w_hbm, home_ref, own_ref, source_ref, ids_ref, first_ref, rows_ref, *refs
    ):
        out_ref, *piece_outs = refs[:4]
        qkv_ref, id_ref, merge_ref, qkv_w_ref, proj_w_ref, sems = refs[4:]
        start = Copies(sems)
        def bring(src, dst):
            cuts = [(at, min(half, src.shape[0] - at)) for at in range(0, src.shape[0], half)]
            return [(at, size, start(src.at[pl.ds(at, size)], dst.at[pl.ds(at, size)])) for at, size in cuts]

        def product(x, ref, copies):
            parts = []
            for at, size, copy in copies:
                copy.wait()
                parts.append(jnp.dot(x[:, at : at + size], ref[at : at + size, :], preferred_element_type=F32))
            return functools.reduce(jnp.add, parts)

        here = first_ref.shape[0]
        merge_w = bring(merge_hbm.at[pl.ds(here, depth - here)], merge_ref)
        qkv_w = bring(qkv_w_hbm, qkv_w_ref)
        proj_w = start(proj_w_hbm, proj_w_ref)
        id_ref[...] = id_columns(ids_ref[-(-own // 128) :, :], count)
        take = columns_of(rows_of(plan, rows_ref, "take_two"), 4 * count) - float(own)
        x = own_ref[...].astype(F32) + select_rows(take, source_ref[...])
        x = jnp.concatenate([x[n * count : (n + 1) * count] for n in range(4)], axis=1)
        stacked = layer_norm(x).astype(BF16)
        merged = jnp.dot(stacked[:, :here], first_ref[...], preferred_element_type=F32)
        merged = (merged + product(stacked[:, here:], merge_ref, merge_w)).astype(BF16).astype(F32)
        normed = layer_norm(merged).astype(BF16)
        qkv_ref[...] = product(normed, qkv_w_ref, qkv_w).astype(BF16)
        proj_w.wait()

        def finish(w, out):
            out = jnp.dot(out, proj_w_ref[...], preferred_element_type=F32)
            out_ref[...] = (merged + out).astype(BF16)

        attend_windows(lambda w, at: qkv_ref[:, at : at + 128], lambda w: id_ref[...], 1, inner, finish)
        sent = select_rows(columns_of(rows_of(plan, rows_ref, "send_three"), sum(plan.room_three)), out_ref[...])
        sent = sent.astype(BF16)
        for n, sizes in enumerate(plan.three):

            @pl.when(flags_ref[0] == n)
            def _():
                at = 0
                for ref, size, space in zip(piece_outs, sizes, plan.room_three):
                    ref[:size, :] = sent[at : at + size, :half]
                    ref[size : 2 * size, :] = sent[at : at + size, half:]
                    at += space

        for n, fine_sizes in enumerate(plan.four):
            if sum(fine_sizes):

                @pl.when(flags_ref[0] == n)
                def _():
                    at = 0
                    for ref, size, more, space in zip(piece_outs, plan.three[n], fine_sizes, plan.room_four):
                        ref[2 * size : 2 * size + more, :] = home_ref[at : at + more, :]
                        at += space

    most = [max(2 * three[k] + four[k] for three, four in zip(plan.three, plan.four)) for k in range(3)]
    outs = shapes([count], width) + shapes(most, half)
    scratch = [pltpu.VMEM((count, 3 * inner), BF16)]
    shapes_in = [(count, 128), (depth - merge_first.shape[0], width), w_qkv.shape, w_proj.shape]
    scratch += [pltpu.VMEM(shape, BF16) for shape in shapes_in]
    args = [flags, w_merge, w_qkv, w_proj, home, x_own, source, ids, merge_first, rows]
    in_specs = [SMEM] + [HBM] * 3 + [VMEM] * (len(args) - 4)
    copies = depth // half + width // half + 3
    out, *sent = call(body, outs, args, in_specs, scratch, copies, 3 << 30, 12 << 20, 24)
    return out, sent


def fine_output(part, source, rows, plan, block_rows, block_cols, partial):
    own, width = part.shape

    def body(part_hbm, source_ref, rows_ref, out_ref, part_ref, stage_ref, sems):
        start = Copies(sems)
        cuts = [pl.ds(at, TOK) for at in range(0, own, TOK)]
        held = [start(part_hbm.at[cut], part_ref.at[cut]) for cut in cuts]
        take = columns_of(rows_of(plan, rows_ref, "fine_out"), own) - float(own)
        leave = []
        for n, (cut, copy) in enumerate(zip(cuts, held)):
            got = select_rows(take[n * TOK : (n + 1) * TOK], source_ref[...])
            copy.wait()
            out = part_ref[cut, :].astype(F32) + got
            if partial:
                out_ref[cut, :] = out.astype(BF16)
            else:
                lines = TOK // block_cols
                layer, line = divmod(n * lines, block_rows)
                there = (layer, pl.ds(line, lines))
                stage_ref[there] = out.reshape(lines, block_cols, width).astype(BF16)
                leave.append(start(stage_ref.at[there], out_ref.at[there]))
        for copy in leave:
            copy.wait()

    shape = (2, block_rows, block_cols, width)
    outs = shapes([own], width) if partial else [pltpu.HBM(shape, BF16)]
    scratch = [pltpu.VMEM(part.shape, BF16), pltpu.VMEM(shape, BF16)]
    return call(body, outs, [part, source, rows], [HBM, VMEM, VMEM], scratch, 2 * own // TOK, 1 << 30, 4 << 20)[0]


def coarse_output(coarse, got, rows, which, plan, block_rows, block_cols, part=None):
    own, width = coarse.shape
    half = width // 2
    sizes, more = plan.three[which], plan.four[which]
    parts = [] if part is None else [part]

    def padded(parts, sizes, room):
        out = []
        for value, size, space in zip(parts, sizes, room):
            out.append(value)
            if size < space:
                out.append(jnp.zeros((space - size, value.shape[1]), F32))
        return out

    def body(coarse_ref, *refs):
        got_refs, refs = refs[:3], refs[3:]
        part_refs, (rows_ref, out_ref, *fine_outs, _) = refs[: len(parts)], refs[len(parts) :]
        got = [ref[...].astype(F32) for ref in got_refs]
        back = [jnp.concatenate([x[:size], x[size : 2 * size]], axis=1) for x, size in zip(got, sizes)]
        source = stack_rows([coarse_ref[...].astype(F32)] + padded(back, sizes, plan.room_three))
        out = select_rows(columns_of(rows_of(plan, rows_ref, "coarse_out"), own), source.astype(BF16)).astype(BF16)
        for n in range(own // 2):
            out_ref[n // block_cols, n % block_cols] = out[2 * n : 2 * n + 2]
        for part_ref, fine_ref in zip(part_refs, fine_outs):
            fine = stack_rows(padded([x[2 * size :] for x, size in zip(got, sizes)], more, plan.room_four))
            base = part_ref.shape[0] + sum(plan.room_two)
            take = columns_of(rows_of(plan, rows_ref, "fine_out"), part_ref.shape[0]) - float(base)
            out = part_ref[...].astype(F32) + select_rows(take, fine.astype(BF16))
            fine_ref[...] = out.reshape(fine_ref.shape).astype(BF16)

    outs = [jax.ShapeDtypeStruct((block_rows, block_cols, 2, width), BF16)]
    outs += [jax.ShapeDtypeStruct((2, 2 * block_rows, 2 * block_cols, half), BF16) for _ in parts]
    args = [coarse, *got, *parts, rows]
    out, *fine = call(body, outs, args, [VMEM] * len(args), [], 1, 1 << 28, 1 << 20)
    return out.transpose(2, 0, 1, 3), *fine


def on_device(tokens, regions, shifts, fine_qkv, fine_proj, merge_weight, coarse_qkv, coarse_proj):
    _, rows, cols, _ = tokens.shape
    plan = Plan(rows, cols)

    def first(which, sign, sent, *args):
        got = exchange(sent, plan.one[which], sign)
        return lay(got, plan.room_one), before_fine(*args, plan, rows, cols)

    def second(which, sign, sent, *args):
        got = exchange(sent, plan.two[which], sign)
        return lay(got, plan.room_two), before_coarse(*args, plan)

    def third(which, sign, sent, part, source, coarse, table):
        sizes = [2 * n + m for n, m in zip(plan.three[which], plan.four[which])]
        got = exchange(sent, sizes, sign)
        partial = sum(plan.four[which]) > 0
        fine_out = fine_output(part, source, table, plan, rows, cols, partial)
        place = (table, which, plan, rows // 2, cols // 2)
        if partial:
            coarse_out, fine_out = coarse_output(coarse, got, *place, part=fine_out)
        else:
            (coarse_out,) = coarse_output(coarse, got, *place)
        return fine_out, coarse_out

    def branches(stage, pairs):
        return [functools.partial(stage, which, sign) for which, sign in pairs]

    sent, source, table, flags, one, two, three = first_pieces(shifts, tokens, plan)
    got, (ids, x, weights) = choose(
        one, branches(first, plan.one_branches), sent, flags, regions, source, table, [fine_qkv]
    )
    fine, sent = fine_level(x, got, ids, *weights, fine_proj, table, plan)
    got, (x, part, home, merge_first) = choose(
        two, branches(second, plan.two_branches), sent, flags, fine, table, merge_weight
    )
    coarse, sent = coarse_level(
        flags, home, x, got, ids, merge_first, merge_weight, coarse_qkv, coarse_proj, table, plan
    )
    return choose(three, branches(third, plan.three_branches), sent, part, got, coarse, table)


def solution(mesh):
    return jax.shard_map(
        on_device,
        mesh=mesh,
        in_specs=(P(None, "lat", "lon", None), P(), P(), P(), P(), P(), P(), P()),
        out_specs=(P(None, "lat", "lon", None), P(None, "lat", "lon", None)),
        check_vma=False,
    )
```

```python
import functools

import jax
import jax.numpy as jnp
import numpy as np
from jax import lax
from jax.experimental import pallas as pl
from jax.experimental.pallas import tpu as pltpu
from jax.sharding import PartitionSpec as P

HD = 32
WH = 6
WW = 12
TOK = 2 * WH * WW
EPS = 1e-05
BIG = 1e30
SCALE = float(np.log2(np.e) / np.sqrt(HD))

NT = (((1,), (1,)), ((), ()))
TN = (((0,), (0,)), ((), ()))
F32 = jnp.float32
BF16 = jnp.bfloat16
I32 = jnp.int32

PAIRS = [(WH - 1, t) for t in range(1, WH)] + [(t, WH - 1) for t in range(1, WH - 1)]


def up16(count):
    return -(-count // 16) * 16


def natural(rows, cols):
    return [(l, r, c) for l in range(2) for r in range(rows) for c in range(cols)]


def windowed(rows, cols):
    return [
        (l, wr * WH + r, wc * WW + c)
        for wr in range(rows // WH)
        for wc in range(cols // WW)
        for l in range(2)
        for r in range(WH)
        for c in range(WW)
    ]


def moved(order, d):
    return [(l, r + d, c + 2 * d) for l, r, c in order]


def exchange_places(held, wanted, rows, cols, sign):
    at = {place: n for n, place in enumerate(held)}
    found = []
    for dr, dc in ((sign, 0), (0, sign), (sign, sign)):
        numbers, places = [], []
        for l, r, c in sorted(set(wanted) - set(held)):
            n = at.get((l, r - dr * rows, c - dc * cols))
            if n is not None:
                numbers.append(n)
                places.append((l, r, c))
        found.append((numbers, places))
    return found


def offsets(t0, t1):
    a = t0 if t0 <= 2 else t0 - WH
    big_a = t1 if t1 <= 2 else t1 - WH
    ahead = 1 if 2 * big_a > a or 2 * big_a - a == 0 and a < 0 else -1
    return a, big_a, ahead


def classes_of(needs, slack):
    rounded = [tuple(-(-size // 8) * 8 for size in need) for need in needs]
    heavy = [sum(need[1:3]) * 2 + sum(need[4:]) for need in rounded]
    limits = []
    for size in sorted(set(heavy)):
        if not limits or size > limits[-1][0] * slack:
            limits.append([size, size])
        limits[-1][1] = size
    which = [next(n for n, limit in enumerate(limits) if size <= limit[1]) for size in heavy]
    sizes = [
        [max(need[k] for need, w in zip(rounded, which) if w == n) for k in range(len(needs[0]))]
        for n in range(len(limits))
    ]
    return sizes, which


def rooms(sizes):
    return [up16(max(size[k] for size in sizes)) for k in range(len(sizes[0]))]


class Plan:
    def __init__(self, rows, cols):
        crows, ccols = rows // 2, cols // 2
        block, cblock = natural(rows, cols), natural(crows, ccols)
        cases = []
        for t0, t1 in PAIRS:
            a, big_a, ahead = offsets(t0, t1)
            fine = moved(windowed(rows, cols), a)
            coarse = moved(cblock, big_a)
            quarters = [
                (l, 2 * r + dr, 2 * c + dc)
                for dr, dc in ((0, 0), (1, 0), (0, 1), (1, 1))
                for l, r, c in coarse
            ]
            come = 1 if a > 0 else -1
            one = exchange_places(block, fine, rows, cols, come)
            home = [p for p in block if p not in set(fine)]
            wanted = quarters + (home if come == -ahead else [])
            two = exchange_places(fine, wanted, rows, cols, ahead)
            back = 1 if big_a < 0 else -1
            three = exchange_places(coarse, cblock, crows, ccols, back)
            got = set(fine).union(*[places for _, places in two])
            four = exchange_places(fine, [p for p in block if p not in got], rows, cols, back)
            cases.append((come, ahead, back, fine, coarse, quarters, one, two, three, four))

        def needs(which):
            return [[len(numbers) for numbers, _ in case[which]] for case in cases]

        self.one, one_class = classes_of(needs(6), 1.15)
        self.two, two_class = classes_of(needs(7), 1.15)
        sizes, three_class = classes_of([three + four for three, four in zip(needs(8), needs(9))], 1.0)
        self.three, self.four = [size[:3] for size in sizes], [size[3:] for size in sizes]
        self.room_one, self.room_two = rooms(self.one), rooms(self.two)
        self.room_three, self.room_four = rooms(self.three), rooms(self.four)

        def branches(which_class, direction):
            pairs = [(n, case[direction]) for n, case in zip(which_class, cases)]
            found = sorted(set(pairs))
            return found, [found.index(pair) for pair in pairs]

        self.one_branches, one_at = branches(one_class, 0)
        self.two_branches, two_at = branches(two_class, 1)
        self.three_branches, three_at = branches(three_class, 2)
        self.flags = dict(
            three_class=three_class,
            one_at=one_at, two_at=two_at, three_at=three_at,
            a=[offsets(*pair)[0] for pair in PAIRS], big_a=[offsets(*pair)[1] for pair in PAIRS],
        )

        found = {}
        for n, (come, ahead, back, fine, coarse, quarters, one, two, three, four) in enumerate(cases):

            def send(exchanged, room):
                return [n for (numbers, _), size in zip(exchanged, room) for n in numbers + [-1] * (size - len(numbers))]

            def source(held, *exchanges):
                places = list(held)
                for exchanged, room in exchanges:
                    for (_, got), size in zip(exchanged, room):
                        places += got + [None] * (size - len(got))
                return {p: n for n, p in enumerate(places) if p is not None}

            first, second = source(block, (one, self.room_one)), source(fine, (two, self.room_two))
            third = source(coarse, (three, self.room_three))
            last = source(fine, (two, self.room_two), (four, self.room_four))
            out = [(l, r, c) for r in range(crows) for c in range(ccols) for l in range(2)]
            rows_of = dict(
                send_one=send(one, self.room_one),
                take_one=[first[p] for p in fine],
                send_two=send(two, self.room_two),
                take_two=[second[p] for p in quarters],
                send_three=send(three, self.room_three),
                send_four=send(four, self.room_four),
                fine_out=[last[p] for p in block],
                coarse_out=[third[p] for p in out],
            )
            for name, row in rows_of.items():
                found.setdefault(name, []).append(row)
        parts, self.at, top = [], {}, 0
        for name, lists in found.items():
            length = -(-max(len(row) for row in lists) // 128)
            part = np.full((len(PAIRS), length * 128), -1, np.float32)
            for n, row in enumerate(lists):
                part[n, : len(row)] = row
            parts.append(part.reshape(len(PAIRS), length, 128))
            self.at[name] = (top, length)
            top += length
        parts.append(np.zeros((len(PAIRS), -top % 8, 128), np.float32))
        self.table = np.concatenate(parts, axis=1)


def case_of(shifts_ref):
    t0, t1 = shifts_ref[0], shifts_ref[1]
    return jnp.where(t0 == WH - 1, t1 - 1, t0 + WH - 2)


def lookup(values, case):
    out = jnp.int32(values[0])
    for n, value in enumerate(values[1:], 1):
        out = jnp.where(case == n, value, out)
    return out


def columns_of(rows, count):
    parts = [jnp.broadcast_to(rows[j : j + 1], (128, 128)).T for j in range(-(-count // 128))]
    return stack_rows(parts)[:count]


def select_rows(index, source):
    lane = lax.broadcasted_iota(I32, (1, 128), 1).astype(F32)
    size = source.shape[0]
    pick = [jnp.where(index == lane + float(at), 1.0, 0.0).astype(BF16) for at in range(0, size, 128)]
    pick = jnp.concatenate(pick, axis=1)[:, :size]
    return jnp.dot(pick, source, preferred_element_type=F32)


def stack_rows(parts):
    return parts[0] if len(parts) == 1 else jnp.concatenate(parts, axis=0)


def layer_norm(values):
    center = jnp.mean(values, axis=-1, keepdims=True)
    values = values - center
    spread = jnp.mean(values * values, axis=-1, keepdims=True)
    return values * lax.rsqrt(spread + EPS)


def attend_windows(qkv_of, id_of, windows, inner, finish):
    lane = lax.broadcasted_iota(I32, (1, 128), 1)
    forbid = jnp.where(lane < 8, BIG, 0.0).astype(BF16)
    groups = inner // 128
    units = [(w, g) for w in range(windows) for g in range(groups)]
    scores, weights, outs = {}, {}, {}

    def score(w, g):
        key_id = id_of(w)
        not_id = (key_id - 1).astype(BF16) * forbid
        q = qkv_of(w, g * 128)
        keys = jnp.concatenate([qkv_of(w, inner + g * 128), key_id], axis=1)
        queries = []
        for h in range(4):
            mine = jnp.where((lane >= h * HD) & (lane < (h + 1) * HD), 1.0, 0.0).astype(BF16)
            queries.append(jnp.concatenate([q * mine, not_id], axis=1))
        scores[w, g] = lax.dot_general(stack_rows(queries), keys, NT, preferred_element_type=F32)

    def soften(w, g):
        s = scores.pop((w, g))
        weights[w, g] = jnp.exp2((s - jnp.max(s, axis=1, keepdims=True)) * SCALE).astype(BF16)

    def gather(w, g):
        v = qkv_of(w, 2 * inner + g * 128)
        values = jnp.concatenate([v, jnp.ones_like(v)], axis=1)
        out = jnp.dot(weights.pop((w, g)), values, preferred_element_type=F32)
        picked, total = out[:TOK, :128], out[:TOK, 128:]
        for h in range(1, 4):
            rows = slice(h * TOK, (h + 1) * TOK)
            picked = jnp.where(lane < h * HD, picked, out[rows, :128])
            total = jnp.where(lane < h * HD, total, out[rows, 128:])
        outs[w, g] = (picked / total).astype(BF16)
        if g == groups - 1:
            finish(w, jnp.concatenate([outs.pop((w, k)) for k in range(groups)], axis=1))

    for n in range(len(units) + 2):
        if n < len(units):
            score(*units[n])
        if 0 <= n - 1 < len(units):
            soften(*units[n - 1])
        if 0 <= n - 2 < len(units):
            gather(*units[n - 2])


ANY = pl.BlockSpec(memory_space=pl.ANY)
HBM = pl.BlockSpec(memory_space=pltpu.HBM)
VMEM = pl.BlockSpec(memory_space=pltpu.VMEM)
SMEM = pl.BlockSpec(memory_space=pltpu.SMEM)


def call(body, outs, args, in_specs, scratch, copies, flops, moved_bytes, vmem=8):
    args = [
        pltpu.with_memory_space_constraint(arg, spec.memory_space) for arg, spec in zip(args, in_specs, strict=True)
    ]
    spaces = [getattr(out, "memory_space", pltpu.SMEM if out.dtype == I32 else pltpu.VMEM) for out in outs]
    out_specs = [pl.BlockSpec(memory_space=space) for space in spaces]
    return pl.pallas_call(
        body,
        out_shape=outs,
        in_specs=in_specs,
        out_specs=out_specs,
        scratch_shapes=list(scratch) + [pltpu.SemaphoreType.DMA((copies,))],
        compiler_params=pltpu.CompilerParams(vmem_limit_bytes=vmem << 20),
        cost_estimate=pl.CostEstimate(flops=flops, bytes_accessed=moved_bytes, transcendentals=0),
    )(*args)


def shapes(sizes, width, space=pltpu.VMEM):
    return [space((n, width), BF16) for n in sizes]


class Copies:
    def __init__(self, sems):
        self.sems, self.used = sems, 0

    def __call__(self, src, dst):
        copy = pltpu.make_async_copy(src, dst, self.sems.at[self.used])
        self.used += 1
        copy.start()
        return copy


def lay(pieces, room):
    width = pieces[0].shape[1]

    def body(*refs):
        out_ref = refs[len(pieces)]
        at = 0
        for ref, space in zip(refs, room):
            rows = ref.shape[0]
            out_ref[at : at + rows, :] = ref[...]
            if rows < space:
                out_ref[at + rows : at + space, :] = jnp.zeros((space - rows, width), BF16)
            at += space

    return call(body, shapes([sum(room)], width), pieces, [VMEM] * 3, [], 1, 0, 1 << 18)[0]


def flat(ref):
    layers, rows, cols, width = ref.shape
    return ref[...].astype(F32).reshape(layers * rows * cols, width).astype(BF16)


def put_pieces(value, refs):
    at = 0
    for ref in refs:
        ref[...] = value[at : at + ref.shape[0]].astype(BF16)
        at += ref.shape[0]


def rows_of(plan, table_ref, name, *lead):
    top, length = plan.at[name]
    return table_ref[(*lead, slice(top, top + length), slice(None))]


def exchange(pieces, sizes, sign):
    lat, lon = lax.axis_size("lat"), lax.axis_size("lon")
    row, col, both = [piece[:size] for piece, size in zip(pieces, sizes)]
    pairs = [((i + sign) % lat * lon + (j + sign) % lon, i * lon + j) for i in range(lat) for j in range(lon)]
    col = lax.ppermute(col, "lon", [((j + sign) % lon, j) for j in range(lon)])
    both = lax.ppermute(both, ("lat", "lon"), pairs)
    row = lax.ppermute(row, "lat", [((i + sign) % lat, i) for i in range(lat)])
    return [row, col, both]


def choose(index, branches, *args):
    flat_args, tree = jax.tree.flatten(args)
    out_trees = []

    def closed(branch):
        def run(*leaves):
            out, out_tree = jax.tree.flatten(branch(*jax.tree.unflatten(tree, leaves)))
            out_trees.append(out_tree)
            return out

        return jax.make_jaxpr(run)(*flat_args)

    out = lax.cond_p.bind(index, *flat_args, branches=tuple(closed(branch) for branch in branches))
    return jax.tree.unflatten(out_trees[0], out)


FLAGS = ("three_class", "a", "big_a")


def first_pieces(shifts, tokens, plan):
    width = tokens.shape[-1]
    count = tokens.size // width
    kinds = 3

    def body(shifts_hbm, tokens_hbm, table_hbm, *refs):
        outs, refs = refs[:kinds], refs[kinds:]
        source_ref, rows_ref, flags_ref, *at_refs, shifts_ref, tokens_ref, table_ref, sems = refs
        start = Copies(sems)
        shift = start(shifts_hbm, shifts_ref)
        held = start(tokens_hbm, tokens_ref)
        table = start(table_hbm, table_ref)
        shift.wait()
        case = case_of(shifts_ref)
        for ref, name in zip(at_refs, ("one_at", "two_at", "three_at")):
            ref[0] = lookup(plan.flags[name], case)
        for n, name in enumerate(FLAGS):
            flags_ref[n] = lookup(plan.flags[name], case)
        held.wait()
        source_ref[...] = flat(tokens_ref)
        table.wait()
        rows_ref[...] = table_ref[case]
        index = columns_of(rows_of(plan, table_ref, "send_one", case), sum(plan.room_one))
        put_pieces(select_rows(index, source_ref[...]), outs)

    outs = shapes([*plan.room_one, count], width)
    outs += [pltpu.VMEM(plan.table.shape[1:], F32), pltpu.SMEM((8,), I32)]
    outs += [pltpu.SMEM((1,), I32)] * 3
    scratch = [pltpu.SMEM((2,), I32), pltpu.VMEM(tokens.shape, BF16), pltpu.VMEM(plan.table.shape, F32)]
    got = call(body, outs, [shifts, tokens, plan.table], [HBM] * 3, scratch, 3, 1 << 28, 1 << 20)
    sent, (source, rows, flags, one, two, three) = got[:kinds], got[kinds:]
    return sent, source, rows, flags, one[0], two[0], three[0]


def before_fine(flags, regions, tokens, table, weights, plan, rows, cols):
    _, lat, lon = regions.shape
    width = tokens.shape[1]
    flat_regions = regions.reshape(2 * lat, lon)
    fine, coarse = windowed(rows, cols), natural(rows // 2, cols // 2)

    def lanes(places, scale, is_fine):
        places = np.asarray([(l, scale * r, scale * c, is_fine) for l, r, c in places], np.float32)
        return np.pad(places, ((0, -len(places) % 128), (0, 0))).T.reshape(4, -1, 128)

    places = np.concatenate([lanes(fine, 1, 1), lanes(coarse, 2, 0)], axis=1)
    lines = places.shape[1]

    def body(flags_ref, rows_ref, tokens_ref, regions_hbm, places_hbm, *refs):
        weights_hbm, refs = refs[: len(weights)], refs[len(weights) :]
        id_ref, x_ref, *refs = refs
        weight_refs, (regions_ref, places_ref, sems) = refs[: len(weights)], refs[len(weights) :]
        start = Copies(sems)
        waits = [start(regions_hbm, regions_ref), start(places_hbm, places_ref)]
        later = [
            start(src.at[:, pl.ds(0, dst.shape[1])], dst) for src, dst in zip(weights_hbm, weight_refs)
        ]
        for copy in waits:
            copy.wait()
        a = flags_ref[1].astype(F32)
        big_a = 2.0 * flags_ref[2].astype(F32)
        is_fine = places_ref[3]
        d = is_fine * a + (1.0 - is_fine) * big_a
        row = places_ref[1] + d + (lax.axis_index("lat") * rows).astype(F32)
        col = places_ref[2] + 2.0 * d + (lax.axis_index("lon") * cols).astype(F32)
        wrapped = jnp.where((row < 0) | (row >= lat), 4.0, 0.0)
        row = jnp.where(row < 0, row + lat, jnp.where(row >= lat, row - lat, row))
        col = jnp.where(col < 0, col + lon, jnp.where(col >= lon, col - lon, col))
        row = row + places_ref[0] * lat

        def along(values):
            return jnp.concatenate([values[n : n + 1] for n in range(lines)], axis=1)

        line = lax.broadcasted_iota(I32, (2 * lat, 1), 0).astype(F32)
        pick = jnp.where(line == along(row), 1.0, 0.0).astype(BF16)
        known = regions_ref[...].astype(F32).astype(BF16)
        picked = lax.dot_general(known, pick, TN, preferred_element_type=F32)
        line = lax.broadcasted_iota(I32, (lon, 1), 0).astype(F32)
        ids = jnp.sum(jnp.where(line == along(col), picked, 0.0), axis=0, keepdims=True) + along(wrapped)
        for n in range(lines):
            id_ref[n : n + 1, :] = ids[:, n * 128 : (n + 1) * 128]
        take = columns_of(rows_of(plan, rows_ref, "take_one"), len(fine))
        x_ref[...] = select_rows(take, tokens_ref[...]).astype(BF16)
        for copy in later:
            copy.wait()

    outs = [pltpu.VMEM((lines, 128), F32)] + shapes([len(fine)], width)
    outs += [pltpu.VMEM((w.shape[0], min(w.shape[1], 2 * weights[1].shape[0])), BF16) for w in weights]
    scratch = [pltpu.VMEM(flat_regions.shape, I32), pltpu.VMEM(places.shape, F32)]
    args = [flags, table, tokens, flat_regions, places, *weights]
    in_specs = [SMEM, VMEM, VMEM] + [HBM] * (2 + len(weights))
    ids, x, *weights = call(body, outs, args, in_specs, scratch, 2 + len(weights), 1 << 28, 4 << 20)
    return ids, x, weights


def id_columns(lines, count):
    lane = lax.broadcasted_iota(I32, (1, 128), 1).astype(F32)
    return jnp.where(columns_of(lines, count) == lane, 1.0, 0.0).astype(BF16)


def before_coarse(flags, fine, table, weight, plan):
    own, width = fine.shape
    half = 5 * weight.shape[0] // 16

    def body(flags_ref, rows_ref, fine_ref, weight_hbm, x_ref, part_hbm, home_ref, weight_ref, part_ref, sems):
        start = Copies(sems)
        later = start(weight_hbm.at[pl.ds(0, half)], weight_ref)
        take = columns_of(rows_of(plan, rows_ref, "fine_out"), own)
        part_ref[...] = select_rows(take, fine_ref[...]).astype(BF16)
        leave = start(part_ref, part_hbm)
        take = columns_of(rows_of(plan, rows_ref, "take_two"), own)
        x_ref[...] = select_rows(take, fine_ref[...]).astype(BF16)

        @pl.when(needs_fine(flags_ref, plan))
        def _():
            index = columns_of(rows_of(plan, rows_ref, "send_four"), sum(plan.room_four))
            home_ref[...] = select_rows(index, fine_ref[...]).astype(BF16)

        leave.wait()
        later.wait()

    outs = shapes([own], width) + shapes([own], width, pltpu.HBM)
    outs += shapes([sum(plan.room_four)], width) + shapes([half], weight.shape[1])
    scratch = [pltpu.VMEM(fine.shape, BF16)]
    args = [flags, table, fine, weight]
    return call(body, outs, args, [SMEM, VMEM, VMEM, HBM], scratch, 2, 1 << 28, 4 << 20)


def needs_fine(flags_ref, plan):
    with_fine = [n for n, sizes in enumerate(plan.four) if sum(sizes)]
    return functools.reduce(jnp.logical_or, [flags_ref[0] == n for n in with_fine])


def fine_level(x_own, source, ids, w_qk, w_proj, w_qkv, rows, plan):
    count, width = x_own.shape
    inner = w_proj.shape[0]

    def body(own_ref, source_ref, ids_ref, qk_w_ref, proj_w_ref, qkv_w_hbm, rows_ref, out_ref, *refs):
        *piece_outs, x_ref, qkv_ref, id_ref, v_w_ref, sems = refs
        v_w = Copies(sems)(qkv_w_hbm.at[:, pl.ds(2 * inner, inner)], v_w_ref)
        id_ref[...] = id_columns(ids_ref[: -(-count // 128), :], count)
        take = columns_of(rows_of(plan, rows_ref, "take_one"), count) - float(count)
        x = own_ref[...].astype(F32) + select_rows(take, source_ref[...])
        x_ref[...] = x
        normed = layer_norm(x).astype(BF16)
        v_w.wait()
        qkv_ref[:, : 2 * inner] = jnp.dot(normed, qk_w_ref[...], preferred_element_type=F32).astype(BF16)
        qkv_ref[:, 2 * inner :] = jnp.dot(normed, v_w_ref[...], preferred_element_type=F32).astype(BF16)

        def finish(w, out):
            at = slice(w * TOK, (w + 1) * TOK)
            out = jnp.dot(out, proj_w_ref[...], preferred_element_type=F32)
            out_ref[at, :] = (x_ref[at, :] + out).astype(BF16)

        attend_windows(
            lambda w, at: qkv_ref[w * TOK : (w + 1) * TOK, at : at + 128],
            lambda w: id_ref[w * TOK : (w + 1) * TOK, :],
            count // TOK,
            inner,
            finish,
        )
        index = columns_of(rows_of(plan, rows_ref, "send_two"), sum(plan.room_two))
        put_pieces(select_rows(index, out_ref[...]), piece_outs)

    outs = shapes([count, *plan.room_two], width)
    scratch = [
        pltpu.VMEM((count, width), F32),
        pltpu.VMEM((count, 3 * inner), BF16),
        pltpu.VMEM((count, 128), BF16),
        pltpu.VMEM((width, inner), BF16),
    ]
    args = [x_own, source, ids, w_qk, w_proj, w_qkv, rows]
    out, *sent = call(body, outs, args, [VMEM] * 5 + [HBM, VMEM], scratch, 1, 3 << 30, 6 << 20, 14)
    return out, sent


def coarse_level(flags, home, x_own, source, ids, merge_first, w_merge, w_qkv, w_proj, rows, plan):
    depth, width = w_merge.shape
    own, half = x_own.shape
    count = own // 4
    inner = w_proj.shape[0]

    def body(
        flags_ref, merge_hbm, qkv_w_hbm, proj_w_hbm, home_ref, own_ref, source_ref, ids_ref, first_ref, rows_ref, *refs
    ):
        out_ref, *piece_outs = refs[:4]
        qkv_ref, id_ref, merge_ref, qkv_w_ref, proj_w_ref, sems = refs[4:]
        start = Copies(sems)
        here = first_ref.shape[0]
        merge_w = start(merge_hbm.at[pl.ds(here, depth - here)], merge_ref)
        qkv_w = start(qkv_w_hbm, qkv_w_ref)
        proj_w = start(proj_w_hbm, proj_w_ref)
        id_ref[...] = id_columns(ids_ref[-(-own // 128) :, :], count)
        take = columns_of(rows_of(plan, rows_ref, "take_two"), 4 * count) - float(own)
        x = own_ref[...].astype(F32) + select_rows(take, source_ref[...])
        x = jnp.concatenate([x[n * count : (n + 1) * count] for n in range(4)], axis=1)
        stacked = layer_norm(x).astype(BF16)
        merge_w.wait()
        merged = jnp.dot(stacked[:, :here], first_ref[...], preferred_element_type=F32)
        merged = merged + jnp.dot(stacked[:, here:], merge_ref[...], preferred_element_type=F32)
        merged = merged.astype(BF16).astype(F32)
        normed = layer_norm(merged).astype(BF16)
        qkv_w.wait()
        proj_w.wait()
        qkv_ref[...] = jnp.dot(normed, qkv_w_ref[...], preferred_element_type=F32).astype(BF16)

        def finish(w, out):
            out = jnp.dot(out, proj_w_ref[...], preferred_element_type=F32)
            out_ref[...] = (merged + out).astype(BF16)

        attend_windows(lambda w, at: qkv_ref[:, at : at + 128], lambda w: id_ref[...], 1, inner, finish)
        sent = select_rows(columns_of(rows_of(plan, rows_ref, "send_three"), sum(plan.room_three)), out_ref[...])
        sent = sent.astype(BF16)
        for n, sizes in enumerate(plan.three):

            @pl.when(flags_ref[0] == n)
            def _():
                at = 0
                for ref, size, space in zip(piece_outs, sizes, plan.room_three):
                    ref[:size, :] = sent[at : at + size, :half]
                    ref[size : 2 * size, :] = sent[at : at + size, half:]
                    at += space

        for n, fine_sizes in enumerate(plan.four):
            if sum(fine_sizes):

                @pl.when(flags_ref[0] == n)
                def _():
                    at = 0
                    for ref, size, more, space in zip(piece_outs, plan.three[n], fine_sizes, plan.room_four):
                        ref[2 * size : 2 * size + more, :] = home_ref[at : at + more, :]
                        at += space

    most = [max(2 * three[k] + four[k] for three, four in zip(plan.three, plan.four)) for k in range(3)]
    outs = shapes([count], width) + shapes(most, half)
    scratch = [pltpu.VMEM((count, 3 * inner), BF16)]
    shapes_in = [(count, 128), (depth - merge_first.shape[0], width), w_qkv.shape, w_proj.shape]
    scratch += [pltpu.VMEM(shape, BF16) for shape in shapes_in]
    args = [flags, w_merge, w_qkv, w_proj, home, x_own, source, ids, merge_first, rows]
    in_specs = [SMEM] + [HBM] * 3 + [VMEM] * (len(args) - 4)
    out, *sent = call(body, outs, args, in_specs, scratch, 3, 3 << 30, 12 << 20, 24)
    return out, sent


def fine_output(part, source, rows, plan, block_rows, block_cols, partial):
    own, width = part.shape

    def body(part_hbm, source_ref, rows_ref, out_ref, part_ref, stage_ref, sems):
        start = Copies(sems)
        cuts = [pl.ds(at, TOK) for at in range(0, own, TOK)]
        held = [start(part_hbm.at[cut], part_ref.at[cut]) for cut in cuts]
        take = columns_of(rows_of(plan, rows_ref, "fine_out"), own) - float(own)
        leave = []
        for n, (cut, copy) in enumerate(zip(cuts, held)):
            got = select_rows(take[n * TOK : (n + 1) * TOK], source_ref[...])
            copy.wait()
            out = part_ref[cut, :].astype(F32) + got
            if partial:
                out_ref[cut, :] = out.astype(BF16)
            else:
                lines = TOK // block_cols
                layer, line = divmod(n * lines, block_rows)
                there = (layer, pl.ds(line, lines))
                stage_ref[there] = out.reshape(lines, block_cols, width).astype(BF16)
                leave.append(start(stage_ref.at[there], out_ref.at[there]))
        for copy in leave:
            copy.wait()

    shape = (2, block_rows, block_cols, width)
    outs = shapes([own], width) if partial else [pltpu.HBM(shape, BF16)]
    scratch = [pltpu.VMEM(part.shape, BF16), pltpu.VMEM(shape, BF16)]
    return call(body, outs, [part, source, rows], [HBM, VMEM, VMEM], scratch, 2 * own // TOK, 1 << 30, 4 << 20)[0]


def coarse_output(coarse, got, rows, which, plan, block_rows, block_cols, part=None):
    own, width = coarse.shape
    half = width // 2
    sizes, more = plan.three[which], plan.four[which]
    parts = [] if part is None else [part]

    def padded(parts, sizes, room):
        out = []
        for value, size, space in zip(parts, sizes, room):
            out.append(value)
            if size < space:
                out.append(jnp.zeros((space - size, value.shape[1]), F32))
        return out

    def body(coarse_ref, *refs):
        got_refs, refs = refs[:3], refs[3:]
        part_refs, (rows_ref, out_ref, *fine_outs, _) = refs[: len(parts)], refs[len(parts) :]
        got = [ref[...].astype(F32) for ref in got_refs]
        back = [jnp.concatenate([x[:size], x[size : 2 * size]], axis=1) for x, size in zip(got, sizes)]
        source = stack_rows([coarse_ref[...].astype(F32)] + padded(back, sizes, plan.room_three))
        out = select_rows(columns_of(rows_of(plan, rows_ref, "coarse_out"), own), source.astype(BF16)).astype(BF16)
        for n in range(own // 2):
            out_ref[n // block_cols, n % block_cols] = out[2 * n : 2 * n + 2]
        for part_ref, fine_ref in zip(part_refs, fine_outs):
            fine = stack_rows(padded([x[2 * size :] for x, size in zip(got, sizes)], more, plan.room_four))
            base = part_ref.shape[0] + sum(plan.room_two)
            take = columns_of(rows_of(plan, rows_ref, "fine_out"), part_ref.shape[0]) - float(base)
            out = part_ref[...].astype(F32) + select_rows(take, fine.astype(BF16))
            fine_ref[...] = out.reshape(fine_ref.shape).astype(BF16)

    outs = [jax.ShapeDtypeStruct((block_rows, block_cols, 2, width), BF16)]
    outs += [jax.ShapeDtypeStruct((2, 2 * block_rows, 2 * block_cols, half), BF16) for _ in parts]
    args = [coarse, *got, *parts, rows]
    out, *fine = call(body, outs, args, [VMEM] * len(args), [], 1, 1 << 28, 1 << 20)
    return out.transpose(2, 0, 1, 3), *fine


def on_device(tokens, regions, shifts, fine_qkv, fine_proj, merge_weight, coarse_qkv, coarse_proj):
    _, rows, cols, _ = tokens.shape
    plan = Plan(rows, cols)

    def first(which, sign, sent, *args):
        got = exchange(sent, plan.one[which], sign)
        return lay(got, plan.room_one), before_fine(*args, plan, rows, cols)

    def second(which, sign, sent, *args):
        got = exchange(sent, plan.two[which], sign)
        return lay(got, plan.room_two), before_coarse(*args, plan)

    def third(which, sign, sent, part, source, coarse, table):
        sizes = [2 * n + m for n, m in zip(plan.three[which], plan.four[which])]
        got = exchange(sent, sizes, sign)
        partial = sum(plan.four[which]) > 0
        fine_out = fine_output(part, source, table, plan, rows, cols, partial)
        place = (table, which, plan, rows // 2, cols // 2)
        if partial:
            coarse_out, fine_out = coarse_output(coarse, got, *place, part=fine_out)
        else:
            (coarse_out,) = coarse_output(coarse, got, *place)
        return fine_out, coarse_out

    def branches(stage, pairs):
        return [functools.partial(stage, which, sign) for which, sign in pairs]

    sent, source, table, flags, one, two, three = first_pieces(shifts, tokens, plan)
    got, (ids, x, weights) = choose(
        one, branches(first, plan.one_branches), sent, flags, regions, source, table, [fine_qkv, fine_proj]
    )
    fine, sent = fine_level(x, got, ids, *weights, fine_qkv, table, plan)
    got, (x, part, home, merge_first) = choose(
        two, branches(second, plan.two_branches), sent, flags, fine, table, merge_weight
    )
    coarse, sent = coarse_level(
        flags, home, x, got, ids, merge_first, merge_weight, coarse_qkv, coarse_proj, table, plan
    )
    return choose(three, branches(third, plan.three_branches), sent, part, got, coarse, table)


def solution(mesh):
    return jax.shard_map(
        on_device,
        mesh=mesh,
        in_specs=(P(None, "lat", "lon", None), P(), P(), P(), P(), P(), P(), P()),
        out_specs=(P(None, "lat", "lon", None), P(None, "lat", "lon", None)),
        check_vma=False,
    )
```

```python
import functools

import jax
import jax.numpy as jnp
import numpy as np
from jax import lax
from jax.experimental import pallas as pl
from jax.experimental.pallas import tpu as pltpu
from jax.sharding import PartitionSpec as P

HD = 32
WH = 6
WW = 12
TOK = 2 * WH * WW
EPS = 1e-05
BIG = 1e30
SCALE = float(np.log2(np.e) / np.sqrt(HD))

NT = (((1,), (1,)), ((), ()))
TN = (((0,), (0,)), ((), ()))
F32 = jnp.float32
BF16 = jnp.bfloat16
I32 = jnp.int32

PAIRS = [(WH - 1, t) for t in range(1, WH)] + [(t, WH - 1) for t in range(1, WH - 1)]


def up16(count):
    return -(-count // 16) * 16


def natural(rows, cols):
    return [(l, r, c) for l in range(2) for r in range(rows) for c in range(cols)]


def windowed(rows, cols, come):
    windows = [(wr, wc) for wr in range(rows // WH) for wc in range(cols // WW)]
    return [
        (l, wr * WH + r, wc * WW + c)
        for wr, wc in windows[::-come]
        for l in range(2)
        for r in range(WH)
        for c in range(WW)
    ]


def moved(order, d):
    return [(l, r + d, c + 2 * d) for l, r, c in order]


def exchange_places(held, wanted, rows, cols, sign):
    at = {place: n for n, place in enumerate(held)}
    found = []
    for dr, dc in ((sign, 0), (0, sign), (sign, sign)):
        numbers, places = [], []
        for l, r, c in sorted(set(wanted) - set(held)):
            n = at.get((l, r - dr * rows, c - dc * cols))
            if n is not None:
                numbers.append(n)
                places.append((l, r, c))
        found.append((numbers, places))
    return found


def offsets(t0, t1):
    a = t0 if t0 <= 2 else t0 - WH
    big_a = t1 if t1 <= 2 else t1 - WH
    ahead = 1 if 2 * big_a > a or 2 * big_a - a == 0 and a < 0 else -1
    return a, big_a, ahead


def classes_of(needs, slack):
    rounded = [tuple(-(-size // 8) * 8 for size in need) for need in needs]
    heavy = [sum(need[1:3]) * 2 + sum(need[4:]) for need in rounded]
    limits = []
    for size in sorted(set(heavy)):
        if not limits or size > limits[-1][0] * slack:
            limits.append([size, size])
        limits[-1][1] = size
    which = [next(n for n, limit in enumerate(limits) if size <= limit[1]) for size in heavy]
    sizes = [
        [max(need[k] for need, w in zip(rounded, which) if w == n) for k in range(len(needs[0]))]
        for n in range(len(limits))
    ]
    return sizes, which


def rooms(sizes):
    return [up16(max(size[k] for size in sizes)) for k in range(len(sizes[0]))]


class Plan:
    def __init__(self, rows, cols):
        crows, ccols = rows // 2, cols // 2
        block, cblock = natural(rows, cols), natural(crows, ccols)
        cases = []
        for t0, t1 in PAIRS:
            a, big_a, ahead = offsets(t0, t1)
            come = 1 if a > 0 else -1
            fine = moved(windowed(rows, cols, come), a)
            coarse = moved(cblock, big_a)
            quarters = [
                (l, 2 * r + dr, 2 * c + dc)
                for dr, dc in ((0, 0), (1, 0), (0, 1), (1, 1))
                for l, r, c in coarse
            ]
            one = exchange_places(block, fine, rows, cols, come)
            home = [p for p in block if p not in set(fine)]
            wanted = quarters + (home if come == -ahead else [])
            two = exchange_places(fine, wanted, rows, cols, ahead)
            back = 1 if big_a < 0 else -1
            three = exchange_places(coarse, cblock, crows, ccols, back)
            got = set(fine).union(*[places for _, places in two])
            four = exchange_places(fine, [p for p in block if p not in got], rows, cols, back)
            cases.append((come, ahead, back, fine, coarse, quarters, one, two, three, four))

        def needs(which):
            return [[len(numbers) for numbers, _ in case[which]] for case in cases]

        self.one, one_class = classes_of(needs(6), 1.15)
        self.two, two_class = classes_of(needs(7), 1.15)
        sizes, three_class = classes_of([three + four for three, four in zip(needs(8), needs(9))], 1.0)
        self.three, self.four = [size[:3] for size in sizes], [size[3:] for size in sizes]
        self.room_one, self.room_two = rooms(self.one), rooms(self.two)
        self.room_three, self.room_four = rooms(self.three), rooms(self.four)

        def branches(which_class, direction):
            pairs = [(n, case[direction]) for n, case in zip(which_class, cases)]
            found = sorted(set(pairs))
            return found, [found.index(pair) for pair in pairs]

        self.one_branches, one_at = branches(one_class, 0)
        self.two_branches, two_at = branches(two_class, 1)
        self.three_branches, three_at = branches(three_class, 2)
        self.flags = dict(
            three_class=three_class,
            one_at=one_at, two_at=two_at, three_at=three_at,
            a=[offsets(*pair)[0] for pair in PAIRS], big_a=[offsets(*pair)[1] for pair in PAIRS],
        )

        found = {}
        for n, (come, ahead, back, fine, coarse, quarters, one, two, three, four) in enumerate(cases):

            def send(exchanged, room):
                return [n for (numbers, _), size in zip(exchanged, room) for n in numbers + [-1] * (size - len(numbers))]

            def source(held, *exchanges):
                places = list(held)
                for exchanged, room in exchanges:
                    for (_, got), size in zip(exchanged, room):
                        places += got + [None] * (size - len(got))
                return {p: n for n, p in enumerate(places) if p is not None}

            first, second = source(block, (one, self.room_one)), source(fine, (two, self.room_two))
            third = source(coarse, (three, self.room_three))
            last = source(fine, (two, self.room_two), (four, self.room_four))
            out = [(l, r, c) for r in range(crows) for c in range(ccols) for l in range(2)]
            rows_of = dict(
                send_one=send(one, self.room_one),
                take_one=[first[p] for p in fine],
                send_two=send(two, self.room_two),
                take_two=[second[p] for p in quarters],
                send_three=send(three, self.room_three),
                send_four=send(four, self.room_four),
                fine_out=[last[p] for p in block],
                coarse_out=[third[p] for p in out],
            )
            for name, row in rows_of.items():
                found.setdefault(name, []).append(row)
        parts, self.at, top = [], {}, 0
        for name, lists in found.items():
            length = -(-max(len(row) for row in lists) // 128)
            part = np.full((len(PAIRS), length * 128), -1, np.float32)
            for n, row in enumerate(lists):
                part[n, : len(row)] = row
            parts.append(part.reshape(len(PAIRS), length, 128))
            self.at[name] = (top, length)
            top += length
        parts.append(np.zeros((len(PAIRS), -top % 8, 128), np.float32))
        self.table = np.concatenate(parts, axis=1)


def case_of(shifts_ref):
    t0, t1 = shifts_ref[0], shifts_ref[1]
    return jnp.where(t0 == WH - 1, t1 - 1, t0 + WH - 2)


def lookup(values, case):
    out = jnp.int32(values[0])
    for n, value in enumerate(values[1:], 1):
        out = jnp.where(case == n, value, out)
    return out


def columns_of(rows, count):
    parts = [jnp.broadcast_to(rows[j : j + 1], (128, 128)).T for j in range(-(-count // 128))]
    return stack_rows(parts)[:count]


def select_rows(index, source):
    lane = lax.broadcasted_iota(I32, (1, 128), 1).astype(F32)
    size = source.shape[0]
    pick = [jnp.where(index == lane + float(at), 1.0, 0.0).astype(BF16) for at in range(0, size, 128)]
    pick = jnp.concatenate(pick, axis=1)[:, :size]
    return jnp.dot(pick, source, preferred_element_type=F32)


def stack_rows(parts):
    return parts[0] if len(parts) == 1 else jnp.concatenate(parts, axis=0)


def layer_norm(values):
    center = jnp.mean(values, axis=-1, keepdims=True)
    values = values - center
    spread = jnp.mean(values * values, axis=-1, keepdims=True)
    return values * lax.rsqrt(spread + EPS)


def attend_windows(qkv_of, id_of, windows, inner, finish):
    lane = lax.broadcasted_iota(I32, (1, 128), 1)
    forbid = jnp.where(lane < 8, BIG, 0.0).astype(BF16)
    groups = inner // 128
    units = [(w, g) for w in range(windows) for g in range(groups)]
    scores, weights, outs = {}, {}, {}

    def score(w, g):
        key_id = id_of(w)
        not_id = (key_id - 1).astype(BF16) * forbid
        q = qkv_of(w, g * 128)
        keys = jnp.concatenate([qkv_of(w, inner + g * 128), key_id], axis=1)
        queries = []
        for h in range(4):
            mine = jnp.where((lane >= h * HD) & (lane < (h + 1) * HD), 1.0, 0.0).astype(BF16)
            queries.append(jnp.concatenate([q * mine, not_id], axis=1))
        scores[w, g] = lax.dot_general(stack_rows(queries), keys, NT, preferred_element_type=F32)

    def soften(w, g):
        s = scores.pop((w, g))
        weights[w, g] = jnp.exp2((s - jnp.max(s, axis=1, keepdims=True)) * SCALE).astype(BF16)

    def gather(w, g):
        v = qkv_of(w, 2 * inner + g * 128)
        values = jnp.concatenate([v, jnp.ones_like(v)], axis=1)
        out = jnp.dot(weights.pop((w, g)), values, preferred_element_type=F32)
        picked, total = out[:TOK, :128], out[:TOK, 128:]
        for h in range(1, 4):
            rows = slice(h * TOK, (h + 1) * TOK)
            picked = jnp.where(lane < h * HD, picked, out[rows, :128])
            total = jnp.where(lane < h * HD, total, out[rows, 128:])
        outs[w, g] = (picked / total).astype(BF16)
        if g == groups - 1:
            finish(w, jnp.concatenate([outs.pop((w, k)) for k in range(groups)], axis=1))

    for n in range(len(units) + 2):
        if n < len(units):
            score(*units[n])
        if 0 <= n - 1 < len(units):
            soften(*units[n - 1])
        if 0 <= n - 2 < len(units):
            gather(*units[n - 2])


ANY = pl.BlockSpec(memory_space=pl.ANY)
HBM = pl.BlockSpec(memory_space=pltpu.HBM)
VMEM = pl.BlockSpec(memory_space=pltpu.VMEM)
SMEM = pl.BlockSpec(memory_space=pltpu.SMEM)


def call(body, outs, args, in_specs, scratch, copies, flops, moved_bytes, vmem=8):
    args = [
        pltpu.with_memory_space_constraint(arg, spec.memory_space) for arg, spec in zip(args, in_specs, strict=True)
    ]
    spaces = [getattr(out, "memory_space", pltpu.SMEM if out.dtype == I32 else pltpu.VMEM) for out in outs]
    out_specs = [pl.BlockSpec(memory_space=space) for space in spaces]
    return pl.pallas_call(
        body,
        out_shape=outs,
        in_specs=in_specs,
        out_specs=out_specs,
        scratch_shapes=list(scratch) + [pltpu.SemaphoreType.DMA((copies,))],
        compiler_params=pltpu.CompilerParams(vmem_limit_bytes=vmem << 20),
        cost_estimate=pl.CostEstimate(flops=flops, bytes_accessed=moved_bytes, transcendentals=0),
    )(*args)


def shapes(sizes, width, space=pltpu.VMEM):
    return [space((n, width), BF16) for n in sizes]


class Copies:
    def __init__(self, sems):
        self.sems, self.used = sems, 0

    def __call__(self, src, dst):
        copy = pltpu.make_async_copy(src, dst, self.sems.at[self.used])
        self.used += 1
        copy.start()
        return copy


def lay(pieces, room):
    width = pieces[0].shape[1]

    def body(*refs):
        out_ref = refs[len(pieces)]
        at = 0
        for ref, space in zip(refs, room):
            rows = ref.shape[0]
            out_ref[at : at + rows, :] = ref[...]
            if rows < space:
                out_ref[at + rows : at + space, :] = jnp.zeros((space - rows, width), BF16)
            at += space

    return call(body, shapes([sum(room)], width), pieces, [VMEM] * 3, [], 1, 0, 1 << 18)[0]


def flat(ref):
    layers, rows, cols, width = ref.shape
    return ref[...].astype(F32).reshape(layers * rows * cols, width).astype(BF16)


def put_pieces(value, refs):
    at = 0
    for ref in refs:
        ref[...] = value[at : at + ref.shape[0]].astype(BF16)
        at += ref.shape[0]


def rows_of(plan, table_ref, name, *lead):
    top, length = plan.at[name]
    return table_ref[(*lead, slice(top, top + length), slice(None))]


def exchange(pieces, sizes, sign):
    lat, lon = lax.axis_size("lat"), lax.axis_size("lon")
    row, col, both = [piece[:size] for piece, size in zip(pieces, sizes)]
    pairs = [((i + sign) % lat * lon + (j + sign) % lon, i * lon + j) for i in range(lat) for j in range(lon)]
    col = lax.ppermute(col, "lon", [((j + sign) % lon, j) for j in range(lon)])
    both = lax.ppermute(both, ("lat", "lon"), pairs)
    row = lax.ppermute(row, "lat", [((i + sign) % lat, i) for i in range(lat)])
    return [row, col, both]


def choose(index, branches, *args):
    flat_args, tree = jax.tree.flatten(args)
    out_trees = []

    def closed(branch):
        def run(*leaves):
            out, out_tree = jax.tree.flatten(branch(*jax.tree.unflatten(tree, leaves)))
            out_trees.append(out_tree)
            return out

        return jax.make_jaxpr(run)(*flat_args)

    out = lax.cond_p.bind(index, *flat_args, branches=tuple(closed(branch) for branch in branches))
    return jax.tree.unflatten(out_trees[0], out)


FLAGS = ("three_class", "a", "big_a")


def first_pieces(shifts, tokens, plan):
    width = tokens.shape[-1]
    count = tokens.size // width
    kinds = 3

    def body(shifts_hbm, tokens_hbm, table_hbm, *refs):
        outs, refs = refs[:kinds], refs[kinds:]
        source_ref, rows_ref, flags_ref, *at_refs, shifts_ref, tokens_ref, table_ref, sems = refs
        start = Copies(sems)
        shift = start(shifts_hbm, shifts_ref)
        held = start(tokens_hbm, tokens_ref)
        table = start(table_hbm, table_ref)
        shift.wait()
        case = case_of(shifts_ref)
        for ref, name in zip(at_refs, ("one_at", "two_at", "three_at")):
            ref[0] = lookup(plan.flags[name], case)
        for n, name in enumerate(FLAGS):
            flags_ref[n] = lookup(plan.flags[name], case)
        held.wait()
        source_ref[...] = flat(tokens_ref)
        table.wait()
        rows_ref[...] = table_ref[case]
        index = columns_of(rows_of(plan, table_ref, "send_one", case), sum(plan.room_one))
        put_pieces(select_rows(index, source_ref[...]), outs)

    outs = shapes([*plan.room_one, count], width)
    outs += [pltpu.VMEM(plan.table.shape[1:], F32), pltpu.SMEM((8,), I32)]
    outs += [pltpu.SMEM((1,), I32)] * 3
    scratch = [pltpu.SMEM((2,), I32), pltpu.VMEM(tokens.shape, BF16), pltpu.VMEM(plan.table.shape, F32)]
    got = call(body, outs, [shifts, tokens, plan.table], [HBM] * 3, scratch, 3, 1 << 28, 1 << 20)
    sent, (source, rows, flags, one, two, three) = got[:kinds], got[kinds:]
    return sent, source, rows, flags, one[0], two[0], three[0]


def before_fine(flags, regions, tokens, table, weights, plan, rows, cols, come):
    _, lat, lon = regions.shape
    width = tokens.shape[1]
    flat_regions = regions.reshape(2 * lat, lon)
    fine, coarse = windowed(rows, cols, come), natural(rows // 2, cols // 2)
    rest = len(fine) - TOK
    inner = weights[1].shape[0]

    def lanes(places, scale, is_fine):
        places = np.asarray([(l, scale * r, scale * c, is_fine) for l, r, c in places], np.float32)
        return np.pad(places, ((0, -len(places) % 128), (0, 0))).T.reshape(4, -1, 128)

    places = np.concatenate([lanes(fine, 1, 1), lanes(coarse, 2, 0)], axis=1)
    lines = places.shape[1]

    def body(flags_ref, rows_ref, tokens_ref, regions_hbm, places_hbm, *refs):
        weights_hbm, refs = refs[: len(weights)], refs[len(weights) :]
        id_ref, x_ref, done_ref, *refs = refs
        weight_refs, (regions_ref, places_ref, v_w_ref, qkv_ref, sems) = refs[: len(weights)], refs[len(weights) :]
        start = Copies(sems)
        waits = [start(regions_hbm, regions_ref), start(places_hbm, places_ref)]
        later = [
            start(src.at[:, pl.ds(0, dst.shape[1])], dst) for src, dst in zip(weights_hbm, weight_refs)
        ]
        later.append(start(weights_hbm[0].at[:, pl.ds(2 * inner, inner)], v_w_ref))
        for copy in waits:
            copy.wait()
        a = flags_ref[1].astype(F32)
        big_a = 2.0 * flags_ref[2].astype(F32)
        is_fine = places_ref[3]
        d = is_fine * a + (1.0 - is_fine) * big_a
        row = places_ref[1] + d + (lax.axis_index("lat") * rows).astype(F32)
        col = places_ref[2] + 2.0 * d + (lax.axis_index("lon") * cols).astype(F32)
        wrapped = jnp.where((row < 0) | (row >= lat), 4.0, 0.0)
        row = jnp.where(row < 0, row + lat, jnp.where(row >= lat, row - lat, row))
        col = jnp.where(col < 0, col + lon, jnp.where(col >= lon, col - lon, col))
        row = row + places_ref[0] * lat

        def along(values):
            return jnp.concatenate([values[n : n + 1] for n in range(lines)], axis=1)

        line = lax.broadcasted_iota(I32, (2 * lat, 1), 0).astype(F32)
        pick = jnp.where(line == along(row), 1.0, 0.0).astype(BF16)
        known = regions_ref[...].astype(F32).astype(BF16)
        picked = lax.dot_general(known, pick, TN, preferred_element_type=F32)
        line = lax.broadcasted_iota(I32, (lon, 1), 0).astype(F32)
        ids = jnp.sum(jnp.where(line == along(col), picked, 0.0), axis=0, keepdims=True) + along(wrapped)
        for n in range(lines):
            id_ref[n : n + 1, :] = ids[:, n * 128 : (n + 1) * 128]
        take = columns_of(rows_of(plan, rows_ref, "take_one"), len(fine))
        x = select_rows(take, tokens_ref[...])
        x_ref[...] = x[:rest].astype(BF16)
        x = x[rest:]
        normed = layer_norm(x).astype(BF16)
        for copy in later:
            copy.wait()
        qkv_ref[:, : 2 * inner] = jnp.dot(normed, weight_refs[0][...], preferred_element_type=F32).astype(BF16)
        qkv_ref[:, 2 * inner :] = jnp.dot(normed, v_w_ref[...], preferred_element_type=F32).astype(BF16)
        hot = id_columns(id_ref[: -(-len(fine) // 128), :], len(fine))[rest:]

        def finish(w, out):
            out = jnp.dot(out, weight_refs[1][...], preferred_element_type=F32)
            done_ref[...] = (x + out).astype(BF16)

        attend_windows(lambda w, at: qkv_ref[:, at : at + 128], lambda w: hot, 1, inner, finish)

    outs = [pltpu.VMEM((lines, 128), F32)] + shapes([rest, TOK], width)
    outs += [pltpu.VMEM((w.shape[0], min(w.shape[1], 2 * inner)), BF16) for w in weights]
    scratch = [pltpu.VMEM(flat_regions.shape, I32), pltpu.VMEM(places.shape, F32)]
    scratch += [pltpu.VMEM((width, inner), BF16), pltpu.VMEM((TOK, 3 * inner), BF16)]
    args = [flags, table, tokens, flat_regions, places, *weights]
    in_specs = [SMEM, VMEM, VMEM] + [HBM] * (2 + len(weights))
    ids, x, done, *weights = call(body, outs, args, in_specs, scratch, 3 + len(weights), 1 << 28, 4 << 20)
    return ids, x, done, weights


def id_columns(lines, count):
    lane = lax.broadcasted_iota(I32, (1, 128), 1).astype(F32)
    return jnp.where(columns_of(lines, count) == lane, 1.0, 0.0).astype(BF16)


def before_coarse(flags, fine, table, weight, plan):
    own, width = fine.shape
    half = 5 * weight.shape[0] // 16

    def body(flags_ref, rows_ref, fine_ref, weight_hbm, x_ref, part_hbm, home_ref, weight_ref, part_ref, sems):
        start = Copies(sems)
        later = start(weight_hbm.at[pl.ds(0, half)], weight_ref)
        take = columns_of(rows_of(plan, rows_ref, "fine_out"), own)
        part_ref[...] = select_rows(take, fine_ref[...]).astype(BF16)
        leave = start(part_ref, part_hbm)
        take = columns_of(rows_of(plan, rows_ref, "take_two"), own)
        x_ref[...] = select_rows(take, fine_ref[...]).astype(BF16)

        @pl.when(needs_fine(flags_ref, plan))
        def _():
            index = columns_of(rows_of(plan, rows_ref, "send_four"), sum(plan.room_four))
            home_ref[...] = select_rows(index, fine_ref[...]).astype(BF16)

        leave.wait()
        later.wait()

    outs = shapes([own], width) + shapes([own], width, pltpu.HBM)
    outs += shapes([sum(plan.room_four)], width) + shapes([half], weight.shape[1])
    scratch = [pltpu.VMEM(fine.shape, BF16)]
    args = [flags, table, fine, weight]
    return call(body, outs, args, [SMEM, VMEM, VMEM, HBM], scratch, 2, 1 << 28, 4 << 20)


def needs_fine(flags_ref, plan):
    with_fine = [n for n, sizes in enumerate(plan.four) if sum(sizes)]
    return functools.reduce(jnp.logical_or, [flags_ref[0] == n for n in with_fine])


def fine_level(x_own, done, source, ids, w_qk, w_proj, w_qkv, rows, plan):
    count, width = x_own.shape
    total = count + TOK
    inner = w_proj.shape[0]

    def body(own_ref, done_ref, source_ref, ids_ref, qk_w_ref, proj_w_ref, qkv_w_hbm, rows_ref, out_ref, *refs):
        *piece_outs, x_ref, qkv_ref, id_ref, v_w_ref, sems = refs
        v_w = Copies(sems)(qkv_w_hbm.at[:, pl.ds(2 * inner, inner)], v_w_ref)
        id_ref[...] = id_columns(ids_ref[: -(-count // 128), :], count)
        take = columns_of(rows_of(plan, rows_ref, "take_one"), count) - float(total)
        x = own_ref[...].astype(F32) + select_rows(take, source_ref[...])
        x_ref[...] = x
        normed = layer_norm(x).astype(BF16)
        v_w.wait()
        qkv_ref[:, : 2 * inner] = jnp.dot(normed, qk_w_ref[...], preferred_element_type=F32).astype(BF16)
        qkv_ref[:, 2 * inner :] = jnp.dot(normed, v_w_ref[...], preferred_element_type=F32).astype(BF16)

        def finish(w, out):
            at = slice(w * TOK, (w + 1) * TOK)
            out = jnp.dot(out, proj_w_ref[...], preferred_element_type=F32)
            out_ref[at, :] = (x_ref[at, :] + out).astype(BF16)

        attend_windows(
            lambda w, at: qkv_ref[w * TOK : (w + 1) * TOK, at : at + 128],
            lambda w: id_ref[w * TOK : (w + 1) * TOK, :],
            count // TOK,
            inner,
            finish,
        )
        out_ref[count:, :] = done_ref[...]
        index = columns_of(rows_of(plan, rows_ref, "send_two"), sum(plan.room_two))
        put_pieces(select_rows(index, out_ref[...]), piece_outs)

    outs = shapes([total, *plan.room_two], width)
    scratch = [
        pltpu.VMEM((count, width), F32),
        pltpu.VMEM((count, 3 * inner), BF16),
        pltpu.VMEM((count, 128), BF16),
        pltpu.VMEM((width, inner), BF16),
    ]
    args = [x_own, done, source, ids, w_qk, w_proj, w_qkv, rows]
    out, *sent = call(body, outs, args, [VMEM] * 6 + [HBM, VMEM], scratch, 1, 3 << 30, 6 << 20, 14)
    return out, sent


def coarse_level(flags, home, x_own, source, ids, merge_first, w_merge, w_qkv, w_proj, rows, plan):
    depth, width = w_merge.shape
    own, half = x_own.shape
    count = own // 4
    inner = w_proj.shape[0]

    def body(
        flags_ref, merge_hbm, qkv_w_hbm, proj_w_hbm, home_ref, own_ref, source_ref, ids_ref, first_ref, rows_ref, *refs
    ):
        out_ref, *piece_outs = refs[:4]
        qkv_ref, id_ref, merge_ref, qkv_w_ref, proj_w_ref, sems = refs[4:]
        start = Copies(sems)
        here = first_ref.shape[0]
        merge_w = start(merge_hbm.at[pl.ds(here, depth - here)], merge_ref)
        qkv_w = start(qkv_w_hbm, qkv_w_ref)
        proj_w = start(proj_w_hbm, proj_w_ref)
        id_ref[...] = id_columns(ids_ref[-(-own // 128) :, :], count)
        take = columns_of(rows_of(plan, rows_ref, "take_two"), 4 * count) - float(own)
        x = own_ref[...].astype(F32) + select_rows(take, source_ref[...])
        x = jnp.concatenate([x[n * count : (n + 1) * count] for n in range(4)], axis=1)
        stacked = layer_norm(x).astype(BF16)
        merge_w.wait()
        merged = jnp.dot(stacked[:, :here], first_ref[...], preferred_element_type=F32)
        merged = merged + jnp.dot(stacked[:, here:], merge_ref[...], preferred_element_type=F32)
        merged = merged.astype(BF16).astype(F32)
        normed = layer_norm(merged).astype(BF16)
        qkv_w.wait()
        proj_w.wait()
        qkv_ref[...] = jnp.dot(normed, qkv_w_ref[...], preferred_element_type=F32).astype(BF16)

        def finish(w, out):
            out = jnp.dot(out, proj_w_ref[...], preferred_element_type=F32)
            out_ref[...] = (merged + out).astype(BF16)

        attend_windows(lambda w, at: qkv_ref[:, at : at + 128], lambda w: id_ref[...], 1, inner, finish)
        sent = select_rows(columns_of(rows_of(plan, rows_ref, "send_three"), sum(plan.room_three)), out_ref[...])
        sent = sent.astype(BF16)
        for n, sizes in enumerate(plan.three):

            @pl.when(flags_ref[0] == n)
            def _():
                at = 0
                for ref, size, space in zip(piece_outs, sizes, plan.room_three):
                    ref[:size, :] = sent[at : at + size, :half]
                    ref[size : 2 * size, :] = sent[at : at + size, half:]
                    at += space

        for n, fine_sizes in enumerate(plan.four):
            if sum(fine_sizes):

                @pl.when(flags_ref[0] == n)
                def _():
                    at = 0
                    for ref, size, more, space in zip(piece_outs, plan.three[n], fine_sizes, plan.room_four):
                        ref[2 * size : 2 * size + more, :] = home_ref[at : at + more, :]
                        at += space

    most = [max(2 * three[k] + four[k] for three, four in zip(plan.three, plan.four)) for k in range(3)]
    outs = shapes([count], width) + shapes(most, half)
    scratch = [pltpu.VMEM((count, 3 * inner), BF16)]
    shapes_in = [(count, 128), (depth - merge_first.shape[0], width), w_qkv.shape, w_proj.shape]
    scratch += [pltpu.VMEM(shape, BF16) for shape in shapes_in]
    args = [flags, w_merge, w_qkv, w_proj, home, x_own, source, ids, merge_first, rows]
    in_specs = [SMEM] + [HBM] * 3 + [VMEM] * (len(args) - 4)
    out, *sent = call(body, outs, args, in_specs, scratch, 3, 3 << 30, 12 << 20, 24)
    return out, sent


def fine_output(part, source, rows, plan, block_rows, block_cols, partial):
    own, width = part.shape

    def body(part_hbm, source_ref, rows_ref, out_ref, part_ref, stage_ref, sems):
        start = Copies(sems)
        cuts = [pl.ds(at, TOK) for at in range(0, own, TOK)]
        held = [start(part_hbm.at[cut], part_ref.at[cut]) for cut in cuts]
        take = columns_of(rows_of(plan, rows_ref, "fine_out"), own) - float(own)
        leave = []
        for n, (cut, copy) in enumerate(zip(cuts, held)):
            got = select_rows(take[n * TOK : (n + 1) * TOK], source_ref[...])
            copy.wait()
            out = part_ref[cut, :].astype(F32) + got
            if partial:
                out_ref[cut, :] = out.astype(BF16)
            else:
                lines = TOK // block_cols
                layer, line = divmod(n * lines, block_rows)
                there = (layer, pl.ds(line, lines))
                stage_ref[there] = out.reshape(lines, block_cols, width).astype(BF16)
                leave.append(start(stage_ref.at[there], out_ref.at[there]))
        for copy in leave:
            copy.wait()

    shape = (2, block_rows, block_cols, width)
    outs = shapes([own], width) if partial else [pltpu.HBM(shape, BF16)]
    scratch = [pltpu.VMEM(part.shape, BF16), pltpu.VMEM(shape, BF16)]
    return call(body, outs, [part, source, rows], [HBM, VMEM, VMEM], scratch, 2 * own // TOK, 1 << 30, 4 << 20)[0]


def coarse_output(coarse, got, rows, which, plan, block_rows, block_cols, part=None):
    own, width = coarse.shape
    half = width // 2
    sizes, more = plan.three[which], plan.four[which]
    parts = [] if part is None else [part]

    def padded(parts, sizes, room):
        out = []
        for value, size, space in zip(parts, sizes, room):
            out.append(value)
            if size < space:
                out.append(jnp.zeros((space - size, value.shape[1]), F32))
        return out

    def body(coarse_ref, *refs):
        got_refs, refs = refs[:3], refs[3:]
        part_refs, (rows_ref, out_ref, *fine_outs, _) = refs[: len(parts)], refs[len(parts) :]
        got = [ref[...].astype(F32) for ref in got_refs]
        back = [jnp.concatenate([x[:size], x[size : 2 * size]], axis=1) for x, size in zip(got, sizes)]
        source = stack_rows([coarse_ref[...].astype(F32)] + padded(back, sizes, plan.room_three))
        out = select_rows(columns_of(rows_of(plan, rows_ref, "coarse_out"), own), source.astype(BF16)).astype(BF16)
        for n in range(own // 2):
            out_ref[n // block_cols, n % block_cols] = out[2 * n : 2 * n + 2]
        for part_ref, fine_ref in zip(part_refs, fine_outs):
            fine = stack_rows(padded([x[2 * size :] for x, size in zip(got, sizes)], more, plan.room_four))
            base = part_ref.shape[0] + sum(plan.room_two)
            take = columns_of(rows_of(plan, rows_ref, "fine_out"), part_ref.shape[0]) - float(base)
            out = part_ref[...].astype(F32) + select_rows(take, fine.astype(BF16))
            fine_ref[...] = out.reshape(fine_ref.shape).astype(BF16)

    outs = [jax.ShapeDtypeStruct((block_rows, block_cols, 2, width), BF16)]
    outs += [jax.ShapeDtypeStruct((2, 2 * block_rows, 2 * block_cols, half), BF16) for _ in parts]
    args = [coarse, *got, *parts, rows]
    out, *fine = call(body, outs, args, [VMEM] * len(args), [], 1, 1 << 28, 1 << 20)
    return out.transpose(2, 0, 1, 3), *fine


def on_device(tokens, regions, shifts, fine_qkv, fine_proj, merge_weight, coarse_qkv, coarse_proj):
    _, rows, cols, _ = tokens.shape
    plan = Plan(rows, cols)

    def first(which, sign, sent, *args):
        got = exchange(sent, plan.one[which], sign)
        return lay(got, plan.room_one), before_fine(*args, plan, rows, cols, sign)

    def second(which, sign, sent, *args):
        got = exchange(sent, plan.two[which], sign)
        return lay(got, plan.room_two), before_coarse(*args, plan)

    def third(which, sign, sent, part, source, coarse, table):
        sizes = [2 * n + m for n, m in zip(plan.three[which], plan.four[which])]
        got = exchange(sent, sizes, sign)
        partial = sum(plan.four[which]) > 0
        fine_out = fine_output(part, source, table, plan, rows, cols, partial)
        place = (table, which, plan, rows // 2, cols // 2)
        if partial:
            coarse_out, fine_out = coarse_output(coarse, got, *place, part=fine_out)
        else:
            (coarse_out,) = coarse_output(coarse, got, *place)
        return fine_out, coarse_out

    def branches(stage, pairs):
        return [functools.partial(stage, which, sign) for which, sign in pairs]

    sent, source, table, flags, one, two, three = first_pieces(shifts, tokens, plan)
    got, (ids, x, done, weights) = choose(
        one, branches(first, plan.one_branches), sent, flags, regions, source, table, [fine_qkv, fine_proj]
    )
    fine, sent = fine_level(x, done, got, ids, *weights, fine_qkv, table, plan)
    got, (x, part, home, merge_first) = choose(
        two, branches(second, plan.two_branches), sent, flags, fine, table, merge_weight
    )
    coarse, sent = coarse_level(
        flags, home, x, got, ids, merge_first, merge_weight, coarse_qkv, coarse_proj, table, plan
    )
    return choose(three, branches(third, plan.three_branches), sent, part, got, coarse, table)


def solution(mesh):
    return jax.shard_map(
        on_device,
        mesh=mesh,
        in_specs=(P(None, "lat", "lon", None), P(), P(), P(), P(), P(), P(), P()),
        out_specs=(P(None, "lat", "lon", None), P(None, "lat", "lon", None)),
        check_vma=False,
    )
```

```python
import functools

import jax
import jax.numpy as jnp
import numpy as np
from jax import lax
from jax.experimental import pallas as pl
from jax.experimental.pallas import tpu as pltpu
from jax.sharding import PartitionSpec as P

HD = 32
WH = 6
WW = 12
TOK = 2 * WH * WW
EPS = 1e-05
BIG = 1e30
SCALE = float(np.log2(np.e) / np.sqrt(HD))

NT = (((1,), (1,)), ((), ()))
TN = (((0,), (0,)), ((), ()))
F32 = jnp.float32
BF16 = jnp.bfloat16
I32 = jnp.int32

PAIRS = [(WH - 1, t) for t in range(1, WH)] + [(t, WH - 1) for t in range(1, WH - 1)]


def up16(count):
    return -(-count // 16) * 16


def natural(rows, cols):
    return [(l, r, c) for l in range(2) for r in range(rows) for c in range(cols)]


def windowed(rows, cols):
    return [
        (l, wr * WH + r, wc * WW + c)
        for wr in range(rows // WH)
        for wc in range(cols // WW)
        for l in range(2)
        for r in range(WH)
        for c in range(WW)
    ]


def moved(order, d):
    return [(l, r + d, c + 2 * d) for l, r, c in order]


def exchange_places(held, wanted, rows, cols, sign):
    at = {place: n for n, place in enumerate(held)}
    found = []
    for dr, dc in ((sign, 0), (0, sign), (sign, sign)):
        numbers, places = [], []
        for l, r, c in sorted(set(wanted) - set(held)):
            n = at.get((l, r - dr * rows, c - dc * cols))
            if n is not None:
                numbers.append(n)
                places.append((l, r, c))
        found.append((numbers, places))
    return found


def offsets(t0, t1):
    a = t0 if t0 <= 2 else t0 - WH
    big_a = t1 if t1 <= 2 else t1 - WH
    ahead = 1 if 2 * big_a > a or 2 * big_a - a == 0 and a < 0 else -1
    return a, big_a, ahead


def classes_of(needs, slack):
    rounded = [tuple(-(-size // 8) * 8 for size in need) for need in needs]
    heavy = [sum(need[1:3]) * 2 + sum(need[4:]) for need in rounded]
    limits = []
    for size in sorted(set(heavy)):
        if not limits or size > limits[-1][0] * slack:
            limits.append([size, size])
        limits[-1][1] = size
    which = [next(n for n, limit in enumerate(limits) if size <= limit[1]) for size in heavy]
    sizes = [
        [max(need[k] for need, w in zip(rounded, which) if w == n) for k in range(len(needs[0]))]
        for n in range(len(limits))
    ]
    return sizes, which


def rooms(sizes):
    return [up16(max(size[k] for size in sizes)) for k in range(len(sizes[0]))]


class Plan:
    def __init__(self, rows, cols):
        crows, ccols = rows // 2, cols // 2
        block, cblock = natural(rows, cols), natural(crows, ccols)
        cases = []
        for t0, t1 in PAIRS:
            a, big_a, ahead = offsets(t0, t1)
            fine = moved(windowed(rows, cols), a)
            coarse = moved(cblock, big_a)
            quarters = [
                (l, 2 * r + dr, 2 * c + dc)
                for dr, dc in ((0, 0), (1, 0), (0, 1), (1, 1))
                for l, r, c in coarse
            ]
            come = 1 if a > 0 else -1
            one = exchange_places(block, fine, rows, cols, come)
            home = [p for p in block if p not in set(fine)]
            wanted = quarters + (home if come == -ahead else [])
            two = exchange_places(fine, wanted, rows, cols, ahead)
            back = 1 if big_a < 0 else -1
            three = exchange_places(coarse, cblock, crows, ccols, back)
            got = set(fine).union(*[places for _, places in two])
            four = exchange_places(fine, [p for p in block if p not in got], rows, cols, back)
            cases.append((come, ahead, back, fine, coarse, quarters, one, two, three, four))

        def needs(which):
            return [[len(numbers) for numbers, _ in case[which]] for case in cases]

        self.one, one_class = classes_of(needs(6), 1.15)
        self.two, two_class = classes_of(needs(7), 1.15)
        sizes, three_class = classes_of([three + four for three, four in zip(needs(8), needs(9))], 1.0)
        self.three, self.four = [size[:3] for size in sizes], [size[3:] for size in sizes]
        self.room_one, self.room_two = rooms(self.one), rooms(self.two)
        self.room_three, self.room_four = rooms(self.three), rooms(self.four)

        def branches(which_class, direction):
            pairs = [(n, case[direction]) for n, case in zip(which_class, cases)]
            found = sorted(set(pairs))
            return found, [found.index(pair) for pair in pairs]

        self.one_branches, one_at = branches(one_class, 0)
        self.two_branches, two_at = branches(two_class, 1)
        self.three_branches, three_at = branches(three_class, 2)
        self.flags = dict(
            three_class=three_class,
            one_at=one_at, two_at=two_at, three_at=three_at,
            a=[offsets(*pair)[0] for pair in PAIRS], big_a=[offsets(*pair)[1] for pair in PAIRS],
        )

        found = {}
        for n, (come, ahead, back, fine, coarse, quarters, one, two, three, four) in enumerate(cases):

            def send(exchanged, room):
                return [n for (numbers, _), size in zip(exchanged, room) for n in numbers + [-1] * (size - len(numbers))]

            def source(held, *exchanges):
                places = list(held)
                for exchanged, room in exchanges:
                    for (_, got), size in zip(exchanged, room):
                        places += got + [None] * (size - len(got))
                return {p: n for n, p in enumerate(places) if p is not None}

            first, second = source(block, (one, self.room_one)), source(fine, (two, self.room_two))
            third = source(coarse, (three, self.room_three))
            last = source(fine, (two, self.room_two), (four, self.room_four))
            out = [(l, r, c) for r in range(crows) for c in range(ccols) for l in range(2)]
            rows_of = dict(
                send_one=send(one, self.room_one),
                take_one=[first[p] for p in fine],
                send_two=send(two, self.room_two),
                take_two=[second[p] for p in quarters],
                send_three=send(three, self.room_three),
                send_four=send(four, self.room_four),
                fine_out=[last[p] for p in block],
                coarse_out=[third[p] for p in out],
            )
            for name, row in rows_of.items():
                found.setdefault(name, []).append(row)
        parts, self.at, top = [], {}, 0
        for name, lists in found.items():
            length = -(-max(len(row) for row in lists) // 128)
            part = np.full((len(PAIRS), length * 128), -1, np.float32)
            for n, row in enumerate(lists):
                part[n, : len(row)] = row
            parts.append(part.reshape(len(PAIRS), length, 128))
            self.at[name] = (top, length)
            top += length
        parts.append(np.zeros((len(PAIRS), -top % 8, 128), np.float32))
        self.table = np.concatenate(parts, axis=1)


def case_of(shifts_ref):
    t0, t1 = shifts_ref[0], shifts_ref[1]
    return jnp.where(t0 == WH - 1, t1 - 1, t0 + WH - 2)


def lookup(values, case):
    out = jnp.int32(values[0])
    for n, value in enumerate(values[1:], 1):
        out = jnp.where(case == n, value, out)
    return out


def columns_of(rows, count):
    parts = [jnp.broadcast_to(rows[j : j + 1], (128, 128)).T for j in range(-(-count // 128))]
    return stack_rows(parts)[:count]


def select_rows(index, source):
    lane = lax.broadcasted_iota(I32, (1, 128), 1).astype(F32)
    size = source.shape[0]
    pick = [jnp.where(index == lane + float(at), 1.0, 0.0).astype(BF16) for at in range(0, size, 128)]
    pick = jnp.concatenate(pick, axis=1)[:, :size]
    return jnp.dot(pick, source, preferred_element_type=F32)


def stack_rows(parts):
    return parts[0] if len(parts) == 1 else jnp.concatenate(parts, axis=0)


def layer_norm(values):
    center = jnp.mean(values, axis=-1, keepdims=True)
    values = values - center
    spread = jnp.mean(values * values, axis=-1, keepdims=True)
    return values * lax.rsqrt(spread + EPS)


def attend_windows(qkv_of, id_of, windows, inner, finish):
    lane = lax.broadcasted_iota(I32, (1, 128), 1)
    forbid = jnp.where(lane < 8, BIG, 0.0).astype(BF16)
    groups = inner // 128
    units = [(w, g) for w in range(windows) for g in range(groups)]
    scores, weights, outs = {}, {}, {}

    def score(w, g):
        key_id = id_of(w)
        not_id = (key_id - 1).astype(BF16) * forbid
        q = qkv_of(w, g * 128)
        keys = jnp.concatenate([qkv_of(w, inner + g * 128), key_id], axis=1)
        queries = []
        for h in range(4):
            mine = jnp.where((lane >= h * HD) & (lane < (h + 1) * HD), 1.0, 0.0).astype(BF16)
            queries.append(jnp.concatenate([q * mine, not_id], axis=1))
        scores[w, g] = lax.dot_general(stack_rows(queries), keys, NT, preferred_element_type=F32)

    def soften(w, g):
        s = scores.pop((w, g))
        weights[w, g] = jnp.exp2((s - jnp.max(s, axis=1, keepdims=True)) * SCALE).astype(BF16)

    def gather(w, g):
        v = qkv_of(w, 2 * inner + g * 128)
        values = jnp.concatenate([v, jnp.ones_like(v)], axis=1)
        out = jnp.dot(weights.pop((w, g)), values, preferred_element_type=F32)
        picked, total = out[:TOK, :128], out[:TOK, 128:]
        for h in range(1, 4):
            rows = slice(h * TOK, (h + 1) * TOK)
            picked = jnp.where(lane < h * HD, picked, out[rows, :128])
            total = jnp.where(lane < h * HD, total, out[rows, 128:])
        outs[w, g] = (picked / total).astype(BF16)
        if g == groups - 1:
            finish(w, jnp.concatenate([outs.pop((w, k)) for k in range(groups)], axis=1))

    for n in range(len(units) + 2):
        if n < len(units):
            score(*units[n])
        if 0 <= n - 1 < len(units):
            soften(*units[n - 1])
        if 0 <= n - 2 < len(units):
            gather(*units[n - 2])


ANY = pl.BlockSpec(memory_space=pl.ANY)
HBM = pl.BlockSpec(memory_space=pltpu.HBM)
VMEM = pl.BlockSpec(memory_space=pltpu.VMEM)
SMEM = pl.BlockSpec(memory_space=pltpu.SMEM)


def call(body, outs, args, in_specs, scratch, copies, flops, moved_bytes, vmem=8):
    args = [
        pltpu.with_memory_space_constraint(arg, spec.memory_space) for arg, spec in zip(args, in_specs, strict=True)
    ]
    spaces = [getattr(out, "memory_space", pltpu.SMEM if out.dtype == I32 else pltpu.VMEM) for out in outs]
    out_specs = [pl.BlockSpec(memory_space=space) for space in spaces]
    return pl.pallas_call(
        body,
        out_shape=outs,
        in_specs=in_specs,
        out_specs=out_specs,
        scratch_shapes=list(scratch) + [pltpu.SemaphoreType.DMA((copies,))],
        compiler_params=pltpu.CompilerParams(vmem_limit_bytes=vmem << 20),
        cost_estimate=pl.CostEstimate(flops=flops, bytes_accessed=moved_bytes, transcendentals=0),
    )(*args)


def shapes(sizes, width, space=pltpu.VMEM):
    return [space((n, width), BF16) for n in sizes]


class Copies:
    def __init__(self, sems):
        self.sems, self.used = sems, 0

    def __call__(self, src, dst):
        copy = pltpu.make_async_copy(src, dst, self.sems.at[self.used])
        self.used += 1
        copy.start()
        return copy


def lay(pieces, room):
    width = pieces[0].shape[1]

    def body(*refs):
        out_ref = refs[len(pieces)]
        at = 0
        for ref, space in zip(refs, room):
            rows = ref.shape[0]
            out_ref[at : at + rows, :] = ref[...]
            if rows < space:
                out_ref[at + rows : at + space, :] = jnp.zeros((space - rows, width), BF16)
            at += space

    return call(body, shapes([sum(room)], width), pieces, [VMEM] * 3, [], 1, 0, 1 << 18)[0]


def flat(ref):
    layers, rows, cols, width = ref.shape
    return ref[...].astype(F32).reshape(layers * rows * cols, width).astype(BF16)


def put_pieces(value, refs):
    at = 0
    for ref in refs:
        ref[...] = value[at : at + ref.shape[0]].astype(BF16)
        at += ref.shape[0]


def rows_of(plan, table_ref, name, *lead):
    top, length = plan.at[name]
    return table_ref[(*lead, slice(top, top + length), slice(None))]


def exchange(pieces, sizes, sign):
    lat, lon = lax.axis_size("lat"), lax.axis_size("lon")
    row, col, both = [piece[:size] for piece, size in zip(pieces, sizes)]
    pairs = [((i + sign) % lat * lon + (j + sign) % lon, i * lon + j) for i in range(lat) for j in range(lon)]
    col = lax.ppermute(col, "lon", [((j + sign) % lon, j) for j in range(lon)])
    both = lax.ppermute(both, ("lat", "lon"), pairs)
    row = lax.ppermute(row, "lat", [((i + sign) % lat, i) for i in range(lat)])
    return [row, col, both]


def choose(index, branches, *args):
    flat_args, tree = jax.tree.flatten(args)
    out_trees = []

    def closed(branch):
        def run(*leaves):
            out, out_tree = jax.tree.flatten(branch(*jax.tree.unflatten(tree, leaves)))
            out_trees.append(out_tree)
            return out

        return jax.make_jaxpr(run)(*flat_args)

    out = lax.cond_p.bind(index, *flat_args, branches=tuple(closed(branch) for branch in branches))
    return jax.tree.unflatten(out_trees[0], out)


FLAGS = ("three_class", "a", "big_a")


def first_pieces(shifts, tokens, plan):
    width = tokens.shape[-1]
    count = tokens.size // width
    kinds = 3

    def body(shifts_hbm, tokens_hbm, table_hbm, *refs):
        outs, refs = refs[:kinds], refs[kinds:]
        source_ref, rows_ref, flags_ref, *at_refs, shifts_ref, tokens_ref, table_ref, sems = refs
        start = Copies(sems)
        shift = start(shifts_hbm, shifts_ref)
        held = start(tokens_hbm, tokens_ref)
        table = start(table_hbm, table_ref)
        shift.wait()
        case = case_of(shifts_ref)
        for ref, name in zip(at_refs, ("one_at", "two_at", "three_at")):
            ref[0] = lookup(plan.flags[name], case)
        for n, name in enumerate(FLAGS):
            flags_ref[n] = lookup(plan.flags[name], case)
        held.wait()
        source_ref[...] = flat(tokens_ref)
        table.wait()
        rows_ref[...] = table_ref[case]
        index = columns_of(rows_of(plan, table_ref, "send_one", case), sum(plan.room_one))
        put_pieces(select_rows(index, source_ref[...]), outs)

    outs = shapes([*plan.room_one, count], width)
    outs += [pltpu.VMEM(plan.table.shape[1:], F32), pltpu.SMEM((8,), I32)]
    outs += [pltpu.SMEM((1,), I32)] * 3
    scratch = [pltpu.SMEM((2,), I32), pltpu.VMEM(tokens.shape, BF16), pltpu.VMEM(plan.table.shape, F32)]
    got = call(body, outs, [shifts, tokens, plan.table], [HBM] * 3, scratch, 3, 1 << 28, 1 << 20)
    sent, (source, rows, flags, one, two, three) = got[:kinds], got[kinds:]
    return sent, source, rows, flags, one[0], two[0], three[0]


def before_fine(flags, regions, tokens, table, weights, plan, rows, cols):
    _, lat, lon = regions.shape
    width = tokens.shape[1]
    flat_regions = regions.reshape(2 * lat, lon)
    fine, coarse = windowed(rows, cols), natural(rows // 2, cols // 2)

    def lanes(places, scale, is_fine):
        places = np.asarray([(l, scale * r, scale * c, is_fine) for l, r, c in places], np.float32)
        return np.pad(places, ((0, -len(places) % 128), (0, 0))).T.reshape(4, -1, 128)

    places = np.concatenate([lanes(fine, 1, 1), lanes(coarse, 2, 0)], axis=1)
    lines = places.shape[1]

    def body(flags_ref, rows_ref, tokens_ref, regions_hbm, places_hbm, *refs):
        weights_hbm, refs = refs[: len(weights)], refs[len(weights) :]
        id_ref, x_ref, *refs = refs
        weight_refs, (regions_ref, places_ref, sems) = refs[: len(weights)], refs[len(weights) :]
        start = Copies(sems)
        waits = [start(regions_hbm, regions_ref), start(places_hbm, places_ref)]
        later = [
            start(src.at[:, pl.ds(0, dst.shape[1])], dst) for src, dst in zip(weights_hbm, weight_refs)
        ]
        for copy in waits:
            copy.wait()
        a = flags_ref[1].astype(F32)
        big_a = 2.0 * flags_ref[2].astype(F32)
        is_fine = places_ref[3]
        d = is_fine * a + (1.0 - is_fine) * big_a
        row = places_ref[1] + d + (lax.axis_index("lat") * rows).astype(F32)
        col = places_ref[2] + 2.0 * d + (lax.axis_index("lon") * cols).astype(F32)
        wrapped = jnp.where((row < 0) | (row >= lat), 4.0, 0.0)
        row = jnp.where(row < 0, row + lat, jnp.where(row >= lat, row - lat, row))
        col = jnp.where(col < 0, col + lon, jnp.where(col >= lon, col - lon, col))
        row = row + places_ref[0] * lat

        def along(values):
            return jnp.concatenate([values[n : n + 1] for n in range(lines)], axis=1)

        line = lax.broadcasted_iota(I32, (2 * lat, 1), 0).astype(F32)
        pick = jnp.where(line == along(row), 1.0, 0.0).astype(BF16)
        known = regions_ref[...].astype(F32).astype(BF16)
        picked = lax.dot_general(known, pick, TN, preferred_element_type=F32)
        line = lax.broadcasted_iota(I32, (lon, 1), 0).astype(F32)
        ids = jnp.sum(jnp.where(line == along(col), picked, 0.0), axis=0, keepdims=True) + along(wrapped)
        for n in range(lines):
            id_ref[n : n + 1, :] = ids[:, n * 128 : (n + 1) * 128]
        take = columns_of(rows_of(plan, rows_ref, "take_one"), len(fine))
        x_ref[...] = select_rows(take, tokens_ref[...]).astype(BF16)
        for copy in later:
            copy.wait()

    outs = [pltpu.VMEM((lines, 128), F32)] + shapes([len(fine)], width)
    outs += [pltpu.VMEM((w.shape[0], min(w.shape[1], 2 * weights[1].shape[0])), BF16) for w in weights]
    scratch = [pltpu.VMEM(flat_regions.shape, I32), pltpu.VMEM(places.shape, F32)]
    args = [flags, table, tokens, flat_regions, places, *weights]
    in_specs = [SMEM, VMEM, VMEM] + [HBM] * (2 + len(weights))
    ids, x, *weights = call(body, outs, args, in_specs, scratch, 2 + len(weights), 1 << 28, 4 << 20)
    return ids, x, weights


def id_columns(lines, count):
    lane = lax.broadcasted_iota(I32, (1, 128), 1).astype(F32)
    return jnp.where(columns_of(lines, count) == lane, 1.0, 0.0).astype(BF16)


def before_coarse(flags, fine, table, weight, plan):
    own, width = fine.shape
    half = 5 * weight.shape[0] // 16

    def body(flags_ref, rows_ref, fine_ref, weight_hbm, x_ref, part_hbm, home_ref, weight_ref, part_ref, sems):
        start = Copies(sems)
        later = start(weight_hbm.at[pl.ds(0, half)], weight_ref)
        take = columns_of(rows_of(plan, rows_ref, "fine_out"), own)
        part_ref[...] = select_rows(take, fine_ref[...]).astype(BF16)
        leave = start(part_ref, part_hbm)
        take = columns_of(rows_of(plan, rows_ref, "take_two"), own)
        x_ref[...] = select_rows(take, fine_ref[...]).astype(BF16)

        @pl.when(needs_fine(flags_ref, plan))
        def _():
            index = columns_of(rows_of(plan, rows_ref, "send_four"), sum(plan.room_four))
            home_ref[...] = select_rows(index, fine_ref[...]).astype(BF16)

        leave.wait()
        later.wait()

    outs = shapes([own], width) + shapes([own], width, pltpu.HBM)
    outs += shapes([sum(plan.room_four)], width) + shapes([half], weight.shape[1])
    scratch = [pltpu.VMEM(fine.shape, BF16)]
    args = [flags, table, fine, weight]
    return call(body, outs, args, [SMEM, VMEM, VMEM, HBM], scratch, 2, 1 << 28, 4 << 20)


def needs_fine(flags_ref, plan):
    with_fine = [n for n, sizes in enumerate(plan.four) if sum(sizes)]
    return functools.reduce(jnp.logical_or, [flags_ref[0] == n for n in with_fine])


def fine_level(x_own, source, ids, w_qk, w_proj, w_qkv, rows, plan):
    count, width = x_own.shape
    inner = w_proj.shape[0]

    def body(own_ref, source_ref, ids_ref, qk_w_ref, proj_w_ref, qkv_w_hbm, rows_ref, out_ref, *refs):
        *piece_outs, x_ref, qkv_ref, id_ref, v_w_ref, sems = refs
        v_w = Copies(sems)(qkv_w_hbm.at[:, pl.ds(2 * inner, inner)], v_w_ref)
        id_ref[...] = id_columns(ids_ref[: -(-count // 128), :], count)
        take = columns_of(rows_of(plan, rows_ref, "take_one"), count) - float(count)
        x = own_ref[...].astype(F32) + select_rows(take, source_ref[...])
        x_ref[...] = x
        normed = layer_norm(x).astype(BF16)
        v_w.wait()
        qkv_ref[:, : 2 * inner] = jnp.dot(normed, qk_w_ref[...], preferred_element_type=F32).astype(BF16)
        qkv_ref[:, 2 * inner :] = jnp.dot(normed, v_w_ref[...], preferred_element_type=F32).astype(BF16)

        def window(w, carry):
            rows = pl.ds(pl.multiple_of(w * TOK, TOK), TOK)

            def finish(_, out):
                out = jnp.dot(out, proj_w_ref[...], preferred_element_type=F32)
                out_ref[rows, :] = (x_ref[rows, :] + out).astype(BF16)

            attend_windows(
                lambda _, at: qkv_ref[rows, at : at + 128], lambda _: id_ref[rows, :], 1, inner, finish
            )
            return carry

        lax.fori_loop(0, count // TOK, window, 0)
        index = columns_of(rows_of(plan, rows_ref, "send_two"), sum(plan.room_two))
        put_pieces(select_rows(index, out_ref[...]), piece_outs)

    outs = shapes([count, *plan.room_two], width)
    scratch = [
        pltpu.VMEM((count, width), F32),
        pltpu.VMEM((count, 3 * inner), BF16),
        pltpu.VMEM((count, 128), BF16),
        pltpu.VMEM((width, inner), BF16),
    ]
    args = [x_own, source, ids, w_qk, w_proj, w_qkv, rows]
    out, *sent = call(body, outs, args, [VMEM] * 5 + [HBM, VMEM], scratch, 1, 3 << 30, 6 << 20, 14)
    return out, sent


def coarse_level(flags, home, x_own, source, ids, merge_first, w_merge, w_qkv, w_proj, rows, plan):
    depth, width = w_merge.shape
    own, half = x_own.shape
    count = own // 4
    inner = w_proj.shape[0]

    def body(
        flags_ref, merge_hbm, qkv_w_hbm, proj_w_hbm, home_ref, own_ref, source_ref, ids_ref, first_ref, rows_ref, *refs
    ):
        out_ref, *piece_outs = refs[:4]
        qkv_ref, id_ref, merge_ref, qkv_w_ref, proj_w_ref, sems = refs[4:]
        start = Copies(sems)
        here = first_ref.shape[0]
        merge_w = start(merge_hbm.at[pl.ds(here, depth - here)], merge_ref)
        qkv_w = start(qkv_w_hbm, qkv_w_ref)
        proj_w = start(proj_w_hbm, proj_w_ref)
        id_ref[...] = id_columns(ids_ref[-(-own // 128) :, :], count)
        take = columns_of(rows_of(plan, rows_ref, "take_two"), 4 * count) - float(own)
        x = own_ref[...].astype(F32) + select_rows(take, source_ref[...])
        x = jnp.concatenate([x[n * count : (n + 1) * count] for n in range(4)], axis=1)
        stacked = layer_norm(x).astype(BF16)
        merge_w.wait()
        merged = jnp.dot(stacked[:, :here], first_ref[...], preferred_element_type=F32)
        merged = merged + jnp.dot(stacked[:, here:], merge_ref[...], preferred_element_type=F32)
        merged = merged.astype(BF16).astype(F32)
        normed = layer_norm(merged).astype(BF16)
        qkv_w.wait()
        proj_w.wait()
        qkv_ref[...] = jnp.dot(normed, qkv_w_ref[...], preferred_element_type=F32).astype(BF16)

        def finish(w, out):
            out = jnp.dot(out, proj_w_ref[...], preferred_element_type=F32)
            out_ref[...] = (merged + out).astype(BF16)

        attend_windows(lambda w, at: qkv_ref[:, at : at + 128], lambda w: id_ref[...], 1, inner, finish)
        sent = select_rows(columns_of(rows_of(plan, rows_ref, "send_three"), sum(plan.room_three)), out_ref[...])
        sent = sent.astype(BF16)
        for n, sizes in enumerate(plan.three):

            @pl.when(flags_ref[0] == n)
            def _():
                at = 0
                for ref, size, space in zip(piece_outs, sizes, plan.room_three):
                    ref[:size, :] = sent[at : at + size, :half]
                    ref[size : 2 * size, :] = sent[at : at + size, half:]
                    at += space

        for n, fine_sizes in enumerate(plan.four):
            if sum(fine_sizes):

                @pl.when(flags_ref[0] == n)
                def _():
                    at = 0
                    for ref, size, more, space in zip(piece_outs, plan.three[n], fine_sizes, plan.room_four):
                        ref[2 * size : 2 * size + more, :] = home_ref[at : at + more, :]
                        at += space

    most = [max(2 * three[k] + four[k] for three, four in zip(plan.three, plan.four)) for k in range(3)]
    outs = shapes([count], width) + shapes(most, half)
    scratch = [pltpu.VMEM((count, 3 * inner), BF16)]
    shapes_in = [(count, 128), (depth - merge_first.shape[0], width), w_qkv.shape, w_proj.shape]
    scratch += [pltpu.VMEM(shape, BF16) for shape in shapes_in]
    args = [flags, w_merge, w_qkv, w_proj, home, x_own, source, ids, merge_first, rows]
    in_specs = [SMEM] + [HBM] * 3 + [VMEM] * (len(args) - 4)
    out, *sent = call(body, outs, args, in_specs, scratch, 3, 3 << 30, 12 << 20, 24)
    return out, sent


def fine_output(part, source, rows, plan, block_rows, block_cols, partial):
    own, width = part.shape

    def body(part_hbm, source_ref, rows_ref, out_ref, part_ref, stage_ref, sems):
        start = Copies(sems)
        cuts = [pl.ds(at, TOK) for at in range(0, own, TOK)]
        held = [start(part_hbm.at[cut], part_ref.at[cut]) for cut in cuts]
        take = columns_of(rows_of(plan, rows_ref, "fine_out"), own) - float(own)
        leave = []
        for n, (cut, copy) in enumerate(zip(cuts, held)):
            got = select_rows(take[n * TOK : (n + 1) * TOK], source_ref[...])
            copy.wait()
            out = part_ref[cut, :].astype(F32) + got
            if partial:
                out_ref[cut, :] = out.astype(BF16)
            else:
                lines = TOK // block_cols
                layer, line = divmod(n * lines, block_rows)
                there = (layer, pl.ds(line, lines))
                stage_ref[there] = out.reshape(lines, block_cols, width).astype(BF16)
                leave.append(start(stage_ref.at[there], out_ref.at[there]))
        for copy in leave:
            copy.wait()

    shape = (2, block_rows, block_cols, width)
    outs = shapes([own], width) if partial else [pltpu.HBM(shape, BF16)]
    scratch = [pltpu.VMEM(part.shape, BF16), pltpu.VMEM(shape, BF16)]
    return call(body, outs, [part, source, rows], [HBM, VMEM, VMEM], scratch, 2 * own // TOK, 1 << 30, 4 << 20)[0]


def coarse_output(coarse, got, rows, which, plan, block_rows, block_cols, part=None):
    own, width = coarse.shape
    half = width // 2
    sizes, more = plan.three[which], plan.four[which]
    parts = [] if part is None else [part]

    def padded(parts, sizes, room):
        out = []
        for value, size, space in zip(parts, sizes, room):
            out.append(value)
            if size < space:
                out.append(jnp.zeros((space - size, value.shape[1]), F32))
        return out

    def body(coarse_ref, *refs):
        got_refs, refs = refs[:3], refs[3:]
        part_refs, (rows_ref, out_ref, *fine_outs, _) = refs[: len(parts)], refs[len(parts) :]
        got = [ref[...].astype(F32) for ref in got_refs]
        back = [jnp.concatenate([x[:size], x[size : 2 * size]], axis=1) for x, size in zip(got, sizes)]
        source = stack_rows([coarse_ref[...].astype(F32)] + padded(back, sizes, plan.room_three))
        out = select_rows(columns_of(rows_of(plan, rows_ref, "coarse_out"), own), source.astype(BF16)).astype(BF16)
        for n in range(own // 2):
            out_ref[n // block_cols, n % block_cols] = out[2 * n : 2 * n + 2]
        for part_ref, fine_ref in zip(part_refs, fine_outs):
            fine = stack_rows(padded([x[2 * size :] for x, size in zip(got, sizes)], more, plan.room_four))
            base = part_ref.shape[0] + sum(plan.room_two)
            take = columns_of(rows_of(plan, rows_ref, "fine_out"), part_ref.shape[0]) - float(base)
            out = part_ref[...].astype(F32) + select_rows(take, fine.astype(BF16))
            fine_ref[...] = out.reshape(fine_ref.shape).astype(BF16)

    outs = [jax.ShapeDtypeStruct((block_rows, block_cols, 2, width), BF16)]
    outs += [jax.ShapeDtypeStruct((2, 2 * block_rows, 2 * block_cols, half), BF16) for _ in parts]
    args = [coarse, *got, *parts, rows]
    out, *fine = call(body, outs, args, [VMEM] * len(args), [], 1, 1 << 28, 1 << 20)
    return out.transpose(2, 0, 1, 3), *fine


def on_device(tokens, regions, shifts, fine_qkv, fine_proj, merge_weight, coarse_qkv, coarse_proj):
    _, rows, cols, _ = tokens.shape
    plan = Plan(rows, cols)

    def first(which, sign, sent, *args):
        got = exchange(sent, plan.one[which], sign)
        return lay(got, plan.room_one), before_fine(*args, plan, rows, cols)

    def second(which, sign, sent, *args):
        got = exchange(sent, plan.two[which], sign)
        return lay(got, plan.room_two), before_coarse(*args, plan)

    def third(which, sign, sent, part, source, coarse, table):
        sizes = [2 * n + m for n, m in zip(plan.three[which], plan.four[which])]
        got = exchange(sent, sizes, sign)
        partial = sum(plan.four[which]) > 0
        fine_out = fine_output(part, source, table, plan, rows, cols, partial)
        place = (table, which, plan, rows // 2, cols // 2)
        if partial:
            coarse_out, fine_out = coarse_output(coarse, got, *place, part=fine_out)
        else:
            (coarse_out,) = coarse_output(coarse, got, *place)
        return fine_out, coarse_out

    def branches(stage, pairs):
        return [functools.partial(stage, which, sign) for which, sign in pairs]

    sent, source, table, flags, one, two, three = first_pieces(shifts, tokens, plan)
    got, (ids, x, weights) = choose(
        one, branches(first, plan.one_branches), sent, flags, regions, source, table, [fine_qkv, fine_proj]
    )
    fine, sent = fine_level(x, got, ids, *weights, fine_qkv, table, plan)
    got, (x, part, home, merge_first) = choose(
        two, branches(second, plan.two_branches), sent, flags, fine, table, merge_weight
    )
    coarse, sent = coarse_level(
        flags, home, x, got, ids, merge_first, merge_weight, coarse_qkv, coarse_proj, table, plan
    )
    return choose(three, branches(third, plan.three_branches), sent, part, got, coarse, table)


def solution(mesh):
    return jax.shard_map(
        on_device,
        mesh=mesh,
        in_specs=(P(None, "lat", "lon", None), P(), P(), P(), P(), P(), P(), P()),
        out_specs=(P(None, "lat", "lon", None), P(None, "lat", "lon", None)),
        check_vma=False,
    )
```

```python
import functools

import jax
import jax.numpy as jnp
import numpy as np
from jax import lax
from jax.experimental import pallas as pl
from jax.experimental.pallas import tpu as pltpu
from jax.sharding import PartitionSpec as P

HD = 32
WH = 6
WW = 12
TOK = 2 * WH * WW
EPS = 1e-05
BIG = 1e30
SCALE = float(np.log2(np.e) / np.sqrt(HD))

NT = (((1,), (1,)), ((), ()))
TN = (((0,), (0,)), ((), ()))
F32 = jnp.float32
BF16 = jnp.bfloat16
I32 = jnp.int32

PAIRS = [(WH - 1, t) for t in range(1, WH)] + [(t, WH - 1) for t in range(1, WH - 1)]


def up16(count):
    return -(-count // 16) * 16


def natural(rows, cols):
    return [(l, r, c) for l in range(2) for r in range(rows) for c in range(cols)]


def windowed(rows, cols):
    return [
        (l, wr * WH + r, wc * WW + c)
        for wr in range(rows // WH)
        for wc in range(cols // WW)
        for l in range(2)
        for r in range(WH)
        for c in range(WW)
    ]


def moved(order, d):
    return [(l, r + d, c + 2 * d) for l, r, c in order]


def exchange_places(held, wanted, rows, cols, sign):
    at = {place: n for n, place in enumerate(held)}
    found = []
    for dr, dc in ((sign, 0), (0, sign), (sign, sign)):
        numbers, places = [], []
        for l, r, c in sorted(set(wanted) - set(held)):
            n = at.get((l, r - dr * rows, c - dc * cols))
            if n is not None:
                numbers.append(n)
                places.append((l, r, c))
        found.append((numbers, places))
    return found


def offsets(t0, t1):
    a = t0 if t0 <= 2 else t0 - WH
    big_a = t1 if t1 <= 2 else t1 - WH
    ahead = 1 if 2 * big_a > a or 2 * big_a - a == 0 and a < 0 else -1
    return a, big_a, ahead


def classes_of(needs, slack):
    rounded = [tuple(-(-size // 8) * 8 for size in need) for need in needs]
    heavy = [sum(need[1:3]) * 2 + sum(need[4:]) for need in rounded]
    limits = []
    for size in sorted(set(heavy)):
        if not limits or size > limits[-1][0] * slack:
            limits.append([size, size])
        limits[-1][1] = size
    which = [next(n for n, limit in enumerate(limits) if size <= limit[1]) for size in heavy]
    sizes = [
        [max(need[k] for need, w in zip(rounded, which) if w == n) for k in range(len(needs[0]))]
        for n in range(len(limits))
    ]
    return sizes, which


def rooms(sizes):
    return [up16(max(size[k] for size in sizes)) for k in range(len(sizes[0]))]


class Plan:
    def __init__(self, rows, cols):
        crows, ccols = rows // 2, cols // 2
        block, cblock = natural(rows, cols), natural(crows, ccols)
        cases = []
        for t0, t1 in PAIRS:
            a, big_a, ahead = offsets(t0, t1)
            fine = moved(windowed(rows, cols), a)
            coarse = moved(cblock, big_a)
            quarters = [
                (l, 2 * r + dr, 2 * c + dc)
                for dr, dc in ((0, 0), (1, 0), (0, 1), (1, 1))
                for l, r, c in coarse
            ]
            come = 1 if a > 0 else -1
            one = exchange_places(block, fine, rows, cols, come)
            home = [p for p in block if p not in set(fine)]
            wanted = quarters + (home if come == -ahead else [])
            two = exchange_places(fine, wanted, rows, cols, ahead)
            back = 1 if big_a < 0 else -1
            three = exchange_places(coarse, cblock, crows, ccols, back)
            got = set(fine).union(*[places for _, places in two])
            four = exchange_places(fine, [p for p in block if p not in got], rows, cols, back)
            cases.append((come, ahead, back, fine, coarse, quarters, one, two, three, four))

        def needs(which):
            return [[len(numbers) for numbers, _ in case[which]] for case in cases]

        self.one, one_class = classes_of(needs(6), 1.15)
        self.two, two_class = classes_of(needs(7), 1.15)
        sizes, three_class = classes_of([three + four for three, four in zip(needs(8), needs(9))], 1.0)
        self.three, self.four = [size[:3] for size in sizes], [size[3:] for size in sizes]
        self.room_one, self.room_two = rooms(self.one), rooms(self.two)
        self.room_three, self.room_four = rooms(self.three), rooms(self.four)

        def branches(which_class, direction):
            pairs = [(n, case[direction]) for n, case in zip(which_class, cases)]
            found = sorted(set(pairs))
            return found, [found.index(pair) for pair in pairs]

        self.one_branches, one_at = branches(one_class, 0)
        self.two_branches, two_at = branches(two_class, 1)
        self.three_branches, three_at = branches(three_class, 2)
        self.flags = dict(
            three_class=three_class,
            one_at=one_at, two_at=two_at, three_at=three_at,
            a=[offsets(*pair)[0] for pair in PAIRS], big_a=[offsets(*pair)[1] for pair in PAIRS],
        )

        found = {}
        for n, (come, ahead, back, fine, coarse, quarters, one, two, three, four) in enumerate(cases):

            def send(exchanged, room):
                return [n for (numbers, _), size in zip(exchanged, room) for n in numbers + [-1] * (size - len(numbers))]

            def source(held, *exchanges):
                places = list(held)
                for exchanged, room in exchanges:
                    for (_, got), size in zip(exchanged, room):
                        places += got + [None] * (size - len(got))
                return {p: n for n, p in enumerate(places) if p is not None}

            first, second = source(block, (one, self.room_one)), source(fine, (two, self.room_two))
            third = source(coarse, (three, self.room_three))
            last = source(fine, (two, self.room_two), (four, self.room_four))
            out = [(l, r, c) for r in range(crows) for c in range(ccols) for l in range(2)]
            rows_of = dict(
                send_one=send(one, self.room_one),
                take_one=[first[p] for p in fine],
                send_two=send(two, self.room_two),
                take_two=[second[p] for p in quarters],
                send_three=send(three, self.room_three),
                send_four=send(four, self.room_four),
                fine_out=[last[p] for p in block],
                coarse_out=[third[p] for p in out],
            )
            for name, row in rows_of.items():
                found.setdefault(name, []).append(row)
        parts, self.at, top = [], {}, 0
        for name, lists in found.items():
            length = -(-max(len(row) for row in lists) // 128)
            part = np.full((len(PAIRS), length * 128), -1, np.float32)
            for n, row in enumerate(lists):
                part[n, : len(row)] = row
            parts.append(part.reshape(len(PAIRS), length, 128))
            self.at[name] = (top, length)
            top += length
        parts.append(np.zeros((len(PAIRS), -top % 8, 128), np.float32))
        self.table = np.concatenate(parts, axis=1)


def case_of(shifts_ref):
    t0, t1 = shifts_ref[0], shifts_ref[1]
    return jnp.where(t0 == WH - 1, t1 - 1, t0 + WH - 2)


def lookup(values, case):
    out = jnp.int32(values[0])
    for n, value in enumerate(values[1:], 1):
        out = jnp.where(case == n, value, out)
    return out


def columns_of(rows, count):
    parts = [jnp.broadcast_to(rows[j : j + 1], (128, 128)).T for j in range(-(-count // 128))]
    return stack_rows(parts)[:count]


def select_rows(index, source):
    lane = lax.broadcasted_iota(I32, (1, 128), 1).astype(F32)
    size = source.shape[0]
    pick = [jnp.where(index == lane + float(at), 1.0, 0.0).astype(BF16) for at in range(0, size, 128)]
    pick = jnp.concatenate(pick, axis=1)[:, :size]
    return jnp.dot(pick, source, preferred_element_type=F32)


def stack_rows(parts):
    return parts[0] if len(parts) == 1 else jnp.concatenate(parts, axis=0)


def layer_norm(values):
    center = jnp.mean(values, axis=-1, keepdims=True)
    values = values - center
    spread = jnp.mean(values * values, axis=-1, keepdims=True)
    return values * lax.rsqrt(spread + EPS)


def attend_windows(qkv_of, id_of, windows, inner, finish):
    lane = lax.broadcasted_iota(I32, (1, 128), 1)
    forbid = jnp.where(lane < 8, BIG, 0.0).astype(BF16)
    groups = inner // 128
    units = [(w, g) for w in range(windows) for g in range(groups)]
    scores, weights, outs = {}, {}, {}

    def score(w, g):
        key_id = id_of(w)
        not_id = (key_id - 1).astype(BF16) * forbid
        q = qkv_of(w, g * 128)
        keys = jnp.concatenate([qkv_of(w, inner + g * 128), key_id], axis=1)
        queries = []
        for h in range(4):
            mine = jnp.where((lane >= h * HD) & (lane < (h + 1) * HD), 1.0, 0.0).astype(BF16)
            queries.append(jnp.concatenate([q * mine, not_id], axis=1))
        scores[w, g] = lax.dot_general(stack_rows(queries), keys, NT, preferred_element_type=F32)

    def soften(w, g):
        s = scores.pop((w, g))
        weights[w, g] = jnp.exp2((s - jnp.max(s, axis=1, keepdims=True)) * SCALE).astype(BF16)

    def gather(w, g):
        v = qkv_of(w, 2 * inner + g * 128)
        values = jnp.concatenate([v, jnp.ones_like(v)], axis=1)
        out = jnp.dot(weights.pop((w, g)), values, preferred_element_type=F32)
        picked, total = out[:TOK, :128], out[:TOK, 128:]
        for h in range(1, 4):
            rows = slice(h * TOK, (h + 1) * TOK)
            picked = jnp.where(lane < h * HD, picked, out[rows, :128])
            total = jnp.where(lane < h * HD, total, out[rows, 128:])
        outs[w, g] = (picked / total).astype(BF16)
        if g == groups - 1:
            finish(w, jnp.concatenate([outs.pop((w, k)) for k in range(groups)], axis=1))

    pairs = [units[n : n + 2] for n in range(0, len(units), 2)]
    for n in range(len(pairs) + 2):
        if n < len(pairs):
            for unit in pairs[n]:
                score(*unit)
        if 0 <= n - 1 < len(pairs):
            for unit in pairs[n - 1]:
                soften(*unit)
        if 0 <= n - 2 < len(pairs):
            for unit in pairs[n - 2]:
                gather(*unit)


ANY = pl.BlockSpec(memory_space=pl.ANY)
HBM = pl.BlockSpec(memory_space=pltpu.HBM)
VMEM = pl.BlockSpec(memory_space=pltpu.VMEM)
SMEM = pl.BlockSpec(memory_space=pltpu.SMEM)


def call(body, outs, args, in_specs, scratch, copies, flops, moved_bytes, vmem=8):
    args = [
        pltpu.with_memory_space_constraint(arg, spec.memory_space) for arg, spec in zip(args, in_specs, strict=True)
    ]
    spaces = [getattr(out, "memory_space", pltpu.SMEM if out.dtype == I32 else pltpu.VMEM) for out in outs]
    out_specs = [pl.BlockSpec(memory_space=space) for space in spaces]
    return pl.pallas_call(
        body,
        out_shape=outs,
        in_specs=in_specs,
        out_specs=out_specs,
        scratch_shapes=list(scratch) + [pltpu.SemaphoreType.DMA((copies,))],
        compiler_params=pltpu.CompilerParams(vmem_limit_bytes=vmem << 20),
        cost_estimate=pl.CostEstimate(flops=flops, bytes_accessed=moved_bytes, transcendentals=0),
    )(*args)


def shapes(sizes, width, space=pltpu.VMEM):
    return [space((n, width), BF16) for n in sizes]


class Copies:
    def __init__(self, sems):
        self.sems, self.used = sems, 0

    def __call__(self, src, dst):
        copy = pltpu.make_async_copy(src, dst, self.sems.at[self.used])
        self.used += 1
        copy.start()
        return copy


def lay(pieces, room):
    width = pieces[0].shape[1]

    def body(*refs):
        out_ref = refs[len(pieces)]
        at = 0
        for ref, space in zip(refs, room):
            rows = ref.shape[0]
            out_ref[at : at + rows, :] = ref[...]
            if rows < space:
                out_ref[at + rows : at + space, :] = jnp.zeros((space - rows, width), BF16)
            at += space

    return call(body, shapes([sum(room)], width), pieces, [VMEM] * 3, [], 1, 0, 1 << 18)[0]


def flat(ref):
    layers, rows, cols, width = ref.shape
    return ref[...].astype(F32).reshape(layers * rows * cols, width).astype(BF16)


def put_pieces(value, refs):
    at = 0
    for ref in refs:
        ref[...] = value[at : at + ref.shape[0]].astype(BF16)
        at += ref.shape[0]


def rows_of(plan, table_ref, name, *lead):
    top, length = plan.at[name]
    return table_ref[(*lead, slice(top, top + length), slice(None))]


def exchange(pieces, sizes, sign):
    lat, lon = lax.axis_size("lat"), lax.axis_size("lon")
    row, col, both = [piece[:size] for piece, size in zip(pieces, sizes)]
    pairs = [((i + sign) % lat * lon + (j + sign) % lon, i * lon + j) for i in range(lat) for j in range(lon)]
    col = lax.ppermute(col, "lon", [((j + sign) % lon, j) for j in range(lon)])
    both = lax.ppermute(both, ("lat", "lon"), pairs)
    row = lax.ppermute(row, "lat", [((i + sign) % lat, i) for i in range(lat)])
    return [row, col, both]


def choose(index, branches, *args):
    flat_args, tree = jax.tree.flatten(args)
    out_trees = []

    def closed(branch):
        def run(*leaves):
            out, out_tree = jax.tree.flatten(branch(*jax.tree.unflatten(tree, leaves)))
            out_trees.append(out_tree)
            return out

        return jax.make_jaxpr(run)(*flat_args)

    out = lax.cond_p.bind(index, *flat_args, branches=tuple(closed(branch) for branch in branches))
    return jax.tree.unflatten(out_trees[0], out)


FLAGS = ("three_class", "a", "big_a")


def first_pieces(shifts, tokens, plan):
    width = tokens.shape[-1]
    count = tokens.size // width
    kinds = 3

    def body(shifts_hbm, tokens_hbm, table_hbm, *refs):
        outs, refs = refs[:kinds], refs[kinds:]
        source_ref, rows_ref, flags_ref, *at_refs, shifts_ref, tokens_ref, table_ref, sems = refs
        start = Copies(sems)
        shift = start(shifts_hbm, shifts_ref)
        held = start(tokens_hbm, tokens_ref)
        table = start(table_hbm, table_ref)
        shift.wait()
        case = case_of(shifts_ref)
        for ref, name in zip(at_refs, ("one_at", "two_at", "three_at")):
            ref[0] = lookup(plan.flags[name], case)
        for n, name in enumerate(FLAGS):
            flags_ref[n] = lookup(plan.flags[name], case)
        held.wait()
        source_ref[...] = flat(tokens_ref)
        table.wait()
        rows_ref[...] = table_ref[case]
        index = columns_of(rows_of(plan, table_ref, "send_one", case), sum(plan.room_one))
        put_pieces(select_rows(index, source_ref[...]), outs)

    outs = shapes([*plan.room_one, count], width)
    outs += [pltpu.VMEM(plan.table.shape[1:], F32), pltpu.SMEM((8,), I32)]
    outs += [pltpu.SMEM((1,), I32)] * 3
    scratch = [pltpu.SMEM((2,), I32), pltpu.VMEM(tokens.shape, BF16), pltpu.VMEM(plan.table.shape, F32)]
    got = call(body, outs, [shifts, tokens, plan.table], [HBM] * 3, scratch, 3, 1 << 28, 1 << 20)
    sent, (source, rows, flags, one, two, three) = got[:kinds], got[kinds:]
    return sent, source, rows, flags, one[0], two[0], three[0]


def before_fine(flags, regions, tokens, table, weights, plan, rows, cols):
    _, lat, lon = regions.shape
    width = tokens.shape[1]
    flat_regions = regions.reshape(2 * lat, lon)
    fine, coarse = windowed(rows, cols), natural(rows // 2, cols // 2)

    def lanes(places, scale, is_fine):
        places = np.asarray([(l, scale * r, scale * c, is_fine) for l, r, c in places], np.float32)
        return np.pad(places, ((0, -len(places) % 128), (0, 0))).T.reshape(4, -1, 128)

    places = np.concatenate([lanes(fine, 1, 1), lanes(coarse, 2, 0)], axis=1)
    lines = places.shape[1]

    def body(flags_ref, rows_ref, tokens_ref, regions_hbm, places_hbm, *refs):
        weights_hbm, refs = refs[: len(weights)], refs[len(weights) :]
        id_ref, x_ref, *refs = refs
        weight_refs, (regions_ref, places_ref, sems) = refs[: len(weights)], refs[len(weights) :]
        start = Copies(sems)
        waits = [start(regions_hbm, regions_ref), start(places_hbm, places_ref)]
        later = [
            start(src.at[:, pl.ds(0, dst.shape[1])], dst) for src, dst in zip(weights_hbm, weight_refs)
        ]
        for copy in waits:
            copy.wait()
        a = flags_ref[1].astype(F32)
        big_a = 2.0 * flags_ref[2].astype(F32)
        is_fine = places_ref[3]
        d = is_fine * a + (1.0 - is_fine) * big_a
        row = places_ref[1] + d + (lax.axis_index("lat") * rows).astype(F32)
        col = places_ref[2] + 2.0 * d + (lax.axis_index("lon") * cols).astype(F32)
        wrapped = jnp.where((row < 0) | (row >= lat), 4.0, 0.0)
        row = jnp.where(row < 0, row + lat, jnp.where(row >= lat, row - lat, row))
        col = jnp.where(col < 0, col + lon, jnp.where(col >= lon, col - lon, col))
        row = row + places_ref[0] * lat

        def along(values):
            return jnp.concatenate([values[n : n + 1] for n in range(lines)], axis=1)

        line = lax.broadcasted_iota(I32, (2 * lat, 1), 0).astype(F32)
        pick = jnp.where(line == along(row), 1.0, 0.0).astype(BF16)
        known = regions_ref[...].astype(F32).astype(BF16)
        picked = lax.dot_general(known, pick, TN, preferred_element_type=F32)
        line = lax.broadcasted_iota(I32, (lon, 1), 0).astype(F32)
        ids = jnp.sum(jnp.where(line == along(col), picked, 0.0), axis=0, keepdims=True) + along(wrapped)
        for n in range(lines):
            id_ref[n : n + 1, :] = ids[:, n * 128 : (n + 1) * 128]
        take = columns_of(rows_of(plan, rows_ref, "take_one"), len(fine))
        x_ref[...] = select_rows(take, tokens_ref[...]).astype(BF16)
        for copy in later:
            copy.wait()

    outs = [pltpu.VMEM((lines, 128), F32)] + shapes([len(fine)], width)
    outs += [pltpu.VMEM((w.shape[0], min(w.shape[1], 2 * weights[1].shape[0])), BF16) for w in weights]
    scratch = [pltpu.VMEM(flat_regions.shape, I32), pltpu.VMEM(places.shape, F32)]
    args = [flags, table, tokens, flat_regions, places, *weights]
    in_specs = [SMEM, VMEM, VMEM] + [HBM] * (2 + len(weights))
    ids, x, *weights = call(body, outs, args, in_specs, scratch, 2 + len(weights), 1 << 28, 4 << 20)
    return ids, x, weights


def id_columns(lines, count):
    lane = lax.broadcasted_iota(I32, (1, 128), 1).astype(F32)
    return jnp.where(columns_of(lines, count) == lane, 1.0, 0.0).astype(BF16)


def before_coarse(flags, fine, table, weight, plan):
    own, width = fine.shape
    half = 5 * weight.shape[0] // 16

    def body(flags_ref, rows_ref, fine_ref, weight_hbm, x_ref, part_hbm, home_ref, weight_ref, part_ref, sems):
        start = Copies(sems)
        later = start(weight_hbm.at[pl.ds(0, half)], weight_ref)
        take = columns_of(rows_of(plan, rows_ref, "fine_out"), own)
        part_ref[...] = select_rows(take, fine_ref[...]).astype(BF16)
        leave = start(part_ref, part_hbm)
        take = columns_of(rows_of(plan, rows_ref, "take_two"), own)
        x_ref[...] = select_rows(take, fine_ref[...]).astype(BF16)

        @pl.when(needs_fine(flags_ref, plan))
        def _():
            index = columns_of(rows_of(plan, rows_ref, "send_four"), sum(plan.room_four))
            home_ref[...] = select_rows(index, fine_ref[...]).astype(BF16)

        leave.wait()
        later.wait()

    outs = shapes([own], width) + shapes([own], width, pltpu.HBM)
    outs += shapes([sum(plan.room_four)], width) + shapes([half], weight.shape[1])
    scratch = [pltpu.VMEM(fine.shape, BF16)]
    args = [flags, table, fine, weight]
    return call(body, outs, args, [SMEM, VMEM, VMEM, HBM], scratch, 2, 1 << 28, 4 << 20)


def needs_fine(flags_ref, plan):
    with_fine = [n for n, sizes in enumerate(plan.four) if sum(sizes)]
    return functools.reduce(jnp.logical_or, [flags_ref[0] == n for n in with_fine])


def fine_level(x_own, source, ids, w_qk, w_proj, w_qkv, rows, plan):
    count, width = x_own.shape
    inner = w_proj.shape[0]

    def body(own_ref, source_ref, ids_ref, qk_w_ref, proj_w_ref, qkv_w_hbm, rows_ref, out_ref, *refs):
        *piece_outs, x_ref, qkv_ref, id_ref, v_w_ref, sems = refs
        v_w = Copies(sems)(qkv_w_hbm.at[:, pl.ds(2 * inner, inner)], v_w_ref)
        id_ref[...] = id_columns(ids_ref[: -(-count // 128), :], count)
        take = columns_of(rows_of(plan, rows_ref, "take_one"), count) - float(count)
        x = own_ref[...].astype(F32) + select_rows(take, source_ref[...])
        x_ref[...] = x
        normed = layer_norm(x).astype(BF16)
        v_w.wait()
        qkv_ref[:, : 2 * inner] = jnp.dot(normed, qk_w_ref[...], preferred_element_type=F32).astype(BF16)
        qkv_ref[:, 2 * inner :] = jnp.dot(normed, v_w_ref[...], preferred_element_type=F32).astype(BF16)

        def finish(w, out):
            at = slice(w * TOK, (w + 1) * TOK)
            out = jnp.dot(out, proj_w_ref[...], preferred_element_type=F32)
            out_ref[at, :] = (x_ref[at, :] + out).astype(BF16)

        attend_windows(
            lambda w, at: qkv_ref[w * TOK : (w + 1) * TOK, at : at + 128],
            lambda w: id_ref[w * TOK : (w + 1) * TOK, :],
            count // TOK,
            inner,
            finish,
        )
        index = columns_of(rows_of(plan, rows_ref, "send_two"), sum(plan.room_two))
        put_pieces(select_rows(index, out_ref[...]), piece_outs)

    outs = shapes([count, *plan.room_two], width)
    scratch = [
        pltpu.VMEM((count, width), F32),
        pltpu.VMEM((count, 3 * inner), BF16),
        pltpu.VMEM((count, 128), BF16),
        pltpu.VMEM((width, inner), BF16),
    ]
    args = [x_own, source, ids, w_qk, w_proj, w_qkv, rows]
    out, *sent = call(body, outs, args, [VMEM] * 5 + [HBM, VMEM], scratch, 1, 3 << 30, 6 << 20, 14)
    return out, sent


def coarse_level(flags, home, x_own, source, ids, merge_first, w_merge, w_qkv, w_proj, rows, plan):
    depth, width = w_merge.shape
    own, half = x_own.shape
    count = own // 4
    inner = w_proj.shape[0]

    def body(
        flags_ref, merge_hbm, qkv_w_hbm, proj_w_hbm, home_ref, own_ref, source_ref, ids_ref, first_ref, rows_ref, *refs
    ):
        out_ref, *piece_outs = refs[:4]
        qkv_ref, id_ref, merge_ref, qkv_w_ref, proj_w_ref, sems = refs[4:]
        start = Copies(sems)
        here = first_ref.shape[0]
        merge_w = start(merge_hbm.at[pl.ds(here, depth - here)], merge_ref)
        qkv_w = start(qkv_w_hbm, qkv_w_ref)
        proj_w = start(proj_w_hbm, proj_w_ref)
        id_ref[...] = id_columns(ids_ref[-(-own // 128) :, :], count)
        take = columns_of(rows_of(plan, rows_ref, "take_two"), 4 * count) - float(own)
        x = own_ref[...].astype(F32) + select_rows(take, source_ref[...])
        x = jnp.concatenate([x[n * count : (n + 1) * count] for n in range(4)], axis=1)
        stacked = layer_norm(x).astype(BF16)
        merge_w.wait()
        merged = jnp.dot(stacked[:, :here], first_ref[...], preferred_element_type=F32)
        merged = merged + jnp.dot(stacked[:, here:], merge_ref[...], preferred_element_type=F32)
        merged = merged.astype(BF16).astype(F32)
        normed = layer_norm(merged).astype(BF16)
        qkv_w.wait()
        proj_w.wait()
        qkv_ref[...] = jnp.dot(normed, qkv_w_ref[...], preferred_element_type=F32).astype(BF16)

        def finish(w, out):
            out = jnp.dot(out, proj_w_ref[...], preferred_element_type=F32)
            out_ref[...] = (merged + out).astype(BF16)

        attend_windows(lambda w, at: qkv_ref[:, at : at + 128], lambda w: id_ref[...], 1, inner, finish)
        sent = select_rows(columns_of(rows_of(plan, rows_ref, "send_three"), sum(plan.room_three)), out_ref[...])
        sent = sent.astype(BF16)
        for n, sizes in enumerate(plan.three):

            @pl.when(flags_ref[0] == n)
            def _():
                at = 0
                for ref, size, space in zip(piece_outs, sizes, plan.room_three):
                    ref[:size, :] = sent[at : at + size, :half]
                    ref[size : 2 * size, :] = sent[at : at + size, half:]
                    at += space

        for n, fine_sizes in enumerate(plan.four):
            if sum(fine_sizes):

                @pl.when(flags_ref[0] == n)
                def _():
                    at = 0
                    for ref, size, more, space in zip(piece_outs, plan.three[n], fine_sizes, plan.room_four):
                        ref[2 * size : 2 * size + more, :] = home_ref[at : at + more, :]
                        at += space

    most = [max(2 * three[k] + four[k] for three, four in zip(plan.three, plan.four)) for k in range(3)]
    outs = shapes([count], width) + shapes(most, half)
    scratch = [pltpu.VMEM((count, 3 * inner), BF16)]
    shapes_in = [(count, 128), (depth - merge_first.shape[0], width), w_qkv.shape, w_proj.shape]
    scratch += [pltpu.VMEM(shape, BF16) for shape in shapes_in]
    args = [flags, w_merge, w_qkv, w_proj, home, x_own, source, ids, merge_first, rows]
    in_specs = [SMEM] + [HBM] * 3 + [VMEM] * (len(args) - 4)
    out, *sent = call(body, outs, args, in_specs, scratch, 3, 3 << 30, 12 << 20, 24)
    return out, sent


def fine_output(part, source, rows, plan, block_rows, block_cols, partial):
    own, width = part.shape

    def body(part_hbm, source_ref, rows_ref, out_ref, part_ref, stage_ref, sems):
        start = Copies(sems)
        cuts = [pl.ds(at, TOK) for at in range(0, own, TOK)]
        held = [start(part_hbm.at[cut], part_ref.at[cut]) for cut in cuts]
        take = columns_of(rows_of(plan, rows_ref, "fine_out"), own) - float(own)
        leave = []
        for n, (cut, copy) in enumerate(zip(cuts, held)):
            got = select_rows(take[n * TOK : (n + 1) * TOK], source_ref[...])
            copy.wait()
            out = part_ref[cut, :].astype(F32) + got
            if partial:
                out_ref[cut, :] = out.astype(BF16)
            else:
                lines = TOK // block_cols
                layer, line = divmod(n * lines, block_rows)
                there = (layer, pl.ds(line, lines))
                stage_ref[there] = out.reshape(lines, block_cols, width).astype(BF16)
                leave.append(start(stage_ref.at[there], out_ref.at[there]))
        for copy in leave:
            copy.wait()

    shape = (2, block_rows, block_cols, width)
    outs = shapes([own], width) if partial else [pltpu.HBM(shape, BF16)]
    scratch = [pltpu.VMEM(part.shape, BF16), pltpu.VMEM(shape, BF16)]
    return call(body, outs, [part, source, rows], [HBM, VMEM, VMEM], scratch, 2 * own // TOK, 1 << 30, 4 << 20)[0]


def coarse_output(coarse, got, rows, which, plan, block_rows, block_cols, part=None):
    own, width = coarse.shape
    half = width // 2
    sizes, more = plan.three[which], plan.four[which]
    parts = [] if part is None else [part]

    def padded(parts, sizes, room):
        out = []
        for value, size, space in zip(parts, sizes, room):
            out.append(value)
            if size < space:
                out.append(jnp.zeros((space - size, value.shape[1]), F32))
        return out

    def body(coarse_ref, *refs):
        got_refs, refs = refs[:3], refs[3:]
        part_refs, (rows_ref, out_ref, *fine_outs, _) = refs[: len(parts)], refs[len(parts) :]
        got = [ref[...].astype(F32) for ref in got_refs]
        back = [jnp.concatenate([x[:size], x[size : 2 * size]], axis=1) for x, size in zip(got, sizes)]
        source = stack_rows([coarse_ref[...].astype(F32)] + padded(back, sizes, plan.room_three))
        out = select_rows(columns_of(rows_of(plan, rows_ref, "coarse_out"), own), source.astype(BF16)).astype(BF16)
        for n in range(own // 2):
            out_ref[n // block_cols, n % block_cols] = out[2 * n : 2 * n + 2]
        for part_ref, fine_ref in zip(part_refs, fine_outs):
            fine = stack_rows(padded([x[2 * size :] for x, size in zip(got, sizes)], more, plan.room_four))
            base = part_ref.shape[0] + sum(plan.room_two)
            take = columns_of(rows_of(plan, rows_ref, "fine_out"), part_ref.shape[0]) - float(base)
            out = part_ref[...].astype(F32) + select_rows(take, fine.astype(BF16))
            fine_ref[...] = out.reshape(fine_ref.shape).astype(BF16)

    outs = [jax.ShapeDtypeStruct((block_rows, block_cols, 2, width), BF16)]
    outs += [jax.ShapeDtypeStruct((2, 2 * block_rows, 2 * block_cols, half), BF16) for _ in parts]
    args = [coarse, *got, *parts, rows]
    out, *fine = call(body, outs, args, [VMEM] * len(args), [], 1, 1 << 28, 1 << 20)
    return out.transpose(2, 0, 1, 3), *fine


def on_device(tokens, regions, shifts, fine_qkv, fine_proj, merge_weight, coarse_qkv, coarse_proj):
    _, rows, cols, _ = tokens.shape
    plan = Plan(rows, cols)

    def first(which, sign, sent, *args):
        got = exchange(sent, plan.one[which], sign)
        return lay(got, plan.room_one), before_fine(*args, plan, rows, cols)

    def second(which, sign, sent, *args):
        got = exchange(sent, plan.two[which], sign)
        return lay(got, plan.room_two), before_coarse(*args, plan)

    def third(which, sign, sent, part, source, coarse, table):
        sizes = [2 * n + m for n, m in zip(plan.three[which], plan.four[which])]
        got = exchange(sent, sizes, sign)
        partial = sum(plan.four[which]) > 0
        fine_out = fine_output(part, source, table, plan, rows, cols, partial)
        place = (table, which, plan, rows // 2, cols // 2)
        if partial:
            coarse_out, fine_out = coarse_output(coarse, got, *place, part=fine_out)
        else:
            (coarse_out,) = coarse_output(coarse, got, *place)
        return fine_out, coarse_out

    def branches(stage, pairs):
        return [functools.partial(stage, which, sign) for which, sign in pairs]

    sent, source, table, flags, one, two, three = first_pieces(shifts, tokens, plan)
    got, (ids, x, weights) = choose(
        one, branches(first, plan.one_branches), sent, flags, regions, source, table, [fine_qkv, fine_proj]
    )
    fine, sent = fine_level(x, got, ids, *weights, fine_qkv, table, plan)
    got, (x, part, home, merge_first) = choose(
        two, branches(second, plan.two_branches), sent, flags, fine, table, merge_weight
    )
    coarse, sent = coarse_level(
        flags, home, x, got, ids, merge_first, merge_weight, coarse_qkv, coarse_proj, table, plan
    )
    return choose(three, branches(third, plan.three_branches), sent, part, got, coarse, table)


def solution(mesh):
    return jax.shard_map(
        on_device,
        mesh=mesh,
        in_specs=(P(None, "lat", "lon", None), P(), P(), P(), P(), P(), P(), P()),
        out_specs=(P(None, "lat", "lon", None), P(None, "lat", "lon", None)),
        check_vma=False,
    )
```

```python
import functools

import jax
import jax.numpy as jnp
import numpy as np
from jax import lax
from jax.experimental import pallas as pl
from jax.experimental.pallas import tpu as pltpu
from jax.sharding import PartitionSpec as P

HD = 32
WH = 6
WW = 12
TOK = 2 * WH * WW
EPS = 1e-05
BIG = 1e30
SCALE = float(np.log2(np.e) / np.sqrt(HD))

NT = (((1,), (1,)), ((), ()))
TN = (((0,), (0,)), ((), ()))
F32 = jnp.float32
BF16 = jnp.bfloat16
I32 = jnp.int32

PAIRS = [(WH - 1, t) for t in range(1, WH)] + [(t, WH - 1) for t in range(1, WH - 1)]


def up16(count):
    return -(-count // 16) * 16


def natural(rows, cols):
    return [(l, r, c) for l in range(2) for r in range(rows) for c in range(cols)]


def windowed(rows, cols):
    return [
        (l, wr * WH + r, wc * WW + c)
        for wr in range(rows // WH)
        for wc in range(cols // WW)
        for l in range(2)
        for r in range(WH)
        for c in range(WW)
    ]


def moved(order, d):
    return [(l, r + d, c + 2 * d) for l, r, c in order]


def exchange_places(held, wanted, rows, cols, sign):
    at = {place: n for n, place in enumerate(held)}
    found = []
    for dr, dc in ((sign, 0), (0, sign), (sign, sign)):
        numbers, places = [], []
        for l, r, c in sorted(set(wanted) - set(held)):
            n = at.get((l, r - dr * rows, c - dc * cols))
            if n is not None:
                numbers.append(n)
                places.append((l, r, c))
        found.append((numbers, places))
    return found


def offsets(t0, t1):
    a = t0 if t0 <= 2 else t0 - WH
    big_a = t1 if t1 <= 2 else t1 - WH
    ahead = 1 if 2 * big_a > a or 2 * big_a - a == 0 and a < 0 else -1
    return a, big_a, ahead


def classes_of(needs, slack):
    rounded = [tuple(-(-size // 8) * 8 for size in need) for need in needs]
    heavy = [sum(need[1:3]) * 2 + sum(need[4:]) for need in rounded]
    limits = []
    for size in sorted(set(heavy)):
        if not limits or size > limits[-1][0] * slack:
            limits.append([size, size])
        limits[-1][1] = size
    which = [next(n for n, limit in enumerate(limits) if size <= limit[1]) for size in heavy]
    sizes = [
        [max(need[k] for need, w in zip(rounded, which) if w == n) for k in range(len(needs[0]))]
        for n in range(len(limits))
    ]
    return sizes, which


def rooms(sizes):
    return [up16(max(size[k] for size in sizes)) for k in range(len(sizes[0]))]


class Plan:
    def __init__(self, rows, cols):
        crows, ccols = rows // 2, cols // 2
        block, cblock = natural(rows, cols), natural(crows, ccols)
        cases = []
        for t0, t1 in PAIRS:
            a, big_a, ahead = offsets(t0, t1)
            fine = moved(windowed(rows, cols), a)
            coarse = moved(cblock, big_a)
            quarters = [
                (l, 2 * r + dr, 2 * c + dc)
                for dr, dc in ((0, 0), (1, 0), (0, 1), (1, 1))
                for l, r, c in coarse
            ]
            come = 1 if a > 0 else -1
            one = exchange_places(block, fine, rows, cols, come)
            home = [p for p in block if p not in set(fine)]
            wanted = quarters + (home if come == -ahead else [])
            two = exchange_places(fine, wanted, rows, cols, ahead)
            back = 1 if big_a < 0 else -1
            three = exchange_places(coarse, cblock, crows, ccols, back)
            got = set(fine).union(*[places for _, places in two])
            four = exchange_places(fine, [p for p in block if p not in got], rows, cols, back)
            cases.append((come, ahead, back, fine, coarse, quarters, one, two, three, four))

        def needs(which):
            return [[len(numbers) for numbers, _ in case[which]] for case in cases]

        self.one, one_class = classes_of(needs(6), 1.15)
        self.two, two_class = classes_of(needs(7), 1.15)
        sizes, three_class = classes_of([three + four for three, four in zip(needs(8), needs(9))], 1.0)
        self.three, self.four = [size[:3] for size in sizes], [size[3:] for size in sizes]
        self.room_one, self.room_two = rooms(self.one), rooms(self.two)
        self.room_three, self.room_four = rooms(self.three), rooms(self.four)

        def branches(which_class, direction):
            pairs = [(n, case[direction]) for n, case in zip(which_class, cases)]
            found = sorted(set(pairs))
            return found, [found.index(pair) for pair in pairs]

        self.one_branches, one_at = branches(one_class, 0)
        self.two_branches, two_at = branches(two_class, 1)
        self.three_branches, three_at = branches(three_class, 2)
        self.flags = dict(
            three_class=three_class,
            one_at=one_at, two_at=two_at, three_at=three_at,
            a=[offsets(*pair)[0] for pair in PAIRS], big_a=[offsets(*pair)[1] for pair in PAIRS],
        )

        found = {}
        for n, (come, ahead, back, fine, coarse, quarters, one, two, three, four) in enumerate(cases):

            def send(exchanged, room):
                return [n for (numbers, _), size in zip(exchanged, room) for n in numbers + [-1] * (size - len(numbers))]

            def source(held, *exchanges):
                places = list(held)
                for exchanged, room in exchanges:
                    for (_, got), size in zip(exchanged, room):
                        places += got + [None] * (size - len(got))
                return {p: n for n, p in enumerate(places) if p is not None}

            first, second = source(block, (one, self.room_one)), source(fine, (two, self.room_two))
            third = source(coarse, (three, self.room_three))
            last = source(fine, (two, self.room_two), (four, self.room_four))
            out = [(l, r, c) for r in range(crows) for c in range(ccols) for l in range(2)]
            rows_of = dict(
                send_one=send(one, self.room_one),
                take_one=[first[p] for p in fine],
                send_two=send(two, self.room_two),
                take_two=[second[p] for p in quarters],
                send_three=send(three, self.room_three),
                send_four=send(four, self.room_four),
                fine_out=[last[p] for p in block],
                coarse_out=[third[p] for p in out],
            )
            for name, row in rows_of.items():
                found.setdefault(name, []).append(row)
        parts, self.at, top = [], {}, 0
        for name, lists in found.items():
            length = -(-max(len(row) for row in lists) // 128)
            part = np.full((len(PAIRS), length * 128), -1, np.float32)
            for n, row in enumerate(lists):
                part[n, : len(row)] = row
            parts.append(part.reshape(len(PAIRS), length, 128))
            self.at[name] = (top, length)
            top += length
        parts.append(np.zeros((len(PAIRS), -top % 8, 128), np.float32))
        self.table = np.concatenate(parts, axis=1)


def case_of(shifts_ref):
    t0, t1 = shifts_ref[0], shifts_ref[1]
    return jnp.where(t0 == WH - 1, t1 - 1, t0 + WH - 2)


def lookup(values, case):
    out = jnp.int32(values[0])
    for n, value in enumerate(values[1:], 1):
        out = jnp.where(case == n, value, out)
    return out


def columns_of(rows, count):
    parts = [jnp.broadcast_to(rows[j : j + 1], (128, 128)).T for j in range(-(-count // 128))]
    return stack_rows(parts)[:count]


def select_rows(index, source):
    lane = lax.broadcasted_iota(I32, (1, 128), 1).astype(F32)
    size = source.shape[0]
    pick = [jnp.where(index == lane + float(at), 1.0, 0.0).astype(BF16) for at in range(0, size, 128)]
    pick = jnp.concatenate(pick, axis=1)[:, :size]
    return jnp.dot(pick, source, preferred_element_type=F32)


def stack_rows(parts):
    return parts[0] if len(parts) == 1 else jnp.concatenate(parts, axis=0)


def layer_norm(values):
    center = jnp.mean(values, axis=-1, keepdims=True)
    values = values - center
    spread = jnp.mean(values * values, axis=-1, keepdims=True)
    return values * lax.rsqrt(spread + EPS)


def attend_windows(qkv_of, id_of, windows, inner, finish):
    lane = lax.broadcasted_iota(I32, (1, 128), 1)
    forbid = jnp.where(lane < 8, BIG, 0.0).astype(BF16)
    groups = inner // 128
    units = [(w, g) for w in range(windows) for g in range(groups)]
    scores, weights, outs = {}, {}, {}

    def score(w, g):
        key_id = id_of(w)
        not_id = (key_id - 1).astype(BF16) * forbid
        q = qkv_of(w, g * 128)
        keys = jnp.concatenate([qkv_of(w, inner + g * 128), key_id], axis=1)
        queries = []
        for h in range(4):
            mine = jnp.where((lane >= h * HD) & (lane < (h + 1) * HD), 1.0, 0.0).astype(BF16)
            queries.append(jnp.concatenate([q * mine, not_id], axis=1))
        scores[w, g] = lax.dot_general(stack_rows(queries), keys, NT, preferred_element_type=F32)

    def soften(w, g):
        s = scores.pop((w, g))
        weights[w, g] = jnp.exp2((s - jnp.max(s, axis=1, keepdims=True)) * SCALE).astype(BF16)

    def gather(w, g):
        v = qkv_of(w, 2 * inner + g * 128)
        values = jnp.concatenate([v, jnp.ones_like(v)], axis=1)
        out = jnp.dot(weights.pop((w, g)), values, preferred_element_type=F32)
        picked, total = out[:TOK, :128], out[:TOK, 128:]
        for h in range(1, 4):
            rows = slice(h * TOK, (h + 1) * TOK)
            picked = jnp.where(lane < h * HD, picked, out[rows, :128])
            total = jnp.where(lane < h * HD, total, out[rows, 128:])
        outs[w, g] = (picked / total).astype(BF16)
        if g == groups - 1:
            finish(w, jnp.concatenate([outs.pop((w, k)) for k in range(groups)], axis=1))

    for n in range(len(units) + 2):
        if n < len(units):
            score(*units[n])
        if 0 <= n - 1 < len(units):
            soften(*units[n - 1])
        if 0 <= n - 2 < len(units):
            gather(*units[n - 2])


ANY = pl.BlockSpec(memory_space=pl.ANY)
HBM = pl.BlockSpec(memory_space=pltpu.HBM)
VMEM = pl.BlockSpec(memory_space=pltpu.VMEM)
SMEM = pl.BlockSpec(memory_space=pltpu.SMEM)


def call(body, outs, args, in_specs, scratch, copies, flops, moved_bytes, vmem=8):
    args = [
        pltpu.with_memory_space_constraint(arg, spec.memory_space) for arg, spec in zip(args, in_specs, strict=True)
    ]
    spaces = [getattr(out, "memory_space", pltpu.SMEM if out.dtype == I32 else pltpu.VMEM) for out in outs]
    out_specs = [pl.BlockSpec(memory_space=space) for space in spaces]
    return pl.pallas_call(
        body,
        out_shape=outs,
        in_specs=in_specs,
        out_specs=out_specs,
        scratch_shapes=list(scratch) + [pltpu.SemaphoreType.DMA((copies,))],
        compiler_params=pltpu.CompilerParams(vmem_limit_bytes=vmem << 20),
        cost_estimate=pl.CostEstimate(flops=flops, bytes_accessed=moved_bytes, transcendentals=0),
    )(*args)


def shapes(sizes, width, space=pltpu.VMEM):
    return [space((n, width), BF16) for n in sizes]


class Copies:
    def __init__(self, sems):
        self.sems, self.used = sems, 0

    def __call__(self, src, dst):
        copy = pltpu.make_async_copy(src, dst, self.sems.at[self.used])
        self.used += 1
        copy.start()
        return copy


def lay(pieces, room):
    width = pieces[0].shape[1]

    def body(*refs):
        out_ref = refs[len(pieces)]
        at = 0
        for ref, space in zip(refs, room):
            rows = ref.shape[0]
            out_ref[at : at + rows, :] = ref[...]
            if rows < space:
                out_ref[at + rows : at + space, :] = jnp.zeros((space - rows, width), BF16)
            at += space

    return call(body, shapes([sum(room)], width), pieces, [VMEM] * 3, [], 1, 0, 1 << 18)[0]


def flat(ref):
    layers, rows, cols, width = ref.shape
    return ref[...].astype(F32).reshape(layers * rows * cols, width).astype(BF16)


def put_pieces(value, refs):
    at = 0
    for ref in refs:
        ref[...] = value[at : at + ref.shape[0]].astype(BF16)
        at += ref.shape[0]


def rows_of(plan, table_ref, name, *lead):
    top, length = plan.at[name]
    return table_ref[(*lead, slice(top, top + length), slice(None))]


def exchange(pieces, sizes, sign):
    lat, lon = lax.axis_size("lat"), lax.axis_size("lon")
    row, col, both = [piece[:size] for piece, size in zip(pieces, sizes)]
    pairs = [((i + sign) % lat * lon + (j + sign) % lon, i * lon + j) for i in range(lat) for j in range(lon)]
    col = lax.ppermute(col, "lon", [((j + sign) % lon, j) for j in range(lon)])
    both = lax.ppermute(both, ("lat", "lon"), pairs)
    row = lax.ppermute(row, "lat", [((i + sign) % lat, i) for i in range(lat)])
    return [row, col, both]


def choose(index, branches, *args):
    flat_args, tree = jax.tree.flatten(args)
    out_trees = []

    def closed(branch):
        def run(*leaves):
            out, out_tree = jax.tree.flatten(branch(*jax.tree.unflatten(tree, leaves)))
            out_trees.append(out_tree)
            return out

        return jax.make_jaxpr(run)(*flat_args)

    out = lax.cond_p.bind(index, *flat_args, branches=tuple(closed(branch) for branch in branches))
    return jax.tree.unflatten(out_trees[0], out)


FLAGS = ("three_class", "a", "big_a")


def first_pieces(shifts, tokens, plan):
    width = tokens.shape[-1]
    count = tokens.size // width
    kinds = 3

    def body(shifts_hbm, tokens_hbm, table_hbm, *refs):
        outs, refs = refs[:kinds], refs[kinds:]
        source_ref, rows_ref, flags_ref, *at_refs, shifts_ref, tokens_ref, table_ref, sems = refs
        start = Copies(sems)
        shift = start(shifts_hbm, shifts_ref)
        held = start(tokens_hbm, tokens_ref)
        table = start(table_hbm, table_ref)
        shift.wait()
        case = case_of(shifts_ref)
        for ref, name in zip(at_refs, ("one_at", "two_at", "three_at")):
            ref[0] = lookup(plan.flags[name], case)
        for n, name in enumerate(FLAGS):
            flags_ref[n] = lookup(plan.flags[name], case)
        held.wait()
        source_ref[...] = flat(tokens_ref)
        table.wait()
        rows_ref[...] = table_ref[case]
        index = columns_of(rows_of(plan, table_ref, "send_one", case), sum(plan.room_one))
        put_pieces(select_rows(index, source_ref[...]), outs)

    outs = shapes([*plan.room_one, count], width)
    outs += [pltpu.VMEM(plan.table.shape[1:], F32), pltpu.SMEM((8,), I32)]
    outs += [pltpu.SMEM((1,), I32)] * 3
    scratch = [pltpu.SMEM((2,), I32), pltpu.VMEM(tokens.shape, BF16), pltpu.VMEM(plan.table.shape, F32)]
    got = call(body, outs, [shifts, tokens, plan.table], [HBM] * 3, scratch, 3, 1 << 28, 1 << 20)
    sent, (source, rows, flags, one, two, three) = got[:kinds], got[kinds:]
    return sent, source, rows, flags, one[0], two[0], three[0]


def before_fine(flags, regions, tokens, table, weights, plan, rows, cols):
    _, lat, lon = regions.shape
    width = tokens.shape[1]
    flat_regions = regions.reshape(2 * lat, lon)
    fine, coarse = windowed(rows, cols), natural(rows // 2, cols // 2)

    def lanes(places, scale, is_fine):
        places = np.asarray([(l, scale * r, scale * c, is_fine) for l, r, c in places], np.float32)
        return np.pad(places, ((0, -len(places) % 128), (0, 0))).T.reshape(4, -1, 128)

    places = np.concatenate([lanes(fine, 1, 1), lanes(coarse, 2, 0)], axis=1)
    lines = places.shape[1]

    def body(flags_ref, rows_ref, tokens_ref, regions_hbm, places_hbm, *refs):
        weights_hbm, refs = refs[: len(weights)], refs[len(weights) :]
        id_ref, x_ref, *refs = refs
        weight_refs, (regions_ref, places_ref, sems) = refs[: len(weights)], refs[len(weights) :]
        start = Copies(sems)
        waits = [start(regions_hbm, regions_ref), start(places_hbm, places_ref)]
        later = [
            start(src.at[:, pl.ds(0, dst.shape[1])], dst) for src, dst in zip(weights_hbm, weight_refs)
        ]
        for copy in waits:
            copy.wait()
        a = flags_ref[1].astype(F32)
        big_a = 2.0 * flags_ref[2].astype(F32)
        is_fine = places_ref[3]
        d = is_fine * a + (1.0 - is_fine) * big_a
        row = places_ref[1] + d + (lax.axis_index("lat") * rows).astype(F32)
        col = places_ref[2] + 2.0 * d + (lax.axis_index("lon") * cols).astype(F32)
        wrapped = jnp.where((row < 0) | (row >= lat), 4.0, 0.0)
        row = jnp.where(row < 0, row + lat, jnp.where(row >= lat, row - lat, row))
        col = jnp.where(col < 0, col + lon, jnp.where(col >= lon, col - lon, col))
        row = row + places_ref[0] * lat

        def along(values):
            return jnp.concatenate([values[n : n + 1] for n in range(lines)], axis=1)

        line = lax.broadcasted_iota(I32, (2 * lat, 1), 0).astype(F32)
        pick = jnp.where(line == along(row), 1.0, 0.0).astype(BF16)
        known = regions_ref[...].astype(F32).astype(BF16)
        picked = lax.dot_general(known, pick, TN, preferred_element_type=F32)
        line = lax.broadcasted_iota(I32, (lon, 1), 0).astype(F32)
        ids = jnp.sum(jnp.where(line == along(col), picked, 0.0), axis=0, keepdims=True) + along(wrapped)
        for n in range(lines):
            id_ref[n : n + 1, :] = ids[:, n * 128 : (n + 1) * 128]
        take = columns_of(rows_of(plan, rows_ref, "take_one"), len(fine))
        x_ref[...] = select_rows(take, tokens_ref[...]).astype(BF16)
        for copy in later:
            copy.wait()

    outs = [pltpu.VMEM((lines, 128), F32)] + shapes([len(fine)], width)
    outs += [pltpu.VMEM((w.shape[0], min(w.shape[1], 2 * weights[1].shape[0])), BF16) for w in weights]
    scratch = [pltpu.VMEM(flat_regions.shape, I32), pltpu.VMEM(places.shape, F32)]
    args = [flags, table, tokens, flat_regions, places, *weights]
    in_specs = [SMEM, VMEM, VMEM] + [HBM] * (2 + len(weights))
    ids, x, *weights = call(body, outs, args, in_specs, scratch, 2 + len(weights), 1 << 28, 4 << 20)
    return ids, x, weights


def id_columns(lines, count):
    lane = lax.broadcasted_iota(I32, (1, 128), 1).astype(F32)
    return jnp.where(columns_of(lines, count) == lane, 1.0, 0.0).astype(BF16)


def before_coarse(flags, fine, table, weight, plan):
    own, width = fine.shape
    half = 5 * weight.shape[0] // 16

    def body(flags_ref, rows_ref, fine_ref, weight_hbm, x_ref, part_hbm, home_ref, weight_ref, part_ref, sems):
        start = Copies(sems)
        later = start(weight_hbm.at[pl.ds(0, half)], weight_ref)
        take = columns_of(rows_of(plan, rows_ref, "fine_out"), own)
        part_ref[...] = select_rows(take, fine_ref[...]).astype(BF16)
        leave = start(part_ref, part_hbm)
        take = columns_of(rows_of(plan, rows_ref, "take_two"), own)
        x_ref[...] = select_rows(take, fine_ref[...]).astype(BF16)

        @pl.when(needs_fine(flags_ref, plan))
        def _():
            index = columns_of(rows_of(plan, rows_ref, "send_four"), sum(plan.room_four))
            home_ref[...] = select_rows(index, fine_ref[...]).astype(BF16)

        leave.wait()
        later.wait()

    outs = shapes([own], width) + shapes([own], width, pltpu.HBM)
    outs += shapes([sum(plan.room_four)], width) + shapes([half], weight.shape[1])
    scratch = [pltpu.VMEM(fine.shape, BF16)]
    args = [flags, table, fine, weight]
    return call(body, outs, args, [SMEM, VMEM, VMEM, HBM], scratch, 2, 1 << 28, 4 << 20)


def needs_fine(flags_ref, plan):
    with_fine = [n for n, sizes in enumerate(plan.four) if sum(sizes)]
    return functools.reduce(jnp.logical_or, [flags_ref[0] == n for n in with_fine])


def fine_level(x_own, source, ids, w_qk, w_proj, w_qkv, rows, plan):
    count, width = x_own.shape
    inner = w_proj.shape[0]
    half = 2 * TOK
    parts = count // half

    def body(own_ref, source_ref, ids_ref, qk_w_ref, proj_w_ref, qkv_w_hbm, rows_ref, out_ref, *refs):
        piece_outs, refs = refs[:3], refs[3:]
        x_refs, qkv_refs, (id_ref, v_w_ref, sems) = refs[:parts], refs[parts : 2 * parts], refs[2 * parts :]
        v_w = Copies(sems)(qkv_w_hbm.at[:, pl.ds(2 * inner, inner)], v_w_ref)
        id_ref[...] = id_columns(ids_ref[: -(-count // 128), :], count)
        take = columns_of(rows_of(plan, rows_ref, "take_one"), count) - float(count)
        for n, x_ref in enumerate(x_refs):
            rows = slice(n * half, (n + 1) * half)
            x_ref[...] = own_ref[rows, :].astype(F32) + select_rows(take[rows], source_ref[...])
        v_w.wait()
        for x_ref, qkv_ref in zip(x_refs, qkv_refs):
            normed = layer_norm(x_ref[...]).astype(BF16)
            qkv_ref[:, : 2 * inner] = jnp.dot(normed, qk_w_ref[...], preferred_element_type=F32).astype(BF16)
            qkv_ref[:, 2 * inner :] = jnp.dot(normed, v_w_ref[...], preferred_element_type=F32).astype(BF16)
        index = columns_of(rows_of(plan, rows_ref, "send_two"), sum(plan.room_two))
        sent = []

        def inside(w):
            return w * TOK // half, slice(w * TOK % half, w * TOK % half + TOK)

        def finish(w, out):
            n, rows = inside(w)
            out = jnp.dot(out, proj_w_ref[...], preferred_element_type=F32)
            out = (x_refs[n][rows, :] + out).astype(BF16)
            out_ref[w * TOK : (w + 1) * TOK, :] = out
            sent.append(select_rows(index - float(w * TOK), out))

        def qkv_of(w, at):
            n, rows = inside(w)
            return qkv_refs[n][rows, at : at + 128]

        attend_windows(qkv_of, lambda w: id_ref[w * TOK : (w + 1) * TOK, :], count // TOK, inner, finish)
        put_pieces(functools.reduce(jnp.add, sent), piece_outs)

    outs = shapes([count, *plan.room_two], width)
    scratch = [pltpu.VMEM((half, width), F32)] * parts + [pltpu.VMEM((half, 3 * inner), BF16)] * parts
    scratch += [pltpu.VMEM((count, 128), BF16), pltpu.VMEM((width, inner), BF16)]
    args = [x_own, source, ids, w_qk, w_proj, w_qkv, rows]
    out, *sent = call(body, outs, args, [VMEM] * 5 + [HBM, VMEM], scratch, 1, 3 << 30, 6 << 20, 14)
    return out, sent


def coarse_level(flags, home, x_own, source, ids, merge_first, w_merge, w_qkv, w_proj, rows, plan):
    depth, width = w_merge.shape
    own, half = x_own.shape
    count = own // 4
    inner = w_proj.shape[0]

    def body(
        flags_ref, merge_hbm, qkv_w_hbm, proj_w_hbm, home_ref, own_ref, source_ref, ids_ref, first_ref, rows_ref, *refs
    ):
        out_ref, *piece_outs = refs[:4]
        qkv_ref, id_ref, merge_ref, qkv_w_ref, proj_w_ref, sems = refs[4:]
        start = Copies(sems)
        here = first_ref.shape[0]
        merge_w = start(merge_hbm.at[pl.ds(here, depth - here)], merge_ref)
        qkv_w = start(qkv_w_hbm, qkv_w_ref)
        proj_w = start(proj_w_hbm, proj_w_ref)
        id_ref[...] = id_columns(ids_ref[-(-own // 128) :, :], count)
        take = columns_of(rows_of(plan, rows_ref, "take_two"), 4 * count) - float(own)
        x = own_ref[...].astype(F32) + select_rows(take, source_ref[...])
        x = jnp.concatenate([x[n * count : (n + 1) * count] for n in range(4)], axis=1)
        stacked = layer_norm(x).astype(BF16)
        merge_w.wait()
        merged = jnp.dot(stacked[:, :here], first_ref[...], preferred_element_type=F32)
        merged = merged + jnp.dot(stacked[:, here:], merge_ref[...], preferred_element_type=F32)
        merged = merged.astype(BF16).astype(F32)
        normed = layer_norm(merged).astype(BF16)
        qkv_w.wait()
        proj_w.wait()
        qkv_ref[...] = jnp.dot(normed, qkv_w_ref[...], preferred_element_type=F32).astype(BF16)

        def finish(w, out):
            out = jnp.dot(out, proj_w_ref[...], preferred_element_type=F32)
            out_ref[...] = (merged + out).astype(BF16)

        attend_windows(lambda w, at: qkv_ref[:, at : at + 128], lambda w: id_ref[...], 1, inner, finish)
        sent = select_rows(columns_of(rows_of(plan, rows_ref, "send_three"), sum(plan.room_three)), out_ref[...])
        sent = sent.astype(BF16)
        for n, sizes in enumerate(plan.three):

            @pl.when(flags_ref[0] == n)
            def _():
                at = 0
                for ref, size, space in zip(piece_outs, sizes, plan.room_three):
                    ref[:size, :] = sent[at : at + size, :half]
                    ref[size : 2 * size, :] = sent[at : at + size, half:]
                    at += space

        for n, fine_sizes in enumerate(plan.four):
            if sum(fine_sizes):

                @pl.when(flags_ref[0] == n)
                def _():
                    at = 0
                    for ref, size, more, space in zip(piece_outs, plan.three[n], fine_sizes, plan.room_four):
                        ref[2 * size : 2 * size + more, :] = home_ref[at : at + more, :]
                        at += space

    most = [max(2 * three[k] + four[k] for three, four in zip(plan.three, plan.four)) for k in range(3)]
    outs = shapes([count], width) + shapes(most, half)
    scratch = [pltpu.VMEM((count, 3 * inner), BF16)]
    shapes_in = [(count, 128), (depth - merge_first.shape[0], width), w_qkv.shape, w_proj.shape]
    scratch += [pltpu.VMEM(shape, BF16) for shape in shapes_in]
    args = [flags, w_merge, w_qkv, w_proj, home, x_own, source, ids, merge_first, rows]
    in_specs = [SMEM] + [HBM] * 3 + [VMEM] * (len(args) - 4)
    out, *sent = call(body, outs, args, in_specs, scratch, 3, 3 << 30, 12 << 20, 24)
    return out, sent


def fine_output(part, source, rows, plan, block_rows, block_cols, partial):
    own, width = part.shape

    def body(part_hbm, source_ref, rows_ref, out_ref, part_ref, stage_ref, sems):
        start = Copies(sems)
        cuts = [pl.ds(at, TOK) for at in range(0, own, TOK)]
        held = [start(part_hbm.at[cut], part_ref.at[cut]) for cut in cuts]
        take = columns_of(rows_of(plan, rows_ref, "fine_out"), own) - float(own)
        leave = []
        for n, (cut, copy) in enumerate(zip(cuts, held)):
            got = select_rows(take[n * TOK : (n + 1) * TOK], source_ref[...])
            copy.wait()
            out = part_ref[cut, :].astype(F32) + got
            if partial:
                out_ref[cut, :] = out.astype(BF16)
            else:
                lines = TOK // block_cols
                layer, line = divmod(n * lines, block_rows)
                there = (layer, pl.ds(line, lines))
                stage_ref[there] = out.reshape(lines, block_cols, width).astype(BF16)
                leave.append(start(stage_ref.at[there], out_ref.at[there]))
        for copy in leave:
            copy.wait()

    shape = (2, block_rows, block_cols, width)
    outs = shapes([own], width) if partial else [pltpu.HBM(shape, BF16)]
    scratch = [pltpu.VMEM(part.shape, BF16), pltpu.VMEM(shape, BF16)]
    return call(body, outs, [part, source, rows], [HBM, VMEM, VMEM], scratch, 2 * own // TOK, 1 << 30, 4 << 20)[0]


def coarse_output(coarse, got, rows, which, plan, block_rows, block_cols, part=None):
    own, width = coarse.shape
    half = width // 2
    sizes, more = plan.three[which], plan.four[which]
    parts = [] if part is None else [part]

    def padded(parts, sizes, room):
        out = []
        for value, size, space in zip(parts, sizes, room):
            out.append(value)
            if size < space:
                out.append(jnp.zeros((space - size, value.shape[1]), F32))
        return out

    def body(coarse_ref, *refs):
        got_refs, refs = refs[:3], refs[3:]
        part_refs, (rows_ref, out_ref, *fine_outs, _) = refs[: len(parts)], refs[len(parts) :]
        got = [ref[...].astype(F32) for ref in got_refs]
        back = [jnp.concatenate([x[:size], x[size : 2 * size]], axis=1) for x, size in zip(got, sizes)]
        source = stack_rows([coarse_ref[...].astype(F32)] + padded(back, sizes, plan.room_three))
        out = select_rows(columns_of(rows_of(plan, rows_ref, "coarse_out"), own), source.astype(BF16)).astype(BF16)
        for n in range(own // 2):
            out_ref[n // block_cols, n % block_cols] = out[2 * n : 2 * n + 2]
        for part_ref, fine_ref in zip(part_refs, fine_outs):
            fine = stack_rows(padded([x[2 * size :] for x, size in zip(got, sizes)], more, plan.room_four))
            base = part_ref.shape[0] + sum(plan.room_two)
            take = columns_of(rows_of(plan, rows_ref, "fine_out"), part_ref.shape[0]) - float(base)
            out = part_ref[...].astype(F32) + select_rows(take, fine.astype(BF16))
            fine_ref[...] = out.reshape(fine_ref.shape).astype(BF16)

    outs = [jax.ShapeDtypeStruct((block_rows, block_cols, 2, width), BF16)]
    outs += [jax.ShapeDtypeStruct((2, 2 * block_rows, 2 * block_cols, half), BF16) for _ in parts]
    args = [coarse, *got, *parts, rows]
    out, *fine = call(body, outs, args, [VMEM] * len(args), [], 1, 1 << 28, 1 << 20)
    return out.transpose(2, 0, 1, 3), *fine


def on_device(tokens, regions, shifts, fine_qkv, fine_proj, merge_weight, coarse_qkv, coarse_proj):
    _, rows, cols, _ = tokens.shape
    plan = Plan(rows, cols)

    def first(which, sign, sent, *args):
        got = exchange(sent, plan.one[which], sign)
        return lay(got, plan.room_one), before_fine(*args, plan, rows, cols)

    def second(which, sign, sent, *args):
        got = exchange(sent, plan.two[which], sign)
        return lay(got, plan.room_two), before_coarse(*args, plan)

    def third(which, sign, sent, part, source, coarse, table):
        sizes = [2 * n + m for n, m in zip(plan.three[which], plan.four[which])]
        got = exchange(sent, sizes, sign)
        partial = sum(plan.four[which]) > 0
        fine_out = fine_output(part, source, table, plan, rows, cols, partial)
        place = (table, which, plan, rows // 2, cols // 2)
        if partial:
            coarse_out, fine_out = coarse_output(coarse, got, *place, part=fine_out)
        else:
            (coarse_out,) = coarse_output(coarse, got, *place)
        return fine_out, coarse_out

    def branches(stage, pairs):
        return [functools.partial(stage, which, sign) for which, sign in pairs]

    sent, source, table, flags, one, two, three = first_pieces(shifts, tokens, plan)
    got, (ids, x, weights) = choose(
        one, branches(first, plan.one_branches), sent, flags, regions, source, table, [fine_qkv, fine_proj]
    )
    fine, sent = fine_level(x, got, ids, *weights, fine_qkv, table, plan)
    got, (x, part, home, merge_first) = choose(
        two, branches(second, plan.two_branches), sent, flags, fine, table, merge_weight
    )
    coarse, sent = coarse_level(
        flags, home, x, got, ids, merge_first, merge_weight, coarse_qkv, coarse_proj, table, plan
    )
    return choose(three, branches(third, plan.three_branches), sent, part, got, coarse, table)


def solution(mesh):
    return jax.shard_map(
        on_device,
        mesh=mesh,
        in_specs=(P(None, "lat", "lon", None), P(), P(), P(), P(), P(), P(), P()),
        out_specs=(P(None, "lat", "lon", None), P(None, "lat", "lon", None)),
        check_vma=False,
    )
```

```python
import functools

import jax
import jax.numpy as jnp
import numpy as np
from jax import lax
from jax.experimental import pallas as pl
from jax.experimental.pallas import tpu as pltpu
from jax.sharding import PartitionSpec as P

HD = 32
WH = 6
WW = 12
TOK = 2 * WH * WW
EPS = 1e-05
BIG = 1e30
SCALE = float(np.log2(np.e) / np.sqrt(HD))

NT = (((1,), (1,)), ((), ()))
TN = (((0,), (0,)), ((), ()))
F32 = jnp.float32
BF16 = jnp.bfloat16
I32 = jnp.int32

PAIRS = [(WH - 1, t) for t in range(1, WH)] + [(t, WH - 1) for t in range(1, WH - 1)]


def up16(count):
    return -(-count // 16) * 16


def natural(rows, cols):
    return [(l, r, c) for l in range(2) for r in range(rows) for c in range(cols)]


def windowed(rows, cols):
    return [
        (l, wr * WH + r, wc * WW + c)
        for wr in range(rows // WH)
        for wc in range(cols // WW)
        for l in range(2)
        for r in range(WH)
        for c in range(WW)
    ]


def moved(order, d):
    return [(l, r + d, c + 2 * d) for l, r, c in order]


def exchange_places(held, wanted, rows, cols, sign):
    at = {place: n for n, place in enumerate(held)}
    found = []
    for dr, dc in ((sign, 0), (0, sign), (sign, sign)):
        numbers, places = [], []
        for l, r, c in sorted(set(wanted) - set(held)):
            n = at.get((l, r - dr * rows, c - dc * cols))
            if n is not None:
                numbers.append(n)
                places.append((l, r, c))
        found.append((numbers, places))
    return found


def offsets(t0, t1):
    a = t0 if t0 <= 2 else t0 - WH
    big_a = t1 if t1 <= 2 else t1 - WH
    ahead = 1 if 2 * big_a > a or 2 * big_a - a == 0 and a < 0 else -1
    return a, big_a, ahead


def classes_of(needs, slack):
    rounded = [tuple(-(-size // 8) * 8 for size in need) for need in needs]
    heavy = [sum(need[1:3]) * 2 + sum(need[4:]) for need in rounded]
    limits = []
    for size in sorted(set(heavy)):
        if not limits or size > limits[-1][0] * slack:
            limits.append([size, size])
        limits[-1][1] = size
    which = [next(n for n, limit in enumerate(limits) if size <= limit[1]) for size in heavy]
    sizes = [
        [max(need[k] for need, w in zip(rounded, which) if w == n) for k in range(len(needs[0]))]
        for n in range(len(limits))
    ]
    return sizes, which


def rooms(sizes):
    return [up16(max(size[k] for size in sizes)) for k in range(len(sizes[0]))]


class Plan:
    def __init__(self, rows, cols):
        crows, ccols = rows // 2, cols // 2
        block, cblock = natural(rows, cols), natural(crows, ccols)
        cases = []
        for t0, t1 in PAIRS:
            a, big_a, ahead = offsets(t0, t1)
            fine = moved(windowed(rows, cols), a)
            coarse = moved(cblock, big_a)
            quarters = [
                (l, 2 * r + dr, 2 * c + dc)
                for dr, dc in ((0, 0), (1, 0), (0, 1), (1, 1))
                for l, r, c in coarse
            ]
            come = 1 if a > 0 else -1
            one = exchange_places(block, fine, rows, cols, come)
            home = [p for p in block if p not in set(fine)]
            wanted = quarters + (home if come == -ahead else [])
            two = exchange_places(fine, wanted, rows, cols, ahead)
            back = 1 if big_a < 0 else -1
            three = exchange_places(coarse, cblock, crows, ccols, back)
            got = set(fine).union(*[places for _, places in two])
            four = exchange_places(fine, [p for p in block if p not in got], rows, cols, back)
            cases.append((come, ahead, back, fine, coarse, quarters, one, two, three, four))

        def needs(which):
            return [[len(numbers) for numbers, _ in case[which]] for case in cases]

        self.one, one_class = classes_of(needs(6), 1.15)
        self.two, two_class = classes_of(needs(7), 1.15)
        sizes, three_class = classes_of([three + four for three, four in zip(needs(8), needs(9))], 1.0)
        self.three, self.four = [size[:3] for size in sizes], [size[3:] for size in sizes]
        self.room_one, self.room_two = rooms(self.one), rooms(self.two)
        self.room_three, self.room_four = rooms(self.three), rooms(self.four)

        def branches(which_class, direction):
            pairs = [(n, case[direction]) for n, case in zip(which_class, cases)]
            found = sorted(set(pairs))
            return found, [found.index(pair) for pair in pairs]

        self.one_branches, one_at = branches(one_class, 0)
        self.two_branches, two_at = branches(two_class, 1)
        self.three_branches, three_at = branches(three_class, 2)
        self.flags = dict(
            three_class=three_class,
            one_at=one_at, two_at=two_at, three_at=three_at,
            a=[offsets(*pair)[0] for pair in PAIRS], big_a=[offsets(*pair)[1] for pair in PAIRS],
        )

        found = {}
        for n, (come, ahead, back, fine, coarse, quarters, one, two, three, four) in enumerate(cases):

            def send(exchanged, room):
                return [n for (numbers, _), size in zip(exchanged, room) for n in numbers + [-1] * (size - len(numbers))]

            def source(held, *exchanges):
                places = list(held)
                for exchanged, room in exchanges:
                    for (_, got), size in zip(exchanged, room):
                        places += got + [None] * (size - len(got))
                return {p: n for n, p in enumerate(places) if p is not None}

            first, second = source(block, (one, self.room_one)), source(fine, (two, self.room_two))
            third = source(coarse, (three, self.room_three))
            last = source(fine, (two, self.room_two), (four, self.room_four))
            out = [(l, r, c) for r in range(crows) for c in range(ccols) for l in range(2)]
            rows_of = dict(
                send_one=send(one, self.room_one),
                take_one=[first[p] for p in fine],
                send_two=send(two, self.room_two),
                take_two=[second[p] for p in quarters],
                send_three=send(three, self.room_three),
                send_four=send(four, self.room_four),
                fine_out=[last[p] for p in block],
                coarse_out=[third[p] for p in out],
            )
            for name, row in rows_of.items():
                found.setdefault(name, []).append(row)
        parts, self.at, top = [], {}, 0
        for name, lists in found.items():
            length = -(-max(len(row) for row in lists) // 128)
            part = np.full((len(PAIRS), length * 128), -1, np.float32)
            for n, row in enumerate(lists):
                part[n, : len(row)] = row
            parts.append(part.reshape(len(PAIRS), length, 128))
            self.at[name] = (top, length)
            top += length
        parts.append(np.zeros((len(PAIRS), -top % 8, 128), np.float32))
        self.table = np.concatenate(parts, axis=1)


def case_of(shifts_ref):
    t0, t1 = shifts_ref[0], shifts_ref[1]
    return jnp.where(t0 == WH - 1, t1 - 1, t0 + WH - 2)


def lookup(values, case):
    out = jnp.int32(values[0])
    for n, value in enumerate(values[1:], 1):
        out = jnp.where(case == n, value, out)
    return out


def columns_of(rows, count):
    parts = [jnp.broadcast_to(rows[j : j + 1], (128, 128)).T for j in range(-(-count // 128))]
    return stack_rows(parts)[:count]


def select_rows(index, source):
    lane = lax.broadcasted_iota(I32, (1, 128), 1).astype(F32)
    size = source.shape[0]
    pick = [jnp.where(index == lane + float(at), 1.0, 0.0).astype(BF16) for at in range(0, size, 128)]
    pick = jnp.concatenate(pick, axis=1)[:, :size]
    return jnp.dot(pick, source, preferred_element_type=F32)


def stack_rows(parts):
    return parts[0] if len(parts) == 1 else jnp.concatenate(parts, axis=0)


def layer_norm(values):
    center = jnp.mean(values, axis=-1, keepdims=True)
    values = values - center
    spread = jnp.mean(values * values, axis=-1, keepdims=True)
    return values * lax.rsqrt(spread + EPS)


def attend_windows(qkv_of, id_of, windows, inner, finish):
    lane = lax.broadcasted_iota(I32, (1, 128), 1)
    forbid = jnp.where(lane < 8, BIG, 0.0).astype(BF16)
    groups = inner // 128
    units = [(w, g) for w in range(windows) for g in range(groups)]
    scores, weights, outs = {}, {}, {}

    def score(w, g):
        key_id = id_of(w)
        not_id = (key_id - 1).astype(BF16) * forbid
        q = qkv_of(w, g * 128)
        keys = jnp.concatenate([qkv_of(w, inner + g * 128), key_id], axis=1)
        queries = []
        for h in range(4):
            mine = jnp.where((lane >= h * HD) & (lane < (h + 1) * HD), 1.0, 0.0).astype(BF16)
            queries.append(jnp.concatenate([q * mine, not_id], axis=1))
        scores[w, g] = lax.dot_general(stack_rows(queries), keys, NT, preferred_element_type=F32)

    def soften(w, g):
        s = scores.pop((w, g))
        weight = jnp.exp2((s - jnp.max(s, axis=1, keepdims=True)) * SCALE)
        weights[w, g] = weight.astype(BF16), jnp.sum(weight, axis=1, keepdims=True)

    def gather(w, g):
        weight, sums = weights.pop((w, g))
        out = jnp.dot(weight, qkv_of(w, 2 * inner + g * 128), preferred_element_type=F32)
        picked, total = out[:TOK], sums[:TOK]
        for h in range(1, 4):
            rows = slice(h * TOK, (h + 1) * TOK)
            picked = jnp.where(lane < h * HD, picked, out[rows])
            total = jnp.where(lane < h * HD, total, sums[rows])
        outs[w, g] = (picked / total).astype(BF16)
        if g == groups - 1:
            finish(w, jnp.concatenate([outs.pop((w, k)) for k in range(groups)], axis=1))

    for n in range(len(units) + 2):
        if n < len(units):
            score(*units[n])
        if 0 <= n - 1 < len(units):
            soften(*units[n - 1])
        if 0 <= n - 2 < len(units):
            gather(*units[n - 2])


ANY = pl.BlockSpec(memory_space=pl.ANY)
HBM = pl.BlockSpec(memory_space=pltpu.HBM)
VMEM = pl.BlockSpec(memory_space=pltpu.VMEM)
SMEM = pl.BlockSpec(memory_space=pltpu.SMEM)


def call(body, outs, args, in_specs, scratch, copies, flops, moved_bytes, vmem=8):
    args = [
        pltpu.with_memory_space_constraint(arg, spec.memory_space) for arg, spec in zip(args, in_specs, strict=True)
    ]
    spaces = [getattr(out, "memory_space", pltpu.SMEM if out.dtype == I32 else pltpu.VMEM) for out in outs]
    out_specs = [pl.BlockSpec(memory_space=space) for space in spaces]
    return pl.pallas_call(
        body,
        out_shape=outs,
        in_specs=in_specs,
        out_specs=out_specs,
        scratch_shapes=list(scratch) + [pltpu.SemaphoreType.DMA((copies,))],
        compiler_params=pltpu.CompilerParams(vmem_limit_bytes=vmem << 20),
        cost_estimate=pl.CostEstimate(flops=flops, bytes_accessed=moved_bytes, transcendentals=0),
    )(*args)


def shapes(sizes, width, space=pltpu.VMEM):
    return [space((n, width), BF16) for n in sizes]


class Copies:
    def __init__(self, sems):
        self.sems, self.used = sems, 0

    def __call__(self, src, dst):
        copy = pltpu.make_async_copy(src, dst, self.sems.at[self.used])
        self.used += 1
        copy.start()
        return copy


def lay(pieces, room):
    width = pieces[0].shape[1]

    def body(*refs):
        out_ref = refs[len(pieces)]
        at = 0
        for ref, space in zip(refs, room):
            rows = ref.shape[0]
            out_ref[at : at + rows, :] = ref[...]
            if rows < space:
                out_ref[at + rows : at + space, :] = jnp.zeros((space - rows, width), BF16)
            at += space

    return call(body, shapes([sum(room)], width), pieces, [VMEM] * 3, [], 1, 0, 1 << 18)[0]


def flat(ref):
    layers, rows, cols, width = ref.shape
    return ref[...].astype(F32).reshape(layers * rows * cols, width).astype(BF16)


def put_pieces(value, refs):
    at = 0
    for ref in refs:
        ref[...] = value[at : at + ref.shape[0]].astype(BF16)
        at += ref.shape[0]


def rows_of(plan, table_ref, name, *lead):
    top, length = plan.at[name]
    return table_ref[(*lead, slice(top, top + length), slice(None))]


def exchange(pieces, sizes, sign):
    lat, lon = lax.axis_size("lat"), lax.axis_size("lon")
    row, col, both = [piece[:size] for piece, size in zip(pieces, sizes)]
    pairs = [((i + sign) % lat * lon + (j + sign) % lon, i * lon + j) for i in range(lat) for j in range(lon)]
    col = lax.ppermute(col, "lon", [((j + sign) % lon, j) for j in range(lon)])
    both = lax.ppermute(both, ("lat", "lon"), pairs)
    row = lax.ppermute(row, "lat", [((i + sign) % lat, i) for i in range(lat)])
    return [row, col, both]


def choose(index, branches, *args):
    flat_args, tree = jax.tree.flatten(args)
    out_trees = []

    def closed(branch):
        def run(*leaves):
            out, out_tree = jax.tree.flatten(branch(*jax.tree.unflatten(tree, leaves)))
            out_trees.append(out_tree)
            return out

        return jax.make_jaxpr(run)(*flat_args)

    out = lax.cond_p.bind(index, *flat_args, branches=tuple(closed(branch) for branch in branches))
    return jax.tree.unflatten(out_trees[0], out)


FLAGS = ("three_class", "a", "big_a")


def first_pieces(shifts, tokens, plan):
    width = tokens.shape[-1]
    count = tokens.size // width
    kinds = 3

    def body(shifts_hbm, tokens_hbm, table_hbm, *refs):
        outs, refs = refs[:kinds], refs[kinds:]
        source_ref, rows_ref, flags_ref, *at_refs, shifts_ref, tokens_ref, table_ref, sems = refs
        start = Copies(sems)
        shift = start(shifts_hbm, shifts_ref)
        held = start(tokens_hbm, tokens_ref)
        table = start(table_hbm, table_ref)
        shift.wait()
        case = case_of(shifts_ref)
        for ref, name in zip(at_refs, ("one_at", "two_at", "three_at")):
            ref[0] = lookup(plan.flags[name], case)
        for n, name in enumerate(FLAGS):
            flags_ref[n] = lookup(plan.flags[name], case)
        held.wait()
        source_ref[...] = flat(tokens_ref)
        table.wait()
        rows_ref[...] = table_ref[case]
        index = columns_of(rows_of(plan, table_ref, "send_one", case), sum(plan.room_one))
        put_pieces(select_rows(index, source_ref[...]), outs)

    outs = shapes([*plan.room_one, count], width)
    outs += [pltpu.VMEM(plan.table.shape[1:], F32), pltpu.SMEM((8,), I32)]
    outs += [pltpu.SMEM((1,), I32)] * 3
    scratch = [pltpu.SMEM((2,), I32), pltpu.VMEM(tokens.shape, BF16), pltpu.VMEM(plan.table.shape, F32)]
    got = call(body, outs, [shifts, tokens, plan.table], [HBM] * 3, scratch, 3, 1 << 28, 1 << 20)
    sent, (source, rows, flags, one, two, three) = got[:kinds], got[kinds:]
    return sent, source, rows, flags, one[0], two[0], three[0]


def before_fine(flags, regions, tokens, table, weights, plan, rows, cols):
    _, lat, lon = regions.shape
    width = tokens.shape[1]
    flat_regions = regions.reshape(2 * lat, lon)
    fine, coarse = windowed(rows, cols), natural(rows // 2, cols // 2)

    def lanes(places, scale, is_fine):
        places = np.asarray([(l, scale * r, scale * c, is_fine) for l, r, c in places], np.float32)
        return np.pad(places, ((0, -len(places) % 128), (0, 0))).T.reshape(4, -1, 128)

    places = np.concatenate([lanes(fine, 1, 1), lanes(coarse, 2, 0)], axis=1)
    lines = places.shape[1]

    def body(flags_ref, rows_ref, tokens_ref, regions_hbm, places_hbm, *refs):
        weights_hbm, refs = refs[: len(weights)], refs[len(weights) :]
        id_ref, x_ref, *refs = refs
        weight_refs, (regions_ref, places_ref, sems) = refs[: len(weights)], refs[len(weights) :]
        start = Copies(sems)
        waits = [start(regions_hbm, regions_ref), start(places_hbm, places_ref)]
        later = [
            start(src.at[:, pl.ds(0, dst.shape[1])], dst) for src, dst in zip(weights_hbm, weight_refs)
        ]
        for copy in waits:
            copy.wait()
        a = flags_ref[1].astype(F32)
        big_a = 2.0 * flags_ref[2].astype(F32)
        is_fine = places_ref[3]
        d = is_fine * a + (1.0 - is_fine) * big_a
        row = places_ref[1] + d + (lax.axis_index("lat") * rows).astype(F32)
        col = places_ref[2] + 2.0 * d + (lax.axis_index("lon") * cols).astype(F32)
        wrapped = jnp.where((row < 0) | (row >= lat), 4.0, 0.0)
        row = jnp.where(row < 0, row + lat, jnp.where(row >= lat, row - lat, row))
        col = jnp.where(col < 0, col + lon, jnp.where(col >= lon, col - lon, col))
        row = row + places_ref[0] * lat

        def along(values):
            return jnp.concatenate([values[n : n + 1] for n in range(lines)], axis=1)

        line = lax.broadcasted_iota(I32, (2 * lat, 1), 0).astype(F32)
        pick = jnp.where(line == along(row), 1.0, 0.0).astype(BF16)
        known = regions_ref[...].astype(F32).astype(BF16)
        picked = lax.dot_general(known, pick, TN, preferred_element_type=F32)
        line = lax.broadcasted_iota(I32, (lon, 1), 0).astype(F32)
        ids = jnp.sum(jnp.where(line == along(col), picked, 0.0), axis=0, keepdims=True) + along(wrapped)
        for n in range(lines):
            id_ref[n : n + 1, :] = ids[:, n * 128 : (n + 1) * 128]
        take = columns_of(rows_of(plan, rows_ref, "take_one"), len(fine))
        x_ref[...] = select_rows(take, tokens_ref[...]).astype(BF16)
        for copy in later:
            copy.wait()

    outs = [pltpu.VMEM((lines, 128), F32)] + shapes([len(fine)], width)
    outs += [pltpu.VMEM((w.shape[0], min(w.shape[1], 2 * weights[1].shape[0])), BF16) for w in weights]
    scratch = [pltpu.VMEM(flat_regions.shape, I32), pltpu.VMEM(places.shape, F32)]
    args = [flags, table, tokens, flat_regions, places, *weights]
    in_specs = [SMEM, VMEM, VMEM] + [HBM] * (2 + len(weights))
    ids, x, *weights = call(body, outs, args, in_specs, scratch, 2 + len(weights), 1 << 28, 4 << 20)
    return ids, x, weights


def id_columns(lines, count):
    lane = lax.broadcasted_iota(I32, (1, 128), 1).astype(F32)
    return jnp.where(columns_of(lines, count) == lane, 1.0, 0.0).astype(BF16)


def before_coarse(flags, fine, table, weight, plan):
    own, width = fine.shape
    half = 5 * weight.shape[0] // 16

    def body(flags_ref, rows_ref, fine_ref, weight_hbm, x_ref, part_hbm, home_ref, weight_ref, part_ref, sems):
        start = Copies(sems)
        later = start(weight_hbm.at[pl.ds(0, half)], weight_ref)
        take = columns_of(rows_of(plan, rows_ref, "fine_out"), own)
        part_ref[...] = select_rows(take, fine_ref[...]).astype(BF16)
        leave = start(part_ref, part_hbm)
        take = columns_of(rows_of(plan, rows_ref, "take_two"), own)
        x_ref[...] = select_rows(take, fine_ref[...]).astype(BF16)

        @pl.when(needs_fine(flags_ref, plan))
        def _():
            index = columns_of(rows_of(plan, rows_ref, "send_four"), sum(plan.room_four))
            home_ref[...] = select_rows(index, fine_ref[...]).astype(BF16)

        leave.wait()
        later.wait()

    outs = shapes([own], width) + shapes([own], width, pltpu.HBM)
    outs += shapes([sum(plan.room_four)], width) + shapes([half], weight.shape[1])
    scratch = [pltpu.VMEM(fine.shape, BF16)]
    args = [flags, table, fine, weight]
    return call(body, outs, args, [SMEM, VMEM, VMEM, HBM], scratch, 2, 1 << 28, 4 << 20)


def needs_fine(flags_ref, plan):
    with_fine = [n for n, sizes in enumerate(plan.four) if sum(sizes)]
    return functools.reduce(jnp.logical_or, [flags_ref[0] == n for n in with_fine])


def fine_level(x_own, source, ids, w_qk, w_proj, w_qkv, rows, plan):
    count, width = x_own.shape
    inner = w_proj.shape[0]

    def body(own_ref, source_ref, ids_ref, qk_w_ref, proj_w_ref, qkv_w_hbm, rows_ref, out_ref, *refs):
        *piece_outs, x_ref, qkv_ref, id_ref, v_w_ref, sems = refs
        v_w = Copies(sems)(qkv_w_hbm.at[:, pl.ds(2 * inner, inner)], v_w_ref)
        id_ref[...] = id_columns(ids_ref[: -(-count // 128), :], count)
        take = columns_of(rows_of(plan, rows_ref, "take_one"), count) - float(count)
        x = own_ref[...].astype(F32) + select_rows(take, source_ref[...])
        x_ref[...] = x
        normed = layer_norm(x).astype(BF16)
        v_w.wait()
        qkv_ref[:, : 2 * inner] = jnp.dot(normed, qk_w_ref[...], preferred_element_type=F32).astype(BF16)
        qkv_ref[:, 2 * inner :] = jnp.dot(normed, v_w_ref[...], preferred_element_type=F32).astype(BF16)

        def finish(w, out):
            at = slice(w * TOK, (w + 1) * TOK)
            out = jnp.dot(out, proj_w_ref[...], preferred_element_type=F32)
            out_ref[at, :] = (x_ref[at, :] + out).astype(BF16)

        attend_windows(
            lambda w, at: qkv_ref[w * TOK : (w + 1) * TOK, at : at + 128],
            lambda w: id_ref[w * TOK : (w + 1) * TOK, :],
            count // TOK,
            inner,
            finish,
        )
        index = columns_of(rows_of(plan, rows_ref, "send_two"), sum(plan.room_two))
        put_pieces(select_rows(index, out_ref[...]), piece_outs)

    outs = shapes([count, *plan.room_two], width)
    scratch = [
        pltpu.VMEM((count, width), F32),
        pltpu.VMEM((count, 3 * inner), BF16),
        pltpu.VMEM((count, 128), BF16),
        pltpu.VMEM((width, inner), BF16),
    ]
    args = [x_own, source, ids, w_qk, w_proj, w_qkv, rows]
    out, *sent = call(body, outs, args, [VMEM] * 5 + [HBM, VMEM], scratch, 1, 3 << 30, 6 << 20, 14)
    return out, sent


def coarse_level(flags, home, x_own, source, ids, merge_first, w_merge, w_qkv, w_proj, rows, plan):
    depth, width = w_merge.shape
    own, half = x_own.shape
    count = own // 4
    inner = w_proj.shape[0]

    def body(
        flags_ref, merge_hbm, qkv_w_hbm, proj_w_hbm, home_ref, own_ref, source_ref, ids_ref, first_ref, rows_ref, *refs
    ):
        out_ref, *piece_outs = refs[:4]
        qkv_ref, id_ref, merge_ref, qkv_w_ref, proj_w_ref, sems = refs[4:]
        start = Copies(sems)
        here = first_ref.shape[0]
        merge_w = start(merge_hbm.at[pl.ds(here, depth - here)], merge_ref)
        qkv_w = start(qkv_w_hbm, qkv_w_ref)
        proj_w = start(proj_w_hbm, proj_w_ref)
        id_ref[...] = id_columns(ids_ref[-(-own // 128) :, :], count)
        take = columns_of(rows_of(plan, rows_ref, "take_two"), 4 * count) - float(own)
        x = own_ref[...].astype(F32) + select_rows(take, source_ref[...])
        x = jnp.concatenate([x[n * count : (n + 1) * count] for n in range(4)], axis=1)
        stacked = layer_norm(x).astype(BF16)
        merge_w.wait()
        merged = jnp.dot(stacked[:, :here], first_ref[...], preferred_element_type=F32)
        merged = merged + jnp.dot(stacked[:, here:], merge_ref[...], preferred_element_type=F32)
        merged = merged.astype(BF16).astype(F32)
        normed = layer_norm(merged).astype(BF16)
        qkv_w.wait()
        proj_w.wait()
        qkv_ref[...] = jnp.dot(normed, qkv_w_ref[...], preferred_element_type=F32).astype(BF16)

        def finish(w, out):
            out = jnp.dot(out, proj_w_ref[...], preferred_element_type=F32)
            out_ref[...] = (merged + out).astype(BF16)

        attend_windows(lambda w, at: qkv_ref[:, at : at + 128], lambda w: id_ref[...], 1, inner, finish)
        sent = select_rows(columns_of(rows_of(plan, rows_ref, "send_three"), sum(plan.room_three)), out_ref[...])
        sent = sent.astype(BF16)
        for n, sizes in enumerate(plan.three):

            @pl.when(flags_ref[0] == n)
            def _():
                at = 0
                for ref, size, space in zip(piece_outs, sizes, plan.room_three):
                    ref[:size, :] = sent[at : at + size, :half]
                    ref[size : 2 * size, :] = sent[at : at + size, half:]
                    at += space

        for n, fine_sizes in enumerate(plan.four):
            if sum(fine_sizes):

                @pl.when(flags_ref[0] == n)
                def _():
                    at = 0
                    for ref, size, more, space in zip(piece_outs, plan.three[n], fine_sizes, plan.room_four):
                        ref[2 * size : 2 * size + more, :] = home_ref[at : at + more, :]
                        at += space

    most = [max(2 * three[k] + four[k] for three, four in zip(plan.three, plan.four)) for k in range(3)]
    outs = shapes([count], width) + shapes(most, half)
    scratch = [pltpu.VMEM((count, 3 * inner), BF16)]
    shapes_in = [(count, 128), (depth - merge_first.shape[0], width), w_qkv.shape, w_proj.shape]
    scratch += [pltpu.VMEM(shape, BF16) for shape in shapes_in]
    args = [flags, w_merge, w_qkv, w_proj, home, x_own, source, ids, merge_first, rows]
    in_specs = [SMEM] + [HBM] * 3 + [VMEM] * (len(args) - 4)
    out, *sent = call(body, outs, args, in_specs, scratch, 3, 3 << 30, 12 << 20, 24)
    return out, sent


def fine_output(part, source, rows, plan, block_rows, block_cols, partial):
    own, width = part.shape

    def body(part_hbm, source_ref, rows_ref, out_ref, part_ref, stage_ref, sems):
        start = Copies(sems)
        cuts = [pl.ds(at, TOK) for at in range(0, own, TOK)]
        held = [start(part_hbm.at[cut], part_ref.at[cut]) for cut in cuts]
        take = columns_of(rows_of(plan, rows_ref, "fine_out"), own) - float(own)
        leave = []
        for n, (cut, copy) in enumerate(zip(cuts, held)):
            got = select_rows(take[n * TOK : (n + 1) * TOK], source_ref[...])
            copy.wait()
            out = part_ref[cut, :].astype(F32) + got
            if partial:
                out_ref[cut, :] = out.astype(BF16)
            else:
                lines = TOK // block_cols
                layer, line = divmod(n * lines, block_rows)
                there = (layer, pl.ds(line, lines))
                stage_ref[there] = out.reshape(lines, block_cols, width).astype(BF16)
                leave.append(start(stage_ref.at[there], out_ref.at[there]))
        for copy in leave:
            copy.wait()

    shape = (2, block_rows, block_cols, width)
    outs = shapes([own], width) if partial else [pltpu.HBM(shape, BF16)]
    scratch = [pltpu.VMEM(part.shape, BF16), pltpu.VMEM(shape, BF16)]
    return call(body, outs, [part, source, rows], [HBM, VMEM, VMEM], scratch, 2 * own // TOK, 1 << 30, 4 << 20)[0]


def coarse_output(coarse, got, rows, which, plan, block_rows, block_cols, part=None):
    own, width = coarse.shape
    half = width // 2
    sizes, more = plan.three[which], plan.four[which]
    parts = [] if part is None else [part]

    def padded(parts, sizes, room):
        out = []
        for value, size, space in zip(parts, sizes, room):
            out.append(value)
            if size < space:
                out.append(jnp.zeros((space - size, value.shape[1]), F32))
        return out

    def body(coarse_ref, *refs):
        got_refs, refs = refs[:3], refs[3:]
        part_refs, (rows_ref, out_ref, *fine_outs, _) = refs[: len(parts)], refs[len(parts) :]
        got = [ref[...].astype(F32) for ref in got_refs]
        back = [jnp.concatenate([x[:size], x[size : 2 * size]], axis=1) for x, size in zip(got, sizes)]
        source = stack_rows([coarse_ref[...].astype(F32)] + padded(back, sizes, plan.room_three))
        out = select_rows(columns_of(rows_of(plan, rows_ref, "coarse_out"), own), source.astype(BF16)).astype(BF16)
        for n in range(own // 2):
            out_ref[n // block_cols, n % block_cols] = out[2 * n : 2 * n + 2]
        for part_ref, fine_ref in zip(part_refs, fine_outs):
            fine = stack_rows(padded([x[2 * size :] for x, size in zip(got, sizes)], more, plan.room_four))
            base = part_ref.shape[0] + sum(plan.room_two)
            take = columns_of(rows_of(plan, rows_ref, "fine_out"), part_ref.shape[0]) - float(base)
            out = part_ref[...].astype(F32) + select_rows(take, fine.astype(BF16))
            fine_ref[...] = out.reshape(fine_ref.shape).astype(BF16)

    outs = [jax.ShapeDtypeStruct((block_rows, block_cols, 2, width), BF16)]
    outs += [jax.ShapeDtypeStruct((2, 2 * block_rows, 2 * block_cols, half), BF16) for _ in parts]
    args = [coarse, *got, *parts, rows]
    out, *fine = call(body, outs, args, [VMEM] * len(args), [], 1, 1 << 28, 1 << 20)
    return out.transpose(2, 0, 1, 3), *fine


def on_device(tokens, regions, shifts, fine_qkv, fine_proj, merge_weight, coarse_qkv, coarse_proj):
    _, rows, cols, _ = tokens.shape
    plan = Plan(rows, cols)

    def first(which, sign, sent, *args):
        got = exchange(sent, plan.one[which], sign)
        return lay(got, plan.room_one), before_fine(*args, plan, rows, cols)

    def second(which, sign, sent, *args):
        got = exchange(sent, plan.two[which], sign)
        return lay(got, plan.room_two), before_coarse(*args, plan)

    def third(which, sign, sent, part, source, coarse, table):
        sizes = [2 * n + m for n, m in zip(plan.three[which], plan.four[which])]
        got = exchange(sent, sizes, sign)
        partial = sum(plan.four[which]) > 0
        fine_out = fine_output(part, source, table, plan, rows, cols, partial)
        place = (table, which, plan, rows // 2, cols // 2)
        if partial:
            coarse_out, fine_out = coarse_output(coarse, got, *place, part=fine_out)
        else:
            (coarse_out,) = coarse_output(coarse, got, *place)
        return fine_out, coarse_out

    def branches(stage, pairs):
        return [functools.partial(stage, which, sign) for which, sign in pairs]

    sent, source, table, flags, one, two, three = first_pieces(shifts, tokens, plan)
    got, (ids, x, weights) = choose(
        one, branches(first, plan.one_branches), sent, flags, regions, source, table, [fine_qkv, fine_proj]
    )
    fine, sent = fine_level(x, got, ids, *weights, fine_qkv, table, plan)
    got, (x, part, home, merge_first) = choose(
        two, branches(second, plan.two_branches), sent, flags, fine, table, merge_weight
    )
    coarse, sent = coarse_level(
        flags, home, x, got, ids, merge_first, merge_weight, coarse_qkv, coarse_proj, table, plan
    )
    return choose(three, branches(third, plan.three_branches), sent, part, got, coarse, table)


def solution(mesh):
    return jax.shard_map(
        on_device,
        mesh=mesh,
        in_specs=(P(None, "lat", "lon", None), P(), P(), P(), P(), P(), P(), P()),
        out_specs=(P(None, "lat", "lon", None), P(None, "lat", "lon", None)),
        check_vma=False,
    )
```

```python
import functools

import jax
import jax.numpy as jnp
import numpy as np
from jax import lax
from jax.experimental import pallas as pl
from jax.experimental.pallas import tpu as pltpu
from jax.sharding import PartitionSpec as P

HD = 32
WH = 6
WW = 12
TOK = 2 * WH * WW
EPS = 1e-05
BIG = 1e30
SCALE = float(np.log2(np.e) / np.sqrt(HD))

NT = (((1,), (1,)), ((), ()))
TN = (((0,), (0,)), ((), ()))
F32 = jnp.float32
BF16 = jnp.bfloat16
I32 = jnp.int32

PAIRS = [(WH - 1, t) for t in range(1, WH)] + [(t, WH - 1) for t in range(1, WH - 1)]


def up16(count):
    return -(-count // 16) * 16


def natural(rows, cols):
    return [(l, r, c) for l in range(2) for r in range(rows) for c in range(cols)]


def windowed(rows, cols):
    return [
        (l, wr * WH + r, wc * WW + c)
        for wr in range(rows // WH)
        for wc in range(cols // WW)
        for l in range(2)
        for r in range(WH)
        for c in range(WW)
    ]


def moved(order, d):
    return [(l, r + d, c + 2 * d) for l, r, c in order]


def exchange_places(held, wanted, rows, cols, sign):
    at = {place: n for n, place in enumerate(held)}
    found = []
    for dr, dc in ((sign, 0), (0, sign), (sign, sign)):
        numbers, places = [], []
        for l, r, c in sorted(set(wanted) - set(held)):
            n = at.get((l, r - dr * rows, c - dc * cols))
            if n is not None:
                numbers.append(n)
                places.append((l, r, c))
        found.append((numbers, places))
    return found


def offsets(t0, t1):
    a = t0 if t0 <= 2 else t0 - WH
    big_a = t1 if t1 <= 2 else t1 - WH
    ahead = 1 if 2 * big_a > a or 2 * big_a - a == 0 and a < 0 else -1
    return a, big_a, ahead


def classes_of(needs, slack):
    rounded = [tuple(-(-size // 8) * 8 for size in need) for need in needs]
    heavy = [sum(need[1:3]) * 2 + sum(need[4:]) for need in rounded]
    limits = []
    for size in sorted(set(heavy)):
        if not limits or size > limits[-1][0] * slack:
            limits.append([size, size])
        limits[-1][1] = size
    which = [next(n for n, limit in enumerate(limits) if size <= limit[1]) for size in heavy]
    sizes = [
        [max(need[k] for need, w in zip(rounded, which) if w == n) for k in range(len(needs[0]))]
        for n in range(len(limits))
    ]
    return sizes, which


def rooms(sizes):
    return [up16(max(size[k] for size in sizes)) for k in range(len(sizes[0]))]


class Plan:
    def __init__(self, rows, cols):
        crows, ccols = rows // 2, cols // 2
        block, cblock = natural(rows, cols), natural(crows, ccols)
        cases = []
        for t0, t1 in PAIRS:
            a, big_a, ahead = offsets(t0, t1)
            fine = moved(windowed(rows, cols), a)
            coarse = moved(cblock, big_a)
            quarters = [
                (l, 2 * r + dr, 2 * c + dc)
                for dr, dc in ((0, 0), (1, 0), (0, 1), (1, 1))
                for l, r, c in coarse
            ]
            come = 1 if a > 0 else -1
            one = exchange_places(block, fine, rows, cols, come)
            home = [p for p in block if p not in set(fine)]
            wanted = quarters + (home if come == -ahead else [])
            two = exchange_places(fine, wanted, rows, cols, ahead)
            back = 1 if big_a < 0 else -1
            three = exchange_places(coarse, cblock, crows, ccols, back)
            got = set(fine).union(*[places for _, places in two])
            four = exchange_places(fine, [p for p in block if p not in got], rows, cols, back)
            cases.append((come, ahead, back, fine, coarse, quarters, one, two, three, four))

        def needs(which):
            return [[len(numbers) for numbers, _ in case[which]] for case in cases]

        self.one, one_class = classes_of(needs(6), 1.15)
        self.two, two_class = classes_of(needs(7), 1.15)
        sizes, three_class = classes_of([three + four for three, four in zip(needs(8), needs(9))], 1.0)
        self.three, self.four = [size[:3] for size in sizes], [size[3:] for size in sizes]
        self.room_one, self.room_two = rooms(self.one), rooms(self.two)
        self.room_three, self.room_four = rooms(self.three), rooms(self.four)

        def branches(which_class, direction):
            pairs = [(n, case[direction]) for n, case in zip(which_class, cases)]
            found = sorted(set(pairs))
            return found, [found.index(pair) for pair in pairs]

        self.one_branches, one_at = branches(one_class, 0)
        self.two_branches, two_at = branches(two_class, 1)
        self.three_branches, three_at = branches(three_class, 2)
        self.flags = dict(
            three_class=three_class, two_class=two_class,
            one_at=one_at, two_at=two_at, three_at=three_at,
            a=[offsets(*pair)[0] for pair in PAIRS], big_a=[offsets(*pair)[1] for pair in PAIRS],
        )

        found = {}
        for n, (come, ahead, back, fine, coarse, quarters, one, two, three, four) in enumerate(cases):

            def send(exchanged, room):
                return [n for (numbers, _), size in zip(exchanged, room) for n in numbers + [-1] * (size - len(numbers))]

            def source(held, *exchanges):
                places = list(held)
                for exchanged, room in exchanges:
                    for (_, got), size in zip(exchanged, room):
                        places += got + [None] * (size - len(got))
                return {p: n for n, p in enumerate(places) if p is not None}

            first, second = source(block, (one, self.room_one)), source(fine, (two, self.room_two))
            third = source(coarse, (three, self.room_three))
            last = source(fine, (two, self.room_two), (four, self.room_four))
            out = [(l, r, c) for r in range(crows) for c in range(ccols) for l in range(2)]
            rows_of = dict(
                send_one=send(one, self.room_one),
                take_one=[first[p] for p in fine],
                send_two=send(two, self.room_two),
                take_two=[second[p] for p in quarters],
                send_three=send(three, self.room_three),
                send_four=send(four, self.room_four),
                fine_out=[last[p] for p in block],
                coarse_out=[third[p] for p in out],
            )
            for name, row in rows_of.items():
                found.setdefault(name, []).append(row)
        parts, self.at, top = [], {}, 0
        for name, lists in found.items():
            length = -(-max(len(row) for row in lists) // 128)
            part = np.full((len(PAIRS), length * 128), -1, np.float32)
            for n, row in enumerate(lists):
                part[n, : len(row)] = row
            parts.append(part.reshape(len(PAIRS), length, 128))
            self.at[name] = (top, length)
            top += length
        parts.append(np.zeros((len(PAIRS), -top % 8, 128), np.float32))
        self.table = np.concatenate(parts, axis=1)


def case_of(shifts_ref):
    t0, t1 = shifts_ref[0], shifts_ref[1]
    return jnp.where(t0 == WH - 1, t1 - 1, t0 + WH - 2)


def lookup(values, case):
    out = jnp.int32(values[0])
    for n, value in enumerate(values[1:], 1):
        out = jnp.where(case == n, value, out)
    return out


def columns_of(rows, count):
    parts = [jnp.broadcast_to(rows[j : j + 1], (128, 128)).T for j in range(-(-count // 128))]
    return stack_rows(parts)[:count]


def selection(index, size):
    lane = lax.broadcasted_iota(I32, (1, 128), 1).astype(F32)
    pick = [jnp.where(index == lane + float(at), 1.0, 0.0).astype(BF16) for at in range(0, size, 128)]
    return jnp.concatenate(pick, axis=1)[:, :size]


def select_rows(index, source):
    return jnp.dot(selection(index, source.shape[0]), source, preferred_element_type=F32)


def stack_rows(parts):
    return parts[0] if len(parts) == 1 else jnp.concatenate(parts, axis=0)


def layer_norm(values):
    center = jnp.mean(values, axis=-1, keepdims=True)
    values = values - center
    spread = jnp.mean(values * values, axis=-1, keepdims=True)
    return values * lax.rsqrt(spread + EPS)


def attend_windows(qkv_of, id_of, windows, inner, finish):
    lane = lax.broadcasted_iota(I32, (1, 128), 1)
    forbid = jnp.where(lane < 8, BIG, 0.0).astype(BF16)
    groups = inner // 128
    units = [(w, g) for w in range(windows) for g in range(groups)]
    scores, weights, outs = {}, {}, {}

    def score(w, g):
        key_id = id_of(w)
        not_id = (key_id - 1).astype(BF16) * forbid
        q = qkv_of(w, g * 128)
        keys = jnp.concatenate([qkv_of(w, inner + g * 128), key_id], axis=1)
        queries = []
        for h in range(4):
            mine = jnp.where((lane >= h * HD) & (lane < (h + 1) * HD), 1.0, 0.0).astype(BF16)
            queries.append(jnp.concatenate([q * mine, not_id], axis=1))
        scores[w, g] = lax.dot_general(stack_rows(queries), keys, NT, preferred_element_type=F32)

    def soften(w, g):
        s = scores.pop((w, g))
        weights[w, g] = jnp.exp2((s - jnp.max(s, axis=1, keepdims=True)) * SCALE).astype(BF16)

    def gather(w, g):
        v = qkv_of(w, 2 * inner + g * 128)
        values = jnp.concatenate([v, jnp.ones_like(v)], axis=1)
        out = jnp.dot(weights.pop((w, g)), values, preferred_element_type=F32)
        picked, total = out[:TOK, :128], out[:TOK, 128:]
        for h in range(1, 4):
            rows = slice(h * TOK, (h + 1) * TOK)
            picked = jnp.where(lane < h * HD, picked, out[rows, :128])
            total = jnp.where(lane < h * HD, total, out[rows, 128:])
        outs[w, g] = (picked / total).astype(BF16)
        if g == groups - 1:
            finish(w, jnp.concatenate([outs.pop((w, k)) for k in range(groups)], axis=1))

    for n in range(len(units) + 2):
        if n < len(units):
            score(*units[n])
        if 0 <= n - 1 < len(units):
            soften(*units[n - 1])
        if 0 <= n - 2 < len(units):
            gather(*units[n - 2])


ANY = pl.BlockSpec(memory_space=pl.ANY)
HBM = pl.BlockSpec(memory_space=pltpu.HBM)
VMEM = pl.BlockSpec(memory_space=pltpu.VMEM)
SMEM = pl.BlockSpec(memory_space=pltpu.SMEM)


def call(body, outs, args, in_specs, scratch, copies, flops, moved_bytes, vmem=8):
    args = [
        pltpu.with_memory_space_constraint(arg, spec.memory_space) for arg, spec in zip(args, in_specs, strict=True)
    ]
    spaces = [getattr(out, "memory_space", pltpu.SMEM if out.dtype == I32 else pltpu.VMEM) for out in outs]
    out_specs = [pl.BlockSpec(memory_space=space) for space in spaces]
    return pl.pallas_call(
        body,
        out_shape=outs,
        in_specs=in_specs,
        out_specs=out_specs,
        scratch_shapes=list(scratch) + [pltpu.SemaphoreType.DMA((copies,))],
        compiler_params=pltpu.CompilerParams(vmem_limit_bytes=vmem << 20),
        cost_estimate=pl.CostEstimate(flops=flops, bytes_accessed=moved_bytes, transcendentals=0),
    )(*args)


def shapes(sizes, width, space=pltpu.VMEM):
    return [space((n, width), BF16) for n in sizes]


class Copies:
    def __init__(self, sems):
        self.sems, self.used = sems, 0

    def __call__(self, src, dst):
        copy = pltpu.make_async_copy(src, dst, self.sems.at[self.used])
        self.used += 1
        copy.start()
        return copy


def lay(pieces, room):
    width = pieces[0].shape[1]

    def body(*refs):
        out_ref = refs[len(pieces)]
        at = 0
        for ref, space in zip(refs, room):
            rows = ref.shape[0]
            out_ref[at : at + rows, :] = ref[...]
            if rows < space:
                out_ref[at + rows : at + space, :] = jnp.zeros((space - rows, width), BF16)
            at += space

    return call(body, shapes([sum(room)], width), pieces, [VMEM] * 3, [], 1, 0, 1 << 18)[0]


def flat(ref):
    layers, rows, cols, width = ref.shape
    return ref[...].astype(F32).reshape(layers * rows * cols, width).astype(BF16)


def put_pieces(value, refs):
    at = 0
    for ref in refs:
        ref[...] = value[at : at + ref.shape[0]].astype(BF16)
        at += ref.shape[0]


def rows_of(plan, table_ref, name, *lead):
    top, length = plan.at[name]
    return table_ref[(*lead, slice(top, top + length), slice(None))]


def exchange(pieces, sizes, sign):
    lat, lon = lax.axis_size("lat"), lax.axis_size("lon")
    row, col, both = [piece[:size] for piece, size in zip(pieces, sizes)]
    pairs = [((i + sign) % lat * lon + (j + sign) % lon, i * lon + j) for i in range(lat) for j in range(lon)]
    col = lax.ppermute(col, "lon", [((j + sign) % lon, j) for j in range(lon)])
    both = lax.ppermute(both, ("lat", "lon"), pairs)
    row = lax.ppermute(row, "lat", [((i + sign) % lat, i) for i in range(lat)])
    return [row, col, both]


def choose(index, branches, *args):
    flat_args, tree = jax.tree.flatten(args)
    out_trees = []

    def closed(branch):
        def run(*leaves):
            out, out_tree = jax.tree.flatten(branch(*jax.tree.unflatten(tree, leaves)))
            out_trees.append(out_tree)
            return out

        return jax.make_jaxpr(run)(*flat_args)

    out = lax.cond_p.bind(index, *flat_args, branches=tuple(closed(branch) for branch in branches))
    return jax.tree.unflatten(out_trees[0], out)


FLAGS = ("three_class", "a", "big_a", "two_class")


def first_pieces(shifts, tokens, plan):
    width = tokens.shape[-1]
    count = tokens.size // width
    kinds = 3

    def body(shifts_hbm, tokens_hbm, table_hbm, *refs):
        outs, refs = refs[:kinds], refs[kinds:]
        source_ref, rows_ref, flags_ref, *at_refs, shifts_ref, tokens_ref, table_ref, sems = refs
        start = Copies(sems)
        shift = start(shifts_hbm, shifts_ref)
        held = start(tokens_hbm, tokens_ref)
        table = start(table_hbm, table_ref)
        shift.wait()
        case = case_of(shifts_ref)
        for ref, name in zip(at_refs, ("one_at", "two_at", "three_at")):
            ref[0] = lookup(plan.flags[name], case)
        for n, name in enumerate(FLAGS):
            flags_ref[n] = lookup(plan.flags[name], case)
        table.wait()
        rows_ref[...] = table_ref[case]
        index = columns_of(rows_of(plan, table_ref, "send_one", case), sum(plan.room_one))
        pick = selection(index, count)
        held.wait()
        source = flat(tokens_ref)
        source_ref[...] = source
        put_pieces(jnp.dot(pick, source, preferred_element_type=F32), outs)

    outs = shapes([*plan.room_one, count], width)
    outs += [pltpu.VMEM(plan.table.shape[1:], F32), pltpu.SMEM((8,), I32)]
    outs += [pltpu.SMEM((1,), I32)] * 3
    scratch = [pltpu.SMEM((2,), I32), pltpu.VMEM(tokens.shape, BF16), pltpu.VMEM(plan.table.shape, F32)]
    got = call(body, outs, [shifts, tokens, plan.table], [HBM] * 3, scratch, 3, 1 << 28, 1 << 20)
    sent, (source, rows, flags, one, two, three) = got[:kinds], got[kinds:]
    return sent, source, rows, flags, one[0], two[0], three[0]


def before_fine(flags, regions, tokens, table, weights, plan, rows, cols):
    _, lat, lon = regions.shape
    width = tokens.shape[1]
    flat_regions = regions.reshape(2 * lat, lon)
    fine, coarse = windowed(rows, cols), natural(rows // 2, cols // 2)

    def lanes(places, scale, is_fine):
        places = np.asarray([(l, scale * r, scale * c, is_fine) for l, r, c in places], np.float32)
        return np.pad(places, ((0, -len(places) % 128), (0, 0))).T.reshape(4, -1, 128)

    places = np.concatenate([lanes(fine, 1, 1), lanes(coarse, 2, 0)], axis=1)
    lines = places.shape[1]

    def body(flags_ref, rows_ref, tokens_ref, regions_hbm, places_hbm, *refs):
        weights_hbm, refs = refs[: len(weights)], refs[len(weights) :]
        id_ref, x_ref, *refs = refs
        weight_refs, (regions_ref, places_ref, sems) = refs[: len(weights)], refs[len(weights) :]
        start = Copies(sems)
        waits = [start(regions_hbm, regions_ref), start(places_hbm, places_ref)]
        later = [
            start(src.at[:, pl.ds(0, dst.shape[1])], dst) for src, dst in zip(weights_hbm, weight_refs)
        ]
        for copy in waits:
            copy.wait()
        a = flags_ref[1].astype(F32)
        big_a = 2.0 * flags_ref[2].astype(F32)
        is_fine = places_ref[3]
        d = is_fine * a + (1.0 - is_fine) * big_a
        row = places_ref[1] + d + (lax.axis_index("lat") * rows).astype(F32)
        col = places_ref[2] + 2.0 * d + (lax.axis_index("lon") * cols).astype(F32)
        wrapped = jnp.where((row < 0) | (row >= lat), 4.0, 0.0)
        row = jnp.where(row < 0, row + lat, jnp.where(row >= lat, row - lat, row))
        col = jnp.where(col < 0, col + lon, jnp.where(col >= lon, col - lon, col))
        row = row + places_ref[0] * lat

        def along(values):
            return jnp.concatenate([values[n : n + 1] for n in range(lines)], axis=1)

        line = lax.broadcasted_iota(I32, (2 * lat, 1), 0).astype(F32)
        pick = jnp.where(line == along(row), 1.0, 0.0).astype(BF16)
        known = regions_ref[...].astype(F32).astype(BF16)
        picked = lax.dot_general(known, pick, TN, preferred_element_type=F32)
        line = lax.broadcasted_iota(I32, (lon, 1), 0).astype(F32)
        ids = jnp.sum(jnp.where(line == along(col), picked, 0.0), axis=0, keepdims=True) + along(wrapped)
        for n in range(lines):
            id_ref[n : n + 1, :] = ids[:, n * 128 : (n + 1) * 128]
        take = columns_of(rows_of(plan, rows_ref, "take_one"), len(fine))
        x_ref[...] = select_rows(take, tokens_ref[...]).astype(BF16)
        for copy in later:
            copy.wait()

    outs = [pltpu.VMEM((lines, 128), F32)] + shapes([len(fine)], width)
    outs += [pltpu.VMEM((w.shape[0], min(w.shape[1], 2 * weights[1].shape[0])), BF16) for w in weights]
    scratch = [pltpu.VMEM(flat_regions.shape, I32), pltpu.VMEM(places.shape, F32)]
    args = [flags, table, tokens, flat_regions, places, *weights]
    in_specs = [SMEM, VMEM, VMEM] + [HBM] * (2 + len(weights))
    ids, x, *weights = call(body, outs, args, in_specs, scratch, 2 + len(weights), 1 << 28, 4 << 20)
    return ids, x, weights


def id_columns(lines, count):
    lane = lax.broadcasted_iota(I32, (1, 128), 1).astype(F32)
    return jnp.where(columns_of(lines, count) == lane, 1.0, 0.0).astype(BF16)


def before_coarse(flags, fine, table, weight, plan):
    own, width = fine.shape
    half = 5 * weight.shape[0] // 16

    def body(flags_ref, rows_ref, fine_ref, weight_hbm, x_ref, part_hbm, home_ref, weight_ref, part_ref, sems):
        start = Copies(sems)
        later = start(weight_hbm.at[pl.ds(0, half)], weight_ref)
        take = columns_of(rows_of(plan, rows_ref, "fine_out"), own)
        part_ref[...] = select_rows(take, fine_ref[...]).astype(BF16)
        leave = start(part_ref, part_hbm)
        take = columns_of(rows_of(plan, rows_ref, "take_two"), own)
        x_ref[...] = select_rows(take, fine_ref[...]).astype(BF16)

        @pl.when(needs_fine(flags_ref, plan))
        def _():
            index = columns_of(rows_of(plan, rows_ref, "send_four"), sum(plan.room_four))
            home_ref[...] = select_rows(index, fine_ref[...]).astype(BF16)

        leave.wait()
        later.wait()

    outs = shapes([own], width) + shapes([own], width, pltpu.HBM)
    outs += shapes([sum(plan.room_four)], width) + shapes([half], weight.shape[1])
    scratch = [pltpu.VMEM(fine.shape, BF16)]
    args = [flags, table, fine, weight]
    return call(body, outs, args, [SMEM, VMEM, VMEM, HBM], scratch, 2, 1 << 28, 4 << 20)


def needs_fine(flags_ref, plan):
    with_fine = [n for n, sizes in enumerate(plan.four) if sum(sizes)]
    return functools.reduce(jnp.logical_or, [flags_ref[0] == n for n in with_fine])


def fine_level(flags, x_own, source, ids, w_qk, w_proj, w_qkv, rows, plan):
    count, width = x_own.shape
    inner = w_proj.shape[0]

    few = [n for n, size in enumerate(plan.two) if size[1] <= 128]
    first = [up16(max(plan.two[n][k] for n in few)) for k in range(3)]
    tops = [sum(plan.room_two[:k]) for k in range(3)]

    def body(flags_ref, own_ref, source_ref, ids_ref, qk_w_ref, proj_w_ref, qkv_w_hbm, rows_ref, out_ref, *refs):
        *piece_outs, x_ref, qkv_ref, id_ref, v_w_ref, sems = refs
        v_w = Copies(sems)(qkv_w_hbm.at[:, pl.ds(2 * inner, inner)], v_w_ref)
        id_ref[...] = id_columns(ids_ref[: -(-count // 128), :], count)
        take = columns_of(rows_of(plan, rows_ref, "take_one"), count) - float(count)
        x = own_ref[...].astype(F32) + select_rows(take, source_ref[...])
        x_ref[...] = x
        normed = layer_norm(x).astype(BF16)
        v_w.wait()
        qkv_ref[:, : 2 * inner] = jnp.dot(normed, qk_w_ref[...], preferred_element_type=F32).astype(BF16)
        qkv_ref[:, 2 * inner :] = jnp.dot(normed, v_w_ref[...], preferred_element_type=F32).astype(BF16)

        def finish(w, out):
            at = slice(w * TOK, (w + 1) * TOK)
            out = jnp.dot(out, proj_w_ref[...], preferred_element_type=F32)
            out_ref[at, :] = (x_ref[at, :] + out).astype(BF16)

        attend_windows(
            lambda w, at: qkv_ref[w * TOK : (w + 1) * TOK, at : at + 128],
            lambda w: id_ref[w * TOK : (w + 1) * TOK, :],
            count // TOK,
            inner,
            finish,
        )
        index = columns_of(rows_of(plan, rows_ref, "send_two"), sum(plan.room_two))

        def send(cuts):
            picked = stack_rows([index[top + low : top + high] for top, (low, high) in zip(tops, cuts)])
            picked = select_rows(picked, out_ref[...]).astype(BF16)
            at = 0
            for ref, (low, high) in zip(piece_outs, cuts):
                ref[low:high, :] = picked[at : at + high - low]
                at += high - low

        send([(0, size) for size in first])

        @pl.when(flags_ref[3] > max(few))
        def _():
            send(list(zip(first, plan.room_two)))

    outs = shapes([count, *plan.room_two], width)
    scratch = [
        pltpu.VMEM((count, width), F32),
        pltpu.VMEM((count, 3 * inner), BF16),
        pltpu.VMEM((count, 128), BF16),
        pltpu.VMEM((width, inner), BF16),
    ]
    args = [flags, x_own, source, ids, w_qk, w_proj, w_qkv, rows]
    out, *sent = call(body, outs, args, [SMEM] + [VMEM] * 5 + [HBM, VMEM], scratch, 1, 3 << 30, 6 << 20, 14)
    return out, sent


def coarse_level(flags, home, x_own, source, ids, merge_first, w_merge, w_qkv, w_proj, rows, plan):
    depth, width = w_merge.shape
    own, half = x_own.shape
    count = own // 4
    inner = w_proj.shape[0]

    def body(
        flags_ref, merge_hbm, qkv_w_hbm, proj_w_hbm, home_ref, own_ref, source_ref, ids_ref, first_ref, rows_ref, *refs
    ):
        out_ref, *piece_outs = refs[:4]
        qkv_ref, id_ref, merge_ref, qkv_w_ref, proj_w_ref, sems = refs[4:]
        start = Copies(sems)
        here = first_ref.shape[0]
        merge_w = start(merge_hbm.at[pl.ds(here, depth - here)], merge_ref)
        qkv_w = start(qkv_w_hbm, qkv_w_ref)
        proj_w = start(proj_w_hbm, proj_w_ref)
        id_ref[...] = id_columns(ids_ref[-(-own // 128) :, :], count)
        take = columns_of(rows_of(plan, rows_ref, "take_two"), 4 * count) - float(own)
        x = own_ref[...].astype(F32) + select_rows(take, source_ref[...])
        x = jnp.concatenate([x[n * count : (n + 1) * count] for n in range(4)], axis=1)
        stacked = layer_norm(x).astype(BF16)
        merge_w.wait()
        merged = jnp.dot(stacked[:, :here], first_ref[...], preferred_element_type=F32)
        merged = merged + jnp.dot(stacked[:, here:], merge_ref[...], preferred_element_type=F32)
        merged = merged.astype(BF16).astype(F32)
        normed = layer_norm(merged).astype(BF16)
        qkv_w.wait()
        proj_w.wait()
        qkv_ref[...] = jnp.dot(normed, qkv_w_ref[...], preferred_element_type=F32).astype(BF16)

        def finish(w, out):
            out = jnp.dot(out, proj_w_ref[...], preferred_element_type=F32)
            out_ref[...] = (merged + out).astype(BF16)

        attend_windows(lambda w, at: qkv_ref[:, at : at + 128], lambda w: id_ref[...], 1, inner, finish)
        sent = select_rows(columns_of(rows_of(plan, rows_ref, "send_three"), sum(plan.room_three)), out_ref[...])
        sent = sent.astype(BF16)
        for n, sizes in enumerate(plan.three):

            @pl.when(flags_ref[0] == n)
            def _():
                at = 0
                for ref, size, space in zip(piece_outs, sizes, plan.room_three):
                    ref[:size, :] = sent[at : at + size, :half]
                    ref[size : 2 * size, :] = sent[at : at + size, half:]
                    at += space

        for n, fine_sizes in enumerate(plan.four):
            if sum(fine_sizes):

                @pl.when(flags_ref[0] == n)
                def _():
                    at = 0
                    for ref, size, more, space in zip(piece_outs, plan.three[n], fine_sizes, plan.room_four):
                        ref[2 * size : 2 * size + more, :] = home_ref[at : at + more, :]
                        at += space

    most = [max(2 * three[k] + four[k] for three, four in zip(plan.three, plan.four)) for k in range(3)]
    outs = shapes([count], width) + shapes(most, half)
    scratch = [pltpu.VMEM((count, 3 * inner), BF16)]
    shapes_in = [(count, 128), (depth - merge_first.shape[0], width), w_qkv.shape, w_proj.shape]
    scratch += [pltpu.VMEM(shape, BF16) for shape in shapes_in]
    args = [flags, w_merge, w_qkv, w_proj, home, x_own, source, ids, merge_first, rows]
    in_specs = [SMEM] + [HBM] * 3 + [VMEM] * (len(args) - 4)
    out, *sent = call(body, outs, args, in_specs, scratch, 3, 3 << 30, 12 << 20, 24)
    return out, sent


def fine_output(part, source, rows, plan, block_rows, block_cols, partial):
    own, width = part.shape

    def body(part_hbm, source_ref, rows_ref, out_ref, part_ref, stage_ref, sems):
        start = Copies(sems)
        cuts = [pl.ds(at, TOK) for at in range(0, own, TOK)]
        held = [start(part_hbm.at[cut], part_ref.at[cut]) for cut in cuts]
        take = columns_of(rows_of(plan, rows_ref, "fine_out"), own) - float(own)
        leave = []
        for n, (cut, copy) in enumerate(zip(cuts, held)):
            got = select_rows(take[n * TOK : (n + 1) * TOK], source_ref[...])
            copy.wait()
            out = part_ref[cut, :].astype(F32) + got
            if partial:
                out_ref[cut, :] = out.astype(BF16)
            else:
                lines = TOK // block_cols
                layer, line = divmod(n * lines, block_rows)
                there = (layer, pl.ds(line, lines))
                stage_ref[there] = out.reshape(lines, block_cols, width).astype(BF16)
                leave.append(start(stage_ref.at[there], out_ref.at[there]))
        for copy in leave:
            copy.wait()

    shape = (2, block_rows, block_cols, width)
    outs = shapes([own], width) if partial else [pltpu.HBM(shape, BF16)]
    scratch = [pltpu.VMEM(part.shape, BF16), pltpu.VMEM(shape, BF16)]
    return call(body, outs, [part, source, rows], [HBM, VMEM, VMEM], scratch, 2 * own // TOK, 1 << 30, 4 << 20)[0]


def coarse_output(coarse, got, rows, which, plan, block_rows, block_cols, part=None):
    own, width = coarse.shape
    half = width // 2
    sizes, more = plan.three[which], plan.four[which]
    parts = [] if part is None else [part]

    def padded(parts, sizes, room):
        out = []
        for value, size, space in zip(parts, sizes, room):
            out.append(value)
            if size < space:
                out.append(jnp.zeros((space - size, value.shape[1]), F32))
        return out

    def body(coarse_ref, *refs):
        got_refs, refs = refs[:3], refs[3:]
        part_refs, (rows_ref, out_ref, *fine_outs, _) = refs[: len(parts)], refs[len(parts) :]
        got = [ref[...].astype(F32) for ref in got_refs]
        back = [jnp.concatenate([x[:size], x[size : 2 * size]], axis=1) for x, size in zip(got, sizes)]
        source = stack_rows([coarse_ref[...].astype(F32)] + padded(back, sizes, plan.room_three))
        out = select_rows(columns_of(rows_of(plan, rows_ref, "coarse_out"), own), source.astype(BF16)).astype(BF16)
        for n in range(own // 2):
            out_ref[n // block_cols, n % block_cols] = out[2 * n : 2 * n + 2]
        for part_ref, fine_ref in zip(part_refs, fine_outs):
            fine = stack_rows(padded([x[2 * size :] for x, size in zip(got, sizes)], more, plan.room_four))
            base = part_ref.shape[0] + sum(plan.room_two)
            take = columns_of(rows_of(plan, rows_ref, "fine_out"), part_ref.shape[0]) - float(base)
            out = part_ref[...].astype(F32) + select_rows(take, fine.astype(BF16))
            fine_ref[...] = out.reshape(fine_ref.shape).astype(BF16)

    outs = [jax.ShapeDtypeStruct((block_rows, block_cols, 2, width), BF16)]
    outs += [jax.ShapeDtypeStruct((2, 2 * block_rows, 2 * block_cols, half), BF16) for _ in parts]
    args = [coarse, *got, *parts, rows]
    out, *fine = call(body, outs, args, [VMEM] * len(args), [], 1, 1 << 28, 1 << 20)
    return out.transpose(2, 0, 1, 3), *fine


def on_device(tokens, regions, shifts, fine_qkv, fine_proj, merge_weight, coarse_qkv, coarse_proj):
    _, rows, cols, _ = tokens.shape
    plan = Plan(rows, cols)

    def first(which, sign, sent, *args):
        got = exchange(sent, plan.one[which], sign)
        return lay(got, plan.room_one), before_fine(*args, plan, rows, cols)

    def second(which, sign, sent, *args):
        got = exchange(sent, plan.two[which], sign)
        return lay(got, plan.room_two), before_coarse(*args, plan)

    def third(which, sign, sent, part, source, coarse, table):
        sizes = [2 * n + m for n, m in zip(plan.three[which], plan.four[which])]
        got = exchange(sent, sizes, sign)
        partial = sum(plan.four[which]) > 0
        fine_out = fine_output(part, source, table, plan, rows, cols, partial)
        place = (table, which, plan, rows // 2, cols // 2)
        if partial:
            coarse_out, fine_out = coarse_output(coarse, got, *place, part=fine_out)
        else:
            (coarse_out,) = coarse_output(coarse, got, *place)
        return fine_out, coarse_out

    def branches(stage, pairs):
        return [functools.partial(stage, which, sign) for which, sign in pairs]

    sent, source, table, flags, one, two, three = first_pieces(shifts, tokens, plan)
    got, (ids, x, weights) = choose(
        one, branches(first, plan.one_branches), sent, flags, regions, source, table, [fine_qkv, fine_proj]
    )
    fine, sent = fine_level(flags, x, got, ids, *weights, fine_qkv, table, plan)
    got, (x, part, home, merge_first) = choose(
        two, branches(second, plan.two_branches), sent, flags, fine, table, merge_weight
    )
    coarse, sent = coarse_level(
        flags, home, x, got, ids, merge_first, merge_weight, coarse_qkv, coarse_proj, table, plan
    )
    return choose(three, branches(third, plan.three_branches), sent, part, got, coarse, table)


def solution(mesh):
    return jax.shard_map(
        on_device,
        mesh=mesh,
        in_specs=(P(None, "lat", "lon", None), P(), P(), P(), P(), P(), P(), P()),
        out_specs=(P(None, "lat", "lon", None), P(None, "lat", "lon", None)),
        check_vma=False,
    )
```

```python
import functools

import jax
import jax.numpy as jnp
import numpy as np
from jax import lax
from jax.experimental import pallas as pl
from jax.experimental.pallas import tpu as pltpu
from jax.sharding import PartitionSpec as P

HD = 32
WH = 6
WW = 12
TOK = 2 * WH * WW
EPS = 1e-05
BIG = 1e30
SCALE = float(np.log2(np.e) / np.sqrt(HD))

NT = (((1,), (1,)), ((), ()))
TN = (((0,), (0,)), ((), ()))
F32 = jnp.float32
BF16 = jnp.bfloat16
I32 = jnp.int32

PAIRS = [(WH - 1, t) for t in range(1, WH)] + [(t, WH - 1) for t in range(1, WH - 1)]


def up16(count):
    return -(-count // 16) * 16


def natural(rows, cols):
    return [(l, r, c) for l in range(2) for r in range(rows) for c in range(cols)]


def windowed(rows, cols):
    return [
        (l, wr * WH + r, wc * WW + c)
        for wr in range(rows // WH)
        for wc in range(cols // WW)
        for l in range(2)
        for r in range(WH)
        for c in range(WW)
    ]


def moved(order, d):
    return [(l, r + d, c + 2 * d) for l, r, c in order]


def exchange_places(held, wanted, rows, cols, sign):
    at = {place: n for n, place in enumerate(held)}
    found = []
    for dr, dc in ((sign, 0), (0, sign), (sign, sign)):
        numbers, places = [], []
        for l, r, c in sorted(set(wanted) - set(held)):
            n = at.get((l, r - dr * rows, c - dc * cols))
            if n is not None:
                numbers.append(n)
                places.append((l, r, c))
        found.append((numbers, places))
    return found


def offsets(t0, t1):
    a = t0 if t0 <= 2 else t0 - WH
    big_a = t1 if t1 <= 2 else t1 - WH
    ahead = 1 if 2 * big_a > a or 2 * big_a - a == 0 and a < 0 else -1
    return a, big_a, ahead


def classes_of(needs, slack):
    rounded = [tuple(-(-size // 8) * 8 for size in need) for need in needs]
    heavy = [sum(need[1:3]) * 2 + sum(need[4:]) for need in rounded]
    limits = []
    for size in sorted(set(heavy)):
        if not limits or size > limits[-1][0] * slack:
            limits.append([size, size])
        limits[-1][1] = size
    which = [next(n for n, limit in enumerate(limits) if size <= limit[1]) for size in heavy]
    sizes = [
        [max(need[k] for need, w in zip(rounded, which) if w == n) for k in range(len(needs[0]))]
        for n in range(len(limits))
    ]
    return sizes, which


def rooms(sizes):
    return [up16(max(size[k] for size in sizes)) for k in range(len(sizes[0]))]


class Plan:
    def __init__(self, rows, cols):
        crows, ccols = rows // 2, cols // 2
        block, cblock = natural(rows, cols), natural(crows, ccols)
        cases = []
        for t0, t1 in PAIRS:
            a, big_a, ahead = offsets(t0, t1)
            fine = moved(windowed(rows, cols), a)
            coarse = moved(cblock, big_a)
            quarters = [
                (l, 2 * r + dr, 2 * c + dc)
                for dr, dc in ((0, 0), (1, 0), (0, 1), (1, 1))
                for l, r, c in coarse
            ]
            come = 1 if a > 0 else -1
            one = exchange_places(block, fine, rows, cols, come)
            home = [p for p in block if p not in set(fine)]
            wanted = quarters + (home if come == -ahead and 2 * big_a != a else [])
            two = exchange_places(fine, wanted, rows, cols, ahead)
            back = 1 if big_a < 0 else -1
            three = exchange_places(coarse, cblock, crows, ccols, back)
            got = set(fine).union(*[places for _, places in two])
            four = exchange_places(fine, [p for p in block if p not in got], rows, cols, back)
            cases.append((come, ahead, back, fine, coarse, quarters, one, two, three, four))

        def needs(which):
            return [[len(numbers) for numbers, _ in case[which]] for case in cases]

        self.one, one_class = classes_of(needs(6), 1.15)
        self.two, two_class = classes_of(needs(7), 1.15)
        sizes, three_class = classes_of([three + four for three, four in zip(needs(8), needs(9))], 1.0)
        self.three, self.four = [size[:3] for size in sizes], [size[3:] for size in sizes]
        self.room_one, self.room_two = rooms(self.one), rooms(self.two)
        self.room_three, self.room_four = rooms(self.three), rooms(self.four)

        def branches(which_class, direction):
            pairs = [(n, case[direction]) for n, case in zip(which_class, cases)]
            found = sorted(set(pairs))
            return found, [found.index(pair) for pair in pairs]

        self.one_branches, one_at = branches(one_class, 0)
        self.two_branches, two_at = branches(two_class, 1)
        self.three_branches, three_at = branches(three_class, 2)
        self.flags = dict(
            three_class=three_class,
            one_at=one_at, two_at=two_at, three_at=three_at,
            a=[offsets(*pair)[0] for pair in PAIRS], big_a=[offsets(*pair)[1] for pair in PAIRS],
        )

        found = {}
        for n, (come, ahead, back, fine, coarse, quarters, one, two, three, four) in enumerate(cases):

            def send(exchanged, room):
                return [n for (numbers, _), size in zip(exchanged, room) for n in numbers + [-1] * (size - len(numbers))]

            def source(held, *exchanges):
                places = list(held)
                for exchanged, room in exchanges:
                    for (_, got), size in zip(exchanged, room):
                        places += got + [None] * (size - len(got))
                return {p: n for n, p in enumerate(places) if p is not None}

            first, second = source(block, (one, self.room_one)), source(fine, (two, self.room_two))
            third = source(coarse, (three, self.room_three))
            last = source(fine, (two, self.room_two), (four, self.room_four))
            out = [(l, r, c) for r in range(crows) for c in range(ccols) for l in range(2)]
            rows_of = dict(
                send_one=send(one, self.room_one),
                take_one=[first[p] for p in fine],
                send_two=send(two, self.room_two),
                take_two=[second[p] for p in quarters],
                send_three=send(three, self.room_three),
                send_four=send(four, self.room_four),
                fine_out=[last[p] for p in block],
                coarse_out=[third[p] for p in out],
            )
            for name, row in rows_of.items():
                found.setdefault(name, []).append(row)
        parts, self.at, top = [], {}, 0
        for name, lists in found.items():
            length = -(-max(len(row) for row in lists) // 128)
            part = np.full((len(PAIRS), length * 128), -1, np.float32)
            for n, row in enumerate(lists):
                part[n, : len(row)] = row
            parts.append(part.reshape(len(PAIRS), length, 128))
            self.at[name] = (top, length)
            top += length
        parts.append(np.zeros((len(PAIRS), -top % 8, 128), np.float32))
        self.table = np.concatenate(parts, axis=1)


def case_of(shifts_ref):
    t0, t1 = shifts_ref[0], shifts_ref[1]
    return jnp.where(t0 == WH - 1, t1 - 1, t0 + WH - 2)


def lookup(values, case):
    out = jnp.int32(values[0])
    for n, value in enumerate(values[1:], 1):
        out = jnp.where(case == n, value, out)
    return out


def columns_of(rows, count):
    parts = [jnp.broadcast_to(rows[j : j + 1], (128, 128)).T for j in range(-(-count // 128))]
    return stack_rows(parts)[:count]


def select_rows(index, source):
    lane = lax.broadcasted_iota(I32, (1, 128), 1).astype(F32)
    size = source.shape[0]
    pick = [jnp.where(index == lane + float(at), 1.0, 0.0).astype(BF16) for at in range(0, size, 128)]
    pick = jnp.concatenate(pick, axis=1)[:, :size]
    return jnp.dot(pick, source, preferred_element_type=F32)


def stack_rows(parts):
    return parts[0] if len(parts) == 1 else jnp.concatenate(parts, axis=0)


def layer_norm(values):
    center = jnp.mean(values, axis=-1, keepdims=True)
    values = values - center
    spread = jnp.mean(values * values, axis=-1, keepdims=True)
    return values * lax.rsqrt(spread + EPS)


def attend_windows(qkv_of, id_of, windows, inner, finish):
    lane = lax.broadcasted_iota(I32, (1, 128), 1)
    forbid = jnp.where(lane < 8, BIG, 0.0).astype(BF16)
    groups = inner // 128
    units = [(w, g) for w in range(windows) for g in range(groups)]
    scores, weights, outs = {}, {}, {}

    def score(w, g):
        key_id = id_of(w)
        not_id = (key_id - 1).astype(BF16) * forbid
        q = qkv_of(w, g * 128)
        keys = jnp.concatenate([qkv_of(w, inner + g * 128), key_id], axis=1)
        queries = []
        for h in range(4):
            mine = jnp.where((lane >= h * HD) & (lane < (h + 1) * HD), 1.0, 0.0).astype(BF16)
            queries.append(jnp.concatenate([q * mine, not_id], axis=1))
        scores[w, g] = lax.dot_general(stack_rows(queries), keys, NT, preferred_element_type=F32)

    def soften(w, g):
        s = scores.pop((w, g))
        weights[w, g] = jnp.exp2((s - jnp.max(s, axis=1, keepdims=True)) * SCALE).astype(BF16)

    def gather(w, g):
        v = qkv_of(w, 2 * inner + g * 128)
        values = jnp.concatenate([v, jnp.ones_like(v)], axis=1)
        out = jnp.dot(weights.pop((w, g)), values, preferred_element_type=F32)
        picked, total = out[:TOK, :128], out[:TOK, 128:]
        for h in range(1, 4):
            rows = slice(h * TOK, (h + 1) * TOK)
            picked = jnp.where(lane < h * HD, picked, out[rows, :128])
            total = jnp.where(lane < h * HD, total, out[rows, 128:])
        outs[w, g] = (picked / total).astype(BF16)
        if g == groups - 1:
            finish(w, jnp.concatenate([outs.pop((w, k)) for k in range(groups)], axis=1))

    for n in range(len(units) + 2):
        if n < len(units):
            score(*units[n])
        if 0 <= n - 1 < len(units):
            soften(*units[n - 1])
        if 0 <= n - 2 < len(units):
            gather(*units[n - 2])


ANY = pl.BlockSpec(memory_space=pl.ANY)
HBM = pl.BlockSpec(memory_space=pltpu.HBM)
VMEM = pl.BlockSpec(memory_space=pltpu.VMEM)
SMEM = pl.BlockSpec(memory_space=pltpu.SMEM)


def call(body, outs, args, in_specs, scratch, copies, flops, moved_bytes, vmem=8):
    args = [
        pltpu.with_memory_space_constraint(arg, spec.memory_space) for arg, spec in zip(args, in_specs, strict=True)
    ]
    spaces = [getattr(out, "memory_space", pltpu.SMEM if out.dtype == I32 else pltpu.VMEM) for out in outs]
    out_specs = [pl.BlockSpec(memory_space=space) for space in spaces]
    return pl.pallas_call(
        body,
        out_shape=outs,
        in_specs=in_specs,
        out_specs=out_specs,
        scratch_shapes=list(scratch) + [pltpu.SemaphoreType.DMA((copies,))],
        compiler_params=pltpu.CompilerParams(vmem_limit_bytes=vmem << 20),
        cost_estimate=pl.CostEstimate(flops=flops, bytes_accessed=moved_bytes, transcendentals=0),
    )(*args)


def shapes(sizes, width, space=pltpu.VMEM):
    return [space((n, width), BF16) for n in sizes]


class Copies:
    def __init__(self, sems):
        self.sems, self.used = sems, 0

    def __call__(self, src, dst):
        copy = pltpu.make_async_copy(src, dst, self.sems.at[self.used])
        self.used += 1
        copy.start()
        return copy


def lay(pieces, room):
    pieces = [piece for piece in pieces if piece is not None]
    if not pieces:
        return None
    width = pieces[0].shape[1]

    def body(*refs):
        out_ref = refs[len(pieces)]
        at = 0
        for ref, space in zip(refs, room):
            rows = ref.shape[0]
            out_ref[at : at + rows, :] = ref[...]
            if rows < space:
                out_ref[at + rows : at + space, :] = jnp.zeros((space - rows, width), BF16)
            at += space

    return call(body, shapes([sum(room)], width), pieces, [VMEM] * 3, [], 1, 0, 1 << 18)[0]


def zeros(shape):
    def body(out_ref, _):
        out_ref[...] = jnp.zeros(shape, BF16)

    return call(body, [pltpu.VMEM(shape, BF16)], [], [], [], 1, 0, 1 << 18)[0]


def flat(ref):
    layers, rows, cols, width = ref.shape
    return ref[...].astype(F32).reshape(layers * rows * cols, width).astype(BF16)


def put_pieces(value, refs):
    at = 0
    for ref in refs:
        ref[...] = value[at : at + ref.shape[0]].astype(BF16)
        at += ref.shape[0]


def rows_of(plan, table_ref, name, *lead):
    top, length = plan.at[name]
    return table_ref[(*lead, slice(top, top + length), slice(None))]


def exchange(pieces, sizes, sign):
    if not any(sizes):
        return [None] * 3
    lat, lon = lax.axis_size("lat"), lax.axis_size("lon")
    row, col, both = [piece[:size] for piece, size in zip(pieces, sizes)]
    pairs = [((i + sign) % lat * lon + (j + sign) % lon, i * lon + j) for i in range(lat) for j in range(lon)]
    col = lax.ppermute(col, "lon", [((j + sign) % lon, j) for j in range(lon)])
    both = lax.ppermute(both, ("lat", "lon"), pairs)
    row = lax.ppermute(row, "lat", [((i + sign) % lat, i) for i in range(lat)])
    return [row, col, both]


def choose(index, branches, *args):
    flat_args, tree = jax.tree.flatten(args)
    out_trees = []

    def closed(branch):
        def run(*leaves):
            out, out_tree = jax.tree.flatten(branch(*jax.tree.unflatten(tree, leaves)))
            out_trees.append(out_tree)
            return out

        return jax.make_jaxpr(run)(*flat_args)

    out = lax.cond_p.bind(index, *flat_args, branches=tuple(closed(branch) for branch in branches))
    return jax.tree.unflatten(out_trees[0], out)


FLAGS = ("three_class", "a", "big_a")


def first_pieces(shifts, tokens, plan):
    width = tokens.shape[-1]
    count = tokens.size // width
    kinds = 3

    def body(shifts_hbm, tokens_hbm, table_hbm, *refs):
        outs, refs = refs[:kinds], refs[kinds:]
        source_ref, rows_ref, flags_ref, *at_refs, shifts_ref, tokens_ref, table_ref, sems = refs
        start = Copies(sems)
        shift = start(shifts_hbm, shifts_ref)
        held = start(tokens_hbm, tokens_ref)
        table = start(table_hbm, table_ref)
        shift.wait()
        case = case_of(shifts_ref)
        for ref, name in zip(at_refs, ("one_at", "two_at", "three_at")):
            ref[0] = lookup(plan.flags[name], case)
        for n, name in enumerate(FLAGS):
            flags_ref[n] = lookup(plan.flags[name], case)
        held.wait()
        source_ref[...] = flat(tokens_ref)
        table.wait()
        rows_ref[...] = table_ref[case]
        index = columns_of(rows_of(plan, table_ref, "send_one", case), sum(plan.room_one))
        put_pieces(select_rows(index, source_ref[...]), outs)

    outs = shapes([*plan.room_one, count], width)
    outs += [pltpu.VMEM(plan.table.shape[1:], F32), pltpu.SMEM((8,), I32)]
    outs += [pltpu.SMEM((1,), I32)] * 3
    scratch = [pltpu.SMEM((2,), I32), pltpu.VMEM(tokens.shape, BF16), pltpu.VMEM(plan.table.shape, F32)]
    got = call(body, outs, [shifts, tokens, plan.table], [HBM] * 3, scratch, 3, 1 << 28, 1 << 20)
    sent, (source, rows, flags, one, two, three) = got[:kinds], got[kinds:]
    return sent, source, rows, flags, one[0], two[0], three[0]


def before_fine(flags, regions, tokens, table, weights, plan, rows, cols):
    _, lat, lon = regions.shape
    width = tokens.shape[1]
    flat_regions = regions.reshape(2 * lat, lon)
    fine, coarse = windowed(rows, cols), natural(rows // 2, cols // 2)

    def lanes(places, scale, is_fine):
        places = np.asarray([(l, scale * r, scale * c, is_fine) for l, r, c in places], np.float32)
        return np.pad(places, ((0, -len(places) % 128), (0, 0))).T.reshape(4, -1, 128)

    places = np.concatenate([lanes(fine, 1, 1), lanes(coarse, 2, 0)], axis=1)
    lines = places.shape[1]

    def body(flags_ref, rows_ref, tokens_ref, regions_hbm, places_hbm, *refs):
        weights_hbm, refs = refs[: len(weights)], refs[len(weights) :]
        id_ref, x_ref, *refs = refs
        weight_refs, (regions_ref, places_ref, sems) = refs[: len(weights)], refs[len(weights) :]
        start = Copies(sems)
        waits = [start(regions_hbm, regions_ref), start(places_hbm, places_ref)]
        later = [
            start(src.at[:, pl.ds(0, dst.shape[1])], dst) for src, dst in zip(weights_hbm, weight_refs)
        ]
        for copy in waits:
            copy.wait()
        a = flags_ref[1].astype(F32)
        big_a = 2.0 * flags_ref[2].astype(F32)
        is_fine = places_ref[3]
        d = is_fine * a + (1.0 - is_fine) * big_a
        row = places_ref[1] + d + (lax.axis_index("lat") * rows).astype(F32)
        col = places_ref[2] + 2.0 * d + (lax.axis_index("lon") * cols).astype(F32)
        wrapped = jnp.where((row < 0) | (row >= lat), 4.0, 0.0)
        row = jnp.where(row < 0, row + lat, jnp.where(row >= lat, row - lat, row))
        col = jnp.where(col < 0, col + lon, jnp.where(col >= lon, col - lon, col))
        row = row + places_ref[0] * lat

        def along(values):
            return jnp.concatenate([values[n : n + 1] for n in range(lines)], axis=1)

        line = lax.broadcasted_iota(I32, (2 * lat, 1), 0).astype(F32)
        pick = jnp.where(line == along(row), 1.0, 0.0).astype(BF16)
        known = regions_ref[...].astype(F32).astype(BF16)
        picked = lax.dot_general(known, pick, TN, preferred_element_type=F32)
        line = lax.broadcasted_iota(I32, (lon, 1), 0).astype(F32)
        ids = jnp.sum(jnp.where(line == along(col), picked, 0.0), axis=0, keepdims=True) + along(wrapped)
        for n in range(lines):
            id_ref[n : n + 1, :] = ids[:, n * 128 : (n + 1) * 128]
        take = columns_of(rows_of(plan, rows_ref, "take_one"), len(fine))
        x_ref[...] = select_rows(take, tokens_ref[...]).astype(BF16)
        for copy in later:
            copy.wait()

    outs = [pltpu.VMEM((lines, 128), F32)] + shapes([len(fine)], width)
    outs += [pltpu.VMEM((w.shape[0], min(w.shape[1], 2 * weights[1].shape[0])), BF16) for w in weights]
    scratch = [pltpu.VMEM(flat_regions.shape, I32), pltpu.VMEM(places.shape, F32)]
    args = [flags, table, tokens, flat_regions, places, *weights]
    in_specs = [SMEM, VMEM, VMEM] + [HBM] * (2 + len(weights))
    ids, x, *weights = call(body, outs, args, in_specs, scratch, 2 + len(weights), 1 << 28, 4 << 20)
    return ids, x, weights


def id_columns(lines, count):
    lane = lax.broadcasted_iota(I32, (1, 128), 1).astype(F32)
    return jnp.where(columns_of(lines, count) == lane, 1.0, 0.0).astype(BF16)


def before_coarse(flags, fine, table, weight, plan):
    own, width = fine.shape
    half = 9 * weight.shape[0] // 32

    def body(flags_ref, rows_ref, fine_ref, weight_hbm, x_ref, part_hbm, home_ref, weight_ref, part_ref, sems):
        start = Copies(sems)
        later = start(weight_hbm.at[pl.ds(0, half)], weight_ref)
        take = columns_of(rows_of(plan, rows_ref, "fine_out"), own)
        part_ref[...] = select_rows(take, fine_ref[...]).astype(BF16)
        leave = start(part_ref, part_hbm)
        take = columns_of(rows_of(plan, rows_ref, "take_two"), own)
        x_ref[...] = select_rows(take, fine_ref[...]).astype(BF16)

        @pl.when(needs_fine(flags_ref, plan))
        def _():
            index = columns_of(rows_of(plan, rows_ref, "send_four"), sum(plan.room_four))
            home_ref[...] = select_rows(index, fine_ref[...]).astype(BF16)

        leave.wait()
        later.wait()

    outs = shapes([own], width) + shapes([own], width, pltpu.HBM)
    outs += shapes([sum(plan.room_four)], width) + shapes([half], weight.shape[1])
    scratch = [pltpu.VMEM(fine.shape, BF16)]
    args = [flags, table, fine, weight]
    return call(body, outs, args, [SMEM, VMEM, VMEM, HBM], scratch, 2, 1 << 28, 4 << 20)


def needs_fine(flags_ref, plan):
    with_fine = [n for n, sizes in enumerate(plan.four) if sum(sizes)]
    return functools.reduce(jnp.logical_or, [flags_ref[0] == n for n in with_fine])


def fine_level(x_own, source, ids, w_qk, w_proj, w_qkv, rows, plan):
    count, width = x_own.shape
    inner = w_proj.shape[0]

    def body(own_ref, source_ref, ids_ref, qk_w_ref, proj_w_ref, qkv_w_hbm, rows_ref, out_ref, *refs):
        *piece_outs, x_ref, qkv_ref, id_ref, v_w_ref, sems = refs
        v_w = Copies(sems)(qkv_w_hbm.at[:, pl.ds(2 * inner, inner)], v_w_ref)
        id_ref[...] = id_columns(ids_ref[: -(-count // 128), :], count)
        take = columns_of(rows_of(plan, rows_ref, "take_one"), count) - float(count)
        x = own_ref[...].astype(F32) + select_rows(take, source_ref[...])
        x_ref[...] = x
        normed = layer_norm(x).astype(BF16)
        v_w.wait()
        qkv_ref[:, : 2 * inner] = jnp.dot(normed, qk_w_ref[...], preferred_element_type=F32).astype(BF16)
        qkv_ref[:, 2 * inner :] = jnp.dot(normed, v_w_ref[...], preferred_element_type=F32).astype(BF16)

        def finish(w, out):
            at = slice(w * TOK, (w + 1) * TOK)
            out = jnp.dot(out, proj_w_ref[...], preferred_element_type=F32)
            out_ref[at, :] = (x_ref[at, :] + out).astype(BF16)

        attend_windows(
            lambda w, at: qkv_ref[w * TOK : (w + 1) * TOK, at : at + 128],
            lambda w: id_ref[w * TOK : (w + 1) * TOK, :],
            count // TOK,
            inner,
            finish,
        )
        index = columns_of(rows_of(plan, rows_ref, "send_two"), sum(plan.room_two))
        put_pieces(select_rows(index, out_ref[...]), piece_outs)

    outs = shapes([count, *plan.room_two], width)
    scratch = [
        pltpu.VMEM((count, width), F32),
        pltpu.VMEM((count, 3 * inner), BF16),
        pltpu.VMEM((count, 128), BF16),
        pltpu.VMEM((width, inner), BF16),
    ]
    args = [x_own, source, ids, w_qk, w_proj, w_qkv, rows]
    out, *sent = call(body, outs, args, [VMEM] * 5 + [HBM, VMEM], scratch, 1, 3 << 30, 6 << 20, 14)
    return out, sent


def coarse_level(flags, home, x_own, source, ids, merge_first, w_merge, w_qkv, w_proj, rows, plan):
    depth, width = w_merge.shape
    own, half = x_own.shape
    count = own // 4
    inner = w_proj.shape[0]

    def body(
        flags_ref, merge_hbm, qkv_w_hbm, proj_w_hbm, home_ref, own_ref, source_ref, ids_ref, first_ref, rows_ref, *refs
    ):
        out_ref, *piece_outs = refs[:4]
        qkv_ref, id_ref, merge_ref, qkv_w_ref, proj_w_ref, sems = refs[4:]
        start = Copies(sems)
        here = first_ref.shape[0]
        merge_w = start(merge_hbm.at[pl.ds(here, depth - here)], merge_ref)
        qkv_w = start(qkv_w_hbm, qkv_w_ref)
        proj_w = start(proj_w_hbm, proj_w_ref)
        id_ref[...] = id_columns(ids_ref[-(-own // 128) :, :], count)
        take = columns_of(rows_of(plan, rows_ref, "take_two"), 4 * count) - float(own)
        x = own_ref[...].astype(F32) + select_rows(take, source_ref[...])
        x = jnp.concatenate([x[n * count : (n + 1) * count] for n in range(4)], axis=1)
        stacked = layer_norm(x).astype(BF16)
        merge_w.wait()
        merged = jnp.dot(stacked[:, :here], first_ref[...], preferred_element_type=F32)
        merged = merged + jnp.dot(stacked[:, here:], merge_ref[...], preferred_element_type=F32)
        merged = merged.astype(BF16).astype(F32)
        normed = layer_norm(merged).astype(BF16)
        qkv_w.wait()
        proj_w.wait()
        qkv_ref[...] = jnp.dot(normed, qkv_w_ref[...], preferred_element_type=F32).astype(BF16)

        def finish(w, out):
            out = jnp.dot(out, proj_w_ref[...], preferred_element_type=F32)
            out_ref[...] = (merged + out).astype(BF16)

        attend_windows(lambda w, at: qkv_ref[:, at : at + 128], lambda w: id_ref[...], 1, inner, finish)
        sent = select_rows(columns_of(rows_of(plan, rows_ref, "send_three"), sum(plan.room_three)), out_ref[...])
        sent = sent.astype(BF16)
        for n, sizes in enumerate(plan.three):

            @pl.when(flags_ref[0] == n)
            def _():
                at = 0
                for ref, size, space in zip(piece_outs, sizes, plan.room_three):
                    ref[:size, :] = sent[at : at + size, :half]
                    ref[size : 2 * size, :] = sent[at : at + size, half:]
                    at += space

        for n, fine_sizes in enumerate(plan.four):
            if sum(fine_sizes):

                @pl.when(flags_ref[0] == n)
                def _():
                    at = 0
                    for ref, size, more, space in zip(piece_outs, plan.three[n], fine_sizes, plan.room_four):
                        ref[2 * size : 2 * size + more, :] = home_ref[at : at + more, :]
                        at += space

    most = [max(2 * three[k] + four[k] for three, four in zip(plan.three, plan.four)) for k in range(3)]
    outs = shapes([count], width) + shapes(most, half)
    scratch = [pltpu.VMEM((count, 3 * inner), BF16)]
    shapes_in = [(count, 128), (depth - merge_first.shape[0], width), w_qkv.shape, w_proj.shape]
    scratch += [pltpu.VMEM(shape, BF16) for shape in shapes_in]
    args = [flags, w_merge, w_qkv, w_proj, home, x_own, source, ids, merge_first, rows]
    in_specs = [SMEM] + [HBM] * 3 + [VMEM] * (len(args) - 4)
    out, *sent = call(body, outs, args, in_specs, scratch, 3, 3 << 30, 12 << 20, 24)
    return out, sent


def fine_output(part, source, rows, plan, block_rows, block_cols, partial):
    own, width = part.shape

    def body(part_hbm, source_ref, rows_ref, out_ref, part_ref, stage_ref, sems):
        start = Copies(sems)
        cuts = [pl.ds(at, TOK) for at in range(0, own, TOK)]
        held = [start(part_hbm.at[cut], part_ref.at[cut]) for cut in cuts]
        take = columns_of(rows_of(plan, rows_ref, "fine_out"), own) - float(own)
        leave = []
        for n, (cut, copy) in enumerate(zip(cuts, held)):
            got = select_rows(take[n * TOK : (n + 1) * TOK], source_ref[...])
            copy.wait()
            out = part_ref[cut, :].astype(F32) + got
            if partial:
                out_ref[cut, :] = out.astype(BF16)
            else:
                lines = TOK // block_cols
                layer, line = divmod(n * lines, block_rows)
                there = (layer, pl.ds(line, lines))
                stage_ref[there] = out.reshape(lines, block_cols, width).astype(BF16)
                leave.append(start(stage_ref.at[there], out_ref.at[there]))
        for copy in leave:
            copy.wait()

    shape = (2, block_rows, block_cols, width)
    outs = shapes([own], width) if partial else [pltpu.HBM(shape, BF16)]
    scratch = [pltpu.VMEM(part.shape, BF16), pltpu.VMEM(shape, BF16)]
    return call(body, outs, [part, source, rows], [HBM, VMEM, VMEM], scratch, 2 * own // TOK, 1 << 30, 4 << 20)[0]


def coarse_output(coarse, got, rows, which, plan, block_rows, block_cols, part=None):
    own, width = coarse.shape
    half = width // 2
    sizes, more = plan.three[which], plan.four[which]
    parts = [] if part is None else [part]

    def padded(parts, sizes, room):
        out = []
        for value, size, space in zip(parts, sizes, room):
            out.append(value)
            if size < space:
                out.append(jnp.zeros((space - size, value.shape[1]), F32))
        return out

    def body(coarse_ref, *refs):
        got_refs, refs = refs[:3], refs[3:]
        part_refs, (rows_ref, out_ref, *fine_outs, _) = refs[: len(parts)], refs[len(parts) :]
        got = [ref[...].astype(F32) for ref in got_refs]
        back = [jnp.concatenate([x[:size], x[size : 2 * size]], axis=1) for x, size in zip(got, sizes)]
        source = stack_rows([coarse_ref[...].astype(F32)] + padded(back, sizes, plan.room_three))
        out = select_rows(columns_of(rows_of(plan, rows_ref, "coarse_out"), own), source.astype(BF16)).astype(BF16)
        for n in range(own // 2):
            out_ref[n // block_cols, n % block_cols] = out[2 * n : 2 * n + 2]
        for part_ref, fine_ref in zip(part_refs, fine_outs):
            fine = stack_rows(padded([x[2 * size :] for x, size in zip(got, sizes)], more, plan.room_four))
            base = part_ref.shape[0] + sum(plan.room_two)
            take = columns_of(rows_of(plan, rows_ref, "fine_out"), part_ref.shape[0]) - float(base)
            out = part_ref[...].astype(F32) + select_rows(take, fine.astype(BF16))
            fine_ref[...] = out.reshape(fine_ref.shape).astype(BF16)

    outs = [jax.ShapeDtypeStruct((block_rows, block_cols, 2, width), BF16)]
    outs += [jax.ShapeDtypeStruct((2, 2 * block_rows, 2 * block_cols, half), BF16) for _ in parts]
    args = [coarse, *got, *parts, rows]
    out, *fine = call(body, outs, args, [VMEM] * len(args), [], 1, 1 << 28, 1 << 20)
    return out.transpose(2, 0, 1, 3), *fine


def on_device(tokens, regions, shifts, fine_qkv, fine_proj, merge_weight, coarse_qkv, coarse_proj):
    _, rows, cols, _ = tokens.shape
    plan = Plan(rows, cols)

    def first(which, sign, sent, *args):
        got = exchange(sent, plan.one[which], sign)
        return lay(got, plan.room_one), before_fine(*args, plan, rows, cols)

    def second(which, sign, sent, *args):
        got = lay(exchange(sent, plan.two[which], sign), plan.room_two)
        if got is None:
            got = zeros((sum(plan.room_two), sent[0].shape[1]))
        return got, before_coarse(*args, plan)

    def third(which, sign, sent, part, source, coarse, table):
        sizes = [2 * n + m for n, m in zip(plan.three[which], plan.four[which])]
        got = exchange(sent, sizes, sign)
        partial = sum(plan.four[which]) > 0
        fine_out = fine_output(part, source, table, plan, rows, cols, partial)
        place = (table, which, plan, rows // 2, cols // 2)
        if partial:
            coarse_out, fine_out = coarse_output(coarse, got, *place, part=fine_out)
        else:
            (coarse_out,) = coarse_output(coarse, got, *place)
        return fine_out, coarse_out

    def branches(stage, pairs):
        return [functools.partial(stage, which, sign) for which, sign in pairs]

    sent, source, table, flags, one, two, three = first_pieces(shifts, tokens, plan)
    got, (ids, x, weights) = choose(
        one, branches(first, plan.one_branches), sent, flags, regions, source, table, [fine_qkv, fine_proj]
    )
    fine, sent = fine_level(x, got, ids, *weights, fine_qkv, table, plan)
    got, (x, part, home, merge_first) = choose(
        two, branches(second, plan.two_branches), sent, flags, fine, table, merge_weight
    )
    coarse, sent = coarse_level(
        flags, home, x, got, ids, merge_first, merge_weight, coarse_qkv, coarse_proj, table, plan
    )
    return choose(three, branches(third, plan.three_branches), sent, part, got, coarse, table)


def solution(mesh):
    return jax.shard_map(
        on_device,
        mesh=mesh,
        in_specs=(P(None, "lat", "lon", None), P(), P(), P(), P(), P(), P(), P()),
        out_specs=(P(None, "lat", "lon", None), P(None, "lat", "lon", None)),
        check_vma=False,
    )
```

```python
import functools

import jax
import jax.numpy as jnp
import numpy as np
from jax import lax
from jax.experimental import pallas as pl
from jax.experimental.pallas import tpu as pltpu
from jax.sharding import PartitionSpec as P

HD = 32
WH = 6
WW = 12
TOK = 2 * WH * WW
EPS = 1e-05
BIG = 1e30
SCALE = float(np.log2(np.e) / np.sqrt(HD))

NT = (((1,), (1,)), ((), ()))
TN = (((0,), (0,)), ((), ()))
F32 = jnp.float32
BF16 = jnp.bfloat16
I32 = jnp.int32

PAIRS = [(WH - 1, t) for t in range(1, WH)] + [(t, WH - 1) for t in range(1, WH - 1)]


def up16(count):
    return -(-count // 16) * 16


def natural(rows, cols):
    return [(l, r, c) for l in range(2) for r in range(rows) for c in range(cols)]


def windowed(rows, cols):
    return [
        (l, wr * WH + r, wc * WW + c)
        for wr in range(rows // WH)
        for wc in range(cols // WW)
        for l in range(2)
        for r in range(WH)
        for c in range(WW)
    ]


def moved(order, d):
    return [(l, r + d, c + 2 * d) for l, r, c in order]


def exchange_places(held, wanted, rows, cols, sign):
    at = {place: n for n, place in enumerate(held)}
    found = []
    for dr, dc in ((sign, 0), (0, sign), (sign, sign)):
        numbers, places = [], []
        for l, r, c in sorted(set(wanted) - set(held)):
            n = at.get((l, r - dr * rows, c - dc * cols))
            if n is not None:
                numbers.append(n)
                places.append((l, r, c))
        found.append((numbers, places))
    return found


def offsets(t0, t1):
    a = t0 if t0 <= 2 else t0 - WH
    big_a = t1 if t1 <= 2 else t1 - WH
    ahead = 1 if 2 * big_a > a or 2 * big_a - a == 0 and a < 0 else -1
    return a, big_a, ahead


def classes_of(needs, slack):
    rounded = [tuple(-(-size // 8) * 8 for size in need) for need in needs]
    heavy = [sum(need[1:3]) * 2 + sum(need[4:]) for need in rounded]
    limits = []
    for size in sorted(set(heavy)):
        if not limits or size > limits[-1][0] * slack:
            limits.append([size, size])
        limits[-1][1] = size
    which = [next(n for n, limit in enumerate(limits) if size <= limit[1]) for size in heavy]
    sizes = [
        [max(need[k] for need, w in zip(rounded, which) if w == n) for k in range(len(needs[0]))]
        for n in range(len(limits))
    ]
    return sizes, which


def rooms(sizes):
    return [up16(max(size[k] for size in sizes)) for k in range(len(sizes[0]))]


class Plan:
    def __init__(self, rows, cols):
        crows, ccols = rows // 2, cols // 2
        block, cblock = natural(rows, cols), natural(crows, ccols)
        cases = []
        for t0, t1 in PAIRS:
            a, big_a, ahead = offsets(t0, t1)
            fine = moved(windowed(rows, cols), a)
            coarse = moved(cblock, big_a)
            quarters = [
                (l, 2 * r + dr, 2 * c + dc)
                for dr, dc in ((0, 0), (1, 0), (0, 1), (1, 1))
                for l, r, c in coarse
            ]
            come = 1 if a > 0 else -1
            one = exchange_places(block, fine, rows, cols, come)
            home = [p for p in block if p not in set(fine)]
            wanted = quarters + (home if come == -ahead and 2 * big_a != a else [])
            two = exchange_places(fine, wanted, rows, cols, ahead)
            back = 1 if big_a < 0 else -1
            three = exchange_places(coarse, cblock, crows, ccols, back)
            got = set(fine).union(*[places for _, places in two])
            four = exchange_places(fine, [p for p in block if p not in got], rows, cols, back)
            cases.append((come, ahead, back, fine, coarse, quarters, one, two, three, four))

        def needs(which):
            return [[len(numbers) for numbers, _ in case[which]] for case in cases]

        self.one, one_class = classes_of(needs(6), 1.15)
        self.two, two_class = classes_of(needs(7), 1.15)
        sizes, three_class = classes_of([three + four for three, four in zip(needs(8), needs(9))], 1.0)
        self.three, self.four = [size[:3] for size in sizes], [size[3:] for size in sizes]
        self.room_one, self.room_two = rooms(self.one), rooms(self.two)
        self.room_three, self.room_four = rooms(self.three), rooms(self.four)

        def branches(which_class, direction):
            pairs = [(n, case[direction]) for n, case in zip(which_class, cases)]
            found = sorted(set(pairs))
            return found, [found.index(pair) for pair in pairs]

        self.one_branches, one_at = branches(one_class, 0)
        self.two_branches, two_at = branches(two_class, 1)
        self.three_branches, three_at = branches(three_class, 2)
        self.flags = dict(
            three_class=three_class,
            one_at=one_at, two_at=two_at, three_at=three_at,
            a=[offsets(*pair)[0] for pair in PAIRS], big_a=[offsets(*pair)[1] for pair in PAIRS],
        )

        found = {}
        for n, (come, ahead, back, fine, coarse, quarters, one, two, three, four) in enumerate(cases):

            def send(exchanged, room):
                return [n for (numbers, _), size in zip(exchanged, room) for n in numbers + [-1] * (size - len(numbers))]

            def source(held, *exchanges):
                places = list(held)
                for exchanged, room in exchanges:
                    for (_, got), size in zip(exchanged, room):
                        places += got + [None] * (size - len(got))
                return {p: n for n, p in enumerate(places) if p is not None}

            first, second = source(block, (one, self.room_one)), source(fine, (two, self.room_two))
            third = source(coarse, (three, self.room_three))
            last = source(fine, (two, self.room_two), (four, self.room_four))
            out = [(l, r, c) for r in range(crows) for c in range(ccols) for l in range(2)]
            rows_of = dict(
                send_one=send(one, self.room_one),
                take_one=[first[p] for p in fine],
                send_two=send(two, self.room_two),
                take_two=[second[p] for p in quarters],
                send_three=send(three, self.room_three),
                send_four=send(four, self.room_four),
                fine_out=[last[p] for p in block],
                coarse_out=[third[p] for p in out],
            )
            for name, row in rows_of.items():
                found.setdefault(name, []).append(row)
        parts, self.at, top = [], {}, 0
        for name, lists in found.items():
            length = -(-max(len(row) for row in lists) // 128)
            part = np.full((len(PAIRS), length * 128), -1, np.float32)
            for n, row in enumerate(lists):
                part[n, : len(row)] = row
            parts.append(part.reshape(len(PAIRS), length, 128))
            self.at[name] = (top, length)
            top += length
        parts.append(np.zeros((len(PAIRS), -top % 8, 128), np.float32))
        self.table = np.concatenate(parts, axis=1)


def case_of(shifts_ref):
    t0, t1 = shifts_ref[0], shifts_ref[1]
    return jnp.where(t0 == WH - 1, t1 - 1, t0 + WH - 2)


def lookup(values, case):
    out = jnp.int32(values[0])
    for n, value in enumerate(values[1:], 1):
        out = jnp.where(case == n, value, out)
    return out


def columns_of(rows, count):
    parts = [jnp.broadcast_to(rows[j : j + 1], (128, 128)).T for j in range(-(-count // 128))]
    return stack_rows(parts)[:count]


def select_rows(index, source):
    lane = lax.broadcasted_iota(I32, (1, 128), 1).astype(F32)
    size = source.shape[0]
    pick = [jnp.where(index == lane + float(at), 1.0, 0.0).astype(BF16) for at in range(0, size, 128)]
    pick = jnp.concatenate(pick, axis=1)[:, :size]
    return jnp.dot(pick, source, preferred_element_type=F32)


def stack_rows(parts):
    return parts[0] if len(parts) == 1 else jnp.concatenate(parts, axis=0)


def layer_norm(values):
    center = jnp.mean(values, axis=-1, keepdims=True)
    values = values - center
    spread = jnp.mean(values * values, axis=-1, keepdims=True)
    return values * lax.rsqrt(spread + EPS)


def attend_windows(qkv_of, id_of, windows, inner, finish):
    lane = lax.broadcasted_iota(I32, (1, 128), 1)
    forbid = jnp.where(lane < 8, BIG, 0.0).astype(BF16)
    groups = inner // 128
    units = [(w, g) for w in range(windows) for g in range(groups)]
    scores, weights, outs = {}, {}, {}

    def score(w, g):
        key_id = id_of(w)
        not_id = (key_id - 1).astype(BF16) * forbid
        q = qkv_of(w, g * 128)
        keys = jnp.concatenate([qkv_of(w, inner + g * 128), key_id], axis=1)
        queries = []
        for h in range(4):
            mine = jnp.where((lane >= h * HD) & (lane < (h + 1) * HD), 1.0, 0.0).astype(BF16)
            queries.append(jnp.concatenate([q * mine, not_id], axis=1))
        scores[w, g] = lax.dot_general(stack_rows(queries), keys, NT, preferred_element_type=F32)

    def soften(w, g):
        s = scores.pop((w, g))
        weights[w, g] = jnp.exp2((s - jnp.max(s, axis=1, keepdims=True)) * SCALE).astype(BF16)

    def gather(w, g):
        v = qkv_of(w, 2 * inner + g * 128)
        values = jnp.concatenate([v, jnp.ones_like(v)], axis=1)
        out = jnp.dot(weights.pop((w, g)), values, preferred_element_type=F32)
        picked, total = out[:TOK, :128], out[:TOK, 128:]
        for h in range(1, 4):
            rows = slice(h * TOK, (h + 1) * TOK)
            picked = jnp.where(lane < h * HD, picked, out[rows, :128])
            total = jnp.where(lane < h * HD, total, out[rows, 128:])
        outs[w, g] = (picked / total).astype(BF16)
        if g == groups - 1:
            finish(w, jnp.concatenate([outs.pop((w, k)) for k in range(groups)], axis=1))

    for n in range(len(units) + 2):
        if n < len(units):
            score(*units[n])
        if 0 <= n - 1 < len(units):
            soften(*units[n - 1])
        if 0 <= n - 2 < len(units):
            gather(*units[n - 2])


ANY = pl.BlockSpec(memory_space=pl.ANY)
HBM = pl.BlockSpec(memory_space=pltpu.HBM)
VMEM = pl.BlockSpec(memory_space=pltpu.VMEM)
SMEM = pl.BlockSpec(memory_space=pltpu.SMEM)


def call(body, outs, args, in_specs, scratch, copies, flops, moved_bytes, vmem=8):
    args = [
        pltpu.with_memory_space_constraint(arg, spec.memory_space) for arg, spec in zip(args, in_specs, strict=True)
    ]
    spaces = [getattr(out, "memory_space", pltpu.SMEM if out.dtype == I32 else pltpu.VMEM) for out in outs]
    out_specs = [pl.BlockSpec(memory_space=space) for space in spaces]
    return pl.pallas_call(
        body,
        out_shape=outs,
        in_specs=in_specs,
        out_specs=out_specs,
        scratch_shapes=list(scratch) + [pltpu.SemaphoreType.DMA((copies,))],
        compiler_params=pltpu.CompilerParams(vmem_limit_bytes=vmem << 20),
        cost_estimate=pl.CostEstimate(flops=flops, bytes_accessed=moved_bytes, transcendentals=0),
    )(*args)


def shapes(sizes, width, space=pltpu.VMEM):
    return [space((n, width), BF16) for n in sizes]


class Copies:
    def __init__(self, sems):
        self.sems, self.used = sems, 0

    def __call__(self, src, dst):
        copy = pltpu.make_async_copy(src, dst, self.sems.at[self.used])
        self.used += 1
        copy.start()
        return copy


def lay(pieces, room):
    pieces = [piece for piece in pieces if piece is not None]
    if not pieces:
        return None
    width = pieces[0].shape[1]

    def body(*refs):
        out_ref = refs[len(pieces)]
        at = 0
        for ref, space in zip(refs, room):
            rows = ref.shape[0]
            out_ref[at : at + rows, :] = ref[...]
            if rows < space:
                out_ref[at + rows : at + space, :] = jnp.zeros((space - rows, width), BF16)
            at += space

    return call(body, shapes([sum(room)], width), pieces, [VMEM] * 3, [], 1, 0, 1 << 18)[0]


def zeros(shape):
    def body(out_ref, _):
        out_ref[...] = jnp.zeros(shape, BF16)

    return call(body, [pltpu.VMEM(shape, BF16)], [], [], [], 1, 0, 1 << 18)[0]


def flat(ref):
    layers, rows, cols, width = ref.shape
    return ref[...].astype(F32).reshape(layers * rows * cols, width).astype(BF16)


def put_pieces(value, refs):
    at = 0
    for ref in refs:
        ref[...] = value[at : at + ref.shape[0]].astype(BF16)
        at += ref.shape[0]


def rows_of(plan, table_ref, name, *lead):
    top, length = plan.at[name]
    return table_ref[(*lead, slice(top, top + length), slice(None))]


def exchange(pieces, sizes, sign):
    if not any(sizes):
        return [None] * 3
    lat, lon = lax.axis_size("lat"), lax.axis_size("lon")
    row, col, both = [piece[:size] for piece, size in zip(pieces, sizes)]
    pairs = [((i + sign) % lat * lon + (j + sign) % lon, i * lon + j) for i in range(lat) for j in range(lon)]
    col = lax.ppermute(col, "lon", [((j + sign) % lon, j) for j in range(lon)])
    both = lax.ppermute(both, ("lat", "lon"), pairs)
    row = lax.ppermute(row, "lat", [((i + sign) % lat, i) for i in range(lat)])
    return [row, col, both]


def choose(index, branches, *args):
    flat_args, tree = jax.tree.flatten(args)
    out_trees = []

    def closed(branch):
        def run(*leaves):
            out, out_tree = jax.tree.flatten(branch(*jax.tree.unflatten(tree, leaves)))
            out_trees.append(out_tree)
            return out

        return jax.make_jaxpr(run)(*flat_args)

    out = lax.cond_p.bind(index, *flat_args, branches=tuple(closed(branch) for branch in branches))
    return jax.tree.unflatten(out_trees[0], out)


FLAGS = ("three_class", "a", "big_a")


def first_pieces(shifts, tokens, plan):
    width = tokens.shape[-1]
    count = tokens.size // width
    kinds = 3

    def body(shifts_hbm, tokens_hbm, table_hbm, *refs):
        outs, refs = refs[:kinds], refs[kinds:]
        rows_ref, flags_ref, *at_refs, shifts_ref, tokens_ref, table_ref, source_ref, sems = refs
        start = Copies(sems)
        shift = start(shifts_hbm, shifts_ref)
        held = start(tokens_hbm, tokens_ref)
        table = start(table_hbm, table_ref)
        shift.wait()
        case = case_of(shifts_ref)
        for ref, name in zip(at_refs, ("one_at", "two_at", "three_at")):
            ref[0] = lookup(plan.flags[name], case)
        for n, name in enumerate(FLAGS):
            flags_ref[n] = lookup(plan.flags[name], case)
        held.wait()
        source_ref[...] = flat(tokens_ref)
        table.wait()
        rows_ref[...] = table_ref[case]
        index = columns_of(rows_of(plan, table_ref, "send_one", case), sum(plan.room_one))
        put_pieces(select_rows(index, source_ref[...]), outs)

    outs = shapes(plan.room_one, width)
    outs += [pltpu.VMEM(plan.table.shape[1:], F32), pltpu.SMEM((8,), I32)]
    outs += [pltpu.SMEM((1,), I32)] * 3
    scratch = [pltpu.SMEM((2,), I32), pltpu.VMEM(tokens.shape, BF16), pltpu.VMEM(plan.table.shape, F32)]
    scratch += [pltpu.VMEM((count, width), BF16)]
    got = call(body, outs, [shifts, tokens, plan.table], [HBM] * 3, scratch, 3, 1 << 28, 1 << 20)
    sent, (rows, flags, one, two, three) = got[:kinds], got[kinds:]
    return sent, rows, flags, one[0], two[0], three[0]


def before_fine(flags, regions, tokens, table, weights, plan):
    _, lat, lon = regions.shape
    _, rows, cols, width = tokens.shape
    flat_regions = regions.reshape(2 * lat, lon)
    fine, coarse = windowed(rows, cols), natural(rows // 2, cols // 2)

    def lanes(places, scale, is_fine):
        places = np.asarray([(l, scale * r, scale * c, is_fine) for l, r, c in places], np.float32)
        return np.pad(places, ((0, -len(places) % 128), (0, 0))).T.reshape(4, -1, 128)

    places = np.concatenate([lanes(fine, 1, 1), lanes(coarse, 2, 0)], axis=1)
    lines = places.shape[1]

    def body(flags_ref, rows_ref, tokens_hbm, regions_hbm, places_hbm, *refs):
        weights_hbm, refs = refs[: len(weights)], refs[len(weights) :]
        id_ref, x_ref, *refs = refs
        weight_refs, (regions_ref, places_ref, tokens_ref, sems) = refs[: len(weights)], refs[len(weights) :]
        start = Copies(sems)
        waits = [start(regions_hbm, regions_ref), start(places_hbm, places_ref)]
        held = start(tokens_hbm, tokens_ref)
        later = [start(src, dst) for src, dst in zip(weights_hbm, weight_refs)]
        for copy in waits:
            copy.wait()
        a = flags_ref[1].astype(F32)
        big_a = 2.0 * flags_ref[2].astype(F32)
        is_fine = places_ref[3]
        d = is_fine * a + (1.0 - is_fine) * big_a
        row = places_ref[1] + d + (lax.axis_index("lat") * rows).astype(F32)
        col = places_ref[2] + 2.0 * d + (lax.axis_index("lon") * cols).astype(F32)
        wrapped = jnp.where((row < 0) | (row >= lat), 4.0, 0.0)
        row = jnp.where(row < 0, row + lat, jnp.where(row >= lat, row - lat, row))
        col = jnp.where(col < 0, col + lon, jnp.where(col >= lon, col - lon, col))
        row = row + places_ref[0] * lat

        def along(values):
            return jnp.concatenate([values[n : n + 1] for n in range(lines)], axis=1)

        line = lax.broadcasted_iota(I32, (2 * lat, 1), 0).astype(F32)
        pick = jnp.where(line == along(row), 1.0, 0.0).astype(BF16)
        known = regions_ref[...].astype(F32).astype(BF16)
        picked = lax.dot_general(known, pick, TN, preferred_element_type=F32)
        line = lax.broadcasted_iota(I32, (lon, 1), 0).astype(F32)
        ids = jnp.sum(jnp.where(line == along(col), picked, 0.0), axis=0, keepdims=True) + along(wrapped)
        for n in range(lines):
            id_ref[n : n + 1, :] = ids[:, n * 128 : (n + 1) * 128]
        take = columns_of(rows_of(plan, rows_ref, "take_one"), len(fine))
        held.wait()
        x_ref[...] = select_rows(take, flat(tokens_ref)).astype(BF16)
        for copy in later:
            copy.wait()

    outs = [pltpu.VMEM((lines, 128), F32)] + shapes([len(fine)], width)
    outs += [pltpu.VMEM(w.shape, BF16) for w in weights]
    scratch = [pltpu.VMEM(flat_regions.shape, I32), pltpu.VMEM(places.shape, F32), pltpu.VMEM(tokens.shape, BF16)]
    args = [flags, table, tokens, flat_regions, places, *weights]
    in_specs = [SMEM, VMEM] + [HBM] * (3 + len(weights))
    ids, x, *weights = call(body, outs, args, in_specs, scratch, 3 + len(weights), 1 << 28, 4 << 20)
    return ids, x, weights


def id_columns(lines, count):
    lane = lax.broadcasted_iota(I32, (1, 128), 1).astype(F32)
    return jnp.where(columns_of(lines, count) == lane, 1.0, 0.0).astype(BF16)


def before_coarse(flags, fine, table, weight, plan):
    own, width = fine.shape
    half = 9 * weight.shape[0] // 32

    def body(flags_ref, rows_ref, fine_ref, weight_hbm, x_ref, part_hbm, home_ref, weight_ref, part_ref, sems):
        start = Copies(sems)
        later = start(weight_hbm.at[pl.ds(0, half)], weight_ref)
        take = columns_of(rows_of(plan, rows_ref, "fine_out"), own)
        part_ref[...] = select_rows(take, fine_ref[...]).astype(BF16)
        leave = start(part_ref, part_hbm)
        take = columns_of(rows_of(plan, rows_ref, "take_two"), own)
        x_ref[...] = select_rows(take, fine_ref[...]).astype(BF16)

        @pl.when(needs_fine(flags_ref, plan))
        def _():
            index = columns_of(rows_of(plan, rows_ref, "send_four"), sum(plan.room_four))
            home_ref[...] = select_rows(index, fine_ref[...]).astype(BF16)

        leave.wait()
        later.wait()

    outs = shapes([own], width) + shapes([own], width, pltpu.HBM)
    outs += shapes([sum(plan.room_four)], width) + shapes([half], weight.shape[1])
    scratch = [pltpu.VMEM(fine.shape, BF16)]
    args = [flags, table, fine, weight]
    return call(body, outs, args, [SMEM, VMEM, VMEM, HBM], scratch, 2, 1 << 28, 4 << 20)


def needs_fine(flags_ref, plan):
    with_fine = [n for n, sizes in enumerate(plan.four) if sum(sizes)]
    return functools.reduce(jnp.logical_or, [flags_ref[0] == n for n in with_fine])


def fine_level(x_own, source, ids, w_qkv, w_proj, rows, plan):
    count, width = x_own.shape
    inner = w_proj.shape[0]

    def body(own_ref, source_ref, ids_ref, qkv_w_ref, proj_w_ref, rows_ref, out_ref, *refs):
        *piece_outs, x_ref, qkv_ref, id_ref, _ = refs
        id_ref[...] = id_columns(ids_ref[: -(-count // 128), :], count)
        take = columns_of(rows_of(plan, rows_ref, "take_one"), count) - float(count)
        x = own_ref[...].astype(F32) + select_rows(take, source_ref[...])
        x_ref[...] = x
        normed = layer_norm(x).astype(BF16)
        qkv_ref[...] = jnp.dot(normed, qkv_w_ref[...], preferred_element_type=F32).astype(BF16)

        def finish(w, out):
            at = slice(w * TOK, (w + 1) * TOK)
            out = jnp.dot(out, proj_w_ref[...], preferred_element_type=F32)
            out_ref[at, :] = (x_ref[at, :] + out).astype(BF16)

        attend_windows(
            lambda w, at: qkv_ref[w * TOK : (w + 1) * TOK, at : at + 128],
            lambda w: id_ref[w * TOK : (w + 1) * TOK, :],
            count // TOK,
            inner,
            finish,
        )
        index = columns_of(rows_of(plan, rows_ref, "send_two"), sum(plan.room_two))
        put_pieces(select_rows(index, out_ref[...]), piece_outs)

    outs = shapes([count, *plan.room_two], width)
    scratch = [
        pltpu.VMEM((count, width), F32),
        pltpu.VMEM((count, 3 * inner), BF16),
        pltpu.VMEM((count, 128), BF16),
    ]
    args = [x_own, source, ids, w_qkv, w_proj, rows]
    out, *sent = call(body, outs, args, [VMEM] * len(args), scratch, 1, 3 << 30, 6 << 20, 14)
    return out, sent


def coarse_level(flags, home, x_own, source, ids, merge_first, w_merge, w_qkv, w_proj, rows, plan):
    depth, width = w_merge.shape
    own, half = x_own.shape
    count = own // 4
    inner = w_proj.shape[0]

    def body(
        flags_ref, merge_hbm, qkv_w_hbm, proj_w_hbm, home_ref, own_ref, source_ref, ids_ref, first_ref, rows_ref, *refs
    ):
        out_ref, *piece_outs = refs[:4]
        qkv_ref, id_ref, merge_ref, qkv_w_ref, proj_w_ref, sems = refs[4:]
        start = Copies(sems)
        here = first_ref.shape[0]
        merge_w = start(merge_hbm.at[pl.ds(here, depth - here)], merge_ref)
        qkv_w = start(qkv_w_hbm, qkv_w_ref)
        proj_w = start(proj_w_hbm, proj_w_ref)
        id_ref[...] = id_columns(ids_ref[-(-own // 128) :, :], count)
        take = columns_of(rows_of(plan, rows_ref, "take_two"), 4 * count) - float(own)
        x = own_ref[...].astype(F32) + select_rows(take, source_ref[...])
        x = jnp.concatenate([x[n * count : (n + 1) * count] for n in range(4)], axis=1)
        stacked = layer_norm(x).astype(BF16)
        merge_w.wait()
        merged = jnp.dot(stacked[:, :here], first_ref[...], preferred_element_type=F32)
        merged = merged + jnp.dot(stacked[:, here:], merge_ref[...], preferred_element_type=F32)
        merged = merged.astype(BF16).astype(F32)
        normed = layer_norm(merged).astype(BF16)
        qkv_w.wait()
        proj_w.wait()
        qkv_ref[...] = jnp.dot(normed, qkv_w_ref[...], preferred_element_type=F32).astype(BF16)

        def finish(w, out):
            out = jnp.dot(out, proj_w_ref[...], preferred_element_type=F32)
            out_ref[...] = (merged + out).astype(BF16)

        attend_windows(lambda w, at: qkv_ref[:, at : at + 128], lambda w: id_ref[...], 1, inner, finish)
        sent = select_rows(columns_of(rows_of(plan, rows_ref, "send_three"), sum(plan.room_three)), out_ref[...])
        sent = sent.astype(BF16)
        for n, sizes in enumerate(plan.three):

            @pl.when(flags_ref[0] == n)
            def _():
                at = 0
                for ref, size, space in zip(piece_outs, sizes, plan.room_three):
                    ref[:size, :] = sent[at : at + size, :half]
                    ref[size : 2 * size, :] = sent[at : at + size, half:]
                    at += space

        for n, fine_sizes in enumerate(plan.four):
            if sum(fine_sizes):

                @pl.when(flags_ref[0] == n)
                def _():
                    at = 0
                    for ref, size, more, space in zip(piece_outs, plan.three[n], fine_sizes, plan.room_four):
                        ref[2 * size : 2 * size + more, :] = home_ref[at : at + more, :]
                        at += space

    most = [max(2 * three[k] + four[k] for three, four in zip(plan.three, plan.four)) for k in range(3)]
    outs = shapes([count], width) + shapes(most, half)
    scratch = [pltpu.VMEM((count, 3 * inner), BF16)]
    shapes_in = [(count, 128), (depth - merge_first.shape[0], width), w_qkv.shape, w_proj.shape]
    scratch += [pltpu.VMEM(shape, BF16) for shape in shapes_in]
    args = [flags, w_merge, w_qkv, w_proj, home, x_own, source, ids, merge_first, rows]
    in_specs = [SMEM] + [HBM] * 3 + [VMEM] * (len(args) - 4)
    out, *sent = call(body, outs, args, in_specs, scratch, 3, 3 << 30, 12 << 20, 24)
    return out, sent


def fine_output(part, source, rows, plan, block_rows, block_cols, partial):
    own, width = part.shape

    def body(part_hbm, source_ref, rows_ref, out_ref, part_ref, stage_ref, sems):
        start = Copies(sems)
        cuts = [pl.ds(at, TOK) for at in range(0, own, TOK)]
        held = [start(part_hbm.at[cut], part_ref.at[cut]) for cut in cuts]
        take = columns_of(rows_of(plan, rows_ref, "fine_out"), own) - float(own)
        leave = []
        for n, (cut, copy) in enumerate(zip(cuts, held)):
            got = select_rows(take[n * TOK : (n + 1) * TOK], source_ref[...])
            copy.wait()
            out = part_ref[cut, :].astype(F32) + got
            if partial:
                out_ref[cut, :] = out.astype(BF16)
            else:
                lines = TOK // block_cols
                layer, line = divmod(n * lines, block_rows)
                there = (layer, pl.ds(line, lines))
                stage_ref[there] = out.reshape(lines, block_cols, width).astype(BF16)
                leave.append(start(stage_ref.at[there], out_ref.at[there]))
        for copy in leave:
            copy.wait()

    shape = (2, block_rows, block_cols, width)
    outs = shapes([own], width) if partial else [pltpu.HBM(shape, BF16)]
    scratch = [pltpu.VMEM(part.shape, BF16), pltpu.VMEM(shape, BF16)]
    return call(body, outs, [part, source, rows], [HBM, VMEM, VMEM], scratch, 2 * own // TOK, 1 << 30, 4 << 20)[0]


def coarse_output(coarse, got, rows, which, plan, block_rows, block_cols, part=None):
    own, width = coarse.shape
    half = width // 2
    sizes, more = plan.three[which], plan.four[which]
    parts = [] if part is None else [part]

    def padded(parts, sizes, room):
        out = []
        for value, size, space in zip(parts, sizes, room):
            out.append(value)
            if size < space:
                out.append(jnp.zeros((space - size, value.shape[1]), F32))
        return out

    def body(coarse_ref, *refs):
        got_refs, refs = refs[:3], refs[3:]
        part_refs, (rows_ref, out_ref, *fine_outs, _) = refs[: len(parts)], refs[len(parts) :]
        got = [ref[...].astype(F32) for ref in got_refs]
        back = [jnp.concatenate([x[:size], x[size : 2 * size]], axis=1) for x, size in zip(got, sizes)]
        source = stack_rows([coarse_ref[...].astype(F32)] + padded(back, sizes, plan.room_three))
        out = select_rows(columns_of(rows_of(plan, rows_ref, "coarse_out"), own), source.astype(BF16)).astype(BF16)
        for n in range(own // 2):
            out_ref[n // block_cols, n % block_cols] = out[2 * n : 2 * n + 2]
        for part_ref, fine_ref in zip(part_refs, fine_outs):
            fine = stack_rows(padded([x[2 * size :] for x, size in zip(got, sizes)], more, plan.room_four))
            base = part_ref.shape[0] + sum(plan.room_two)
            take = columns_of(rows_of(plan, rows_ref, "fine_out"), part_ref.shape[0]) - float(base)
            out = part_ref[...].astype(F32) + select_rows(take, fine.astype(BF16))
            fine_ref[...] = out.reshape(fine_ref.shape).astype(BF16)

    outs = [jax.ShapeDtypeStruct((block_rows, block_cols, 2, width), BF16)]
    outs += [jax.ShapeDtypeStruct((2, 2 * block_rows, 2 * block_cols, half), BF16) for _ in parts]
    args = [coarse, *got, *parts, rows]
    out, *fine = call(body, outs, args, [VMEM] * len(args), [], 1, 1 << 28, 1 << 20)
    return out.transpose(2, 0, 1, 3), *fine


def on_device(tokens, regions, shifts, fine_qkv, fine_proj, merge_weight, coarse_qkv, coarse_proj):
    _, rows, cols, _ = tokens.shape
    plan = Plan(rows, cols)

    def first(which, sign, sent, *args):
        got = exchange(sent, plan.one[which], sign)
        return lay(got, plan.room_one), before_fine(*args, plan)

    def second(which, sign, sent, *args):
        got = lay(exchange(sent, plan.two[which], sign), plan.room_two)
        if got is None:
            got = zeros((sum(plan.room_two), sent[0].shape[1]))
        return got, before_coarse(*args, plan)

    def third(which, sign, sent, part, source, coarse, table):
        sizes = [2 * n + m for n, m in zip(plan.three[which], plan.four[which])]
        got = exchange(sent, sizes, sign)
        partial = sum(plan.four[which]) > 0
        fine_out = fine_output(part, source, table, plan, rows, cols, partial)
        place = (table, which, plan, rows // 2, cols // 2)
        if partial:
            coarse_out, fine_out = coarse_output(coarse, got, *place, part=fine_out)
        else:
            (coarse_out,) = coarse_output(coarse, got, *place)
        return fine_out, coarse_out

    def branches(stage, pairs):
        return [functools.partial(stage, which, sign) for which, sign in pairs]

    sent, table, flags, one, two, three = first_pieces(shifts, tokens, plan)
    got, (ids, x, weights) = choose(
        one, branches(first, plan.one_branches), sent, flags, regions, tokens, table, [fine_qkv, fine_proj]
    )
    fine, sent = fine_level(x, got, ids, *weights, table, plan)
    got, (x, part, home, merge_first) = choose(
        two, branches(second, plan.two_branches), sent, flags, fine, table, merge_weight
    )
    coarse, sent = coarse_level(
        flags, home, x, got, ids, merge_first, merge_weight, coarse_qkv, coarse_proj, table, plan
    )
    return choose(three, branches(third, plan.three_branches), sent, part, got, coarse, table)


def solution(mesh):
    return jax.shard_map(
        on_device,
        mesh=mesh,
        in_specs=(P(None, "lat", "lon", None), P(), P(), P(), P(), P(), P(), P()),
        out_specs=(P(None, "lat", "lon", None), P(None, "lat", "lon", None)),
        check_vma=False,
    )
```

```python
import functools

import jax
import jax.numpy as jnp
import numpy as np
from jax import lax
from jax.experimental import pallas as pl
from jax.experimental.pallas import tpu as pltpu
from jax.sharding import PartitionSpec as P

HD = 32
WH = 6
WW = 12
TOK = 2 * WH * WW
EPS = 1e-05
BIG = 1e30
SCALE = float(1.0 / np.sqrt(HD))

NT = (((1,), (1,)), ((), ()))
TN = (((0,), (0,)), ((), ()))
F32 = jnp.float32
BF16 = jnp.bfloat16
I32 = jnp.int32

PAIRS = [(WH - 1, t) for t in range(1, WH)] + [(t, WH - 1) for t in range(1, WH - 1)]


def up16(count):
    return -(-count // 16) * 16


def natural(rows, cols):
    return [(l, r, c) for l in range(2) for r in range(rows) for c in range(cols)]


def windowed(rows, cols):
    return [
        (l, wr * WH + r, wc * WW + c)
        for wr in range(rows // WH)
        for wc in range(cols // WW)
        for l in range(2)
        for r in range(WH)
        for c in range(WW)
    ]


def moved(order, d):
    return [(l, r + d, c + 2 * d) for l, r, c in order]


def exchange_places(held, wanted, rows, cols, sign):
    at = {place: n for n, place in enumerate(held)}
    found = []
    for dr, dc in ((sign, 0), (0, sign), (sign, sign)):
        numbers, places = [], []
        for l, r, c in sorted(set(wanted) - set(held)):
            n = at.get((l, r - dr * rows, c - dc * cols))
            if n is not None:
                numbers.append(n)
                places.append((l, r, c))
        found.append((numbers, places))
    return found


def offsets(t0, t1):
    a = t0 if t0 <= 2 else t0 - WH
    big_a = t1 if t1 <= 2 else t1 - WH
    ahead = 1 if 2 * big_a > a or 2 * big_a - a == 0 and a < 0 else -1
    return a, big_a, ahead


def classes_of(needs, slack):
    rounded = [tuple(-(-size // 8) * 8 for size in need) for need in needs]
    heavy = [sum(need[1:3]) * 2 + sum(need[4:]) for need in rounded]
    limits = []
    for size in sorted(set(heavy)):
        if not limits or size > limits[-1][0] * slack:
            limits.append([size, size])
        limits[-1][1] = size
    which = [next(n for n, limit in enumerate(limits) if size <= limit[1]) for size in heavy]
    sizes = [
        [max(need[k] for need, w in zip(rounded, which) if w == n) for k in range(len(needs[0]))]
        for n in range(len(limits))
    ]
    return sizes, which


def rooms(sizes):
    return [up16(max(size[k] for size in sizes)) for k in range(len(sizes[0]))]


class Plan:
    def __init__(self, rows, cols):
        crows, ccols = rows // 2, cols // 2
        block, cblock = natural(rows, cols), natural(crows, ccols)
        cases = []
        for t0, t1 in PAIRS:
            a, big_a, ahead = offsets(t0, t1)
            fine = moved(windowed(rows, cols), a)
            coarse = moved(cblock, big_a)
            quarters = [
                (l, 2 * r + dr, 2 * c + dc)
                for dr, dc in ((0, 0), (1, 0), (0, 1), (1, 1))
                for l, r, c in coarse
            ]
            come = 1 if a > 0 else -1
            one = exchange_places(block, fine, rows, cols, come)
            home = [p for p in block if p not in set(fine)]
            wanted = quarters + (home if come == -ahead and 2 * big_a != a else [])
            two = exchange_places(fine, wanted, rows, cols, ahead)
            back = 1 if big_a < 0 else -1
            three = exchange_places(coarse, cblock, crows, ccols, back)
            got = set(fine).union(*[places for _, places in two])
            four = exchange_places(fine, [p for p in block if p not in got], rows, cols, back)
            cases.append((come, ahead, back, fine, coarse, quarters, one, two, three, four))

        def needs(which):
            return [[len(numbers) for numbers, _ in case[which]] for case in cases]

        self.one, one_class = classes_of(needs(6), 1.15)
        self.two, two_class = classes_of(needs(7), 1.15)
        sizes, three_class = classes_of([three + four for three, four in zip(needs(8), needs(9))], 1.0)
        self.three, self.four = [size[:3] for size in sizes], [size[3:] for size in sizes]
        self.room_one, self.room_two = rooms(self.one), rooms(self.two)
        self.room_three, self.room_four = rooms(self.three), rooms(self.four)

        def branches(which_class, direction):
            pairs = [(n, case[direction]) for n, case in zip(which_class, cases)]
            found = sorted(set(pairs))
            return found, [found.index(pair) for pair in pairs]

        self.one_branches, one_at = branches(one_class, 0)
        self.two_branches, two_at = branches(two_class, 1)
        self.three_branches, three_at = branches(three_class, 2)
        self.flags = dict(
            three_class=three_class,
            one_at=one_at, two_at=two_at, three_at=three_at,
            a=[offsets(*pair)[0] for pair in PAIRS], big_a=[offsets(*pair)[1] for pair in PAIRS],
        )

        found = {}
        for n, (come, ahead, back, fine, coarse, quarters, one, two, three, four) in enumerate(cases):

            def send(exchanged, room):
                return [n for (numbers, _), size in zip(exchanged, room) for n in numbers + [-1] * (size - len(numbers))]

            def source(held, *exchanges):
                places = list(held)
                for exchanged, room in exchanges:
                    for (_, got), size in zip(exchanged, room):
                        places += got + [None] * (size - len(got))
                return {p: n for n, p in enumerate(places) if p is not None}

            first, second = source(block, (one, self.room_one)), source(fine, (two, self.room_two))
            third = source(coarse, (three, self.room_three))
            last = source(fine, (two, self.room_two), (four, self.room_four))
            out = [(l, r, c) for r in range(crows) for c in range(ccols) for l in range(2)]
            rows_of = dict(
                send_one=send(one, self.room_one),
                take_one=[first[p] for p in fine],
                send_two=send(two, self.room_two),
                take_two=[second[p] for p in quarters],
                send_three=send(three, self.room_three),
                send_four=send(four, self.room_four),
                fine_out=[last[p] for p in block],
                coarse_out=[third[p] for p in out],
            )
            for name, row in rows_of.items():
                found.setdefault(name, []).append(row)
        parts, self.at, top = [], {}, 0
        for name, lists in found.items():
            length = -(-max(len(row) for row in lists) // 128)
            part = np.full((len(PAIRS), length * 128), -1, np.float32)
            for n, row in enumerate(lists):
                part[n, : len(row)] = row
            parts.append(part.reshape(len(PAIRS), length, 128))
            self.at[name] = (top, length)
            top += length
        parts.append(np.zeros((len(PAIRS), -top % 8, 128), np.float32))
        self.table = np.concatenate(parts, axis=1)


def case_of(shifts_ref):
    t0, t1 = shifts_ref[0], shifts_ref[1]
    return jnp.where(t0 == WH - 1, t1 - 1, t0 + WH - 2)


def lookup(values, case):
    out = jnp.int32(values[0])
    for n, value in enumerate(values[1:], 1):
        out = jnp.where(case == n, value, out)
    return out


def columns_of(rows, count):
    parts = [jnp.broadcast_to(rows[j : j + 1], (128, 128)).T for j in range(-(-count // 128))]
    return stack_rows(parts)[:count]


def select_rows(index, source):
    lane = lax.broadcasted_iota(I32, (1, 128), 1).astype(F32)
    size = source.shape[0]
    pick = [jnp.where(index == lane + float(at), 1.0, 0.0).astype(BF16) for at in range(0, size, 128)]
    pick = jnp.concatenate(pick, axis=1)[:, :size]
    return jnp.dot(pick, source, preferred_element_type=F32)


def stack_rows(parts):
    return parts[0] if len(parts) == 1 else jnp.concatenate(parts, axis=0)


def layer_norm(values):
    center = jnp.mean(values, axis=-1, keepdims=True)
    values = values - center
    spread = jnp.mean(values * values, axis=-1, keepdims=True)
    return values * lax.rsqrt(spread + EPS)


def attend_windows(qkv_of, id_of, windows, inner, finish):
    lane = lax.broadcasted_iota(I32, (1, 128), 1)
    forbid = jnp.where(lane < 8, BIG, 0.0).astype(BF16)
    groups = inner // 128
    units = [(w, g) for w in range(windows) for g in range(groups)]
    scores, weights, outs = {}, {}, {}

    def score(w, g):
        key_id = id_of(w)
        not_id = (key_id - 1).astype(BF16) * forbid
        q = qkv_of(w, g * 128)
        keys = jnp.concatenate([qkv_of(w, inner + g * 128), key_id], axis=1)
        queries = []
        for h in range(4):
            mine = jnp.where((lane >= h * HD) & (lane < (h + 1) * HD), 1.0, 0.0).astype(BF16)
            queries.append(jnp.concatenate([q * mine, not_id], axis=1))
        scores[w, g] = lax.dot_general(stack_rows(queries), keys, NT, preferred_element_type=F32)

    def soften(w, g):
        s = scores.pop((w, g))
        weights[w, g] = jnp.exp((s - jnp.max(s, axis=1, keepdims=True)) * SCALE).astype(BF16)

    def gather(w, g):
        v = qkv_of(w, 2 * inner + g * 128)
        values = jnp.concatenate([v, jnp.ones_like(v)], axis=1)
        out = jnp.dot(weights.pop((w, g)), values, preferred_element_type=F32)
        picked, total = out[:TOK, :128], out[:TOK, 128:]
        for h in range(1, 4):
            rows = slice(h * TOK, (h + 1) * TOK)
            picked = jnp.where(lane < h * HD, picked, out[rows, :128])
            total = jnp.where(lane < h * HD, total, out[rows, 128:])
        outs[w, g] = (picked / total).astype(BF16)
        if g == groups - 1:
            finish(w, jnp.concatenate([outs.pop((w, k)) for k in range(groups)], axis=1))

    for n in range(len(units) + 2):
        if n < len(units):
            score(*units[n])
        if 0 <= n - 1 < len(units):
            soften(*units[n - 1])
        if 0 <= n - 2 < len(units):
            gather(*units[n - 2])


ANY = pl.BlockSpec(memory_space=pl.ANY)
HBM = pl.BlockSpec(memory_space=pltpu.HBM)
VMEM = pl.BlockSpec(memory_space=pltpu.VMEM)
SMEM = pl.BlockSpec(memory_space=pltpu.SMEM)


def call(body, outs, args, in_specs, scratch, copies, flops, moved_bytes, vmem=8):
    args = [
        pltpu.with_memory_space_constraint(arg, spec.memory_space) for arg, spec in zip(args, in_specs, strict=True)
    ]
    spaces = [getattr(out, "memory_space", pltpu.SMEM if out.dtype == I32 else pltpu.VMEM) for out in outs]
    out_specs = [pl.BlockSpec(memory_space=space) for space in spaces]
    return pl.pallas_call(
        body,
        out_shape=outs,
        in_specs=in_specs,
        out_specs=out_specs,
        scratch_shapes=list(scratch) + [pltpu.SemaphoreType.DMA((copies,))],
        compiler_params=pltpu.CompilerParams(vmem_limit_bytes=vmem << 20),
        cost_estimate=pl.CostEstimate(flops=flops, bytes_accessed=moved_bytes, transcendentals=0),
    )(*args)


def shapes(sizes, width, space=pltpu.VMEM):
    return [space((n, width), BF16) for n in sizes]


class Copies:
    def __init__(self, sems):
        self.sems, self.used = sems, 0

    def __call__(self, src, dst):
        copy = pltpu.make_async_copy(src, dst, self.sems.at[self.used])
        self.used += 1
        copy.start()
        return copy


def lay(pieces, room):
    pieces = [piece for piece in pieces if piece is not None]
    if not pieces:
        return None
    width = pieces[0].shape[1]

    def body(*refs):
        out_ref = refs[len(pieces)]
        at = 0
        for ref, space in zip(refs, room):
            rows = ref.shape[0]
            out_ref[at : at + rows, :] = ref[...]
            if rows < space:
                out_ref[at + rows : at + space, :] = jnp.zeros((space - rows, width), BF16)
            at += space

    return call(body, shapes([sum(room)], width), pieces, [VMEM] * 3, [], 1, 0, 1 << 18)[0]


def zeros(shape):
    def body(out_ref, _):
        out_ref[...] = jnp.zeros(shape, BF16)

    return call(body, [pltpu.VMEM(shape, BF16)], [], [], [], 1, 0, 1 << 18)[0]


def flat(ref):
    layers, rows, cols, width = ref.shape
    return ref[...].astype(F32).reshape(layers * rows * cols, width).astype(BF16)


def put_pieces(value, refs):
    at = 0
    for ref in refs:
        ref[...] = value[at : at + ref.shape[0]].astype(BF16)
        at += ref.shape[0]


def rows_of(plan, table_ref, name, *lead):
    top, length = plan.at[name]
    return table_ref[(*lead, slice(top, top + length), slice(None))]


def exchange(pieces, sizes, sign):
    if not any(sizes):
        return [None] * 3
    lat, lon = lax.axis_size("lat"), lax.axis_size("lon")
    row, col, both = [piece[:size] for piece, size in zip(pieces, sizes)]
    pairs = [((i + sign) % lat * lon + (j + sign) % lon, i * lon + j) for i in range(lat) for j in range(lon)]
    col = lax.ppermute(col, "lon", [((j + sign) % lon, j) for j in range(lon)])
    both = lax.ppermute(both, ("lat", "lon"), pairs)
    row = lax.ppermute(row, "lat", [((i + sign) % lat, i) for i in range(lat)])
    return [row, col, both]


def choose(index, branches, *args):
    flat_args, tree = jax.tree.flatten(args)
    out_trees = []

    def closed(branch):
        def run(*leaves):
            out, out_tree = jax.tree.flatten(branch(*jax.tree.unflatten(tree, leaves)))
            out_trees.append(out_tree)
            return out

        return jax.make_jaxpr(run)(*flat_args)

    out = lax.cond_p.bind(index, *flat_args, branches=tuple(closed(branch) for branch in branches))
    return jax.tree.unflatten(out_trees[0], out)


FLAGS = ("three_class", "a", "big_a")


def first_pieces(shifts, tokens, plan):
    width = tokens.shape[-1]
    count = tokens.size // width
    kinds = 3

    def body(shifts_hbm, tokens_hbm, table_hbm, *refs):
        outs, refs = refs[:kinds], refs[kinds:]
        source_ref, rows_ref, flags_ref, *at_refs, shifts_ref, tokens_ref, table_ref, sems = refs
        start = Copies(sems)
        shift = start(shifts_hbm, shifts_ref)
        held = start(tokens_hbm, tokens_ref)
        table = start(table_hbm, table_ref)
        shift.wait()
        case = case_of(shifts_ref)
        for ref, name in zip(at_refs, ("one_at", "two_at", "three_at")):
            ref[0] = lookup(plan.flags[name], case)
        for n, name in enumerate(FLAGS):
            flags_ref[n] = lookup(plan.flags[name], case)
        held.wait()
        source_ref[...] = flat(tokens_ref)
        table.wait()
        rows_ref[...] = table_ref[case]
        index = columns_of(rows_of(plan, table_ref, "send_one", case), sum(plan.room_one))
        put_pieces(select_rows(index, source_ref[...]), outs)

    outs = shapes([*plan.room_one, count], width)
    outs += [pltpu.VMEM(plan.table.shape[1:], F32), pltpu.SMEM((8,), I32)]
    outs += [pltpu.SMEM((1,), I32)] * 3
    scratch = [pltpu.SMEM((2,), I32), pltpu.VMEM(tokens.shape, BF16), pltpu.VMEM(plan.table.shape, F32)]
    got = call(body, outs, [shifts, tokens, plan.table], [HBM] * 3, scratch, 3, 1 << 28, 1 << 20)
    sent, (source, rows, flags, one, two, three) = got[:kinds], got[kinds:]
    return sent, source, rows, flags, one[0], two[0], three[0]


def before_fine(flags, regions, tokens, table, weights, plan, rows, cols):
    _, lat, lon = regions.shape
    width = tokens.shape[1]
    flat_regions = regions.reshape(2 * lat, lon)
    fine, coarse = windowed(rows, cols), natural(rows // 2, cols // 2)

    def lanes(places, scale, is_fine):
        places = np.asarray([(l, scale * r, scale * c, is_fine) for l, r, c in places], np.float32)
        return np.pad(places, ((0, -len(places) % 128), (0, 0))).T.reshape(4, -1, 128)

    places = np.concatenate([lanes(fine, 1, 1), lanes(coarse, 2, 0)], axis=1)
    lines = places.shape[1]

    def body(flags_ref, rows_ref, tokens_ref, regions_hbm, places_hbm, *refs):
        weights_hbm, refs = refs[: len(weights)], refs[len(weights) :]
        id_ref, x_ref, *refs = refs
        weight_refs, (regions_ref, places_ref, sems) = refs[: len(weights)], refs[len(weights) :]
        start = Copies(sems)
        waits = [start(regions_hbm, regions_ref), start(places_hbm, places_ref)]
        later = [
            start(src.at[:, pl.ds(0, dst.shape[1])], dst) for src, dst in zip(weights_hbm, weight_refs)
        ]
        for copy in waits:
            copy.wait()
        a = flags_ref[1].astype(F32)
        big_a = 2.0 * flags_ref[2].astype(F32)
        is_fine = places_ref[3]
        d = is_fine * a + (1.0 - is_fine) * big_a
        row = places_ref[1] + d + (lax.axis_index("lat") * rows).astype(F32)
        col = places_ref[2] + 2.0 * d + (lax.axis_index("lon") * cols).astype(F32)
        wrapped = jnp.where((row < 0) | (row >= lat), 4.0, 0.0)
        row = jnp.where(row < 0, row + lat, jnp.where(row >= lat, row - lat, row))
        col = jnp.where(col < 0, col + lon, jnp.where(col >= lon, col - lon, col))
        row = row + places_ref[0] * lat

        def along(values):
            return jnp.concatenate([values[n : n + 1] for n in range(lines)], axis=1)

        line = lax.broadcasted_iota(I32, (2 * lat, 1), 0).astype(F32)
        pick = jnp.where(line == along(row), 1.0, 0.0).astype(BF16)
        known = regions_ref[...].astype(F32).astype(BF16)
        picked = lax.dot_general(known, pick, TN, preferred_element_type=F32)
        line = lax.broadcasted_iota(I32, (lon, 1), 0).astype(F32)
        ids = jnp.sum(jnp.where(line == along(col), picked, 0.0), axis=0, keepdims=True) + along(wrapped)
        for n in range(lines):
            id_ref[n : n + 1, :] = ids[:, n * 128 : (n + 1) * 128]
        take = columns_of(rows_of(plan, rows_ref, "take_one"), len(fine))
        x_ref[...] = select_rows(take, tokens_ref[...]).astype(BF16)
        for copy in later:
            copy.wait()

    outs = [pltpu.VMEM((lines, 128), F32)] + shapes([len(fine)], width)
    outs += [pltpu.VMEM((w.shape[0], min(w.shape[1], 2 * weights[1].shape[0])), BF16) for w in weights]
    scratch = [pltpu.VMEM(flat_regions.shape, I32), pltpu.VMEM(places.shape, F32)]
    args = [flags, table, tokens, flat_regions, places, *weights]
    in_specs = [SMEM, VMEM, VMEM] + [HBM] * (2 + len(weights))
    ids, x, *weights = call(body, outs, args, in_specs, scratch, 2 + len(weights), 1 << 28, 4 << 20)
    return ids, x, weights


def id_columns(lines, count):
    lane = lax.broadcasted_iota(I32, (1, 128), 1).astype(F32)
    return jnp.where(columns_of(lines, count) == lane, 1.0, 0.0).astype(BF16)


def before_coarse(flags, fine, table, weight, plan):
    own, width = fine.shape
    half = 9 * weight.shape[0] // 32

    def body(flags_ref, rows_ref, fine_ref, weight_hbm, x_ref, part_hbm, home_ref, weight_ref, part_ref, sems):
        start = Copies(sems)
        later = start(weight_hbm.at[pl.ds(0, half)], weight_ref)
        take = columns_of(rows_of(plan, rows_ref, "fine_out"), own)
        part_ref[...] = select_rows(take, fine_ref[...]).astype(BF16)
        leave = start(part_ref, part_hbm)
        take = columns_of(rows_of(plan, rows_ref, "take_two"), own)
        x_ref[...] = select_rows(take, fine_ref[...]).astype(BF16)

        @pl.when(needs_fine(flags_ref, plan))
        def _():
            index = columns_of(rows_of(plan, rows_ref, "send_four"), sum(plan.room_four))
            home_ref[...] = select_rows(index, fine_ref[...]).astype(BF16)

        leave.wait()
        later.wait()

    outs = shapes([own], width) + shapes([own], width, pltpu.HBM)
    outs += shapes([sum(plan.room_four)], width) + shapes([half], weight.shape[1])
    scratch = [pltpu.VMEM(fine.shape, BF16)]
    args = [flags, table, fine, weight]
    return call(body, outs, args, [SMEM, VMEM, VMEM, HBM], scratch, 2, 1 << 28, 4 << 20)


def needs_fine(flags_ref, plan):
    with_fine = [n for n, sizes in enumerate(plan.four) if sum(sizes)]
    return functools.reduce(jnp.logical_or, [flags_ref[0] == n for n in with_fine])


def fine_level(x_own, source, ids, w_qk, w_proj, w_qkv, rows, plan):
    count, width = x_own.shape
    inner = w_proj.shape[0]

    def body(own_ref, source_ref, ids_ref, qk_w_ref, proj_w_ref, qkv_w_hbm, rows_ref, out_ref, *refs):
        *piece_outs, x_ref, qkv_ref, id_ref, v_w_ref, sems = refs
        v_w = Copies(sems)(qkv_w_hbm.at[:, pl.ds(2 * inner, inner)], v_w_ref)
        id_ref[...] = id_columns(ids_ref[: -(-count // 128), :], count)
        take = columns_of(rows_of(plan, rows_ref, "take_one"), count) - float(count)
        x = own_ref[...].astype(F32) + select_rows(take, source_ref[...])
        x_ref[...] = x
        normed = layer_norm(x).astype(BF16)
        v_w.wait()
        qkv_ref[:, : 2 * inner] = jnp.dot(normed, qk_w_ref[...], preferred_element_type=F32).astype(BF16)
        qkv_ref[:, 2 * inner :] = jnp.dot(normed, v_w_ref[...], preferred_element_type=F32).astype(BF16)

        def finish(w, out):
            at = slice(w * TOK, (w + 1) * TOK)
            out = jnp.dot(out, proj_w_ref[...], preferred_element_type=F32)
            out_ref[at, :] = (x_ref[at, :] + out).astype(BF16)

        attend_windows(
            lambda w, at: qkv_ref[w * TOK : (w + 1) * TOK, at : at + 128],
            lambda w: id_ref[w * TOK : (w + 1) * TOK, :],
            count // TOK,
            inner,
            finish,
        )
        index = columns_of(rows_of(plan, rows_ref, "send_two"), sum(plan.room_two))
        put_pieces(select_rows(index, out_ref[...]), piece_outs)

    outs = shapes([count, *plan.room_two], width)
    scratch = [
        pltpu.VMEM((count, width), F32),
        pltpu.VMEM((count, 3 * inner), BF16),
        pltpu.VMEM((count, 128), BF16),
        pltpu.VMEM((width, inner), BF16),
    ]
    args = [x_own, source, ids, w_qk, w_proj, w_qkv, rows]
    out, *sent = call(body, outs, args, [VMEM] * 5 + [HBM, VMEM], scratch, 1, 3 << 30, 6 << 20, 14)
    return out, sent


def coarse_level(flags, home, x_own, source, ids, merge_first, w_merge, w_qkv, w_proj, rows, plan):
    depth, width = w_merge.shape
    own, half = x_own.shape
    count = own // 4
    inner = w_proj.shape[0]

    def body(
        flags_ref, merge_hbm, qkv_w_hbm, proj_w_hbm, home_ref, own_ref, source_ref, ids_ref, first_ref, rows_ref, *refs
    ):
        out_ref, *piece_outs = refs[:4]
        qkv_ref, id_ref, merge_ref, qkv_w_ref, proj_w_ref, sems = refs[4:]
        start = Copies(sems)
        here = first_ref.shape[0]
        merge_w = start(merge_hbm.at[pl.ds(here, depth - here)], merge_ref)
        qkv_w = start(qkv_w_hbm, qkv_w_ref)
        proj_w = start(proj_w_hbm, proj_w_ref)
        id_ref[...] = id_columns(ids_ref[-(-own // 128) :, :], count)
        take = columns_of(rows_of(plan, rows_ref, "take_two"), 4 * count) - float(own)
        x = own_ref[...].astype(F32) + select_rows(take, source_ref[...])
        x = jnp.concatenate([x[n * count : (n + 1) * count] for n in range(4)], axis=1)
        stacked = layer_norm(x).astype(BF16)
        merge_w.wait()
        merged = jnp.dot(stacked[:, :here], first_ref[...], preferred_element_type=F32)
        merged = merged + jnp.dot(stacked[:, here:], merge_ref[...], preferred_element_type=F32)
        merged = merged.astype(BF16).astype(F32)
        normed = layer_norm(merged).astype(BF16)
        qkv_w.wait()
        proj_w.wait()
        qkv_ref[...] = jnp.dot(normed, qkv_w_ref[...], preferred_element_type=F32).astype(BF16)

        def finish(w, out):
            out = jnp.dot(out, proj_w_ref[...], preferred_element_type=F32)
            out_ref[...] = (merged + out).astype(BF16)

        attend_windows(lambda w, at: qkv_ref[:, at : at + 128], lambda w: id_ref[...], 1, inner, finish)
        sent = select_rows(columns_of(rows_of(plan, rows_ref, "send_three"), sum(plan.room_three)), out_ref[...])
        sent = sent.astype(BF16)
        for n, sizes in enumerate(plan.three):

            @pl.when(flags_ref[0] == n)
            def _():
                at = 0
                for ref, size, space in zip(piece_outs, sizes, plan.room_three):
                    ref[:size, :] = sent[at : at + size, :half]
                    ref[size : 2 * size, :] = sent[at : at + size, half:]
                    at += space

        for n, fine_sizes in enumerate(plan.four):
            if sum(fine_sizes):

                @pl.when(flags_ref[0] == n)
                def _():
                    at = 0
                    for ref, size, more, space in zip(piece_outs, plan.three[n], fine_sizes, plan.room_four):
                        ref[2 * size : 2 * size + more, :] = home_ref[at : at + more, :]
                        at += space

    most = [max(2 * three[k] + four[k] for three, four in zip(plan.three, plan.four)) for k in range(3)]
    outs = shapes([count], width) + shapes(most, half)
    scratch = [pltpu.VMEM((count, 3 * inner), BF16)]
    shapes_in = [(count, 128), (depth - merge_first.shape[0], width), w_qkv.shape, w_proj.shape]
    scratch += [pltpu.VMEM(shape, BF16) for shape in shapes_in]
    args = [flags, w_merge, w_qkv, w_proj, home, x_own, source, ids, merge_first, rows]
    in_specs = [SMEM] + [HBM] * 3 + [VMEM] * (len(args) - 4)
    out, *sent = call(body, outs, args, in_specs, scratch, 3, 3 << 30, 12 << 20, 24)
    return out, sent


def fine_output(part, source, rows, plan, block_rows, block_cols, partial):
    own, width = part.shape

    def body(part_hbm, source_ref, rows_ref, out_ref, part_ref, stage_ref, sems):
        start = Copies(sems)
        cuts = [pl.ds(at, TOK) for at in range(0, own, TOK)]
        held = [start(part_hbm.at[cut], part_ref.at[cut]) for cut in cuts]
        take = columns_of(rows_of(plan, rows_ref, "fine_out"), own) - float(own)
        leave = []
        for n, (cut, copy) in enumerate(zip(cuts, held)):
            got = select_rows(take[n * TOK : (n + 1) * TOK], source_ref[...])
            copy.wait()
            out = part_ref[cut, :].astype(F32) + got
            if partial:
                out_ref[cut, :] = out.astype(BF16)
            else:
                lines = TOK // block_cols
                layer, line = divmod(n * lines, block_rows)
                there = (layer, pl.ds(line, lines))
                stage_ref[there] = out.reshape(lines, block_cols, width).astype(BF16)
                leave.append(start(stage_ref.at[there], out_ref.at[there]))
        for copy in leave:
            copy.wait()

    shape = (2, block_rows, block_cols, width)
    outs = shapes([own], width) if partial else [pltpu.HBM(shape, BF16)]
    scratch = [pltpu.VMEM(part.shape, BF16), pltpu.VMEM(shape, BF16)]
    return call(body, outs, [part, source, rows], [HBM, VMEM, VMEM], scratch, 2 * own // TOK, 1 << 30, 4 << 20)[0]


def coarse_output(coarse, got, rows, which, plan, block_rows, block_cols, part=None):
    own, width = coarse.shape
    half = width // 2
    sizes, more = plan.three[which], plan.four[which]
    parts = [] if part is None else [part]

    def padded(parts, sizes, room):
        out = []
        for value, size, space in zip(parts, sizes, room):
            out.append(value)
            if size < space:
                out.append(jnp.zeros((space - size, value.shape[1]), F32))
        return out

    def body(coarse_ref, *refs):
        got_refs, refs = refs[:3], refs[3:]
        part_refs, (rows_ref, out_ref, *fine_outs, _) = refs[: len(parts)], refs[len(parts) :]
        got = [ref[...].astype(F32) for ref in got_refs]
        back = [jnp.concatenate([x[:size], x[size : 2 * size]], axis=1) for x, size in zip(got, sizes)]
        source = stack_rows([coarse_ref[...].astype(F32)] + padded(back, sizes, plan.room_three))
        out = select_rows(columns_of(rows_of(plan, rows_ref, "coarse_out"), own), source.astype(BF16)).astype(BF16)
        for n in range(own // 2):
            out_ref[n // block_cols, n % block_cols] = out[2 * n : 2 * n + 2]
        for part_ref, fine_ref in zip(part_refs, fine_outs):
            fine = stack_rows(padded([x[2 * size :] for x, size in zip(got, sizes)], more, plan.room_four))
            base = part_ref.shape[0] + sum(plan.room_two)
            take = columns_of(rows_of(plan, rows_ref, "fine_out"), part_ref.shape[0]) - float(base)
            out = part_ref[...].astype(F32) + select_rows(take, fine.astype(BF16))
            fine_ref[...] = out.reshape(fine_ref.shape).astype(BF16)

    outs = [jax.ShapeDtypeStruct((block_rows, block_cols, 2, width), BF16)]
    outs += [jax.ShapeDtypeStruct((2, 2 * block_rows, 2 * block_cols, half), BF16) for _ in parts]
    args = [coarse, *got, *parts, rows]
    out, *fine = call(body, outs, args, [VMEM] * len(args), [], 1, 1 << 28, 1 << 20)
    return out.transpose(2, 0, 1, 3), *fine


def on_device(tokens, regions, shifts, fine_qkv, fine_proj, merge_weight, coarse_qkv, coarse_proj):
    _, rows, cols, _ = tokens.shape
    plan = Plan(rows, cols)

    def first(which, sign, sent, *args):
        got = exchange(sent, plan.one[which], sign)
        return lay(got, plan.room_one), before_fine(*args, plan, rows, cols)

    def second(which, sign, sent, *args):
        got = lay(exchange(sent, plan.two[which], sign), plan.room_two)
        if got is None:
            got = zeros((sum(plan.room_two), sent[0].shape[1]))
        return got, before_coarse(*args, plan)

    def third(which, sign, sent, part, source, coarse, table):
        sizes = [2 * n + m for n, m in zip(plan.three[which], plan.four[which])]
        got = exchange(sent, sizes, sign)
        partial = sum(plan.four[which]) > 0
        fine_out = fine_output(part, source, table, plan, rows, cols, partial)
        place = (table, which, plan, rows // 2, cols // 2)
        if partial:
            coarse_out, fine_out = coarse_output(coarse, got, *place, part=fine_out)
        else:
            (coarse_out,) = coarse_output(coarse, got, *place)
        return fine_out, coarse_out

    def branches(stage, pairs):
        return [functools.partial(stage, which, sign) for which, sign in pairs]

    sent, source, table, flags, one, two, three = first_pieces(shifts, tokens, plan)
    got, (ids, x, weights) = choose(
        one, branches(first, plan.one_branches), sent, flags, regions, source, table, [fine_qkv, fine_proj]
    )
    fine, sent = fine_level(x, got, ids, *weights, fine_qkv, table, plan)
    got, (x, part, home, merge_first) = choose(
        two, branches(second, plan.two_branches), sent, flags, fine, table, merge_weight
    )
    coarse, sent = coarse_level(
        flags, home, x, got, ids, merge_first, merge_weight, coarse_qkv, coarse_proj, table, plan
    )
    return choose(three, branches(third, plan.three_branches), sent, part, got, coarse, table)


def solution(mesh):
    return jax.shard_map(
        on_device,
        mesh=mesh,
        in_specs=(P(None, "lat", "lon", None), P(), P(), P(), P(), P(), P(), P()),
        out_specs=(P(None, "lat", "lon", None), P(None, "lat", "lon", None)),
        check_vma=False,
    )
```

```python
import functools

import jax
import jax.numpy as jnp
import numpy as np
from jax import lax
from jax.experimental import pallas as pl
from jax.experimental.pallas import tpu as pltpu
from jax.sharding import PartitionSpec as P

HD = 32
WH = 6
WW = 12
TOK = 2 * WH * WW
EPS = 1e-05
BIG = 1e30
SCALE = float(np.log2(np.e) / np.sqrt(HD))

NT = (((1,), (1,)), ((), ()))
TN = (((0,), (0,)), ((), ()))
F32 = jnp.float32
BF16 = jnp.bfloat16
I32 = jnp.int32

PAIRS = [(WH - 1, t) for t in range(1, WH)] + [(t, WH - 1) for t in range(1, WH - 1)]


def up16(count):
    return -(-count // 16) * 16


def natural(rows, cols):
    return [(l, r, c) for l in range(2) for r in range(rows) for c in range(cols)]


def windowed(rows, cols):
    return [
        (l, wr * WH + r, wc * WW + c)
        for wr in range(rows // WH)
        for wc in range(cols // WW)
        for l in range(2)
        for r in range(WH)
        for c in range(WW)
    ]


def moved(order, d):
    return [(l, r + d, c + 2 * d) for l, r, c in order]


def exchange_places(held, wanted, rows, cols, sign):
    at = {place: n for n, place in enumerate(held)}
    found = []
    for dr, dc in ((sign, 0), (0, sign), (sign, sign)):
        numbers, places = [], []
        for l, r, c in sorted(set(wanted) - set(held)):
            n = at.get((l, r - dr * rows, c - dc * cols))
            if n is not None:
                numbers.append(n)
                places.append((l, r, c))
        found.append((numbers, places))
    return found


def offsets(t0, t1):
    a = t0 if t0 <= 2 else t0 - WH
    big_a = t1 if t1 <= 2 else t1 - WH
    ahead = 1 if 2 * big_a > a or 2 * big_a - a == 0 and a < 0 else -1
    return a, big_a, ahead


def classes_of(needs, slack):
    rounded = [tuple(-(-size // 8) * 8 for size in need) for need in needs]
    heavy = [sum(need[1:3]) * 2 + sum(need[4:]) for need in rounded]
    limits = []
    for size in sorted(set(heavy)):
        if not limits or size > limits[-1][0] * slack:
            limits.append([size, size])
        limits[-1][1] = size
    which = [next(n for n, limit in enumerate(limits) if size <= limit[1]) for size in heavy]
    sizes = [
        [max(need[k] for need, w in zip(rounded, which) if w == n) for k in range(len(needs[0]))]
        for n in range(len(limits))
    ]
    return sizes, which


def rooms(sizes):
    return [up16(max(size[k] for size in sizes)) for k in range(len(sizes[0]))]


class Plan:
    def __init__(self, rows, cols):
        crows, ccols = rows // 2, cols // 2
        block, cblock = natural(rows, cols), natural(crows, ccols)
        cases = []
        for t0, t1 in PAIRS:
            a, big_a, ahead = offsets(t0, t1)
            fine = moved(windowed(rows, cols), a)
            coarse = moved(cblock, big_a)
            quarters = [
                (l, 2 * r + dr, 2 * c + dc)
                for dr, dc in ((0, 0), (1, 0), (0, 1), (1, 1))
                for l, r, c in coarse
            ]
            come = 1 if a > 0 else -1
            one = exchange_places(block, fine, rows, cols, come)
            home = [p for p in block if p not in set(fine)]
            wanted = quarters + (home if come == -ahead and 2 * big_a != a else [])
            two = exchange_places(fine, wanted, rows, cols, ahead)
            back = 1 if big_a < 0 else -1
            three = exchange_places(coarse, cblock, crows, ccols, back)
            got = set(fine).union(*[places for _, places in two])
            four = exchange_places(fine, [p for p in block if p not in got], rows, cols, back)
            cases.append((come, ahead, back, fine, coarse, quarters, one, two, three, four))

        def needs(which):
            return [[len(numbers) for numbers, _ in case[which]] for case in cases]

        self.one, one_class = classes_of(needs(6), 1.15)
        self.two, two_class = classes_of(needs(7), 1.0)
        sizes, three_class = classes_of([three + four for three, four in zip(needs(8), needs(9))], 1.0)
        self.three, self.four = [size[:3] for size in sizes], [size[3:] for size in sizes]
        self.room_one, self.room_two = rooms(self.one), rooms(self.two)
        self.room_three, self.room_four = rooms(self.three), rooms(self.four)

        def branches(which_class, direction):
            pairs = [(n, case[direction]) for n, case in zip(which_class, cases)]
            found = sorted(set(pairs))
            return found, [found.index(pair) for pair in pairs]

        self.one_branches, one_at = branches(one_class, 0)
        self.two_branches, two_at = branches(two_class, 1)
        self.three_branches, three_at = branches(three_class, 2)
        self.flags = dict(
            three_class=three_class,
            one_at=one_at, two_at=two_at, three_at=three_at,
            a=[offsets(*pair)[0] for pair in PAIRS], big_a=[offsets(*pair)[1] for pair in PAIRS],
        )

        found = {}
        for n, (come, ahead, back, fine, coarse, quarters, one, two, three, four) in enumerate(cases):

            def send(exchanged, room):
                return [n for (numbers, _), size in zip(exchanged, room) for n in numbers + [-1] * (size - len(numbers))]

            def source(held, *exchanges):
                places = list(held)
                for exchanged, room in exchanges:
                    for (_, got), size in zip(exchanged, room):
                        places += got + [None] * (size - len(got))
                return {p: n for n, p in enumerate(places) if p is not None}

            first, second = source(block, (one, self.room_one)), source(fine, (two, self.room_two))
            third = source(coarse, (three, self.room_three))
            last = source(fine, (two, self.room_two), (four, self.room_four))
            out = [(l, r, c) for r in range(crows) for c in range(ccols) for l in range(2)]
            rows_of = dict(
                send_one=send(one, self.room_one),
                take_one=[first[p] for p in fine],
                send_two=send(two, self.room_two),
                take_two=[second[p] for p in quarters],
                send_three=send(three, self.room_three),
                send_four=send(four, self.room_four),
                fine_out=[last[p] for p in block],
                coarse_out=[third[p] for p in out],
            )
            for name, row in rows_of.items():
                found.setdefault(name, []).append(row)
        parts, self.at, top = [], {}, 0
        for name, lists in found.items():
            length = -(-max(len(row) for row in lists) // 128)
            part = np.full((len(PAIRS), length * 128), -1, np.float32)
            for n, row in enumerate(lists):
                part[n, : len(row)] = row
            parts.append(part.reshape(len(PAIRS), length, 128))
            self.at[name] = (top, length)
            top += length
        parts.append(np.zeros((len(PAIRS), -top % 8, 128), np.float32))
        self.table = np.concatenate(parts, axis=1)


def case_of(shifts_ref):
    t0, t1 = shifts_ref[0], shifts_ref[1]
    return jnp.where(t0 == WH - 1, t1 - 1, t0 + WH - 2)


def lookup(values, case):
    out = jnp.int32(values[0])
    for n, value in enumerate(values[1:], 1):
        out = jnp.where(case == n, value, out)
    return out


def columns_of(rows, count):
    parts = [jnp.broadcast_to(rows[j : j + 1], (128, 128)).T for j in range(-(-count // 128))]
    return stack_rows(parts)[:count]


def select_rows(index, source):
    lane = lax.broadcasted_iota(I32, (1, 128), 1).astype(F32)
    size = source.shape[0]
    pick = [jnp.where(index == lane + float(at), 1.0, 0.0).astype(BF16) for at in range(0, size, 128)]
    pick = jnp.concatenate(pick, axis=1)[:, :size]
    return jnp.dot(pick, source, preferred_element_type=F32)


def stack_rows(parts):
    return parts[0] if len(parts) == 1 else jnp.concatenate(parts, axis=0)


def layer_norm(values):
    center = jnp.mean(values, axis=-1, keepdims=True)
    values = values - center
    spread = jnp.mean(values * values, axis=-1, keepdims=True)
    return values * lax.rsqrt(spread + EPS)


def attend_windows(qkv_of, id_of, windows, inner, finish):
    lane = lax.broadcasted_iota(I32, (1, 128), 1)
    forbid = jnp.where(lane < 8, BIG, 0.0).astype(BF16)
    groups = inner // 128
    units = [(w, g) for w in range(windows) for g in range(groups)]
    scores, weights, outs = {}, {}, {}

    def score(w, g):
        key_id = id_of(w)
        not_id = (key_id - 1).astype(BF16) * forbid
        q = qkv_of(w, g * 128)
        keys = jnp.concatenate([qkv_of(w, inner + g * 128), key_id], axis=1)
        queries = []
        for h in range(4):
            mine = jnp.where((lane >= h * HD) & (lane < (h + 1) * HD), 1.0, 0.0).astype(BF16)
            queries.append(jnp.concatenate([q * mine, not_id], axis=1))
        scores[w, g] = lax.dot_general(stack_rows(queries), keys, NT, preferred_element_type=F32)

    def soften(w, g):
        s = scores.pop((w, g))
        weights[w, g] = jnp.exp2((s - jnp.max(s, axis=1, keepdims=True)) * SCALE).astype(BF16)

    def gather(w, g):
        v = qkv_of(w, 2 * inner + g * 128)
        values = jnp.concatenate([v, jnp.ones_like(v)], axis=1)
        out = jnp.dot(weights.pop((w, g)), values, preferred_element_type=F32)
        picked, total = out[:TOK, :128], out[:TOK, 128:]
        for h in range(1, 4):
            rows = slice(h * TOK, (h + 1) * TOK)
            picked = jnp.where(lane < h * HD, picked, out[rows, :128])
            total = jnp.where(lane < h * HD, total, out[rows, 128:])
        outs[w, g] = (picked / total).astype(BF16)
        if g == groups - 1:
            finish(w, jnp.concatenate([outs.pop((w, k)) for k in range(groups)], axis=1))

    for n in range(len(units) + 2):
        if n < len(units):
            score(*units[n])
        if 0 <= n - 1 < len(units):
            soften(*units[n - 1])
        if 0 <= n - 2 < len(units):
            gather(*units[n - 2])


ANY = pl.BlockSpec(memory_space=pl.ANY)
HBM = pl.BlockSpec(memory_space=pltpu.HBM)
VMEM = pl.BlockSpec(memory_space=pltpu.VMEM)
SMEM = pl.BlockSpec(memory_space=pltpu.SMEM)


def call(body, outs, args, in_specs, scratch, copies, flops, moved_bytes, vmem=8):
    args = [
        pltpu.with_memory_space_constraint(arg, spec.memory_space) for arg, spec in zip(args, in_specs, strict=True)
    ]
    spaces = [getattr(out, "memory_space", pltpu.SMEM if out.dtype == I32 else pltpu.VMEM) for out in outs]
    out_specs = [pl.BlockSpec(memory_space=space) for space in spaces]
    return pl.pallas_call(
        body,
        out_shape=outs,
        in_specs=in_specs,
        out_specs=out_specs,
        scratch_shapes=list(scratch) + [pltpu.SemaphoreType.DMA((copies,))],
        compiler_params=pltpu.CompilerParams(vmem_limit_bytes=vmem << 20),
        cost_estimate=pl.CostEstimate(flops=flops, bytes_accessed=moved_bytes, transcendentals=0),
    )(*args)


def shapes(sizes, width, space=pltpu.VMEM):
    return [space((n, width), BF16) for n in sizes]


class Copies:
    def __init__(self, sems):
        self.sems, self.used = sems, 0

    def __call__(self, src, dst):
        copy = pltpu.make_async_copy(src, dst, self.sems.at[self.used])
        self.used += 1
        copy.start()
        return copy


def lay(pieces, room):
    pieces = [piece for piece in pieces if piece is not None]
    if not pieces:
        return None
    width = pieces[0].shape[1]

    def body(*refs):
        out_ref = refs[len(pieces)]
        at = 0
        for ref, space in zip(refs, room):
            rows = ref.shape[0]
            out_ref[at : at + rows, :] = ref[...]
            if rows < space:
                out_ref[at + rows : at + space, :] = jnp.zeros((space - rows, width), BF16)
            at += space

    return call(body, shapes([sum(room)], width), pieces, [VMEM] * 3, [], 1, 0, 1 << 18)[0]


def zeros(shape):
    def body(out_ref, _):
        out_ref[...] = jnp.zeros(shape, BF16)

    return call(body, [pltpu.VMEM(shape, BF16)], [], [], [], 1, 0, 1 << 18)[0]


def flat(ref):
    layers, rows, cols, width = ref.shape
    return ref[...].astype(F32).reshape(layers * rows * cols, width).astype(BF16)


def put_pieces(value, refs):
    at = 0
    for ref in refs:
        ref[...] = value[at : at + ref.shape[0]].astype(BF16)
        at += ref.shape[0]


def rows_of(plan, table_ref, name, *lead):
    top, length = plan.at[name]
    return table_ref[(*lead, slice(top, top + length), slice(None))]


def exchange(pieces, sizes, sign):
    if not any(sizes):
        return [None] * 3
    lat, lon = lax.axis_size("lat"), lax.axis_size("lon")
    row, col, both = [piece[:size] for piece, size in zip(pieces, sizes)]
    pairs = [((i + sign) % lat * lon + (j + sign) % lon, i * lon + j) for i in range(lat) for j in range(lon)]
    col = lax.ppermute(col, "lon", [((j + sign) % lon, j) for j in range(lon)])
    both = lax.ppermute(both, ("lat", "lon"), pairs)
    row = lax.ppermute(row, "lat", [((i + sign) % lat, i) for i in range(lat)])
    return [row, col, both]


def choose(index, branches, *args):
    flat_args, tree = jax.tree.flatten(args)
    out_trees = []

    def closed(branch):
        def run(*leaves):
            out, out_tree = jax.tree.flatten(branch(*jax.tree.unflatten(tree, leaves)))
            out_trees.append(out_tree)
            return out

        return jax.make_jaxpr(run)(*flat_args)

    out = lax.cond_p.bind(index, *flat_args, branches=tuple(closed(branch) for branch in branches))
    return jax.tree.unflatten(out_trees[0], out)


FLAGS = ("three_class", "a", "big_a")


def first_pieces(shifts, tokens, plan):
    width = tokens.shape[-1]
    count = tokens.size // width
    kinds = 3

    def body(shifts_hbm, tokens_hbm, table_hbm, *refs):
        outs, refs = refs[:kinds], refs[kinds:]
        source_ref, rows_ref, flags_ref, *at_refs, shifts_ref, tokens_ref, table_ref, sems = refs
        start = Copies(sems)
        shift = start(shifts_hbm, shifts_ref)
        held = start(tokens_hbm, tokens_ref)
        table = start(table_hbm, table_ref)
        shift.wait()
        case = case_of(shifts_ref)
        for ref, name in zip(at_refs, ("one_at", "two_at", "three_at")):
            ref[0] = lookup(plan.flags[name], case)
        for n, name in enumerate(FLAGS):
            flags_ref[n] = lookup(plan.flags[name], case)
        held.wait()
        source_ref[...] = flat(tokens_ref)
        table.wait()
        rows_ref[...] = table_ref[case]
        index = columns_of(rows_of(plan, table_ref, "send_one", case), sum(plan.room_one))
        put_pieces(select_rows(index, source_ref[...]), outs)

    outs = shapes([*plan.room_one, count], width)
    outs += [pltpu.VMEM(plan.table.shape[1:], F32), pltpu.SMEM((8,), I32)]
    outs += [pltpu.SMEM((1,), I32)] * 3
    scratch = [pltpu.SMEM((2,), I32), pltpu.VMEM(tokens.shape, BF16), pltpu.VMEM(plan.table.shape, F32)]
    got = call(body, outs, [shifts, tokens, plan.table], [HBM] * 3, scratch, 3, 1 << 28, 1 << 20)
    sent, (source, rows, flags, one, two, three) = got[:kinds], got[kinds:]
    return sent, source, rows, flags, one[0], two[0], three[0]


def before_fine(flags, regions, tokens, table, weights, plan, rows, cols):
    _, lat, lon = regions.shape
    width = tokens.shape[1]
    flat_regions = regions.reshape(2 * lat, lon)
    fine, coarse = windowed(rows, cols), natural(rows // 2, cols // 2)

    def lanes(places, scale, is_fine):
        places = np.asarray([(l, scale * r, scale * c, is_fine) for l, r, c in places], np.float32)
        return np.pad(places, ((0, -len(places) % 128), (0, 0))).T.reshape(4, -1, 128)

    places = np.concatenate([lanes(fine, 1, 1), lanes(coarse, 2, 0)], axis=1)
    lines = places.shape[1]

    def body(flags_ref, rows_ref, tokens_ref, regions_hbm, places_hbm, *refs):
        weights_hbm, refs = refs[: len(weights)], refs[len(weights) :]
        id_ref, x_ref, *refs = refs
        weight_refs, (regions_ref, places_ref, sems) = refs[: len(weights)], refs[len(weights) :]
        start = Copies(sems)
        waits = [start(regions_hbm, regions_ref), start(places_hbm, places_ref)]
        later = [
            start(src.at[:, pl.ds(0, dst.shape[1])], dst) for src, dst in zip(weights_hbm, weight_refs)
        ]
        for copy in waits:
            copy.wait()
        a = flags_ref[1].astype(F32)
        big_a = 2.0 * flags_ref[2].astype(F32)
        is_fine = places_ref[3]
        d = is_fine * a + (1.0 - is_fine) * big_a
        row = places_ref[1] + d + (lax.axis_index("lat") * rows).astype(F32)
        col = places_ref[2] + 2.0 * d + (lax.axis_index("lon") * cols).astype(F32)
        wrapped = jnp.where((row < 0) | (row >= lat), 4.0, 0.0)
        row = jnp.where(row < 0, row + lat, jnp.where(row >= lat, row - lat, row))
        col = jnp.where(col < 0, col + lon, jnp.where(col >= lon, col - lon, col))
        row = row + places_ref[0] * lat

        def along(values):
            return jnp.concatenate([values[n : n + 1] for n in range(lines)], axis=1)

        line = lax.broadcasted_iota(I32, (2 * lat, 1), 0).astype(F32)
        pick = jnp.where(line == along(row), 1.0, 0.0).astype(BF16)
        known = regions_ref[...].astype(F32).astype(BF16)
        picked = lax.dot_general(known, pick, TN, preferred_element_type=F32)
        line = lax.broadcasted_iota(I32, (lon, 1), 0).astype(F32)
        ids = jnp.sum(jnp.where(line == along(col), picked, 0.0), axis=0, keepdims=True) + along(wrapped)
        for n in range(lines):
            id_ref[n : n + 1, :] = ids[:, n * 128 : (n + 1) * 128]
        take = columns_of(rows_of(plan, rows_ref, "take_one"), len(fine))
        x_ref[...] = select_rows(take, tokens_ref[...]).astype(BF16)
        for copy in later:
            copy.wait()

    outs = [pltpu.VMEM((lines, 128), F32)] + shapes([len(fine)], width)
    outs += [pltpu.VMEM((w.shape[0], min(w.shape[1], 2 * weights[1].shape[0])), BF16) for w in weights]
    scratch = [pltpu.VMEM(flat_regions.shape, I32), pltpu.VMEM(places.shape, F32)]
    args = [flags, table, tokens, flat_regions, places, *weights]
    in_specs = [SMEM, VMEM, VMEM] + [HBM] * (2 + len(weights))
    ids, x, *weights = call(body, outs, args, in_specs, scratch, 2 + len(weights), 1 << 28, 4 << 20)
    return ids, x, weights


def id_columns(lines, count):
    lane = lax.broadcasted_iota(I32, (1, 128), 1).astype(F32)
    return jnp.where(columns_of(lines, count) == lane, 1.0, 0.0).astype(BF16)


def before_coarse(flags, fine, table, weight, plan):
    own, width = fine.shape
    half = 9 * weight.shape[0] // 32

    def body(flags_ref, rows_ref, fine_ref, weight_hbm, x_ref, part_hbm, home_ref, weight_ref, part_ref, sems):
        start = Copies(sems)
        later = start(weight_hbm.at[pl.ds(0, half)], weight_ref)
        take = columns_of(rows_of(plan, rows_ref, "fine_out"), own)
        part_ref[...] = select_rows(take, fine_ref[...]).astype(BF16)
        leave = start(part_ref, part_hbm)
        take = columns_of(rows_of(plan, rows_ref, "take_two"), own)
        x_ref[...] = select_rows(take, fine_ref[...]).astype(BF16)

        @pl.when(needs_fine(flags_ref, plan))
        def _():
            index = columns_of(rows_of(plan, rows_ref, "send_four"), sum(plan.room_four))
            home_ref[...] = select_rows(index, fine_ref[...]).astype(BF16)

        leave.wait()
        later.wait()

    outs = shapes([own], width) + shapes([own], width, pltpu.HBM)
    outs += shapes([sum(plan.room_four)], width) + shapes([half], weight.shape[1])
    scratch = [pltpu.VMEM(fine.shape, BF16)]
    args = [flags, table, fine, weight]
    return call(body, outs, args, [SMEM, VMEM, VMEM, HBM], scratch, 2, 1 << 28, 4 << 20)


def needs_fine(flags_ref, plan):
    with_fine = [n for n, sizes in enumerate(plan.four) if sum(sizes)]
    return functools.reduce(jnp.logical_or, [flags_ref[0] == n for n in with_fine])


def fine_level(x_own, source, ids, w_qk, w_proj, w_qkv, rows, plan):
    count, width = x_own.shape
    inner = w_proj.shape[0]

    def body(own_ref, source_ref, ids_ref, qk_w_ref, proj_w_ref, qkv_w_hbm, rows_ref, out_ref, *refs):
        *piece_outs, x_ref, qkv_ref, id_ref, v_w_ref, sems = refs
        v_w = Copies(sems)(qkv_w_hbm.at[:, pl.ds(2 * inner, inner)], v_w_ref)
        id_ref[...] = id_columns(ids_ref[: -(-count // 128), :], count)
        take = columns_of(rows_of(plan, rows_ref, "take_one"), count) - float(count)
        x = own_ref[...].astype(F32) + select_rows(take, source_ref[...])
        x_ref[...] = x
        normed = layer_norm(x).astype(BF16)
        v_w.wait()
        qkv_ref[:, : 2 * inner] = jnp.dot(normed, qk_w_ref[...], preferred_element_type=F32).astype(BF16)
        qkv_ref[:, 2 * inner :] = jnp.dot(normed, v_w_ref[...], preferred_element_type=F32).astype(BF16)

        def finish(w, out):
            at = slice(w * TOK, (w + 1) * TOK)
            out = jnp.dot(out, proj_w_ref[...], preferred_element_type=F32)
            out_ref[at, :] = (x_ref[at, :] + out).astype(BF16)

        attend_windows(
            lambda w, at: qkv_ref[w * TOK : (w + 1) * TOK, at : at + 128],
            lambda w: id_ref[w * TOK : (w + 1) * TOK, :],
            count // TOK,
            inner,
            finish,
        )
        index = columns_of(rows_of(plan, rows_ref, "send_two"), sum(plan.room_two))
        put_pieces(select_rows(index, out_ref[...]), piece_outs)

    outs = shapes([count, *plan.room_two], width)
    scratch = [
        pltpu.VMEM((count, width), F32),
        pltpu.VMEM((count, 3 * inner), BF16),
        pltpu.VMEM((count, 128), BF16),
        pltpu.VMEM((width, inner), BF16),
    ]
    args = [x_own, source, ids, w_qk, w_proj, w_qkv, rows]
    out, *sent = call(body, outs, args, [VMEM] * 5 + [HBM, VMEM], scratch, 1, 3 << 30, 6 << 20, 14)
    return out, sent


def coarse_level(flags, home, x_own, source, ids, merge_first, w_merge, w_qkv, w_proj, rows, plan):
    depth, width = w_merge.shape
    own, half = x_own.shape
    count = own // 4
    inner = w_proj.shape[0]

    def body(
        flags_ref, merge_hbm, qkv_w_hbm, proj_w_hbm, home_ref, own_ref, source_ref, ids_ref, first_ref, rows_ref, *refs
    ):
        out_ref, *piece_outs = refs[:4]
        qkv_ref, id_ref, merge_ref, qkv_w_ref, proj_w_ref, sems = refs[4:]
        start = Copies(sems)
        here = first_ref.shape[0]
        merge_w = start(merge_hbm.at[pl.ds(here, depth - here)], merge_ref)
        qkv_w = start(qkv_w_hbm, qkv_w_ref)
        proj_w = start(proj_w_hbm, proj_w_ref)
        id_ref[...] = id_columns(ids_ref[-(-own // 128) :, :], count)
        take = columns_of(rows_of(plan, rows_ref, "take_two"), 4 * count) - float(own)
        x = own_ref[...].astype(F32) + select_rows(take, source_ref[...])
        x = jnp.concatenate([x[n * count : (n + 1) * count] for n in range(4)], axis=1)
        stacked = layer_norm(x).astype(BF16)
        merge_w.wait()
        merged = jnp.dot(stacked[:, :here], first_ref[...], preferred_element_type=F32)
        merged = merged + jnp.dot(stacked[:, here:], merge_ref[...], preferred_element_type=F32)
        merged = merged.astype(BF16).astype(F32)
        normed = layer_norm(merged).astype(BF16)
        qkv_w.wait()
        proj_w.wait()
        qkv_ref[...] = jnp.dot(normed, qkv_w_ref[...], preferred_element_type=F32).astype(BF16)

        def finish(w, out):
            out = jnp.dot(out, proj_w_ref[...], preferred_element_type=F32)
            out_ref[...] = (merged + out).astype(BF16)

        attend_windows(lambda w, at: qkv_ref[:, at : at + 128], lambda w: id_ref[...], 1, inner, finish)
        sent = select_rows(columns_of(rows_of(plan, rows_ref, "send_three"), sum(plan.room_three)), out_ref[...])
        sent = sent.astype(BF16)
        for n, sizes in enumerate(plan.three):

            @pl.when(flags_ref[0] == n)
            def _():
                at = 0
                for ref, size, space in zip(piece_outs, sizes, plan.room_three):
                    ref[:size, :] = sent[at : at + size, :half]
                    ref[size : 2 * size, :] = sent[at : at + size, half:]
                    at += space

        for n, fine_sizes in enumerate(plan.four):
            if sum(fine_sizes):

                @pl.when(flags_ref[0] == n)
                def _():
                    at = 0
                    for ref, size, more, space in zip(piece_outs, plan.three[n], fine_sizes, plan.room_four):
                        ref[2 * size : 2 * size + more, :] = home_ref[at : at + more, :]
                        at += space

    most = [max(2 * three[k] + four[k] for three, four in zip(plan.three, plan.four)) for k in range(3)]
    outs = shapes([count], width) + shapes(most, half)
    scratch = [pltpu.VMEM((count, 3 * inner), BF16)]
    shapes_in = [(count, 128), (depth - merge_first.shape[0], width), w_qkv.shape, w_proj.shape]
    scratch += [pltpu.VMEM(shape, BF16) for shape in shapes_in]
    args = [flags, w_merge, w_qkv, w_proj, home, x_own, source, ids, merge_first, rows]
    in_specs = [SMEM] + [HBM] * 3 + [VMEM] * (len(args) - 4)
    out, *sent = call(body, outs, args, in_specs, scratch, 3, 3 << 30, 12 << 20, 24)
    return out, sent


def fine_output(part, source, rows, plan, block_rows, block_cols, partial):
    own, width = part.shape

    def body(part_hbm, source_ref, rows_ref, out_ref, part_ref, stage_ref, sems):
        start = Copies(sems)
        cuts = [pl.ds(at, TOK) for at in range(0, own, TOK)]
        held = [start(part_hbm.at[cut], part_ref.at[cut]) for cut in cuts]
        take = columns_of(rows_of(plan, rows_ref, "fine_out"), own) - float(own)
        leave = []
        for n, (cut, copy) in enumerate(zip(cuts, held)):
            got = select_rows(take[n * TOK : (n + 1) * TOK], source_ref[...])
            copy.wait()
            out = part_ref[cut, :].astype(F32) + got
            if partial:
                out_ref[cut, :] = out.astype(BF16)
            else:
                lines = TOK // block_cols
                layer, line = divmod(n * lines, block_rows)
                there = (layer, pl.ds(line, lines))
                stage_ref[there] = out.reshape(lines, block_cols, width).astype(BF16)
                leave.append(start(stage_ref.at[there], out_ref.at[there]))
        for copy in leave:
            copy.wait()

    shape = (2, block_rows, block_cols, width)
    outs = shapes([own], width) if partial else [pltpu.HBM(shape, BF16)]
    scratch = [pltpu.VMEM(part.shape, BF16), pltpu.VMEM(shape, BF16)]
    return call(body, outs, [part, source, rows], [HBM, VMEM, VMEM], scratch, 2 * own // TOK, 1 << 30, 4 << 20)[0]


def coarse_output(coarse, got, rows, which, plan, block_rows, block_cols, part=None):
    own, width = coarse.shape
    half = width // 2
    sizes, more = plan.three[which], plan.four[which]
    parts = [] if part is None else [part]

    def padded(parts, sizes, room):
        out = []
        for value, size, space in zip(parts, sizes, room):
            out.append(value)
            if size < space:
                out.append(jnp.zeros((space - size, value.shape[1]), F32))
        return out

    def body(coarse_ref, *refs):
        got_refs, refs = refs[:3], refs[3:]
        part_refs, (rows_ref, out_ref, *fine_outs, _) = refs[: len(parts)], refs[len(parts) :]
        got = [ref[...].astype(F32) for ref in got_refs]
        back = [jnp.concatenate([x[:size], x[size : 2 * size]], axis=1) for x, size in zip(got, sizes)]
        source = stack_rows([coarse_ref[...].astype(F32)] + padded(back, sizes, plan.room_three))
        out = select_rows(columns_of(rows_of(plan, rows_ref, "coarse_out"), own), source.astype(BF16)).astype(BF16)
        for n in range(own // 2):
            out_ref[n // block_cols, n % block_cols] = out[2 * n : 2 * n + 2]
        for part_ref, fine_ref in zip(part_refs, fine_outs):
            fine = stack_rows(padded([x[2 * size :] for x, size in zip(got, sizes)], more, plan.room_four))
            base = part_ref.shape[0] + sum(plan.room_two)
            take = columns_of(rows_of(plan, rows_ref, "fine_out"), part_ref.shape[0]) - float(base)
            out = part_ref[...].astype(F32) + select_rows(take, fine.astype(BF16))
            fine_ref[...] = out.reshape(fine_ref.shape).astype(BF16)

    outs = [jax.ShapeDtypeStruct((block_rows, block_cols, 2, width), BF16)]
    outs += [jax.ShapeDtypeStruct((2, 2 * block_rows, 2 * block_cols, half), BF16) for _ in parts]
    args = [coarse, *got, *parts, rows]
    out, *fine = call(body, outs, args, [VMEM] * len(args), [], 1, 1 << 28, 1 << 20)
    return out.transpose(2, 0, 1, 3), *fine


def on_device(tokens, regions, shifts, fine_qkv, fine_proj, merge_weight, coarse_qkv, coarse_proj):
    _, rows, cols, _ = tokens.shape
    plan = Plan(rows, cols)

    def first(which, sign, sent, *args):
        got = exchange(sent, plan.one[which], sign)
        return lay(got, plan.room_one), before_fine(*args, plan, rows, cols)

    def second(which, sign, sent, *args):
        got = lay(exchange(sent, plan.two[which], sign), plan.room_two)
        if got is None:
            got = zeros((sum(plan.room_two), sent[0].shape[1]))
        return got, before_coarse(*args, plan)

    def third(which, sign, sent, part, source, coarse, table):
        sizes = [2 * n + m for n, m in zip(plan.three[which], plan.four[which])]
        got = exchange(sent, sizes, sign)
        partial = sum(plan.four[which]) > 0
        fine_out = fine_output(part, source, table, plan, rows, cols, partial)
        place = (table, which, plan, rows // 2, cols // 2)
        if partial:
            coarse_out, fine_out = coarse_output(coarse, got, *place, part=fine_out)
        else:
            (coarse_out,) = coarse_output(coarse, got, *place)
        return fine_out, coarse_out

    def branches(stage, pairs):
        return [functools.partial(stage, which, sign) for which, sign in pairs]

    sent, source, table, flags, one, two, three = first_pieces(shifts, tokens, plan)
    got, (ids, x, weights) = choose(
        one, branches(first, plan.one_branches), sent, flags, regions, source, table, [fine_qkv, fine_proj]
    )
    fine, sent = fine_level(x, got, ids, *weights, fine_qkv, table, plan)
    got, (x, part, home, merge_first) = choose(
        two, branches(second, plan.two_branches), sent, flags, fine, table, merge_weight
    )
    coarse, sent = coarse_level(
        flags, home, x, got, ids, merge_first, merge_weight, coarse_qkv, coarse_proj, table, plan
    )
    return choose(three, branches(third, plan.three_branches), sent, part, got, coarse, table)


def solution(mesh):
    return jax.shard_map(
        on_device,
        mesh=mesh,
        in_specs=(P(None, "lat", "lon", None), P(), P(), P(), P(), P(), P(), P()),
        out_specs=(P(None, "lat", "lon", None), P(None, "lat", "lon", None)),
        check_vma=False,
    )
```

```python
import functools

import jax
import jax.numpy as jnp
import numpy as np
from jax import lax
from jax.experimental import pallas as pl
from jax.experimental.pallas import tpu as pltpu
from jax.sharding import PartitionSpec as P

HD = 32
WH = 6
WW = 12
TOK = 2 * WH * WW
EPS = 1e-05
BIG = 1e30
SCALE = float(np.log2(np.e) / np.sqrt(HD))

NT = (((1,), (1,)), ((), ()))
TN = (((0,), (0,)), ((), ()))
F32 = jnp.float32
BF16 = jnp.bfloat16
I32 = jnp.int32

PAIRS = [(WH - 1, t) for t in range(1, WH)] + [(t, WH - 1) for t in range(1, WH - 1)]


def up16(count):
    return -(-count // 16) * 16


def natural(rows, cols):
    return [(l, r, c) for l in range(2) for r in range(rows) for c in range(cols)]


def windowed(rows, cols):
    return [
        (l, wr * WH + r, wc * WW + c)
        for wr in range(rows // WH)
        for wc in range(cols // WW)
        for l in range(2)
        for r in range(WH)
        for c in range(WW)
    ]


def moved(order, d):
    return [(l, r + d, c + 2 * d) for l, r, c in order]


def exchange_places(held, wanted, rows, cols, sign):
    at = {place: n for n, place in enumerate(held)}
    found = []
    for dr, dc in ((sign, 0), (0, sign), (sign, sign)):
        numbers, places = [], []
        for l, r, c in sorted(set(wanted) - set(held)):
            n = at.get((l, r - dr * rows, c - dc * cols))
            if n is not None:
                numbers.append(n)
                places.append((l, r, c))
        found.append((numbers, places))
    return found


def offsets(t0, t1):
    a = t0 if t0 <= 2 else t0 - WH
    big_a = t1 if t1 <= 2 else t1 - WH
    ahead = 1 if 2 * big_a > a or 2 * big_a - a == 0 and a < 0 else -1
    return a, big_a, ahead


def classes_of(needs, slack):
    rounded = [tuple(-(-size // 8) * 8 for size in need) for need in needs]
    heavy = [sum(need[1:3]) * 2 + sum(need[4:]) for need in rounded]
    limits = []
    for size in sorted(set(heavy)):
        if not limits or size > limits[-1][0] * slack:
            limits.append([size, size])
        limits[-1][1] = size
    which = [next(n for n, limit in enumerate(limits) if size <= limit[1]) for size in heavy]
    sizes = [
        [max(need[k] for need, w in zip(rounded, which) if w == n) for k in range(len(needs[0]))]
        for n in range(len(limits))
    ]
    return sizes, which


def rooms(sizes):
    return [up16(max(size[k] for size in sizes)) for k in range(len(sizes[0]))]


class Plan:
    def __init__(self, rows, cols):
        crows, ccols = rows // 2, cols // 2
        block, cblock = natural(rows, cols), natural(crows, ccols)
        cases = []
        for t0, t1 in PAIRS:
            a, big_a, ahead = offsets(t0, t1)
            fine = moved(windowed(rows, cols), a)
            coarse = moved(cblock, big_a)
            quarters = [
                (l, 2 * r + dr, 2 * c + dc)
                for dr, dc in ((0, 0), (1, 0), (0, 1), (1, 1))
                for l, r, c in coarse
            ]
            come = 1 if a > 0 else -1
            one = exchange_places(block, fine, rows, cols, come)
            home = [p for p in block if p not in set(fine)]
            wanted = quarters + (home if come == -ahead and abs(2 * big_a - a) >= abs(a) else [])
            two = exchange_places(fine, wanted, rows, cols, ahead)
            back = 1 if big_a < 0 else -1
            three = exchange_places(coarse, cblock, crows, ccols, back)
            got = set(fine).union(*[places for _, places in two])
            four = exchange_places(fine, [p for p in block if p not in got], rows, cols, back)
            cases.append((come, ahead, back, fine, coarse, quarters, one, two, three, four))

        def needs(which):
            return [[len(numbers) for numbers, _ in case[which]] for case in cases]

        self.one, one_class = classes_of(needs(6), 1.15)
        self.two, two_class = classes_of(needs(7), 1.15)
        sizes, three_class = classes_of([three + four for three, four in zip(needs(8), needs(9))], 1.0)
        self.three, self.four = [size[:3] for size in sizes], [size[3:] for size in sizes]
        self.room_one, self.room_two = rooms(self.one), rooms(self.two)
        self.room_three, self.room_four = rooms(self.three), rooms(self.four)

        def branches(which_class, direction):
            pairs = [(n, case[direction]) for n, case in zip(which_class, cases)]
            found = sorted(set(pairs))
            return found, [found.index(pair) for pair in pairs]

        self.one_branches, one_at = branches(one_class, 0)
        self.two_branches, two_at = branches(two_class, 1)
        self.three_branches, three_at = branches(three_class, 2)
        self.flags = dict(
            three_class=three_class,
            one_at=one_at, two_at=two_at, three_at=three_at,
            a=[offsets(*pair)[0] for pair in PAIRS], big_a=[offsets(*pair)[1] for pair in PAIRS],
        )

        found = {}
        for n, (come, ahead, back, fine, coarse, quarters, one, two, three, four) in enumerate(cases):

            def send(exchanged, room):
                return [n for (numbers, _), size in zip(exchanged, room) for n in numbers + [-1] * (size - len(numbers))]

            def source(held, *exchanges):
                places = list(held)
                for exchanged, room in exchanges:
                    for (_, got), size in zip(exchanged, room):
                        places += got + [None] * (size - len(got))
                return {p: n for n, p in enumerate(places) if p is not None}

            first, second = source(block, (one, self.room_one)), source(fine, (two, self.room_two))
            third = source(coarse, (three, self.room_three))
            last = source(fine, (two, self.room_two), (four, self.room_four))
            out = [(l, r, c) for r in range(crows) for c in range(ccols) for l in range(2)]
            rows_of = dict(
                send_one=send(one, self.room_one),
                take_one=[first[p] for p in fine],
                send_two=send(two, self.room_two),
                take_two=[second[p] for p in quarters],
                send_three=send(three, self.room_three),
                send_four=send(four, self.room_four),
                fine_out=[last[p] for p in block],
                coarse_out=[third[p] for p in out],
            )
            for name, row in rows_of.items():
                found.setdefault(name, []).append(row)
        parts, self.at, top = [], {}, 0
        for name, lists in found.items():
            length = -(-max(len(row) for row in lists) // 128)
            part = np.full((len(PAIRS), length * 128), -1, np.float32)
            for n, row in enumerate(lists):
                part[n, : len(row)] = row
            parts.append(part.reshape(len(PAIRS), length, 128))
            self.at[name] = (top, length)
            top += length
        parts.append(np.zeros((len(PAIRS), -top % 8, 128), np.float32))
        self.table = np.concatenate(parts, axis=1)


def case_of(shifts_ref):
    t0, t1 = shifts_ref[0], shifts_ref[1]
    return jnp.where(t0 == WH - 1, t1 - 1, t0 + WH - 2)


def lookup(values, case):
    out = jnp.int32(values[0])
    for n, value in enumerate(values[1:], 1):
        out = jnp.where(case == n, value, out)
    return out


def columns_of(rows, count):
    parts = [jnp.broadcast_to(rows[j : j + 1], (128, 128)).T for j in range(-(-count // 128))]
    return stack_rows(parts)[:count]


def select_rows(index, source):
    lane = lax.broadcasted_iota(I32, (1, 128), 1).astype(F32)
    size = source.shape[0]
    pick = [jnp.where(index == lane + float(at), 1.0, 0.0).astype(BF16) for at in range(0, size, 128)]
    pick = jnp.concatenate(pick, axis=1)[:, :size]
    return jnp.dot(pick, source, preferred_element_type=F32)


def stack_rows(parts):
    return parts[0] if len(parts) == 1 else jnp.concatenate(parts, axis=0)


def layer_norm(values):
    center = jnp.mean(values, axis=-1, keepdims=True)
    values = values - center
    spread = jnp.mean(values * values, axis=-1, keepdims=True)
    return values * lax.rsqrt(spread + EPS)


def attend_windows(qkv_of, id_of, windows, inner, finish):
    lane = lax.broadcasted_iota(I32, (1, 128), 1)
    forbid = jnp.where(lane < 8, BIG, 0.0).astype(BF16)
    groups = inner // 128
    units = [(w, g) for w in range(windows) for g in range(groups)]
    scores, weights, outs = {}, {}, {}

    def score(w, g):
        key_id = id_of(w)
        not_id = (key_id - 1).astype(BF16) * forbid
        q = qkv_of(w, g * 128)
        keys = jnp.concatenate([qkv_of(w, inner + g * 128), key_id], axis=1)
        queries = []
        for h in range(4):
            mine = jnp.where((lane >= h * HD) & (lane < (h + 1) * HD), 1.0, 0.0).astype(BF16)
            queries.append(jnp.concatenate([q * mine, not_id], axis=1))
        scores[w, g] = lax.dot_general(stack_rows(queries), keys, NT, preferred_element_type=F32)

    def soften(w, g):
        s = scores.pop((w, g))
        weights[w, g] = jnp.exp2((s - jnp.max(s, axis=1, keepdims=True)) * SCALE).astype(BF16)

    def gather(w, g):
        v = qkv_of(w, 2 * inner + g * 128)
        values = jnp.concatenate([v, jnp.ones_like(v)], axis=1)
        out = jnp.dot(weights.pop((w, g)), values, preferred_element_type=F32)
        picked, total = out[:TOK, :128], out[:TOK, 128:]
        for h in range(1, 4):
            rows = slice(h * TOK, (h + 1) * TOK)
            picked = jnp.where(lane < h * HD, picked, out[rows, :128])
            total = jnp.where(lane < h * HD, total, out[rows, 128:])
        outs[w, g] = (picked / total).astype(BF16)
        if g == groups - 1:
            finish(w, jnp.concatenate([outs.pop((w, k)) for k in range(groups)], axis=1))

    for n in range(len(units) + 2):
        if n < len(units):
            score(*units[n])
        if 0 <= n - 1 < len(units):
            soften(*units[n - 1])
        if 0 <= n - 2 < len(units):
            gather(*units[n - 2])


ANY = pl.BlockSpec(memory_space=pl.ANY)
HBM = pl.BlockSpec(memory_space=pltpu.HBM)
VMEM = pl.BlockSpec(memory_space=pltpu.VMEM)
SMEM = pl.BlockSpec(memory_space=pltpu.SMEM)


def call(body, outs, args, in_specs, scratch, copies, flops, moved_bytes, vmem=8):
    args = [
        pltpu.with_memory_space_constraint(arg, spec.memory_space) for arg, spec in zip(args, in_specs, strict=True)
    ]
    spaces = [getattr(out, "memory_space", pltpu.SMEM if out.dtype == I32 else pltpu.VMEM) for out in outs]
    out_specs = [pl.BlockSpec(memory_space=space) for space in spaces]
    return pl.pallas_call(
        body,
        out_shape=outs,
        in_specs=in_specs,
        out_specs=out_specs,
        scratch_shapes=list(scratch) + [pltpu.SemaphoreType.DMA((copies,))],
        compiler_params=pltpu.CompilerParams(vmem_limit_bytes=vmem << 20),
        cost_estimate=pl.CostEstimate(flops=flops, bytes_accessed=moved_bytes, transcendentals=0),
    )(*args)


def shapes(sizes, width, space=pltpu.VMEM):
    return [space((n, width), BF16) for n in sizes]


class Copies:
    def __init__(self, sems):
        self.sems, self.used = sems, 0

    def __call__(self, src, dst):
        copy = pltpu.make_async_copy(src, dst, self.sems.at[self.used])
        self.used += 1
        copy.start()
        return copy


def lay(pieces, room):
    pieces = [piece for piece in pieces if piece is not None]
    if not pieces:
        return None
    width = pieces[0].shape[1]

    def body(*refs):
        out_ref = refs[len(pieces)]
        at = 0
        for ref, space in zip(refs, room):
            rows = ref.shape[0]
            out_ref[at : at + rows, :] = ref[...]
            if rows < space:
                out_ref[at + rows : at + space, :] = jnp.zeros((space - rows, width), BF16)
            at += space

    return call(body, shapes([sum(room)], width), pieces, [VMEM] * 3, [], 1, 0, 1 << 18)[0]


def zeros(shape):
    def body(out_ref, _):
        out_ref[...] = jnp.zeros(shape, BF16)

    return call(body, [pltpu.VMEM(shape, BF16)], [], [], [], 1, 0, 1 << 18)[0]


def flat(ref):
    layers, rows, cols, width = ref.shape
    return ref[...].astype(F32).reshape(layers * rows * cols, width).astype(BF16)


def put_pieces(value, refs):
    at = 0
    for ref in refs:
        ref[...] = value[at : at + ref.shape[0]].astype(BF16)
        at += ref.shape[0]


def rows_of(plan, table_ref, name, *lead):
    top, length = plan.at[name]
    return table_ref[(*lead, slice(top, top + length), slice(None))]


def exchange(pieces, sizes, sign):
    if not any(sizes):
        return [None] * 3
    lat, lon = lax.axis_size("lat"), lax.axis_size("lon")
    row, col, both = [piece[:size] for piece, size in zip(pieces, sizes)]
    pairs = [((i + sign) % lat * lon + (j + sign) % lon, i * lon + j) for i in range(lat) for j in range(lon)]
    col = lax.ppermute(col, "lon", [((j + sign) % lon, j) for j in range(lon)])
    both = lax.ppermute(both, ("lat", "lon"), pairs)
    row = lax.ppermute(row, "lat", [((i + sign) % lat, i) for i in range(lat)])
    return [row, col, both]


def choose(index, branches, *args):
    flat_args, tree = jax.tree.flatten(args)
    out_trees = []

    def closed(branch):
        def run(*leaves):
            out, out_tree = jax.tree.flatten(branch(*jax.tree.unflatten(tree, leaves)))
            out_trees.append(out_tree)
            return out

        return jax.make_jaxpr(run)(*flat_args)

    out = lax.cond_p.bind(index, *flat_args, branches=tuple(closed(branch) for branch in branches))
    return jax.tree.unflatten(out_trees[0], out)


FLAGS = ("three_class", "a", "big_a")


def first_pieces(shifts, tokens, plan):
    width = tokens.shape[-1]
    count = tokens.size // width
    kinds = 3

    def body(shifts_hbm, tokens_hbm, table_hbm, *refs):
        outs, refs = refs[:kinds], refs[kinds:]
        source_ref, rows_ref, flags_ref, *at_refs, shifts_ref, tokens_ref, table_ref, sems = refs
        start = Copies(sems)
        shift = start(shifts_hbm, shifts_ref)
        held = start(tokens_hbm, tokens_ref)
        table = start(table_hbm, table_ref)
        shift.wait()
        case = case_of(shifts_ref)
        for ref, name in zip(at_refs, ("one_at", "two_at", "three_at")):
            ref[0] = lookup(plan.flags[name], case)
        for n, name in enumerate(FLAGS):
            flags_ref[n] = lookup(plan.flags[name], case)
        held.wait()
        source_ref[...] = flat(tokens_ref)
        table.wait()
        rows_ref[...] = table_ref[case]
        index = columns_of(rows_of(plan, table_ref, "send_one", case), sum(plan.room_one))
        put_pieces(select_rows(index, source_ref[...]), outs)

    outs = shapes([*plan.room_one, count], width)
    outs += [pltpu.VMEM(plan.table.shape[1:], F32), pltpu.SMEM((8,), I32)]
    outs += [pltpu.SMEM((1,), I32)] * 3
    scratch = [pltpu.SMEM((2,), I32), pltpu.VMEM(tokens.shape, BF16), pltpu.VMEM(plan.table.shape, F32)]
    got = call(body, outs, [shifts, tokens, plan.table], [HBM] * 3, scratch, 3, 1 << 28, 1 << 20)
    sent, (source, rows, flags, one, two, three) = got[:kinds], got[kinds:]
    return sent, source, rows, flags, one[0], two[0], three[0]


def before_fine(flags, regions, tokens, table, weights, plan, rows, cols):
    _, lat, lon = regions.shape
    width = tokens.shape[1]
    flat_regions = regions.reshape(2 * lat, lon)
    fine, coarse = windowed(rows, cols), natural(rows // 2, cols // 2)

    def lanes(places, scale, is_fine):
        places = np.asarray([(l, scale * r, scale * c, is_fine) for l, r, c in places], np.float32)
        return np.pad(places, ((0, -len(places) % 128), (0, 0))).T.reshape(4, -1, 128)

    places = np.concatenate([lanes(fine, 1, 1), lanes(coarse, 2, 0)], axis=1)
    lines = places.shape[1]

    def body(flags_ref, rows_ref, tokens_ref, regions_hbm, places_hbm, *refs):
        weights_hbm, refs = refs[: len(weights)], refs[len(weights) :]
        id_ref, x_ref, *refs = refs
        weight_refs, (regions_ref, places_ref, sems) = refs[: len(weights)], refs[len(weights) :]
        start = Copies(sems)
        waits = [start(regions_hbm, regions_ref), start(places_hbm, places_ref)]
        later = [
            start(src.at[:, pl.ds(0, dst.shape[1])], dst) for src, dst in zip(weights_hbm, weight_refs)
        ]
        for copy in waits:
            copy.wait()
        a = flags_ref[1].astype(F32)
        big_a = 2.0 * flags_ref[2].astype(F32)
        is_fine = places_ref[3]
        d = is_fine * a + (1.0 - is_fine) * big_a
        row = places_ref[1] + d + (lax.axis_index("lat") * rows).astype(F32)
        col = places_ref[2] + 2.0 * d + (lax.axis_index("lon") * cols).astype(F32)
        wrapped = jnp.where((row < 0) | (row >= lat), 4.0, 0.0)
        row = jnp.where(row < 0, row + lat, jnp.where(row >= lat, row - lat, row))
        col = jnp.where(col < 0, col + lon, jnp.where(col >= lon, col - lon, col))
        row = row + places_ref[0] * lat

        def along(values):
            return jnp.concatenate([values[n : n + 1] for n in range(lines)], axis=1)

        line = lax.broadcasted_iota(I32, (2 * lat, 1), 0).astype(F32)
        pick = jnp.where(line == along(row), 1.0, 0.0).astype(BF16)
        known = regions_ref[...].astype(F32).astype(BF16)
        picked = lax.dot_general(known, pick, TN, preferred_element_type=F32)
        line = lax.broadcasted_iota(I32, (lon, 1), 0).astype(F32)
        ids = jnp.sum(jnp.where(line == along(col), picked, 0.0), axis=0, keepdims=True) + along(wrapped)
        for n in range(lines):
            id_ref[n : n + 1, :] = ids[:, n * 128 : (n + 1) * 128]
        take = columns_of(rows_of(plan, rows_ref, "take_one"), len(fine))
        x_ref[...] = select_rows(take, tokens_ref[...]).astype(BF16)
        for copy in later:
            copy.wait()

    outs = [pltpu.VMEM((lines, 128), F32)] + shapes([len(fine)], width)
    outs += [pltpu.VMEM((w.shape[0], min(w.shape[1], 2 * weights[1].shape[0])), BF16) for w in weights]
    scratch = [pltpu.VMEM(flat_regions.shape, I32), pltpu.VMEM(places.shape, F32)]
    args = [flags, table, tokens, flat_regions, places, *weights]
    in_specs = [SMEM, VMEM, VMEM] + [HBM] * (2 + len(weights))
    ids, x, *weights = call(body, outs, args, in_specs, scratch, 2 + len(weights), 1 << 28, 4 << 20)
    return ids, x, weights


def id_columns(lines, count):
    lane = lax.broadcasted_iota(I32, (1, 128), 1).astype(F32)
    return jnp.where(columns_of(lines, count) == lane, 1.0, 0.0).astype(BF16)


def before_coarse(flags, fine, table, weight, plan):
    own, width = fine.shape
    half = weight.shape[0] // 4

    def body(flags_ref, rows_ref, fine_ref, weight_hbm, x_ref, part_hbm, home_ref, weight_ref, part_ref, sems):
        start = Copies(sems)
        later = start(weight_hbm.at[pl.ds(0, half)], weight_ref)
        take = columns_of(rows_of(plan, rows_ref, "fine_out"), own)
        part_ref[...] = select_rows(take, fine_ref[...]).astype(BF16)
        leave = start(part_ref, part_hbm)
        take = columns_of(rows_of(plan, rows_ref, "take_two"), own)
        x_ref[...] = select_rows(take, fine_ref[...]).astype(BF16)

        @pl.when(needs_fine(flags_ref, plan))
        def _():
            index = columns_of(rows_of(plan, rows_ref, "send_four"), sum(plan.room_four))
            home_ref[...] = select_rows(index, fine_ref[...]).astype(BF16)

        leave.wait()
        later.wait()

    outs = shapes([own], width) + shapes([own], width, pltpu.HBM)
    outs += shapes([sum(plan.room_four)], width) + shapes([half], weight.shape[1])
    scratch = [pltpu.VMEM(fine.shape, BF16)]
    args = [flags, table, fine, weight]
    return call(body, outs, args, [SMEM, VMEM, VMEM, HBM], scratch, 2, 1 << 28, 4 << 20)


def needs_fine(flags_ref, plan):
    with_fine = [n for n, sizes in enumerate(plan.four) if sum(sizes)]
    return functools.reduce(jnp.logical_or, [flags_ref[0] == n for n in with_fine])


def fine_level(x_own, source, ids, w_qk, w_proj, w_qkv, rows, plan):
    count, width = x_own.shape
    inner = w_proj.shape[0]

    def body(own_ref, source_ref, ids_ref, qk_w_ref, proj_w_ref, qkv_w_hbm, rows_ref, out_ref, *refs):
        *piece_outs, x_ref, qkv_ref, id_ref, v_w_ref, sems = refs
        v_w = Copies(sems)(qkv_w_hbm.at[:, pl.ds(2 * inner, inner)], v_w_ref)
        id_ref[...] = id_columns(ids_ref[: -(-count // 128), :], count)
        take = columns_of(rows_of(plan, rows_ref, "take_one"), count) - float(count)
        x = own_ref[...].astype(F32) + select_rows(take, source_ref[...])
        x_ref[...] = x
        normed = layer_norm(x).astype(BF16)
        v_w.wait()
        qkv_ref[:, : 2 * inner] = jnp.dot(normed, qk_w_ref[...], preferred_element_type=F32).astype(BF16)
        qkv_ref[:, 2 * inner :] = jnp.dot(normed, v_w_ref[...], preferred_element_type=F32).astype(BF16)

        def finish(w, out):
            at = slice(w * TOK, (w + 1) * TOK)
            out = jnp.dot(out, proj_w_ref[...], preferred_element_type=F32)
            out_ref[at, :] = (x_ref[at, :] + out).astype(BF16)

        attend_windows(
            lambda w, at: qkv_ref[w * TOK : (w + 1) * TOK, at : at + 128],
            lambda w: id_ref[w * TOK : (w + 1) * TOK, :],
            count // TOK,
            inner,
            finish,
        )
        index = columns_of(rows_of(plan, rows_ref, "send_two"), sum(plan.room_two))
        put_pieces(select_rows(index, out_ref[...]), piece_outs)

    outs = shapes([count, *plan.room_two], width)
    scratch = [
        pltpu.VMEM((count, width), F32),
        pltpu.VMEM((count, 3 * inner), BF16),
        pltpu.VMEM((count, 128), BF16),
        pltpu.VMEM((width, inner), BF16),
    ]
    args = [x_own, source, ids, w_qk, w_proj, w_qkv, rows]
    out, *sent = call(body, outs, args, [VMEM] * 5 + [HBM, VMEM], scratch, 1, 3 << 30, 6 << 20, 14)
    return out, sent


def coarse_level(flags, home, x_own, source, ids, merge_first, w_merge, w_qkv, w_proj, rows, plan):
    depth, width = w_merge.shape
    own, half = x_own.shape
    count = own // 4
    inner = w_proj.shape[0]

    def body(
        flags_ref, merge_hbm, qkv_w_hbm, proj_w_hbm, home_ref, own_ref, source_ref, ids_ref, first_ref, rows_ref, *refs
    ):
        out_ref, *piece_outs = refs[:4]
        qkv_ref, id_ref, merge_ref, qkv_w_ref, proj_w_ref, sems = refs[4:]
        start = Copies(sems)
        here = first_ref.shape[0]
        merge_w = start(merge_hbm.at[pl.ds(here, depth - here)], merge_ref)
        qkv_w = start(qkv_w_hbm, qkv_w_ref)
        proj_w = start(proj_w_hbm, proj_w_ref)
        id_ref[...] = id_columns(ids_ref[-(-own // 128) :, :], count)
        take = columns_of(rows_of(plan, rows_ref, "take_two"), 4 * count) - float(own)
        x = own_ref[...].astype(F32) + select_rows(take, source_ref[...])
        x = jnp.concatenate([x[n * count : (n + 1) * count] for n in range(4)], axis=1)
        stacked = layer_norm(x).astype(BF16)
        merge_w.wait()
        merged = jnp.dot(stacked[:, :here], first_ref[...], preferred_element_type=F32)
        merged = merged + jnp.dot(stacked[:, here:], merge_ref[...], preferred_element_type=F32)
        merged = merged.astype(BF16).astype(F32)
        normed = layer_norm(merged).astype(BF16)
        qkv_w.wait()
        proj_w.wait()
        qkv_ref[...] = jnp.dot(normed, qkv_w_ref[...], preferred_element_type=F32).astype(BF16)

        def finish(w, out):
            out = jnp.dot(out, proj_w_ref[...], preferred_element_type=F32)
            out_ref[...] = (merged + out).astype(BF16)

        attend_windows(lambda w, at: qkv_ref[:, at : at + 128], lambda w: id_ref[...], 1, inner, finish)
        sent = select_rows(columns_of(rows_of(plan, rows_ref, "send_three"), sum(plan.room_three)), out_ref[...])
        sent = sent.astype(BF16)
        for n, sizes in enumerate(plan.three):

            @pl.when(flags_ref[0] == n)
            def _():
                at = 0
                for ref, size, space in zip(piece_outs, sizes, plan.room_three):
                    ref[:size, :] = sent[at : at + size, :half]
                    ref[size : 2 * size, :] = sent[at : at + size, half:]
                    at += space

        for n, fine_sizes in enumerate(plan.four):
            if sum(fine_sizes):

                @pl.when(flags_ref[0] == n)
                def _():
                    at = 0
                    for ref, size, more, space in zip(piece_outs, plan.three[n], fine_sizes, plan.room_four):
                        ref[2 * size : 2 * size + more, :] = home_ref[at : at + more, :]
                        at += space

    most = [max(2 * three[k] + four[k] for three, four in zip(plan.three, plan.four)) for k in range(3)]
    outs = shapes([count], width) + shapes(most, half)
    scratch = [pltpu.VMEM((count, 3 * inner), BF16)]
    shapes_in = [(count, 128), (depth - merge_first.shape[0], width), w_qkv.shape, w_proj.shape]
    scratch += [pltpu.VMEM(shape, BF16) for shape in shapes_in]
    args = [flags, w_merge, w_qkv, w_proj, home, x_own, source, ids, merge_first, rows]
    in_specs = [SMEM] + [HBM] * 3 + [VMEM] * (len(args) - 4)
    out, *sent = call(body, outs, args, in_specs, scratch, 3, 3 << 30, 12 << 20, 24)
    return out, sent


def fine_output(part, source, rows, plan, block_rows, block_cols, partial):
    own, width = part.shape

    def body(part_hbm, source_ref, rows_ref, out_ref, part_ref, stage_ref, sems):
        start = Copies(sems)
        cuts = [pl.ds(at, TOK) for at in range(0, own, TOK)]
        held = [start(part_hbm.at[cut], part_ref.at[cut]) for cut in cuts]
        take = columns_of(rows_of(plan, rows_ref, "fine_out"), own) - float(own)
        leave = []
        for n, (cut, copy) in enumerate(zip(cuts, held)):
            got = select_rows(take[n * TOK : (n + 1) * TOK], source_ref[...])
            copy.wait()
            out = part_ref[cut, :].astype(F32) + got
            if partial:
                out_ref[cut, :] = out.astype(BF16)
            else:
                lines = TOK // block_cols
                layer, line = divmod(n * lines, block_rows)
                there = (layer, pl.ds(line, lines))
                stage_ref[there] = out.reshape(lines, block_cols, width).astype(BF16)
                leave.append(start(stage_ref.at[there], out_ref.at[there]))
        for copy in leave:
            copy.wait()

    shape = (2, block_rows, block_cols, width)
    outs = shapes([own], width) if partial else [pltpu.HBM(shape, BF16)]
    scratch = [pltpu.VMEM(part.shape, BF16), pltpu.VMEM(shape, BF16)]
    return call(body, outs, [part, source, rows], [HBM, VMEM, VMEM], scratch, 2 * own // TOK, 1 << 30, 4 << 20)[0]


def coarse_output(coarse, got, rows, which, plan, block_rows, block_cols, part=None):
    own, width = coarse.shape
    half = width // 2
    sizes, more = plan.three[which], plan.four[which]
    parts = [] if part is None else [part]

    def padded(parts, sizes, room):
        out = []
        for value, size, space in zip(parts, sizes, room):
            out.append(value)
            if size < space:
                out.append(jnp.zeros((space - size, value.shape[1]), F32))
        return out

    def body(coarse_ref, *refs):
        got_refs, refs = refs[:3], refs[3:]
        part_refs, (rows_ref, out_ref, *fine_outs, _) = refs[: len(parts)], refs[len(parts) :]
        got = [ref[...].astype(F32) for ref in got_refs]
        back = [jnp.concatenate([x[:size], x[size : 2 * size]], axis=1) for x, size in zip(got, sizes)]
        source = stack_rows([coarse_ref[...].astype(F32)] + padded(back, sizes, plan.room_three))
        out = select_rows(columns_of(rows_of(plan, rows_ref, "coarse_out"), own), source.astype(BF16)).astype(BF16)
        for n in range(own // 2):
            out_ref[n // block_cols, n % block_cols] = out[2 * n : 2 * n + 2]
        for part_ref, fine_ref in zip(part_refs, fine_outs):
            fine = stack_rows(padded([x[2 * size :] for x, size in zip(got, sizes)], more, plan.room_four))
            base = part_ref.shape[0] + sum(plan.room_two)
            take = columns_of(rows_of(plan, rows_ref, "fine_out"), part_ref.shape[0]) - float(base)
            out = part_ref[...].astype(F32) + select_rows(take, fine.astype(BF16))
            fine_ref[...] = out.reshape(fine_ref.shape).astype(BF16)

    outs = [jax.ShapeDtypeStruct((block_rows, block_cols, 2, width), BF16)]
    outs += [jax.ShapeDtypeStruct((2, 2 * block_rows, 2 * block_cols, half), BF16) for _ in parts]
    args = [coarse, *got, *parts, rows]
    out, *fine = call(body, outs, args, [VMEM] * len(args), [], 1, 1 << 28, 1 << 20)
    return out.transpose(2, 0, 1, 3), *fine


def on_device(tokens, regions, shifts, fine_qkv, fine_proj, merge_weight, coarse_qkv, coarse_proj):
    _, rows, cols, _ = tokens.shape
    plan = Plan(rows, cols)

    def first(which, sign, sent, *args):
        got = exchange(sent, plan.one[which], sign)
        return lay(got, plan.room_one), before_fine(*args, plan, rows, cols)

    def second(which, sign, sent, *args):
        got = lay(exchange(sent, plan.two[which], sign), plan.room_two)
        if got is None:
            got = zeros((sum(plan.room_two), sent[0].shape[1]))
        return got, before_coarse(*args, plan)

    def third(which, sign, sent, part, source, coarse, table):
        sizes = [2 * n + m for n, m in zip(plan.three[which], plan.four[which])]
        got = exchange(sent, sizes, sign)
        partial = sum(plan.four[which]) > 0
        fine_out = fine_output(part, source, table, plan, rows, cols, partial)
        place = (table, which, plan, rows // 2, cols // 2)
        if partial:
            coarse_out, fine_out = coarse_output(coarse, got, *place, part=fine_out)
        else:
            (coarse_out,) = coarse_output(coarse, got, *place)
        return fine_out, coarse_out

    def branches(stage, pairs):
        return [functools.partial(stage, which, sign) for which, sign in pairs]

    sent, source, table, flags, one, two, three = first_pieces(shifts, tokens, plan)
    got, (ids, x, weights) = choose(
        one, branches(first, plan.one_branches), sent, flags, regions, source, table, [fine_qkv, fine_proj]
    )
    fine, sent = fine_level(x, got, ids, *weights, fine_qkv, table, plan)
    got, (x, part, home, merge_first) = choose(
        two, branches(second, plan.two_branches), sent, flags, fine, table, merge_weight
    )
    coarse, sent = coarse_level(
        flags, home, x, got, ids, merge_first, merge_weight, coarse_qkv, coarse_proj, table, plan
    )
    return choose(three, branches(third, plan.three_branches), sent, part, got, coarse, table)


def solution(mesh):
    return jax.shard_map(
        on_device,
        mesh=mesh,
        in_specs=(P(None, "lat", "lon", None), P(), P(), P(), P(), P(), P(), P()),
        out_specs=(P(None, "lat", "lon", None), P(None, "lat", "lon", None)),
        check_vma=False,
    )
```
